32 devices in a mesh: gx: 4 (over z), gy: 4 (over y, x), gz: 2 (over core).
Axes of the slice: x: 2, y: 2, z: 4, core: 2. Of those that a mesh axis runs over, the one named last changes fastest.
Arguments:
- spacetime: float32 [22, 16, 16, 256], P(None, 'gx', 'gy', 'gz'), may hold values from -0.2 to 1.12, as said below
- fluid: float32 [8, 16, 16, 256], P(None, 'gx', 'gy', 'gz'), may hold values from -20 to 20, as said below
Outputs:
- spacetime_next: float32 [22, 16, 16, 256], P(None, 'gx', 'gy', 'gz')
- fluid_next: float32 [8, 16, 16, 256], P(None, 'gx', 'gy', 'gz')
The draws below stay inside these ranges and needn't reach their ends.
Inputs may be any that keep to these rules, and one draw needn't show every extreme that they name: `spacetime`: chi and the lapse are positive and at most one; the conformal metric's entries are each within 0.12 of those of the identity. `fluid`: the first five components are densitized conserved values of states with positive density and pressure and speeds below one; the face fields have zero discrete divergence up to rounding.
All inputs are finite; a program needn't handle non-finite values.
Results may differ from the reference program's by a relative error of at most 0.0003.
Values sent between devices are 32-bit elements; how exact they have to be, the bound alone decides.
No kernel may reach another device: no remote copies, remote signals or barrier semaphores. Data moves between devices by JAX's collectives and lax.ppermute only.
A program may use at most 64 MiB of HBM per device.

```python
import math
import jax
import jax.numpy as jnp
from jax import lax

FIELDS = 22
GHOST = 3
RECOVERY_STEPS = 4
CX = 4
CY = 4
NX = 16
NY = 16
NZ = 256
N_GX = 4
N_GY = 4


def positions():
    along_x = (jnp.arange(NX, dtype=jnp.float32) / NX)[:, None, None]
    along_y = (jnp.arange(NY, dtype=jnp.float32) / NY)[None, :, None]
    along_z = (jnp.arange(NZ, dtype=jnp.float32) / NZ)[None, None, :]
    return (along_x, along_y, along_z)


def spacetime_fields(key):
    rough_part = jax.random.uniform(jax.random.fold_in(key, 11), (FIELDS, NX, NY, NZ), jnp.float32, -1.0, 1.0)
    along_x, along_y, along_z = positions()
    trend_value = (along_x + along_y + along_z) / 3.0
    identity = [1.0, 0.0, 0.0, 1.0, 0.0, 1.0]
    pieces = [0.75 + 0.25 * rough_part[0]]
    pieces = pieces + [identity[s] + 0.12 * rough_part[1 + s] for s in range(6)]
    pieces = pieces + [(0.3 + 0.6 * trend_value) * (0.85 + 0.15 * rough_part[7])]
    pieces = pieces + [0.1 * rough_part[8 + i] for i in range(3)]
    pieces = pieces + [0.2 * rough_part[11]]
    pieces = pieces + [0.1 * rough_part[12 + s] for s in range(6)]
    pieces = pieces + [0.1 * rough_part[18 + i] for i in range(3)]
    pieces = pieces + [0.05 * rough_part[21]]
    return jnp.stack(pieces)


def draw_spacetime(key, part):
    return spacetime_fields(key)


def draw_fluid(key, part):
    conformal = spacetime_fields(key)[0]
    keys_all = jax.random.split(jax.random.fold_in(key, 23), 4)
    shape_one = (NX, NY, NZ)
    rest_mass = jnp.exp(jax.random.uniform(keys_all[0], shape_one, jnp.float32, math.log(0.2), 0.0))
    pressure = rest_mass * jnp.exp(jax.random.uniform(keys_all[1], shape_one, jnp.float32, math.log(0.0005), math.log(0.4)))
    four_vel = jax.random.uniform(keys_all[2], (3,) + shape_one, jnp.float32, -0.5, 0.5)
    potential = jax.random.uniform(keys_all[3], (3,) + shape_one, jnp.float32, -0.15, 0.15)
    face_fields = []
    for d in range(3):
        e = (d + 1) % 3
        f = (d + 2) % 3
        face_fields.append(jnp.roll(potential[f], -1, axis=e) - potential[f] - jnp.roll(potential[e], -1, axis=f) + potential[e])
    volume = 1.0 / (conformal * jnp.sqrt(conformal))
    magnetic = [0.5 * (face_fields[d] + jnp.roll(face_fields[d], -1, axis=d)) / volume for d in range(3)]
    lorentz = jnp.sqrt(1.0 + four_vel[0] * four_vel[0] + four_vel[1] * four_vel[1] + four_vel[2] * four_vel[2])
    velocity = [four_vel[i] / lorentz for i in range(3)]
    along_b = velocity[0] * magnetic[0] + velocity[1] * magnetic[1] + velocity[2] * magnetic[2]
    time_b = lorentz * along_b
    space_b = [magnetic[i] / lorentz + time_b * velocity[i] for i in range(3)]
    b_square = (magnetic[0] * magnetic[0] + magnetic[1] * magnetic[1] + magnetic[2] * magnetic[2]) / (lorentz * lorentz) + along_b * along_b
    inertia = rest_mass + 2.0 * pressure + b_square
    total_pressure = pressure + 0.5 * b_square
    density = rest_mass * lorentz
    lorentz_sq = lorentz * lorentz
    momenta = [inertia * lorentz_sq * velocity[j] - time_b * space_b[j] for j in range(3)]
    energy = inertia * lorentz_sq - total_pressure - time_b * time_b - density
    return jnp.stack([volume * density] + [volume * member for member in momenta] + [volume * energy] + face_fields)


def setup_inputs(seed: int = 0) -> dict:
    seeds = jax.random.split(jax.random.key(seed), 3)
    spacetime = draw_spacetime(jax.random.fold_in(seeds[2], 71), 0)
    fluid = draw_fluid(jax.random.fold_in(seeds[2], 71), 0)
    return {"spacetime": spacetime, "fluid": fluid}


INDEX_PAIRS = ((0, 0), (0, 1), (0, 2), (1, 1), (1, 2), (2, 2))
FIRST_WEIGHTS = ((-2, 1.0 / 12.0), (-1, -8.0 / 12.0), (1, 8.0 / 12.0), (2, -1.0 / 12.0))
SECOND_WEIGHTS = ((-2, -1.0 / 12.0), (-1, 16.0 / 12.0), (0, -30.0 / 12.0), (1, 16.0 / 12.0), (2, -1.0 / 12.0))
KREISS_WEIGHTS = ((-3, 1.0 / 64.0), (-2, -6.0 / 64.0), (-1, 15.0 / 64.0), (0, -20.0 / 64.0), (1, 15.0 / 64.0), (2, -6.0 / 64.0), (3, 1.0 / 64.0))
COURANT = 0.25
DISSIPATION = 0.2
KAPPA_ONE = 0.02
SHIFT_DAMPING = 1.0
SPEED_CAP = 0.99
PRESSURE_FLOOR = 0.01
FOUR_PI = 4.0 * math.pi

def add_all(pieces):
    summed = pieces[0]
    for member in pieces[1:]:
        summed = summed + member
    return summed

def inner_three(first_vec, second_vec):
    return add_all([first_vec[i] * second_vec[i] for i in range(3)])

def pair_slot(i, j):
    return INDEX_PAIRS.index((min(i, j), max(i, j)))

def symmetric(stack, offset):
    return [[stack[offset + pair_slot(i, j)] for j in range(3)] for i in range(3)]

def full_matrix(table):
    return [[table[min(i, j), max(i, j)] for j in range(3)] for i in range(3)]

def others(direction):
    return [b for b in range(3) if b != direction]

def window(values, direction, low_cut, high_cut):
    position = values.ndim - 3 + direction
    return lax.slice_in_dim(values, low_cut, values.shape[position] - high_cut, axis=position)

def interior(values, directions):
    for direction in directions:
        values = window(values, direction, GHOST, GHOST)
    return values

def stencil(values, direction, weights):
    summed = None
    for offset, weight in weights:
        term_value = weight * window(values, direction, GHOST + offset, GHOST - offset)
        summed = term_value if summed is None else summed + term_value
    return summed

def first_derivs(padded):
    return [stencil(interior(padded, others(a)), a, FIRST_WEIGHTS) for a in range(3)]

def second_derivs(padded):
    result = {}
    for a in range(3):
        for b in range(a, 3):
            if a == b:
                result[a, b] = stencil(interior(padded, others(a)), a, SECOND_WEIGHTS)
            else:
                remaining = [c for c in range(3) if c != a and c != b]
                result[a, b] = stencil(stencil(interior(padded, remaining), a, FIRST_WEIGHTS), b, FIRST_WEIGHTS)
    return result

def dissipation(padded):
    summed = stencil(interior(padded, others(0)), 0, KREISS_WEIGHTS)
    for a in (1, 2):
        summed = summed + stencil(interior(padded, others(a)), a, KREISS_WEIGHTS)
    return DISSIPATION * summed

def inverse_metric(metric):
    cofactor = {}
    cofactor[0, 0] = metric[1][1] * metric[2][2] - metric[1][2] * metric[1][2]
    cofactor[0, 1] = metric[0][2] * metric[1][2] - metric[0][1] * metric[2][2]
    cofactor[0, 2] = metric[0][1] * metric[1][2] - metric[0][2] * metric[1][1]
    cofactor[1, 1] = metric[0][0] * metric[2][2] - metric[0][2] * metric[0][2]
    cofactor[1, 2] = metric[0][1] * metric[0][2] - metric[0][0] * metric[1][2]
    cofactor[2, 2] = metric[0][0] * metric[1][1] - metric[0][1] * metric[0][1]
    determinant = metric[0][0] * cofactor[0, 0] + metric[0][1] * cofactor[0, 1] + metric[0][2] * cofactor[0, 2]
    return full_matrix({pair: cofactor[pair] / determinant for pair in INDEX_PAIRS})

def wave_speed(current):
    inverse = inverse_metric(symmetric(current, 1))
    speeds = [jnp.abs(current[8 + d]) + jnp.sqrt(2.0 * current[7] * current[0] * inverse[d][d]) for d in range(3)]
    return jnp.maximum(jnp.maximum(speeds[0], speeds[1]), speeds[2])

def stress_parts(rest_mass, pressure, four_vel, magnetic):
    lorentz = jnp.sqrt(1.0 + inner_three(four_vel, four_vel))
    velocity = [four_vel[i] / lorentz for i in range(3)]
    along_b = inner_three(velocity, magnetic)
    time_b = lorentz * along_b
    space_b = [magnetic[i] / lorentz + time_b * velocity[i] for i in range(3)]
    b_square = inner_three(magnetic, magnetic) / (lorentz * lorentz) + along_b * along_b
    enthalpy = rest_mass + 2.0 * pressure
    inertia = enthalpy + b_square
    total_pressure = pressure + 0.5 * b_square
    return (lorentz, velocity, time_b, space_b, b_square, enthalpy, inertia, total_pressure)

def face_state(rest_mass, pressure, four_vel, magnetic, d):
    lorentz, velocity, time_b, space_b, b_square, enthalpy, inertia, total_pressure = stress_parts(rest_mass, pressure, four_vel, magnetic)
    lorentz_sq = lorentz * lorentz
    density = rest_mass * lorentz
    conserved = [density] + [inertia * lorentz_sq * velocity[j] - time_b * space_b[j] for j in range(3)]
    conserved = conserved + [inertia * lorentz_sq - total_pressure - time_b * time_b - density]
    flux_list = [density * velocity[d]]
    for j in range(3):
        flux_j = inertia * lorentz_sq * velocity[d] * velocity[j] - space_b[d] * space_b[j]
        if j == d:
            flux_j = flux_j + total_pressure
        flux_list.append(flux_j)
    flux_list.append(inertia * lorentz_sq * velocity[d] - time_b * space_b[d] - density * velocity[d])
    speed_sq = inner_three(velocity, velocity)
    sound_sq = 2.0 * pressure / enthalpy
    alfven_sq = b_square / inertia
    fast_sq = sound_sq + alfven_sq - sound_sq * alfven_sq
    spread = jnp.sqrt(fast_sq * (1.0 - speed_sq) * (1.0 - speed_sq * fast_sq - velocity[d] * velocity[d] * (1.0 - fast_sq)))
    middle = velocity[d] * (1.0 - fast_sq)
    fastest = jnp.maximum(jnp.abs(middle + spread), jnp.abs(middle - spread)) / (1.0 - speed_sq * fast_sq)
    return (conserved, flux_list, fastest)

def recover(conserved, magnetic):
    density = conserved[0]
    momenta = [conserved[1 + i] for i in range(3)]
    energy = conserved[4] + density
    mom_sq = inner_three(momenta, momenta)
    mag_sq = inner_three(magnetic, magnetic)
    cross = inner_three(momenta, magnetic)
    cross_sq = cross * cross

    def recovered_state(guess_z):
        speed_sq = (mom_sq * guess_z * guess_z + cross_sq * (2.0 * guess_z + mag_sq)) / (guess_z * guess_z * (guess_z + mag_sq) * (guess_z + mag_sq))
        inv_lorentz_sq = 1.0 - jnp.minimum(speed_sq, SPEED_CAP)
        rest_mass = density * jnp.sqrt(inv_lorentz_sq)
        pressure = 0.5 * (guess_z * inv_lorentz_sq - rest_mass)
        return (inv_lorentz_sq, rest_mass, pressure)
    guess_z = jnp.maximum(energy - 0.5 * mag_sq, density)
    for attempt in range(RECOVERY_STEPS):
        inv_lorentz_sq, rest_mass, pressure = recovered_state(guess_z)
        residual = guess_z + mag_sq - pressure - 0.5 * mag_sq * inv_lorentz_sq - 0.5 * cross_sq / (guess_z * guess_z) - energy
        guess_z = jnp.maximum(guess_z - residual / (1.0 - 0.5 * inv_lorentz_sq), density)
    inv_lorentz_sq, rest_mass, pressure = recovered_state(guess_z)
    pressure = jnp.maximum(pressure, PRESSURE_FLOOR * rest_mass)
    lorentz = 1.0 / jnp.sqrt(inv_lorentz_sq)
    four_vel = [lorentz * (momenta[i] + cross * magnetic[i] / guess_z) / (guess_z + mag_sq) for i in range(3)]
    return (rest_mass, pressure, four_vel)

def limited(low_side, high_side):
    return 0.5 * (jnp.sign(low_side) + jnp.sign(high_side)) * jnp.minimum(jnp.abs(low_side), jnp.abs(high_side))

def corner_box(values):
    for direction in range(3):
        values = window(values, direction, 0, 1)
    return values

def owned_box(values):
    for direction in range(3):
        values = window(values, direction, GHOST, GHOST - 1)
    return values

def edge_cells(values):
    for direction in range(3):
        values = window(values, direction, GHOST - 1, 1)
    return values

def face_average(values, d):
    paired = window(values, d, GHOST - 1, GHOST - 1)
    return interior(0.5 * (window(paired, d, 0, 1) + window(paired, d, 1, 0)), others(d))

def edge_average(values, d):
    values = window(values, d, 1, 1)
    for e in others(d):
        values = 0.5 * (window(values, e, 0, 1) + window(values, e, 1, 0))
    return values

def edge_difference(edge_vals, d, e):
    edge_vals = window(edge_vals, d, 0, 1)
    return window(edge_vals, e, 1, 0) - window(edge_vals, e, 0, 1)

def fluid_rates(padded_st, padded_fl, current, gradient):
    chi_box = corner_box(padded_st[0])
    volume_box = 1.0 / (chi_box * jnp.sqrt(chi_box))
    centred = []
    for d in range(3):
        averaged = 0.5 * (window(padded_fl[5 + d], d, 0, 1) + window(padded_fl[5 + d], d, 1, 0))
        for e in others(d):
            averaged = window(averaged, e, 0, 1)
        centred.append(averaged)
    magnetic_box = [centred[d] / volume_box for d in range(3)]
    conserved_box = corner_box(padded_fl[:5]) / volume_box
    rest_mass, pressure, four_vel = recover(conserved_box, magnetic_box)
    primitives = jnp.stack([rest_mass, pressure] + four_vel + magnetic_box)
    hydro_rate = [0.0] * 5
    for d in range(3):
        line_prims = window(primitives, d, 1, 0)
        for e in others(d):
            line_prims = window(line_prims, e, GHOST, GHOST - 1)
        low_diff = window(line_prims, d, 1, 1) - window(line_prims, d, 0, 2)
        high_diff = window(line_prims, d, 2, 0) - window(line_prims, d, 1, 1)
        slopes = limited(low_diff, high_diff)
        centre = window(line_prims, d, 1, 1)
        left_state = window(centre, d, 0, 1) + 0.5 * window(slopes, d, 0, 1)
        right_state = window(centre, d, 1, 0) - 0.5 * window(slopes, d, 1, 0)
        lapse_face = face_average(padded_st[7], d)
        chi_face = face_average(padded_st[0], d)
        volume_face = 1.0 / (chi_face * jnp.sqrt(chi_face))
        normal = interior(window(padded_fl[5 + d], d, GHOST, GHOST - 1), others(d)) / volume_face
        fluxes = []
        for one_side in (left_state, right_state):
            magnetic = [one_side[5 + i] for i in range(3)]
            magnetic[d] = normal
            fluxes.append(face_state(one_side[0], one_side[1], [one_side[2], one_side[3], one_side[4]], magnetic, d))
        cons_left, flux_left, fast_left = fluxes[0]
        cons_right, flux_right, fast_right = fluxes[1]
        signal = jnp.maximum(fast_left, fast_right)
        weight = lapse_face * volume_face
        for q in range(5):
            face_flux = weight * (0.5 * (flux_left[q] + flux_right[q]) - 0.5 * signal * (cons_right[q] - cons_left[q]))
            hydro_rate[q] = hydro_rate[q] - (window(face_flux, d, 1, 0) - window(face_flux, d, 0, 1))
    owned_prims = owned_box(primitives)
    lorentz, velocity, time_b, space_b, b_square, enthalpy, inertia, total_pressure = stress_parts(owned_prims[0], owned_prims[1], [owned_prims[2], owned_prims[3], owned_prims[4]], [owned_prims[5], owned_prims[6], owned_prims[7]])
    lorentz_sq = lorentz * lorentz
    stress_pairs = {}
    for i, j in INDEX_PAIRS:
        stress_ij = inertia * lorentz_sq * velocity[i] * velocity[j] - space_b[i] * space_b[j]
        if i == j:
            stress_ij = stress_ij + total_pressure
        stress_pairs[i, j] = stress_ij
    stress = full_matrix(stress_pairs)
    held = interior(padded_fl[:5], (0, 1, 2))
    conformal = current[0]
    volume = 1.0 / (conformal * jnp.sqrt(conformal))
    lapse_now = current[7]
    lapse_grad = [gradient[k][7] for k in range(3)]
    trace_total = current[11] + 2.0 * current[21]
    metric = symmetric(current, 1)
    traceless = symmetric(current, 12)
    curv_phys = full_matrix({pair: (traceless[pair[0]][pair[1]] + metric[pair[0]][pair[1]] * trace_total / 3.0) / conformal for pair in INDEX_PAIRS})
    total_energy = held[4] + held[0]
    for i in range(3):
        hydro_rate[1 + i] = hydro_rate[1 + i] - total_energy * lapse_grad[i] + add_all([held[1 + k] * gradient[i][8 + k] for k in range(3)])
    hydro_rate[4] = hydro_rate[4] + lapse_now * volume * add_all([stress[i][j] * curv_phys[i][j] for i in range(3) for j in range(3)]) - add_all([held[1 + j] * lapse_grad[j] for j in range(3)])
    matter = {'energy': total_energy / volume, 'momentum': [held[1 + i] / volume for i in range(3)], 'stress': stress}
    four_edge = [edge_cells(four_vel[i]) for i in range(3)]
    lorentz_edge = jnp.sqrt(1.0 + inner_three(four_edge, four_edge))
    vel_edge = [four_edge[i] / lorentz_edge for i in range(3)]
    mag_edge = [edge_cells(centred[i]) for i in range(3)]
    lapse_cells = padded_st[7]
    for direction in range(3):
        lapse_cells = window(lapse_cells, direction, GHOST - 1, GHOST - 1)
    electric = [-lapse_cells * (vel_edge[(i + 1) % 3] * mag_edge[(i + 2) % 3] - vel_edge[(i + 2) % 3] * mag_edge[(i + 1) % 3]) for i in range(3)]
    edge_vals = [edge_average(electric[i], i) for i in range(3)]
    field_rate = []
    for d in range(3):
        e = (d + 1) % 3
        f = (d + 2) % 3
        field_rate.append(-(edge_difference(edge_vals[f], d, e) - edge_difference(edge_vals[e], d, f)))
    return (hydro_rate, field_rate, matter)

def z4c_rates(padded_st, current, gradient, matter):
    curvature = second_derivs(padded_st[:11])

    def hessian(field, a, b):
        return curvature[min(a, b), max(a, b)][field]
    conformal = current[0]
    metric = symmetric(current, 1)
    lapse_now = current[7]
    shift_vec = [current[8 + i] for i in range(3)]
    extrinsic = current[11]
    traceless = symmetric(current, 12)
    connection = [current[18 + i] for i in range(3)]
    z_theta = current[21]
    inverse = inverse_metric(metric)
    metric_grad = [[[gradient[k][1 + pair_slot(i, j)] for j in range(3)] for i in range(3)] for k in range(3)]
    lowered = [[[0.5 * (metric_grad[j][i][k] + metric_grad[k][i][j] - metric_grad[i][j][k]) for k in range(3)] for j in range(3)] for i in range(3)]
    raised = [[[add_all([inverse[i][l] * lowered[l][j][k] for l in range(3)]) for k in range(3)] for j in range(3)] for i in range(3)]
    contracted = [add_all([inverse[j][k] * raised[i][j][k] for j in range(3) for k in range(3)]) for i in range(3)]
    chi_grad = [gradient[k][0] for k in range(3)]
    lapse_grad = [gradient[k][7] for k in range(3)]
    chi_cov = full_matrix({pair: hessian(0, pair[0], pair[1]) - add_all([raised[k][pair[0]][pair[1]] * chi_grad[k] for k in range(3)]) for pair in INDEX_PAIRS})
    chi_lap = add_all([inverse[i][j] * chi_cov[i][j] for i in range(3) for j in range(3)])
    chi_square = add_all([inverse[i][j] * chi_grad[i] * chi_grad[j] for i in range(3) for j in range(3)])
    cross_term = add_all([inverse[i][j] * chi_grad[i] * lapse_grad[j] for i in range(3) for j in range(3)])
    lapse_cov = full_matrix({pair: hessian(7, pair[0], pair[1]) - add_all([raised[k][pair[0]][pair[1]] * lapse_grad[k] for k in range(3)]) + (chi_grad[pair[0]] * lapse_grad[pair[1]] + chi_grad[pair[1]] * lapse_grad[pair[0]] - metric[pair[0]][pair[1]] * cross_term) / (2.0 * conformal) for pair in INDEX_PAIRS})
    lapse_lap = conformal * add_all([inverse[i][j] * lapse_cov[i][j] for i in range(3) for j in range(3)])
    ricci_pairs = {}
    for i, j in INDEX_PAIRS:
        slot_index = 1 + pair_slot(i, j)
        second_part = -0.5 * add_all([inverse[l][m] * hessian(slot_index, l, m) for l in range(3) for m in range(3)])
        connection_part = 0.5 * add_all([metric[k][i] * gradient[j][18 + k] + metric[k][j] * gradient[i][18 + k] for k in range(3)])
        contracted_part = 0.5 * add_all([contracted[k] * (lowered[i][j][k] + lowered[j][i][k]) for k in range(3)])
        quadratic = add_all([inverse[l][m] * (raised[k][l][i] * lowered[j][k][m] + raised[k][l][j] * lowered[i][k][m] + raised[k][i][m] * lowered[k][l][j]) for l in range(3) for m in range(3) for k in range(3)])
        conformal_part = (chi_cov[i][j] + metric[i][j] * chi_lap) / (2.0 * conformal) - (chi_grad[i] * chi_grad[j] + 3.0 * metric[i][j] * chi_square) / (4.0 * conformal * conformal)
        ricci_pairs[i, j] = second_part + connection_part + contracted_part + quadratic + conformal_part
    ricci_ten = full_matrix(ricci_pairs)
    ricci_scalar = conformal * add_all([inverse[i][j] * ricci_ten[i][j] for i in range(3) for j in range(3)])
    stress = matter['stress']
    density_adm = matter['energy']
    momentum = matter['momentum']
    stress_trace = conformal * add_all([inverse[i][j] * stress[i][j] for i in range(3) for j in range(3)])
    raised_a = full_matrix({pair: add_all([inverse[pair[0]][k] * inverse[pair[1]][l] * traceless[k][l] for k in range(3) for l in range(3)]) for pair in INDEX_PAIRS})
    a_square = add_all([traceless[i][j] * raised_a[i][j] for i in range(3) for j in range(3)])
    shift_grad = [[gradient[k][8 + i] for i in range(3)] for k in range(3)]
    shift_div = add_all([shift_grad[k][k] for k in range(3)])
    trace_total = extrinsic + 2.0 * z_theta

    def advect(field):
        return add_all([shift_vec[k] * gradient[k][field] for k in range(3)])
    rate_list = [None] * current.shape[0]
    rate_list[0] = advect(0) + 2.0 / 3.0 * conformal * (lapse_now * trace_total - shift_div)
    rate_list[7] = advect(7) - 2.0 * lapse_now * extrinsic
    for i in range(3):
        rate_list[8 + i] = advect(8 + i) + 0.75 * connection[i] - SHIFT_DAMPING * shift_vec[i]
    rate_list[11] = advect(11) - lapse_lap + lapse_now * (a_square + trace_total * trace_total / 3.0) + FOUR_PI * lapse_now * (stress_trace + density_adm) + KAPPA_ONE * lapse_now * z_theta
    source = [[-lapse_cov[i][j] + lapse_now * (ricci_ten[i][j] - 2.0 * FOUR_PI * stress[i][j]) for j in range(3)] for i in range(3)]
    source_trace = add_all([inverse[i][j] * source[i][j] for i in range(3) for j in range(3)])
    for i, j in INDEX_PAIRS:
        slot_index = pair_slot(i, j)
        rate_list[1 + slot_index] = advect(1 + slot_index) + add_all([metric[i][k] * shift_grad[j][k] + metric[j][k] * shift_grad[i][k] for k in range(3)]) - 2.0 / 3.0 * metric[i][j] * shift_div - 2.0 * lapse_now * traceless[i][j]
        product = add_all([traceless[i][k] * inverse[k][l] * traceless[l][j] for k in range(3) for l in range(3)])
        rate_list[12 + slot_index] = advect(12 + slot_index) + add_all([traceless[i][k] * shift_grad[j][k] + traceless[j][k] * shift_grad[i][k] for k in range(3)]) - 2.0 / 3.0 * traceless[i][j] * shift_div + conformal * (source[i][j] - metric[i][j] * source_trace / 3.0) + lapse_now * (trace_total * traceless[i][j] - 2.0 * product)
    for i in range(3):
        bracket = add_all([raised[i][j][k] * raised_a[j][k] for j in range(3) for k in range(3)])
        bracket = bracket - 1.5 * add_all([raised_a[i][j] * chi_grad[j] for j in range(3)]) / conformal
        bracket = bracket - add_all([inverse[i][j] * (2.0 * gradient[j][11] + gradient[j][21]) for j in range(3)]) / 3.0
        bracket = bracket - 2.0 * FOUR_PI * add_all([inverse[i][j] * momentum[j] for j in range(3)])
        rate_list[18 + i] = advect(18 + i) - add_all([contracted[j] * shift_grad[j][i] for j in range(3)]) + 2.0 / 3.0 * contracted[i] * shift_div + add_all([inverse[j][k] * hessian(8 + i, j, k) for j in range(3) for k in range(3)]) + add_all([inverse[i][j] * hessian(8 + k, j, k) for j in range(3) for k in range(3)]) / 3.0 - 2.0 * add_all([raised_a[i][j] * lapse_grad[j] for j in range(3)]) + 2.0 * lapse_now * bracket - 2.0 * KAPPA_ONE * lapse_now * (connection[i] - contracted[i])
    rate_list[21] = advect(21) + 0.5 * lapse_now * (ricci_scalar - a_square + 2.0 / 3.0 * trace_total * trace_total - 4.0 * FOUR_PI * density_adm) - 2.0 * KAPPA_ONE * lapse_now * z_theta
    return jnp.stack(rate_list) + dissipation(padded_st)

def tendencies(padded_st, padded_fl):
    gradient = first_derivs(padded_st)
    current = interior(padded_st, (0, 1, 2))
    hydro_rate, field_rate, matter = fluid_rates(padded_st, padded_fl, current, gradient)
    spacetime_rate = z4c_rates(padded_st, current, gradient, matter)
    return (spacetime_rate, jnp.stack(hydro_rate + field_rate))

def regroup(rates, count):
    rates = rates.reshape((N_GX, N_GY, count, CX, CY, rates.shape[-1]))
    rates = jnp.transpose(rates, (2, 0, 3, 1, 4, 5))
    return rates.reshape((count, N_GX * CX, N_GY * CY, rates.shape[-1]))

def reference(spacetime, fluid):
    timestep = COURANT / jnp.max(wave_speed(spacetime))
    widths = ((0, 0), (GHOST, GHOST), (GHOST, GHOST), (GHOST, GHOST))
    padded_st = jnp.pad(spacetime, widths, mode='wrap')
    padded_fl = jnp.pad(fluid, widths, mode='wrap')

    def block_rates(block_index):
        offset_x = block_index // N_GY * CX
        offset_y = block_index % N_GY * CY
        block_st = lax.dynamic_slice_in_dim(padded_st, offset_x, CX + 2 * GHOST, axis=1)
        block_st = lax.dynamic_slice_in_dim(block_st, offset_y, CY + 2 * GHOST, axis=2)
        block_fl = lax.dynamic_slice_in_dim(padded_fl, offset_x, CX + 2 * GHOST, axis=1)
        block_fl = lax.dynamic_slice_in_dim(block_fl, offset_y, CY + 2 * GHOST, axis=2)
        return tendencies(block_st, block_fl)
    spacetime_rate, fluid_rate = lax.map(block_rates, jnp.arange(N_GX * N_GY, dtype=jnp.int32))
    spacetime_rate = regroup(spacetime_rate, spacetime.shape[0])
    fluid_rate = regroup(fluid_rate, fluid.shape[0])
    return (spacetime + timestep * spacetime_rate, fluid + timestep * fluid_rate)
```

```python
import functools
import math

import jax
import jax.numpy as jnp
from jax import lax
from jax.experimental import pallas as pl
from jax.experimental.pallas import tpu as pltpu
from jax.sharding import PartitionSpec as P

RECOVERY_STEPS = 4
INDEX_PAIRS = ((0, 0), (0, 1), (0, 2), (1, 1), (1, 2), (2, 2))
COURANT = 0.25
DISSIPATION = 0.2
KAPPA_ONE = 0.02
SHIFT_DAMPING = 1.0
SPEED_CAP = 0.99
PRESSURE_FLOOR = 0.01
FOUR_PI = 4.0 * math.pi

CURVED = 11
FLUID = 8


def total(pieces):
    summed = pieces[0]
    for member in pieces[1:]:
        summed = summed + member
    return summed


def dot(first_vec, second_vec):
    return total([first_vec[i] * second_vec[i] for i in range(3)])


def slot_of(i, j):
    return INDEX_PAIRS.index((min(i, j), max(i, j)))


def symmetric(entries):
    return [[entries[slot_of(i, j)] for j in range(3)] for i in range(3)]


def trace_with(inverse, tensor):
    return (
        inverse[0][0] * tensor[0][0]
        + inverse[1][1] * tensor[1][1]
        + inverse[2][2] * tensor[2][2]
        + 2.0
        * (
            inverse[0][1] * tensor[0][1]
            + inverse[0][2] * tensor[0][2]
            + inverse[1][2] * tensor[1][2]
        )
    )


def inverse_metric(metric):
    cofactor = [
        metric[1][1] * metric[2][2] - metric[1][2] * metric[1][2],
        metric[0][2] * metric[1][2] - metric[0][1] * metric[2][2],
        metric[0][1] * metric[1][2] - metric[0][2] * metric[1][1],
        metric[0][0] * metric[2][2] - metric[0][2] * metric[0][2],
        metric[0][1] * metric[0][2] - metric[0][0] * metric[1][2],
        metric[0][0] * metric[1][1] - metric[0][1] * metric[0][1],
    ]
    determinant = (
        metric[0][0] * cofactor[0] + metric[0][1] * cofactor[1] + metric[0][2] * cofactor[2]
    )
    over = 1.0 / determinant
    return symmetric([c * over for c in cofactor])


class Tile:
    def __init__(self, cy, cz):
        self.cy, self.rows, self.lanes = cy, 2 * cy, cz
        shape = (self.rows, cz)
        self.row = lax.broadcasted_iota(jnp.int32, shape, 0)
        self.lane = lax.broadcasted_iota(jnp.int32, shape, 1)
        self.slot = lax.rem(self.row, cy)

    def turn(self, tile, amount):
        amount = amount % self.rows
        return tile if amount == 0 else pltpu.roll(tile, amount, 0)

    def spin(self, tile, amount):
        amount = amount % self.lanes
        return tile if amount == 0 else pltpu.roll(tile, amount, 1)

    def swap(self, tile):
        return self.turn(tile, self.cy)

    def odd(self, a, b):
        return self.turn(jnp.where(self.row < self.cy, b, a), self.cy)

    def odd_swapped(self, a, b):
        return self.turn(jnp.where(self.row < self.cy, a, b), self.cy)

    def y_up(self, main, beyond, k):
        return self.turn(jnp.where(self.slot < k, beyond, main), -k)

    def y_down(self, main, beyond, k):
        return self.turn(jnp.where(self.slot >= self.cy - k, beyond, main), k)

    def z_up(self, main, beyond, k):
        return self.spin(jnp.where(self.lane < k, beyond, main), -k)

    def z_down(self, main, beyond, k):
        return self.spin(jnp.where(self.lane >= self.lanes - k, beyond, main), k)

    def join_low(self, u, v):
        return jnp.where(self.slot < 2, self.swap(u), self.turn(v, 2))

    def join_high(self, u, v):
        return jnp.where(self.slot >= self.cy - 2, self.swap(u), self.turn(self.swap(v), -2))

    def part_first(self, from_above, from_below):
        return jnp.where(self.slot < 2, from_above, from_below)

    def part_second(self, from_above, from_below):
        return self.turn(jnp.where(self.slot < 2, from_below, from_above), 2)


def third_list(fields):
    return list(range(fields + 1))


def pairs_of(items):
    return [(items[i], items[min(i + 1, len(items) - 1)]) for i in range(0, len(items), 2)]


def pack_kernel(st, fl, zst, zfl, *outs):
    fields, rows, lanes = st.shape
    cy = rows // 4
    t = Tile(cy, lanes)
    low, high = 0, 1
    x_low, x_high, y_low, y_high, c_ll, c_lh, c_hl, c_hh = outs
    half = t.rows

    def own(ref, q):
        return [ref[q, 0:half, :], ref[q, half : 2 * half, :]]

    tiles, beyond = [], []
    for q in range(fields):
        tiles.append(own(st, q))
        beyond.append(own(zst, q) if q < CURVED else None)
    for q in range(FLUID - 1):
        tiles.append(own(fl, q))
        beyond.append(own(zfl, q))
    along, along_z = own(fl, FLUID - 1), own(zfl, FLUID - 1)
    tiles.append([0.5 * (along[p] + t.z_up(along[p], along_z[p], 1)) for p in range(2)])
    beyond.append([0.5 * (along_z[p] + t.z_up(along_z[p], along[p], 1)) for p in range(2)])

    packed = [None] * 4
    place = 0
    for q, (first, second) in enumerate(tiles):
        x_low[q] = first
        x_high[q] = second
        y_low[q] = t.join_low(first, second)
        y_high[q] = t.join_high(first, second)
        if beyond[q] is not None:
            zf, zs = beyond[q]
            for m, piece in enumerate((zf, zs, t.join_low(zf, zs), t.join_high(zf, zs))):
                piece = t.spin(piece, 4 * place + 2)
                packed[m] = (
                    piece if place == 0 else jnp.where(t.lane < 4 * place, packed[m], piece)
                )
            place += 1
    for n, (a, b) in enumerate(pairs_of(third_list(fields))):
        slot = fields + FLUID + n
        xa, xb = (tiles[q if q < fields else fields + 5] for q in (a, b))
        x_low[slot] = jnp.where(t.row < cy, xa[1], t.swap(xb[1]))
        x_high[slot] = jnp.where(t.row < cy, t.swap(xb[0]), xa[0])
        ya, yb = (tiles[q if q < fields else fields + 6] for q in (a, b))
        w = [t.swap(ya[0]), t.swap(ya[1]), t.swap(yb[0]), t.swap(yb[1])]
        s = t.slot
        y_low[slot] = jnp.where(
            s == 2,
            w[0],
            jnp.where(s == 3, t.turn(w[1], 1), jnp.where(s == 0, t.turn(w[2], -2), t.turn(w[3], -1))),
        )
        y_high[slot] = jnp.where(
            s == 1,
            w[0],
            jnp.where(s == 0, t.turn(w[1], -1), jnp.where(s == 3, t.turn(w[2], 2), t.turn(w[3], 1))),
        )
    last = x_low.shape[0] - 1
    for out, piece in zip((x_low, x_high, y_low, y_high), packed):
        out[last] = piece
    edge = list(range(CURVED)) + list(range(fields, fields + FLUID))
    for side, (to_low, to_high) in enumerate(((c_ll, c_lh), (c_hl, c_hh))):
        for n, (a, b) in enumerate(pairs_of(edge)):
            to_low[n] = t.join_low(tiles[a][side], tiles[b][side])
            to_high[n] = t.join_high(tiles[a][side], tiles[b][side])
        end = to_low.shape[0] - 1
        za, zb = beyond[fields + 5][side], beyond[fields + 6][side]
        to_low[end] = t.join_low(za, zb)
        to_high[end] = t.join_high(za, zb)


def speed_kernel(st, out):
    def entry(q):
        return st[q]

    inverse = inverse_metric(symmetric([entry(1 + s) for s in range(6)]))
    scale = 2.0 * entry(7) * entry(0)
    speeds = [jnp.abs(entry(8 + d)) + jnp.sqrt(scale * inverse[d][d]) for d in range(3)]
    top = jnp.maximum(jnp.maximum(speeds[0], speeds[1]), speeds[2])
    top = jnp.max(jnp.max(top, axis=1, keepdims=True), axis=0, keepdims=True)
    out[...] = jnp.broadcast_to(top, out.shape)


def limited(a, b):
    return jnp.maximum(jnp.minimum(a, b), 0.0) + jnp.minimum(jnp.maximum(a, b), 0.0)


def recover(conserved, magnetic):
    density = conserved[0]
    momenta = conserved[1:4]
    energy = conserved[4] + density
    mom_sq = dot(momenta, momenta)
    mag_sq = dot(magnetic, magnetic)
    cross = dot(momenta, magnetic)
    cross_sq = cross * cross

    def state(z):
        grown = z + mag_sq
        over = 1.0 / (z * grown)
        speed_sq = (mom_sq * z * z + cross_sq * (2.0 * z + mag_sq)) * over * over
        kept = 1.0 - jnp.minimum(speed_sq, SPEED_CAP)
        rest = density * jnp.sqrt(kept)
        return kept, rest, 0.5 * (z * kept - rest), grown * over

    z = jnp.maximum(energy - 0.5 * mag_sq, density)
    for _ in range(RECOVERY_STEPS):
        kept, rest, pressure, over_z = state(z)
        residual = (
            z
            + mag_sq
            - pressure
            - 0.5 * mag_sq * kept
            - 0.5 * cross_sq * over_z * over_z
            - energy
        )
        z = jnp.maximum(z - residual / (1.0 - 0.5 * kept), density)
    kept, rest, pressure, over_z = state(z)
    pressure = jnp.maximum(pressure, PRESSURE_FLOOR * rest)
    scale = lax.rsqrt(kept) / (z + mag_sq)
    along = cross * over_z
    four_vel = [scale * (momenta[i] + along * magnetic[i]) for i in range(3)]
    return [rest, pressure] + four_vel


def stress_parts(rest, pressure, u, magnetic):
    lorentz_sq = 1.0 + dot(u, u)
    over = lax.rsqrt(lorentz_sq)
    over_sq = over * over
    time_b = dot(u, magnetic)
    grown_b = [magnetic[i] + time_b * u[i] for i in range(3)]
    b_square = (dot(magnetic, magnetic) + time_b * time_b) * over_sq
    enthalpy = rest + 2.0 * pressure
    inertia = enthalpy + b_square
    return lorentz_sq, over, over_sq, time_b, grown_b, b_square, enthalpy, inertia


def face_state(rest, pressure, u, magnetic, d):
    lorentz_sq, over, over_sq, time_b, grown_b, b_square, enthalpy, inertia = stress_parts(
        rest, pressure, u, magnetic
    )
    total_pressure = pressure + 0.5 * b_square
    lorentz = lorentz_sq * over
    density = rest * lorentz
    carried = inertia * lorentz
    time_over = time_b * over
    conserved = [density]
    conserved += [carried * u[j] - time_over * grown_b[j] for j in range(3)]
    conserved += [inertia * lorentz_sq - total_pressure - time_b * time_b - density]
    mass_flux = rest * u[d]
    flux = [mass_flux]
    pushed = inertia * u[d]
    b_over = grown_b[d] * over_sq
    for j in range(3):
        flux_j = pushed * u[j] - b_over * grown_b[j]
        flux.append(flux_j + total_pressure if j == d else flux_j)
    flux.append(carried * u[d] - time_over * grown_b[d] - mass_flux)
    ratio = 1.0 / (enthalpy * inertia)
    sound_sq = 2.0 * pressure * inertia * ratio
    alfven_sq = b_square * enthalpy * ratio
    fast_sq = sound_sq + alfven_sq - sound_sq * alfven_sq
    slow = 1.0 - fast_sq
    velocity = u[d] * over
    rest_part = 1.0 - dot(u, u) * over_sq * fast_sq
    spread = jnp.sqrt(fast_sq * over_sq * (rest_part - velocity * velocity * slow))
    fastest = (jnp.abs(velocity * slow) + spread) / rest_part
    return conserved, flux, fastest


def face_flux(left, right, normal, weight, d):
    sides = []
    for state in (left, right):
        magnetic = [normal if i == d else state[5 + i] for i in range(3)]
        sides.append(face_state(state[0], state[1], state[2:5], magnetic, d))
    (cons_l, flux_l, fast_l), (cons_r, flux_r, fast_r) = sides
    signal = jnp.maximum(fast_l, fast_r)
    scale = 0.5 * weight
    return [scale * (flux_l[q] + flux_r[q] - signal * (cons_r[q] - cons_l[q])) for q in range(5)]


def volume_over(conformal):
    return conformal * jnp.sqrt(conformal)


def first_diff(down_two, down, up, up_two):
    return (8.0 / 12.0) * (up - down) + (1.0 / 12.0) * (down_two - up_two)


def main_kernel(
    st, fl, zst, zfl, x_below, x_above, y_below, y_above, c_bb, c_ba, c_ab, c_aa, tops,
    st_out, fl_out, pairs, sides, thirds, pairs_z, sides_z, grads, seconds, damped, tensors,
):
    fields, rows, lanes = st.shape
    cy = rows // 4
    t = Tile(cy, lanes)
    half = t.rows
    own = rows // half

    def third_place(q):
        return fields + FLUID + q // 2, q % 2

    def beside(q, p):
        if p == 1:
            return t.part_first(y_above[q], y_below[q])
        return t.part_second(y_above[q], y_below[q])

    edge = list(range(CURVED)) + list(range(fields, fields + FLUID))

    def corner(q, p):
        place = edge.index(q)
        above, below = ((c_ba, c_bb), (c_aa, c_ab))[0 if p == 0 else 1]
        part = t.part_first if place % 2 == 0 else t.part_second
        return part(above[place // 2], below[place // 2])

    def x_third(q, upper):
        tile, which = third_place(q)
        found = x_above[tile] if upper else x_below[tile]
        return t.swap(found) if which else found

    def y_third(q, p):
        tile, which = third_place(q)
        above, below = y_above[tile], y_below[tile]
        turn_above, turn_below = ((0, 0), (-1, 1), (2, -2), (1, -1))[2 * which + p - 1]
        return jnp.where(t.slot == 2, t.turn(above, turn_above), t.turn(below, turn_below))

    last = x_below.shape[0] - 1
    z_xb, z_xa = x_below[last], x_above[last]
    z_y = [
        t.part_first(y_above[last], y_below[last]),
        t.part_second(y_above[last], y_below[last]),
    ]

    def z_place(q):
        return 4 * edge.index(q) + 2

    def rows_of(ref, q, p):
        return ref[q, (p - 1) * half : p * half, :]

    for q in range(fields):
        pairs[q, 0] = x_third(q, False)
        pairs[q, 1] = x_below[q]
        for p in range(1, own + 1):
            pairs[q, 1 + p] = rows_of(st, q, p)
            sides[q, p] = beside(q, p)
            thirds[q, p - 1] = y_third(q, p)
        pairs[q, 2 + own] = x_above[q]
        pairs[q, 3 + own] = x_third(q, True)
        if q < CURVED:
            sides[q, 0] = corner(q, 0)
            sides[q, own + 1] = corner(q, own + 1)
            pairs_z[q, 0] = t.spin(z_xb, -z_place(q))
            pairs_z[q, own + 1] = t.spin(z_xa, -z_place(q))
            for p in range(1, own + 1):
                pairs_z[q, p] = rows_of(zst, q, p)
                sides_z[q, p - 1] = t.spin(z_y[p - 1], -z_place(q))

    span = range(own + 2)
    inner = range(1, own + 1)

    def plane(q):
        if q < fields:
            return (
                [pairs[q, 1 + p] for p in span],
                [sides[q, p] for p in span],
                [pairs_z[q, p] for p in span],
                [sides_z[q, p - 1] if 1 <= p <= own else None for p in span],
            )
        f = q - fields
        v = [x_below[q]] + [rows_of(fl, f, p) for p in inner] + [x_above[q]]
        h = [corner(q, 0)] + [beside(q, p) for p in inner] + [corner(q, own + 1)]
        place = z_place(q)
        vz = [t.spin(z_xb, -place)] + [rows_of(zfl, f, p) for p in inner] + [t.spin(z_xa, -place)]
        hz = [None] + [t.spin(z_y[p - 1], -place) for p in inner] + [None]
        return v, h, vz, hz

    end = c_bb.shape[0] - 1

    def corner_z(p, which):
        above, below = ((c_ba, c_bb), (c_aa, c_ab))[0 if p == 0 else 1]
        part = t.part_first if which == 0 else t.part_second
        return part(above[end], below[end])

    v, h, vz, hz = plane(fields + 5)
    hz[own + 1] = corner_z(own + 1, 0)
    v_next = v[1:] + [x_third(fields, True)]
    face_x = v
    bx = (
        [0.5 * (v[p] + t.odd(v[p], v_next[p])) for p in span],
        [0.5 * (h[p] + t.odd_swapped(h[p], h[min(p + 1, own + 1)])) for p in span],
        [0.5 * (vz[p] + t.odd(vz[p], vz[min(p + 1, own + 1)])) for p in span],
        [None] + [0.5 * (hz[p] + t.odd_swapped(hz[p], hz[p + 1])) for p in inner] + [None],
    )
    v, h, vz, hz = plane(fields + 6)
    hz[0] = corner_z(0, 1)
    hz[own + 1] = corner_z(own + 1, 1)
    face_y = v, h
    full = [
        jnp.where(t.slot == 2, y_third(fields, p), h[p]) if 1 <= p <= own else h[p] for p in span
    ]
    by = (
        [0.5 * (v[p] + t.y_up(v[p], h[p], 1)) for p in span],
        [0.5 * (h[p] + t.y_up(full[p], v[p], 1)) for p in span],
        [0.5 * (vz[p] + t.y_up(vz[p], hz[p], 1)) for p in span],
        [None] + [0.5 * (hz[p] + t.y_up(hz[p], vz[p], 1)) for p in inner] + [None],
    )
    v, h, vz, hz = plane(fields + 7)
    for p in inner:
        raw, raw_z = rows_of(fl, 7, p), rows_of(zfl, 7, p)
        v[p] = 0.5 * (raw + t.z_up(raw, raw_z, 1))
        vz[p] = 0.5 * (raw_z + t.z_up(raw_z, raw, 1))
    bz = (v, h, vz, hz)

    chi, alpha = plane(0), plane(7)
    cons = [plane(fields + q) for q in range(5)]
    centred = [bx, by, bz]
    spots = [(0, p) for p in span] + [(1, p) for p in span] + [(2, p) for p in span]
    spots += [(3, p) for p in inner]
    prims = [[[None] * (own + 2) for _ in range(4)] for _ in range(8)]
    electric = [[[None] * (own + 2) for _ in range(4)] for _ in range(3)]
    batch = 4
    for start in range(0, len(spots), batch):
        group = spots[start : start + batch]

        def gather(planes):
            return jnp.concatenate([planes[k][p] for k, p in group], axis=0)

        shrink = volume_over(gather(chi))
        mag_raw = [gather(centred[i]) for i in range(3)]
        mag = [m * shrink for m in mag_raw]
        values = recover([gather(c) * shrink for c in cons], mag)
        u = values[2:5]
        factor = gather(alpha) * lax.rsqrt(1.0 + dot(u, u))
        field = [
            factor * (u[(i + 2) % 3] * mag_raw[(i + 1) % 3] - u[(i + 1) % 3] * mag_raw[(i + 2) % 3])
            for i in range(3)
        ]
        for n, (k, p) in enumerate(group):
            for i, value in enumerate(values + mag):
                prims[i][k][p] = value[n * half : (n + 1) * half]
            for i in range(3):
                electric[i][k][p] = field[i][n * half : (n + 1) * half]

    hydro = [[None] * (own + 2) for _ in range(5)]

    def weigh(chi_face, alpha_face):
        shrink = volume_over(chi_face)
        return shrink, alpha_face / shrink

    odd_prims = [[t.odd(f[0][p], f[0][min(p + 1, own + 1)]) for p in span] for f in prims]
    fluxes = [None]
    odd_chi = [t.odd(chi[0][p], chi[0][min(p + 1, own + 1)]) for p in span]
    odd_alpha = [t.odd(alpha[0][p], alpha[0][min(p + 1, own + 1)]) for p in span]
    for p in range(1, own + 2):
        left, right = [], []
        for f, o in zip(prims, odd_prims):
            f = f[0]
            here = f[p] - o[p - 1]
            left.append(o[p - 1] + 0.5 * limited(o[p - 1] - f[p - 1], here))
            right.append(f[p] - 0.5 * limited(here, o[p] - f[p]))
        shrink, weight = weigh(
            0.5 * (chi[0][p] + odd_chi[p - 1]), 0.5 * (alpha[0][p] + odd_alpha[p - 1])
        )
        fluxes.append(face_flux(left, right, face_x[p] * shrink, weight, 0))
    for p in inner:
        for q in range(5):
            hydro[q][p] = fluxes[p][q] - t.odd(fluxes[p][q], fluxes[p + 1][q])

    for d, kind, up, down in ((1, 1, t.y_up, t.y_down), (2, 2, t.z_up, t.z_down)):
        for p in inner:
            found = []
            for here, there in ((0, kind), (kind, 0)):
                left, right = [], []
                for f in prims:
                    a, b = f[here][p], f[there][p]
                    below = down(a, b, 1)
                    middle = a - below
                    left.append(below + 0.5 * limited(below - down(a, b, 2), middle))
                    right.append(a - 0.5 * limited(middle, up(a, b, 1) - a))
                shrink, weight = weigh(
                    0.5 * (chi[here][p] + down(chi[here][p], chi[there][p], 1)),
                    0.5 * (alpha[here][p] + down(alpha[here][p], alpha[there][p], 1)),
                )
                if d == 1:
                    normal = face_y[0 if here == 0 else 1][p]
                else:
                    normal = rows_of(fl if here == 0 else zfl, 7, p)
                found.append(face_flux(left, right, normal * shrink, weight, d))
            for q in range(5):
                hydro[q][p] = hydro[q][p] + found[0][q] - up(found[0][q], found[1][q], 1)

    ex, ey, ez = electric
    ez_x = [
        [ez[0][p] + t.odd(ez[0][p - 1], ez[0][p]) if p else None for p in span],
        [ez[1][p] + t.odd_swapped(ez[1][p - 1], ez[1][p]) if p else None for p in span],
    ]
    ey_x = [
        [ey[k][p] + t.odd(ey[k][p - 1], ey[k][p]) if p else None for p in span] for k in (0, 2)
    ]
    edge_z = [None] + [ez_x[0][p] + t.y_down(ez_x[0][p], ez_x[1][p], 1) for p in span[1:]]
    edge_z_h = [None] + [ez_x[1][p] + t.y_down(ez_x[1][p], ez_x[0][p], 1) for p in inner]
    edge_y = [None] + [ey_x[0][p] + t.z_down(ey_x[0][p], ey_x[1][p], 1) for p in span[1:]]
    edge_y_z = [None] + [ey_x[1][p] + t.z_down(ey_x[1][p], ey_x[0][p], 1) for p in inner]
    dt = COURANT / jnp.max(tops[...], axis=0, keepdims=True)
    for p in inner:
        ex_y = ex[0][p] + t.y_down(ex[0][p], ex[1][p], 1)
        ex_y_h = ex[1][p] + t.y_down(ex[1][p], ex[0][p], 1)
        ex_y_z = ex[2][p] + t.y_down(ex[2][p], ex[3][p], 1)
        ex_y_hz = ex[3][p] + t.y_down(ex[3][p], ex[2][p], 1)
        edge_x = ex_y + t.z_down(ex_y, ex_y_z, 1)
        edge_x_h = ex_y_h + t.z_down(ex_y_h, ex_y_hz, 1)
        edge_x_z = ex_y_z + t.z_down(ex_y_z, ex_y, 1)
        x_rate = (t.z_up(edge_y[p], edge_y_z[p], 1) - edge_y[p]) - (
            t.y_up(edge_z[p], edge_z_h[p], 1) - edge_z[p]
        )
        y_rate = (t.odd(edge_z[p], edge_z[p + 1]) - edge_z[p]) - (
            t.z_up(edge_x, edge_x_z, 1) - edge_x
        )
        z_rate = (t.y_up(edge_x, edge_x_h, 1) - edge_x) - (
            t.odd(edge_y[p], edge_y[p + 1]) - edge_y[p]
        )
        quarter = 0.25 * dt
        for i, rate in enumerate((x_rate, y_rate, z_rate)):
            fl_out[5 + i, (p - 1) * half : p * half, :] = rows_of(fl, 5 + i, p) + quarter * rate
        for q in range(5):
            tensors[p - 1, 6 + q] = hydro[q][p]
        parts = stress_parts(
            prims[0][0][p],
            prims[1][0][p],
            [prims[2 + i][0][p] for i in range(3)],
            [prims[5 + i][0][p] for i in range(3)],
        )
        lorentz_sq, over, over_sq, time_b, grown_b, b_square, enthalpy, inertia = parts
        total_pressure = prims[1][0][p] + 0.5 * b_square
        for s, (i, j) in enumerate(INDEX_PAIRS):
            value = inertia * prims[2 + i][0][p] * prims[2 + j][0][p] - over_sq * (
                grown_b[i] * grown_b[j]
            )
            tensors[p - 1, s] = value + total_pressure if i == j else value

    def pair_step(index, carry):
        p = index + 1
        base = pl.multiple_of(index * half, half)

        for q in range(fields):
            centre = pairs[q, p + 1]
            x_m3 = t.odd(pairs[q, p - 1], pairs[q, p])
            x_m2 = pairs[q, p]
            x_m1 = t.odd(pairs[q, p], centre)
            x_p1 = t.odd(centre, pairs[q, p + 2])
            x_p2 = pairs[q, p + 2]
            x_p3 = t.odd(pairs[q, p + 2], pairs[q, p + 3])
            side, third = sides[q, p], thirds[q, p - 1]
            y_m1, y_m2 = t.y_down(centre, side, 1), t.y_down(centre, side, 2)
            y_p1, y_p2 = t.y_up(centre, side, 1), t.y_up(centre, side, 2)
            y_m3 = t.turn(
                jnp.where(t.slot >= cy - 2, side, jnp.where(t.slot == cy - 3, third, centre)), 3
            )
            y_p3 = t.turn(jnp.where(t.slot < 2, side, jnp.where(t.slot == 2, third, centre)), -3)
            beyond = zst[q, pl.ds(base, half), :]
            z_m1, z_m2, z_m3 = (t.z_down(centre, beyond, k) for k in (1, 2, 3))
            z_p1, z_p2, z_p3 = (t.z_up(centre, beyond, k) for k in (1, 2, 3))
            dx = first_diff(x_m2, x_m1, x_p1, x_p2)
            dy = first_diff(y_m2, y_m1, y_p1, y_p2)
            grads[q, 0] = dx
            grads[q, 1] = dy
            grads[q, 2] = first_diff(z_m2, z_m1, z_p1, z_p2)
            near = [x_m1 + x_p1, y_m1 + y_p1, z_m1 + z_p1]
            far = [x_m2 + x_p2, y_m2 + y_p2, z_m2 + z_p2]
            outer = (x_m3 + x_p3) + (y_m3 + y_p3) + (z_m3 + z_p3)
            damped[q] = (DISSIPATION / 64.0) * (
                outer - 6.0 * (far[0] + far[1] + far[2]) + 15.0 * (near[0] + near[1] + near[2])
                - 60.0 * centre
            )
            if q < CURVED:
                for s, d in ((0, 0), (3, 1), (5, 2)):
                    seconds[q, s] = (1.0 / 12.0) * (16.0 * near[d] - far[d] - 30.0 * centre)
                s_m, s_c, s_p = sides[q, p - 1], side, sides[q, p + 1]
                dx_side = first_diff(s_m, t.odd_swapped(s_m, s_c), t.odd_swapped(s_c, s_p), s_p)
                seconds[q, 1] = first_diff(
                    t.y_down(dx, dx_side, 2),
                    t.y_down(dx, dx_side, 1),
                    t.y_up(dx, dx_side, 1),
                    t.y_up(dx, dx_side, 2),
                )
                b_m, b_c, b_p = pairs_z[q, p - 1], pairs_z[q, p], pairs_z[q, p + 1]
                dx_z = first_diff(b_m, t.odd(b_m, b_c), t.odd(b_c, b_p), b_p)
                b_s = sides_z[q, p - 1]
                dy_z = first_diff(
                    t.y_down(b_c, b_s, 2),
                    t.y_down(b_c, b_s, 1),
                    t.y_up(b_c, b_s, 1),
                    t.y_up(b_c, b_s, 2),
                )
                for s, inside, outside in ((2, dx, dx_z), (4, dy, dy_z)):
                    seconds[q, s] = first_diff(
                        t.z_down(inside, outside, 2),
                        t.z_down(inside, outside, 1),
                        t.z_up(inside, outside, 1),
                        t.z_up(inside, outside, 2),
                    )

        def value(q):
            return pairs[q, p + 1]

        def fluid_value(q):
            return fl[q, pl.ds(base, half), :]

        conformal, lapse = value(0), value(7)
        over_chi = 1.0 / conformal
        metric = symmetric([value(1 + s) for s in range(6)])
        shift = [value(8 + i) for i in range(3)]
        extrinsic, theta = value(11), value(21)
        traceless = symmetric([value(12 + s) for s in range(6)])
        connection = [value(18 + i) for i in range(3)]
        inverse = inverse_metric(metric)
        grad = [[grads[q, k] for k in range(3)] for q in range(fields)]
        chi_grad, lapse_grad = grad[0], grad[7]
        shift_grad = [[grad[8 + i][k] for i in range(3)] for k in range(3)]
        trace_k = extrinsic + 2.0 * theta

        stress = symmetric([tensors[p - 1, s] for s in range(6)])
        held = [fluid_value(q) for q in range(5)]
        shrink = volume_over(conformal)
        energy = held[4] + held[0]
        third_k = trace_k * (1.0 / 3.0)
        curved = [
            [
                (traceless[i][j] + metric[i][j] * third_k) if i <= j else None for j in range(3)
            ]
            for i in range(3)
        ]
        work = (
            stress[0][0] * curved[0][0]
            + stress[1][1] * curved[1][1]
            + stress[2][2] * curved[2][2]
            + 2.0
            * (
                stress[0][1] * curved[0][1]
                + stress[0][2] * curved[0][2]
                + stress[1][2] * curved[1][2]
            )
        )
        rates = [tensors[p - 1, 6 + q] for q in range(5)]
        for i in range(3):
            rates[1 + i] = (
                rates[1 + i]
                - energy * lapse_grad[i]
                + total([held[1 + k] * grad[8 + k][i] for k in range(3)])
            )
        rates[4] = (
            rates[4] + lapse * work * over_chi / shrink - dot(held[1:4], lapse_grad)
        )
        for q in range(5):
            fl_out[q, pl.ds(base, half), :] = held[q] + dt * rates[q]
        density = energy * shrink
        momentum = [held[1 + i] * shrink for i in range(3)]

        lowered = [[[None] * 3 for _ in range(3)] for _ in range(3)]
        for i in range(3):
            for j in range(3):
                for k in range(j, 3):
                    got = 0.5 * (
                        grad[1 + slot_of(i, k)][j]
                        + grad[1 + slot_of(i, j)][k]
                        - grad[1 + slot_of(j, k)][i]
                    )
                    lowered[i][j][k] = lowered[i][k][j] = got
        raised = [[[None] * 3 for _ in range(3)] for _ in range(3)]
        for i in range(3):
            for j in range(3):
                for k in range(j, 3):
                    got = total([inverse[i][l] * lowered[l][j][k] for l in range(3)])
                    raised[i][j][k] = raised[i][k][j] = got
        contracted = [trace_with(inverse, raised[i]) for i in range(3)]

        def hessian(q):
            return symmetric([seconds[q, s] for s in range(6)])

        def second_cov(q, slope):
            return symmetric(
                [
                    seconds[q, s] - total([raised[k][i][j] * slope[k] for k in range(3)])
                    for s, (i, j) in enumerate(INDEX_PAIRS)
                ]
            )

        chi_cov = second_cov(0, chi_grad)
        chi_lap = trace_with(inverse, chi_cov)
        raised_chi = [dot(inverse[i], chi_grad) for i in range(3)]
        chi_square = dot(raised_chi, chi_grad)
        cross_term = dot(raised_chi, lapse_grad)
        half_chi = 0.5 * over_chi
        plain_cov = second_cov(7, lapse_grad)
        lapse_cov = symmetric(
            [
                plain_cov[i][j]
                + (
                    chi_grad[i] * lapse_grad[j]
                    + chi_grad[j] * lapse_grad[i]
                    - metric[i][j] * cross_term
                )
                * half_chi
                for i, j in INDEX_PAIRS
            ]
        )
        lapse_lap = conformal * trace_with(inverse, lapse_cov)

        mixed = [
            [[dot(inverse[l], lowered[k][j]) for j in range(3)] for k in range(3)]
            for l in range(3)
        ]
        quarter_sq = half_chi * half_chi
        metric_factor = chi_lap * half_chi - 3.0 * chi_square * quarter_sq
        ricci = []
        for i, j in INDEX_PAIRS:
            second_part = -0.5 * trace_with(inverse, hessian(1 + slot_of(i, j)))
            connection_part = 0.5 * total(
                [metric[k][i] * grad[18 + k][j] + metric[k][j] * grad[18 + k][i] for k in range(3)]
            )
            contracted_part = 0.5 * total(
                [contracted[k] * (lowered[i][j][k] + lowered[j][i][k]) for k in range(3)]
            )
            if i == j:
                quadratic = total(
                    [
                        raised[k][l][i] * (2.0 * mixed[l][i][k] + mixed[l][k][i])
                        for k in range(3)
                        for l in range(3)
                    ]
                )
            else:
                quadratic = total(
                    [
                        raised[k][l][i] * (mixed[l][j][k] + mixed[l][k][j])
                        + raised[k][l][j] * mixed[l][i][k]
                        for k in range(3)
                        for l in range(3)
                    ]
                )
            conformal_part = (
                chi_cov[i][j] * half_chi
                + metric[i][j] * metric_factor
                - chi_grad[i] * chi_grad[j] * quarter_sq
            )
            ricci.append(
                second_part + connection_part + contracted_part + quadratic + conformal_part
            )
        ricci = symmetric(ricci)
        ricci_scalar = conformal * trace_with(inverse, ricci)
        stress_trace = conformal * trace_with(inverse, stress)

        up_a = [
            [total([inverse[i][k] * traceless[k][j] for k in range(3)]) for j in range(3)]
            for i in range(3)
        ]
        raised_a = symmetric(
            [total([up_a[i][l] * inverse[j][l] for l in range(3)]) for i, j in INDEX_PAIRS]
        )
        a_square = trace_with(traceless, raised_a)
        shift_div = shift_grad[0][0] + shift_grad[1][1] + shift_grad[2][2]
        two_thirds_div = (2.0 / 3.0) * shift_div

        def finish(q, rate):
            rate = rate + dot(shift, grad[q]) + damped[q]
            st_out[q, pl.ds(base, half), :] = value(q) + dt * rate

        finish(0, (2.0 / 3.0) * conformal * (lapse * trace_k - shift_div))
        finish(7, -2.0 * lapse * extrinsic)
        for i in range(3):
            finish(8 + i, 0.75 * connection[i] - SHIFT_DAMPING * shift[i])
        finish(
            11,
            lapse
            * (
                a_square
                + trace_k * trace_k * (1.0 / 3.0)
                + FOUR_PI * (stress_trace + density)
                + KAPPA_ONE * theta
            )
            - lapse_lap,
        )
        source = symmetric(
            [
                lapse * (ricci[i][j] - 2.0 * FOUR_PI * stress[i][j]) - lapse_cov[i][j]
                for i, j in INDEX_PAIRS
            ]
        )
        third_trace = trace_with(inverse, source) * (1.0 / 3.0)
        for s, (i, j) in enumerate(INDEX_PAIRS):
            finish(
                1 + s,
                total(
                    [
                        metric[i][k] * shift_grad[j][k] + metric[j][k] * shift_grad[i][k]
                        for k in range(3)
                    ]
                )
                - metric[i][j] * two_thirds_div
                - 2.0 * lapse * traceless[i][j],
            )
            product = total([traceless[i][k] * up_a[k][j] for k in range(3)])
            finish(
                12 + s,
                total(
                    [
                        traceless[i][k] * shift_grad[j][k] + traceless[j][k] * shift_grad[i][k]
                        for k in range(3)
                    ]
                )
                - traceless[i][j] * two_thirds_div
                + conformal * (source[i][j] - metric[i][j] * third_trace)
                + lapse * (trace_k * traceless[i][j] - 2.0 * product),
            )
        for i in range(3):
            bracket = (
                trace_with(raised_a, raised[i])
                - 1.5 * dot(raised_a[i], chi_grad) * over_chi
                - dot(inverse[i], [2.0 * grad[11][j] + grad[21][j] for j in range(3)]) * (1.0 / 3.0)
                - 2.0 * FOUR_PI * dot(inverse[i], momentum)
            )
            spread = [
                seconds[8, slot_of(j, 0)] + seconds[9, slot_of(j, 1)] + seconds[10, slot_of(j, 2)]
                for j in range(3)
            ]
            finish(
                18 + i,
                contracted[i] * two_thirds_div
                - total([contracted[j] * shift_grad[j][i] for j in range(3)])
                + trace_with(inverse, hessian(8 + i))
                + dot(inverse[i], spread) * (1.0 / 3.0)
                - 2.0 * dot(raised_a[i], lapse_grad)
                + 2.0
                * lapse
                * (bracket - KAPPA_ONE * (connection[i] - contracted[i])),
            )
        finish(
            21,
            0.5
            * lapse
            * (
                ricci_scalar
                - a_square
                + (2.0 / 3.0) * trace_k * trace_k
                - 4.0 * FOUR_PI * density
            )
            - 2.0 * KAPPA_ONE * lapse * theta,
        )
        return carry

    lax.fori_loop(0, own, pair_step, 0)


def per_device(spacetime, fluid):
    fields, cx, cy, cz = spacetime.shape
    rows = cx * cy
    st = spacetime.reshape(fields, rows, cz)
    fl = fluid.reshape(FLUID, rows, cz)
    sizes = [lax.axis_size(a) for a in ("gx", "gy", "gz")]
    tile = (2 * cy, cz)
    f32 = jnp.float32

    def shape(*dims):
        return jax.ShapeDtypeStruct(dims, f32)

    def beyond(cells):
        n = sizes[2]
        after = lax.ppermute(cells, "gz", [((i + 1) % n, i) for i in range(n)])
        if n == 2:
            return after
        before = lax.ppermute(cells, "gz", [(i, (i + 1) % n) for i in range(n)])
        lane = lax.broadcasted_iota(jnp.int32, cells.shape, 2)
        return jnp.where(lane < cz // 2, after, before)

    params = pltpu.CompilerParams(vmem_limit_bytes=48 * 1024 * 1024)
    zst, zfl = beyond(st), beyond(fl)
    top = pl.pallas_call(
        speed_kernel, out_shape=shape(1, cz), compiler_params=params, name="speed"
    )(st)
    tops = lax.all_gather(top, ("gx", "gy", "gz"), axis=0, tiled=True)
    thirds = len(pairs_of(third_list(fields)))
    face = shape(fields + FLUID + thirds + 1, *tile)
    corner = shape(len(pairs_of(list(range(CURVED + FLUID)))) + 1, *tile)
    sent = pl.pallas_call(
        pack_kernel, out_shape=[face] * 4 + [corner] * 4, compiler_params=params, name="pack"
    )(st, fl, zst, zfl)

    def move(cells, dx, dy):
        nx, ny = sizes[0], sizes[1]
        hops = [
            (i * ny + j, ((i + dx) % nx) * ny + (j + dy) % ny) for i in range(nx) for j in range(ny)
        ]
        return lax.ppermute(cells, ("gx", "gy"), hops)

    x_low, x_high, y_low, y_high, c_ll, c_lh, c_hl, c_hh = sent
    x_above = move(x_low, -1, 0)
    x_below = move(x_high, 1, 0)
    y_above = move(y_low, 0, -1)
    y_below = move(y_high, 0, 1)
    c_aa = move(c_ll, -1, -1)
    c_ab = move(c_lh, -1, 1)
    c_ba = move(c_hl, 1, -1)
    c_bb = move(c_hh, 1, 1)
    own = cx // 2
    st_next, fl_next = pl.pallas_call(
        main_kernel,
        out_shape=[shape(*st.shape), shape(*fl.shape)],
        scratch_shapes=[
            pltpu.VMEM((fields, own + 4) + tile, f32),
            pltpu.VMEM((fields, own + 2) + tile, f32),
            pltpu.VMEM((fields, own) + tile, f32),
            pltpu.VMEM((CURVED, own + 2) + tile, f32),
            pltpu.VMEM((CURVED, own) + tile, f32),
            pltpu.VMEM((fields, 3) + tile, f32),
            pltpu.VMEM((CURVED, 6) + tile, f32),
            pltpu.VMEM((fields,) + tile, f32),
            pltpu.VMEM((own, 11) + tile, f32),
        ],
        compiler_params=params,
        name="update",
    )(st, fl, zst, zfl, x_below, x_above, y_below, y_above, c_bb, c_ba, c_ab, c_aa, tops)
    return st_next.reshape(spacetime.shape), fl_next.reshape(fluid.shape)


def solution(mesh):
    spec = P(None, "gx", "gy", "gz")
    return jax.shard_map(
        per_device, mesh=mesh, in_specs=(spec, spec), out_specs=(spec, spec), check_vma=False
    )
```

```python
import functools
import math

import jax
import jax.numpy as jnp
from jax import lax
from jax.experimental import pallas as pl
from jax.experimental.pallas import tpu as pltpu
from jax.sharding import PartitionSpec as P

RECOVERY_STEPS = 4
INDEX_PAIRS = ((0, 0), (0, 1), (0, 2), (1, 1), (1, 2), (2, 2))
COURANT = 0.25
DISSIPATION = 0.2
KAPPA_ONE = 0.02
SHIFT_DAMPING = 1.0
SPEED_CAP = 0.99
PRESSURE_FLOOR = 0.01
FOUR_PI = 4.0 * math.pi

CURVED = 11
FLUID = 8


def total(pieces):
    summed = pieces[0]
    for member in pieces[1:]:
        summed = summed + member
    return summed


def dot(first_vec, second_vec):
    return total([first_vec[i] * second_vec[i] for i in range(3)])


def slot_of(i, j):
    return INDEX_PAIRS.index((min(i, j), max(i, j)))


def symmetric(entries):
    return [[entries[slot_of(i, j)] for j in range(3)] for i in range(3)]


def trace_with(inverse, tensor):
    return (
        inverse[0][0] * tensor[0][0]
        + inverse[1][1] * tensor[1][1]
        + inverse[2][2] * tensor[2][2]
        + 2.0
        * (
            inverse[0][1] * tensor[0][1]
            + inverse[0][2] * tensor[0][2]
            + inverse[1][2] * tensor[1][2]
        )
    )


def inverse_metric(metric):
    cofactor = [
        metric[1][1] * metric[2][2] - metric[1][2] * metric[1][2],
        metric[0][2] * metric[1][2] - metric[0][1] * metric[2][2],
        metric[0][1] * metric[1][2] - metric[0][2] * metric[1][1],
        metric[0][0] * metric[2][2] - metric[0][2] * metric[0][2],
        metric[0][1] * metric[0][2] - metric[0][0] * metric[1][2],
        metric[0][0] * metric[1][1] - metric[0][1] * metric[0][1],
    ]
    determinant = (
        metric[0][0] * cofactor[0] + metric[0][1] * cofactor[1] + metric[0][2] * cofactor[2]
    )
    over = 1.0 / determinant
    return symmetric([c * over for c in cofactor])


class Tile:
    def __init__(self, cy, cz):
        self.cy, self.rows, self.lanes = cy, 2 * cy, cz
        shape = (self.rows, cz)
        self.row = lax.broadcasted_iota(jnp.int32, shape, 0)
        self.lane = lax.broadcasted_iota(jnp.int32, shape, 1)
        self.slot = lax.rem(self.row, cy)

    def turn(self, tile, amount):
        amount = amount % self.rows
        return tile if amount == 0 else pltpu.roll(tile, amount, 0)

    def spin(self, tile, amount):
        amount = amount % self.lanes
        return tile if amount == 0 else pltpu.roll(tile, amount, 1)

    def swap(self, tile):
        return self.turn(tile, self.cy)

    def odd(self, a, b):
        return self.turn(jnp.where(self.row < self.cy, b, a), self.cy)

    def odd_swapped(self, a, b):
        return self.turn(jnp.where(self.row < self.cy, a, b), self.cy)

    def y_up(self, main, beyond, k):
        return self.turn(jnp.where(self.slot < k, beyond, main), -k)

    def y_down(self, main, beyond, k):
        return self.turn(jnp.where(self.slot >= self.cy - k, beyond, main), k)

    def z_up(self, main, beyond, k):
        return self.spin(jnp.where(self.lane < k, beyond, main), -k)

    def z_down(self, main, beyond, k):
        return self.spin(jnp.where(self.lane >= self.lanes - k, beyond, main), k)

    def join_low(self, u, v):
        return jnp.where(self.slot < 2, self.swap(u), self.turn(v, 2))

    def join_high(self, u, v):
        return jnp.where(self.slot >= self.cy - 2, self.swap(u), self.turn(self.swap(v), -2))

    def part_first(self, from_above, from_below):
        return jnp.where(self.slot < 2, from_above, from_below)

    def part_second(self, from_above, from_below):
        return self.turn(jnp.where(self.slot < 2, from_below, from_above), 2)


def edge_list(tiles):
    fields = next(n for n in range(tiles) if face_tiles(n) == tiles)
    return list(range(CURVED)) + list(range(fields, fields + FLUID))


def face_tiles(fields):
    return fields + FLUID + len(pairs_of(third_list(fields))) + 1


def third_list(fields):
    return list(range(fields + 1))


def pairs_of(items):
    return [(items[i], items[min(i + 1, len(items) - 1)]) for i in range(0, len(items), 2)]


def top_speed(st):
    inverse = inverse_metric(symmetric([st[1 + s] for s in range(6)]))
    scale = 2.0 * st[7] * st[0]
    speeds = [jnp.abs(st[8 + d]) + jnp.sqrt(scale * inverse[d][d]) for d in range(3)]
    top = jnp.maximum(jnp.maximum(speeds[0], speeds[1]), speeds[2])
    return jnp.max(jnp.max(top, axis=1, keepdims=True), axis=0, keepdims=True)


def pack_kernel(st, fl, zst, zfl, *outs):
    fields, rows, lanes = st.shape
    cy = rows // 4
    t = Tile(cy, lanes)
    x_low, x_high, y_low, y_high, top_out = outs
    half = t.rows

    def own(ref, q):
        return [ref[q, 0:half, :], ref[q, half : 2 * half, :]]

    tiles, beyond = [], []
    for q in range(fields):
        tiles.append(own(st, q))
        beyond.append(own(zst, q) if q < CURVED else None)
    for q in range(FLUID - 1):
        tiles.append(own(fl, q))
        beyond.append(own(zfl, q))
    along, along_z = own(fl, FLUID - 1), own(zfl, FLUID - 1)
    tiles.append([0.5 * (along[p] + t.z_up(along[p], along_z[p], 1)) for p in range(2)])
    beyond.append([0.5 * (along_z[p] + t.z_up(along_z[p], along[p], 1)) for p in range(2)])

    packed = [None] * 4
    place = 0
    for q, (first, second) in enumerate(tiles):
        x_low[q] = first
        x_high[q] = second
        y_low[q] = t.join_low(first, second)
        y_high[q] = t.join_high(first, second)
        if beyond[q] is not None:
            zf, zs = beyond[q]
            for m, piece in enumerate((zf, zs, t.join_low(zf, zs), t.join_high(zf, zs))):
                piece = t.spin(piece, 4 * place + 2)
                packed[m] = (
                    piece if place == 0 else jnp.where(t.lane < 4 * place, packed[m], piece)
                )
            place += 1
    for n, (a, b) in enumerate(pairs_of(third_list(fields))):
        slot = fields + FLUID + n
        xa, xb = (tiles[q if q < fields else fields + 5] for q in (a, b))
        x_low[slot] = jnp.where(t.row < cy, xa[1], t.swap(xb[1]))
        x_high[slot] = jnp.where(t.row < cy, t.swap(xb[0]), xa[0])
        ya, yb = (tiles[q if q < fields else fields + 6] for q in (a, b))
        w = [t.swap(ya[0]), t.swap(ya[1]), t.swap(yb[0]), t.swap(yb[1])]
        s = t.slot
        y_low[slot] = jnp.where(
            s == 2,
            w[0],
            jnp.where(s == 3, t.turn(w[1], 1), jnp.where(s == 0, t.turn(w[2], -2), t.turn(w[3], -1))),
        )
        y_high[slot] = jnp.where(
            s == 1,
            w[0],
            jnp.where(s == 0, t.turn(w[1], -1), jnp.where(s == 3, t.turn(w[2], 2), t.turn(w[3], 1))),
        )
    top = jnp.maximum(top_speed(st), top_speed(zst))
    top_out[...] = jnp.broadcast_to(top, top_out.shape)
    last = x_low.shape[0] - 1
    for out, piece in zip((x_low, x_high, y_low, y_high), packed):
        out[last] = jnp.where(t.lane < 4 * place, piece, top)


def relay_kernel(x_below, x_above, top, top_two, to_low, to_high, line_top):
    cy, lanes = x_below.shape[1] // 2, x_below.shape[2]
    t = Tile(cy, lanes)
    last = x_below.shape[0] - 1
    line = jnp.maximum(top[...], top_two[...])
    for beside in (x_below, x_above):
        line = jnp.maximum(line, beside[last, 0:1, lanes - 1 : lanes])
    line_top[...] = line
    edge = edge_list(x_below.shape[0])
    for n, q in enumerate(edge + [last]):
        low = t.join_low(x_below[q], x_above[q])
        high = t.join_high(x_below[q], x_above[q])
        if q == last:
            low = jnp.where(t.lane < 4 * len(edge), low, line)
            high = jnp.where(t.lane < 4 * len(edge), high, line)
        to_low[n] = low
        to_high[n] = high


def stage_kernel(st, fl, st_out, fl_out, sems):
    copies = [
        pltpu.make_async_copy(st, st_out, sems.at[0]),
        pltpu.make_async_copy(fl, fl_out, sems.at[1]),
    ]
    for copy in copies:
        copy.start()
    for copy in copies:
        copy.wait()


def limited(a, b):
    return jnp.maximum(jnp.minimum(a, b), 0.0) + jnp.minimum(jnp.maximum(a, b), 0.0)


def recover(conserved, magnetic):
    density = conserved[0]
    momenta = conserved[1:4]
    energy = conserved[4] + density
    mom_sq = dot(momenta, momenta)
    mag_sq = dot(magnetic, magnetic)
    cross = dot(momenta, magnetic)
    cross_sq = cross * cross

    def state(z):
        grown = z + mag_sq
        over = 1.0 / (z * grown)
        speed_sq = (mom_sq * z * z + cross_sq * (2.0 * z + mag_sq)) * over * over
        kept = 1.0 - jnp.minimum(speed_sq, SPEED_CAP)
        rest = density * jnp.sqrt(kept)
        return kept, rest, 0.5 * (z * kept - rest), grown * over

    z = jnp.maximum(energy - 0.5 * mag_sq, density)
    for _ in range(RECOVERY_STEPS):
        kept, rest, pressure, over_z = state(z)
        residual = (
            z
            + mag_sq
            - pressure
            - 0.5 * mag_sq * kept
            - 0.5 * cross_sq * over_z * over_z
            - energy
        )
        z = jnp.maximum(z - residual / (1.0 - 0.5 * kept), density)
    kept, rest, pressure, over_z = state(z)
    pressure = jnp.maximum(pressure, PRESSURE_FLOOR * rest)
    scale = lax.rsqrt(kept) / (z + mag_sq)
    along = cross * over_z
    four_vel = [scale * (momenta[i] + along * magnetic[i]) for i in range(3)]
    return [rest, pressure] + four_vel


def stress_parts(rest, pressure, u, magnetic):
    lorentz_sq = 1.0 + dot(u, u)
    over = lax.rsqrt(lorentz_sq)
    over_sq = over * over
    time_b = dot(u, magnetic)
    grown_b = [magnetic[i] + time_b * u[i] for i in range(3)]
    b_square = (dot(magnetic, magnetic) + time_b * time_b) * over_sq
    enthalpy = rest + 2.0 * pressure
    inertia = enthalpy + b_square
    return lorentz_sq, over, over_sq, time_b, grown_b, b_square, enthalpy, inertia


def face_state(rest, pressure, u, magnetic, d):
    lorentz_sq, over, over_sq, time_b, grown_b, b_square, enthalpy, inertia = stress_parts(
        rest, pressure, u, magnetic
    )
    total_pressure = pressure + 0.5 * b_square
    lorentz = lorentz_sq * over
    density = rest * lorentz
    carried = inertia * lorentz
    time_over = time_b * over
    conserved = [density]
    conserved += [carried * u[j] - time_over * grown_b[j] for j in range(3)]
    conserved += [inertia * lorentz_sq - total_pressure - time_b * time_b - density]
    mass_flux = rest * u[d]
    flux = [mass_flux]
    pushed = inertia * u[d]
    b_over = grown_b[d] * over_sq
    for j in range(3):
        flux_j = pushed * u[j] - b_over * grown_b[j]
        flux.append(flux_j + total_pressure if j == d else flux_j)
    flux.append(carried * u[d] - time_over * grown_b[d] - mass_flux)
    ratio = 1.0 / (enthalpy * inertia)
    sound_sq = 2.0 * pressure * inertia * ratio
    alfven_sq = b_square * enthalpy * ratio
    fast_sq = sound_sq + alfven_sq - sound_sq * alfven_sq
    slow = 1.0 - fast_sq
    velocity = u[d] * over
    rest_part = 1.0 - dot(u, u) * over_sq * fast_sq
    spread = jnp.sqrt(fast_sq * over_sq * (rest_part - velocity * velocity * slow))
    fastest = (jnp.abs(velocity * slow) + spread) / rest_part
    return conserved, flux, fastest


def face_flux(left, right, normal, weight, d):
    sides = []
    for state in (left, right):
        magnetic = [normal if i == d else state[5 + i] for i in range(3)]
        sides.append(face_state(state[0], state[1], state[2:5], magnetic, d))
    (cons_l, flux_l, fast_l), (cons_r, flux_r, fast_r) = sides
    signal = jnp.maximum(fast_l, fast_r)
    scale = 0.5 * weight
    return [scale * (flux_l[q] + flux_r[q] - signal * (cons_r[q] - cons_l[q])) for q in range(5)]


def volume_over(conformal):
    return conformal * jnp.sqrt(conformal)


def first_diff(down_two, down, up, up_two):
    return (8.0 / 12.0) * (up - down) + (1.0 / 12.0) * (down_two - up_two)


def main_kernel(
    st, fl, zst, zfl, x_below, x_above, y_below, y_above, c_below, c_above, line_top, line_two,
    st_out, fl_out, pairs, sides, thirds, pairs_z, sides_z, grads, seconds, damped, tensors,
):
    fields, rows, lanes = st.shape
    cy = rows // 4
    t = Tile(cy, lanes)
    half = t.rows
    own = rows // half

    def third_place(q):
        return fields + FLUID + q // 2, q % 2

    def beside(q, p):
        if p == 1:
            return t.part_first(y_above[q], y_below[q])
        return t.part_second(y_above[q], y_below[q])

    edge = edge_list(x_below.shape[0])

    def corner(q, p):
        place = edge.index(q) if q is not None else len(edge)
        part = t.part_first if p == 0 else t.part_second
        return part(c_above[place], c_below[place])

    def x_third(q, upper):
        tile, which = third_place(q)
        found = x_above[tile] if upper else x_below[tile]
        return t.swap(found) if which else found

    def y_third(q, p):
        tile, which = third_place(q)
        above, below = y_above[tile], y_below[tile]
        turn_above, turn_below = ((0, 0), (-1, 1), (2, -2), (1, -1))[2 * which + p - 1]
        return jnp.where(t.slot == 2, t.turn(above, turn_above), t.turn(below, turn_below))

    last = x_below.shape[0] - 1
    z_xb, z_xa = x_below[last], x_above[last]
    z_y = [
        t.part_first(y_above[last], y_below[last]),
        t.part_second(y_above[last], y_below[last]),
    ]

    def z_place(q):
        return 4 * edge.index(q) + 2

    def rows_of(ref, q, p):
        return ref[q, (p - 1) * half : p * half, :]

    for q in range(fields):
        pairs[q, 0] = x_third(q, False)
        pairs[q, 1] = x_below[q]
        for p in range(1, own + 1):
            pairs[q, 1 + p] = rows_of(st, q, p)
            sides[q, p] = beside(q, p)
            thirds[q, p - 1] = y_third(q, p)
        pairs[q, 2 + own] = x_above[q]
        pairs[q, 3 + own] = x_third(q, True)
        if q < CURVED:
            sides[q, 0] = corner(q, 0)
            sides[q, own + 1] = corner(q, own + 1)
            pairs_z[q, 0] = t.spin(z_xb, -z_place(q))
            pairs_z[q, own + 1] = t.spin(z_xa, -z_place(q))
            for p in range(1, own + 1):
                pairs_z[q, p] = rows_of(zst, q, p)
                sides_z[q, p - 1] = t.spin(z_y[p - 1], -z_place(q))

    span = range(own + 2)
    inner = range(1, own + 1)

    def plane(q):
        if q < fields:
            return (
                [pairs[q, 1 + p] for p in span],
                [sides[q, p] for p in span],
                [pairs_z[q, p] for p in span],
                [sides_z[q, p - 1] if 1 <= p <= own else None for p in span],
            )
        f = q - fields
        v = [x_below[q]] + [rows_of(fl, f, p) for p in inner] + [x_above[q]]
        h = [corner(q, 0)] + [beside(q, p) for p in inner] + [corner(q, own + 1)]
        place = z_place(q)
        vz = [t.spin(z_xb, -place)] + [rows_of(zfl, f, p) for p in inner] + [t.spin(z_xa, -place)]
        hz = [None] + [t.spin(z_y[p - 1], -place) for p in inner] + [None]
        return v, h, vz, hz

    def corner_z(q, p):
        return t.spin(corner(None, p), -z_place(q))

    v, h, vz, hz = plane(fields + 5)
    hz[own + 1] = corner_z(fields + 5, own + 1)
    v_next = v[1:] + [x_third(fields, True)]
    face_x = v
    bx = (
        [0.5 * (v[p] + t.odd(v[p], v_next[p])) for p in span],
        [0.5 * (h[p] + t.odd_swapped(h[p], h[min(p + 1, own + 1)])) for p in span],
        [0.5 * (vz[p] + t.odd(vz[p], vz[min(p + 1, own + 1)])) for p in span],
        [None] + [0.5 * (hz[p] + t.odd_swapped(hz[p], hz[p + 1])) for p in inner] + [None],
    )
    v, h, vz, hz = plane(fields + 6)
    hz[0] = corner_z(fields + 6, 0)
    hz[own + 1] = corner_z(fields + 6, own + 1)
    face_y = v, h
    full = [
        jnp.where(t.slot == 2, y_third(fields, p), h[p]) if 1 <= p <= own else h[p] for p in span
    ]
    by = (
        [0.5 * (v[p] + t.y_up(v[p], h[p], 1)) for p in span],
        [0.5 * (h[p] + t.y_up(full[p], v[p], 1)) for p in span],
        [0.5 * (vz[p] + t.y_up(vz[p], hz[p], 1)) for p in span],
        [None] + [0.5 * (hz[p] + t.y_up(hz[p], vz[p], 1)) for p in inner] + [None],
    )
    v, h, vz, hz = plane(fields + 7)
    for p in inner:
        raw, raw_z = rows_of(fl, 7, p), rows_of(zfl, 7, p)
        v[p] = 0.5 * (raw + t.z_up(raw, raw_z, 1))
        vz[p] = 0.5 * (raw_z + t.z_up(raw_z, raw, 1))
    bz = (v, h, vz, hz)

    chi, alpha = plane(0), plane(7)
    cons = [plane(fields + q) for q in range(5)]
    centred = [bx, by, bz]
    spots = [(0, p) for p in span] + [(1, p) for p in span] + [(2, p) for p in span]
    spots += [(3, p) for p in inner]
    prims = [[[None] * (own + 2) for _ in range(4)] for _ in range(8)]
    electric = [[[None] * (own + 2) for _ in range(4)] for _ in range(3)]
    batch = 4
    for start in range(0, len(spots), batch):
        group = spots[start : start + batch]

        def gather(planes):
            return jnp.concatenate([planes[k][p] for k, p in group], axis=0)

        shrink = volume_over(gather(chi))
        mag_raw = [gather(centred[i]) for i in range(3)]
        mag = [m * shrink for m in mag_raw]
        values = recover([gather(c) * shrink for c in cons], mag)
        u = values[2:5]
        factor = gather(alpha) * lax.rsqrt(1.0 + dot(u, u))
        field = [
            factor * (u[(i + 2) % 3] * mag_raw[(i + 1) % 3] - u[(i + 1) % 3] * mag_raw[(i + 2) % 3])
            for i in range(3)
        ]
        for n, (k, p) in enumerate(group):
            for i, value in enumerate(values + mag):
                prims[i][k][p] = value[n * half : (n + 1) * half]
            for i in range(3):
                electric[i][k][p] = field[i][n * half : (n + 1) * half]

    hydro = [[None] * (own + 2) for _ in range(5)]

    def weigh(chi_face, alpha_face):
        shrink = volume_over(chi_face)
        return shrink, alpha_face / shrink

    odd_prims = [[t.odd(f[0][p], f[0][min(p + 1, own + 1)]) for p in span] for f in prims]
    fluxes = [None]
    odd_chi = [t.odd(chi[0][p], chi[0][min(p + 1, own + 1)]) for p in span]
    odd_alpha = [t.odd(alpha[0][p], alpha[0][min(p + 1, own + 1)]) for p in span]
    for p in range(1, own + 2):
        left, right = [], []
        for f, o in zip(prims, odd_prims):
            f = f[0]
            here = f[p] - o[p - 1]
            left.append(o[p - 1] + 0.5 * limited(o[p - 1] - f[p - 1], here))
            right.append(f[p] - 0.5 * limited(here, o[p] - f[p]))
        shrink, weight = weigh(
            0.5 * (chi[0][p] + odd_chi[p - 1]), 0.5 * (alpha[0][p] + odd_alpha[p - 1])
        )
        fluxes.append(face_flux(left, right, face_x[p] * shrink, weight, 0))
    for p in inner:
        for q in range(5):
            hydro[q][p] = fluxes[p][q] - t.odd(fluxes[p][q], fluxes[p + 1][q])

    for d, kind, up, down in ((1, 1, t.y_up, t.y_down), (2, 2, t.z_up, t.z_down)):
        for p in inner:
            found = []
            for here, there in ((0, kind), (kind, 0)):
                left, right = [], []
                for f in prims:
                    a, b = f[here][p], f[there][p]
                    below = down(a, b, 1)
                    middle = a - below
                    left.append(below + 0.5 * limited(below - down(a, b, 2), middle))
                    right.append(a - 0.5 * limited(middle, up(a, b, 1) - a))
                shrink, weight = weigh(
                    0.5 * (chi[here][p] + down(chi[here][p], chi[there][p], 1)),
                    0.5 * (alpha[here][p] + down(alpha[here][p], alpha[there][p], 1)),
                )
                if d == 1:
                    normal = face_y[0 if here == 0 else 1][p]
                else:
                    normal = rows_of(fl if here == 0 else zfl, 7, p)
                found.append(face_flux(left, right, normal * shrink, weight, d))
            for q in range(5):
                hydro[q][p] = hydro[q][p] + found[0][q] - up(found[0][q], found[1][q], 1)

    ex, ey, ez = electric
    ez_x = [
        [ez[0][p] + t.odd(ez[0][p - 1], ez[0][p]) if p else None for p in span],
        [ez[1][p] + t.odd_swapped(ez[1][p - 1], ez[1][p]) if p else None for p in span],
    ]
    ey_x = [
        [ey[k][p] + t.odd(ey[k][p - 1], ey[k][p]) if p else None for p in span] for k in (0, 2)
    ]
    edge_z = [None] + [ez_x[0][p] + t.y_down(ez_x[0][p], ez_x[1][p], 1) for p in span[1:]]
    edge_z_h = [None] + [ez_x[1][p] + t.y_down(ez_x[1][p], ez_x[0][p], 1) for p in inner]
    edge_y = [None] + [ey_x[0][p] + t.z_down(ey_x[0][p], ey_x[1][p], 1) for p in span[1:]]
    edge_y_z = [None] + [ey_x[1][p] + t.z_down(ey_x[1][p], ey_x[0][p], 1) for p in inner]
    top = jnp.maximum(line_top[...], line_two[...])
    for lines in (c_below, c_above):
        top = jnp.maximum(top, lines[len(edge), 0:1, lanes - 1 : lanes])
    dt = COURANT / top
    for p in inner:
        ex_y = ex[0][p] + t.y_down(ex[0][p], ex[1][p], 1)
        ex_y_h = ex[1][p] + t.y_down(ex[1][p], ex[0][p], 1)
        ex_y_z = ex[2][p] + t.y_down(ex[2][p], ex[3][p], 1)
        ex_y_hz = ex[3][p] + t.y_down(ex[3][p], ex[2][p], 1)
        edge_x = ex_y + t.z_down(ex_y, ex_y_z, 1)
        edge_x_h = ex_y_h + t.z_down(ex_y_h, ex_y_hz, 1)
        edge_x_z = ex_y_z + t.z_down(ex_y_z, ex_y, 1)
        x_rate = (t.z_up(edge_y[p], edge_y_z[p], 1) - edge_y[p]) - (
            t.y_up(edge_z[p], edge_z_h[p], 1) - edge_z[p]
        )
        y_rate = (t.odd(edge_z[p], edge_z[p + 1]) - edge_z[p]) - (
            t.z_up(edge_x, edge_x_z, 1) - edge_x
        )
        z_rate = (t.y_up(edge_x, edge_x_h, 1) - edge_x) - (
            t.odd(edge_y[p], edge_y[p + 1]) - edge_y[p]
        )
        quarter = 0.25 * dt
        for i, rate in enumerate((x_rate, y_rate, z_rate)):
            fl_out[5 + i, (p - 1) * half : p * half, :] = rows_of(fl, 5 + i, p) + quarter * rate
        for q in range(5):
            tensors[p - 1, 6 + q] = hydro[q][p]
        parts = stress_parts(
            prims[0][0][p],
            prims[1][0][p],
            [prims[2 + i][0][p] for i in range(3)],
            [prims[5 + i][0][p] for i in range(3)],
        )
        lorentz_sq, over, over_sq, time_b, grown_b, b_square, enthalpy, inertia = parts
        total_pressure = prims[1][0][p] + 0.5 * b_square
        for s, (i, j) in enumerate(INDEX_PAIRS):
            value = inertia * prims[2 + i][0][p] * prims[2 + j][0][p] - over_sq * (
                grown_b[i] * grown_b[j]
            )
            tensors[p - 1, s] = value + total_pressure if i == j else value

    def pair_step(index, carry):
        p = index + 1
        base = pl.multiple_of(index * half, half)

        for q in range(fields):
            centre = pairs[q, p + 1]
            x_m3 = t.odd(pairs[q, p - 1], pairs[q, p])
            x_m2 = pairs[q, p]
            x_m1 = t.odd(pairs[q, p], centre)
            x_p1 = t.odd(centre, pairs[q, p + 2])
            x_p2 = pairs[q, p + 2]
            x_p3 = t.odd(pairs[q, p + 2], pairs[q, p + 3])
            side, third = sides[q, p], thirds[q, p - 1]
            y_m1, y_m2 = t.y_down(centre, side, 1), t.y_down(centre, side, 2)
            y_p1, y_p2 = t.y_up(centre, side, 1), t.y_up(centre, side, 2)
            y_m3 = t.turn(
                jnp.where(t.slot >= cy - 2, side, jnp.where(t.slot == cy - 3, third, centre)), 3
            )
            y_p3 = t.turn(jnp.where(t.slot < 2, side, jnp.where(t.slot == 2, third, centre)), -3)
            beyond = zst[q, pl.ds(base, half), :]
            z_m1, z_m2, z_m3 = (t.z_down(centre, beyond, k) for k in (1, 2, 3))
            z_p1, z_p2, z_p3 = (t.z_up(centre, beyond, k) for k in (1, 2, 3))
            dx = first_diff(x_m2, x_m1, x_p1, x_p2)
            dy = first_diff(y_m2, y_m1, y_p1, y_p2)
            grads[q, 0] = dx
            grads[q, 1] = dy
            grads[q, 2] = first_diff(z_m2, z_m1, z_p1, z_p2)
            near = [x_m1 + x_p1, y_m1 + y_p1, z_m1 + z_p1]
            far = [x_m2 + x_p2, y_m2 + y_p2, z_m2 + z_p2]
            outer = (x_m3 + x_p3) + (y_m3 + y_p3) + (z_m3 + z_p3)
            damped[q] = (DISSIPATION / 64.0) * (
                outer - 6.0 * (far[0] + far[1] + far[2]) + 15.0 * (near[0] + near[1] + near[2])
                - 60.0 * centre
            )
            if q < CURVED:
                for s, d in ((0, 0), (3, 1), (5, 2)):
                    seconds[q, s] = (1.0 / 12.0) * (16.0 * near[d] - far[d] - 30.0 * centre)
                s_m, s_c, s_p = sides[q, p - 1], side, sides[q, p + 1]
                dx_side = first_diff(s_m, t.odd_swapped(s_m, s_c), t.odd_swapped(s_c, s_p), s_p)
                seconds[q, 1] = first_diff(
                    t.y_down(dx, dx_side, 2),
                    t.y_down(dx, dx_side, 1),
                    t.y_up(dx, dx_side, 1),
                    t.y_up(dx, dx_side, 2),
                )
                b_m, b_c, b_p = pairs_z[q, p - 1], pairs_z[q, p], pairs_z[q, p + 1]
                dx_z = first_diff(b_m, t.odd(b_m, b_c), t.odd(b_c, b_p), b_p)
                b_s = sides_z[q, p - 1]
                dy_z = first_diff(
                    t.y_down(b_c, b_s, 2),
                    t.y_down(b_c, b_s, 1),
                    t.y_up(b_c, b_s, 1),
                    t.y_up(b_c, b_s, 2),
                )
                for s, inside, outside in ((2, dx, dx_z), (4, dy, dy_z)):
                    seconds[q, s] = first_diff(
                        t.z_down(inside, outside, 2),
                        t.z_down(inside, outside, 1),
                        t.z_up(inside, outside, 1),
                        t.z_up(inside, outside, 2),
                    )

        def value(q):
            return pairs[q, p + 1]

        def fluid_value(q):
            return fl[q, pl.ds(base, half), :]

        conformal, lapse = value(0), value(7)
        over_chi = 1.0 / conformal
        metric = symmetric([value(1 + s) for s in range(6)])
        shift = [value(8 + i) for i in range(3)]
        extrinsic, theta = value(11), value(21)
        traceless = symmetric([value(12 + s) for s in range(6)])
        connection = [value(18 + i) for i in range(3)]
        inverse = inverse_metric(metric)
        grad = [[grads[q, k] for k in range(3)] for q in range(fields)]
        chi_grad, lapse_grad = grad[0], grad[7]
        shift_grad = [[grad[8 + i][k] for i in range(3)] for k in range(3)]
        trace_k = extrinsic + 2.0 * theta

        stress = symmetric([tensors[p - 1, s] for s in range(6)])
        held = [fluid_value(q) for q in range(5)]
        shrink = volume_over(conformal)
        energy = held[4] + held[0]
        third_k = trace_k * (1.0 / 3.0)
        curved = [
            [
                (traceless[i][j] + metric[i][j] * third_k) if i <= j else None for j in range(3)
            ]
            for i in range(3)
        ]
        work = (
            stress[0][0] * curved[0][0]
            + stress[1][1] * curved[1][1]
            + stress[2][2] * curved[2][2]
            + 2.0
            * (
                stress[0][1] * curved[0][1]
                + stress[0][2] * curved[0][2]
                + stress[1][2] * curved[1][2]
            )
        )
        rates = [tensors[p - 1, 6 + q] for q in range(5)]
        for i in range(3):
            rates[1 + i] = (
                rates[1 + i]
                - energy * lapse_grad[i]
                + total([held[1 + k] * grad[8 + k][i] for k in range(3)])
            )
        rates[4] = (
            rates[4] + lapse * work * over_chi / shrink - dot(held[1:4], lapse_grad)
        )
        for q in range(5):
            fl_out[q, pl.ds(base, half), :] = held[q] + dt * rates[q]
        density = energy * shrink
        momentum = [held[1 + i] * shrink for i in range(3)]

        lowered = [[[None] * 3 for _ in range(3)] for _ in range(3)]
        for i in range(3):
            for j in range(3):
                for k in range(j, 3):
                    got = 0.5 * (
                        grad[1 + slot_of(i, k)][j]
                        + grad[1 + slot_of(i, j)][k]
                        - grad[1 + slot_of(j, k)][i]
                    )
                    lowered[i][j][k] = lowered[i][k][j] = got
        raised = [[[None] * 3 for _ in range(3)] for _ in range(3)]
        for i in range(3):
            for j in range(3):
                for k in range(j, 3):
                    got = total([inverse[i][l] * lowered[l][j][k] for l in range(3)])
                    raised[i][j][k] = raised[i][k][j] = got
        contracted = [trace_with(inverse, raised[i]) for i in range(3)]

        def hessian(q):
            return symmetric([seconds[q, s] for s in range(6)])

        def second_cov(q, slope):
            return symmetric(
                [
                    seconds[q, s] - total([raised[k][i][j] * slope[k] for k in range(3)])
                    for s, (i, j) in enumerate(INDEX_PAIRS)
                ]
            )

        chi_cov = second_cov(0, chi_grad)
        chi_lap = trace_with(inverse, chi_cov)
        raised_chi = [dot(inverse[i], chi_grad) for i in range(3)]
        chi_square = dot(raised_chi, chi_grad)
        cross_term = dot(raised_chi, lapse_grad)
        half_chi = 0.5 * over_chi
        plain_cov = second_cov(7, lapse_grad)
        lapse_cov = symmetric(
            [
                plain_cov[i][j]
                + (
                    chi_grad[i] * lapse_grad[j]
                    + chi_grad[j] * lapse_grad[i]
                    - metric[i][j] * cross_term
                )
                * half_chi
                for i, j in INDEX_PAIRS
            ]
        )
        lapse_lap = conformal * trace_with(inverse, lapse_cov)

        mixed = [
            [[dot(inverse[l], lowered[k][j]) for j in range(3)] for k in range(3)]
            for l in range(3)
        ]
        quarter_sq = half_chi * half_chi
        metric_factor = chi_lap * half_chi - 3.0 * chi_square * quarter_sq
        ricci = []
        for i, j in INDEX_PAIRS:
            second_part = -0.5 * trace_with(inverse, hessian(1 + slot_of(i, j)))
            connection_part = 0.5 * total(
                [metric[k][i] * grad[18 + k][j] + metric[k][j] * grad[18 + k][i] for k in range(3)]
            )
            contracted_part = 0.5 * total(
                [contracted[k] * (lowered[i][j][k] + lowered[j][i][k]) for k in range(3)]
            )
            if i == j:
                quadratic = total(
                    [
                        raised[k][l][i] * (2.0 * mixed[l][i][k] + mixed[l][k][i])
                        for k in range(3)
                        for l in range(3)
                    ]
                )
            else:
                quadratic = total(
                    [
                        raised[k][l][i] * (mixed[l][j][k] + mixed[l][k][j])
                        + raised[k][l][j] * mixed[l][i][k]
                        for k in range(3)
                        for l in range(3)
                    ]
                )
            conformal_part = (
                chi_cov[i][j] * half_chi
                + metric[i][j] * metric_factor
                - chi_grad[i] * chi_grad[j] * quarter_sq
            )
            ricci.append(
                second_part + connection_part + contracted_part + quadratic + conformal_part
            )
        ricci = symmetric(ricci)
        ricci_scalar = conformal * trace_with(inverse, ricci)
        stress_trace = conformal * trace_with(inverse, stress)

        up_a = [
            [total([inverse[i][k] * traceless[k][j] for k in range(3)]) for j in range(3)]
            for i in range(3)
        ]
        raised_a = symmetric(
            [total([up_a[i][l] * inverse[j][l] for l in range(3)]) for i, j in INDEX_PAIRS]
        )
        a_square = trace_with(traceless, raised_a)
        shift_div = shift_grad[0][0] + shift_grad[1][1] + shift_grad[2][2]
        two_thirds_div = (2.0 / 3.0) * shift_div

        def finish(q, rate):
            rate = rate + dot(shift, grad[q]) + damped[q]
            st_out[q, pl.ds(base, half), :] = value(q) + dt * rate

        finish(0, (2.0 / 3.0) * conformal * (lapse * trace_k - shift_div))
        finish(7, -2.0 * lapse * extrinsic)
        for i in range(3):
            finish(8 + i, 0.75 * connection[i] - SHIFT_DAMPING * shift[i])
        finish(
            11,
            lapse
            * (
                a_square
                + trace_k * trace_k * (1.0 / 3.0)
                + FOUR_PI * (stress_trace + density)
                + KAPPA_ONE * theta
            )
            - lapse_lap,
        )
        source = symmetric(
            [
                lapse * (ricci[i][j] - 2.0 * FOUR_PI * stress[i][j]) - lapse_cov[i][j]
                for i, j in INDEX_PAIRS
            ]
        )
        third_trace = trace_with(inverse, source) * (1.0 / 3.0)
        for s, (i, j) in enumerate(INDEX_PAIRS):
            finish(
                1 + s,
                total(
                    [
                        metric[i][k] * shift_grad[j][k] + metric[j][k] * shift_grad[i][k]
                        for k in range(3)
                    ]
                )
                - metric[i][j] * two_thirds_div
                - 2.0 * lapse * traceless[i][j],
            )
            product = total([traceless[i][k] * up_a[k][j] for k in range(3)])
            finish(
                12 + s,
                total(
                    [
                        traceless[i][k] * shift_grad[j][k] + traceless[j][k] * shift_grad[i][k]
                        for k in range(3)
                    ]
                )
                - traceless[i][j] * two_thirds_div
                + conformal * (source[i][j] - metric[i][j] * third_trace)
                + lapse * (trace_k * traceless[i][j] - 2.0 * product),
            )
        for i in range(3):
            bracket = (
                trace_with(raised_a, raised[i])
                - 1.5 * dot(raised_a[i], chi_grad) * over_chi
                - dot(inverse[i], [2.0 * grad[11][j] + grad[21][j] for j in range(3)]) * (1.0 / 3.0)
                - 2.0 * FOUR_PI * dot(inverse[i], momentum)
            )
            spread = [
                seconds[8, slot_of(j, 0)] + seconds[9, slot_of(j, 1)] + seconds[10, slot_of(j, 2)]
                for j in range(3)
            ]
            finish(
                18 + i,
                contracted[i] * two_thirds_div
                - total([contracted[j] * shift_grad[j][i] for j in range(3)])
                + trace_with(inverse, hessian(8 + i))
                + dot(inverse[i], spread) * (1.0 / 3.0)
                - 2.0 * dot(raised_a[i], lapse_grad)
                + 2.0
                * lapse
                * (bracket - KAPPA_ONE * (connection[i] - contracted[i])),
            )
        finish(
            21,
            0.5
            * lapse
            * (
                ricci_scalar
                - a_square
                + (2.0 / 3.0) * trace_k * trace_k
                - 4.0 * FOUR_PI * density
            )
            - 2.0 * KAPPA_ONE * lapse * theta,
        )
        return carry

    lax.fori_loop(0, own, pair_step, 0)


def per_device(spacetime, fluid):
    fields, cx, cy, cz = spacetime.shape
    rows = cx * cy
    st = spacetime.reshape(fields, rows, cz)
    fl = fluid.reshape(FLUID, rows, cz)
    sizes = [lax.axis_size(a) for a in ("gx", "gy", "gz")]
    tile = (2 * cy, cz)
    f32 = jnp.float32

    def shape(*dims):
        return jax.ShapeDtypeStruct(dims, f32)

    def beyond(cells):
        n = sizes[2]
        after = lax.ppermute(cells, "gz", [((i + 1) % n, i) for i in range(n)])
        if n == 2:
            return after
        before = lax.ppermute(cells, "gz", [(i, (i + 1) % n) for i in range(n)])
        lane = lax.broadcasted_iota(jnp.int32, cells.shape, 2)
        return jnp.where(lane < cz // 2, after, before)

    params = pltpu.CompilerParams(vmem_limit_bytes=48 * 1024 * 1024)
    zst, zfl = beyond(st), beyond(fl)
    st, fl = pl.pallas_call(
        stage_kernel,
        out_shape=[shape(*st.shape), shape(*fl.shape)],
        in_specs=[pl.BlockSpec(memory_space=pl.ANY)] * 2,
        scratch_shapes=[pltpu.SemaphoreType.DMA((2,))],
        compiler_params=params,
        name="stage",
    )(st, fl)
    face = shape(face_tiles(fields), *tile)
    corner = shape(CURVED + FLUID + 1, *tile)
    lane_row = shape(1, cz)
    x_low, x_high, y_low, y_high, top = pl.pallas_call(
        pack_kernel, out_shape=[face] * 4 + [lane_row], compiler_params=params, name="pack"
    )(st, fl, zst, zfl)

    def move(cells, dx, dy):
        nx, ny = sizes[0], sizes[1]
        hops = [
            (i * ny + j, ((i + dx) % nx) * ny + (j + dy) % ny) for i in range(nx) for j in range(ny)
        ]
        return lax.ppermute(cells, ("gx", "gy"), hops)

    short = sizes[0] <= 4 and sizes[1] <= 4 and sizes[2] <= 2
    x_above = move(x_low, -1, 0)
    x_below = move(x_high, 1, 0)
    top_two = move(top, 2, 0) if short and sizes[0] == 4 else top
    y_above = move(y_low, 0, -1)
    y_below = move(y_high, 0, 1)
    c_low, c_high, line_top = pl.pallas_call(
        relay_kernel,
        out_shape=[corner, corner, lane_row],
        compiler_params=params,
        name="relay",
    )(x_below, x_above, top, top_two)
    c_above = move(c_low, 0, -1)
    c_below = move(c_high, 0, 1)
    if not short:
        line_two = lax.pmax(line_top, ("gx", "gy", "gz"))
    else:
        line_two = move(line_top, 0, 2) if sizes[1] == 4 else line_top
    own = cx // 2
    st_next, fl_next = pl.pallas_call(
        main_kernel,
        out_shape=[shape(*st.shape), shape(*fl.shape)],
        scratch_shapes=[
            pltpu.VMEM((fields, own + 4) + tile, f32),
            pltpu.VMEM((fields, own + 2) + tile, f32),
            pltpu.VMEM((fields, own) + tile, f32),
            pltpu.VMEM((CURVED, own + 2) + tile, f32),
            pltpu.VMEM((CURVED, own) + tile, f32),
            pltpu.VMEM((fields, 3) + tile, f32),
            pltpu.VMEM((CURVED, 6) + tile, f32),
            pltpu.VMEM((fields,) + tile, f32),
            pltpu.VMEM((own, 11) + tile, f32),
        ],
        compiler_params=params,
        name="update",
    )(st, fl, zst, zfl, x_below, x_above, y_below, y_above, c_below, c_above, line_top, line_two)
    return st_next.reshape(spacetime.shape), fl_next.reshape(fluid.shape)


def solution(mesh):
    spec = P(None, "gx", "gy", "gz")
    return jax.shard_map(
        per_device, mesh=mesh, in_specs=(spec, spec), out_specs=(spec, spec), check_vma=False
    )
```

```python
import functools
import math

import jax
import jax.numpy as jnp
from jax import lax
from jax.experimental import pallas as pl
from jax.experimental.pallas import tpu as pltpu
from jax.sharding import PartitionSpec as P

RECOVERY_STEPS = 4
INDEX_PAIRS = ((0, 0), (0, 1), (0, 2), (1, 1), (1, 2), (2, 2))
COURANT = 0.25
DISSIPATION = 0.2
KAPPA_ONE = 0.02
SHIFT_DAMPING = 1.0
SPEED_CAP = 0.99
PRESSURE_FLOOR = 0.01
FOUR_PI = 4.0 * math.pi

CURVED = 11
FLUID = 8


def total(pieces):
    summed = pieces[0]
    for member in pieces[1:]:
        summed = summed + member
    return summed


def dot(first_vec, second_vec):
    return total([first_vec[i] * second_vec[i] for i in range(3)])


def slot_of(i, j):
    return INDEX_PAIRS.index((min(i, j), max(i, j)))


def symmetric(entries):
    return [[entries[slot_of(i, j)] for j in range(3)] for i in range(3)]


def trace_with(inverse, tensor):
    return (
        inverse[0][0] * tensor[0][0]
        + inverse[1][1] * tensor[1][1]
        + inverse[2][2] * tensor[2][2]
        + 2.0
        * (
            inverse[0][1] * tensor[0][1]
            + inverse[0][2] * tensor[0][2]
            + inverse[1][2] * tensor[1][2]
        )
    )


def inverse_metric(metric):
    cofactor = [
        metric[1][1] * metric[2][2] - metric[1][2] * metric[1][2],
        metric[0][2] * metric[1][2] - metric[0][1] * metric[2][2],
        metric[0][1] * metric[1][2] - metric[0][2] * metric[1][1],
        metric[0][0] * metric[2][2] - metric[0][2] * metric[0][2],
        metric[0][1] * metric[0][2] - metric[0][0] * metric[1][2],
        metric[0][0] * metric[1][1] - metric[0][1] * metric[0][1],
    ]
    determinant = (
        metric[0][0] * cofactor[0] + metric[0][1] * cofactor[1] + metric[0][2] * cofactor[2]
    )
    over = 1.0 / determinant
    return symmetric([c * over for c in cofactor])


class Tile:
    def __init__(self, cy, cz):
        self.cy, self.rows, self.lanes = cy, 2 * cy, cz
        shape = (self.rows, cz)
        self.row = lax.broadcasted_iota(jnp.int32, shape, 0)
        self.lane = lax.broadcasted_iota(jnp.int32, shape, 1)
        self.slot = lax.rem(self.row, cy)

    def turn(self, tile, amount):
        amount = amount % self.rows
        return tile if amount == 0 else pltpu.roll(tile, amount, 0)

    def spin(self, tile, amount):
        amount = amount % self.lanes
        return tile if amount == 0 else pltpu.roll(tile, amount, 1)

    def swap(self, tile):
        return self.turn(tile, self.cy)

    def odd(self, a, b):
        return self.turn(jnp.where(self.row < self.cy, b, a), self.cy)

    def odd_swapped(self, a, b):
        return self.turn(jnp.where(self.row < self.cy, a, b), self.cy)

    def y_up(self, main, beyond, k):
        return self.turn(jnp.where(self.slot < k, beyond, main), -k)

    def y_down(self, main, beyond, k):
        return self.turn(jnp.where(self.slot >= self.cy - k, beyond, main), k)

    def z_up(self, main, beyond, k):
        return self.spin(jnp.where(self.lane < k, beyond, main), -k)

    def z_down(self, main, beyond, k):
        return self.spin(jnp.where(self.lane >= self.lanes - k, beyond, main), k)

    def join_low(self, u, v):
        return jnp.where(self.slot < 2, self.swap(u), self.turn(v, 2))

    def join_high(self, u, v):
        return jnp.where(self.slot >= self.cy - 2, self.swap(u), self.turn(self.swap(v), -2))

    def part_first(self, from_above, from_below):
        return jnp.where(self.slot < 2, from_above, from_below)

    def part_second(self, from_above, from_below):
        return self.turn(jnp.where(self.slot < 2, from_below, from_above), 2)


def edge_list(tiles):
    fields = next(n for n in range(tiles) if face_tiles(n) == tiles)
    return list(range(CURVED)) + list(range(fields, fields + FLUID))


def face_tiles(fields):
    return fields + FLUID + len(pairs_of(third_list(fields))) + 1


def third_list(fields):
    return list(range(fields + 1))


def pairs_of(items):
    return [(items[i], items[min(i + 1, len(items) - 1)]) for i in range(0, len(items), 2)]


def top_speed(st):
    inverse = inverse_metric(symmetric([st[1 + s] for s in range(6)]))
    scale = 2.0 * st[7] * st[0]
    speeds = [jnp.abs(st[8 + d]) + jnp.sqrt(scale * inverse[d][d]) for d in range(3)]
    top = jnp.maximum(jnp.maximum(speeds[0], speeds[1]), speeds[2])
    return jnp.max(jnp.max(top, axis=1, keepdims=True), axis=0, keepdims=True)


def pack_kernel(cells, zst, zfl, *outs):
    fields, rows, lanes = zst.shape
    st, fl = cells.at[0:fields], cells.at[fields : fields + FLUID]
    cy = rows // 4
    t = Tile(cy, lanes)
    x_low, x_high, y_low, y_high, top_out = outs
    half = t.rows

    def own(ref, q):
        return [ref[q, 0:half, :], ref[q, half : 2 * half, :]]

    tiles, beyond = [], []
    for q in range(fields):
        tiles.append(own(st, q))
        beyond.append(own(zst, q) if q < CURVED else None)
    for q in range(FLUID - 1):
        tiles.append(own(fl, q))
        beyond.append(own(zfl, q))
    along, along_z = own(fl, FLUID - 1), own(zfl, FLUID - 1)
    tiles.append([0.5 * (along[p] + t.z_up(along[p], along_z[p], 1)) for p in range(2)])
    beyond.append([0.5 * (along_z[p] + t.z_up(along_z[p], along[p], 1)) for p in range(2)])

    packed = [None] * 4
    place = 0
    for q, (first, second) in enumerate(tiles):
        x_low[q] = first
        x_high[q] = second
        y_low[q] = t.join_low(first, second)
        y_high[q] = t.join_high(first, second)
        if beyond[q] is not None:
            zf, zs = beyond[q]
            for m, piece in enumerate((zf, zs, t.join_low(zf, zs), t.join_high(zf, zs))):
                piece = t.spin(piece, 4 * place + 2)
                packed[m] = (
                    piece if place == 0 else jnp.where(t.lane < 4 * place, packed[m], piece)
                )
            place += 1
    for n, (a, b) in enumerate(pairs_of(third_list(fields))):
        slot = fields + FLUID + n
        xa, xb = (tiles[q if q < fields else fields + 5] for q in (a, b))
        x_low[slot] = jnp.where(t.row < cy, xa[1], t.swap(xb[1]))
        x_high[slot] = jnp.where(t.row < cy, t.swap(xb[0]), xa[0])
        ya, yb = (tiles[q if q < fields else fields + 6] for q in (a, b))
        w = [t.swap(ya[0]), t.swap(ya[1]), t.swap(yb[0]), t.swap(yb[1])]
        s = t.slot
        y_low[slot] = jnp.where(
            s == 2,
            w[0],
            jnp.where(s == 3, t.turn(w[1], 1), jnp.where(s == 0, t.turn(w[2], -2), t.turn(w[3], -1))),
        )
        y_high[slot] = jnp.where(
            s == 1,
            w[0],
            jnp.where(s == 0, t.turn(w[1], -1), jnp.where(s == 3, t.turn(w[2], 2), t.turn(w[3], 1))),
        )
    top = jnp.maximum(top_speed(st), top_speed(zst))
    top_out[...] = jnp.broadcast_to(top, top_out.shape)
    last = x_low.shape[0] - 1
    for out, piece in zip((x_low, x_high, y_low, y_high), packed):
        out[last] = jnp.where(t.lane < 4 * place, piece, top)


def relay_kernel(x_below, x_above, y_below, top, top_two, to_low, to_high, line_top):
    cy, lanes = x_below.shape[1] // 2, x_below.shape[2]
    t = Tile(cy, lanes)
    last = x_below.shape[0] - 1
    line = jnp.maximum(top[...], top_two[...])
    for beside in (x_below, x_above, y_below):
        line = jnp.maximum(line, beside[last, 0:1, lanes - 1 : lanes])
    line_top[...] = line
    edge = edge_list(x_below.shape[0])
    for n, q in enumerate(edge + [last]):
        low = t.join_low(x_below[q], x_above[q])
        high = t.join_high(x_below[q], x_above[q])
        if q == last:
            low = jnp.where(t.lane < 4 * len(edge), low, line)
            high = jnp.where(t.lane < 4 * len(edge), high, line)
        to_low[n] = low
        to_high[n] = high


def limited(a, b):
    return jnp.maximum(jnp.minimum(a, b), 0.0) + jnp.minimum(jnp.maximum(a, b), 0.0)


def recover(conserved, magnetic):
    density = conserved[0]
    momenta = conserved[1:4]
    energy = conserved[4] + density
    mom_sq = dot(momenta, momenta)
    mag_sq = dot(magnetic, magnetic)
    cross = dot(momenta, magnetic)
    cross_sq = cross * cross

    def state(z):
        grown = z + mag_sq
        over = 1.0 / (z * grown)
        speed_sq = (mom_sq * z * z + cross_sq * (2.0 * z + mag_sq)) * over * over
        kept = 1.0 - jnp.minimum(speed_sq, SPEED_CAP)
        rest = density * jnp.sqrt(kept)
        return kept, rest, 0.5 * (z * kept - rest), grown * over

    z = jnp.maximum(energy - 0.5 * mag_sq, density)
    for _ in range(RECOVERY_STEPS):
        kept, rest, pressure, over_z = state(z)
        residual = (
            z
            + mag_sq
            - pressure
            - 0.5 * mag_sq * kept
            - 0.5 * cross_sq * over_z * over_z
            - energy
        )
        z = jnp.maximum(z - residual / (1.0 - 0.5 * kept), density)
    kept, rest, pressure, over_z = state(z)
    pressure = jnp.maximum(pressure, PRESSURE_FLOOR * rest)
    scale = lax.rsqrt(kept) / (z + mag_sq)
    along = cross * over_z
    four_vel = [scale * (momenta[i] + along * magnetic[i]) for i in range(3)]
    return [rest, pressure] + four_vel


def stress_parts(rest, pressure, u, magnetic):
    lorentz_sq = 1.0 + dot(u, u)
    over = lax.rsqrt(lorentz_sq)
    over_sq = over * over
    time_b = dot(u, magnetic)
    grown_b = [magnetic[i] + time_b * u[i] for i in range(3)]
    b_square = (dot(magnetic, magnetic) + time_b * time_b) * over_sq
    enthalpy = rest + 2.0 * pressure
    inertia = enthalpy + b_square
    return lorentz_sq, over, over_sq, time_b, grown_b, b_square, enthalpy, inertia


def face_state(rest, pressure, u, magnetic, d):
    lorentz_sq, over, over_sq, time_b, grown_b, b_square, enthalpy, inertia = stress_parts(
        rest, pressure, u, magnetic
    )
    total_pressure = pressure + 0.5 * b_square
    lorentz = lorentz_sq * over
    density = rest * lorentz
    carried = inertia * lorentz
    time_over = time_b * over
    conserved = [density]
    conserved += [carried * u[j] - time_over * grown_b[j] for j in range(3)]
    conserved += [inertia * lorentz_sq - total_pressure - time_b * time_b - density]
    mass_flux = rest * u[d]
    flux = [mass_flux]
    pushed = inertia * u[d]
    b_over = grown_b[d] * over_sq
    for j in range(3):
        flux_j = pushed * u[j] - b_over * grown_b[j]
        flux.append(flux_j + total_pressure if j == d else flux_j)
    flux.append(carried * u[d] - time_over * grown_b[d] - mass_flux)
    ratio = 1.0 / (enthalpy * inertia)
    sound_sq = 2.0 * pressure * inertia * ratio
    alfven_sq = b_square * enthalpy * ratio
    fast_sq = sound_sq + alfven_sq - sound_sq * alfven_sq
    slow = 1.0 - fast_sq
    velocity = u[d] * over
    rest_part = 1.0 - dot(u, u) * over_sq * fast_sq
    spread = jnp.sqrt(fast_sq * over_sq * (rest_part - velocity * velocity * slow))
    fastest = (jnp.abs(velocity * slow) + spread) / rest_part
    return conserved, flux, fastest


def face_flux(left, right, normal, weight, d):
    sides = []
    for state in (left, right):
        magnetic = [normal if i == d else state[5 + i] for i in range(3)]
        sides.append(face_state(state[0], state[1], state[2:5], magnetic, d))
    (cons_l, flux_l, fast_l), (cons_r, flux_r, fast_r) = sides
    signal = jnp.maximum(fast_l, fast_r)
    scale = 0.5 * weight
    return [scale * (flux_l[q] + flux_r[q] - signal * (cons_r[q] - cons_l[q])) for q in range(5)]


def volume_over(conformal):
    return conformal * jnp.sqrt(conformal)


def first_diff(down_two, down, up, up_two):
    return (8.0 / 12.0) * (up - down) + (1.0 / 12.0) * (down_two - up_two)


def main_kernel(
    cells, zst, zfl, x_below, y_below, x_above, y_above, c_below, c_above, line_two, line_top,
    st_out, fl_out, pairs, sides, thirds, pairs_z, sides_z, grads, seconds, damped, tensors,
):
    fields, rows, lanes = zst.shape
    st, fl = cells.at[0:fields], cells.at[fields : fields + FLUID]
    cy = rows // 4
    t = Tile(cy, lanes)
    half = t.rows
    own = rows // half

    def third_place(q):
        return fields + FLUID + q // 2, q % 2

    def beside(q, p):
        if p == 1:
            return t.part_first(y_above[q], y_below[q])
        return t.part_second(y_above[q], y_below[q])

    edge = edge_list(x_below.shape[0])

    def corner(q, p):
        place = edge.index(q) if q is not None else len(edge)
        part = t.part_first if p == 0 else t.part_second
        return part(c_above[place], c_below[place])

    def x_third(q, upper):
        tile, which = third_place(q)
        found = x_above[tile] if upper else x_below[tile]
        return t.swap(found) if which else found

    def y_third(q, p):
        tile, which = third_place(q)
        above, below = y_above[tile], y_below[tile]
        turn_above, turn_below = ((0, 0), (-1, 1), (2, -2), (1, -1))[2 * which + p - 1]
        return jnp.where(t.slot == 2, t.turn(above, turn_above), t.turn(below, turn_below))

    last = x_below.shape[0] - 1
    z_xb, z_xa = x_below[last], x_above[last]
    z_y = [
        t.part_first(y_above[last], y_below[last]),
        t.part_second(y_above[last], y_below[last]),
    ]

    def z_place(q):
        return 4 * edge.index(q) + 2

    def rows_of(ref, q, p):
        return ref[q, (p - 1) * half : p * half, :]

    for q in range(fields):
        pairs[q, 0] = x_third(q, False)
        pairs[q, 1] = x_below[q]
        for p in range(1, own + 1):
            pairs[q, 1 + p] = rows_of(st, q, p)
            sides[q, p] = beside(q, p)
            thirds[q, p - 1] = y_third(q, p)
        pairs[q, 2 + own] = x_above[q]
        pairs[q, 3 + own] = x_third(q, True)
        if q < CURVED:
            sides[q, 0] = corner(q, 0)
            sides[q, own + 1] = corner(q, own + 1)
            pairs_z[q, 0] = t.spin(z_xb, -z_place(q))
            pairs_z[q, own + 1] = t.spin(z_xa, -z_place(q))
            for p in range(1, own + 1):
                pairs_z[q, p] = rows_of(zst, q, p)
                sides_z[q, p - 1] = t.spin(z_y[p - 1], -z_place(q))

    span = range(own + 2)
    inner = range(1, own + 1)

    def plane(q):
        if q < fields:
            return (
                [pairs[q, 1 + p] for p in span],
                [sides[q, p] for p in span],
                [pairs_z[q, p] for p in span],
                [sides_z[q, p - 1] if 1 <= p <= own else None for p in span],
            )
        f = q - fields
        v = [x_below[q]] + [rows_of(fl, f, p) for p in inner] + [x_above[q]]
        h = [corner(q, 0)] + [beside(q, p) for p in inner] + [corner(q, own + 1)]
        place = z_place(q)
        vz = [t.spin(z_xb, -place)] + [rows_of(zfl, f, p) for p in inner] + [t.spin(z_xa, -place)]
        hz = [None] + [t.spin(z_y[p - 1], -place) for p in inner] + [None]
        return v, h, vz, hz

    def corner_z(q, p):
        return t.spin(corner(None, p), -z_place(q))

    v, h, vz, hz = plane(fields + 5)
    hz[own + 1] = corner_z(fields + 5, own + 1)
    v_next = v[1:] + [x_third(fields, True)]
    face_x = v
    bx = (
        [0.5 * (v[p] + t.odd(v[p], v_next[p])) for p in span],
        [0.5 * (h[p] + t.odd_swapped(h[p], h[min(p + 1, own + 1)])) for p in span],
        [0.5 * (vz[p] + t.odd(vz[p], vz[min(p + 1, own + 1)])) for p in span],
        [None] + [0.5 * (hz[p] + t.odd_swapped(hz[p], hz[p + 1])) for p in inner] + [None],
    )
    v, h, vz, hz = plane(fields + 6)
    hz[0] = corner_z(fields + 6, 0)
    hz[own + 1] = corner_z(fields + 6, own + 1)
    face_y = v, h
    full = [
        jnp.where(t.slot == 2, y_third(fields, p), h[p]) if 1 <= p <= own else h[p] for p in span
    ]
    by = (
        [0.5 * (v[p] + t.y_up(v[p], h[p], 1)) for p in span],
        [0.5 * (h[p] + t.y_up(full[p], v[p], 1)) for p in span],
        [0.5 * (vz[p] + t.y_up(vz[p], hz[p], 1)) for p in span],
        [None] + [0.5 * (hz[p] + t.y_up(hz[p], vz[p], 1)) for p in inner] + [None],
    )
    v, h, vz, hz = plane(fields + 7)
    for p in inner:
        raw, raw_z = rows_of(fl, 7, p), rows_of(zfl, 7, p)
        v[p] = 0.5 * (raw + t.z_up(raw, raw_z, 1))
        vz[p] = 0.5 * (raw_z + t.z_up(raw_z, raw, 1))
    bz = (v, h, vz, hz)

    chi, alpha = plane(0), plane(7)
    cons = [plane(fields + q) for q in range(5)]
    centred = [bx, by, bz]
    spots = [(0, p) for p in span] + [(1, p) for p in span] + [(2, p) for p in span]
    spots += [(3, p) for p in inner]
    prims = [[[None] * (own + 2) for _ in range(4)] for _ in range(8)]
    electric = [[[None] * (own + 2) for _ in range(4)] for _ in range(3)]
    batch = 4
    for start in range(0, len(spots), batch):
        group = spots[start : start + batch]

        def gather(planes):
            return jnp.concatenate([planes[k][p] for k, p in group], axis=0)

        shrink = volume_over(gather(chi))
        mag_raw = [gather(centred[i]) for i in range(3)]
        mag = [m * shrink for m in mag_raw]
        values = recover([gather(c) * shrink for c in cons], mag)
        u = values[2:5]
        factor = gather(alpha) * lax.rsqrt(1.0 + dot(u, u))
        field = [
            factor * (u[(i + 2) % 3] * mag_raw[(i + 1) % 3] - u[(i + 1) % 3] * mag_raw[(i + 2) % 3])
            for i in range(3)
        ]
        for n, (k, p) in enumerate(group):
            for i, value in enumerate(values + mag):
                prims[i][k][p] = value[n * half : (n + 1) * half]
            for i in range(3):
                electric[i][k][p] = field[i][n * half : (n + 1) * half]

    hydro = [[None] * (own + 2) for _ in range(5)]

    def weigh(chi_face, alpha_face):
        shrink = volume_over(chi_face)
        return shrink, alpha_face / shrink

    odd_prims = [[t.odd(f[0][p], f[0][min(p + 1, own + 1)]) for p in span] for f in prims]
    fluxes = [None]
    odd_chi = [t.odd(chi[0][p], chi[0][min(p + 1, own + 1)]) for p in span]
    odd_alpha = [t.odd(alpha[0][p], alpha[0][min(p + 1, own + 1)]) for p in span]
    for p in range(1, own + 2):
        left, right = [], []
        for f, o in zip(prims, odd_prims):
            f = f[0]
            here = f[p] - o[p - 1]
            left.append(o[p - 1] + 0.5 * limited(o[p - 1] - f[p - 1], here))
            right.append(f[p] - 0.5 * limited(here, o[p] - f[p]))
        shrink, weight = weigh(
            0.5 * (chi[0][p] + odd_chi[p - 1]), 0.5 * (alpha[0][p] + odd_alpha[p - 1])
        )
        fluxes.append(face_flux(left, right, face_x[p] * shrink, weight, 0))
    for p in inner:
        for q in range(5):
            hydro[q][p] = fluxes[p][q] - t.odd(fluxes[p][q], fluxes[p + 1][q])

    for d, kind, up, down in ((1, 1, t.y_up, t.y_down), (2, 2, t.z_up, t.z_down)):
        for p in inner:
            found = []
            for here, there in ((0, kind), (kind, 0)):
                left, right = [], []
                for f in prims:
                    a, b = f[here][p], f[there][p]
                    below = down(a, b, 1)
                    middle = a - below
                    left.append(below + 0.5 * limited(below - down(a, b, 2), middle))
                    right.append(a - 0.5 * limited(middle, up(a, b, 1) - a))
                shrink, weight = weigh(
                    0.5 * (chi[here][p] + down(chi[here][p], chi[there][p], 1)),
                    0.5 * (alpha[here][p] + down(alpha[here][p], alpha[there][p], 1)),
                )
                if d == 1:
                    normal = face_y[0 if here == 0 else 1][p]
                else:
                    normal = rows_of(fl if here == 0 else zfl, 7, p)
                found.append(face_flux(left, right, normal * shrink, weight, d))
            for q in range(5):
                hydro[q][p] = hydro[q][p] + found[0][q] - up(found[0][q], found[1][q], 1)

    ex, ey, ez = electric
    ez_x = [
        [ez[0][p] + t.odd(ez[0][p - 1], ez[0][p]) if p else None for p in span],
        [ez[1][p] + t.odd_swapped(ez[1][p - 1], ez[1][p]) if p else None for p in span],
    ]
    ey_x = [
        [ey[k][p] + t.odd(ey[k][p - 1], ey[k][p]) if p else None for p in span] for k in (0, 2)
    ]
    edge_z = [None] + [ez_x[0][p] + t.y_down(ez_x[0][p], ez_x[1][p], 1) for p in span[1:]]
    edge_z_h = [None] + [ez_x[1][p] + t.y_down(ez_x[1][p], ez_x[0][p], 1) for p in inner]
    edge_y = [None] + [ey_x[0][p] + t.z_down(ey_x[0][p], ey_x[1][p], 1) for p in span[1:]]
    edge_y_z = [None] + [ey_x[1][p] + t.z_down(ey_x[1][p], ey_x[0][p], 1) for p in inner]
    top = jnp.maximum(line_top[...], line_two[...])
    for lines in (c_below, c_above):
        top = jnp.maximum(top, lines[len(edge), 0:1, lanes - 1 : lanes])
    dt = COURANT / top
    for p in inner:
        ex_y = ex[0][p] + t.y_down(ex[0][p], ex[1][p], 1)
        ex_y_h = ex[1][p] + t.y_down(ex[1][p], ex[0][p], 1)
        ex_y_z = ex[2][p] + t.y_down(ex[2][p], ex[3][p], 1)
        ex_y_hz = ex[3][p] + t.y_down(ex[3][p], ex[2][p], 1)
        edge_x = ex_y + t.z_down(ex_y, ex_y_z, 1)
        edge_x_h = ex_y_h + t.z_down(ex_y_h, ex_y_hz, 1)
        edge_x_z = ex_y_z + t.z_down(ex_y_z, ex_y, 1)
        x_rate = (t.z_up(edge_y[p], edge_y_z[p], 1) - edge_y[p]) - (
            t.y_up(edge_z[p], edge_z_h[p], 1) - edge_z[p]
        )
        y_rate = (t.odd(edge_z[p], edge_z[p + 1]) - edge_z[p]) - (
            t.z_up(edge_x, edge_x_z, 1) - edge_x
        )
        z_rate = (t.y_up(edge_x, edge_x_h, 1) - edge_x) - (
            t.odd(edge_y[p], edge_y[p + 1]) - edge_y[p]
        )
        quarter = 0.25 * dt
        for i, rate in enumerate((x_rate, y_rate, z_rate)):
            fl_out[5 + i, (p - 1) * half : p * half, :] = rows_of(fl, 5 + i, p) + quarter * rate
        for q in range(5):
            tensors[p - 1, 6 + q] = hydro[q][p]
        parts = stress_parts(
            prims[0][0][p],
            prims[1][0][p],
            [prims[2 + i][0][p] for i in range(3)],
            [prims[5 + i][0][p] for i in range(3)],
        )
        lorentz_sq, over, over_sq, time_b, grown_b, b_square, enthalpy, inertia = parts
        total_pressure = prims[1][0][p] + 0.5 * b_square
        for s, (i, j) in enumerate(INDEX_PAIRS):
            value = inertia * prims[2 + i][0][p] * prims[2 + j][0][p] - over_sq * (
                grown_b[i] * grown_b[j]
            )
            tensors[p - 1, s] = value + total_pressure if i == j else value

    def pair_step(index, carry):
        p = index + 1
        base = pl.multiple_of(index * half, half)

        for q in range(fields):
            centre = pairs[q, p + 1]
            x_m3 = t.odd(pairs[q, p - 1], pairs[q, p])
            x_m2 = pairs[q, p]
            x_m1 = t.odd(pairs[q, p], centre)
            x_p1 = t.odd(centre, pairs[q, p + 2])
            x_p2 = pairs[q, p + 2]
            x_p3 = t.odd(pairs[q, p + 2], pairs[q, p + 3])
            side, third = sides[q, p], thirds[q, p - 1]
            y_m1, y_m2 = t.y_down(centre, side, 1), t.y_down(centre, side, 2)
            y_p1, y_p2 = t.y_up(centre, side, 1), t.y_up(centre, side, 2)
            y_m3 = t.turn(
                jnp.where(t.slot >= cy - 2, side, jnp.where(t.slot == cy - 3, third, centre)), 3
            )
            y_p3 = t.turn(jnp.where(t.slot < 2, side, jnp.where(t.slot == 2, third, centre)), -3)
            beyond = zst[q, pl.ds(base, half), :]
            z_m1, z_m2, z_m3 = (t.z_down(centre, beyond, k) for k in (1, 2, 3))
            z_p1, z_p2, z_p3 = (t.z_up(centre, beyond, k) for k in (1, 2, 3))
            dx = first_diff(x_m2, x_m1, x_p1, x_p2)
            dy = first_diff(y_m2, y_m1, y_p1, y_p2)
            grads[q, 0] = dx
            grads[q, 1] = dy
            grads[q, 2] = first_diff(z_m2, z_m1, z_p1, z_p2)
            near = [x_m1 + x_p1, y_m1 + y_p1, z_m1 + z_p1]
            far = [x_m2 + x_p2, y_m2 + y_p2, z_m2 + z_p2]
            outer = (x_m3 + x_p3) + (y_m3 + y_p3) + (z_m3 + z_p3)
            damped[q] = (DISSIPATION / 64.0) * (
                outer - 6.0 * (far[0] + far[1] + far[2]) + 15.0 * (near[0] + near[1] + near[2])
                - 60.0 * centre
            )
            if q < CURVED:
                for s, d in ((0, 0), (3, 1), (5, 2)):
                    seconds[q, s] = (1.0 / 12.0) * (16.0 * near[d] - far[d] - 30.0 * centre)
                s_m, s_c, s_p = sides[q, p - 1], side, sides[q, p + 1]
                dx_side = first_diff(s_m, t.odd_swapped(s_m, s_c), t.odd_swapped(s_c, s_p), s_p)
                seconds[q, 1] = first_diff(
                    t.y_down(dx, dx_side, 2),
                    t.y_down(dx, dx_side, 1),
                    t.y_up(dx, dx_side, 1),
                    t.y_up(dx, dx_side, 2),
                )
                b_m, b_c, b_p = pairs_z[q, p - 1], pairs_z[q, p], pairs_z[q, p + 1]
                dx_z = first_diff(b_m, t.odd(b_m, b_c), t.odd(b_c, b_p), b_p)
                b_s = sides_z[q, p - 1]
                dy_z = first_diff(
                    t.y_down(b_c, b_s, 2),
                    t.y_down(b_c, b_s, 1),
                    t.y_up(b_c, b_s, 1),
                    t.y_up(b_c, b_s, 2),
                )
                for s, inside, outside in ((2, dx, dx_z), (4, dy, dy_z)):
                    seconds[q, s] = first_diff(
                        t.z_down(inside, outside, 2),
                        t.z_down(inside, outside, 1),
                        t.z_up(inside, outside, 1),
                        t.z_up(inside, outside, 2),
                    )

        def value(q):
            return pairs[q, p + 1]

        def fluid_value(q):
            return fl[q, pl.ds(base, half), :]

        conformal, lapse = value(0), value(7)
        over_chi = 1.0 / conformal
        metric = symmetric([value(1 + s) for s in range(6)])
        shift = [value(8 + i) for i in range(3)]
        extrinsic, theta = value(11), value(21)
        traceless = symmetric([value(12 + s) for s in range(6)])
        connection = [value(18 + i) for i in range(3)]
        inverse = inverse_metric(metric)
        grad = [[grads[q, k] for k in range(3)] for q in range(fields)]
        chi_grad, lapse_grad = grad[0], grad[7]
        shift_grad = [[grad[8 + i][k] for i in range(3)] for k in range(3)]
        trace_k = extrinsic + 2.0 * theta

        stress = symmetric([tensors[p - 1, s] for s in range(6)])
        held = [fluid_value(q) for q in range(5)]
        shrink = volume_over(conformal)
        energy = held[4] + held[0]
        third_k = trace_k * (1.0 / 3.0)
        curved = [
            [
                (traceless[i][j] + metric[i][j] * third_k) if i <= j else None for j in range(3)
            ]
            for i in range(3)
        ]
        work = (
            stress[0][0] * curved[0][0]
            + stress[1][1] * curved[1][1]
            + stress[2][2] * curved[2][2]
            + 2.0
            * (
                stress[0][1] * curved[0][1]
                + stress[0][2] * curved[0][2]
                + stress[1][2] * curved[1][2]
            )
        )
        rates = [tensors[p - 1, 6 + q] for q in range(5)]
        for i in range(3):
            rates[1 + i] = (
                rates[1 + i]
                - energy * lapse_grad[i]
                + total([held[1 + k] * grad[8 + k][i] for k in range(3)])
            )
        rates[4] = (
            rates[4] + lapse * work * over_chi / shrink - dot(held[1:4], lapse_grad)
        )
        for q in range(5):
            fl_out[q, pl.ds(base, half), :] = held[q] + dt * rates[q]
        density = energy * shrink
        momentum = [held[1 + i] * shrink for i in range(3)]

        lowered = [[[None] * 3 for _ in range(3)] for _ in range(3)]
        for i in range(3):
            for j in range(3):
                for k in range(j, 3):
                    got = 0.5 * (
                        grad[1 + slot_of(i, k)][j]
                        + grad[1 + slot_of(i, j)][k]
                        - grad[1 + slot_of(j, k)][i]
                    )
                    lowered[i][j][k] = lowered[i][k][j] = got
        raised = [[[None] * 3 for _ in range(3)] for _ in range(3)]
        for i in range(3):
            for j in range(3):
                for k in range(j, 3):
                    got = total([inverse[i][l] * lowered[l][j][k] for l in range(3)])
                    raised[i][j][k] = raised[i][k][j] = got
        contracted = [trace_with(inverse, raised[i]) for i in range(3)]

        def hessian(q):
            return symmetric([seconds[q, s] for s in range(6)])

        def second_cov(q, slope):
            return symmetric(
                [
                    seconds[q, s] - total([raised[k][i][j] * slope[k] for k in range(3)])
                    for s, (i, j) in enumerate(INDEX_PAIRS)
                ]
            )

        chi_cov = second_cov(0, chi_grad)
        chi_lap = trace_with(inverse, chi_cov)
        raised_chi = [dot(inverse[i], chi_grad) for i in range(3)]
        chi_square = dot(raised_chi, chi_grad)
        cross_term = dot(raised_chi, lapse_grad)
        half_chi = 0.5 * over_chi
        plain_cov = second_cov(7, lapse_grad)
        lapse_cov = symmetric(
            [
                plain_cov[i][j]
                + (
                    chi_grad[i] * lapse_grad[j]
                    + chi_grad[j] * lapse_grad[i]
                    - metric[i][j] * cross_term
                )
                * half_chi
                for i, j in INDEX_PAIRS
            ]
        )
        lapse_lap = conformal * trace_with(inverse, lapse_cov)

        mixed = [
            [[dot(inverse[l], lowered[k][j]) for j in range(3)] for k in range(3)]
            for l in range(3)
        ]
        quarter_sq = half_chi * half_chi
        metric_factor = chi_lap * half_chi - 3.0 * chi_square * quarter_sq
        ricci = []
        for i, j in INDEX_PAIRS:
            second_part = -0.5 * trace_with(inverse, hessian(1 + slot_of(i, j)))
            connection_part = 0.5 * total(
                [metric[k][i] * grad[18 + k][j] + metric[k][j] * grad[18 + k][i] for k in range(3)]
            )
            contracted_part = 0.5 * total(
                [contracted[k] * (lowered[i][j][k] + lowered[j][i][k]) for k in range(3)]
            )
            if i == j:
                quadratic = total(
                    [
                        raised[k][l][i] * (2.0 * mixed[l][i][k] + mixed[l][k][i])
                        for k in range(3)
                        for l in range(3)
                    ]
                )
            else:
                quadratic = total(
                    [
                        raised[k][l][i] * (mixed[l][j][k] + mixed[l][k][j])
                        + raised[k][l][j] * mixed[l][i][k]
                        for k in range(3)
                        for l in range(3)
                    ]
                )
            conformal_part = (
                chi_cov[i][j] * half_chi
                + metric[i][j] * metric_factor
                - chi_grad[i] * chi_grad[j] * quarter_sq
            )
            ricci.append(
                second_part + connection_part + contracted_part + quadratic + conformal_part
            )
        ricci = symmetric(ricci)
        ricci_scalar = conformal * trace_with(inverse, ricci)
        stress_trace = conformal * trace_with(inverse, stress)

        up_a = [
            [total([inverse[i][k] * traceless[k][j] for k in range(3)]) for j in range(3)]
            for i in range(3)
        ]
        raised_a = symmetric(
            [total([up_a[i][l] * inverse[j][l] for l in range(3)]) for i, j in INDEX_PAIRS]
        )
        a_square = trace_with(traceless, raised_a)
        shift_div = shift_grad[0][0] + shift_grad[1][1] + shift_grad[2][2]
        two_thirds_div = (2.0 / 3.0) * shift_div

        def finish(q, rate):
            rate = rate + dot(shift, grad[q]) + damped[q]
            st_out[q, pl.ds(base, half), :] = value(q) + dt * rate

        finish(0, (2.0 / 3.0) * conformal * (lapse * trace_k - shift_div))
        finish(7, -2.0 * lapse * extrinsic)
        for i in range(3):
            finish(8 + i, 0.75 * connection[i] - SHIFT_DAMPING * shift[i])
        finish(
            11,
            lapse
            * (
                a_square
                + trace_k * trace_k * (1.0 / 3.0)
                + FOUR_PI * (stress_trace + density)
                + KAPPA_ONE * theta
            )
            - lapse_lap,
        )
        source = symmetric(
            [
                lapse * (ricci[i][j] - 2.0 * FOUR_PI * stress[i][j]) - lapse_cov[i][j]
                for i, j in INDEX_PAIRS
            ]
        )
        third_trace = trace_with(inverse, source) * (1.0 / 3.0)
        for s, (i, j) in enumerate(INDEX_PAIRS):
            finish(
                1 + s,
                total(
                    [
                        metric[i][k] * shift_grad[j][k] + metric[j][k] * shift_grad[i][k]
                        for k in range(3)
                    ]
                )
                - metric[i][j] * two_thirds_div
                - 2.0 * lapse * traceless[i][j],
            )
            product = total([traceless[i][k] * up_a[k][j] for k in range(3)])
            finish(
                12 + s,
                total(
                    [
                        traceless[i][k] * shift_grad[j][k] + traceless[j][k] * shift_grad[i][k]
                        for k in range(3)
                    ]
                )
                - traceless[i][j] * two_thirds_div
                + conformal * (source[i][j] - metric[i][j] * third_trace)
                + lapse * (trace_k * traceless[i][j] - 2.0 * product),
            )
        for i in range(3):
            bracket = (
                trace_with(raised_a, raised[i])
                - 1.5 * dot(raised_a[i], chi_grad) * over_chi
                - dot(inverse[i], [2.0 * grad[11][j] + grad[21][j] for j in range(3)]) * (1.0 / 3.0)
                - 2.0 * FOUR_PI * dot(inverse[i], momentum)
            )
            spread = [
                seconds[8, slot_of(j, 0)] + seconds[9, slot_of(j, 1)] + seconds[10, slot_of(j, 2)]
                for j in range(3)
            ]
            finish(
                18 + i,
                contracted[i] * two_thirds_div
                - total([contracted[j] * shift_grad[j][i] for j in range(3)])
                + trace_with(inverse, hessian(8 + i))
                + dot(inverse[i], spread) * (1.0 / 3.0)
                - 2.0 * dot(raised_a[i], lapse_grad)
                + 2.0
                * lapse
                * (bracket - KAPPA_ONE * (connection[i] - contracted[i])),
            )
        finish(
            21,
            0.5
            * lapse
            * (
                ricci_scalar
                - a_square
                + (2.0 / 3.0) * trace_k * trace_k
                - 4.0 * FOUR_PI * density
            )
            - 2.0 * KAPPA_ONE * lapse * theta,
        )
        return carry

    lax.fori_loop(0, own, pair_step, 0)


def per_device(spacetime, fluid):
    fields, cx, cy, cz = spacetime.shape
    rows = cx * cy
    st = spacetime.reshape(fields, rows, cz)
    fl = fluid.reshape(FLUID, rows, cz)
    sizes = [lax.axis_size(a) for a in ("gx", "gy", "gz")]
    tile = (2 * cy, cz)
    f32 = jnp.float32

    def shape(*dims):
        return jax.ShapeDtypeStruct(dims, f32)

    def beyond(cells):
        n = sizes[2]
        after = lax.ppermute(cells, "gz", [((i + 1) % n, i) for i in range(n)])
        if n == 2:
            return after
        before = lax.ppermute(cells, "gz", [(i, (i + 1) % n) for i in range(n)])
        lane = lax.broadcasted_iota(jnp.int32, cells.shape, 2)
        return jnp.where(lane < cz // 2, after, before)

    params = pltpu.CompilerParams(vmem_limit_bytes=48 * 1024 * 1024)
    zst, zfl = beyond(st), beyond(fl)
    cells = jnp.concatenate([st, fl], axis=0)
    face = shape(face_tiles(fields), *tile)
    corner = shape(CURVED + FLUID + 1, *tile)
    lane_row = shape(1, cz)
    x_low, x_high, y_low, y_high, top = pl.pallas_call(
        pack_kernel, out_shape=[face] * 4 + [lane_row], compiler_params=params, name="pack"
    )(cells, zst, zfl)

    def move(cells, dx, dy):
        nx, ny = sizes[0], sizes[1]
        hops = [
            (i * ny + j, ((i + dx) % nx) * ny + (j + dy) % ny) for i in range(nx) for j in range(ny)
        ]
        return lax.ppermute(cells, ("gx", "gy"), hops)

    short = sizes[0] <= 4 and sizes[1] <= 4 and sizes[2] <= 2
    x_below = move(x_high, 1, 0)
    y_below = move(y_high, 0, 1)
    x_above = move(x_low, -1, 0)
    y_above = move(y_low, 0, -1)
    top_two = move(top, 2, 0) if short and sizes[0] == 4 else top
    c_low, c_high, line_top = pl.pallas_call(
        relay_kernel,
        out_shape=[corner, corner, lane_row],
        compiler_params=params,
        name="relay",
    )(x_below, x_above, y_below, top, top_two)
    c_above = move(c_low, 0, -1)
    c_below = move(c_high, 0, 1)
    if not short:
        line_two = lax.pmax(line_top, ("gx", "gy", "gz"))
    else:
        line_two = move(line_top, 0, 2) if sizes[1] == 4 else line_top
    own = cx // 2
    st_next, fl_next = pl.pallas_call(
        main_kernel,
        out_shape=[shape(*st.shape), shape(*fl.shape)],
        scratch_shapes=[
            pltpu.VMEM((fields, own + 4) + tile, f32),
            pltpu.VMEM((fields, own + 2) + tile, f32),
            pltpu.VMEM((fields, own) + tile, f32),
            pltpu.VMEM((CURVED, own + 2) + tile, f32),
            pltpu.VMEM((CURVED, own) + tile, f32),
            pltpu.VMEM((fields, 3) + tile, f32),
            pltpu.VMEM((CURVED, 6) + tile, f32),
            pltpu.VMEM((fields,) + tile, f32),
            pltpu.VMEM((own, 11) + tile, f32),
        ],
        compiler_params=params,
        name="update",
    )(cells, zst, zfl, x_below, y_below, x_above, y_above, c_below, c_above, line_two, line_top)
    return st_next.reshape(spacetime.shape), fl_next.reshape(fluid.shape)


def solution(mesh):
    spec = P(None, "gx", "gy", "gz")
    return jax.shard_map(
        per_device, mesh=mesh, in_specs=(spec, spec), out_specs=(spec, spec), check_vma=False
    )
```

```python
import functools
import math

import jax
import jax.numpy as jnp
from jax import lax
from jax.experimental import pallas as pl
from jax.experimental.pallas import tpu as pltpu
from jax.sharding import PartitionSpec as P

RECOVERY_STEPS = 4
INDEX_PAIRS = ((0, 0), (0, 1), (0, 2), (1, 1), (1, 2), (2, 2))
COURANT = 0.25
DISSIPATION = 0.2
KAPPA_ONE = 0.02
SHIFT_DAMPING = 1.0
SPEED_CAP = 0.99
PRESSURE_FLOOR = 0.01
FOUR_PI = 4.0 * math.pi

CURVED = 11
FLUID = 8


def total(pieces):
    summed = pieces[0]
    for member in pieces[1:]:
        summed = summed + member
    return summed


def dot(first_vec, second_vec):
    return total([first_vec[i] * second_vec[i] for i in range(3)])


def slot_of(i, j):
    return INDEX_PAIRS.index((min(i, j), max(i, j)))


def symmetric(entries):
    return [[entries[slot_of(i, j)] for j in range(3)] for i in range(3)]


def trace_with(inverse, tensor):
    return (
        inverse[0][0] * tensor[0][0]
        + inverse[1][1] * tensor[1][1]
        + inverse[2][2] * tensor[2][2]
        + 2.0
        * (
            inverse[0][1] * tensor[0][1]
            + inverse[0][2] * tensor[0][2]
            + inverse[1][2] * tensor[1][2]
        )
    )


def inverse_metric(metric):
    cofactor = [
        metric[1][1] * metric[2][2] - metric[1][2] * metric[1][2],
        metric[0][2] * metric[1][2] - metric[0][1] * metric[2][2],
        metric[0][1] * metric[1][2] - metric[0][2] * metric[1][1],
        metric[0][0] * metric[2][2] - metric[0][2] * metric[0][2],
        metric[0][1] * metric[0][2] - metric[0][0] * metric[1][2],
        metric[0][0] * metric[1][1] - metric[0][1] * metric[0][1],
    ]
    determinant = (
        metric[0][0] * cofactor[0] + metric[0][1] * cofactor[1] + metric[0][2] * cofactor[2]
    )
    over = 1.0 / determinant
    return symmetric([c * over for c in cofactor])


class Tile:
    def __init__(self, cy, cz):
        self.cy, self.rows, self.lanes = cy, 2 * cy, cz
        shape = (self.rows, cz)
        self.row = lax.broadcasted_iota(jnp.int32, shape, 0)
        self.lane = lax.broadcasted_iota(jnp.int32, shape, 1)
        self.slot = lax.rem(self.row, cy)

    def turn(self, tile, amount):
        amount = amount % self.rows
        return tile if amount == 0 else pltpu.roll(tile, amount, 0)

    def spin(self, tile, amount):
        amount = amount % self.lanes
        return tile if amount == 0 else pltpu.roll(tile, amount, 1)

    def swap(self, tile):
        return self.turn(tile, self.cy)

    def odd(self, a, b):
        return self.turn(jnp.where(self.row < self.cy, b, a), self.cy)

    def odd_swapped(self, a, b):
        return self.turn(jnp.where(self.row < self.cy, a, b), self.cy)

    def y_up(self, main, beyond, k):
        return self.turn(jnp.where(self.slot < k, beyond, main), -k)

    def y_down(self, main, beyond, k):
        return self.turn(jnp.where(self.slot >= self.cy - k, beyond, main), k)

    def z_up(self, main, beyond, k):
        return self.spin(jnp.where(self.lane < k, beyond, main), -k)

    def z_down(self, main, beyond, k):
        return self.spin(jnp.where(self.lane >= self.lanes - k, beyond, main), k)

    def corner_rows(self, side, turn):
        places = ((0, 2), (self.cy - 1, self.cy + 1))[side]
        first, second = [(place + turn) % self.rows for place in places]
        return (self.row == first) | (self.row == second)

    def join_low(self, u, v):
        return jnp.where(self.slot < 2, self.swap(u), self.turn(v, 2))

    def join_high(self, u, v):
        return jnp.where(self.slot >= self.cy - 2, self.swap(u), self.turn(self.swap(v), -2))

    def part_first(self, from_above, from_below):
        return jnp.where(self.slot < 2, from_above, from_below)

    def part_second(self, from_above, from_below):
        return self.turn(jnp.where(self.slot < 2, from_below, from_above), 2)


def edge_list(tiles):
    fields = next(n for n in range(tiles) if face_tiles(n) == tiles)
    return list(range(CURVED)) + list(range(fields, fields + FLUID))


CORNER_TURNS = (0, 1, 4, 5)


def corner_lists(edge):
    faces = edge[CURVED + 5 : CURVED + 7]
    return edge[:CURVED] + faces, edge[CURVED : CURVED + 5] + edge[CURVED + 7 :]


def face_tiles(fields):
    return fields + FLUID + len(pairs_of(third_list(fields))) + 1


def third_list(fields):
    return list(range(fields + 1))


def pairs_of(items):
    return [(items[i], items[min(i + 1, len(items) - 1)]) for i in range(0, len(items), 2)]


def top_speed(st):
    inverse = inverse_metric(symmetric([st[1 + s] for s in range(6)]))
    scale = 2.0 * st[7] * st[0]
    speeds = [jnp.abs(st[8 + d]) + jnp.sqrt(scale * inverse[d][d]) for d in range(3)]
    top = jnp.maximum(jnp.maximum(speeds[0], speeds[1]), speeds[2])
    return jnp.max(jnp.max(top, axis=1, keepdims=True), axis=0, keepdims=True)


def pack_kernel(cells, zst, zfl, *outs):
    fields, rows, lanes = zst.shape
    st, fl = cells.at[0:fields], cells.at[fields : fields + FLUID]
    cy = rows // 4
    t = Tile(cy, lanes)
    x_low, x_high, y_low, y_high, top_out = outs
    half = t.rows

    def own(ref, q):
        return [ref[q, 0:half, :], ref[q, half : 2 * half, :]]

    tiles, beyond = [], []
    for q in range(fields):
        tiles.append(own(st, q))
        beyond.append(own(zst, q) if q < CURVED else None)
    for q in range(FLUID - 1):
        tiles.append(own(fl, q))
        beyond.append(own(zfl, q))
    along, along_z = own(fl, FLUID - 1), own(zfl, FLUID - 1)
    tiles.append([0.5 * (along[p] + t.z_up(along[p], along_z[p], 1)) for p in range(2)])
    beyond.append([0.5 * (along_z[p] + t.z_up(along_z[p], along[p], 1)) for p in range(2)])

    packed = [None] * 4
    place = 0
    for q, (first, second) in enumerate(tiles):
        x_low[q] = first
        x_high[q] = second
        y_low[q] = t.join_low(first, second)
        y_high[q] = t.join_high(first, second)
        if beyond[q] is not None:
            zf, zs = beyond[q]
            for m, piece in enumerate((zf, zs, t.join_low(zf, zs), t.join_high(zf, zs))):
                piece = t.spin(piece, 4 * place + 2)
                packed[m] = (
                    piece if place == 0 else jnp.where(t.lane < 4 * place, packed[m], piece)
                )
            place += 1
    for n, (a, b) in enumerate(pairs_of(third_list(fields))):
        slot = fields + FLUID + n
        xa, xb = (tiles[q if q < fields else fields + 5] for q in (a, b))
        x_low[slot] = jnp.where(t.row < cy, xa[1], t.swap(xb[1]))
        x_high[slot] = jnp.where(t.row < cy, t.swap(xb[0]), xa[0])
        ya, yb = (tiles[q if q < fields else fields + 6] for q in (a, b))
        w = [t.swap(ya[0]), t.swap(ya[1]), t.swap(yb[0]), t.swap(yb[1])]
        s = t.slot
        y_low[slot] = jnp.where(
            s == 2,
            w[0],
            jnp.where(s == 3, t.turn(w[1], 1), jnp.where(s == 0, t.turn(w[2], -2), t.turn(w[3], -1))),
        )
        y_high[slot] = jnp.where(
            s == 1,
            w[0],
            jnp.where(s == 0, t.turn(w[1], -1), jnp.where(s == 3, t.turn(w[2], 2), t.turn(w[3], 1))),
        )
    top = jnp.maximum(top_speed(st), top_speed(zst))
    top_out[...] = jnp.broadcast_to(top, top_out.shape)
    last = x_low.shape[0] - 1
    for out, piece in zip((x_low, x_high, y_low, y_high), packed):
        out[last] = jnp.where(t.lane < 4 * place, piece, top)


def relay_kernel(x_below, x_above, y_below, top, top_two, to_low, to_high, line_top):
    cy, lanes = x_below.shape[1] // 2, x_below.shape[2]
    t = Tile(cy, lanes)
    last = x_below.shape[0] - 1
    line = jnp.maximum(top[...], top_two[...])
    for beside in (x_below, x_above, y_below):
        line = jnp.maximum(line, beside[last, 0:1, lanes - 1 : lanes])
    line_top[...] = line
    edge = edge_list(x_below.shape[0])
    whole, single = corner_lists(edge)
    for n, q in enumerate(whole + [last]):
        low = t.join_low(x_below[q], x_above[q])
        high = t.join_high(x_below[q], x_above[q])
        if q == last:
            low = jnp.where(t.lane < 4 * len(edge), low, line)
            high = jnp.where(t.lane < 4 * len(edge), high, line)
        to_low[n] = low
        to_high[n] = high
    for n in range(0, len(single), 4):
        low, high = None, None
        for turn, q in zip(CORNER_TURNS, single[n : n + 4]):
            below = t.turn(t.join_low(x_below[q], x_above[q]), turn)
            above = t.turn(t.join_high(x_below[q], x_above[q]), turn)
            if low is None:
                low, high = below, above
            else:
                low = jnp.where(t.corner_rows(0, turn), below, low)
                high = jnp.where(t.corner_rows(1, turn), above, high)
        to_low[len(whole) + 1 + n // 4] = low
        to_high[len(whole) + 1 + n // 4] = high


def limited(a, b):
    return jnp.maximum(jnp.minimum(a, b), 0.0) + jnp.minimum(jnp.maximum(a, b), 0.0)


def recover(conserved, magnetic):
    density = conserved[0]
    momenta = conserved[1:4]
    energy = conserved[4] + density
    mom_sq = dot(momenta, momenta)
    mag_sq = dot(magnetic, magnetic)
    cross = dot(momenta, magnetic)
    cross_sq = cross * cross

    def state(z):
        grown = z + mag_sq
        over = 1.0 / (z * grown)
        speed_sq = (mom_sq * z * z + cross_sq * (2.0 * z + mag_sq)) * over * over
        kept = 1.0 - jnp.minimum(speed_sq, SPEED_CAP)
        rest = density * jnp.sqrt(kept)
        return kept, rest, 0.5 * (z * kept - rest), grown * over

    z = jnp.maximum(energy - 0.5 * mag_sq, density)
    for _ in range(RECOVERY_STEPS):
        kept, rest, pressure, over_z = state(z)
        residual = (
            z
            + mag_sq
            - pressure
            - 0.5 * mag_sq * kept
            - 0.5 * cross_sq * over_z * over_z
            - energy
        )
        z = jnp.maximum(z - residual / (1.0 - 0.5 * kept), density)
    kept, rest, pressure, over_z = state(z)
    pressure = jnp.maximum(pressure, PRESSURE_FLOOR * rest)
    scale = lax.rsqrt(kept) / (z + mag_sq)
    along = cross * over_z
    four_vel = [scale * (momenta[i] + along * magnetic[i]) for i in range(3)]
    return [rest, pressure] + four_vel


def stress_parts(rest, pressure, u, magnetic):
    lorentz_sq = 1.0 + dot(u, u)
    over = lax.rsqrt(lorentz_sq)
    over_sq = over * over
    time_b = dot(u, magnetic)
    grown_b = [magnetic[i] + time_b * u[i] for i in range(3)]
    b_square = (dot(magnetic, magnetic) + time_b * time_b) * over_sq
    enthalpy = rest + 2.0 * pressure
    inertia = enthalpy + b_square
    return lorentz_sq, over, over_sq, time_b, grown_b, b_square, enthalpy, inertia


def face_state(rest, pressure, u, magnetic, d):
    lorentz_sq, over, over_sq, time_b, grown_b, b_square, enthalpy, inertia = stress_parts(
        rest, pressure, u, magnetic
    )
    total_pressure = pressure + 0.5 * b_square
    lorentz = lorentz_sq * over
    density = rest * lorentz
    carried = inertia * lorentz
    time_over = time_b * over
    conserved = [density]
    conserved += [carried * u[j] - time_over * grown_b[j] for j in range(3)]
    conserved += [inertia * lorentz_sq - total_pressure - time_b * time_b - density]
    mass_flux = rest * u[d]
    flux = [mass_flux]
    pushed = inertia * u[d]
    b_over = grown_b[d] * over_sq
    for j in range(3):
        flux_j = pushed * u[j] - b_over * grown_b[j]
        flux.append(flux_j + total_pressure if j == d else flux_j)
    flux.append(carried * u[d] - time_over * grown_b[d] - mass_flux)
    ratio = 1.0 / (enthalpy * inertia)
    sound_sq = 2.0 * pressure * inertia * ratio
    alfven_sq = b_square * enthalpy * ratio
    fast_sq = sound_sq + alfven_sq - sound_sq * alfven_sq
    slow = 1.0 - fast_sq
    velocity = u[d] * over
    rest_part = 1.0 - dot(u, u) * over_sq * fast_sq
    spread = jnp.sqrt(fast_sq * over_sq * (rest_part - velocity * velocity * slow))
    fastest = (jnp.abs(velocity * slow) + spread) / rest_part
    return conserved, flux, fastest


def face_flux(left, right, normal, weight, d):
    sides = []
    for state in (left, right):
        magnetic = [normal if i == d else state[5 + i] for i in range(3)]
        sides.append(face_state(state[0], state[1], state[2:5], magnetic, d))
    (cons_l, flux_l, fast_l), (cons_r, flux_r, fast_r) = sides
    signal = jnp.maximum(fast_l, fast_r)
    scale = 0.5 * weight
    return [scale * (flux_l[q] + flux_r[q] - signal * (cons_r[q] - cons_l[q])) for q in range(5)]


def volume_over(conformal):
    return conformal * jnp.sqrt(conformal)


def first_diff(down_two, down, up, up_two):
    return (8.0 / 12.0) * (up - down) + (1.0 / 12.0) * (down_two - up_two)


class Halo:
    def __init__(self, cells, zst, zfl, x_below, y_below, x_above, y_above, c_below, c_above):
        self.fields, self.block, self.lanes = zst.shape
        self.st = cells.at[0 : self.fields]
        self.fl = cells.at[self.fields : self.fields + FLUID]
        self.zst, self.zfl = zst, zfl
        self.x_below, self.x_above = x_below, x_above
        self.y_below, self.y_above = y_below, y_above
        self.c_below, self.c_above = c_below, c_above
        self.cy = self.block // 4
        self.t = Tile(self.cy, self.lanes)
        self.half = self.t.rows
        self.own = self.block // self.half
        self.inner = range(1, self.own + 1)
        self.span = range(self.own + 2)
        self.edge = edge_list(x_below.shape[0])
        self.last = x_below.shape[0] - 1

    def rows_of(self, ref, q, p):
        return ref[q, (p - 1) * self.half : p * self.half, :]

    def main(self, q, p):
        if q < self.fields:
            return self.rows_of(self.st, q, p)
        return self.rows_of(self.fl, q - self.fields, p)

    def beyond(self, q, p):
        if q < self.fields:
            return self.rows_of(self.zst, q, p)
        return self.rows_of(self.zfl, q - self.fields, p)

    def part(self, second):
        return self.t.part_second if second else self.t.part_first

    def beside(self, q, p):
        return self.part(p == 2)(self.y_above[q], self.y_below[q])

    def third_place(self, q):
        return self.fields + FLUID + q // 2, q % 2

    def x_third(self, q, upper):
        tile, which = self.third_place(q)
        found = self.x_above[tile] if upper else self.x_below[tile]
        return self.t.swap(found) if which else found

    def y_third(self, q, p):
        t = self.t
        tile, which = self.third_place(q)
        turn_above, turn_below = ((0, 0), (-1, 1), (2, -2), (1, -1))[2 * which + p - 1]
        above, below = t.turn(self.y_above[tile], turn_above), t.turn(self.y_below[tile], turn_below)
        return jnp.where(t.slot == 2, above, below)

    def z_place(self, q):
        return 4 * self.edge.index(q) + 2

    def x_beyond(self, q, upper):
        tile = self.x_above[self.last] if upper else self.x_below[self.last]
        return self.t.spin(tile, -self.z_place(q))

    def y_beyond(self, q, p):
        return self.t.spin(self.beside(self.last, p), -self.z_place(q))

    def corner(self, q, p):
        whole, single = corner_lists(self.edge)
        if q in single:
            n = single.index(q)
            place, turn = len(whole) + 1 + n // 4, CORNER_TURNS[n % 4]
        else:
            place, turn = whole.index(q), 0
        above, below = self.t.turn(self.c_above[place], -turn), self.t.turn(self.c_below[place], -turn)
        return self.part(p > 0)(above, below)

    def corner_beyond(self, q, p):
        place = len(corner_lists(self.edge)[0])
        tile = self.part(p > 0)(self.c_above[place], self.c_below[place])
        return self.t.spin(tile, -self.z_place(q))

    def plane(self, q):
        own, inner = self.own, self.inner
        return (
            [self.x_below[q]] + [self.main(q, p) for p in inner] + [self.x_above[q]],
            [self.corner(q, 0)] + [self.beside(q, p) for p in inner] + [self.corner(q, own + 1)],
            [self.x_beyond(q, False)]
            + [self.beyond(q, p) for p in inner]
            + [self.x_beyond(q, True)],
            [None] + [self.y_beyond(q, p) for p in inner] + [None],
        )


def weigh(chi_face, alpha_face):
    shrink = volume_over(chi_face)
    return shrink, alpha_face / shrink


def primitives(half, spots, cons, centred, chi, alpha, batch):
    found = {}
    for start in range(0, len(spots), batch):
        group = spots[start : start + batch]

        def gather(planes):
            return jnp.concatenate([planes[k][p] for k, p in group], axis=0)

        shrink = volume_over(gather(chi))
        mag_raw = [gather(centred[i]) for i in range(3)]
        mag = [m * shrink for m in mag_raw]
        values = recover([gather(c) * shrink for c in cons], mag)
        u = values[2:5]
        factor = gather(alpha) * lax.rsqrt(1.0 + dot(u, u))
        field = [
            factor * (u[(i + 2) % 3] * mag_raw[(i + 1) % 3] - u[(i + 1) % 3] * mag_raw[(i + 2) % 3])
            for i in range(3)
        ]
        for n, spot in enumerate(group):
            found[spot] = [value[n * half : (n + 1) * half] for value in values + mag + field]
    return found


def ring_fluxes(prims, chi, alpha, normals, d, up, down):
    found = []
    for here, there in ((0, 1), (1, 0)):
        left, right = [], []
        for a, b in zip(prims[here], prims[there]):
            below = down(a, b, 1)
            middle = a - below
            left.append(below + 0.5 * limited(below - down(a, b, 2), middle))
            right.append(a - 0.5 * limited(middle, up(a, b, 1) - a))
        shrink, weight = weigh(
            0.5 * (chi[here] + down(chi[here], chi[there], 1)),
            0.5 * (alpha[here] + down(alpha[here], alpha[there], 1)),
        )
        found.append(face_flux(left, right, normals[here] * shrink, weight, d))
    return [a - up(a, b, 1) for a, b in zip(*found)]


def early_kernel(
    cells, zst, zfl, x_below, y_below, x_above, y_above,
    st_rate, hydro_rate, slopes, shared, pairs, sides, thirds, pairs_z, sides_z, grads, seconds, damped, tensors,
):
    halo = Halo(cells, zst, zfl, x_below, y_below, x_above, y_above, None, None)
    t, fields, half, own, cy = halo.t, halo.fields, halo.half, halo.own, halo.cy
    st, fl, inner = halo.st, halo.fl, halo.inner

    for q in range(fields):
        pairs[q, 0] = halo.x_third(q, False)
        pairs[q, 1] = x_below[q]
        for p in inner:
            pairs[q, 1 + p] = halo.main(q, p)
            sides[q, p - 1] = halo.beside(q, p)
            thirds[q, p - 1] = halo.y_third(q, p)
        pairs[q, 2 + own] = x_above[q]
        pairs[q, 3 + own] = halo.x_third(q, True)
        if q < CURVED:
            pairs_z[q, 0] = halo.x_beyond(q, False)
            pairs_z[q, own + 1] = halo.x_beyond(q, True)
            for p in inner:
                pairs_z[q, p] = halo.beyond(q, p)
                sides_z[q, p - 1] = halo.y_beyond(q, p)

    def both(q):
        return [[None] + [read(q, p) for p in inner] for read in (halo.main, halo.beyond)]

    bx, by, bz = both(fields + 5), both(fields + 6), both(fields + 7)
    normals = bz
    bx = [
        [None] + [0.5 * (v[p] + t.odd(v[p], (v[1:] + [end])[p])) for p in inner]
        for v, end in zip(bx, (x_above[fields + 5], halo.x_beyond(fields + 5, True)))
    ]
    by = [
        [None] + [0.5 * (v[p] + t.y_up(v[p], read(fields + 6, p), 1)) for p in inner]
        for v, read in zip(by, (halo.beside, halo.y_beyond))
    ]
    bz = [
        [None] + [0.5 * (a[p] + t.z_up(a[p], b[p], 1)) for p in inner]
        for a, b in ((bz[0], bz[1]), (bz[1], bz[0]))
    ]
    chi, alpha = both(0), both(7)
    spots = [(k, p) for k in range(2) for p in inner]
    found = primitives(
        half, spots, [both(fields + q) for q in range(5)], [bx, by, bz], chi, alpha, len(spots)
    )
    for (k, p), values in found.items():
        for i, value in enumerate(values):
            shared[k * own + p - 1, i] = value
    for p in inner:
        prims = [found[k, p][:8] for k in range(2)]
        changes = ring_fluxes(
            prims,
            [chi[k][p] for k in range(2)],
            [alpha[k][p] for k in range(2)],
            [normals[k][p] for k in range(2)],
            2,
            t.z_up,
            t.z_down,
        )
        for q in range(5):
            tensors[p - 1, 6 + q] = changes[q]
        rest, pressure = prims[0][:2]
        u = prims[0][2:5]
        parts = stress_parts(rest, pressure, u, prims[0][5:8])
        lorentz_sq, over, over_sq, time_b, grown_b, b_square, enthalpy, inertia = parts
        total_pressure = pressure + 0.5 * b_square
        for s, (i, j) in enumerate(INDEX_PAIRS):
            value = inertia * u[i] * u[j] - over_sq * (grown_b[i] * grown_b[j])
            tensors[p - 1, s] = value + total_pressure if i == j else value

    def pair_step(index, carry):
        p = index + 1
        base = pl.multiple_of(index * half, half)

        for q in range(fields):
            centre = pairs[q, p + 1]
            x_m3 = t.odd(pairs[q, p - 1], pairs[q, p])
            x_m2 = pairs[q, p]
            x_m1 = t.odd(pairs[q, p], centre)
            x_p1 = t.odd(centre, pairs[q, p + 2])
            x_p2 = pairs[q, p + 2]
            x_p3 = t.odd(pairs[q, p + 2], pairs[q, p + 3])
            side, third = sides[q, index], thirds[q, index]
            y_m1, y_m2 = t.y_down(centre, side, 1), t.y_down(centre, side, 2)
            y_p1, y_p2 = t.y_up(centre, side, 1), t.y_up(centre, side, 2)
            y_m3 = t.turn(
                jnp.where(t.slot >= cy - 2, side, jnp.where(t.slot == cy - 3, third, centre)), 3
            )
            y_p3 = t.turn(jnp.where(t.slot < 2, side, jnp.where(t.slot == 2, third, centre)), -3)
            beyond = zst[q, pl.ds(base, half), :]
            z_m1, z_m2, z_m3 = (t.z_down(centre, beyond, k) for k in (1, 2, 3))
            z_p1, z_p2, z_p3 = (t.z_up(centre, beyond, k) for k in (1, 2, 3))
            dx = first_diff(x_m2, x_m1, x_p1, x_p2)
            dy = first_diff(y_m2, y_m1, y_p1, y_p2)
            grads[q, 0] = dx
            if q < CURVED:
                slopes[q, index] = dx
            grads[q, 1] = dy
            grads[q, 2] = first_diff(z_m2, z_m1, z_p1, z_p2)
            near = [x_m1 + x_p1, y_m1 + y_p1, z_m1 + z_p1]
            far = [x_m2 + x_p2, y_m2 + y_p2, z_m2 + z_p2]
            outer = (x_m3 + x_p3) + (y_m3 + y_p3) + (z_m3 + z_p3)
            damped[q] = (DISSIPATION / 64.0) * (
                outer - 6.0 * (far[0] + far[1] + far[2]) + 15.0 * (near[0] + near[1] + near[2])
                - 60.0 * centre
            )
            if q < CURVED:
                for s, d in ((0, 0), (3, 1), (5, 2)):
                    seconds[q, s] = (1.0 / 12.0) * (16.0 * near[d] - far[d] - 30.0 * centre)
                b_m, b_c, b_p = pairs_z[q, p - 1], pairs_z[q, p], pairs_z[q, p + 1]
                dx_z = first_diff(b_m, t.odd(b_m, b_c), t.odd(b_c, b_p), b_p)
                b_s = sides_z[q, p - 1]
                dy_z = first_diff(
                    t.y_down(b_c, b_s, 2),
                    t.y_down(b_c, b_s, 1),
                    t.y_up(b_c, b_s, 1),
                    t.y_up(b_c, b_s, 2),
                )
                for s, inside, outside in ((2, dx, dx_z), (4, dy, dy_z)):
                    seconds[q, s] = first_diff(
                        t.z_down(inside, outside, 2),
                        t.z_down(inside, outside, 1),
                        t.z_up(inside, outside, 1),
                        t.z_up(inside, outside, 2),
                    )

        def value(q):
            return pairs[q, p + 1]

        def fluid_value(q):
            return fl[q, pl.ds(base, half), :]

        conformal, lapse = value(0), value(7)
        over_chi = 1.0 / conformal
        metric = symmetric([value(1 + s) for s in range(6)])
        shift = [value(8 + i) for i in range(3)]
        extrinsic, theta = value(11), value(21)
        traceless = symmetric([value(12 + s) for s in range(6)])
        connection = [value(18 + i) for i in range(3)]
        inverse = inverse_metric(metric)
        grad = [[grads[q, k] for k in range(3)] for q in range(fields)]
        chi_grad, lapse_grad = grad[0], grad[7]
        shift_grad = [[grad[8 + i][k] for i in range(3)] for k in range(3)]
        trace_k = extrinsic + 2.0 * theta

        stress = symmetric([tensors[p - 1, s] for s in range(6)])
        held = [fluid_value(q) for q in range(5)]
        shrink = volume_over(conformal)
        energy = held[4] + held[0]
        third_k = trace_k * (1.0 / 3.0)
        curved = [
            [
                (traceless[i][j] + metric[i][j] * third_k) if i <= j else None for j in range(3)
            ]
            for i in range(3)
        ]
        work = (
            stress[0][0] * curved[0][0]
            + stress[1][1] * curved[1][1]
            + stress[2][2] * curved[2][2]
            + 2.0
            * (
                stress[0][1] * curved[0][1]
                + stress[0][2] * curved[0][2]
                + stress[1][2] * curved[1][2]
            )
        )
        rates = [tensors[p - 1, 6 + q] for q in range(5)]
        for i in range(3):
            rates[1 + i] = (
                rates[1 + i]
                - energy * lapse_grad[i]
                + total([held[1 + k] * grad[8 + k][i] for k in range(3)])
            )
        rates[4] = (
            rates[4] + lapse * work * over_chi / shrink - dot(held[1:4], lapse_grad)
        )
        for q in range(5):
            hydro_rate[q, pl.ds(base, half), :] = rates[q]
        density = energy * shrink
        momentum = [held[1 + i] * shrink for i in range(3)]

        lowered = [[[None] * 3 for _ in range(3)] for _ in range(3)]
        for i in range(3):
            for j in range(3):
                for k in range(j, 3):
                    got = 0.5 * (
                        grad[1 + slot_of(i, k)][j]
                        + grad[1 + slot_of(i, j)][k]
                        - grad[1 + slot_of(j, k)][i]
                    )
                    lowered[i][j][k] = lowered[i][k][j] = got
        raised = [[[None] * 3 for _ in range(3)] for _ in range(3)]
        for i in range(3):
            for j in range(3):
                for k in range(j, 3):
                    got = total([inverse[i][l] * lowered[l][j][k] for l in range(3)])
                    raised[i][j][k] = raised[i][k][j] = got
        contracted = [trace_with(inverse, raised[i]) for i in range(3)]

        def hessian_trace(q):
            return (
                inverse[0][0] * seconds[q, 0]
                + inverse[1][1] * seconds[q, 3]
                + inverse[2][2] * seconds[q, 5]
                + 2.0 * (inverse[0][2] * seconds[q, 2] + inverse[1][2] * seconds[q, 4])
            )

        def second_cov(q, slope):
            bent = [total([raised[k][i][j] * slope[k] for k in range(3)]) for i, j in INDEX_PAIRS]
            return symmetric(
                [-bent[s] if s == 1 else seconds[q, s] - bent[s] for s in range(len(bent))]
            )

        chi_cov = second_cov(0, chi_grad)
        chi_lap = trace_with(inverse, chi_cov)
        raised_chi = [dot(inverse[i], chi_grad) for i in range(3)]
        chi_square = dot(raised_chi, chi_grad)
        cross_term = dot(raised_chi, lapse_grad)
        half_chi = 0.5 * over_chi
        plain_cov = second_cov(7, lapse_grad)
        lapse_cov = symmetric(
            [
                plain_cov[i][j]
                + (
                    chi_grad[i] * lapse_grad[j]
                    + chi_grad[j] * lapse_grad[i]
                    - metric[i][j] * cross_term
                )
                * half_chi
                for i, j in INDEX_PAIRS
            ]
        )
        lapse_lap = conformal * trace_with(inverse, lapse_cov)

        mixed = [
            [[dot(inverse[l], lowered[k][j]) for j in range(3)] for k in range(3)]
            for l in range(3)
        ]
        quarter_sq = half_chi * half_chi
        metric_factor = chi_lap * half_chi - 3.0 * chi_square * quarter_sq
        ricci = []
        for i, j in INDEX_PAIRS:
            second_part = -0.5 * hessian_trace(1 + slot_of(i, j))
            connection_part = 0.5 * total(
                [metric[k][i] * grad[18 + k][j] + metric[k][j] * grad[18 + k][i] for k in range(3)]
            )
            contracted_part = 0.5 * total(
                [contracted[k] * (lowered[i][j][k] + lowered[j][i][k]) for k in range(3)]
            )
            if i == j:
                quadratic = total(
                    [
                        raised[k][l][i] * (2.0 * mixed[l][i][k] + mixed[l][k][i])
                        for k in range(3)
                        for l in range(3)
                    ]
                )
            else:
                quadratic = total(
                    [
                        raised[k][l][i] * (mixed[l][j][k] + mixed[l][k][j])
                        + raised[k][l][j] * mixed[l][i][k]
                        for k in range(3)
                        for l in range(3)
                    ]
                )
            conformal_part = (
                chi_cov[i][j] * half_chi
                + metric[i][j] * metric_factor
                - chi_grad[i] * chi_grad[j] * quarter_sq
            )
            ricci.append(
                second_part + connection_part + contracted_part + quadratic + conformal_part
            )
        ricci = symmetric(ricci)
        ricci_scalar = conformal * trace_with(inverse, ricci)
        stress_trace = conformal * trace_with(inverse, stress)

        up_a = [
            [total([inverse[i][k] * traceless[k][j] for k in range(3)]) for j in range(3)]
            for i in range(3)
        ]
        raised_a = symmetric(
            [total([up_a[i][l] * inverse[j][l] for l in range(3)]) for i, j in INDEX_PAIRS]
        )
        a_square = trace_with(traceless, raised_a)
        shift_div = shift_grad[0][0] + shift_grad[1][1] + shift_grad[2][2]
        two_thirds_div = (2.0 / 3.0) * shift_div

        def finish(q, rate):
            rate = rate + dot(shift, grad[q]) + damped[q]
            st_rate[q, pl.ds(base, half), :] = rate

        finish(0, (2.0 / 3.0) * conformal * (lapse * trace_k - shift_div))
        finish(7, -2.0 * lapse * extrinsic)
        for i in range(3):
            finish(8 + i, 0.75 * connection[i] - SHIFT_DAMPING * shift[i])
        finish(
            11,
            lapse
            * (
                a_square
                + trace_k * trace_k * (1.0 / 3.0)
                + FOUR_PI * (stress_trace + density)
                + KAPPA_ONE * theta
            )
            - lapse_lap,
        )
        source = symmetric(
            [
                lapse * (ricci[i][j] - 2.0 * FOUR_PI * stress[i][j]) - lapse_cov[i][j]
                for i, j in INDEX_PAIRS
            ]
        )
        third_trace = trace_with(inverse, source) * (1.0 / 3.0)
        for s, (i, j) in enumerate(INDEX_PAIRS):
            finish(
                1 + s,
                total(
                    [
                        metric[i][k] * shift_grad[j][k] + metric[j][k] * shift_grad[i][k]
                        for k in range(3)
                    ]
                )
                - metric[i][j] * two_thirds_div
                - 2.0 * lapse * traceless[i][j],
            )
            product = total([traceless[i][k] * up_a[k][j] for k in range(3)])
            finish(
                12 + s,
                total(
                    [
                        traceless[i][k] * shift_grad[j][k] + traceless[j][k] * shift_grad[i][k]
                        for k in range(3)
                    ]
                )
                - traceless[i][j] * two_thirds_div
                + conformal * (source[i][j] - metric[i][j] * third_trace)
                + lapse * (trace_k * traceless[i][j] - 2.0 * product),
            )
        for i in range(3):
            bracket = (
                trace_with(raised_a, raised[i])
                - 1.5 * dot(raised_a[i], chi_grad) * over_chi
                - dot(inverse[i], [2.0 * grad[11][j] + grad[21][j] for j in range(3)]) * (1.0 / 3.0)
                - 2.0 * FOUR_PI * dot(inverse[i], momentum)
            )
            spread = [
                seconds[8, 0] + seconds[10, 2],
                seconds[9, 3] + seconds[10, 4],
                seconds[8, 2] + seconds[9, 4] + seconds[10, 5],
            ]
            finish(
                18 + i,
                contracted[i] * two_thirds_div
                - total([contracted[j] * shift_grad[j][i] for j in range(3)])
                + hessian_trace(8 + i)
                + dot(inverse[i], spread) * (1.0 / 3.0)
                - 2.0 * dot(raised_a[i], lapse_grad)
                + 2.0
                * lapse
                * (bracket - KAPPA_ONE * (connection[i] - contracted[i])),
            )
        finish(
            21,
            0.5
            * lapse
            * (
                ricci_scalar
                - a_square
                + (2.0 / 3.0) * trace_k * trace_k
                - 4.0 * FOUR_PI * density
            )
            - 2.0 * KAPPA_ONE * lapse * theta,
        )
        return carry

    lax.fori_loop(0, own, pair_step, 0)


def late_kernel(
    cells, zst, zfl, x_below, y_below, x_above, y_above, c_below, c_above, line_two, line_top,
    st_rate, hydro_rate, slopes, shared, st_out, fl_out,
):
    halo = Halo(cells, zst, zfl, x_below, y_below, x_above, y_above, c_below, c_above)
    t, fields, half, own = halo.t, halo.fields, halo.half, halo.own
    inner, span = halo.inner, halo.span

    top = jnp.maximum(line_top[...], line_two[...])
    speed_tile = len(corner_lists(halo.edge)[0])
    for lines in (c_below, c_above):
        top = jnp.maximum(top, lines[speed_tile, 0:1, halo.lanes - 1 : halo.lanes])
    dt = COURANT / top

    for p in inner:
        place = slice((p - 1) * half, p * half)
        mixed = []
        for q in range(CURVED):
            s_m, s_c, s_p = (
                halo.beside(q, n) if 1 <= n <= own else halo.corner(q, n) for n in (p - 1, p, p + 1)
            )
            slope = slopes[q, p - 1]
            slope_side = first_diff(s_m, t.odd_swapped(s_m, s_c), t.odd_swapped(s_c, s_p), s_p)
            mixed.append(
                first_diff(
                    t.y_down(slope, slope_side, 2),
                    t.y_down(slope, slope_side, 1),
                    t.y_up(slope, slope_side, 1),
                    t.y_up(slope, slope_side, 2),
                )
            )
        conformal, lapse = halo.main(0, p), halo.main(7, p)
        metric = [halo.main(1 + s, p) for s in range(6)]
        inverse = inverse_metric(symmetric(metric))
        half_chi = 0.5 / conformal
        cross = inverse[0][1]
        chi_trace = 2.0 * cross * mixed[0] * half_chi
        ricci = [metric[s] * chi_trace - cross * mixed[1 + s] for s in range(6)]
        ricci[1] = ricci[1] + mixed[0] * half_chi
        source = [lapse * r for r in ricci]
        source[1] = source[1] - mixed[7]
        third_trace = trace_with(inverse, symmetric(source)) * (1.0 / 3.0)
        extra = {
            11: -2.0 * conformal * cross * mixed[7],
            21: 0.5 * lapse * conformal * trace_with(inverse, symmetric(ricci)),
        }
        for s in range(6):
            extra[12 + s] = conformal * (source[s] - metric[s] * third_trace)
        for i in range(3):
            extra[18 + i] = 2.0 * cross * mixed[8 + i] + (1.0 / 3.0) * (
                inverse[i][0] * mixed[9] + inverse[i][1] * mixed[8]
            )
        for q in range(fields):
            rate = st_rate[q, place, :]
            if q in extra:
                rate = rate + extra[q]
            st_out[q, place, :] = halo.main(q, p) + dt * rate

    v, h, vz, hz = halo.plane(fields + 5)
    hz[own + 1] = halo.corner_beyond(fields + 5, own + 1)
    v_next = v[1:] + [halo.x_third(fields, True)]
    face_x = v
    bx = (
        [0.5 * (v[p] + t.odd(v[p], v_next[p])) for p in span],
        [0.5 * (h[p] + t.odd_swapped(h[p], h[min(p + 1, own + 1)])) for p in span],
        [0.5 * (vz[p] + t.odd(vz[p], vz[min(p + 1, own + 1)])) for p in span],
        [None] + [0.5 * (hz[p] + t.odd_swapped(hz[p], hz[p + 1])) for p in inner] + [None],
    )
    v, h, vz, hz = halo.plane(fields + 6)
    hz[0] = halo.corner_beyond(fields + 6, 0)
    hz[own + 1] = halo.corner_beyond(fields + 6, own + 1)
    face_y = v, h
    full = [
        jnp.where(t.slot == 2, halo.y_third(fields, p), h[p]) if 1 <= p <= own else h[p] for p in span
    ]
    by = (
        [0.5 * (v[p] + t.y_up(v[p], h[p], 1)) for p in span],
        [0.5 * (h[p] + t.y_up(full[p], v[p], 1)) for p in span],
        [0.5 * (vz[p] + t.y_up(vz[p], hz[p], 1)) for p in span],
        [None] + [0.5 * (hz[p] + t.y_up(hz[p], vz[p], 1)) for p in inner] + [None],
    )
    v, h, vz, hz = halo.plane(fields + 7)
    bz = (v, h, vz, hz)

    chi, alpha = halo.plane(0), halo.plane(7)
    spots = [(0, 0), (0, own + 1)] + [(1, p) for p in span] + [(2, 0), (2, own + 1)]
    spots += [(3, p) for p in inner]
    found = primitives(
        half, spots, [halo.plane(fields + q) for q in range(5)], [bx, by, bz], chi, alpha, 5
    )
    for k, kind in enumerate((0, 2)):
        for p in inner:
            found[kind, p] = [shared[k * own + p - 1, i] for i in range(11)]

    lines = [[found[0, p][i] for p in span] for i in range(8)] + [chi[0], alpha[0]]
    odd_lines = [[t.odd(f[p], f[min(p + 1, own + 1)]) for p in span] for f in lines]
    fluxes = [None]
    for p in range(1, own + 2):
        left, right = [], []
        for f, o in zip(lines[:8], odd_lines):
            here = f[p] - o[p - 1]
            left.append(o[p - 1] + 0.5 * limited(o[p - 1] - f[p - 1], here))
            right.append(f[p] - 0.5 * limited(here, o[p] - f[p]))
        shrink, weight = weigh(
            0.5 * (lines[8][p] + odd_lines[8][p - 1]), 0.5 * (lines[9][p] + odd_lines[9][p - 1])
        )
        fluxes.append(face_flux(left, right, face_x[p] * shrink, weight, 0))
    for p in inner:
        changes = ring_fluxes(
            [found[k, p][:8] for k in range(2)],
            [chi[k][p] for k in range(2)],
            [alpha[k][p] for k in range(2)],
            [face_y[k][p] for k in range(2)],
            1,
            t.y_up,
            t.y_down,
        )
        place = slice((p - 1) * half, p * half)
        for q in range(5):
            change = fluxes[p][q] - t.odd(fluxes[p][q], fluxes[p + 1][q])
            rate = hydro_rate[q, place, :] + change + changes[q]
            fl_out[q, place, :] = halo.main(fields + q, p) + dt * rate

    ex, ey, ez = (
        [[found[k, p][8 + i] if (k, p) in found else None for p in span] for k in range(4)]
        for i in range(3)
    )
    ez_x = [
        [ez[0][p] + t.odd(ez[0][p - 1], ez[0][p]) if p else None for p in span],
        [ez[1][p] + t.odd_swapped(ez[1][p - 1], ez[1][p]) if p else None for p in span],
    ]
    ey_x = [
        [ey[k][p] + t.odd(ey[k][p - 1], ey[k][p]) if p else None for p in span] for k in (0, 2)
    ]
    edge_z = [None] + [ez_x[0][p] + t.y_down(ez_x[0][p], ez_x[1][p], 1) for p in span[1:]]
    edge_z_h = [None] + [ez_x[1][p] + t.y_down(ez_x[1][p], ez_x[0][p], 1) for p in inner]
    edge_y = [None] + [ey_x[0][p] + t.z_down(ey_x[0][p], ey_x[1][p], 1) for p in span[1:]]
    edge_y_z = [None] + [ey_x[1][p] + t.z_down(ey_x[1][p], ey_x[0][p], 1) for p in inner]
    for p in inner:
        ex_y = ex[0][p] + t.y_down(ex[0][p], ex[1][p], 1)
        ex_y_h = ex[1][p] + t.y_down(ex[1][p], ex[0][p], 1)
        ex_y_z = ex[2][p] + t.y_down(ex[2][p], ex[3][p], 1)
        ex_y_hz = ex[3][p] + t.y_down(ex[3][p], ex[2][p], 1)
        edge_x = ex_y + t.z_down(ex_y, ex_y_z, 1)
        edge_x_h = ex_y_h + t.z_down(ex_y_h, ex_y_hz, 1)
        edge_x_z = ex_y_z + t.z_down(ex_y_z, ex_y, 1)
        x_rate = (t.z_up(edge_y[p], edge_y_z[p], 1) - edge_y[p]) - (
            t.y_up(edge_z[p], edge_z_h[p], 1) - edge_z[p]
        )
        y_rate = (t.odd(edge_z[p], edge_z[p + 1]) - edge_z[p]) - (
            t.z_up(edge_x, edge_x_z, 1) - edge_x
        )
        z_rate = (t.y_up(edge_x, edge_x_h, 1) - edge_x) - (
            t.odd(edge_y[p], edge_y[p + 1]) - edge_y[p]
        )
        quarter = 0.25 * dt
        for i, rate in enumerate((x_rate, y_rate, z_rate)):
            fl_out[5 + i, (p - 1) * half : p * half, :] = (
                halo.main(fields + 5 + i, p) + quarter * rate
            )


def per_device(spacetime, fluid):
    fields, cx, cy, cz = spacetime.shape
    rows = cx * cy
    st = spacetime.reshape(fields, rows, cz)
    fl = fluid.reshape(FLUID, rows, cz)
    sizes = [lax.axis_size(a) for a in ("gx", "gy", "gz")]
    tile = (2 * cy, cz)
    f32 = jnp.float32

    def shape(*dims):
        return jax.ShapeDtypeStruct(dims, f32)

    def beyond(cells):
        n = sizes[2]
        after = lax.ppermute(cells, "gz", [((i + 1) % n, i) for i in range(n)])
        if n == 2:
            return after
        before = lax.ppermute(cells, "gz", [(i, (i + 1) % n) for i in range(n)])
        lane = lax.broadcasted_iota(jnp.int32, cells.shape, 2)
        return jnp.where(lane < cz // 2, after, before)

    params = pltpu.CompilerParams(vmem_limit_bytes=48 * 1024 * 1024)
    zst, zfl = beyond(st), beyond(fl)
    cells = jnp.concatenate([st, fl], axis=0)
    face = shape(face_tiles(fields), *tile)
    whole, single = corner_lists(edge_list(face_tiles(fields)))
    corner = shape(len(whole) + 1 + (len(single) + 3) // 4, *tile)
    lane_row = shape(1, cz)
    x_low, x_high, y_low, y_high, top = pl.pallas_call(
        pack_kernel, out_shape=[face] * 4 + [lane_row], compiler_params=params, name="pack"
    )(cells, zst, zfl)

    def move(cells, dx, dy):
        nx, ny = sizes[0], sizes[1]
        hops = [
            (i * ny + j, ((i + dx) % nx) * ny + (j + dy) % ny) for i in range(nx) for j in range(ny)
        ]
        return lax.ppermute(cells, ("gx", "gy"), hops)

    short = sizes[0] <= 4 and sizes[1] <= 4 and sizes[2] <= 2
    x_below = move(x_high, 1, 0)
    y_below = move(y_high, 0, 1)
    x_above = move(x_low, -1, 0)
    y_above = move(y_low, 0, -1)
    top_two = move(top, 2, 0) if short and sizes[0] == 4 else top
    c_low, c_high, line_top = pl.pallas_call(
        relay_kernel,
        out_shape=[corner, corner, lane_row],
        compiler_params=params,
        name="relay",
    )(x_below, x_above, y_below, top, top_two)
    c_above = move(c_low, 0, -1)
    c_below = move(c_high, 0, 1)
    if not short:
        line_two = lax.pmax(line_top, ("gx", "gy", "gz"))
    else:
        line_two = move(line_top, 0, 2) if sizes[1] == 4 else line_top
    own = cx // 2
    arrived = (cells, zst, zfl, x_below, y_below, x_above, y_above)
    early = pl.pallas_call(
        early_kernel,
        out_shape=[
            shape(*st.shape),
            shape(5, rows, cz),
            shape(CURVED, own, *tile),
            shape(2 * own, 11, *tile),
        ],
        scratch_shapes=[
            pltpu.VMEM((fields, own + 4) + tile, f32),
            pltpu.VMEM((fields, own) + tile, f32),
            pltpu.VMEM((fields, own) + tile, f32),
            pltpu.VMEM((CURVED, own + 2) + tile, f32),
            pltpu.VMEM((CURVED, own) + tile, f32),
            pltpu.VMEM((fields, 3) + tile, f32),
            pltpu.VMEM((CURVED, 6) + tile, f32),
            pltpu.VMEM((fields,) + tile, f32),
            pltpu.VMEM((own, 11) + tile, f32),
        ],
        compiler_params=params,
        name="early",
    )(*arrived)
    st_next, fl_next = pl.pallas_call(
        late_kernel,
        out_shape=[shape(*st.shape), shape(*fl.shape)],
        compiler_params=params,
        name="late",
    )(*arrived, c_below, c_above, line_two, line_top, *early)
    return st_next.reshape(spacetime.shape), fl_next.reshape(fluid.shape)


def solution(mesh):
    spec = P(None, "gx", "gy", "gz")
    return jax.shard_map(
        per_device, mesh=mesh, in_specs=(spec, spec), out_specs=(spec, spec), check_vma=False
    )
```

```python
import functools
import math

import jax
import jax.numpy as jnp
from jax import lax
from jax.experimental import pallas as pl
from jax.experimental.pallas import tpu as pltpu
from jax.sharding import PartitionSpec as P

RECOVERY_STEPS = 4
INDEX_PAIRS = ((0, 0), (0, 1), (0, 2), (1, 1), (1, 2), (2, 2))
COURANT = 0.25
DISSIPATION = 0.2
KAPPA_ONE = 0.02
SHIFT_DAMPING = 1.0
SPEED_CAP = 0.99
PRESSURE_FLOOR = 0.01
FOUR_PI = 4.0 * math.pi

CURVED = 11
FLUID = 8


def total(pieces):
    summed = pieces[0]
    for member in pieces[1:]:
        summed = summed + member
    return summed


def dot(first_vec, second_vec):
    return total([first_vec[i] * second_vec[i] for i in range(3)])


def slot_of(i, j):
    return INDEX_PAIRS.index((min(i, j), max(i, j)))


def symmetric(entries):
    return [[entries[slot_of(i, j)] for j in range(3)] for i in range(3)]


def trace_with(inverse, tensor):
    return (
        inverse[0][0] * tensor[0][0]
        + inverse[1][1] * tensor[1][1]
        + inverse[2][2] * tensor[2][2]
        + 2.0
        * (
            inverse[0][1] * tensor[0][1]
            + inverse[0][2] * tensor[0][2]
            + inverse[1][2] * tensor[1][2]
        )
    )


def inverse_metric(metric):
    cofactor = [
        metric[1][1] * metric[2][2] - metric[1][2] * metric[1][2],
        metric[0][2] * metric[1][2] - metric[0][1] * metric[2][2],
        metric[0][1] * metric[1][2] - metric[0][2] * metric[1][1],
        metric[0][0] * metric[2][2] - metric[0][2] * metric[0][2],
        metric[0][1] * metric[0][2] - metric[0][0] * metric[1][2],
        metric[0][0] * metric[1][1] - metric[0][1] * metric[0][1],
    ]
    determinant = (
        metric[0][0] * cofactor[0] + metric[0][1] * cofactor[1] + metric[0][2] * cofactor[2]
    )
    over = 1.0 / determinant
    return symmetric([c * over for c in cofactor])


class Tile:
    def __init__(self, cy, cz):
        self.cy, self.rows, self.lanes = cy, 2 * cy, cz
        shape = (self.rows, cz)
        self.row = lax.broadcasted_iota(jnp.int32, shape, 0)
        self.lane = lax.broadcasted_iota(jnp.int32, shape, 1)
        self.slot = lax.rem(self.row, cy)

    def turn(self, tile, amount):
        amount = amount % self.rows
        return tile if amount == 0 else pltpu.roll(tile, amount, 0)

    def spin(self, tile, amount):
        amount = amount % self.lanes
        return tile if amount == 0 else pltpu.roll(tile, amount, 1)

    def swap(self, tile):
        return self.turn(tile, self.cy)

    def odd(self, a, b):
        return self.turn(jnp.where(self.row < self.cy, b, a), self.cy)

    def odd_swapped(self, a, b):
        return self.turn(jnp.where(self.row < self.cy, a, b), self.cy)

    def y_up(self, main, beyond, k):
        return self.turn(jnp.where(self.slot < k, beyond, main), -k)

    def y_down(self, main, beyond, k):
        return self.turn(jnp.where(self.slot >= self.cy - k, beyond, main), k)

    def z_up(self, main, beyond, k):
        return self.spin(jnp.where(self.lane < k, beyond, main), -k)

    def z_down(self, main, beyond, k):
        return self.spin(jnp.where(self.lane >= self.lanes - k, beyond, main), k)

    def corner_rows(self, side, turn):
        places = ((0, 2), (self.cy - 1, self.cy + 1))[side]
        first, second = [(place + turn) % self.rows for place in places]
        return (self.row == first) | (self.row == second)

    def join_low(self, u, v):
        return jnp.where(self.slot < 2, self.swap(u), self.turn(v, 2))

    def join_high(self, u, v):
        return jnp.where(self.slot >= self.cy - 2, self.swap(u), self.turn(self.swap(v), -2))

    def part_first(self, from_above, from_below):
        return jnp.where(self.slot < 2, from_above, from_below)

    def part_second(self, from_above, from_below):
        return self.turn(jnp.where(self.slot < 2, from_below, from_above), 2)


def edge_list(tiles):
    fields = next(n for n in range(tiles) if face_tiles(n) == tiles)
    return list(range(CURVED)) + list(range(fields, fields + FLUID))


CORNER_TURNS = (0, 1, 4, 5)


def corner_lists(edge):
    faces = edge[CURVED + 5 : CURVED + 7]
    return edge[:CURVED] + faces, edge[CURVED : CURVED + 5] + edge[CURVED + 7 :]


class SplitFace:
    def __init__(self, near, rest):
        count = near.shape[0] + rest.shape[0]
        self.shape = (count,) + tuple(near.shape[1:])
        first = edge_list(count) + [count - 1]
        second = [q for q in range(count) if q not in first]
        self.places = {q: (near, n) for n, q in enumerate(first)}
        self.places.update({q: (rest, n) for n, q in enumerate(second)})

    def __getitem__(self, key):
        q, rows = (key[0], key[1:]) if isinstance(key, tuple) else (key, ())
        ref, n = self.places[q]
        return ref[(n,) + rows]

    def __setitem__(self, q, tile):
        ref, n = self.places[q]
        ref[n] = tile


def face_tiles(fields):
    return fields + FLUID + len(pairs_of(third_list(fields))) + 1


def third_list(fields):
    return list(range(fields + 1))


def pairs_of(items):
    return [(items[i], items[min(i + 1, len(items) - 1)]) for i in range(0, len(items), 2)]


def top_speed(st):
    inverse = inverse_metric(symmetric([st[1 + s] for s in range(6)]))
    scale = 2.0 * st[7] * st[0]
    speeds = [jnp.abs(st[8 + d]) + jnp.sqrt(scale * inverse[d][d]) for d in range(3)]
    top = jnp.maximum(jnp.maximum(speeds[0], speeds[1]), speeds[2])
    return jnp.max(jnp.max(top, axis=1, keepdims=True), axis=0, keepdims=True)


def pack_kernel(cells, zst, zfl, *outs):
    fields, rows, lanes = zst.shape
    st, fl = cells.at[0:fields], cells.at[fields : fields + FLUID]
    cy = rows // 4
    t = Tile(cy, lanes)
    x_low_near, x_low_rest, x_high_near, x_high_rest, y_low, y_high, top_out = outs
    x_low = SplitFace(x_low_near, x_low_rest)
    x_high = SplitFace(x_high_near, x_high_rest)
    half = t.rows

    def own(ref, q):
        return [ref[q, 0:half, :], ref[q, half : 2 * half, :]]

    tiles, beyond = [], []
    for q in range(fields):
        tiles.append(own(st, q))
        beyond.append(own(zst, q) if q < CURVED else None)
    for q in range(FLUID - 1):
        tiles.append(own(fl, q))
        beyond.append(own(zfl, q))
    along, along_z = own(fl, FLUID - 1), own(zfl, FLUID - 1)
    tiles.append([0.5 * (along[p] + t.z_up(along[p], along_z[p], 1)) for p in range(2)])
    beyond.append([0.5 * (along_z[p] + t.z_up(along_z[p], along[p], 1)) for p in range(2)])

    packed = [None] * 4
    place = 0
    for q, (first, second) in enumerate(tiles):
        x_low[q] = first
        x_high[q] = second
        y_low[q] = t.join_low(first, second)
        y_high[q] = t.join_high(first, second)
        if beyond[q] is not None:
            zf, zs = beyond[q]
            for m, piece in enumerate((zf, zs, t.join_low(zf, zs), t.join_high(zf, zs))):
                piece = t.spin(piece, 4 * place + 2)
                packed[m] = (
                    piece if place == 0 else jnp.where(t.lane < 4 * place, packed[m], piece)
                )
            place += 1
    for n, (a, b) in enumerate(pairs_of(third_list(fields))):
        slot = fields + FLUID + n
        xa, xb = (tiles[q if q < fields else fields + 5] for q in (a, b))
        x_low[slot] = jnp.where(t.row < cy, xa[1], t.swap(xb[1]))
        x_high[slot] = jnp.where(t.row < cy, t.swap(xb[0]), xa[0])
        ya, yb = (tiles[q if q < fields else fields + 6] for q in (a, b))
        w = [t.swap(ya[0]), t.swap(ya[1]), t.swap(yb[0]), t.swap(yb[1])]
        s = t.slot
        y_low[slot] = jnp.where(
            s == 2,
            w[0],
            jnp.where(s == 3, t.turn(w[1], 1), jnp.where(s == 0, t.turn(w[2], -2), t.turn(w[3], -1))),
        )
        y_high[slot] = jnp.where(
            s == 1,
            w[0],
            jnp.where(s == 0, t.turn(w[1], -1), jnp.where(s == 3, t.turn(w[2], 2), t.turn(w[3], 1))),
        )
    top = jnp.maximum(top_speed(st), top_speed(zst))
    top_out[...] = jnp.broadcast_to(top, top_out.shape)
    last = x_low.shape[0] - 1
    for out, piece in zip((x_low, x_high, y_low, y_high), packed):
        out[last] = jnp.where(t.lane < 4 * place, piece, top)


def relay_kernel(x_below, x_above, y_below, top, top_two, to_low, to_high, line_top):
    cy, lanes = x_below.shape[1] // 2, x_below.shape[2]
    t = Tile(cy, lanes)
    last = x_below.shape[0] - 1
    line = jnp.maximum(top[...], top_two[...])
    for beside in (x_below, x_above, y_below):
        end = beside.shape[0] - 1
        line = jnp.maximum(line, beside[end, 0:1, lanes - 1 : lanes])
    line_top[...] = line
    edge = list(range(last))
    whole, single = corner_lists(edge)
    for n, q in enumerate(whole + [last]):
        low = t.join_low(x_below[q], x_above[q])
        high = t.join_high(x_below[q], x_above[q])
        if q == last:
            low = jnp.where(t.lane < 4 * len(edge), low, line)
            high = jnp.where(t.lane < 4 * len(edge), high, line)
        to_low[n] = low
        to_high[n] = high
    for n in range(0, len(single), 4):
        low, high = None, None
        for turn, q in zip(CORNER_TURNS, single[n : n + 4]):
            below = t.turn(t.join_low(x_below[q], x_above[q]), turn)
            above = t.turn(t.join_high(x_below[q], x_above[q]), turn)
            if low is None:
                low, high = below, above
            else:
                low = jnp.where(t.corner_rows(0, turn), below, low)
                high = jnp.where(t.corner_rows(1, turn), above, high)
        to_low[len(whole) + 1 + n // 4] = low
        to_high[len(whole) + 1 + n // 4] = high


def limited(a, b):
    return jnp.maximum(jnp.minimum(a, b), 0.0) + jnp.minimum(jnp.maximum(a, b), 0.0)


def recover(conserved, magnetic):
    density = conserved[0]
    momenta = conserved[1:4]
    energy = conserved[4] + density
    mom_sq = dot(momenta, momenta)
    mag_sq = dot(magnetic, magnetic)
    cross = dot(momenta, magnetic)
    cross_sq = cross * cross

    def state(z):
        grown = z + mag_sq
        over = 1.0 / (z * grown)
        speed_sq = (mom_sq * z * z + cross_sq * (2.0 * z + mag_sq)) * over * over
        kept = 1.0 - jnp.minimum(speed_sq, SPEED_CAP)
        rest = density * jnp.sqrt(kept)
        return kept, rest, 0.5 * (z * kept - rest), grown * over

    z = jnp.maximum(energy - 0.5 * mag_sq, density)
    for _ in range(RECOVERY_STEPS):
        kept, rest, pressure, over_z = state(z)
        residual = (
            z
            + mag_sq
            - pressure
            - 0.5 * mag_sq * kept
            - 0.5 * cross_sq * over_z * over_z
            - energy
        )
        z = jnp.maximum(z - residual / (1.0 - 0.5 * kept), density)
    kept, rest, pressure, over_z = state(z)
    pressure = jnp.maximum(pressure, PRESSURE_FLOOR * rest)
    scale = lax.rsqrt(kept) / (z + mag_sq)
    along = cross * over_z
    four_vel = [scale * (momenta[i] + along * magnetic[i]) for i in range(3)]
    return [rest, pressure] + four_vel


def stress_parts(rest, pressure, u, magnetic):
    lorentz_sq = 1.0 + dot(u, u)
    over = lax.rsqrt(lorentz_sq)
    over_sq = over * over
    time_b = dot(u, magnetic)
    grown_b = [magnetic[i] + time_b * u[i] for i in range(3)]
    b_square = (dot(magnetic, magnetic) + time_b * time_b) * over_sq
    enthalpy = rest + 2.0 * pressure
    inertia = enthalpy + b_square
    return lorentz_sq, over, over_sq, time_b, grown_b, b_square, enthalpy, inertia


def face_state(rest, pressure, u, magnetic, d):
    lorentz_sq, over, over_sq, time_b, grown_b, b_square, enthalpy, inertia = stress_parts(
        rest, pressure, u, magnetic
    )
    total_pressure = pressure + 0.5 * b_square
    lorentz = lorentz_sq * over
    density = rest * lorentz
    carried = inertia * lorentz
    time_over = time_b * over
    conserved = [density]
    conserved += [carried * u[j] - time_over * grown_b[j] for j in range(3)]
    conserved += [inertia * lorentz_sq - total_pressure - time_b * time_b - density]
    mass_flux = rest * u[d]
    flux = [mass_flux]
    pushed = inertia * u[d]
    b_over = grown_b[d] * over_sq
    for j in range(3):
        flux_j = pushed * u[j] - b_over * grown_b[j]
        flux.append(flux_j + total_pressure if j == d else flux_j)
    flux.append(carried * u[d] - time_over * grown_b[d] - mass_flux)
    ratio = 1.0 / (enthalpy * inertia)
    sound_sq = 2.0 * pressure * inertia * ratio
    alfven_sq = b_square * enthalpy * ratio
    fast_sq = sound_sq + alfven_sq - sound_sq * alfven_sq
    slow = 1.0 - fast_sq
    velocity = u[d] * over
    rest_part = 1.0 - dot(u, u) * over_sq * fast_sq
    spread = jnp.sqrt(fast_sq * over_sq * (rest_part - velocity * velocity * slow))
    fastest = (jnp.abs(velocity * slow) + spread) / rest_part
    return conserved, flux, fastest


def face_flux(left, right, normal, weight, d):
    sides = []
    for state in (left, right):
        magnetic = [normal if i == d else state[5 + i] for i in range(3)]
        sides.append(face_state(state[0], state[1], state[2:5], magnetic, d))
    (cons_l, flux_l, fast_l), (cons_r, flux_r, fast_r) = sides
    signal = jnp.maximum(fast_l, fast_r)
    scale = 0.5 * weight
    return [scale * (flux_l[q] + flux_r[q] - signal * (cons_r[q] - cons_l[q])) for q in range(5)]


def volume_over(conformal):
    return conformal * jnp.sqrt(conformal)


def first_diff(down_two, down, up, up_two):
    return (8.0 / 12.0) * (up - down) + (1.0 / 12.0) * (down_two - up_two)


class Halo:
    def __init__(
        self, cells, zst, zfl, x_below, y_below, x_above, y_above, x_below_rest, x_above_rest,
        c_below, c_above,
    ):
        x_below = SplitFace(x_below, x_below_rest)
        x_above = SplitFace(x_above, x_above_rest)
        self.fields, self.block, self.lanes = zst.shape
        self.st = cells.at[0 : self.fields]
        self.fl = cells.at[self.fields : self.fields + FLUID]
        self.zst, self.zfl = zst, zfl
        self.x_below, self.x_above = x_below, x_above
        self.y_below, self.y_above = y_below, y_above
        self.c_below, self.c_above = c_below, c_above
        self.cy = self.block // 4
        self.t = Tile(self.cy, self.lanes)
        self.half = self.t.rows
        self.own = self.block // self.half
        self.inner = range(1, self.own + 1)
        self.span = range(self.own + 2)
        self.edge = edge_list(x_below.shape[0])
        self.last = x_below.shape[0] - 1

    def rows_of(self, ref, q, p):
        return ref[q, (p - 1) * self.half : p * self.half, :]

    def main(self, q, p):
        if q < self.fields:
            return self.rows_of(self.st, q, p)
        return self.rows_of(self.fl, q - self.fields, p)

    def beyond(self, q, p):
        if q < self.fields:
            return self.rows_of(self.zst, q, p)
        return self.rows_of(self.zfl, q - self.fields, p)

    def part(self, second):
        return self.t.part_second if second else self.t.part_first

    def beside(self, q, p):
        return self.part(p == 2)(self.y_above[q], self.y_below[q])

    def third_place(self, q):
        return self.fields + FLUID + q // 2, q % 2

    def x_third(self, q, upper):
        tile, which = self.third_place(q)
        found = self.x_above[tile] if upper else self.x_below[tile]
        return self.t.swap(found) if which else found

    def y_third(self, q, p):
        t = self.t
        tile, which = self.third_place(q)
        turn_above, turn_below = ((0, 0), (-1, 1), (2, -2), (1, -1))[2 * which + p - 1]
        above, below = t.turn(self.y_above[tile], turn_above), t.turn(self.y_below[tile], turn_below)
        return jnp.where(t.slot == 2, above, below)

    def z_place(self, q):
        return 4 * self.edge.index(q) + 2

    def x_beyond(self, q, upper):
        tile = self.x_above[self.last] if upper else self.x_below[self.last]
        return self.t.spin(tile, -self.z_place(q))

    def y_beyond(self, q, p):
        return self.t.spin(self.beside(self.last, p), -self.z_place(q))

    def corner(self, q, p):
        whole, single = corner_lists(self.edge)
        if q in single:
            n = single.index(q)
            place, turn = len(whole) + 1 + n // 4, CORNER_TURNS[n % 4]
        else:
            place, turn = whole.index(q), 0
        above, below = self.t.turn(self.c_above[place], -turn), self.t.turn(self.c_below[place], -turn)
        return self.part(p > 0)(above, below)

    def corner_beyond(self, q, p):
        place = len(corner_lists(self.edge)[0])
        tile = self.part(p > 0)(self.c_above[place], self.c_below[place])
        return self.t.spin(tile, -self.z_place(q))

    def plane(self, q):
        own, inner = self.own, self.inner
        return (
            [self.x_below[q]] + [self.main(q, p) for p in inner] + [self.x_above[q]],
            [self.corner(q, 0)] + [self.beside(q, p) for p in inner] + [self.corner(q, own + 1)],
            [self.x_beyond(q, False)]
            + [self.beyond(q, p) for p in inner]
            + [self.x_beyond(q, True)],
            [None] + [self.y_beyond(q, p) for p in inner] + [None],
        )


def weigh(chi_face, alpha_face):
    shrink = volume_over(chi_face)
    return shrink, alpha_face / shrink


def primitives(half, spots, cons, centred, chi, alpha, batch):
    found = {}
    for start in range(0, len(spots), batch):
        group = spots[start : start + batch]

        def gather(planes):
            return jnp.concatenate([planes[k][p] for k, p in group], axis=0)

        shrink = volume_over(gather(chi))
        mag_raw = [gather(centred[i]) for i in range(3)]
        mag = [m * shrink for m in mag_raw]
        values = recover([gather(c) * shrink for c in cons], mag)
        u = values[2:5]
        factor = gather(alpha) * lax.rsqrt(1.0 + dot(u, u))
        field = [
            factor * (u[(i + 2) % 3] * mag_raw[(i + 1) % 3] - u[(i + 1) % 3] * mag_raw[(i + 2) % 3])
            for i in range(3)
        ]
        for n, spot in enumerate(group):
            found[spot] = [value[n * half : (n + 1) * half] for value in values + mag + field]
    return found


def ring_fluxes(prims, chi, alpha, normals, d, up, down):
    found = []
    for here, there in ((0, 1), (1, 0)):
        left, right = [], []
        for a, b in zip(prims[here], prims[there]):
            below = down(a, b, 1)
            middle = a - below
            left.append(below + 0.5 * limited(below - down(a, b, 2), middle))
            right.append(a - 0.5 * limited(middle, up(a, b, 1) - a))
        shrink, weight = weigh(
            0.5 * (chi[here] + down(chi[here], chi[there], 1)),
            0.5 * (alpha[here] + down(alpha[here], alpha[there], 1)),
        )
        found.append(face_flux(left, right, normals[here] * shrink, weight, d))
    return [a - up(a, b, 1) for a, b in zip(*found)]


def early_kernel(
    cells, zst, zfl, x_below, y_below, x_above, y_above, x_below_rest, x_above_rest,
    st_rate, hydro_rate, slopes, shared, pairs, sides, thirds, pairs_z, sides_z, grads, seconds, damped, tensors,
):
    halo = Halo(
        cells, zst, zfl, x_below, y_below, x_above, y_above, x_below_rest, x_above_rest, None, None
    )
    x_below, x_above = halo.x_below, halo.x_above
    t, fields, half, own, cy = halo.t, halo.fields, halo.half, halo.own, halo.cy
    st, fl, inner = halo.st, halo.fl, halo.inner

    for q in range(fields):
        pairs[q, 0] = halo.x_third(q, False)
        pairs[q, 1] = x_below[q]
        for p in inner:
            pairs[q, 1 + p] = halo.main(q, p)
            sides[q, p - 1] = halo.beside(q, p)
            thirds[q, p - 1] = halo.y_third(q, p)
        pairs[q, 2 + own] = x_above[q]
        pairs[q, 3 + own] = halo.x_third(q, True)
        if q < CURVED:
            pairs_z[q, 0] = halo.x_beyond(q, False)
            pairs_z[q, own + 1] = halo.x_beyond(q, True)
            for p in inner:
                pairs_z[q, p] = halo.beyond(q, p)
                sides_z[q, p - 1] = halo.y_beyond(q, p)

    def both(q):
        return [[None] + [read(q, p) for p in inner] for read in (halo.main, halo.beyond)]

    bx, by, bz = both(fields + 5), both(fields + 6), both(fields + 7)
    normals = bz
    bx = [
        [None] + [0.5 * (v[p] + t.odd(v[p], (v[1:] + [end])[p])) for p in inner]
        for v, end in zip(bx, (x_above[fields + 5], halo.x_beyond(fields + 5, True)))
    ]
    by = [
        [None] + [0.5 * (v[p] + t.y_up(v[p], read(fields + 6, p), 1)) for p in inner]
        for v, read in zip(by, (halo.beside, halo.y_beyond))
    ]
    bz = [
        [None] + [0.5 * (a[p] + t.z_up(a[p], b[p], 1)) for p in inner]
        for a, b in ((bz[0], bz[1]), (bz[1], bz[0]))
    ]
    chi, alpha = both(0), both(7)
    spots = [(k, p) for k in range(2) for p in inner]
    found = primitives(
        half, spots, [both(fields + q) for q in range(5)], [bx, by, bz], chi, alpha, len(spots)
    )
    for (k, p), values in found.items():
        for i, value in enumerate(values):
            shared[k * own + p - 1, i] = value
    for p in inner:
        prims = [found[k, p][:8] for k in range(2)]
        changes = ring_fluxes(
            prims,
            [chi[k][p] for k in range(2)],
            [alpha[k][p] for k in range(2)],
            [normals[k][p] for k in range(2)],
            2,
            t.z_up,
            t.z_down,
        )
        for q in range(5):
            tensors[p - 1, 6 + q] = changes[q]
        rest, pressure = prims[0][:2]
        u = prims[0][2:5]
        parts = stress_parts(rest, pressure, u, prims[0][5:8])
        lorentz_sq, over, over_sq, time_b, grown_b, b_square, enthalpy, inertia = parts
        total_pressure = pressure + 0.5 * b_square
        for s, (i, j) in enumerate(INDEX_PAIRS):
            value = inertia * u[i] * u[j] - over_sq * (grown_b[i] * grown_b[j])
            tensors[p - 1, s] = value + total_pressure if i == j else value

    def pair_step(index, carry):
        p = index + 1
        base = pl.multiple_of(index * half, half)

        for q in range(fields):
            centre = pairs[q, p + 1]
            x_m3 = t.odd(pairs[q, p - 1], pairs[q, p])
            x_m2 = pairs[q, p]
            x_m1 = t.odd(pairs[q, p], centre)
            x_p1 = t.odd(centre, pairs[q, p + 2])
            x_p2 = pairs[q, p + 2]
            x_p3 = t.odd(pairs[q, p + 2], pairs[q, p + 3])
            side, third = sides[q, index], thirds[q, index]
            y_m1, y_m2 = t.y_down(centre, side, 1), t.y_down(centre, side, 2)
            y_p1, y_p2 = t.y_up(centre, side, 1), t.y_up(centre, side, 2)
            y_m3 = t.turn(
                jnp.where(t.slot >= cy - 2, side, jnp.where(t.slot == cy - 3, third, centre)), 3
            )
            y_p3 = t.turn(jnp.where(t.slot < 2, side, jnp.where(t.slot == 2, third, centre)), -3)
            beyond = zst[q, pl.ds(base, half), :]
            z_m1, z_m2, z_m3 = (t.z_down(centre, beyond, k) for k in (1, 2, 3))
            z_p1, z_p2, z_p3 = (t.z_up(centre, beyond, k) for k in (1, 2, 3))
            dx = first_diff(x_m2, x_m1, x_p1, x_p2)
            dy = first_diff(y_m2, y_m1, y_p1, y_p2)
            grads[q, 0] = dx
            if q < CURVED:
                slopes[q, index] = dx
            grads[q, 1] = dy
            grads[q, 2] = first_diff(z_m2, z_m1, z_p1, z_p2)
            near = [x_m1 + x_p1, y_m1 + y_p1, z_m1 + z_p1]
            far = [x_m2 + x_p2, y_m2 + y_p2, z_m2 + z_p2]
            outer = (x_m3 + x_p3) + (y_m3 + y_p3) + (z_m3 + z_p3)
            damped[q] = (DISSIPATION / 64.0) * (
                outer - 6.0 * (far[0] + far[1] + far[2]) + 15.0 * (near[0] + near[1] + near[2])
                - 60.0 * centre
            )
            if q < CURVED:
                for s, d in ((0, 0), (3, 1), (5, 2)):
                    seconds[q, s] = (1.0 / 12.0) * (16.0 * near[d] - far[d] - 30.0 * centre)
                b_m, b_c, b_p = pairs_z[q, p - 1], pairs_z[q, p], pairs_z[q, p + 1]
                dx_z = first_diff(b_m, t.odd(b_m, b_c), t.odd(b_c, b_p), b_p)
                b_s = sides_z[q, p - 1]
                dy_z = first_diff(
                    t.y_down(b_c, b_s, 2),
                    t.y_down(b_c, b_s, 1),
                    t.y_up(b_c, b_s, 1),
                    t.y_up(b_c, b_s, 2),
                )
                for s, inside, outside in ((2, dx, dx_z), (4, dy, dy_z)):
                    seconds[q, s] = first_diff(
                        t.z_down(inside, outside, 2),
                        t.z_down(inside, outside, 1),
                        t.z_up(inside, outside, 1),
                        t.z_up(inside, outside, 2),
                    )

        def value(q):
            return pairs[q, p + 1]

        def fluid_value(q):
            return fl[q, pl.ds(base, half), :]

        conformal, lapse = value(0), value(7)
        over_chi = 1.0 / conformal
        metric = symmetric([value(1 + s) for s in range(6)])
        shift = [value(8 + i) for i in range(3)]
        extrinsic, theta = value(11), value(21)
        traceless = symmetric([value(12 + s) for s in range(6)])
        connection = [value(18 + i) for i in range(3)]
        inverse = inverse_metric(metric)
        grad = [[grads[q, k] for k in range(3)] for q in range(fields)]
        chi_grad, lapse_grad = grad[0], grad[7]
        shift_grad = [[grad[8 + i][k] for i in range(3)] for k in range(3)]
        trace_k = extrinsic + 2.0 * theta

        stress = symmetric([tensors[p - 1, s] for s in range(6)])
        held = [fluid_value(q) for q in range(5)]
        shrink = volume_over(conformal)
        energy = held[4] + held[0]
        third_k = trace_k * (1.0 / 3.0)
        curved = [
            [
                (traceless[i][j] + metric[i][j] * third_k) if i <= j else None for j in range(3)
            ]
            for i in range(3)
        ]
        work = (
            stress[0][0] * curved[0][0]
            + stress[1][1] * curved[1][1]
            + stress[2][2] * curved[2][2]
            + 2.0
            * (
                stress[0][1] * curved[0][1]
                + stress[0][2] * curved[0][2]
                + stress[1][2] * curved[1][2]
            )
        )
        rates = [tensors[p - 1, 6 + q] for q in range(5)]
        for i in range(3):
            rates[1 + i] = (
                rates[1 + i]
                - energy * lapse_grad[i]
                + total([held[1 + k] * grad[8 + k][i] for k in range(3)])
            )
        rates[4] = (
            rates[4] + lapse * work * over_chi / shrink - dot(held[1:4], lapse_grad)
        )
        for q in range(5):
            hydro_rate[q, pl.ds(base, half), :] = rates[q]
        density = energy * shrink
        momentum = [held[1 + i] * shrink for i in range(3)]

        lowered = [[[None] * 3 for _ in range(3)] for _ in range(3)]
        for i in range(3):
            for j in range(3):
                for k in range(j, 3):
                    got = 0.5 * (
                        grad[1 + slot_of(i, k)][j]
                        + grad[1 + slot_of(i, j)][k]
                        - grad[1 + slot_of(j, k)][i]
                    )
                    lowered[i][j][k] = lowered[i][k][j] = got
        raised = [[[None] * 3 for _ in range(3)] for _ in range(3)]
        for i in range(3):
            for j in range(3):
                for k in range(j, 3):
                    got = total([inverse[i][l] * lowered[l][j][k] for l in range(3)])
                    raised[i][j][k] = raised[i][k][j] = got
        contracted = [trace_with(inverse, raised[i]) for i in range(3)]

        def hessian_trace(q):
            return (
                inverse[0][0] * seconds[q, 0]
                + inverse[1][1] * seconds[q, 3]
                + inverse[2][2] * seconds[q, 5]
                + 2.0 * (inverse[0][2] * seconds[q, 2] + inverse[1][2] * seconds[q, 4])
            )

        def second_cov(q, slope):
            bent = [total([raised[k][i][j] * slope[k] for k in range(3)]) for i, j in INDEX_PAIRS]
            return symmetric(
                [-bent[s] if s == 1 else seconds[q, s] - bent[s] for s in range(len(bent))]
            )

        chi_cov = second_cov(0, chi_grad)
        chi_lap = trace_with(inverse, chi_cov)
        raised_chi = [dot(inverse[i], chi_grad) for i in range(3)]
        chi_square = dot(raised_chi, chi_grad)
        cross_term = dot(raised_chi, lapse_grad)
        half_chi = 0.5 * over_chi
        plain_cov = second_cov(7, lapse_grad)
        lapse_cov = symmetric(
            [
                plain_cov[i][j]
                + (
                    chi_grad[i] * lapse_grad[j]
                    + chi_grad[j] * lapse_grad[i]
                    - metric[i][j] * cross_term
                )
                * half_chi
                for i, j in INDEX_PAIRS
            ]
        )
        lapse_lap = conformal * trace_with(inverse, lapse_cov)

        mixed = [
            [[dot(inverse[l], lowered[k][j]) for j in range(3)] for k in range(3)]
            for l in range(3)
        ]
        quarter_sq = half_chi * half_chi
        metric_factor = chi_lap * half_chi - 3.0 * chi_square * quarter_sq
        ricci = []
        for i, j in INDEX_PAIRS:
            second_part = -0.5 * hessian_trace(1 + slot_of(i, j))
            connection_part = 0.5 * total(
                [metric[k][i] * grad[18 + k][j] + metric[k][j] * grad[18 + k][i] for k in range(3)]
            )
            contracted_part = 0.5 * total(
                [contracted[k] * (lowered[i][j][k] + lowered[j][i][k]) for k in range(3)]
            )
            if i == j:
                quadratic = total(
                    [
                        raised[k][l][i] * (2.0 * mixed[l][i][k] + mixed[l][k][i])
                        for k in range(3)
                        for l in range(3)
                    ]
                )
            else:
                quadratic = total(
                    [
                        raised[k][l][i] * (mixed[l][j][k] + mixed[l][k][j])
                        + raised[k][l][j] * mixed[l][i][k]
                        for k in range(3)
                        for l in range(3)
                    ]
                )
            conformal_part = (
                chi_cov[i][j] * half_chi
                + metric[i][j] * metric_factor
                - chi_grad[i] * chi_grad[j] * quarter_sq
            )
            ricci.append(
                second_part + connection_part + contracted_part + quadratic + conformal_part
            )
        ricci = symmetric(ricci)
        ricci_scalar = conformal * trace_with(inverse, ricci)
        stress_trace = conformal * trace_with(inverse, stress)

        up_a = [
            [total([inverse[i][k] * traceless[k][j] for k in range(3)]) for j in range(3)]
            for i in range(3)
        ]
        raised_a = symmetric(
            [total([up_a[i][l] * inverse[j][l] for l in range(3)]) for i, j in INDEX_PAIRS]
        )
        a_square = trace_with(traceless, raised_a)
        shift_div = shift_grad[0][0] + shift_grad[1][1] + shift_grad[2][2]
        two_thirds_div = (2.0 / 3.0) * shift_div

        def finish(q, rate):
            rate = rate + dot(shift, grad[q]) + damped[q]
            st_rate[q, pl.ds(base, half), :] = rate

        finish(0, (2.0 / 3.0) * conformal * (lapse * trace_k - shift_div))
        finish(7, -2.0 * lapse * extrinsic)
        for i in range(3):
            finish(8 + i, 0.75 * connection[i] - SHIFT_DAMPING * shift[i])
        finish(
            11,
            lapse
            * (
                a_square
                + trace_k * trace_k * (1.0 / 3.0)
                + FOUR_PI * (stress_trace + density)
                + KAPPA_ONE * theta
            )
            - lapse_lap,
        )
        source = symmetric(
            [
                lapse * (ricci[i][j] - 2.0 * FOUR_PI * stress[i][j]) - lapse_cov[i][j]
                for i, j in INDEX_PAIRS
            ]
        )
        third_trace = trace_with(inverse, source) * (1.0 / 3.0)
        for s, (i, j) in enumerate(INDEX_PAIRS):
            finish(
                1 + s,
                total(
                    [
                        metric[i][k] * shift_grad[j][k] + metric[j][k] * shift_grad[i][k]
                        for k in range(3)
                    ]
                )
                - metric[i][j] * two_thirds_div
                - 2.0 * lapse * traceless[i][j],
            )
            product = total([traceless[i][k] * up_a[k][j] for k in range(3)])
            finish(
                12 + s,
                total(
                    [
                        traceless[i][k] * shift_grad[j][k] + traceless[j][k] * shift_grad[i][k]
                        for k in range(3)
                    ]
                )
                - traceless[i][j] * two_thirds_div
                + conformal * (source[i][j] - metric[i][j] * third_trace)
                + lapse * (trace_k * traceless[i][j] - 2.0 * product),
            )
        for i in range(3):
            bracket = (
                trace_with(raised_a, raised[i])
                - 1.5 * dot(raised_a[i], chi_grad) * over_chi
                - dot(inverse[i], [2.0 * grad[11][j] + grad[21][j] for j in range(3)]) * (1.0 / 3.0)
                - 2.0 * FOUR_PI * dot(inverse[i], momentum)
            )
            spread = [
                seconds[8, 0] + seconds[10, 2],
                seconds[9, 3] + seconds[10, 4],
                seconds[8, 2] + seconds[9, 4] + seconds[10, 5],
            ]
            finish(
                18 + i,
                contracted[i] * two_thirds_div
                - total([contracted[j] * shift_grad[j][i] for j in range(3)])
                + hessian_trace(8 + i)
                + dot(inverse[i], spread) * (1.0 / 3.0)
                - 2.0 * dot(raised_a[i], lapse_grad)
                + 2.0
                * lapse
                * (bracket - KAPPA_ONE * (connection[i] - contracted[i])),
            )
        finish(
            21,
            0.5
            * lapse
            * (
                ricci_scalar
                - a_square
                + (2.0 / 3.0) * trace_k * trace_k
                - 4.0 * FOUR_PI * density
            )
            - 2.0 * KAPPA_ONE * lapse * theta,
        )
        return carry

    lax.fori_loop(0, own, pair_step, 0)


def late_kernel(
    cells, zst, zfl, x_below, y_below, x_above, y_above, x_below_rest, x_above_rest,
    c_below, c_above, line_two, line_top,
    st_rate, hydro_rate, slopes, shared, st_out, fl_out,
):
    halo = Halo(
        cells, zst, zfl, x_below, y_below, x_above, y_above, x_below_rest, x_above_rest,
        c_below, c_above,
    )
    t, fields, half, own = halo.t, halo.fields, halo.half, halo.own
    inner, span = halo.inner, halo.span

    top = jnp.maximum(line_top[...], line_two[...])
    speed_tile = len(corner_lists(halo.edge)[0])
    for lines in (c_below, c_above):
        top = jnp.maximum(top, lines[speed_tile, 0:1, halo.lanes - 1 : halo.lanes])
    dt = COURANT / top

    for p in inner:
        place = slice((p - 1) * half, p * half)
        mixed = []
        for q in range(CURVED):
            s_m, s_c, s_p = (
                halo.beside(q, n) if 1 <= n <= own else halo.corner(q, n) for n in (p - 1, p, p + 1)
            )
            slope = slopes[q, p - 1]
            slope_side = first_diff(s_m, t.odd_swapped(s_m, s_c), t.odd_swapped(s_c, s_p), s_p)
            mixed.append(
                first_diff(
                    t.y_down(slope, slope_side, 2),
                    t.y_down(slope, slope_side, 1),
                    t.y_up(slope, slope_side, 1),
                    t.y_up(slope, slope_side, 2),
                )
            )
        conformal, lapse = halo.main(0, p), halo.main(7, p)
        metric = [halo.main(1 + s, p) for s in range(6)]
        inverse = inverse_metric(symmetric(metric))
        half_chi = 0.5 / conformal
        cross = inverse[0][1]
        chi_trace = 2.0 * cross * mixed[0] * half_chi
        ricci = [metric[s] * chi_trace - cross * mixed[1 + s] for s in range(6)]
        ricci[1] = ricci[1] + mixed[0] * half_chi
        source = [lapse * r for r in ricci]
        source[1] = source[1] - mixed[7]
        third_trace = trace_with(inverse, symmetric(source)) * (1.0 / 3.0)
        extra = {
            11: -2.0 * conformal * cross * mixed[7],
            21: 0.5 * lapse * conformal * trace_with(inverse, symmetric(ricci)),
        }
        for s in range(6):
            extra[12 + s] = conformal * (source[s] - metric[s] * third_trace)
        for i in range(3):
            extra[18 + i] = 2.0 * cross * mixed[8 + i] + (1.0 / 3.0) * (
                inverse[i][0] * mixed[9] + inverse[i][1] * mixed[8]
            )
        for q in range(fields):
            rate = st_rate[q, place, :]
            if q in extra:
                rate = rate + extra[q]
            st_out[q, place, :] = halo.main(q, p) + dt * rate

    v, h, vz, hz = halo.plane(fields + 5)
    hz[own + 1] = halo.corner_beyond(fields + 5, own + 1)
    v_next = v[1:] + [halo.x_third(fields, True)]
    face_x = v
    bx = (
        [0.5 * (v[p] + t.odd(v[p], v_next[p])) for p in span],
        [0.5 * (h[p] + t.odd_swapped(h[p], h[min(p + 1, own + 1)])) for p in span],
        [0.5 * (vz[p] + t.odd(vz[p], vz[min(p + 1, own + 1)])) for p in span],
        [None] + [0.5 * (hz[p] + t.odd_swapped(hz[p], hz[p + 1])) for p in inner] + [None],
    )
    v, h, vz, hz = halo.plane(fields + 6)
    hz[0] = halo.corner_beyond(fields + 6, 0)
    hz[own + 1] = halo.corner_beyond(fields + 6, own + 1)
    face_y = v, h
    full = [
        jnp.where(t.slot == 2, halo.y_third(fields, p), h[p]) if 1 <= p <= own else h[p] for p in span
    ]
    by = (
        [0.5 * (v[p] + t.y_up(v[p], h[p], 1)) for p in span],
        [0.5 * (h[p] + t.y_up(full[p], v[p], 1)) for p in span],
        [0.5 * (vz[p] + t.y_up(vz[p], hz[p], 1)) for p in span],
        [None] + [0.5 * (hz[p] + t.y_up(hz[p], vz[p], 1)) for p in inner] + [None],
    )
    v, h, vz, hz = halo.plane(fields + 7)
    bz = (v, h, vz, hz)

    chi, alpha = halo.plane(0), halo.plane(7)
    spots = [(0, 0), (0, own + 1)] + [(1, p) for p in span] + [(2, 0), (2, own + 1)]
    spots += [(3, p) for p in inner]
    found = primitives(
        half, spots, [halo.plane(fields + q) for q in range(5)], [bx, by, bz], chi, alpha, 5
    )
    for k, kind in enumerate((0, 2)):
        for p in inner:
            found[kind, p] = [shared[k * own + p - 1, i] for i in range(11)]

    lines = [[found[0, p][i] for p in span] for i in range(8)] + [chi[0], alpha[0]]
    odd_lines = [[t.odd(f[p], f[min(p + 1, own + 1)]) for p in span] for f in lines]
    fluxes = [None]
    for p in range(1, own + 2):
        left, right = [], []
        for f, o in zip(lines[:8], odd_lines):
            here = f[p] - o[p - 1]
            left.append(o[p - 1] + 0.5 * limited(o[p - 1] - f[p - 1], here))
            right.append(f[p] - 0.5 * limited(here, o[p] - f[p]))
        shrink, weight = weigh(
            0.5 * (lines[8][p] + odd_lines[8][p - 1]), 0.5 * (lines[9][p] + odd_lines[9][p - 1])
        )
        fluxes.append(face_flux(left, right, face_x[p] * shrink, weight, 0))
    for p in inner:
        changes = ring_fluxes(
            [found[k, p][:8] for k in range(2)],
            [chi[k][p] for k in range(2)],
            [alpha[k][p] for k in range(2)],
            [face_y[k][p] for k in range(2)],
            1,
            t.y_up,
            t.y_down,
        )
        place = slice((p - 1) * half, p * half)
        for q in range(5):
            change = fluxes[p][q] - t.odd(fluxes[p][q], fluxes[p + 1][q])
            rate = hydro_rate[q, place, :] + change + changes[q]
            fl_out[q, place, :] = halo.main(fields + q, p) + dt * rate

    ex, ey, ez = (
        [[found[k, p][8 + i] if (k, p) in found else None for p in span] for k in range(4)]
        for i in range(3)
    )
    ez_x = [
        [ez[0][p] + t.odd(ez[0][p - 1], ez[0][p]) if p else None for p in span],
        [ez[1][p] + t.odd_swapped(ez[1][p - 1], ez[1][p]) if p else None for p in span],
    ]
    ey_x = [
        [ey[k][p] + t.odd(ey[k][p - 1], ey[k][p]) if p else None for p in span] for k in (0, 2)
    ]
    edge_z = [None] + [ez_x[0][p] + t.y_down(ez_x[0][p], ez_x[1][p], 1) for p in span[1:]]
    edge_z_h = [None] + [ez_x[1][p] + t.y_down(ez_x[1][p], ez_x[0][p], 1) for p in inner]
    edge_y = [None] + [ey_x[0][p] + t.z_down(ey_x[0][p], ey_x[1][p], 1) for p in span[1:]]
    edge_y_z = [None] + [ey_x[1][p] + t.z_down(ey_x[1][p], ey_x[0][p], 1) for p in inner]
    for p in inner:
        ex_y = ex[0][p] + t.y_down(ex[0][p], ex[1][p], 1)
        ex_y_h = ex[1][p] + t.y_down(ex[1][p], ex[0][p], 1)
        ex_y_z = ex[2][p] + t.y_down(ex[2][p], ex[3][p], 1)
        ex_y_hz = ex[3][p] + t.y_down(ex[3][p], ex[2][p], 1)
        edge_x = ex_y + t.z_down(ex_y, ex_y_z, 1)
        edge_x_h = ex_y_h + t.z_down(ex_y_h, ex_y_hz, 1)
        edge_x_z = ex_y_z + t.z_down(ex_y_z, ex_y, 1)
        x_rate = (t.z_up(edge_y[p], edge_y_z[p], 1) - edge_y[p]) - (
            t.y_up(edge_z[p], edge_z_h[p], 1) - edge_z[p]
        )
        y_rate = (t.odd(edge_z[p], edge_z[p + 1]) - edge_z[p]) - (
            t.z_up(edge_x, edge_x_z, 1) - edge_x
        )
        z_rate = (t.y_up(edge_x, edge_x_h, 1) - edge_x) - (
            t.odd(edge_y[p], edge_y[p + 1]) - edge_y[p]
        )
        quarter = 0.25 * dt
        for i, rate in enumerate((x_rate, y_rate, z_rate)):
            fl_out[5 + i, (p - 1) * half : p * half, :] = (
                halo.main(fields + 5 + i, p) + quarter * rate
            )


def per_device(spacetime, fluid):
    fields, cx, cy, cz = spacetime.shape
    rows = cx * cy
    st = spacetime.reshape(fields, rows, cz)
    fl = fluid.reshape(FLUID, rows, cz)
    sizes = [lax.axis_size(a) for a in ("gx", "gy", "gz")]
    tile = (2 * cy, cz)
    f32 = jnp.float32

    def shape(*dims):
        return jax.ShapeDtypeStruct(dims, f32)

    def beyond(cells):
        n = sizes[2]
        after = lax.ppermute(cells, "gz", [((i + 1) % n, i) for i in range(n)])
        if n == 2:
            return after
        before = lax.ppermute(cells, "gz", [(i, (i + 1) % n) for i in range(n)])
        lane = lax.broadcasted_iota(jnp.int32, cells.shape, 2)
        return jnp.where(lane < cz // 2, after, before)

    params = pltpu.CompilerParams(vmem_limit_bytes=48 * 1024 * 1024)
    zst, zfl = beyond(st), beyond(fl)
    cells = jnp.concatenate([st, fl], axis=0)
    face = shape(face_tiles(fields), *tile)
    whole, single = corner_lists(edge_list(face_tiles(fields)))
    corner = shape(len(whole) + 1 + (len(single) + 3) // 4, *tile)
    lane_row = shape(1, cz)
    near = shape(CURVED + FLUID + 1, *tile)
    rest = shape(face.shape[0] - near.shape[0], *tile)
    x_low, x_low_rest, x_high, x_high_rest, y_low, y_high, top = pl.pallas_call(
        pack_kernel,
        out_shape=[near, rest, near, rest, face, face, lane_row],
        compiler_params=params,
        name="pack",
    )(cells, zst, zfl)

    def move(cells, dx, dy):
        nx, ny = sizes[0], sizes[1]
        hops = [
            (i * ny + j, ((i + dx) % nx) * ny + (j + dy) % ny) for i in range(nx) for j in range(ny)
        ]
        return lax.ppermute(cells, ("gx", "gy"), hops)

    short = sizes[0] <= 4 and sizes[1] <= 4 and sizes[2] <= 2
    x_below = move(x_high, 1, 0)
    y_below = move(y_high, 0, 1)
    x_above = move(x_low, -1, 0)
    y_above = move(y_low, 0, -1)
    x_below_rest = move(x_high_rest, 1, 0)
    x_above_rest = move(x_low_rest, -1, 0)
    top_two = move(top, 2, 0) if short and sizes[0] == 4 else top
    c_low, c_high, line_top = pl.pallas_call(
        relay_kernel,
        out_shape=[corner, corner, lane_row],
        compiler_params=params,
        name="relay",
    )(x_below, x_above, y_below, top, top_two)
    c_above = move(c_low, 0, -1)
    c_below = move(c_high, 0, 1)
    if not short:
        line_two = lax.pmax(line_top, ("gx", "gy", "gz"))
    else:
        line_two = move(line_top, 0, 2) if sizes[1] == 4 else line_top
    own = cx // 2
    arrived = (cells, zst, zfl, x_below, y_below, x_above, y_above, x_below_rest, x_above_rest)
    early = pl.pallas_call(
        early_kernel,
        out_shape=[
            shape(*st.shape),
            shape(5, rows, cz),
            shape(CURVED, own, *tile),
            shape(2 * own, 11, *tile),
        ],
        scratch_shapes=[
            pltpu.VMEM((fields, own + 4) + tile, f32),
            pltpu.VMEM((fields, own) + tile, f32),
            pltpu.VMEM((fields, own) + tile, f32),
            pltpu.VMEM((CURVED, own + 2) + tile, f32),
            pltpu.VMEM((CURVED, own) + tile, f32),
            pltpu.VMEM((fields, 3) + tile, f32),
            pltpu.VMEM((CURVED, 6) + tile, f32),
            pltpu.VMEM((fields,) + tile, f32),
            pltpu.VMEM((own, 11) + tile, f32),
        ],
        compiler_params=params,
        name="early",
    )(*arrived)
    st_next, fl_next = pl.pallas_call(
        late_kernel,
        out_shape=[shape(*st.shape), shape(*fl.shape)],
        compiler_params=params,
        name="late",
    )(*arrived, c_below, c_above, line_two, line_top, *early)
    return st_next.reshape(spacetime.shape), fl_next.reshape(fluid.shape)


def solution(mesh):
    spec = P(None, "gx", "gy", "gz")
    return jax.shard_map(
        per_device, mesh=mesh, in_specs=(spec, spec), out_specs=(spec, spec), check_vma=False
    )
```

```python
import functools
import math

import jax
import jax.numpy as jnp
from jax import lax
from jax.experimental import pallas as pl
from jax.experimental.pallas import tpu as pltpu
from jax.sharding import PartitionSpec as P

RECOVERY_STEPS = 4
INDEX_PAIRS = ((0, 0), (0, 1), (0, 2), (1, 1), (1, 2), (2, 2))
COURANT = 0.25
DISSIPATION = 0.2
KAPPA_ONE = 0.02
SHIFT_DAMPING = 1.0
SPEED_CAP = 0.99
PRESSURE_FLOOR = 0.01
FOUR_PI = 4.0 * math.pi

CURVED = 11
FLUID = 8


def total(pieces):
    summed = pieces[0]
    for member in pieces[1:]:
        summed = summed + member
    return summed


def dot(first_vec, second_vec):
    return total([first_vec[i] * second_vec[i] for i in range(3)])


def slot_of(i, j):
    return INDEX_PAIRS.index((min(i, j), max(i, j)))


def symmetric(entries):
    return [[entries[slot_of(i, j)] for j in range(3)] for i in range(3)]


def trace_with(inverse, tensor):
    return (
        inverse[0][0] * tensor[0][0]
        + inverse[1][1] * tensor[1][1]
        + inverse[2][2] * tensor[2][2]
        + 2.0
        * (
            inverse[0][1] * tensor[0][1]
            + inverse[0][2] * tensor[0][2]
            + inverse[1][2] * tensor[1][2]
        )
    )


def inverse_metric(metric):
    cofactor = [
        metric[1][1] * metric[2][2] - metric[1][2] * metric[1][2],
        metric[0][2] * metric[1][2] - metric[0][1] * metric[2][2],
        metric[0][1] * metric[1][2] - metric[0][2] * metric[1][1],
        metric[0][0] * metric[2][2] - metric[0][2] * metric[0][2],
        metric[0][1] * metric[0][2] - metric[0][0] * metric[1][2],
        metric[0][0] * metric[1][1] - metric[0][1] * metric[0][1],
    ]
    determinant = (
        metric[0][0] * cofactor[0] + metric[0][1] * cofactor[1] + metric[0][2] * cofactor[2]
    )
    over = 1.0 / determinant
    return symmetric([c * over for c in cofactor])


class Tile:
    def __init__(self, cy, cz):
        self.cy, self.rows, self.lanes = cy, 2 * cy, cz
        shape = (self.rows, cz)
        self.row = lax.broadcasted_iota(jnp.int32, shape, 0)
        self.lane = lax.broadcasted_iota(jnp.int32, shape, 1)
        self.slot = lax.rem(self.row, cy)

    def turn(self, tile, amount):
        amount = amount % self.rows
        return tile if amount == 0 else pltpu.roll(tile, amount, 0)

    def spin(self, tile, amount):
        amount = amount % self.lanes
        return tile if amount == 0 else pltpu.roll(tile, amount, 1)

    def swap(self, tile):
        return self.turn(tile, self.cy)

    def odd(self, a, b):
        return self.turn(jnp.where(self.row < self.cy, b, a), self.cy)

    def odd_swapped(self, a, b):
        return self.turn(jnp.where(self.row < self.cy, a, b), self.cy)

    def y_up(self, main, beyond, k):
        return self.turn(jnp.where(self.slot < k, beyond, main), -k)

    def y_down(self, main, beyond, k):
        return self.turn(jnp.where(self.slot >= self.cy - k, beyond, main), k)

    def z_up(self, main, beyond, k):
        return self.spin(jnp.where(self.lane < k, beyond, main), -k)

    def z_down(self, main, beyond, k):
        return self.spin(jnp.where(self.lane >= self.lanes - k, beyond, main), k)

    def corner_rows(self, side, turn):
        places = ((0, 2), (self.cy - 1, self.cy + 1))[side]
        first, second = [(place + turn) % self.rows for place in places]
        return (self.row == first) | (self.row == second)

    def join_low(self, u, v):
        return jnp.where(self.slot < 2, self.swap(u), self.turn(v, 2))

    def join_high(self, u, v):
        return jnp.where(self.slot >= self.cy - 2, self.swap(u), self.turn(self.swap(v), -2))

    def part_first(self, from_above, from_below):
        return jnp.where(self.slot < 2, from_above, from_below)

    def part_second(self, from_above, from_below):
        return self.turn(jnp.where(self.slot < 2, from_below, from_above), 2)


def edge_list(tiles):
    fields = next(n for n in range(tiles) if face_tiles(n) == tiles)
    return list(range(CURVED)) + list(range(fields, fields + FLUID))


CORNER_TURNS = (0, 1, 4, 5)


def corner_lists(edge):
    faces = edge[CURVED + 5 : CURVED + 7]
    return edge[:CURVED] + faces, edge[CURVED : CURVED + 5] + edge[CURVED + 7 :]


def face_tiles(fields):
    return fields + FLUID + len(pairs_of(third_list(fields))) + 1


def third_list(fields):
    return list(range(fields + 1))


def pairs_of(items):
    return [(items[i], items[min(i + 1, len(items) - 1)]) for i in range(0, len(items), 2)]


def top_speed(st):
    inverse = inverse_metric(symmetric([st[1 + s] for s in range(6)]))
    scale = 2.0 * st[7] * st[0]
    speeds = [jnp.abs(st[8 + d]) + jnp.sqrt(scale * inverse[d][d]) for d in range(3)]
    top = jnp.maximum(jnp.maximum(speeds[0], speeds[1]), speeds[2])
    return jnp.max(jnp.max(top, axis=1, keepdims=True), axis=0, keepdims=True)


def pack_kernel(cells, zst, zfl, *outs):
    fields, rows, lanes = zst.shape
    st, fl = cells.at[0:fields], cells.at[fields : fields + FLUID]
    cy = rows // 4
    t = Tile(cy, lanes)
    x_low, x_high, y_low, y_high, top_out = outs
    half = t.rows

    def own(ref, q):
        return [ref[q, 0:half, :], ref[q, half : 2 * half, :]]

    tiles, beyond = [], []
    for q in range(fields):
        tiles.append(own(st, q))
        beyond.append(own(zst, q) if q < CURVED else None)
    for q in range(FLUID - 1):
        tiles.append(own(fl, q))
        beyond.append(own(zfl, q))
    along, along_z = own(fl, FLUID - 1), own(zfl, FLUID - 1)
    tiles.append([0.5 * (along[p] + t.z_up(along[p], along_z[p], 1)) for p in range(2)])
    beyond.append([0.5 * (along_z[p] + t.z_up(along_z[p], along[p], 1)) for p in range(2)])

    packed = [None] * 4
    place = 0
    for q, (first, second) in enumerate(tiles):
        x_low[q] = first
        x_high[q] = second
        y_low[q] = t.join_low(first, second)
        y_high[q] = t.join_high(first, second)
        if beyond[q] is not None:
            zf, zs = beyond[q]
            for m, piece in enumerate((zf, zs, t.join_low(zf, zs), t.join_high(zf, zs))):
                piece = t.spin(piece, 4 * place + 2)
                packed[m] = (
                    piece if place == 0 else jnp.where(t.lane < 4 * place, packed[m], piece)
                )
            place += 1
    for n, (a, b) in enumerate(pairs_of(third_list(fields))):
        slot = fields + FLUID + n
        xa, xb = (tiles[q if q < fields else fields + 5] for q in (a, b))
        x_low[slot] = jnp.where(t.row < cy, xa[1], t.swap(xb[1]))
        x_high[slot] = jnp.where(t.row < cy, t.swap(xb[0]), xa[0])
        ya, yb = (tiles[q if q < fields else fields + 6] for q in (a, b))
        w = [t.swap(ya[0]), t.swap(ya[1]), t.swap(yb[0]), t.swap(yb[1])]
        s = t.slot
        y_low[slot] = jnp.where(
            s == 2,
            w[0],
            jnp.where(s == 3, t.turn(w[1], 1), jnp.where(s == 0, t.turn(w[2], -2), t.turn(w[3], -1))),
        )
        y_high[slot] = jnp.where(
            s == 1,
            w[0],
            jnp.where(s == 0, t.turn(w[1], -1), jnp.where(s == 3, t.turn(w[2], 2), t.turn(w[3], 1))),
        )
    top = jnp.maximum(top_speed(st), top_speed(zst))
    top_out[...] = jnp.broadcast_to(top, top_out.shape)
    last = x_low.shape[0] - 1
    for out, piece in zip((x_low, x_high, y_low, y_high), packed):
        out[last] = jnp.where(t.lane < 4 * place, piece, top)


def relay_kernel(place, x_below, x_above, y_below, top, top_two, chunks, line_top):
    cy, lanes = x_below.shape[1] // 2, x_below.shape[2]
    t = Tile(cy, lanes)
    last = x_below.shape[0] - 1
    line = jnp.maximum(top[...], top_two[...])
    for beside in (x_below, x_above, y_below):
        line = jnp.maximum(line, beside[last, 0:1, lanes - 1 : lanes])
    line_top[...] = line
    edge = edge_list(x_below.shape[0])
    whole, single = corner_lists(edge)
    count = chunks.shape[0]
    for other in range(count):
        chunks[other, len(whole)] = jnp.broadcast_to(line, (t.rows, lanes))
    to_low = chunks.at[lax.rem(place[0] + (count - 1), count)]
    to_high = chunks.at[lax.rem(place[0] + 1, count)]
    for n, q in enumerate(whole + [last]):
        low = t.join_low(x_below[q], x_above[q])
        high = t.join_high(x_below[q], x_above[q])
        if q == last:
            low = jnp.where(t.lane < 4 * len(edge), low, line)
            high = jnp.where(t.lane < 4 * len(edge), high, line)
        to_low[n] = low
        to_high[n] = high
    for n in range(0, len(single), 4):
        low, high = None, None
        for turn, q in zip(CORNER_TURNS, single[n : n + 4]):
            below = t.turn(t.join_low(x_below[q], x_above[q]), turn)
            above = t.turn(t.join_high(x_below[q], x_above[q]), turn)
            if low is None:
                low, high = below, above
            else:
                low = jnp.where(t.corner_rows(0, turn), below, low)
                high = jnp.where(t.corner_rows(1, turn), above, high)
        to_low[len(whole) + 1 + n // 4] = low
        to_high[len(whole) + 1 + n // 4] = high


def limited(a, b):
    return jnp.maximum(jnp.minimum(a, b), 0.0) + jnp.minimum(jnp.maximum(a, b), 0.0)


def recover(conserved, magnetic):
    density = conserved[0]
    momenta = conserved[1:4]
    energy = conserved[4] + density
    mom_sq = dot(momenta, momenta)
    mag_sq = dot(magnetic, magnetic)
    cross = dot(momenta, magnetic)
    cross_sq = cross * cross

    def state(z):
        grown = z + mag_sq
        over = 1.0 / (z * grown)
        speed_sq = (mom_sq * z * z + cross_sq * (2.0 * z + mag_sq)) * over * over
        kept = 1.0 - jnp.minimum(speed_sq, SPEED_CAP)
        rest = density * jnp.sqrt(kept)
        return kept, rest, 0.5 * (z * kept - rest), grown * over

    z = jnp.maximum(energy - 0.5 * mag_sq, density)
    for _ in range(RECOVERY_STEPS):
        kept, rest, pressure, over_z = state(z)
        residual = (
            z
            + mag_sq
            - pressure
            - 0.5 * mag_sq * kept
            - 0.5 * cross_sq * over_z * over_z
            - energy
        )
        z = jnp.maximum(z - residual / (1.0 - 0.5 * kept), density)
    kept, rest, pressure, over_z = state(z)
    pressure = jnp.maximum(pressure, PRESSURE_FLOOR * rest)
    scale = lax.rsqrt(kept) / (z + mag_sq)
    along = cross * over_z
    four_vel = [scale * (momenta[i] + along * magnetic[i]) for i in range(3)]
    return [rest, pressure] + four_vel


def stress_parts(rest, pressure, u, magnetic):
    lorentz_sq = 1.0 + dot(u, u)
    over = lax.rsqrt(lorentz_sq)
    over_sq = over * over
    time_b = dot(u, magnetic)
    grown_b = [magnetic[i] + time_b * u[i] for i in range(3)]
    b_square = (dot(magnetic, magnetic) + time_b * time_b) * over_sq
    enthalpy = rest + 2.0 * pressure
    inertia = enthalpy + b_square
    return lorentz_sq, over, over_sq, time_b, grown_b, b_square, enthalpy, inertia


def face_state(rest, pressure, u, magnetic, d):
    lorentz_sq, over, over_sq, time_b, grown_b, b_square, enthalpy, inertia = stress_parts(
        rest, pressure, u, magnetic
    )
    total_pressure = pressure + 0.5 * b_square
    lorentz = lorentz_sq * over
    density = rest * lorentz
    carried = inertia * lorentz
    time_over = time_b * over
    conserved = [density]
    conserved += [carried * u[j] - time_over * grown_b[j] for j in range(3)]
    conserved += [inertia * lorentz_sq - total_pressure - time_b * time_b - density]
    mass_flux = rest * u[d]
    flux = [mass_flux]
    pushed = inertia * u[d]
    b_over = grown_b[d] * over_sq
    for j in range(3):
        flux_j = pushed * u[j] - b_over * grown_b[j]
        flux.append(flux_j + total_pressure if j == d else flux_j)
    flux.append(carried * u[d] - time_over * grown_b[d] - mass_flux)
    ratio = 1.0 / (enthalpy * inertia)
    sound_sq = 2.0 * pressure * inertia * ratio
    alfven_sq = b_square * enthalpy * ratio
    fast_sq = sound_sq + alfven_sq - sound_sq * alfven_sq
    slow = 1.0 - fast_sq
    velocity = u[d] * over
    rest_part = 1.0 - dot(u, u) * over_sq * fast_sq
    spread = jnp.sqrt(fast_sq * over_sq * (rest_part - velocity * velocity * slow))
    fastest = (jnp.abs(velocity * slow) + spread) / rest_part
    return conserved, flux, fastest


def face_flux(left, right, normal, weight, d):
    sides = []
    for state in (left, right):
        magnetic = [normal if i == d else state[5 + i] for i in range(3)]
        sides.append(face_state(state[0], state[1], state[2:5], magnetic, d))
    (cons_l, flux_l, fast_l), (cons_r, flux_r, fast_r) = sides
    signal = jnp.maximum(fast_l, fast_r)
    scale = 0.5 * weight
    return [scale * (flux_l[q] + flux_r[q] - signal * (cons_r[q] - cons_l[q])) for q in range(5)]


def volume_over(conformal):
    return conformal * jnp.sqrt(conformal)


def first_diff(down_two, down, up, up_two):
    return (8.0 / 12.0) * (up - down) + (1.0 / 12.0) * (down_two - up_two)


class Halo:
    def __init__(self, cells, zst, zfl, x_below, y_below, x_above, y_above, c_below, c_above):
        self.fields, self.block, self.lanes = zst.shape
        self.st = cells.at[0 : self.fields]
        self.fl = cells.at[self.fields : self.fields + FLUID]
        self.zst, self.zfl = zst, zfl
        self.x_below, self.x_above = x_below, x_above
        self.y_below, self.y_above = y_below, y_above
        self.c_below, self.c_above = c_below, c_above
        self.cy = self.block // 4
        self.t = Tile(self.cy, self.lanes)
        self.half = self.t.rows
        self.own = self.block // self.half
        self.inner = range(1, self.own + 1)
        self.span = range(self.own + 2)
        self.edge = edge_list(x_below.shape[0])
        self.last = x_below.shape[0] - 1

    def rows_of(self, ref, q, p):
        return ref[q, (p - 1) * self.half : p * self.half, :]

    def main(self, q, p):
        if q < self.fields:
            return self.rows_of(self.st, q, p)
        return self.rows_of(self.fl, q - self.fields, p)

    def beyond(self, q, p):
        if q < self.fields:
            return self.rows_of(self.zst, q, p)
        return self.rows_of(self.zfl, q - self.fields, p)

    def part(self, second):
        return self.t.part_second if second else self.t.part_first

    def beside(self, q, p):
        return self.part(p == 2)(self.y_above[q], self.y_below[q])

    def third_place(self, q):
        return self.fields + FLUID + q // 2, q % 2

    def x_third(self, q, upper):
        tile, which = self.third_place(q)
        found = self.x_above[tile] if upper else self.x_below[tile]
        return self.t.swap(found) if which else found

    def y_third(self, q, p):
        t = self.t
        tile, which = self.third_place(q)
        turn_above, turn_below = ((0, 0), (-1, 1), (2, -2), (1, -1))[2 * which + p - 1]
        above, below = t.turn(self.y_above[tile], turn_above), t.turn(self.y_below[tile], turn_below)
        return jnp.where(t.slot == 2, above, below)

    def z_place(self, q):
        return 4 * self.edge.index(q) + 2

    def x_beyond(self, q, upper):
        tile = self.x_above[self.last] if upper else self.x_below[self.last]
        return self.t.spin(tile, -self.z_place(q))

    def y_beyond(self, q, p):
        return self.t.spin(self.beside(self.last, p), -self.z_place(q))

    def corner(self, q, p):
        whole, single = corner_lists(self.edge)
        if q in single:
            n = single.index(q)
            place, turn = len(whole) + 1 + n // 4, CORNER_TURNS[n % 4]
        else:
            place, turn = whole.index(q), 0
        above, below = self.t.turn(self.c_above[place], -turn), self.t.turn(self.c_below[place], -turn)
        return self.part(p > 0)(above, below)

    def corner_beyond(self, q, p):
        place = len(corner_lists(self.edge)[0])
        tile = self.part(p > 0)(self.c_above[place], self.c_below[place])
        return self.t.spin(tile, -self.z_place(q))

    def plane(self, q):
        own, inner = self.own, self.inner
        return (
            [self.x_below[q]] + [self.main(q, p) for p in inner] + [self.x_above[q]],
            [self.corner(q, 0)] + [self.beside(q, p) for p in inner] + [self.corner(q, own + 1)],
            [self.x_beyond(q, False)]
            + [self.beyond(q, p) for p in inner]
            + [self.x_beyond(q, True)],
            [None] + [self.y_beyond(q, p) for p in inner] + [None],
        )


def weigh(chi_face, alpha_face):
    shrink = volume_over(chi_face)
    return shrink, alpha_face / shrink


def primitives(half, spots, cons, centred, chi, alpha, batch):
    found = {}
    for start in range(0, len(spots), batch):
        group = spots[start : start + batch]

        def gather(planes):
            return jnp.concatenate([planes[k][p] for k, p in group], axis=0)

        shrink = volume_over(gather(chi))
        mag_raw = [gather(centred[i]) for i in range(3)]
        mag = [m * shrink for m in mag_raw]
        values = recover([gather(c) * shrink for c in cons], mag)
        u = values[2:5]
        factor = gather(alpha) * lax.rsqrt(1.0 + dot(u, u))
        field = [
            factor * (u[(i + 2) % 3] * mag_raw[(i + 1) % 3] - u[(i + 1) % 3] * mag_raw[(i + 2) % 3])
            for i in range(3)
        ]
        for n, spot in enumerate(group):
            found[spot] = [value[n * half : (n + 1) * half] for value in values + mag + field]
    return found


def ring_fluxes(prims, chi, alpha, normals, d, up, down):
    found = []
    for here, there in ((0, 1), (1, 0)):
        left, right = [], []
        for a, b in zip(prims[here], prims[there]):
            below = down(a, b, 1)
            middle = a - below
            left.append(below + 0.5 * limited(below - down(a, b, 2), middle))
            right.append(a - 0.5 * limited(middle, up(a, b, 1) - a))
        shrink, weight = weigh(
            0.5 * (chi[here] + down(chi[here], chi[there], 1)),
            0.5 * (alpha[here] + down(alpha[here], alpha[there], 1)),
        )
        found.append(face_flux(left, right, normals[here] * shrink, weight, d))
    return [a - up(a, b, 1) for a, b in zip(*found)]


def early_kernel(
    cells, zst, zfl, x_below, y_below, x_above, y_above,
    st_rate, hydro_rate, slopes, shared, pairs, sides, thirds, pairs_z, sides_z, grads, seconds, damped, tensors,
):
    halo = Halo(cells, zst, zfl, x_below, y_below, x_above, y_above, None, None)
    t, fields, half, own, cy = halo.t, halo.fields, halo.half, halo.own, halo.cy
    st, fl, inner = halo.st, halo.fl, halo.inner

    for q in range(fields):
        pairs[q, 0] = halo.x_third(q, False)
        pairs[q, 1] = x_below[q]
        for p in inner:
            pairs[q, 1 + p] = halo.main(q, p)
            sides[q, p - 1] = halo.beside(q, p)
            thirds[q, p - 1] = halo.y_third(q, p)
        pairs[q, 2 + own] = x_above[q]
        pairs[q, 3 + own] = halo.x_third(q, True)
        if q < CURVED:
            pairs_z[q, 0] = halo.x_beyond(q, False)
            pairs_z[q, own + 1] = halo.x_beyond(q, True)
            for p in inner:
                pairs_z[q, p] = halo.beyond(q, p)
                sides_z[q, p - 1] = halo.y_beyond(q, p)

    def both(q):
        return [[None] + [read(q, p) for p in inner] for read in (halo.main, halo.beyond)]

    bx, by, bz = both(fields + 5), both(fields + 6), both(fields + 7)
    normals = bz
    bx = [
        [None] + [0.5 * (v[p] + t.odd(v[p], (v[1:] + [end])[p])) for p in inner]
        for v, end in zip(bx, (x_above[fields + 5], halo.x_beyond(fields + 5, True)))
    ]
    by = [
        [None] + [0.5 * (v[p] + t.y_up(v[p], read(fields + 6, p), 1)) for p in inner]
        for v, read in zip(by, (halo.beside, halo.y_beyond))
    ]
    bz = [
        [None] + [0.5 * (a[p] + t.z_up(a[p], b[p], 1)) for p in inner]
        for a, b in ((bz[0], bz[1]), (bz[1], bz[0]))
    ]
    chi, alpha = both(0), both(7)
    spots = [(k, p) for k in range(2) for p in inner]
    found = primitives(
        half, spots, [both(fields + q) for q in range(5)], [bx, by, bz], chi, alpha, len(spots)
    )
    for (k, p), values in found.items():
        for i, value in enumerate(values):
            shared[k * own + p - 1, i] = value
    for p in inner:
        prims = [found[k, p][:8] for k in range(2)]
        changes = ring_fluxes(
            prims,
            [chi[k][p] for k in range(2)],
            [alpha[k][p] for k in range(2)],
            [normals[k][p] for k in range(2)],
            2,
            t.z_up,
            t.z_down,
        )
        for q in range(5):
            tensors[p - 1, 6 + q] = changes[q]
        rest, pressure = prims[0][:2]
        u = prims[0][2:5]
        parts = stress_parts(rest, pressure, u, prims[0][5:8])
        lorentz_sq, over, over_sq, time_b, grown_b, b_square, enthalpy, inertia = parts
        total_pressure = pressure + 0.5 * b_square
        for s, (i, j) in enumerate(INDEX_PAIRS):
            value = inertia * u[i] * u[j] - over_sq * (grown_b[i] * grown_b[j])
            tensors[p - 1, s] = value + total_pressure if i == j else value

    def pair_step(index, carry):
        p = index + 1
        base = pl.multiple_of(index * half, half)

        for q in range(fields):
            centre = pairs[q, p + 1]
            x_m3 = t.odd(pairs[q, p - 1], pairs[q, p])
            x_m2 = pairs[q, p]
            x_m1 = t.odd(pairs[q, p], centre)
            x_p1 = t.odd(centre, pairs[q, p + 2])
            x_p2 = pairs[q, p + 2]
            x_p3 = t.odd(pairs[q, p + 2], pairs[q, p + 3])
            side, third = sides[q, index], thirds[q, index]
            y_m1, y_m2 = t.y_down(centre, side, 1), t.y_down(centre, side, 2)
            y_p1, y_p2 = t.y_up(centre, side, 1), t.y_up(centre, side, 2)
            y_m3 = t.turn(
                jnp.where(t.slot >= cy - 2, side, jnp.where(t.slot == cy - 3, third, centre)), 3
            )
            y_p3 = t.turn(jnp.where(t.slot < 2, side, jnp.where(t.slot == 2, third, centre)), -3)
            beyond = zst[q, pl.ds(base, half), :]
            z_m1, z_m2, z_m3 = (t.z_down(centre, beyond, k) for k in (1, 2, 3))
            z_p1, z_p2, z_p3 = (t.z_up(centre, beyond, k) for k in (1, 2, 3))
            dx = first_diff(x_m2, x_m1, x_p1, x_p2)
            dy = first_diff(y_m2, y_m1, y_p1, y_p2)
            grads[q, 0] = dx
            if q < CURVED:
                slopes[q, index] = dx
            grads[q, 1] = dy
            grads[q, 2] = first_diff(z_m2, z_m1, z_p1, z_p2)
            near = [x_m1 + x_p1, y_m1 + y_p1, z_m1 + z_p1]
            far = [x_m2 + x_p2, y_m2 + y_p2, z_m2 + z_p2]
            outer = (x_m3 + x_p3) + (y_m3 + y_p3) + (z_m3 + z_p3)
            damped[q] = (DISSIPATION / 64.0) * (
                outer - 6.0 * (far[0] + far[1] + far[2]) + 15.0 * (near[0] + near[1] + near[2])
                - 60.0 * centre
            )
            if q < CURVED:
                for s, d in ((0, 0), (3, 1), (5, 2)):
                    seconds[q, s] = (1.0 / 12.0) * (16.0 * near[d] - far[d] - 30.0 * centre)
                b_m, b_c, b_p = pairs_z[q, p - 1], pairs_z[q, p], pairs_z[q, p + 1]
                dx_z = first_diff(b_m, t.odd(b_m, b_c), t.odd(b_c, b_p), b_p)
                b_s = sides_z[q, p - 1]
                dy_z = first_diff(
                    t.y_down(b_c, b_s, 2),
                    t.y_down(b_c, b_s, 1),
                    t.y_up(b_c, b_s, 1),
                    t.y_up(b_c, b_s, 2),
                )
                for s, inside, outside in ((2, dx, dx_z), (4, dy, dy_z)):
                    seconds[q, s] = first_diff(
                        t.z_down(inside, outside, 2),
                        t.z_down(inside, outside, 1),
                        t.z_up(inside, outside, 1),
                        t.z_up(inside, outside, 2),
                    )

        def value(q):
            return pairs[q, p + 1]

        def fluid_value(q):
            return fl[q, pl.ds(base, half), :]

        conformal, lapse = value(0), value(7)
        over_chi = 1.0 / conformal
        metric = symmetric([value(1 + s) for s in range(6)])
        shift = [value(8 + i) for i in range(3)]
        extrinsic, theta = value(11), value(21)
        traceless = symmetric([value(12 + s) for s in range(6)])
        connection = [value(18 + i) for i in range(3)]
        inverse = inverse_metric(metric)
        grad = [[grads[q, k] for k in range(3)] for q in range(fields)]
        chi_grad, lapse_grad = grad[0], grad[7]
        shift_grad = [[grad[8 + i][k] for i in range(3)] for k in range(3)]
        trace_k = extrinsic + 2.0 * theta

        stress = symmetric([tensors[p - 1, s] for s in range(6)])
        held = [fluid_value(q) for q in range(5)]
        shrink = volume_over(conformal)
        energy = held[4] + held[0]
        third_k = trace_k * (1.0 / 3.0)
        curved = [
            [
                (traceless[i][j] + metric[i][j] * third_k) if i <= j else None for j in range(3)
            ]
            for i in range(3)
        ]
        work = (
            stress[0][0] * curved[0][0]
            + stress[1][1] * curved[1][1]
            + stress[2][2] * curved[2][2]
            + 2.0
            * (
                stress[0][1] * curved[0][1]
                + stress[0][2] * curved[0][2]
                + stress[1][2] * curved[1][2]
            )
        )
        rates = [tensors[p - 1, 6 + q] for q in range(5)]
        for i in range(3):
            rates[1 + i] = (
                rates[1 + i]
                - energy * lapse_grad[i]
                + total([held[1 + k] * grad[8 + k][i] for k in range(3)])
            )
        rates[4] = (
            rates[4] + lapse * work * over_chi / shrink - dot(held[1:4], lapse_grad)
        )
        for q in range(5):
            hydro_rate[q, pl.ds(base, half), :] = rates[q]
        density = energy * shrink
        momentum = [held[1 + i] * shrink for i in range(3)]

        lowered = [[[None] * 3 for _ in range(3)] for _ in range(3)]
        for i in range(3):
            for j in range(3):
                for k in range(j, 3):
                    got = 0.5 * (
                        grad[1 + slot_of(i, k)][j]
                        + grad[1 + slot_of(i, j)][k]
                        - grad[1 + slot_of(j, k)][i]
                    )
                    lowered[i][j][k] = lowered[i][k][j] = got
        raised = [[[None] * 3 for _ in range(3)] for _ in range(3)]
        for i in range(3):
            for j in range(3):
                for k in range(j, 3):
                    got = total([inverse[i][l] * lowered[l][j][k] for l in range(3)])
                    raised[i][j][k] = raised[i][k][j] = got
        contracted = [trace_with(inverse, raised[i]) for i in range(3)]

        def hessian_trace(q):
            return (
                inverse[0][0] * seconds[q, 0]
                + inverse[1][1] * seconds[q, 3]
                + inverse[2][2] * seconds[q, 5]
                + 2.0 * (inverse[0][2] * seconds[q, 2] + inverse[1][2] * seconds[q, 4])
            )

        def second_cov(q, slope):
            bent = [total([raised[k][i][j] * slope[k] for k in range(3)]) for i, j in INDEX_PAIRS]
            return symmetric(
                [-bent[s] if s == 1 else seconds[q, s] - bent[s] for s in range(len(bent))]
            )

        chi_cov = second_cov(0, chi_grad)
        chi_lap = trace_with(inverse, chi_cov)
        raised_chi = [dot(inverse[i], chi_grad) for i in range(3)]
        chi_square = dot(raised_chi, chi_grad)
        cross_term = dot(raised_chi, lapse_grad)
        half_chi = 0.5 * over_chi
        plain_cov = second_cov(7, lapse_grad)
        lapse_cov = symmetric(
            [
                plain_cov[i][j]
                + (
                    chi_grad[i] * lapse_grad[j]
                    + chi_grad[j] * lapse_grad[i]
                    - metric[i][j] * cross_term
                )
                * half_chi
                for i, j in INDEX_PAIRS
            ]
        )
        lapse_lap = conformal * trace_with(inverse, lapse_cov)

        mixed = [
            [[dot(inverse[l], lowered[k][j]) for j in range(3)] for k in range(3)]
            for l in range(3)
        ]
        quarter_sq = half_chi * half_chi
        metric_factor = chi_lap * half_chi - 3.0 * chi_square * quarter_sq
        ricci = []
        for i, j in INDEX_PAIRS:
            second_part = -0.5 * hessian_trace(1 + slot_of(i, j))
            connection_part = 0.5 * total(
                [metric[k][i] * grad[18 + k][j] + metric[k][j] * grad[18 + k][i] for k in range(3)]
            )
            contracted_part = 0.5 * total(
                [contracted[k] * (lowered[i][j][k] + lowered[j][i][k]) for k in range(3)]
            )
            if i == j:
                quadratic = total(
                    [
                        raised[k][l][i] * (2.0 * mixed[l][i][k] + mixed[l][k][i])
                        for k in range(3)
                        for l in range(3)
                    ]
                )
            else:
                quadratic = total(
                    [
                        raised[k][l][i] * (mixed[l][j][k] + mixed[l][k][j])
                        + raised[k][l][j] * mixed[l][i][k]
                        for k in range(3)
                        for l in range(3)
                    ]
                )
            conformal_part = (
                chi_cov[i][j] * half_chi
                + metric[i][j] * metric_factor
                - chi_grad[i] * chi_grad[j] * quarter_sq
            )
            ricci.append(
                second_part + connection_part + contracted_part + quadratic + conformal_part
            )
        ricci = symmetric(ricci)
        ricci_scalar = conformal * trace_with(inverse, ricci)
        stress_trace = conformal * trace_with(inverse, stress)

        up_a = [
            [total([inverse[i][k] * traceless[k][j] for k in range(3)]) for j in range(3)]
            for i in range(3)
        ]
        raised_a = symmetric(
            [total([up_a[i][l] * inverse[j][l] for l in range(3)]) for i, j in INDEX_PAIRS]
        )
        a_square = trace_with(traceless, raised_a)
        shift_div = shift_grad[0][0] + shift_grad[1][1] + shift_grad[2][2]
        two_thirds_div = (2.0 / 3.0) * shift_div

        def finish(q, rate):
            rate = rate + dot(shift, grad[q]) + damped[q]
            st_rate[q, pl.ds(base, half), :] = rate

        finish(0, (2.0 / 3.0) * conformal * (lapse * trace_k - shift_div))
        finish(7, -2.0 * lapse * extrinsic)
        for i in range(3):
            finish(8 + i, 0.75 * connection[i] - SHIFT_DAMPING * shift[i])
        finish(
            11,
            lapse
            * (
                a_square
                + trace_k * trace_k * (1.0 / 3.0)
                + FOUR_PI * (stress_trace + density)
                + KAPPA_ONE * theta
            )
            - lapse_lap,
        )
        source = symmetric(
            [
                lapse * (ricci[i][j] - 2.0 * FOUR_PI * stress[i][j]) - lapse_cov[i][j]
                for i, j in INDEX_PAIRS
            ]
        )
        third_trace = trace_with(inverse, source) * (1.0 / 3.0)
        for s, (i, j) in enumerate(INDEX_PAIRS):
            finish(
                1 + s,
                total(
                    [
                        metric[i][k] * shift_grad[j][k] + metric[j][k] * shift_grad[i][k]
                        for k in range(3)
                    ]
                )
                - metric[i][j] * two_thirds_div
                - 2.0 * lapse * traceless[i][j],
            )
            product = total([traceless[i][k] * up_a[k][j] for k in range(3)])
            finish(
                12 + s,
                total(
                    [
                        traceless[i][k] * shift_grad[j][k] + traceless[j][k] * shift_grad[i][k]
                        for k in range(3)
                    ]
                )
                - traceless[i][j] * two_thirds_div
                + conformal * (source[i][j] - metric[i][j] * third_trace)
                + lapse * (trace_k * traceless[i][j] - 2.0 * product),
            )
        for i in range(3):
            bracket = (
                trace_with(raised_a, raised[i])
                - 1.5 * dot(raised_a[i], chi_grad) * over_chi
                - dot(inverse[i], [2.0 * grad[11][j] + grad[21][j] for j in range(3)]) * (1.0 / 3.0)
                - 2.0 * FOUR_PI * dot(inverse[i], momentum)
            )
            spread = [
                seconds[8, 0] + seconds[10, 2],
                seconds[9, 3] + seconds[10, 4],
                seconds[8, 2] + seconds[9, 4] + seconds[10, 5],
            ]
            finish(
                18 + i,
                contracted[i] * two_thirds_div
                - total([contracted[j] * shift_grad[j][i] for j in range(3)])
                + hessian_trace(8 + i)
                + dot(inverse[i], spread) * (1.0 / 3.0)
                - 2.0 * dot(raised_a[i], lapse_grad)
                + 2.0
                * lapse
                * (bracket - KAPPA_ONE * (connection[i] - contracted[i])),
            )
        finish(
            21,
            0.5
            * lapse
            * (
                ricci_scalar
                - a_square
                + (2.0 / 3.0) * trace_k * trace_k
                - 4.0 * FOUR_PI * density
            )
            - 2.0 * KAPPA_ONE * lapse * theta,
        )
        return carry

    lax.fori_loop(0, own, pair_step, 0)


def late_kernel(
    place, cells, zst, zfl, x_below, y_below, x_above, y_above, chunks, line_top,
    st_rate, hydro_rate, slopes, shared, st_out, fl_out,
):
    count = chunks.shape[0]
    c_below = chunks.at[lax.rem(place[0] + (count - 1), count)]
    c_above = chunks.at[lax.rem(place[0] + 1, count)]
    halo = Halo(cells, zst, zfl, x_below, y_below, x_above, y_above, c_below, c_above)
    t, fields, half, own = halo.t, halo.fields, halo.half, halo.own
    inner, span = halo.inner, halo.span

    top = line_top[...]
    speed_tile = len(corner_lists(halo.edge)[0])
    for other in range(count):
        top = jnp.maximum(top, chunks[other, speed_tile, 0:1, halo.lanes - 1 : halo.lanes])
    dt = COURANT / top

    for p in inner:
        place = slice((p - 1) * half, p * half)
        mixed = []
        for q in range(CURVED):
            s_m, s_c, s_p = (
                halo.beside(q, n) if 1 <= n <= own else halo.corner(q, n) for n in (p - 1, p, p + 1)
            )
            slope = slopes[q, p - 1]
            slope_side = first_diff(s_m, t.odd_swapped(s_m, s_c), t.odd_swapped(s_c, s_p), s_p)
            mixed.append(
                first_diff(
                    t.y_down(slope, slope_side, 2),
                    t.y_down(slope, slope_side, 1),
                    t.y_up(slope, slope_side, 1),
                    t.y_up(slope, slope_side, 2),
                )
            )
        conformal, lapse = halo.main(0, p), halo.main(7, p)
        metric = [halo.main(1 + s, p) for s in range(6)]
        inverse = inverse_metric(symmetric(metric))
        half_chi = 0.5 / conformal
        cross = inverse[0][1]
        chi_trace = 2.0 * cross * mixed[0] * half_chi
        ricci = [metric[s] * chi_trace - cross * mixed[1 + s] for s in range(6)]
        ricci[1] = ricci[1] + mixed[0] * half_chi
        source = [lapse * r for r in ricci]
        source[1] = source[1] - mixed[7]
        third_trace = trace_with(inverse, symmetric(source)) * (1.0 / 3.0)
        extra = {
            11: -2.0 * conformal * cross * mixed[7],
            21: 0.5 * lapse * conformal * trace_with(inverse, symmetric(ricci)),
        }
        for s in range(6):
            extra[12 + s] = conformal * (source[s] - metric[s] * third_trace)
        for i in range(3):
            extra[18 + i] = 2.0 * cross * mixed[8 + i] + (1.0 / 3.0) * (
                inverse[i][0] * mixed[9] + inverse[i][1] * mixed[8]
            )
        for q in range(fields):
            rate = st_rate[q, place, :]
            if q in extra:
                rate = rate + extra[q]
            st_out[q, place, :] = halo.main(q, p) + dt * rate

    v, h, vz, hz = halo.plane(fields + 5)
    hz[own + 1] = halo.corner_beyond(fields + 5, own + 1)
    v_next = v[1:] + [halo.x_third(fields, True)]
    face_x = v
    bx = (
        [0.5 * (v[p] + t.odd(v[p], v_next[p])) for p in span],
        [0.5 * (h[p] + t.odd_swapped(h[p], h[min(p + 1, own + 1)])) for p in span],
        [0.5 * (vz[p] + t.odd(vz[p], vz[min(p + 1, own + 1)])) for p in span],
        [None] + [0.5 * (hz[p] + t.odd_swapped(hz[p], hz[p + 1])) for p in inner] + [None],
    )
    v, h, vz, hz = halo.plane(fields + 6)
    hz[0] = halo.corner_beyond(fields + 6, 0)
    hz[own + 1] = halo.corner_beyond(fields + 6, own + 1)
    face_y = v, h
    full = [
        jnp.where(t.slot == 2, halo.y_third(fields, p), h[p]) if 1 <= p <= own else h[p] for p in span
    ]
    by = (
        [0.5 * (v[p] + t.y_up(v[p], h[p], 1)) for p in span],
        [0.5 * (h[p] + t.y_up(full[p], v[p], 1)) for p in span],
        [0.5 * (vz[p] + t.y_up(vz[p], hz[p], 1)) for p in span],
        [None] + [0.5 * (hz[p] + t.y_up(hz[p], vz[p], 1)) for p in inner] + [None],
    )
    v, h, vz, hz = halo.plane(fields + 7)
    bz = (v, h, vz, hz)

    chi, alpha = halo.plane(0), halo.plane(7)
    spots = [(0, 0), (0, own + 1)] + [(1, p) for p in span] + [(2, 0), (2, own + 1)]
    spots += [(3, p) for p in inner]
    found = primitives(
        half, spots, [halo.plane(fields + q) for q in range(5)], [bx, by, bz], chi, alpha, 5
    )
    for k, kind in enumerate((0, 2)):
        for p in inner:
            found[kind, p] = [shared[k * own + p - 1, i] for i in range(11)]

    lines = [[found[0, p][i] for p in span] for i in range(8)] + [chi[0], alpha[0]]
    odd_lines = [[t.odd(f[p], f[min(p + 1, own + 1)]) for p in span] for f in lines]
    fluxes = [None]
    for p in range(1, own + 2):
        left, right = [], []
        for f, o in zip(lines[:8], odd_lines):
            here = f[p] - o[p - 1]
            left.append(o[p - 1] + 0.5 * limited(o[p - 1] - f[p - 1], here))
            right.append(f[p] - 0.5 * limited(here, o[p] - f[p]))
        shrink, weight = weigh(
            0.5 * (lines[8][p] + odd_lines[8][p - 1]), 0.5 * (lines[9][p] + odd_lines[9][p - 1])
        )
        fluxes.append(face_flux(left, right, face_x[p] * shrink, weight, 0))
    for p in inner:
        changes = ring_fluxes(
            [found[k, p][:8] for k in range(2)],
            [chi[k][p] for k in range(2)],
            [alpha[k][p] for k in range(2)],
            [face_y[k][p] for k in range(2)],
            1,
            t.y_up,
            t.y_down,
        )
        place = slice((p - 1) * half, p * half)
        for q in range(5):
            change = fluxes[p][q] - t.odd(fluxes[p][q], fluxes[p + 1][q])
            rate = hydro_rate[q, place, :] + change + changes[q]
            fl_out[q, place, :] = halo.main(fields + q, p) + dt * rate

    ex, ey, ez = (
        [[found[k, p][8 + i] if (k, p) in found else None for p in span] for k in range(4)]
        for i in range(3)
    )
    ez_x = [
        [ez[0][p] + t.odd(ez[0][p - 1], ez[0][p]) if p else None for p in span],
        [ez[1][p] + t.odd_swapped(ez[1][p - 1], ez[1][p]) if p else None for p in span],
    ]
    ey_x = [
        [ey[k][p] + t.odd(ey[k][p - 1], ey[k][p]) if p else None for p in span] for k in (0, 2)
    ]
    edge_z = [None] + [ez_x[0][p] + t.y_down(ez_x[0][p], ez_x[1][p], 1) for p in span[1:]]
    edge_z_h = [None] + [ez_x[1][p] + t.y_down(ez_x[1][p], ez_x[0][p], 1) for p in inner]
    edge_y = [None] + [ey_x[0][p] + t.z_down(ey_x[0][p], ey_x[1][p], 1) for p in span[1:]]
    edge_y_z = [None] + [ey_x[1][p] + t.z_down(ey_x[1][p], ey_x[0][p], 1) for p in inner]
    for p in inner:
        ex_y = ex[0][p] + t.y_down(ex[0][p], ex[1][p], 1)
        ex_y_h = ex[1][p] + t.y_down(ex[1][p], ex[0][p], 1)
        ex_y_z = ex[2][p] + t.y_down(ex[2][p], ex[3][p], 1)
        ex_y_hz = ex[3][p] + t.y_down(ex[3][p], ex[2][p], 1)
        edge_x = ex_y + t.z_down(ex_y, ex_y_z, 1)
        edge_x_h = ex_y_h + t.z_down(ex_y_h, ex_y_hz, 1)
        edge_x_z = ex_y_z + t.z_down(ex_y_z, ex_y, 1)
        x_rate = (t.z_up(edge_y[p], edge_y_z[p], 1) - edge_y[p]) - (
            t.y_up(edge_z[p], edge_z_h[p], 1) - edge_z[p]
        )
        y_rate = (t.odd(edge_z[p], edge_z[p + 1]) - edge_z[p]) - (
            t.z_up(edge_x, edge_x_z, 1) - edge_x
        )
        z_rate = (t.y_up(edge_x, edge_x_h, 1) - edge_x) - (
            t.odd(edge_y[p], edge_y[p + 1]) - edge_y[p]
        )
        quarter = 0.25 * dt
        for i, rate in enumerate((x_rate, y_rate, z_rate)):
            fl_out[5 + i, (p - 1) * half : p * half, :] = (
                halo.main(fields + 5 + i, p) + quarter * rate
            )


def per_device(spacetime, fluid):
    fields, cx, cy, cz = spacetime.shape
    rows = cx * cy
    st = spacetime.reshape(fields, rows, cz)
    fl = fluid.reshape(FLUID, rows, cz)
    sizes = [lax.axis_size(a) for a in ("gx", "gy", "gz")]
    tile = (2 * cy, cz)
    f32 = jnp.float32

    def shape(*dims):
        return jax.ShapeDtypeStruct(dims, f32)

    def beyond(cells):
        n = sizes[2]
        after = lax.ppermute(cells, "gz", [((i + 1) % n, i) for i in range(n)])
        if n == 2:
            return after
        before = lax.ppermute(cells, "gz", [(i, (i + 1) % n) for i in range(n)])
        lane = lax.broadcasted_iota(jnp.int32, cells.shape, 2)
        return jnp.where(lane < cz // 2, after, before)

    params = pltpu.CompilerParams(vmem_limit_bytes=48 * 1024 * 1024)
    zst, zfl = beyond(st), beyond(fl)
    cells = jnp.concatenate([st, fl], axis=0)
    face = shape(face_tiles(fields), *tile)
    whole, single = corner_lists(edge_list(face_tiles(fields)))
    corner = shape(len(whole) + 1 + (len(single) + 3) // 4, *tile)
    lane_row = shape(1, cz)
    x_low, x_high, y_low, y_high, top = pl.pallas_call(
        pack_kernel, out_shape=[face] * 4 + [lane_row], compiler_params=params, name="pack"
    )(cells, zst, zfl)

    def move(cells, dx, dy):
        nx, ny = sizes[0], sizes[1]
        hops = [
            (i * ny + j, ((i + dx) % nx) * ny + (j + dy) % ny) for i in range(nx) for j in range(ny)
        ]
        return lax.ppermute(cells, ("gx", "gy"), hops)

    short = sizes[0] <= 4 and sizes[2] <= 2
    x_below = move(x_high, 1, 0)
    y_below = move(y_high, 0, 1)
    x_above = move(x_low, -1, 0)
    y_above = move(y_low, 0, -1)
    top_two = move(top, 2, 0) if short and sizes[0] == 4 else top
    place = lax.axis_index("gy").astype(jnp.int32).reshape(1)
    scalar = pl.BlockSpec(memory_space=pltpu.SMEM)
    whole_array = pl.BlockSpec(memory_space=pltpu.VMEM)
    chunks, line_top = pl.pallas_call(
        relay_kernel,
        out_shape=[shape(sizes[1], *corner.shape), lane_row],
        in_specs=[scalar] + [whole_array] * 5,
        compiler_params=params,
        name="relay",
    )(place, x_below, x_above, y_below, top, top_two)
    chunks = lax.all_to_all(chunks, "gy", 0, 0)
    if not short:
        line_top = lax.pmax(line_top, ("gx", "gy", "gz"))
    own = cx // 2
    arrived = (cells, zst, zfl, x_below, y_below, x_above, y_above)
    early = pl.pallas_call(
        early_kernel,
        out_shape=[
            shape(*st.shape),
            shape(5, rows, cz),
            shape(CURVED, own, *tile),
            shape(2 * own, 11, *tile),
        ],
        scratch_shapes=[
            pltpu.VMEM((fields, own + 4) + tile, f32),
            pltpu.VMEM((fields, own) + tile, f32),
            pltpu.VMEM((fields, own) + tile, f32),
            pltpu.VMEM((CURVED, own + 2) + tile, f32),
            pltpu.VMEM((CURVED, own) + tile, f32),
            pltpu.VMEM((fields, 3) + tile, f32),
            pltpu.VMEM((CURVED, 6) + tile, f32),
            pltpu.VMEM((fields,) + tile, f32),
            pltpu.VMEM((own, 11) + tile, f32),
        ],
        compiler_params=params,
        name="early",
    )(*arrived)
    st_next, fl_next = pl.pallas_call(
        late_kernel,
        out_shape=[shape(*st.shape), shape(*fl.shape)],
        in_specs=[scalar] + [whole_array] * 13,
        compiler_params=params,
        name="late",
    )(place, *arrived, chunks, line_top, *early)
    return st_next.reshape(spacetime.shape), fl_next.reshape(fluid.shape)


def solution(mesh):
    spec = P(None, "gx", "gy", "gz")
    return jax.shard_map(
        per_device, mesh=mesh, in_specs=(spec, spec), out_specs=(spec, spec), check_vma=False
    )
```

```python
import functools
import math

import jax
import jax.numpy as jnp
from jax import lax
from jax.experimental import pallas as pl
from jax.experimental.pallas import tpu as pltpu
from jax.sharding import PartitionSpec as P

RECOVERY_STEPS = 4
INDEX_PAIRS = ((0, 0), (0, 1), (0, 2), (1, 1), (1, 2), (2, 2))
COURANT = 0.25
DISSIPATION = 0.2
KAPPA_ONE = 0.02
SHIFT_DAMPING = 1.0
SPEED_CAP = 0.99
PRESSURE_FLOOR = 0.01
FOUR_PI = 4.0 * math.pi

CURVED = 11
FLUID = 8


def total(pieces):
    summed = pieces[0]
    for member in pieces[1:]:
        summed = summed + member
    return summed


def dot(first_vec, second_vec):
    return total([first_vec[i] * second_vec[i] for i in range(3)])


def slot_of(i, j):
    return INDEX_PAIRS.index((min(i, j), max(i, j)))


def symmetric(entries):
    return [[entries[slot_of(i, j)] for j in range(3)] for i in range(3)]


def trace_with(inverse, tensor):
    return (
        inverse[0][0] * tensor[0][0]
        + inverse[1][1] * tensor[1][1]
        + inverse[2][2] * tensor[2][2]
        + 2.0
        * (
            inverse[0][1] * tensor[0][1]
            + inverse[0][2] * tensor[0][2]
            + inverse[1][2] * tensor[1][2]
        )
    )


def inverse_metric(metric):
    cofactor = [
        metric[1][1] * metric[2][2] - metric[1][2] * metric[1][2],
        metric[0][2] * metric[1][2] - metric[0][1] * metric[2][2],
        metric[0][1] * metric[1][2] - metric[0][2] * metric[1][1],
        metric[0][0] * metric[2][2] - metric[0][2] * metric[0][2],
        metric[0][1] * metric[0][2] - metric[0][0] * metric[1][2],
        metric[0][0] * metric[1][1] - metric[0][1] * metric[0][1],
    ]
    determinant = (
        metric[0][0] * cofactor[0] + metric[0][1] * cofactor[1] + metric[0][2] * cofactor[2]
    )
    over = 1.0 / determinant
    return symmetric([c * over for c in cofactor])


class Tile:
    def __init__(self, cy, cz):
        self.cy, self.rows, self.lanes = cy, 2 * cy, cz
        shape = (self.rows, cz)
        self.row = lax.broadcasted_iota(jnp.int32, shape, 0)
        self.lane = lax.broadcasted_iota(jnp.int32, shape, 1)
        self.slot = lax.rem(self.row, cy)

    def turn(self, tile, amount):
        amount = amount % self.rows
        return tile if amount == 0 else pltpu.roll(tile, amount, 0)

    def spin(self, tile, amount):
        amount = amount % self.lanes
        return tile if amount == 0 else pltpu.roll(tile, amount, 1)

    def swap(self, tile):
        return self.turn(tile, self.cy)

    def odd(self, a, b):
        return self.turn(jnp.where(self.row < self.cy, b, a), self.cy)

    def odd_swapped(self, a, b):
        return self.turn(jnp.where(self.row < self.cy, a, b), self.cy)

    def y_up(self, main, beyond, k):
        return self.turn(jnp.where(self.slot < k, beyond, main), -k)

    def y_down(self, main, beyond, k):
        return self.turn(jnp.where(self.slot >= self.cy - k, beyond, main), k)

    def z_up(self, main, beyond, k):
        return self.spin(jnp.where(self.lane < k, beyond, main), -k)

    def z_down(self, main, beyond, k):
        return self.spin(jnp.where(self.lane >= self.lanes - k, beyond, main), k)

    def corner_rows(self, side, turn):
        places = ((0, 2), (self.cy - 1, self.cy + 1))[side]
        first, second = [(place + turn) % self.rows for place in places]
        return (self.row == first) | (self.row == second)

    def join_low(self, u, v):
        return jnp.where(self.slot < 2, self.swap(u), self.turn(v, 2))

    def join_high(self, u, v):
        return jnp.where(self.slot >= self.cy - 2, self.swap(u), self.turn(self.swap(v), -2))

    def part_first(self, from_above, from_below):
        return jnp.where(self.slot < 2, from_above, from_below)

    def part_second(self, from_above, from_below):
        return self.turn(jnp.where(self.slot < 2, from_below, from_above), 2)


def edge_list(tiles):
    fields = next(n for n in range(tiles) if face_tiles(n) == tiles)
    return list(range(CURVED)) + list(range(fields, fields + FLUID))


CORNER_TURNS = (0, 1, 4, 5)


def corner_lists(edge):
    faces = edge[CURVED + 5 : CURVED + 7]
    return edge[:CURVED] + faces, edge[CURVED : CURVED + 5] + edge[CURVED + 7 :]


def face_tiles(fields):
    return fields + FLUID + len(pairs_of(third_list(fields))) + 1


def third_list(fields):
    return list(range(fields + 1))


def pairs_of(items):
    return [(items[i], items[min(i + 1, len(items) - 1)]) for i in range(0, len(items), 2)]


def top_speed(st):
    inverse = inverse_metric(symmetric([st[1 + s] for s in range(6)]))
    scale = 2.0 * st[7] * st[0]
    speeds = [jnp.abs(st[8 + d]) + jnp.sqrt(scale * inverse[d][d]) for d in range(3)]
    top = jnp.maximum(jnp.maximum(speeds[0], speeds[1]), speeds[2])
    return jnp.max(jnp.max(top, axis=1, keepdims=True), axis=0, keepdims=True)


def pack_kernel(cells, zst, zfl, *outs):
    fields, rows, lanes = zst.shape
    st, fl = cells.at[0:fields], cells.at[fields : fields + FLUID]
    cy = rows // 4
    t = Tile(cy, lanes)
    x_low, x_high, y_low, y_high, top_out = outs
    half = t.rows

    def own(ref, q):
        return [ref[q, 0:half, :], ref[q, half : 2 * half, :]]

    tiles, beyond = [], []
    for q in range(fields):
        tiles.append(own(st, q))
        beyond.append(own(zst, q) if q < CURVED else None)
    for q in range(FLUID - 1):
        tiles.append(own(fl, q))
        beyond.append(own(zfl, q))
    along, along_z = own(fl, FLUID - 1), own(zfl, FLUID - 1)
    tiles.append([0.5 * (along[p] + t.z_up(along[p], along_z[p], 1)) for p in range(2)])
    beyond.append([0.5 * (along_z[p] + t.z_up(along_z[p], along[p], 1)) for p in range(2)])

    packed = [None] * 4
    place = 0
    for q, (first, second) in enumerate(tiles):
        x_low[q] = first
        x_high[q] = second
        y_low[q] = t.join_low(first, second)
        y_high[q] = t.join_high(first, second)
        if beyond[q] is not None:
            zf, zs = beyond[q]
            for m, piece in enumerate((zf, zs, t.join_low(zf, zs), t.join_high(zf, zs))):
                piece = t.spin(piece, 4 * place + 2)
                packed[m] = (
                    piece if place == 0 else jnp.where(t.lane < 4 * place, packed[m], piece)
                )
            place += 1
    for n, (a, b) in enumerate(pairs_of(third_list(fields))):
        slot = fields + FLUID + n
        xa, xb = (tiles[q if q < fields else fields + 5] for q in (a, b))
        x_low[slot] = jnp.where(t.row < cy, xa[1], t.swap(xb[1]))
        x_high[slot] = jnp.where(t.row < cy, t.swap(xb[0]), xa[0])
        ya, yb = (tiles[q if q < fields else fields + 6] for q in (a, b))
        w = [t.swap(ya[0]), t.swap(ya[1]), t.swap(yb[0]), t.swap(yb[1])]
        s = t.slot
        y_low[slot] = jnp.where(
            s == 2,
            w[0],
            jnp.where(s == 3, t.turn(w[1], 1), jnp.where(s == 0, t.turn(w[2], -2), t.turn(w[3], -1))),
        )
        y_high[slot] = jnp.where(
            s == 1,
            w[0],
            jnp.where(s == 0, t.turn(w[1], -1), jnp.where(s == 3, t.turn(w[2], 2), t.turn(w[3], 1))),
        )
    top = jnp.maximum(top_speed(st), top_speed(zst))
    top_out[...] = jnp.broadcast_to(top, top_out.shape)
    last = x_low.shape[0] - 1
    for out, piece in zip((x_low, x_high, y_low, y_high), packed):
        out[last] = jnp.where(t.lane < 4 * place, piece, top)


def relay_kernel(x_below, x_above, y_below, top, top_two, to_low, to_high, line_top):
    cy, lanes = x_below.shape[1] // 2, x_below.shape[2]
    t = Tile(cy, lanes)
    last = x_below.shape[0] - 1
    line = jnp.maximum(top[...], top_two[...])
    for beside in (x_below, x_above, y_below):
        line = jnp.maximum(line, beside[last, 0:1, lanes - 1 : lanes])
    line_top[...] = line
    edge = edge_list(x_below.shape[0])
    whole, single = corner_lists(edge)
    for n, q in enumerate(whole + [last]):
        low = t.join_low(x_below[q], x_above[q])
        high = t.join_high(x_below[q], x_above[q])
        if q == last:
            low = jnp.where(t.lane < 4 * len(edge), low, line)
            high = jnp.where(t.lane < 4 * len(edge), high, line)
        to_low[n] = low
        to_high[n] = high
    for n in range(0, len(single), 4):
        low, high = None, None
        for turn, q in zip(CORNER_TURNS, single[n : n + 4]):
            below = t.turn(t.join_low(x_below[q], x_above[q]), turn)
            above = t.turn(t.join_high(x_below[q], x_above[q]), turn)
            if low is None:
                low, high = below, above
            else:
                low = jnp.where(t.corner_rows(0, turn), below, low)
                high = jnp.where(t.corner_rows(1, turn), above, high)
        to_low[len(whole) + 1 + n // 4] = low
        to_high[len(whole) + 1 + n // 4] = high


def limited(a, b):
    return jnp.maximum(jnp.minimum(a, b), 0.0) + jnp.minimum(jnp.maximum(a, b), 0.0)


def recover(conserved, magnetic):
    density = conserved[0]
    momenta = conserved[1:4]
    energy = conserved[4] + density
    mom_sq = dot(momenta, momenta)
    mag_sq = dot(magnetic, magnetic)
    cross = dot(momenta, magnetic)
    cross_sq = cross * cross

    def state(z):
        grown = z + mag_sq
        over = 1.0 / (z * grown)
        speed_sq = (mom_sq * z * z + cross_sq * (2.0 * z + mag_sq)) * over * over
        kept = 1.0 - jnp.minimum(speed_sq, SPEED_CAP)
        rest = density * jnp.sqrt(kept)
        return kept, rest, 0.5 * (z * kept - rest), grown * over

    z = jnp.maximum(energy - 0.5 * mag_sq, density)
    for _ in range(RECOVERY_STEPS):
        kept, rest, pressure, over_z = state(z)
        residual = (
            z
            + mag_sq
            - pressure
            - 0.5 * mag_sq * kept
            - 0.5 * cross_sq * over_z * over_z
            - energy
        )
        z = jnp.maximum(z - residual / (1.0 - 0.5 * kept), density)
    kept, rest, pressure, over_z = state(z)
    pressure = jnp.maximum(pressure, PRESSURE_FLOOR * rest)
    scale = lax.rsqrt(kept) / (z + mag_sq)
    along = cross * over_z
    four_vel = [scale * (momenta[i] + along * magnetic[i]) for i in range(3)]
    return [rest, pressure] + four_vel


def stress_parts(rest, pressure, u, magnetic):
    lorentz_sq = 1.0 + dot(u, u)
    over = lax.rsqrt(lorentz_sq)
    over_sq = over * over
    time_b = dot(u, magnetic)
    grown_b = [magnetic[i] + time_b * u[i] for i in range(3)]
    b_square = (dot(magnetic, magnetic) + time_b * time_b) * over_sq
    enthalpy = rest + 2.0 * pressure
    inertia = enthalpy + b_square
    return lorentz_sq, over, over_sq, time_b, grown_b, b_square, enthalpy, inertia


def face_state(rest, pressure, u, magnetic, d):
    lorentz_sq, over, over_sq, time_b, grown_b, b_square, enthalpy, inertia = stress_parts(
        rest, pressure, u, magnetic
    )
    total_pressure = pressure + 0.5 * b_square
    lorentz = lorentz_sq * over
    density = rest * lorentz
    carried = inertia * lorentz
    time_over = time_b * over
    conserved = [density]
    conserved += [carried * u[j] - time_over * grown_b[j] for j in range(3)]
    conserved += [inertia * lorentz_sq - total_pressure - time_b * time_b - density]
    mass_flux = rest * u[d]
    flux = [mass_flux]
    pushed = inertia * u[d]
    b_over = grown_b[d] * over_sq
    for j in range(3):
        flux_j = pushed * u[j] - b_over * grown_b[j]
        flux.append(flux_j + total_pressure if j == d else flux_j)
    flux.append(carried * u[d] - time_over * grown_b[d] - mass_flux)
    ratio = 1.0 / (enthalpy * inertia)
    sound_sq = 2.0 * pressure * inertia * ratio
    alfven_sq = b_square * enthalpy * ratio
    fast_sq = sound_sq + alfven_sq - sound_sq * alfven_sq
    slow = 1.0 - fast_sq
    velocity = u[d] * over
    rest_part = 1.0 - dot(u, u) * over_sq * fast_sq
    spread = jnp.sqrt(fast_sq * over_sq * (rest_part - velocity * velocity * slow))
    fastest = (jnp.abs(velocity * slow) + spread) / rest_part
    return conserved, flux, fastest


def face_flux(left, right, normal, weight, d):
    sides = []
    for state in (left, right):
        magnetic = [normal if i == d else state[5 + i] for i in range(3)]
        sides.append(face_state(state[0], state[1], state[2:5], magnetic, d))
    (cons_l, flux_l, fast_l), (cons_r, flux_r, fast_r) = sides
    signal = jnp.maximum(fast_l, fast_r)
    scale = 0.5 * weight
    return [scale * (flux_l[q] + flux_r[q] - signal * (cons_r[q] - cons_l[q])) for q in range(5)]


def volume_over(conformal):
    return conformal * jnp.sqrt(conformal)


def first_diff(down_two, down, up, up_two):
    return (8.0 / 12.0) * (up - down) + (1.0 / 12.0) * (down_two - up_two)


class Halo:
    def __init__(self, cells, zst, zfl, x_below, y_below, x_above, y_above, c_below, c_above):
        self.fields, self.block, self.lanes = zst.shape
        self.st = cells.at[0 : self.fields]
        self.fl = cells.at[self.fields : self.fields + FLUID]
        self.zst, self.zfl = zst, zfl
        self.x_below, self.x_above = x_below, x_above
        self.y_below, self.y_above = y_below, y_above
        self.c_below, self.c_above = c_below, c_above
        self.cy = self.block // 4
        self.t = Tile(self.cy, self.lanes)
        self.half = self.t.rows
        self.own = self.block // self.half
        self.inner = range(1, self.own + 1)
        self.span = range(self.own + 2)
        self.edge = edge_list(x_below.shape[0])
        self.last = x_below.shape[0] - 1

    def rows_of(self, ref, q, p):
        return ref[q, (p - 1) * self.half : p * self.half, :]

    def main(self, q, p):
        if q < self.fields:
            return self.rows_of(self.st, q, p)
        return self.rows_of(self.fl, q - self.fields, p)

    def beyond(self, q, p):
        if q < self.fields:
            return self.rows_of(self.zst, q, p)
        return self.rows_of(self.zfl, q - self.fields, p)

    def part(self, second):
        return self.t.part_second if second else self.t.part_first

    def beside(self, q, p):
        return self.part(p == 2)(self.y_above[q], self.y_below[q])

    def third_place(self, q):
        return self.fields + FLUID + q // 2, q % 2

    def x_third(self, q, upper):
        tile, which = self.third_place(q)
        found = self.x_above[tile] if upper else self.x_below[tile]
        return self.t.swap(found) if which else found

    def y_third(self, q, p):
        t = self.t
        tile, which = self.third_place(q)
        turn_above, turn_below = ((0, 0), (-1, 1), (2, -2), (1, -1))[2 * which + p - 1]
        above, below = t.turn(self.y_above[tile], turn_above), t.turn(self.y_below[tile], turn_below)
        return jnp.where(t.slot == 2, above, below)

    def z_place(self, q):
        return 4 * self.edge.index(q) + 2

    def x_beyond(self, q, upper):
        tile = self.x_above[self.last] if upper else self.x_below[self.last]
        return self.t.spin(tile, -self.z_place(q))

    def y_beyond(self, q, p):
        return self.t.spin(self.beside(self.last, p), -self.z_place(q))

    def corner(self, q, p):
        whole, single = corner_lists(self.edge)
        if q in single:
            n = single.index(q)
            place, turn = len(whole) + 1 + n // 4, CORNER_TURNS[n % 4]
        else:
            place, turn = whole.index(q), 0
        above, below = self.t.turn(self.c_above[place], -turn), self.t.turn(self.c_below[place], -turn)
        return self.part(p > 0)(above, below)

    def corner_beyond(self, q, p):
        place = len(corner_lists(self.edge)[0])
        tile = self.part(p > 0)(self.c_above[place], self.c_below[place])
        return self.t.spin(tile, -self.z_place(q))

    def plane(self, q):
        own, inner = self.own, self.inner
        return (
            [self.x_below[q]] + [self.main(q, p) for p in inner] + [self.x_above[q]],
            [self.corner(q, 0)] + [self.beside(q, p) for p in inner] + [self.corner(q, own + 1)],
            [self.x_beyond(q, False)]
            + [self.beyond(q, p) for p in inner]
            + [self.x_beyond(q, True)],
            [None] + [self.y_beyond(q, p) for p in inner] + [None],
        )


def weigh(chi_face, alpha_face):
    shrink = volume_over(chi_face)
    return shrink, alpha_face / shrink


def primitives(half, spots, cons, centred, chi, alpha, batch):
    found = {}
    for start in range(0, len(spots), batch):
        group = spots[start : start + batch]

        def gather(planes):
            return jnp.concatenate([planes[k][p] for k, p in group], axis=0)

        shrink = volume_over(gather(chi))
        mag_raw = [gather(centred[i]) for i in range(3)]
        mag = [m * shrink for m in mag_raw]
        values = recover([gather(c) * shrink for c in cons], mag)
        u = values[2:5]
        factor = gather(alpha) * lax.rsqrt(1.0 + dot(u, u))
        field = [
            factor * (u[(i + 2) % 3] * mag_raw[(i + 1) % 3] - u[(i + 1) % 3] * mag_raw[(i + 2) % 3])
            for i in range(3)
        ]
        for n, spot in enumerate(group):
            found[spot] = [value[n * half : (n + 1) * half] for value in values + mag + field]
    return found


def ring_fluxes(prims, chi, alpha, normals, d, up, down):
    found = []
    for here, there in ((0, 1), (1, 0)):
        left, right = [], []
        for a, b in zip(prims[here], prims[there]):
            below = down(a, b, 1)
            middle = a - below
            left.append(below + 0.5 * limited(below - down(a, b, 2), middle))
            right.append(a - 0.5 * limited(middle, up(a, b, 1) - a))
        shrink, weight = weigh(
            0.5 * (chi[here] + down(chi[here], chi[there], 1)),
            0.5 * (alpha[here] + down(alpha[here], alpha[there], 1)),
        )
        found.append(face_flux(left, right, normals[here] * shrink, weight, d))
    return [a - up(a, b, 1) for a, b in zip(*found)]


def early_kernel(
    cells, zst, zfl, x_below, y_below, x_above, y_above,
    st_rate, hydro_rate, slopes, shared, pairs, sides, thirds, pairs_z, sides_z, grads, seconds, damped, tensors,
):
    halo = Halo(cells, zst, zfl, x_below, y_below, x_above, y_above, None, None)
    t, fields, half, own, cy = halo.t, halo.fields, halo.half, halo.own, halo.cy
    st, fl, inner = halo.st, halo.fl, halo.inner

    for q in range(fields):
        pairs[q, 0] = halo.x_third(q, False)
        pairs[q, 1] = x_below[q]
        for p in inner:
            pairs[q, 1 + p] = halo.main(q, p)
            sides[q, p - 1] = halo.beside(q, p)
            thirds[q, p - 1] = halo.y_third(q, p)
        pairs[q, 2 + own] = x_above[q]
        pairs[q, 3 + own] = halo.x_third(q, True)
        if q < CURVED:
            pairs_z[q, 0] = halo.x_beyond(q, False)
            pairs_z[q, own + 1] = halo.x_beyond(q, True)
            for p in inner:
                pairs_z[q, p] = halo.beyond(q, p)
                sides_z[q, p - 1] = halo.y_beyond(q, p)

    def both(q):
        return [[None] + [read(q, p) for p in inner] for read in (halo.main, halo.beyond)]

    bx, by, bz = both(fields + 5), both(fields + 6), both(fields + 7)
    normals = bz
    bx = [
        [None] + [0.5 * (v[p] + t.odd(v[p], (v[1:] + [end])[p])) for p in inner]
        for v, end in zip(bx, (x_above[fields + 5], halo.x_beyond(fields + 5, True)))
    ]
    by = [
        [None] + [0.5 * (v[p] + t.y_up(v[p], read(fields + 6, p), 1)) for p in inner]
        for v, read in zip(by, (halo.beside, halo.y_beyond))
    ]
    bz = [
        [None] + [0.5 * (a[p] + t.z_up(a[p], b[p], 1)) for p in inner]
        for a, b in ((bz[0], bz[1]), (bz[1], bz[0]))
    ]
    chi, alpha = both(0), both(7)
    spots = [(k, p) for k in range(2) for p in inner]
    found = primitives(
        half, spots, [both(fields + q) for q in range(5)], [bx, by, bz], chi, alpha, len(spots)
    )
    for (k, p), values in found.items():
        for i, value in enumerate(values):
            shared[k * own + p - 1, i] = value
    for p in inner:
        prims = [found[k, p][:8] for k in range(2)]
        changes = ring_fluxes(
            prims,
            [chi[k][p] for k in range(2)],
            [alpha[k][p] for k in range(2)],
            [normals[k][p] for k in range(2)],
            2,
            t.z_up,
            t.z_down,
        )
        for q in range(5):
            tensors[p - 1, 6 + q] = changes[q]
        rest, pressure = prims[0][:2]
        u = prims[0][2:5]
        parts = stress_parts(rest, pressure, u, prims[0][5:8])
        lorentz_sq, over, over_sq, time_b, grown_b, b_square, enthalpy, inertia = parts
        total_pressure = pressure + 0.5 * b_square
        for s, (i, j) in enumerate(INDEX_PAIRS):
            value = inertia * u[i] * u[j] - over_sq * (grown_b[i] * grown_b[j])
            tensors[p - 1, s] = value + total_pressure if i == j else value

    def pair_step(index):
        p = index + 1
        base = index * half

        for q in range(fields):
            centre = pairs[q, p + 1]
            x_m3 = t.odd(pairs[q, p - 1], pairs[q, p])
            x_m2 = pairs[q, p]
            x_m1 = t.odd(pairs[q, p], centre)
            x_p1 = t.odd(centre, pairs[q, p + 2])
            x_p2 = pairs[q, p + 2]
            x_p3 = t.odd(pairs[q, p + 2], pairs[q, p + 3])
            side, third = sides[q, index], thirds[q, index]
            y_m1, y_m2 = t.y_down(centre, side, 1), t.y_down(centre, side, 2)
            y_p1, y_p2 = t.y_up(centre, side, 1), t.y_up(centre, side, 2)
            y_m3 = t.turn(
                jnp.where(t.slot >= cy - 2, side, jnp.where(t.slot == cy - 3, third, centre)), 3
            )
            y_p3 = t.turn(jnp.where(t.slot < 2, side, jnp.where(t.slot == 2, third, centre)), -3)
            beyond = zst[q, pl.ds(base, half), :]
            z_m1, z_m2, z_m3 = (t.z_down(centre, beyond, k) for k in (1, 2, 3))
            z_p1, z_p2, z_p3 = (t.z_up(centre, beyond, k) for k in (1, 2, 3))
            dx = first_diff(x_m2, x_m1, x_p1, x_p2)
            dy = first_diff(y_m2, y_m1, y_p1, y_p2)
            grads[q, 0] = dx
            if q < CURVED:
                slopes[q, index] = dx
            grads[q, 1] = dy
            grads[q, 2] = first_diff(z_m2, z_m1, z_p1, z_p2)
            near = [x_m1 + x_p1, y_m1 + y_p1, z_m1 + z_p1]
            far = [x_m2 + x_p2, y_m2 + y_p2, z_m2 + z_p2]
            outer = (x_m3 + x_p3) + (y_m3 + y_p3) + (z_m3 + z_p3)
            damped[q] = (DISSIPATION / 64.0) * (
                outer - 6.0 * (far[0] + far[1] + far[2]) + 15.0 * (near[0] + near[1] + near[2])
                - 60.0 * centre
            )
            if q < CURVED:
                for s, d in ((0, 0), (3, 1), (5, 2)):
                    seconds[q, s] = (1.0 / 12.0) * (16.0 * near[d] - far[d] - 30.0 * centre)
                b_m, b_c, b_p = pairs_z[q, p - 1], pairs_z[q, p], pairs_z[q, p + 1]
                dx_z = first_diff(b_m, t.odd(b_m, b_c), t.odd(b_c, b_p), b_p)
                b_s = sides_z[q, p - 1]
                dy_z = first_diff(
                    t.y_down(b_c, b_s, 2),
                    t.y_down(b_c, b_s, 1),
                    t.y_up(b_c, b_s, 1),
                    t.y_up(b_c, b_s, 2),
                )
                for s, inside, outside in ((2, dx, dx_z), (4, dy, dy_z)):
                    seconds[q, s] = first_diff(
                        t.z_down(inside, outside, 2),
                        t.z_down(inside, outside, 1),
                        t.z_up(inside, outside, 1),
                        t.z_up(inside, outside, 2),
                    )

        def value(q):
            return pairs[q, p + 1]

        def fluid_value(q):
            return fl[q, pl.ds(base, half), :]

        conformal, lapse = value(0), value(7)
        over_chi = 1.0 / conformal
        metric = symmetric([value(1 + s) for s in range(6)])
        shift = [value(8 + i) for i in range(3)]
        extrinsic, theta = value(11), value(21)
        traceless = symmetric([value(12 + s) for s in range(6)])
        connection = [value(18 + i) for i in range(3)]
        inverse = inverse_metric(metric)
        grad = [[grads[q, k] for k in range(3)] for q in range(fields)]
        chi_grad, lapse_grad = grad[0], grad[7]
        shift_grad = [[grad[8 + i][k] for i in range(3)] for k in range(3)]
        trace_k = extrinsic + 2.0 * theta

        stress = symmetric([tensors[p - 1, s] for s in range(6)])
        held = [fluid_value(q) for q in range(5)]
        shrink = volume_over(conformal)
        energy = held[4] + held[0]
        third_k = trace_k * (1.0 / 3.0)
        curved = [
            [
                (traceless[i][j] + metric[i][j] * third_k) if i <= j else None for j in range(3)
            ]
            for i in range(3)
        ]
        work = (
            stress[0][0] * curved[0][0]
            + stress[1][1] * curved[1][1]
            + stress[2][2] * curved[2][2]
            + 2.0
            * (
                stress[0][1] * curved[0][1]
                + stress[0][2] * curved[0][2]
                + stress[1][2] * curved[1][2]
            )
        )
        rates = [tensors[p - 1, 6 + q] for q in range(5)]
        for i in range(3):
            rates[1 + i] = (
                rates[1 + i]
                - energy * lapse_grad[i]
                + total([held[1 + k] * grad[8 + k][i] for k in range(3)])
            )
        rates[4] = (
            rates[4] + lapse * work * over_chi / shrink - dot(held[1:4], lapse_grad)
        )
        for q in range(5):
            hydro_rate[q, pl.ds(base, half), :] = rates[q]
        density = energy * shrink
        momentum = [held[1 + i] * shrink for i in range(3)]

        lowered = [[[None] * 3 for _ in range(3)] for _ in range(3)]
        for i in range(3):
            for j in range(3):
                for k in range(j, 3):
                    got = 0.5 * (
                        grad[1 + slot_of(i, k)][j]
                        + grad[1 + slot_of(i, j)][k]
                        - grad[1 + slot_of(j, k)][i]
                    )
                    lowered[i][j][k] = lowered[i][k][j] = got
        raised = [[[None] * 3 for _ in range(3)] for _ in range(3)]
        for i in range(3):
            for j in range(3):
                for k in range(j, 3):
                    got = total([inverse[i][l] * lowered[l][j][k] for l in range(3)])
                    raised[i][j][k] = raised[i][k][j] = got
        contracted = [trace_with(inverse, raised[i]) for i in range(3)]

        def hessian_trace(q):
            return (
                inverse[0][0] * seconds[q, 0]
                + inverse[1][1] * seconds[q, 3]
                + inverse[2][2] * seconds[q, 5]
                + 2.0 * (inverse[0][2] * seconds[q, 2] + inverse[1][2] * seconds[q, 4])
            )

        def second_cov(q, slope):
            bent = [total([raised[k][i][j] * slope[k] for k in range(3)]) for i, j in INDEX_PAIRS]
            return symmetric(
                [-bent[s] if s == 1 else seconds[q, s] - bent[s] for s in range(len(bent))]
            )

        chi_cov = second_cov(0, chi_grad)
        chi_lap = trace_with(inverse, chi_cov)
        raised_chi = [dot(inverse[i], chi_grad) for i in range(3)]
        chi_square = dot(raised_chi, chi_grad)
        cross_term = dot(raised_chi, lapse_grad)
        half_chi = 0.5 * over_chi
        plain_cov = second_cov(7, lapse_grad)
        lapse_cov = symmetric(
            [
                plain_cov[i][j]
                + (
                    chi_grad[i] * lapse_grad[j]
                    + chi_grad[j] * lapse_grad[i]
                    - metric[i][j] * cross_term
                )
                * half_chi
                for i, j in INDEX_PAIRS
            ]
        )
        lapse_lap = conformal * trace_with(inverse, lapse_cov)

        mixed = [
            [[dot(inverse[l], lowered[k][j]) for j in range(3)] for k in range(3)]
            for l in range(3)
        ]
        quarter_sq = half_chi * half_chi
        metric_factor = chi_lap * half_chi - 3.0 * chi_square * quarter_sq
        ricci = []
        for i, j in INDEX_PAIRS:
            second_part = -0.5 * hessian_trace(1 + slot_of(i, j))
            connection_part = 0.5 * total(
                [metric[k][i] * grad[18 + k][j] + metric[k][j] * grad[18 + k][i] for k in range(3)]
            )
            contracted_part = 0.5 * total(
                [contracted[k] * (lowered[i][j][k] + lowered[j][i][k]) for k in range(3)]
            )
            if i == j:
                quadratic = total(
                    [
                        raised[k][l][i] * (2.0 * mixed[l][i][k] + mixed[l][k][i])
                        for k in range(3)
                        for l in range(3)
                    ]
                )
            else:
                quadratic = total(
                    [
                        raised[k][l][i] * (mixed[l][j][k] + mixed[l][k][j])
                        + raised[k][l][j] * mixed[l][i][k]
                        for k in range(3)
                        for l in range(3)
                    ]
                )
            conformal_part = (
                chi_cov[i][j] * half_chi
                + metric[i][j] * metric_factor
                - chi_grad[i] * chi_grad[j] * quarter_sq
            )
            ricci.append(
                second_part + connection_part + contracted_part + quadratic + conformal_part
            )
        ricci = symmetric(ricci)
        ricci_scalar = conformal * trace_with(inverse, ricci)
        stress_trace = conformal * trace_with(inverse, stress)

        up_a = [
            [total([inverse[i][k] * traceless[k][j] for k in range(3)]) for j in range(3)]
            for i in range(3)
        ]
        raised_a = symmetric(
            [total([up_a[i][l] * inverse[j][l] for l in range(3)]) for i, j in INDEX_PAIRS]
        )
        a_square = trace_with(traceless, raised_a)
        shift_div = shift_grad[0][0] + shift_grad[1][1] + shift_grad[2][2]
        two_thirds_div = (2.0 / 3.0) * shift_div

        def finish(q, rate):
            rate = rate + dot(shift, grad[q]) + damped[q]
            st_rate[q, pl.ds(base, half), :] = rate

        finish(0, (2.0 / 3.0) * conformal * (lapse * trace_k - shift_div))
        finish(7, -2.0 * lapse * extrinsic)
        for i in range(3):
            finish(8 + i, 0.75 * connection[i] - SHIFT_DAMPING * shift[i])
        finish(
            11,
            lapse
            * (
                a_square
                + trace_k * trace_k * (1.0 / 3.0)
                + FOUR_PI * (stress_trace + density)
                + KAPPA_ONE * theta
            )
            - lapse_lap,
        )
        source = symmetric(
            [
                lapse * (ricci[i][j] - 2.0 * FOUR_PI * stress[i][j]) - lapse_cov[i][j]
                for i, j in INDEX_PAIRS
            ]
        )
        third_trace = trace_with(inverse, source) * (1.0 / 3.0)
        for s, (i, j) in enumerate(INDEX_PAIRS):
            finish(
                1 + s,
                total(
                    [
                        metric[i][k] * shift_grad[j][k] + metric[j][k] * shift_grad[i][k]
                        for k in range(3)
                    ]
                )
                - metric[i][j] * two_thirds_div
                - 2.0 * lapse * traceless[i][j],
            )
            product = total([traceless[i][k] * up_a[k][j] for k in range(3)])
            finish(
                12 + s,
                total(
                    [
                        traceless[i][k] * shift_grad[j][k] + traceless[j][k] * shift_grad[i][k]
                        for k in range(3)
                    ]
                )
                - traceless[i][j] * two_thirds_div
                + conformal * (source[i][j] - metric[i][j] * third_trace)
                + lapse * (trace_k * traceless[i][j] - 2.0 * product),
            )
        for i in range(3):
            bracket = (
                trace_with(raised_a, raised[i])
                - 1.5 * dot(raised_a[i], chi_grad) * over_chi
                - dot(inverse[i], [2.0 * grad[11][j] + grad[21][j] for j in range(3)]) * (1.0 / 3.0)
                - 2.0 * FOUR_PI * dot(inverse[i], momentum)
            )
            spread = [
                seconds[8, 0] + seconds[10, 2],
                seconds[9, 3] + seconds[10, 4],
                seconds[8, 2] + seconds[9, 4] + seconds[10, 5],
            ]
            finish(
                18 + i,
                contracted[i] * two_thirds_div
                - total([contracted[j] * shift_grad[j][i] for j in range(3)])
                + hessian_trace(8 + i)
                + dot(inverse[i], spread) * (1.0 / 3.0)
                - 2.0 * dot(raised_a[i], lapse_grad)
                + 2.0
                * lapse
                * (bracket - KAPPA_ONE * (connection[i] - contracted[i])),
            )
        finish(
            21,
            0.5
            * lapse
            * (
                ricci_scalar
                - a_square
                + (2.0 / 3.0) * trace_k * trace_k
                - 4.0 * FOUR_PI * density
            )
            - 2.0 * KAPPA_ONE * lapse * theta,
        )

    for index in range(own):
        pair_step(index)


def late_kernel(
    cells, zst, zfl, x_below, y_below, x_above, y_above, c_below, c_above, line_two, line_top,
    st_rate, hydro_rate, slopes, shared, st_out, fl_out,
):
    halo = Halo(cells, zst, zfl, x_below, y_below, x_above, y_above, c_below, c_above)
    t, fields, half, own = halo.t, halo.fields, halo.half, halo.own
    inner, span = halo.inner, halo.span

    top = jnp.maximum(line_top[...], line_two[...])
    speed_tile = len(corner_lists(halo.edge)[0])
    for lines in (c_below, c_above):
        top = jnp.maximum(top, lines[speed_tile, 0:1, halo.lanes - 1 : halo.lanes])
    dt = COURANT / top

    for p in inner:
        place = slice((p - 1) * half, p * half)
        mixed = []
        for q in range(CURVED):
            s_m, s_c, s_p = (
                halo.beside(q, n) if 1 <= n <= own else halo.corner(q, n) for n in (p - 1, p, p + 1)
            )
            slope = slopes[q, p - 1]
            slope_side = first_diff(s_m, t.odd_swapped(s_m, s_c), t.odd_swapped(s_c, s_p), s_p)
            mixed.append(
                first_diff(
                    t.y_down(slope, slope_side, 2),
                    t.y_down(slope, slope_side, 1),
                    t.y_up(slope, slope_side, 1),
                    t.y_up(slope, slope_side, 2),
                )
            )
        conformal, lapse = halo.main(0, p), halo.main(7, p)
        metric = [halo.main(1 + s, p) for s in range(6)]
        inverse = inverse_metric(symmetric(metric))
        half_chi = 0.5 / conformal
        cross = inverse[0][1]
        chi_trace = 2.0 * cross * mixed[0] * half_chi
        ricci = [metric[s] * chi_trace - cross * mixed[1 + s] for s in range(6)]
        ricci[1] = ricci[1] + mixed[0] * half_chi
        source = [lapse * r for r in ricci]
        source[1] = source[1] - mixed[7]
        third_trace = trace_with(inverse, symmetric(source)) * (1.0 / 3.0)
        extra = {
            11: -2.0 * conformal * cross * mixed[7],
            21: 0.5 * lapse * conformal * trace_with(inverse, symmetric(ricci)),
        }
        for s in range(6):
            extra[12 + s] = conformal * (source[s] - metric[s] * third_trace)
        for i in range(3):
            extra[18 + i] = 2.0 * cross * mixed[8 + i] + (1.0 / 3.0) * (
                inverse[i][0] * mixed[9] + inverse[i][1] * mixed[8]
            )
        for q in range(fields):
            rate = st_rate[q, place, :]
            if q in extra:
                rate = rate + extra[q]
            st_out[q, place, :] = halo.main(q, p) + dt * rate

    v, h, vz, hz = halo.plane(fields + 5)
    hz[own + 1] = halo.corner_beyond(fields + 5, own + 1)
    v_next = v[1:] + [halo.x_third(fields, True)]
    face_x = v
    bx = (
        [0.5 * (v[p] + t.odd(v[p], v_next[p])) for p in span],
        [0.5 * (h[p] + t.odd_swapped(h[p], h[min(p + 1, own + 1)])) for p in span],
        [0.5 * (vz[p] + t.odd(vz[p], vz[min(p + 1, own + 1)])) for p in span],
        [None] + [0.5 * (hz[p] + t.odd_swapped(hz[p], hz[p + 1])) for p in inner] + [None],
    )
    v, h, vz, hz = halo.plane(fields + 6)
    hz[0] = halo.corner_beyond(fields + 6, 0)
    hz[own + 1] = halo.corner_beyond(fields + 6, own + 1)
    face_y = v, h
    full = [
        jnp.where(t.slot == 2, halo.y_third(fields, p), h[p]) if 1 <= p <= own else h[p] for p in span
    ]
    by = (
        [0.5 * (v[p] + t.y_up(v[p], h[p], 1)) for p in span],
        [0.5 * (h[p] + t.y_up(full[p], v[p], 1)) for p in span],
        [0.5 * (vz[p] + t.y_up(vz[p], hz[p], 1)) for p in span],
        [None] + [0.5 * (hz[p] + t.y_up(hz[p], vz[p], 1)) for p in inner] + [None],
    )
    v, h, vz, hz = halo.plane(fields + 7)
    bz = (v, h, vz, hz)

    chi, alpha = halo.plane(0), halo.plane(7)
    spots = [(0, 0), (0, own + 1)] + [(1, p) for p in span] + [(2, 0), (2, own + 1)]
    spots += [(3, p) for p in inner]
    found = primitives(
        half, spots, [halo.plane(fields + q) for q in range(5)], [bx, by, bz], chi, alpha, len(spots)
    )
    for k, kind in enumerate((0, 2)):
        for p in inner:
            found[kind, p] = [shared[k * own + p - 1, i] for i in range(11)]

    lines = [[found[0, p][i] for p in span] for i in range(8)] + [chi[0], alpha[0]]
    odd_lines = [[t.odd(f[p], f[min(p + 1, own + 1)]) for p in span] for f in lines]
    fluxes = [None]
    for p in range(1, own + 2):
        left, right = [], []
        for f, o in zip(lines[:8], odd_lines):
            here = f[p] - o[p - 1]
            left.append(o[p - 1] + 0.5 * limited(o[p - 1] - f[p - 1], here))
            right.append(f[p] - 0.5 * limited(here, o[p] - f[p]))
        shrink, weight = weigh(
            0.5 * (lines[8][p] + odd_lines[8][p - 1]), 0.5 * (lines[9][p] + odd_lines[9][p - 1])
        )
        fluxes.append(face_flux(left, right, face_x[p] * shrink, weight, 0))
    for p in inner:
        changes = ring_fluxes(
            [found[k, p][:8] for k in range(2)],
            [chi[k][p] for k in range(2)],
            [alpha[k][p] for k in range(2)],
            [face_y[k][p] for k in range(2)],
            1,
            t.y_up,
            t.y_down,
        )
        place = slice((p - 1) * half, p * half)
        for q in range(5):
            change = fluxes[p][q] - t.odd(fluxes[p][q], fluxes[p + 1][q])
            rate = hydro_rate[q, place, :] + change + changes[q]
            fl_out[q, place, :] = halo.main(fields + q, p) + dt * rate

    ex, ey, ez = (
        [[found[k, p][8 + i] if (k, p) in found else None for p in span] for k in range(4)]
        for i in range(3)
    )
    ez_x = [
        [ez[0][p] + t.odd(ez[0][p - 1], ez[0][p]) if p else None for p in span],
        [ez[1][p] + t.odd_swapped(ez[1][p - 1], ez[1][p]) if p else None for p in span],
    ]
    ey_x = [
        [ey[k][p] + t.odd(ey[k][p - 1], ey[k][p]) if p else None for p in span] for k in (0, 2)
    ]
    edge_z = [None] + [ez_x[0][p] + t.y_down(ez_x[0][p], ez_x[1][p], 1) for p in span[1:]]
    edge_z_h = [None] + [ez_x[1][p] + t.y_down(ez_x[1][p], ez_x[0][p], 1) for p in inner]
    edge_y = [None] + [ey_x[0][p] + t.z_down(ey_x[0][p], ey_x[1][p], 1) for p in span[1:]]
    edge_y_z = [None] + [ey_x[1][p] + t.z_down(ey_x[1][p], ey_x[0][p], 1) for p in inner]
    for p in inner:
        ex_y = ex[0][p] + t.y_down(ex[0][p], ex[1][p], 1)
        ex_y_h = ex[1][p] + t.y_down(ex[1][p], ex[0][p], 1)
        ex_y_z = ex[2][p] + t.y_down(ex[2][p], ex[3][p], 1)
        ex_y_hz = ex[3][p] + t.y_down(ex[3][p], ex[2][p], 1)
        edge_x = ex_y + t.z_down(ex_y, ex_y_z, 1)
        edge_x_h = ex_y_h + t.z_down(ex_y_h, ex_y_hz, 1)
        edge_x_z = ex_y_z + t.z_down(ex_y_z, ex_y, 1)
        x_rate = (t.z_up(edge_y[p], edge_y_z[p], 1) - edge_y[p]) - (
            t.y_up(edge_z[p], edge_z_h[p], 1) - edge_z[p]
        )
        y_rate = (t.odd(edge_z[p], edge_z[p + 1]) - edge_z[p]) - (
            t.z_up(edge_x, edge_x_z, 1) - edge_x
        )
        z_rate = (t.y_up(edge_x, edge_x_h, 1) - edge_x) - (
            t.odd(edge_y[p], edge_y[p + 1]) - edge_y[p]
        )
        quarter = 0.25 * dt
        for i, rate in enumerate((x_rate, y_rate, z_rate)):
            fl_out[5 + i, (p - 1) * half : p * half, :] = (
                halo.main(fields + 5 + i, p) + quarter * rate
            )


def per_device(spacetime, fluid):
    fields, cx, cy, cz = spacetime.shape
    rows = cx * cy
    st = spacetime.reshape(fields, rows, cz)
    fl = fluid.reshape(FLUID, rows, cz)
    sizes = [lax.axis_size(a) for a in ("gx", "gy", "gz")]
    tile = (2 * cy, cz)
    f32 = jnp.float32

    def shape(*dims):
        return jax.ShapeDtypeStruct(dims, f32)

    def beyond(cells):
        n = sizes[2]
        after = lax.ppermute(cells, "gz", [((i + 1) % n, i) for i in range(n)])
        if n == 2:
            return after
        before = lax.ppermute(cells, "gz", [(i, (i + 1) % n) for i in range(n)])
        lane = lax.broadcasted_iota(jnp.int32, cells.shape, 2)
        return jnp.where(lane < cz // 2, after, before)

    params = pltpu.CompilerParams(vmem_limit_bytes=48 * 1024 * 1024)
    zst, zfl = beyond(st), beyond(fl)
    cells = jnp.concatenate([st, fl], axis=0)
    face = shape(face_tiles(fields), *tile)
    whole, single = corner_lists(edge_list(face_tiles(fields)))
    corner = shape(len(whole) + 1 + (len(single) + 3) // 4, *tile)
    lane_row = shape(1, cz)
    x_low, x_high, y_low, y_high, top = pl.pallas_call(
        pack_kernel, out_shape=[face] * 4 + [lane_row], compiler_params=params, name="pack"
    )(cells, zst, zfl)

    def move(cells, dx, dy):
        nx, ny = sizes[0], sizes[1]
        hops = [
            (i * ny + j, ((i + dx) % nx) * ny + (j + dy) % ny) for i in range(nx) for j in range(ny)
        ]
        return lax.ppermute(cells, ("gx", "gy"), hops)

    short = sizes[0] <= 4 and sizes[1] <= 4 and sizes[2] <= 2
    x_below = move(x_high, 1, 0)
    y_below = move(y_high, 0, 1)
    x_above = move(x_low, -1, 0)
    y_above = move(y_low, 0, -1)
    top_two = move(top, 2, 0) if short and sizes[0] == 4 else top
    c_low, c_high, line_top = pl.pallas_call(
        relay_kernel,
        out_shape=[corner, corner, lane_row],
        compiler_params=params,
        name="relay",
    )(x_below, x_above, y_below, top, top_two)
    c_above = move(c_low, 0, -1)
    c_below = move(c_high, 0, 1)
    if not short:
        line_two = lax.pmax(line_top, ("gx", "gy", "gz"))
    else:
        line_two = move(line_top, 0, 2) if sizes[1] == 4 else line_top
    own = cx // 2
    arrived = (cells, zst, zfl, x_below, y_below, x_above, y_above)
    early = pl.pallas_call(
        early_kernel,
        out_shape=[
            shape(*st.shape),
            shape(5, rows, cz),
            shape(CURVED, own, *tile),
            shape(2 * own, 11, *tile),
        ],
        scratch_shapes=[
            pltpu.VMEM((fields, own + 4) + tile, f32),
            pltpu.VMEM((fields, own) + tile, f32),
            pltpu.VMEM((fields, own) + tile, f32),
            pltpu.VMEM((CURVED, own + 2) + tile, f32),
            pltpu.VMEM((CURVED, own) + tile, f32),
            pltpu.VMEM((fields, 3) + tile, f32),
            pltpu.VMEM((CURVED, 6) + tile, f32),
            pltpu.VMEM((fields,) + tile, f32),
            pltpu.VMEM((own, 11) + tile, f32),
        ],
        compiler_params=params,
        name="early",
    )(*arrived)
    st_next, fl_next = pl.pallas_call(
        late_kernel,
        out_shape=[shape(*st.shape), shape(*fl.shape)],
        compiler_params=params,
        name="late",
    )(*arrived, c_below, c_above, line_two, line_top, *early)
    return st_next.reshape(spacetime.shape), fl_next.reshape(fluid.shape)


def solution(mesh):
    spec = P(None, "gx", "gy", "gz")
    return jax.shard_map(
        per_device, mesh=mesh, in_specs=(spec, spec), out_specs=(spec, spec), check_vma=False
    )
```

```python
import functools
import math

import jax
import jax.numpy as jnp
from jax import lax
from jax.experimental import pallas as pl
from jax.experimental.pallas import tpu as pltpu
from jax.sharding import PartitionSpec as P

RECOVERY_STEPS = 4
INDEX_PAIRS = ((0, 0), (0, 1), (0, 2), (1, 1), (1, 2), (2, 2))
COURANT = 0.25
DISSIPATION = 0.2
KAPPA_ONE = 0.02
SHIFT_DAMPING = 1.0
SPEED_CAP = 0.99
PRESSURE_FLOOR = 0.01
FOUR_PI = 4.0 * math.pi

BATCH = 6
CURVED = 11
FLUID = 8


def total(pieces):
    summed = pieces[0]
    for member in pieces[1:]:
        summed = summed + member
    return summed


def dot(first_vec, second_vec):
    return total([first_vec[i] * second_vec[i] for i in range(3)])


def slot_of(i, j):
    return INDEX_PAIRS.index((min(i, j), max(i, j)))


def symmetric(entries):
    return [[entries[slot_of(i, j)] for j in range(3)] for i in range(3)]


def trace_with(inverse, tensor):
    return (
        inverse[0][0] * tensor[0][0]
        + inverse[1][1] * tensor[1][1]
        + inverse[2][2] * tensor[2][2]
        + 2.0
        * (
            inverse[0][1] * tensor[0][1]
            + inverse[0][2] * tensor[0][2]
            + inverse[1][2] * tensor[1][2]
        )
    )


def inverse_metric(metric):
    cofactor = [
        metric[1][1] * metric[2][2] - metric[1][2] * metric[1][2],
        metric[0][2] * metric[1][2] - metric[0][1] * metric[2][2],
        metric[0][1] * metric[1][2] - metric[0][2] * metric[1][1],
        metric[0][0] * metric[2][2] - metric[0][2] * metric[0][2],
        metric[0][1] * metric[0][2] - metric[0][0] * metric[1][2],
        metric[0][0] * metric[1][1] - metric[0][1] * metric[0][1],
    ]
    determinant = (
        metric[0][0] * cofactor[0] + metric[0][1] * cofactor[1] + metric[0][2] * cofactor[2]
    )
    over = 1.0 / determinant
    return symmetric([c * over for c in cofactor])


class Tile:
    def __init__(self, cy, cz):
        self.cy, self.rows, self.lanes = cy, 2 * cy, cz
        shape = (self.rows, cz)
        self.row = lax.broadcasted_iota(jnp.int32, shape, 0)
        self.lane = lax.broadcasted_iota(jnp.int32, shape, 1)
        self.slot = lax.rem(self.row, cy)

    def turn(self, tile, amount):
        amount = amount % self.rows
        return tile if amount == 0 else pltpu.roll(tile, amount, 0)

    def spin(self, tile, amount):
        amount = amount % self.lanes
        return tile if amount == 0 else pltpu.roll(tile, amount, 1)

    def swap(self, tile):
        return self.turn(tile, self.cy)

    def odd(self, a, b):
        return self.turn(jnp.where(self.row < self.cy, b, a), self.cy)

    def odd_swapped(self, a, b):
        return self.turn(jnp.where(self.row < self.cy, a, b), self.cy)

    def y_up(self, main, beyond, k):
        return self.turn(jnp.where(self.slot < k, beyond, main), -k)

    def y_down(self, main, beyond, k):
        return self.turn(jnp.where(self.slot >= self.cy - k, beyond, main), k)

    def z_up(self, main, beyond, k):
        return self.spin(jnp.where(self.lane < k, beyond, main), -k)

    def z_down(self, main, beyond, k):
        return self.spin(jnp.where(self.lane >= self.lanes - k, beyond, main), k)

    def corner_rows(self, side, turn):
        places = ((0, 2), (self.cy - 1, self.cy + 1))[side]
        first, second = [(place + turn) % self.rows for place in places]
        return (self.row == first) | (self.row == second)

    def join_low(self, u, v):
        return jnp.where(self.slot < 2, self.swap(u), self.turn(v, 2))

    def join_high(self, u, v):
        return jnp.where(self.slot >= self.cy - 2, self.swap(u), self.turn(self.swap(v), -2))

    def part_first(self, from_above, from_below):
        return jnp.where(self.slot < 2, from_above, from_below)

    def part_second(self, from_above, from_below):
        return self.turn(jnp.where(self.slot < 2, from_below, from_above), 2)


def edge_list(tiles):
    fields = next(n for n in range(tiles) if face_tiles(n) == tiles)
    return list(range(CURVED)) + list(range(fields, fields + FLUID))


CORNER_TURNS = (0, 1, 4, 5)
CORNER_TILES = CURVED + FLUID // 4 + 1
TOP_ROW = 6


def face_tiles(fields):
    return fields + FLUID + len(pairs_of(third_list(fields))) + 1


def third_list(fields):
    return list(range(fields + 1))


def pairs_of(items):
    return [(items[i], items[min(i + 1, len(items) - 1)]) for i in range(0, len(items), 2)]


def top_speed(st):
    inverse = inverse_metric(symmetric([st[1 + s] for s in range(6)]))
    scale = 2.0 * st[7] * st[0]
    speeds = [jnp.abs(st[8 + d]) + jnp.sqrt(scale * inverse[d][d]) for d in range(3)]
    top = jnp.maximum(jnp.maximum(speeds[0], speeds[1]), speeds[2])
    return jnp.max(jnp.max(top, axis=1, keepdims=True), axis=0, keepdims=True)


def pack_kernel(cells, zst, zfl, *outs):
    fields, rows, lanes = zst.shape
    st, fl = cells.at[0:fields], cells.at[fields : fields + FLUID]
    cy = rows // 4
    t = Tile(cy, lanes)
    x_low, x_high, y_low, y_high, top_out = outs
    half = t.rows

    def own(ref, q):
        return [ref[q, 0:half, :], ref[q, half : 2 * half, :]]

    tiles, beyond = [], []
    for q in range(fields):
        tiles.append(own(st, q))
        beyond.append(own(zst, q) if q < CURVED else None)
    for q in range(FLUID):
        tiles.append(own(fl, q))
        beyond.append(own(zfl, q))

    packed = [None] * 4
    place = 0
    for q, (first, second) in enumerate(tiles):
        x_low[q] = first
        x_high[q] = second
        y_low[q] = t.join_low(first, second)
        y_high[q] = t.join_high(first, second)
        if beyond[q] is not None:
            zf, zs = beyond[q]
            for m, piece in enumerate((zf, zs, t.join_low(zf, zs), t.join_high(zf, zs))):
                piece = t.spin(piece, 4 * place + 2)
                packed[m] = (
                    piece if place == 0 else jnp.where(t.lane < 4 * place, packed[m], piece)
                )
            place += 1
    for n, (a, b) in enumerate(pairs_of(third_list(fields))):
        slot = fields + FLUID + n
        xa, xb = (tiles[q if q < fields else fields + 5] for q in (a, b))
        x_low[slot] = jnp.where(t.row < cy, xa[1], t.swap(xb[1]))
        x_high[slot] = jnp.where(t.row < cy, t.swap(xb[0]), xa[0])
        ya, yb = (tiles[q if q < fields else fields + 6] for q in (a, b))
        w = [t.swap(ya[0]), t.swap(ya[1]), t.swap(yb[0]), t.swap(yb[1])]
        s = t.slot
        y_low[slot] = jnp.where(
            s == 2,
            w[0],
            jnp.where(s == 3, t.turn(w[1], 1), jnp.where(s == 0, t.turn(w[2], -2), t.turn(w[3], -1))),
        )
        y_high[slot] = jnp.where(
            s == 1,
            w[0],
            jnp.where(s == 0, t.turn(w[1], -1), jnp.where(s == 3, t.turn(w[2], 2), t.turn(w[3], 1))),
        )
    top = jnp.maximum(top_speed(st), top_speed(zst))
    top_out[...] = jnp.broadcast_to(top, top_out.shape)
    last = x_low.shape[0] - 1
    for out, piece in zip((x_low, x_high, y_low, y_high), packed):
        out[last] = jnp.where(t.lane < 4 * place, piece, top)


def relay_kernel(x_below, x_above, y_below, top, top_two, to_low, to_high, line_top):
    cy, lanes = x_below.shape[1] // 2, x_below.shape[2]
    t = Tile(cy, lanes)
    last = x_below.shape[0] - 1
    line = jnp.maximum(top[...], top_two[...])
    for beside in (x_below, x_above, y_below):
        line = jnp.maximum(line, beside[last, 0:1, lanes - 1 : lanes])
    line_top[...] = line
    edge = edge_list(x_below.shape[0])
    for q in range(CURVED):
        to_low[q] = t.join_low(x_below[q], x_above[q])
        to_high[q] = t.join_high(x_below[q], x_above[q])
    for n in range(0, FLUID, 4):
        low, high = None, None
        for turn, q in zip(CORNER_TURNS, edge[CURVED + n : CURVED + n + 4]):
            below = t.turn(t.join_low(x_below[q], x_above[q]), turn)
            above = t.turn(t.join_high(x_below[q], x_above[q]), turn)
            if low is None:
                low, high = below, above
            else:
                low = jnp.where(t.corner_rows(0, turn), below, low)
                high = jnp.where(t.corner_rows(1, turn), above, high)
        to_low[CURVED + n // 4] = low
        to_high[CURVED + n // 4] = high
    along_x, along_y = edge[CURVED + 5], edge[CURVED + 6]
    low = t.join_low(x_below[along_y], x_above[along_y])
    high = t.join_high(x_below[along_x], x_above[along_x])
    to_low[CORNER_TILES - 1] = jnp.where(t.row == TOP_ROW, line, low)
    to_high[CORNER_TILES - 1] = jnp.where(t.row == TOP_ROW, line, high)


def limited(a, b):
    return jnp.maximum(jnp.minimum(a, b), 0.0) + jnp.minimum(jnp.maximum(a, b), 0.0)


def recover(conserved, magnetic):
    density = conserved[0]
    momenta = conserved[1:4]
    energy = conserved[4] + density
    mom_sq = dot(momenta, momenta)
    mag_sq = dot(magnetic, magnetic)
    cross = dot(momenta, magnetic)
    cross_sq = cross * cross

    def state(z):
        grown = z + mag_sq
        over = 1.0 / (z * grown)
        speed_sq = (mom_sq * z * z + cross_sq * (2.0 * z + mag_sq)) * over * over
        kept = 1.0 - jnp.minimum(speed_sq, SPEED_CAP)
        rest = density * jnp.sqrt(kept)
        return kept, rest, 0.5 * (z * kept - rest), grown * over

    z = jnp.maximum(energy - 0.5 * mag_sq, density)
    for _ in range(RECOVERY_STEPS):
        kept, rest, pressure, over_z = state(z)
        residual = (
            z
            + mag_sq
            - pressure
            - 0.5 * mag_sq * kept
            - 0.5 * cross_sq * over_z * over_z
            - energy
        )
        z = jnp.maximum(z - residual / (1.0 - 0.5 * kept), density)
    kept, rest, pressure, over_z = state(z)
    pressure = jnp.maximum(pressure, PRESSURE_FLOOR * rest)
    scale = lax.rsqrt(kept) / (z + mag_sq)
    along = cross * over_z
    four_vel = [scale * (momenta[i] + along * magnetic[i]) for i in range(3)]
    return [rest, pressure] + four_vel


def stress_parts(rest, pressure, u, magnetic):
    lorentz_sq = 1.0 + dot(u, u)
    over = lax.rsqrt(lorentz_sq)
    over_sq = over * over
    time_b = dot(u, magnetic)
    grown_b = [magnetic[i] + time_b * u[i] for i in range(3)]
    b_square = (dot(magnetic, magnetic) + time_b * time_b) * over_sq
    enthalpy = rest + 2.0 * pressure
    inertia = enthalpy + b_square
    return lorentz_sq, over, over_sq, time_b, grown_b, b_square, enthalpy, inertia


def face_state(rest, pressure, u, magnetic, d):
    lorentz_sq, over, over_sq, time_b, grown_b, b_square, enthalpy, inertia = stress_parts(
        rest, pressure, u, magnetic
    )
    total_pressure = pressure + 0.5 * b_square
    lorentz = lorentz_sq * over
    density = rest * lorentz
    carried = inertia * lorentz
    time_over = time_b * over
    conserved = [density]
    conserved += [carried * u[j] - time_over * grown_b[j] for j in range(3)]
    conserved += [inertia * lorentz_sq - total_pressure - time_b * time_b - density]
    mass_flux = rest * u[d]
    flux = [mass_flux]
    pushed = inertia * u[d]
    b_over = grown_b[d] * over_sq
    for j in range(3):
        flux_j = pushed * u[j] - b_over * grown_b[j]
        flux.append(flux_j + total_pressure if j == d else flux_j)
    flux.append(carried * u[d] - time_over * grown_b[d] - mass_flux)
    ratio = 1.0 / (enthalpy * inertia)
    sound_sq = 2.0 * pressure * inertia * ratio
    alfven_sq = b_square * enthalpy * ratio
    fast_sq = sound_sq + alfven_sq - sound_sq * alfven_sq
    slow = 1.0 - fast_sq
    velocity = u[d] * over
    rest_part = 1.0 - dot(u, u) * over_sq * fast_sq
    spread = jnp.sqrt(fast_sq * over_sq * (rest_part - velocity * velocity * slow))
    fastest = (jnp.abs(velocity * slow) + spread) / rest_part
    return conserved, flux, fastest


def face_flux(left, right, normal, weight, d):
    sides = []
    for state in (left, right):
        magnetic = [normal if i == d else state[5 + i] for i in range(3)]
        sides.append(face_state(state[0], state[1], state[2:5], magnetic, d))
    (cons_l, flux_l, fast_l), (cons_r, flux_r, fast_r) = sides
    signal = jnp.maximum(fast_l, fast_r)
    scale = 0.5 * weight
    return [scale * (flux_l[q] + flux_r[q] - signal * (cons_r[q] - cons_l[q])) for q in range(5)]


def volume_over(conformal):
    return conformal * jnp.sqrt(conformal)


def first_diff(down_two, down, up, up_two):
    return (8.0 / 12.0) * (up - down) + (1.0 / 12.0) * (down_two - up_two)


class Halo:
    def __init__(self, cells, zst, zfl, x_below, y_below, x_above, y_above, c_below, c_above):
        self.fields, self.block, self.lanes = zst.shape
        self.st = cells.at[0 : self.fields]
        self.fl = cells.at[self.fields : self.fields + FLUID]
        self.zst, self.zfl = zst, zfl
        self.x_below, self.x_above = x_below, x_above
        self.y_below, self.y_above = y_below, y_above
        self.c_below, self.c_above = c_below, c_above
        self.cy = self.block // 4
        self.t = Tile(self.cy, self.lanes)
        self.half = self.t.rows
        self.own = self.block // self.half
        self.inner = range(1, self.own + 1)
        self.span = range(self.own + 2)
        self.edge = edge_list(x_below.shape[0])
        self.last = x_below.shape[0] - 1

    def rows_of(self, ref, q, p):
        return ref[q, (p - 1) * self.half : p * self.half, :]

    def main(self, q, p):
        if q < self.fields:
            return self.rows_of(self.st, q, p)
        return self.rows_of(self.fl, q - self.fields, p)

    def beyond(self, q, p):
        if q < self.fields:
            return self.rows_of(self.zst, q, p)
        return self.rows_of(self.zfl, q - self.fields, p)

    def part(self, second):
        return self.t.part_second if second else self.t.part_first

    def beside(self, q, p):
        return self.part(p == 2)(self.y_above[q], self.y_below[q])

    def third_place(self, q):
        return self.fields + FLUID + q // 2, q % 2

    def x_third(self, q, upper):
        tile, which = self.third_place(q)
        found = self.x_above[tile] if upper else self.x_below[tile]
        return self.t.swap(found) if which else found

    def y_third(self, q, p):
        t = self.t
        tile, which = self.third_place(q)
        turn_above, turn_below = ((0, 0), (-1, 1), (2, -2), (1, -1))[2 * which + p - 1]
        above, below = t.turn(self.y_above[tile], turn_above), t.turn(self.y_below[tile], turn_below)
        return jnp.where(t.slot == 2, above, below)

    def z_place(self, q):
        return 4 * self.edge.index(q) + 2

    def x_beyond(self, q, upper):
        tile = self.x_above[self.last] if upper else self.x_below[self.last]
        return self.t.spin(tile, -self.z_place(q))

    def y_beyond(self, q, p):
        return self.t.spin(self.beside(self.last, p), -self.z_place(q))

    def corner(self, q, p):
        place, turn = q, 0
        if q >= CURVED:
            n = q - self.fields
            place, turn = CURVED + n // 4, CORNER_TURNS[n % 4]
        above, below = self.t.turn(self.c_above[place], -turn), self.t.turn(self.c_below[place], -turn)
        return self.part(p > 0)(above, below)

    def corner_layers(self, p):
        place = CORNER_TILES - 1
        return self.part(p > 0)(self.c_above[place], self.c_below[place])

    def plane(self, q):
        inner = self.inner
        return (
            [self.x_below[q]] + [self.main(q, p) for p in inner] + [self.x_above[q]],
            [None] + [self.beside(q, p) for p in inner] + [None],
            [self.x_beyond(q, False)]
            + [self.beyond(q, p) for p in inner]
            + [self.x_beyond(q, True)],
            [None] + [self.y_beyond(q, p) for p in inner] + [None],
        )


def weigh(chi_face, alpha_face):
    shrink = volume_over(chi_face)
    return shrink, alpha_face / shrink


def primitives(half, spots, cons, centred, chi, alpha, batch):
    found = {}
    for start in range(0, len(spots), batch):
        group = spots[start : start + batch]

        def gather(planes):
            return jnp.concatenate([planes[k][p] for k, p in group], axis=0)

        shrink = volume_over(gather(chi))
        mag_raw = [gather(centred[i]) for i in range(3)]
        mag = [m * shrink for m in mag_raw]
        values = recover([gather(c) * shrink for c in cons], mag)
        u = values[2:5]
        factor = gather(alpha) * lax.rsqrt(1.0 + dot(u, u))
        field = [
            factor * (u[(i + 2) % 3] * mag_raw[(i + 1) % 3] - u[(i + 1) % 3] * mag_raw[(i + 2) % 3])
            for i in range(3)
        ]
        for n, spot in enumerate(group):
            found[spot] = [value[n * half : (n + 1) * half] for value in values + mag + field]
    return found


def ring_fluxes(prims, chi, alpha, normals, d, up, down):
    found = []
    for here, there in ((0, 1), (1, 0)):
        left, right = [], []
        for a, b in zip(prims[here], prims[there]):
            below = down(a, b, 1)
            middle = a - below
            left.append(below + 0.5 * limited(below - down(a, b, 2), middle))
            right.append(a - 0.5 * limited(middle, up(a, b, 1) - a))
        shrink, weight = weigh(
            0.5 * (chi[here] + down(chi[here], chi[there], 1)),
            0.5 * (alpha[here] + down(alpha[here], alpha[there], 1)),
        )
        found.append(face_flux(left, right, normals[here] * shrink, weight, d))
    return [a - up(a, b, 1) for a, b in zip(*found)]


def early_kernel(
    cells, zst, zfl, x_below, y_below, x_above, y_above,
    st_rate, hydro_rate, slopes, electric, pairs, sides, thirds, pairs_z, sides_z, grads, seconds, damped, tensors,
):
    halo = Halo(cells, zst, zfl, x_below, y_below, x_above, y_above, None, None)
    t, fields, half, own, cy = halo.t, halo.fields, halo.half, halo.own, halo.cy
    st, fl, inner = halo.st, halo.fl, halo.inner

    for q in range(fields):
        pairs[q, 0] = halo.x_third(q, False)
        pairs[q, 1] = x_below[q]
        for p in inner:
            pairs[q, 1 + p] = halo.main(q, p)
            sides[q, p - 1] = halo.beside(q, p)
            thirds[q, p - 1] = halo.y_third(q, p)
        pairs[q, 2 + own] = x_above[q]
        pairs[q, 3 + own] = halo.x_third(q, True)
        if q < CURVED:
            pairs_z[q, 0] = halo.x_beyond(q, False)
            pairs_z[q, own + 1] = halo.x_beyond(q, True)
            for p in inner:
                pairs_z[q, p] = halo.beyond(q, p)
                sides_z[q, p - 1] = halo.y_beyond(q, p)

    span = halo.span
    face = [halo.plane(fields + 5 + i) for i in range(3)]

    def halves(kind, p):
        own_x, own_y, own_z = (f[kind][p] for f in face)
        pair = kind in (0, 2)
        known_x = pair or p < own
        last = kind == 0 and p == own + 1
        if pair:
            next_x = halo.x_third(fields, True) if last else face[0][kind][min(p + 1, own + 1)]
            next_x = t.odd(own_x, next_x)
        else:
            next_x = t.odd_swapped(own_x, face[0][kind][p + 1] if known_x else own_x)
        dx = 0.5 * (next_x - own_x)
        dz = 0.5 * (t.z_up(own_z, face[2][kind ^ 2][p], 1) - own_z)
        inside = 1 <= p <= own
        if not pair:
            here = jnp.where(t.slot == 2, halo.y_third(fields, p), own_y) if kind == 1 else own_y
            next_y = t.y_up(here, face[1][kind ^ 1][p], 1)
        else:
            next_y = t.y_up(own_y, face[1][kind ^ 1][p] if inside else own_y, 1)
        dy = 0.5 * (next_y - own_y)
        if pair and not inside:
            dy = jnp.where(t.slot == cy - 1, -(dx + dz), dy)
        if not pair and not known_x:
            dx = jnp.where(t.row < cy, -(dy + dz), dx)
        return own_x + dx, own_y + dy, own_z + dz

    spots = [(0, p) for p in span] + [(1, p) for p in inner]
    spots += [(2, p) for p in span] + [(3, p) for p in inner]
    centred = [[[None] * (own + 2) for _ in range(4)] for _ in range(3)]
    for k, p in spots:
        for i, value in enumerate(halves(k, p)):
            centred[i][k][p] = value
    chi, alpha = halo.plane(0), halo.plane(7)
    found = primitives(
        half, spots, [halo.plane(fields + q) for q in range(5)], centred, chi, alpha, BATCH
    )

    lines = [[found[0, p][i] for p in span] for i in range(8)] + [chi[0], alpha[0]]
    odd_lines = [[t.odd(f[p], f[min(p + 1, own + 1)]) for p in span] for f in lines]
    fluxes = [None]
    for p in range(1, own + 2):
        left, right = [], []
        for f, o in zip(lines[:8], odd_lines):
            here = f[p] - o[p - 1]
            left.append(o[p - 1] + 0.5 * limited(o[p - 1] - f[p - 1], here))
            right.append(f[p] - 0.5 * limited(here, o[p] - f[p]))
        shrink, weight = weigh(
            0.5 * (lines[8][p] + odd_lines[8][p - 1]), 0.5 * (lines[9][p] + odd_lines[9][p - 1])
        )
        fluxes.append(face_flux(left, right, face[0][0][p] * shrink, weight, 0))
    for p in inner:
        changes = [
            ring_fluxes(
                [found[k, p][:8] for k in (0, kind)],
                [chi[k][p] for k in (0, kind)],
                [alpha[k][p] for k in (0, kind)],
                [face[d][k][p] for k in (0, kind)],
                d,
                up,
                down,
            )
            for d, kind, up, down in ((1, 1, t.y_up, t.y_down), (2, 2, t.z_up, t.z_down))
        ]
        for q in range(5):
            change = fluxes[p][q] - t.odd(fluxes[p][q], fluxes[p + 1][q])
            tensors[p - 1, 6 + q] = change + changes[0][q] + changes[1][q]
        rest, pressure = found[0, p][:2]
        u = found[0, p][2:5]
        parts = stress_parts(rest, pressure, u, found[0, p][5:8])
        lorentz_sq, over, over_sq, time_b, grown_b, b_square, enthalpy, inertia = parts
        total_pressure = pressure + 0.5 * b_square
        for s, (i, j) in enumerate(INDEX_PAIRS):
            value = inertia * u[i] * u[j] - over_sq * (grown_b[i] * grown_b[j])
            tensors[p - 1, s] = value + total_pressure if i == j else value

    ex, ey, ez = (
        [[found[k, p][8 + i] if (k, p) in found else None for p in span] for k in range(4)]
        for i in range(3)
    )
    ey_x = [
        [ey[k][p] + t.odd(ey[k][p - 1], ey[k][p]) if p else None for p in span] for k in (0, 2)
    ]
    edge_y = [None] + [ey_x[0][p] + t.z_down(ey_x[0][p], ey_x[1][p], 1) for p in span[1:]]
    for p in span[1:]:
        electric[p - 1] = ez[0][p] + t.odd(ez[0][p - 1], ez[0][p])
    for p in inner:
        electric[own + p] = ez[1][p]
        edge_y_z = ey_x[1][p] + t.z_down(ey_x[1][p], ey_x[0][p], 1)
        ex_y = ex[0][p] + t.y_down(ex[0][p], ex[1][p], 1)
        ex_y_h = ex[1][p] + t.y_down(ex[1][p], ex[0][p], 1)
        ex_y_z = ex[2][p] + t.y_down(ex[2][p], ex[3][p], 1)
        ex_y_hz = ex[3][p] + t.y_down(ex[3][p], ex[2][p], 1)
        edge_x = ex_y + t.z_down(ex_y, ex_y_z, 1)
        edge_x_h = ex_y_h + t.z_down(ex_y_h, ex_y_hz, 1)
        edge_x_z = ex_y_z + t.z_down(ex_y_z, ex_y, 1)
        place = slice((p - 1) * half, p * half)
        hydro_rate[5, place, :] = t.z_up(edge_y[p], edge_y_z, 1) - edge_y[p]
        hydro_rate[6, place, :] = edge_x - t.z_up(edge_x, edge_x_z, 1)
        hydro_rate[7, place, :] = (t.y_up(edge_x, edge_x_h, 1) - edge_x) - (
            t.odd(edge_y[p], edge_y[p + 1]) - edge_y[p]
        )

    def pair_step(index):
        p = index + 1
        base = index * half

        for q in range(fields):
            centre = pairs[q, p + 1]
            x_m3 = t.odd(pairs[q, p - 1], pairs[q, p])
            x_m2 = pairs[q, p]
            x_m1 = t.odd(pairs[q, p], centre)
            x_p1 = t.odd(centre, pairs[q, p + 2])
            x_p2 = pairs[q, p + 2]
            x_p3 = t.odd(pairs[q, p + 2], pairs[q, p + 3])
            side, third = sides[q, index], thirds[q, index]
            y_m1, y_m2 = t.y_down(centre, side, 1), t.y_down(centre, side, 2)
            y_p1, y_p2 = t.y_up(centre, side, 1), t.y_up(centre, side, 2)
            y_m3 = t.turn(
                jnp.where(t.slot >= cy - 2, side, jnp.where(t.slot == cy - 3, third, centre)), 3
            )
            y_p3 = t.turn(jnp.where(t.slot < 2, side, jnp.where(t.slot == 2, third, centre)), -3)
            beyond = zst[q, pl.ds(base, half), :]
            z_m1, z_m2, z_m3 = (t.z_down(centre, beyond, k) for k in (1, 2, 3))
            z_p1, z_p2, z_p3 = (t.z_up(centre, beyond, k) for k in (1, 2, 3))
            dx = first_diff(x_m2, x_m1, x_p1, x_p2)
            dy = first_diff(y_m2, y_m1, y_p1, y_p2)
            grads[q, 0] = dx
            if q < CURVED:
                slopes[q, index] = dx
            grads[q, 1] = dy
            grads[q, 2] = first_diff(z_m2, z_m1, z_p1, z_p2)
            near = [x_m1 + x_p1, y_m1 + y_p1, z_m1 + z_p1]
            far = [x_m2 + x_p2, y_m2 + y_p2, z_m2 + z_p2]
            outer = (x_m3 + x_p3) + (y_m3 + y_p3) + (z_m3 + z_p3)
            damped[q] = (DISSIPATION / 64.0) * (
                outer - 6.0 * (far[0] + far[1] + far[2]) + 15.0 * (near[0] + near[1] + near[2])
                - 60.0 * centre
            )
            if q < CURVED:
                for s, d in ((0, 0), (3, 1), (5, 2)):
                    seconds[q, s] = (1.0 / 12.0) * (16.0 * near[d] - far[d] - 30.0 * centre)
                b_m, b_c, b_p = pairs_z[q, p - 1], pairs_z[q, p], pairs_z[q, p + 1]
                dx_z = first_diff(b_m, t.odd(b_m, b_c), t.odd(b_c, b_p), b_p)
                b_s = sides_z[q, p - 1]
                dy_z = first_diff(
                    t.y_down(b_c, b_s, 2),
                    t.y_down(b_c, b_s, 1),
                    t.y_up(b_c, b_s, 1),
                    t.y_up(b_c, b_s, 2),
                )
                for s, inside, outside in ((2, dx, dx_z), (4, dy, dy_z)):
                    seconds[q, s] = first_diff(
                        t.z_down(inside, outside, 2),
                        t.z_down(inside, outside, 1),
                        t.z_up(inside, outside, 1),
                        t.z_up(inside, outside, 2),
                    )

        def value(q):
            return pairs[q, p + 1]

        def fluid_value(q):
            return fl[q, pl.ds(base, half), :]

        conformal, lapse = value(0), value(7)
        over_chi = 1.0 / conformal
        metric = symmetric([value(1 + s) for s in range(6)])
        shift = [value(8 + i) for i in range(3)]
        extrinsic, theta = value(11), value(21)
        traceless = symmetric([value(12 + s) for s in range(6)])
        connection = [value(18 + i) for i in range(3)]
        inverse = inverse_metric(metric)
        grad = [[grads[q, k] for k in range(3)] for q in range(fields)]
        chi_grad, lapse_grad = grad[0], grad[7]
        shift_grad = [[grad[8 + i][k] for i in range(3)] for k in range(3)]
        trace_k = extrinsic + 2.0 * theta

        stress = symmetric([tensors[p - 1, s] for s in range(6)])
        held = [fluid_value(q) for q in range(5)]
        shrink = volume_over(conformal)
        energy = held[4] + held[0]
        third_k = trace_k * (1.0 / 3.0)
        curved = [
            [
                (traceless[i][j] + metric[i][j] * third_k) if i <= j else None for j in range(3)
            ]
            for i in range(3)
        ]
        work = (
            stress[0][0] * curved[0][0]
            + stress[1][1] * curved[1][1]
            + stress[2][2] * curved[2][2]
            + 2.0
            * (
                stress[0][1] * curved[0][1]
                + stress[0][2] * curved[0][2]
                + stress[1][2] * curved[1][2]
            )
        )
        rates = [tensors[p - 1, 6 + q] for q in range(5)]
        for i in range(3):
            rates[1 + i] = (
                rates[1 + i]
                - energy * lapse_grad[i]
                + total([held[1 + k] * grad[8 + k][i] for k in range(3)])
            )
        rates[4] = (
            rates[4] + lapse * work * over_chi / shrink - dot(held[1:4], lapse_grad)
        )
        for q in range(5):
            hydro_rate[q, pl.ds(base, half), :] = rates[q]
        density = energy * shrink
        momentum = [held[1 + i] * shrink for i in range(3)]

        lowered = [[[None] * 3 for _ in range(3)] for _ in range(3)]
        for i in range(3):
            for j in range(3):
                for k in range(j, 3):
                    got = 0.5 * (
                        grad[1 + slot_of(i, k)][j]
                        + grad[1 + slot_of(i, j)][k]
                        - grad[1 + slot_of(j, k)][i]
                    )
                    lowered[i][j][k] = lowered[i][k][j] = got
        raised = [[[None] * 3 for _ in range(3)] for _ in range(3)]
        for i in range(3):
            for j in range(3):
                for k in range(j, 3):
                    got = total([inverse[i][l] * lowered[l][j][k] for l in range(3)])
                    raised[i][j][k] = raised[i][k][j] = got
        contracted = [trace_with(inverse, raised[i]) for i in range(3)]

        def hessian_trace(q):
            return (
                inverse[0][0] * seconds[q, 0]
                + inverse[1][1] * seconds[q, 3]
                + inverse[2][2] * seconds[q, 5]
                + 2.0 * (inverse[0][2] * seconds[q, 2] + inverse[1][2] * seconds[q, 4])
            )

        def second_cov(q, slope):
            bent = [total([raised[k][i][j] * slope[k] for k in range(3)]) for i, j in INDEX_PAIRS]
            return symmetric(
                [-bent[s] if s == 1 else seconds[q, s] - bent[s] for s in range(len(bent))]
            )

        chi_cov = second_cov(0, chi_grad)
        chi_lap = trace_with(inverse, chi_cov)
        raised_chi = [dot(inverse[i], chi_grad) for i in range(3)]
        chi_square = dot(raised_chi, chi_grad)
        cross_term = dot(raised_chi, lapse_grad)
        half_chi = 0.5 * over_chi
        plain_cov = second_cov(7, lapse_grad)
        lapse_cov = symmetric(
            [
                plain_cov[i][j]
                + (
                    chi_grad[i] * lapse_grad[j]
                    + chi_grad[j] * lapse_grad[i]
                    - metric[i][j] * cross_term
                )
                * half_chi
                for i, j in INDEX_PAIRS
            ]
        )
        lapse_lap = conformal * trace_with(inverse, lapse_cov)

        mixed = [
            [[dot(inverse[l], lowered[k][j]) for j in range(3)] for k in range(3)]
            for l in range(3)
        ]
        quarter_sq = half_chi * half_chi
        metric_factor = chi_lap * half_chi - 3.0 * chi_square * quarter_sq
        ricci = []
        for i, j in INDEX_PAIRS:
            second_part = -0.5 * hessian_trace(1 + slot_of(i, j))
            connection_part = 0.5 * total(
                [metric[k][i] * grad[18 + k][j] + metric[k][j] * grad[18 + k][i] for k in range(3)]
            )
            contracted_part = 0.5 * total(
                [contracted[k] * (lowered[i][j][k] + lowered[j][i][k]) for k in range(3)]
            )
            if i == j:
                quadratic = total(
                    [
                        raised[k][l][i] * (2.0 * mixed[l][i][k] + mixed[l][k][i])
                        for k in range(3)
                        for l in range(3)
                    ]
                )
            else:
                quadratic = total(
                    [
                        raised[k][l][i] * (mixed[l][j][k] + mixed[l][k][j])
                        + raised[k][l][j] * mixed[l][i][k]
                        for k in range(3)
                        for l in range(3)
                    ]
                )
            conformal_part = (
                chi_cov[i][j] * half_chi
                + metric[i][j] * metric_factor
                - chi_grad[i] * chi_grad[j] * quarter_sq
            )
            ricci.append(
                second_part + connection_part + contracted_part + quadratic + conformal_part
            )
        ricci = symmetric(ricci)
        ricci_scalar = conformal * trace_with(inverse, ricci)
        stress_trace = conformal * trace_with(inverse, stress)

        up_a = [
            [total([inverse[i][k] * traceless[k][j] for k in range(3)]) for j in range(3)]
            for i in range(3)
        ]
        raised_a = symmetric(
            [total([up_a[i][l] * inverse[j][l] for l in range(3)]) for i, j in INDEX_PAIRS]
        )
        a_square = trace_with(traceless, raised_a)
        shift_div = shift_grad[0][0] + shift_grad[1][1] + shift_grad[2][2]
        two_thirds_div = (2.0 / 3.0) * shift_div

        def finish(q, rate):
            rate = rate + dot(shift, grad[q]) + damped[q]
            st_rate[q, pl.ds(base, half), :] = rate

        finish(0, (2.0 / 3.0) * conformal * (lapse * trace_k - shift_div))
        finish(7, -2.0 * lapse * extrinsic)
        for i in range(3):
            finish(8 + i, 0.75 * connection[i] - SHIFT_DAMPING * shift[i])
        finish(
            11,
            lapse
            * (
                a_square
                + trace_k * trace_k * (1.0 / 3.0)
                + FOUR_PI * (stress_trace + density)
                + KAPPA_ONE * theta
            )
            - lapse_lap,
        )
        source = symmetric(
            [
                lapse * (ricci[i][j] - 2.0 * FOUR_PI * stress[i][j]) - lapse_cov[i][j]
                for i, j in INDEX_PAIRS
            ]
        )
        third_trace = trace_with(inverse, source) * (1.0 / 3.0)
        for s, (i, j) in enumerate(INDEX_PAIRS):
            finish(
                1 + s,
                total(
                    [
                        metric[i][k] * shift_grad[j][k] + metric[j][k] * shift_grad[i][k]
                        for k in range(3)
                    ]
                )
                - metric[i][j] * two_thirds_div
                - 2.0 * lapse * traceless[i][j],
            )
            product = total([traceless[i][k] * up_a[k][j] for k in range(3)])
            finish(
                12 + s,
                total(
                    [
                        traceless[i][k] * shift_grad[j][k] + traceless[j][k] * shift_grad[i][k]
                        for k in range(3)
                    ]
                )
                - traceless[i][j] * two_thirds_div
                + conformal * (source[i][j] - metric[i][j] * third_trace)
                + lapse * (trace_k * traceless[i][j] - 2.0 * product),
            )
        for i in range(3):
            bracket = (
                trace_with(raised_a, raised[i])
                - 1.5 * dot(raised_a[i], chi_grad) * over_chi
                - dot(inverse[i], [2.0 * grad[11][j] + grad[21][j] for j in range(3)]) * (1.0 / 3.0)
                - 2.0 * FOUR_PI * dot(inverse[i], momentum)
            )
            spread = [
                seconds[8, 0] + seconds[10, 2],
                seconds[9, 3] + seconds[10, 4],
                seconds[8, 2] + seconds[9, 4] + seconds[10, 5],
            ]
            finish(
                18 + i,
                contracted[i] * two_thirds_div
                - total([contracted[j] * shift_grad[j][i] for j in range(3)])
                + hessian_trace(8 + i)
                + dot(inverse[i], spread) * (1.0 / 3.0)
                - 2.0 * dot(raised_a[i], lapse_grad)
                + 2.0
                * lapse
                * (bracket - KAPPA_ONE * (connection[i] - contracted[i])),
            )
        finish(
            21,
            0.5
            * lapse
            * (
                ricci_scalar
                - a_square
                + (2.0 / 3.0) * trace_k * trace_k
                - 4.0 * FOUR_PI * density
            )
            - 2.0 * KAPPA_ONE * lapse * theta,
        )

    for index in range(own):
        pair_step(index)


def late_kernel(
    cells, zst, zfl, x_below, y_below, x_above, y_above, c_below, c_above, line_two, line_top,
    st_rate, hydro_rate, slopes, electric, st_out, fl_out,
):
    halo = Halo(cells, zst, zfl, x_below, y_below, x_above, y_above, c_below, c_above)
    t, fields, half, own = halo.t, halo.fields, halo.half, halo.own
    inner, span = halo.inner, halo.span

    top = jnp.maximum(line_top[...], line_two[...])
    for lines in (c_below, c_above):
        top = jnp.maximum(top, lines[CORNER_TILES - 1, TOP_ROW : TOP_ROW + 1, :])
    dt = COURANT / top

    for p in inner:
        place = slice((p - 1) * half, p * half)
        mixed = []
        for q in range(CURVED):
            s_m, s_c, s_p = (
                halo.beside(q, n) if 1 <= n <= own else halo.corner(q, n) for n in (p - 1, p, p + 1)
            )
            slope = slopes[q, p - 1]
            slope_side = first_diff(s_m, t.odd_swapped(s_m, s_c), t.odd_swapped(s_c, s_p), s_p)
            mixed.append(
                first_diff(
                    t.y_down(slope, slope_side, 2),
                    t.y_down(slope, slope_side, 1),
                    t.y_up(slope, slope_side, 1),
                    t.y_up(slope, slope_side, 2),
                )
            )
        conformal, lapse = halo.main(0, p), halo.main(7, p)
        metric = [halo.main(1 + s, p) for s in range(6)]
        inverse = inverse_metric(symmetric(metric))
        half_chi = 0.5 / conformal
        cross = inverse[0][1]
        chi_trace = 2.0 * cross * mixed[0] * half_chi
        ricci = [metric[s] * chi_trace - cross * mixed[1 + s] for s in range(6)]
        ricci[1] = ricci[1] + mixed[0] * half_chi
        source = [lapse * r for r in ricci]
        source[1] = source[1] - mixed[7]
        third_trace = trace_with(inverse, symmetric(source)) * (1.0 / 3.0)
        extra = {
            11: -2.0 * conformal * cross * mixed[7],
            21: 0.5 * lapse * conformal * trace_with(inverse, symmetric(ricci)),
        }
        for s in range(6):
            extra[12 + s] = conformal * (source[s] - metric[s] * third_trace)
        for i in range(3):
            extra[18 + i] = 2.0 * cross * mixed[8 + i] + (1.0 / 3.0) * (
                inverse[i][0] * mixed[9] + inverse[i][1] * mixed[8]
            )
        for q in range(fields):
            rate = st_rate[q, place, :]
            if q in extra:
                rate = rate + extra[q]
            st_out[q, place, :] = halo.main(q, p) + dt * rate

    end = own + 1
    ends = (0, end)
    bx_face, by_face, bz_face = ({p: halo.corner(fields + 5 + i, p) for p in ends} for i in range(3))
    layers = {p: halo.corner_layers(p) for p in ends}
    bx_face[end] = layers[end]
    by_face[0] = jnp.where(t.slot < 2, layers[0], by_face[0])
    centred = [{}, {}, {}]
    for p in ends:
        following = halo.beside(fields + 5, 1) if p == 0 else bx_face[p]
        edge_cells = x_below if p == 0 else x_above
        dx = 0.5 * (t.odd_swapped(bx_face[p], following) - bx_face[p])
        dy = 0.5 * (t.y_up(by_face[p], edge_cells[fields + 6], 1) - by_face[p])
        centred[0][p] = bx_face[p] + dx
        centred[1][p] = by_face[p] + dy
        centred[2][p] = bz_face[p] - (dx + dy)
    corners = [{p: halo.corner(q, p) for p in ends} for q in [0, 7] + list(range(fields, fields + 5))]
    found = primitives(
        half, [(0, p) for p in ends], [[c] for c in corners[2:]], [[c] for c in centred],
        [corners[0]], [corners[1]], 2,
    )
    ez_h = [found[0, 0][10]] + [electric[own + p] for p in inner] + [found[0, end][10]]
    ez_x_h = [None] + [ez_h[p] + t.odd_swapped(ez_h[p - 1], ez_h[p]) for p in span[1:]]
    ez_x = [None] + [electric[p - 1] for p in span[1:]]
    edge_z = [None] + [ez_x[p] + t.y_down(ez_x[p], ez_x_h[p], 1) for p in span[1:]]
    quarter = 0.25 * dt
    for p in inner:
        place = slice((p - 1) * half, p * half)
        edge_z_h = ez_x_h[p] + t.y_down(ez_x_h[p], ez_x[p], 1)
        for q in range(5):
            fl_out[q, place, :] = halo.main(fields + q, p) + dt * hydro_rate[q, place, :]
        x_rate = hydro_rate[5, place, :] - (t.y_up(edge_z[p], edge_z_h, 1) - edge_z[p])
        y_rate = hydro_rate[6, place, :] + (t.odd(edge_z[p], edge_z[p + 1]) - edge_z[p])
        z_rate = hydro_rate[7, place, :]
        for i, rate in enumerate((x_rate, y_rate, z_rate)):
            fl_out[5 + i, place, :] = halo.main(fields + 5 + i, p) + quarter * rate


def per_device(spacetime, fluid):
    fields, cx, cy, cz = spacetime.shape
    rows = cx * cy
    st = spacetime.reshape(fields, rows, cz)
    fl = fluid.reshape(FLUID, rows, cz)
    sizes = [lax.axis_size(a) for a in ("gx", "gy", "gz")]
    tile = (2 * cy, cz)
    f32 = jnp.float32

    def shape(*dims):
        return jax.ShapeDtypeStruct(dims, f32)

    def beyond(cells):
        n = sizes[2]
        after = lax.ppermute(cells, "gz", [((i + 1) % n, i) for i in range(n)])
        if n == 2:
            return after
        before = lax.ppermute(cells, "gz", [(i, (i + 1) % n) for i in range(n)])
        lane = lax.broadcasted_iota(jnp.int32, cells.shape, 2)
        return jnp.where(lane < cz // 2, after, before)

    params = pltpu.CompilerParams(vmem_limit_bytes=48 * 1024 * 1024)
    zst, zfl = beyond(st), beyond(fl)
    cells = jnp.concatenate([st, fl], axis=0)
    face = shape(face_tiles(fields), *tile)
    corner = shape(CORNER_TILES, *tile)
    lane_row = shape(1, cz)
    x_low, x_high, y_low, y_high, top = pl.pallas_call(
        pack_kernel, out_shape=[face] * 4 + [lane_row], compiler_params=params, name="pack"
    )(cells, zst, zfl)

    def move(cells, dx, dy):
        nx, ny = sizes[0], sizes[1]
        hops = [
            (i * ny + j, ((i + dx) % nx) * ny + (j + dy) % ny) for i in range(nx) for j in range(ny)
        ]
        return lax.ppermute(cells, ("gx", "gy"), hops)

    short = sizes[0] <= 4 and sizes[1] <= 4 and sizes[2] <= 2
    x_below = move(x_high, 1, 0)
    y_below = move(y_high, 0, 1)
    x_above = move(x_low, -1, 0)
    y_above = move(y_low, 0, -1)
    top_two = move(top, 2, 0) if short and sizes[0] == 4 else top
    c_low, c_high, line_top = pl.pallas_call(
        relay_kernel,
        out_shape=[corner, corner, lane_row],
        compiler_params=params,
        name="relay",
    )(x_below, x_above, y_below, top, top_two)
    c_above = move(c_low, 0, -1)
    c_below = move(c_high, 0, 1)
    if not short:
        line_two = lax.pmax(line_top, ("gx", "gy", "gz"))
    else:
        line_two = move(line_top, 0, 2) if sizes[1] == 4 else line_top
    own = cx // 2
    arrived = (cells, zst, zfl, x_below, y_below, x_above, y_above)
    early = pl.pallas_call(
        early_kernel,
        out_shape=[
            shape(*st.shape),
            shape(FLUID, rows, cz),
            shape(CURVED, own, *tile),
            shape(2 * own + 1, *tile),
        ],
        scratch_shapes=[
            pltpu.VMEM((fields, own + 4) + tile, f32),
            pltpu.VMEM((fields, own) + tile, f32),
            pltpu.VMEM((fields, own) + tile, f32),
            pltpu.VMEM((CURVED, own + 2) + tile, f32),
            pltpu.VMEM((CURVED, own) + tile, f32),
            pltpu.VMEM((fields, 3) + tile, f32),
            pltpu.VMEM((CURVED, 6) + tile, f32),
            pltpu.VMEM((fields,) + tile, f32),
            pltpu.VMEM((own, 11) + tile, f32),
        ],
        compiler_params=params,
        name="early",
    )(*arrived)
    st_next, fl_next = pl.pallas_call(
        late_kernel,
        out_shape=[shape(*st.shape), shape(*fl.shape)],
        compiler_params=params,
        name="late",
    )(*arrived, c_below, c_above, line_two, line_top, *early)
    return st_next.reshape(spacetime.shape), fl_next.reshape(fluid.shape)


def solution(mesh):
    spec = P(None, "gx", "gy", "gz")
    return jax.shard_map(
        per_device, mesh=mesh, in_specs=(spec, spec), out_specs=(spec, spec), check_vma=False
    )
```

```python
import functools
import math

import jax
import jax.numpy as jnp
from jax import lax
from jax.experimental import pallas as pl
from jax.experimental.pallas import tpu as pltpu
from jax.sharding import PartitionSpec as P

RECOVERY_STEPS = 4
INDEX_PAIRS = ((0, 0), (0, 1), (0, 2), (1, 1), (1, 2), (2, 2))
COURANT = 0.25
DISSIPATION = 0.2
KAPPA_ONE = 0.02
SHIFT_DAMPING = 1.0
SPEED_CAP = 0.99
PRESSURE_FLOOR = 0.01
FOUR_PI = 4.0 * math.pi

BATCH = 6
CURVED = 11
FLUID = 8


def total(pieces):
    summed = pieces[0]
    for member in pieces[1:]:
        summed = summed + member
    return summed


def dot(first_vec, second_vec):
    return total([first_vec[i] * second_vec[i] for i in range(3)])


def slot_of(i, j):
    return INDEX_PAIRS.index((min(i, j), max(i, j)))


def symmetric(entries):
    return [[entries[slot_of(i, j)] for j in range(3)] for i in range(3)]


def trace_with(inverse, tensor):
    return (
        inverse[0][0] * tensor[0][0]
        + inverse[1][1] * tensor[1][1]
        + inverse[2][2] * tensor[2][2]
        + 2.0
        * (
            inverse[0][1] * tensor[0][1]
            + inverse[0][2] * tensor[0][2]
            + inverse[1][2] * tensor[1][2]
        )
    )


def inverse_metric(metric):
    cofactor = [
        metric[1][1] * metric[2][2] - metric[1][2] * metric[1][2],
        metric[0][2] * metric[1][2] - metric[0][1] * metric[2][2],
        metric[0][1] * metric[1][2] - metric[0][2] * metric[1][1],
        metric[0][0] * metric[2][2] - metric[0][2] * metric[0][2],
        metric[0][1] * metric[0][2] - metric[0][0] * metric[1][2],
        metric[0][0] * metric[1][1] - metric[0][1] * metric[0][1],
    ]
    determinant = (
        metric[0][0] * cofactor[0] + metric[0][1] * cofactor[1] + metric[0][2] * cofactor[2]
    )
    over = 1.0 / determinant
    return symmetric([c * over for c in cofactor])


class Tile:
    def __init__(self, cy, cz):
        self.cy, self.rows, self.lanes = cy, 2 * cy, cz
        shape = (self.rows, cz)
        self.row = lax.broadcasted_iota(jnp.int32, shape, 0)
        self.lane = lax.broadcasted_iota(jnp.int32, shape, 1)
        self.slot = lax.rem(self.row, cy)

    def turn(self, tile, amount):
        amount = amount % self.rows
        return tile if amount == 0 else pltpu.roll(tile, amount, 0)

    def spin(self, tile, amount):
        amount = amount % self.lanes
        return tile if amount == 0 else pltpu.roll(tile, amount, 1)

    def swap(self, tile):
        return self.turn(tile, self.cy)

    def odd(self, a, b):
        return self.turn(jnp.where(self.row < self.cy, b, a), self.cy)

    def odd_swapped(self, a, b):
        return self.turn(jnp.where(self.row < self.cy, a, b), self.cy)

    def y_up(self, main, beyond, k):
        return self.turn(jnp.where(self.slot < k, beyond, main), -k)

    def y_down(self, main, beyond, k):
        return self.turn(jnp.where(self.slot >= self.cy - k, beyond, main), k)

    def z_up(self, main, beyond, k):
        return self.spin(jnp.where(self.lane < k, beyond, main), -k)

    def z_down(self, main, beyond, k):
        return self.spin(jnp.where(self.lane >= self.lanes - k, beyond, main), k)

    def corner_rows(self, side, turn):
        places = ((0, 2), (self.cy - 1, self.cy + 1))[side]
        first, second = [(place + turn) % self.rows for place in places]
        return (self.row == first) | (self.row == second)

    def join_low(self, u, v):
        return jnp.where(self.slot < 2, self.swap(u), self.turn(v, 2))

    def join_high(self, u, v):
        return jnp.where(self.slot >= self.cy - 2, self.swap(u), self.turn(self.swap(v), -2))

    def part_first(self, from_above, from_below):
        return jnp.where(self.slot < 2, from_above, from_below)

    def part_second(self, from_above, from_below):
        return self.turn(jnp.where(self.slot < 2, from_below, from_above), 2)


def edge_list(tiles):
    fields = next(n for n in range(tiles) if face_tiles(n) == tiles)
    return list(range(CURVED)) + list(range(fields, fields + FLUID))


CORNER_TURNS = (0, 1, 4, 5)
CORNER_TILES = CURVED + FLUID // 4 + 1


def face_tiles(fields):
    return fields + FLUID + len(pairs_of(third_list(fields))) + 1


def third_list(fields):
    return list(range(fields + 1))


def pairs_of(items):
    return [(items[i], items[min(i + 1, len(items) - 1)]) for i in range(0, len(items), 2)]


def top_speed(st):
    inverse = inverse_metric(symmetric([st[1 + s] for s in range(6)]))
    scale = 2.0 * st[7] * st[0]
    speeds = [jnp.abs(st[8 + d]) + jnp.sqrt(scale * inverse[d][d]) for d in range(3)]
    top = jnp.maximum(jnp.maximum(speeds[0], speeds[1]), speeds[2])
    return jnp.max(jnp.max(top, axis=1, keepdims=True), axis=0, keepdims=True)


def pack_kernel(cells, zst, zfl, *outs):
    fields, rows, lanes = zst.shape
    st, fl = cells.at[0:fields], cells.at[fields : fields + FLUID]
    cy = rows // 4
    t = Tile(cy, lanes)
    x_low, x_high, y_low, y_high = outs
    half = t.rows

    def own(ref, q):
        return [ref[q, 0:half, :], ref[q, half : 2 * half, :]]

    tiles, beyond = [], []
    for q in range(fields):
        tiles.append(own(st, q))
        beyond.append(own(zst, q) if q < CURVED else None)
    for q in range(FLUID):
        tiles.append(own(fl, q))
        beyond.append(own(zfl, q))

    packed = [None] * 4
    place = 0
    for q, (first, second) in enumerate(tiles):
        x_low[q] = first
        x_high[q] = second
        y_low[q] = t.join_low(first, second)
        y_high[q] = t.join_high(first, second)
        if beyond[q] is not None:
            zf, zs = beyond[q]
            for m, piece in enumerate((zf, zs, t.join_low(zf, zs), t.join_high(zf, zs))):
                piece = t.spin(piece, 4 * place + 2)
                packed[m] = (
                    piece if place == 0 else jnp.where(t.lane < 4 * place, packed[m], piece)
                )
            place += 1
    for n, (a, b) in enumerate(pairs_of(third_list(fields))):
        slot = fields + FLUID + n
        xa, xb = (tiles[q if q < fields else fields + 5] for q in (a, b))
        x_low[slot] = jnp.where(t.row < cy, xa[1], t.swap(xb[1]))
        x_high[slot] = jnp.where(t.row < cy, t.swap(xb[0]), xa[0])
        ya, yb = (tiles[q if q < fields else fields + 6] for q in (a, b))
        w = [t.swap(ya[0]), t.swap(ya[1]), t.swap(yb[0]), t.swap(yb[1])]
        s = t.slot
        y_low[slot] = jnp.where(
            s == 2,
            w[0],
            jnp.where(s == 3, t.turn(w[1], 1), jnp.where(s == 0, t.turn(w[2], -2), t.turn(w[3], -1))),
        )
        y_high[slot] = jnp.where(
            s == 1,
            w[0],
            jnp.where(s == 0, t.turn(w[1], -1), jnp.where(s == 3, t.turn(w[2], 2), t.turn(w[3], 1))),
        )
    last = x_low.shape[0] - 1
    for out, piece in zip((x_low, x_high, y_low, y_high), packed):
        out[last] = piece


def speed_kernel(cells, out):
    out[...] = jnp.broadcast_to(top_speed(cells), out.shape)


def relay_kernel(x_below, x_above, to_low, to_high):
    t = Tile(x_below.shape[1] // 2, x_below.shape[2])
    edge = edge_list(x_below.shape[0])
    for q in range(CURVED):
        to_low[q] = t.join_low(x_below[q], x_above[q])
        to_high[q] = t.join_high(x_below[q], x_above[q])
    for n in range(0, FLUID, 4):
        low, high = None, None
        for turn, q in zip(CORNER_TURNS, edge[CURVED + n : CURVED + n + 4]):
            below = t.turn(t.join_low(x_below[q], x_above[q]), turn)
            above = t.turn(t.join_high(x_below[q], x_above[q]), turn)
            if low is None:
                low, high = below, above
            else:
                low = jnp.where(t.corner_rows(0, turn), below, low)
                high = jnp.where(t.corner_rows(1, turn), above, high)
        to_low[CURVED + n // 4] = low
        to_high[CURVED + n // 4] = high
    along_x, along_y = edge[CURVED + 5], edge[CURVED + 6]
    to_low[CORNER_TILES - 1] = t.join_low(x_below[along_y], x_above[along_y])
    to_high[CORNER_TILES - 1] = t.join_high(x_below[along_x], x_above[along_x])


def limited(a, b):
    return jnp.maximum(jnp.minimum(a, b), 0.0) + jnp.minimum(jnp.maximum(a, b), 0.0)


def recover(conserved, magnetic):
    density = conserved[0]
    momenta = conserved[1:4]
    energy = conserved[4] + density
    mom_sq = dot(momenta, momenta)
    mag_sq = dot(magnetic, magnetic)
    cross = dot(momenta, magnetic)
    cross_sq = cross * cross

    def state(z):
        grown = z + mag_sq
        over = 1.0 / (z * grown)
        speed_sq = (mom_sq * z * z + cross_sq * (2.0 * z + mag_sq)) * over * over
        kept = 1.0 - jnp.minimum(speed_sq, SPEED_CAP)
        rest = density * jnp.sqrt(kept)
        return kept, rest, 0.5 * (z * kept - rest), grown * over

    z = jnp.maximum(energy - 0.5 * mag_sq, density)
    for _ in range(RECOVERY_STEPS):
        kept, rest, pressure, over_z = state(z)
        residual = (
            z
            + mag_sq
            - pressure
            - 0.5 * mag_sq * kept
            - 0.5 * cross_sq * over_z * over_z
            - energy
        )
        z = jnp.maximum(z - residual / (1.0 - 0.5 * kept), density)
    kept, rest, pressure, over_z = state(z)
    pressure = jnp.maximum(pressure, PRESSURE_FLOOR * rest)
    scale = lax.rsqrt(kept) / (z + mag_sq)
    along = cross * over_z
    four_vel = [scale * (momenta[i] + along * magnetic[i]) for i in range(3)]
    return [rest, pressure] + four_vel


def stress_parts(rest, pressure, u, magnetic):
    lorentz_sq = 1.0 + dot(u, u)
    over = lax.rsqrt(lorentz_sq)
    over_sq = over * over
    time_b = dot(u, magnetic)
    grown_b = [magnetic[i] + time_b * u[i] for i in range(3)]
    b_square = (dot(magnetic, magnetic) + time_b * time_b) * over_sq
    enthalpy = rest + 2.0 * pressure
    inertia = enthalpy + b_square
    return lorentz_sq, over, over_sq, time_b, grown_b, b_square, enthalpy, inertia


def face_state(rest, pressure, u, magnetic, d):
    lorentz_sq, over, over_sq, time_b, grown_b, b_square, enthalpy, inertia = stress_parts(
        rest, pressure, u, magnetic
    )
    total_pressure = pressure + 0.5 * b_square
    lorentz = lorentz_sq * over
    density = rest * lorentz
    carried = inertia * lorentz
    time_over = time_b * over
    conserved = [density]
    conserved += [carried * u[j] - time_over * grown_b[j] for j in range(3)]
    conserved += [inertia * lorentz_sq - total_pressure - time_b * time_b - density]
    mass_flux = rest * u[d]
    flux = [mass_flux]
    pushed = inertia * u[d]
    b_over = grown_b[d] * over_sq
    for j in range(3):
        flux_j = pushed * u[j] - b_over * grown_b[j]
        flux.append(flux_j + total_pressure if j == d else flux_j)
    flux.append(carried * u[d] - time_over * grown_b[d] - mass_flux)
    ratio = 1.0 / (enthalpy * inertia)
    sound_sq = 2.0 * pressure * inertia * ratio
    alfven_sq = b_square * enthalpy * ratio
    fast_sq = sound_sq + alfven_sq - sound_sq * alfven_sq
    slow = 1.0 - fast_sq
    velocity = u[d] * over
    rest_part = 1.0 - dot(u, u) * over_sq * fast_sq
    spread = jnp.sqrt(fast_sq * over_sq * (rest_part - velocity * velocity * slow))
    fastest = (jnp.abs(velocity * slow) + spread) / rest_part
    return conserved, flux, fastest


def face_flux(left, right, normal, weight, d):
    sides = []
    for state in (left, right):
        magnetic = [normal if i == d else state[5 + i] for i in range(3)]
        sides.append(face_state(state[0], state[1], state[2:5], magnetic, d))
    (cons_l, flux_l, fast_l), (cons_r, flux_r, fast_r) = sides
    signal = jnp.maximum(fast_l, fast_r)
    scale = 0.5 * weight
    return [scale * (flux_l[q] + flux_r[q] - signal * (cons_r[q] - cons_l[q])) for q in range(5)]


def volume_over(conformal):
    return conformal * jnp.sqrt(conformal)


def first_diff(down_two, down, up, up_two):
    return (8.0 / 12.0) * (up - down) + (1.0 / 12.0) * (down_two - up_two)


class Halo:
    def __init__(self, cells, zst, zfl, x_below, y_below, x_above, y_above, c_below, c_above):
        self.fields, self.block, self.lanes = zst.shape
        self.st = cells.at[0 : self.fields]
        self.fl = cells.at[self.fields : self.fields + FLUID]
        self.zst, self.zfl = zst, zfl
        self.x_below, self.x_above = x_below, x_above
        self.y_below, self.y_above = y_below, y_above
        self.c_below, self.c_above = c_below, c_above
        self.cy = self.block // 4
        self.t = Tile(self.cy, self.lanes)
        self.half = self.t.rows
        self.own = self.block // self.half
        self.inner = range(1, self.own + 1)
        self.span = range(self.own + 2)
        self.edge = edge_list(x_below.shape[0])
        self.last = x_below.shape[0] - 1

    def rows_of(self, ref, q, p):
        return ref[q, (p - 1) * self.half : p * self.half, :]

    def main(self, q, p):
        if q < self.fields:
            return self.rows_of(self.st, q, p)
        return self.rows_of(self.fl, q - self.fields, p)

    def beyond(self, q, p):
        if q < self.fields:
            return self.rows_of(self.zst, q, p)
        return self.rows_of(self.zfl, q - self.fields, p)

    def part(self, second):
        return self.t.part_second if second else self.t.part_first

    def beside(self, q, p):
        return self.part(p == 2)(self.y_above[q], self.y_below[q])

    def third_place(self, q):
        return self.fields + FLUID + q // 2, q % 2

    def x_third(self, q, upper):
        tile, which = self.third_place(q)
        found = self.x_above[tile] if upper else self.x_below[tile]
        return self.t.swap(found) if which else found

    def y_third(self, q, p):
        t = self.t
        tile, which = self.third_place(q)
        turn_above, turn_below = ((0, 0), (-1, 1), (2, -2), (1, -1))[2 * which + p - 1]
        above, below = t.turn(self.y_above[tile], turn_above), t.turn(self.y_below[tile], turn_below)
        return jnp.where(t.slot == 2, above, below)

    def z_place(self, q):
        return 4 * self.edge.index(q) + 2

    def x_beyond(self, q, upper):
        tile = self.x_above[self.last] if upper else self.x_below[self.last]
        return self.t.spin(tile, -self.z_place(q))

    def y_beyond(self, q, p):
        return self.t.spin(self.beside(self.last, p), -self.z_place(q))

    def corner(self, q, p):
        place, turn = q, 0
        if q >= CURVED:
            n = q - self.fields
            place, turn = CURVED + n // 4, CORNER_TURNS[n % 4]
        above, below = self.t.turn(self.c_above[place], -turn), self.t.turn(self.c_below[place], -turn)
        return self.part(p > 0)(above, below)

    def corner_layers(self, p):
        place = CORNER_TILES - 1
        return self.part(p > 0)(self.c_above[place], self.c_below[place])

    def plane(self, q):
        inner = self.inner
        return (
            [self.x_below[q]] + [self.main(q, p) for p in inner] + [self.x_above[q]],
            [None] + [self.beside(q, p) for p in inner] + [None],
            [self.x_beyond(q, False)]
            + [self.beyond(q, p) for p in inner]
            + [self.x_beyond(q, True)],
            [None] + [self.y_beyond(q, p) for p in inner] + [None],
        )


def weigh(chi_face, alpha_face):
    shrink = volume_over(chi_face)
    return shrink, alpha_face / shrink


def primitives(half, spots, cons, centred, chi, alpha, batch):
    found = {}
    for start in range(0, len(spots), batch):
        group = spots[start : start + batch]

        def gather(planes):
            return jnp.concatenate([planes[k][p] for k, p in group], axis=0)

        shrink = volume_over(gather(chi))
        mag_raw = [gather(centred[i]) for i in range(3)]
        mag = [m * shrink for m in mag_raw]
        values = recover([gather(c) * shrink for c in cons], mag)
        u = values[2:5]
        factor = gather(alpha) * lax.rsqrt(1.0 + dot(u, u))
        field = [
            factor * (u[(i + 2) % 3] * mag_raw[(i + 1) % 3] - u[(i + 1) % 3] * mag_raw[(i + 2) % 3])
            for i in range(3)
        ]
        for n, spot in enumerate(group):
            found[spot] = [value[n * half : (n + 1) * half] for value in values + mag + field]
    return found


def ring_fluxes(prims, chi, alpha, normals, d, up, down):
    found = []
    for here, there in ((0, 1), (1, 0)):
        left, right = [], []
        for a, b in zip(prims[here], prims[there]):
            below = down(a, b, 1)
            middle = a - below
            left.append(below + 0.5 * limited(below - down(a, b, 2), middle))
            right.append(a - 0.5 * limited(middle, up(a, b, 1) - a))
        shrink, weight = weigh(
            0.5 * (chi[here] + down(chi[here], chi[there], 1)),
            0.5 * (alpha[here] + down(alpha[here], alpha[there], 1)),
        )
        found.append(face_flux(left, right, normals[here] * shrink, weight, d))
    return [a - up(a, b, 1) for a, b in zip(*found)]


def early_kernel(
    cells, zst, zfl, x_below, y_below, x_above, y_above,
    st_rate, hydro_rate, slopes, electric, pairs, sides, thirds, pairs_z, sides_z, grads, seconds, damped, tensors,
):
    halo = Halo(cells, zst, zfl, x_below, y_below, x_above, y_above, None, None)
    t, fields, half, own, cy = halo.t, halo.fields, halo.half, halo.own, halo.cy
    st, fl, inner = halo.st, halo.fl, halo.inner

    for q in range(fields):
        pairs[q, 0] = halo.x_third(q, False)
        pairs[q, 1] = x_below[q]
        for p in inner:
            pairs[q, 1 + p] = halo.main(q, p)
            sides[q, p - 1] = halo.beside(q, p)
            thirds[q, p - 1] = halo.y_third(q, p)
        pairs[q, 2 + own] = x_above[q]
        pairs[q, 3 + own] = halo.x_third(q, True)
        if q < CURVED:
            pairs_z[q, 0] = halo.x_beyond(q, False)
            pairs_z[q, own + 1] = halo.x_beyond(q, True)
            for p in inner:
                pairs_z[q, p] = halo.beyond(q, p)
                sides_z[q, p - 1] = halo.y_beyond(q, p)

    span = halo.span
    face = [halo.plane(fields + 5 + i) for i in range(3)]

    def halves(kind, p):
        own_x, own_y, own_z = (f[kind][p] for f in face)
        pair = kind in (0, 2)
        known_x = pair or p < own
        last = kind == 0 and p == own + 1
        if pair:
            next_x = halo.x_third(fields, True) if last else face[0][kind][min(p + 1, own + 1)]
            next_x = t.odd(own_x, next_x)
        else:
            next_x = t.odd_swapped(own_x, face[0][kind][p + 1] if known_x else own_x)
        dx = 0.5 * (next_x - own_x)
        dz = 0.5 * (t.z_up(own_z, face[2][kind ^ 2][p], 1) - own_z)
        inside = 1 <= p <= own
        if not pair:
            here = jnp.where(t.slot == 2, halo.y_third(fields, p), own_y) if kind == 1 else own_y
            next_y = t.y_up(here, face[1][kind ^ 1][p], 1)
        else:
            next_y = t.y_up(own_y, face[1][kind ^ 1][p] if inside else own_y, 1)
        dy = 0.5 * (next_y - own_y)
        if pair and not inside:
            dy = jnp.where(t.slot == cy - 1, -(dx + dz), dy)
        if not pair and not known_x:
            dx = jnp.where(t.row < cy, -(dy + dz), dx)
        return own_x + dx, own_y + dy, own_z + dz

    spots = [(0, p) for p in span] + [(1, p) for p in inner]
    spots += [(2, p) for p in span] + [(3, p) for p in inner]
    centred = [[[None] * (own + 2) for _ in range(4)] for _ in range(3)]
    for k, p in spots:
        for i, value in enumerate(halves(k, p)):
            centred[i][k][p] = value
    chi, alpha = halo.plane(0), halo.plane(7)
    found = primitives(
        half, spots, [halo.plane(fields + q) for q in range(5)], centred, chi, alpha, BATCH
    )

    lines = [[found[0, p][i] for p in span] for i in range(8)] + [chi[0], alpha[0]]
    odd_lines = [[t.odd(f[p], f[min(p + 1, own + 1)]) for p in span] for f in lines]
    fluxes = [None]
    for p in range(1, own + 2):
        left, right = [], []
        for f, o in zip(lines[:8], odd_lines):
            here = f[p] - o[p - 1]
            left.append(o[p - 1] + 0.5 * limited(o[p - 1] - f[p - 1], here))
            right.append(f[p] - 0.5 * limited(here, o[p] - f[p]))
        shrink, weight = weigh(
            0.5 * (lines[8][p] + odd_lines[8][p - 1]), 0.5 * (lines[9][p] + odd_lines[9][p - 1])
        )
        fluxes.append(face_flux(left, right, face[0][0][p] * shrink, weight, 0))
    for p in inner:
        changes = [
            ring_fluxes(
                [found[k, p][:8] for k in (0, kind)],
                [chi[k][p] for k in (0, kind)],
                [alpha[k][p] for k in (0, kind)],
                [face[d][k][p] for k in (0, kind)],
                d,
                up,
                down,
            )
            for d, kind, up, down in ((1, 1, t.y_up, t.y_down), (2, 2, t.z_up, t.z_down))
        ]
        for q in range(5):
            change = fluxes[p][q] - t.odd(fluxes[p][q], fluxes[p + 1][q])
            tensors[p - 1, 6 + q] = change + changes[0][q] + changes[1][q]
        rest, pressure = found[0, p][:2]
        u = found[0, p][2:5]
        parts = stress_parts(rest, pressure, u, found[0, p][5:8])
        lorentz_sq, over, over_sq, time_b, grown_b, b_square, enthalpy, inertia = parts
        total_pressure = pressure + 0.5 * b_square
        for s, (i, j) in enumerate(INDEX_PAIRS):
            value = inertia * u[i] * u[j] - over_sq * (grown_b[i] * grown_b[j])
            tensors[p - 1, s] = value + total_pressure if i == j else value

    ex, ey, ez = (
        [[found[k, p][8 + i] if (k, p) in found else None for p in span] for k in range(4)]
        for i in range(3)
    )
    ey_x = [
        [ey[k][p] + t.odd(ey[k][p - 1], ey[k][p]) if p else None for p in span] for k in (0, 2)
    ]
    edge_y = [None] + [ey_x[0][p] + t.z_down(ey_x[0][p], ey_x[1][p], 1) for p in span[1:]]
    for p in span[1:]:
        electric[p - 1] = ez[0][p] + t.odd(ez[0][p - 1], ez[0][p])
    for p in inner:
        electric[own + p] = ez[1][p]
        edge_y_z = ey_x[1][p] + t.z_down(ey_x[1][p], ey_x[0][p], 1)
        ex_y = ex[0][p] + t.y_down(ex[0][p], ex[1][p], 1)
        ex_y_h = ex[1][p] + t.y_down(ex[1][p], ex[0][p], 1)
        ex_y_z = ex[2][p] + t.y_down(ex[2][p], ex[3][p], 1)
        ex_y_hz = ex[3][p] + t.y_down(ex[3][p], ex[2][p], 1)
        edge_x = ex_y + t.z_down(ex_y, ex_y_z, 1)
        edge_x_h = ex_y_h + t.z_down(ex_y_h, ex_y_hz, 1)
        edge_x_z = ex_y_z + t.z_down(ex_y_z, ex_y, 1)
        place = slice((p - 1) * half, p * half)
        hydro_rate[5, place, :] = t.z_up(edge_y[p], edge_y_z, 1) - edge_y[p]
        hydro_rate[6, place, :] = edge_x - t.z_up(edge_x, edge_x_z, 1)
        hydro_rate[7, place, :] = (t.y_up(edge_x, edge_x_h, 1) - edge_x) - (
            t.odd(edge_y[p], edge_y[p + 1]) - edge_y[p]
        )

    def pair_step(index):
        p = index + 1
        base = index * half

        for q in range(fields):
            centre = pairs[q, p + 1]
            x_m3 = t.odd(pairs[q, p - 1], pairs[q, p])
            x_m2 = pairs[q, p]
            x_m1 = t.odd(pairs[q, p], centre)
            x_p1 = t.odd(centre, pairs[q, p + 2])
            x_p2 = pairs[q, p + 2]
            x_p3 = t.odd(pairs[q, p + 2], pairs[q, p + 3])
            side, third = sides[q, index], thirds[q, index]
            y_m1, y_m2 = t.y_down(centre, side, 1), t.y_down(centre, side, 2)
            y_p1, y_p2 = t.y_up(centre, side, 1), t.y_up(centre, side, 2)
            y_m3 = t.turn(
                jnp.where(t.slot >= cy - 2, side, jnp.where(t.slot == cy - 3, third, centre)), 3
            )
            y_p3 = t.turn(jnp.where(t.slot < 2, side, jnp.where(t.slot == 2, third, centre)), -3)
            beyond = zst[q, pl.ds(base, half), :]
            z_m1, z_m2, z_m3 = (t.z_down(centre, beyond, k) for k in (1, 2, 3))
            z_p1, z_p2, z_p3 = (t.z_up(centre, beyond, k) for k in (1, 2, 3))
            dx = first_diff(x_m2, x_m1, x_p1, x_p2)
            dy = first_diff(y_m2, y_m1, y_p1, y_p2)
            grads[q, 0] = dx
            if q < CURVED:
                slopes[q, index] = dx
            grads[q, 1] = dy
            grads[q, 2] = first_diff(z_m2, z_m1, z_p1, z_p2)
            near = [x_m1 + x_p1, y_m1 + y_p1, z_m1 + z_p1]
            far = [x_m2 + x_p2, y_m2 + y_p2, z_m2 + z_p2]
            outer = (x_m3 + x_p3) + (y_m3 + y_p3) + (z_m3 + z_p3)
            damped[q] = (DISSIPATION / 64.0) * (
                outer - 6.0 * (far[0] + far[1] + far[2]) + 15.0 * (near[0] + near[1] + near[2])
                - 60.0 * centre
            )
            if q < CURVED:
                for s, d in ((0, 0), (3, 1), (5, 2)):
                    seconds[q, s] = (1.0 / 12.0) * (16.0 * near[d] - far[d] - 30.0 * centre)
                b_m, b_c, b_p = pairs_z[q, p - 1], pairs_z[q, p], pairs_z[q, p + 1]
                dx_z = first_diff(b_m, t.odd(b_m, b_c), t.odd(b_c, b_p), b_p)
                b_s = sides_z[q, p - 1]
                dy_z = first_diff(
                    t.y_down(b_c, b_s, 2),
                    t.y_down(b_c, b_s, 1),
                    t.y_up(b_c, b_s, 1),
                    t.y_up(b_c, b_s, 2),
                )
                for s, inside, outside in ((2, dx, dx_z), (4, dy, dy_z)):
                    seconds[q, s] = first_diff(
                        t.z_down(inside, outside, 2),
                        t.z_down(inside, outside, 1),
                        t.z_up(inside, outside, 1),
                        t.z_up(inside, outside, 2),
                    )

        def value(q):
            return pairs[q, p + 1]

        def fluid_value(q):
            return fl[q, pl.ds(base, half), :]

        conformal, lapse = value(0), value(7)
        over_chi = 1.0 / conformal
        metric = symmetric([value(1 + s) for s in range(6)])
        shift = [value(8 + i) for i in range(3)]
        extrinsic, theta = value(11), value(21)
        traceless = symmetric([value(12 + s) for s in range(6)])
        connection = [value(18 + i) for i in range(3)]
        inverse = inverse_metric(metric)
        grad = [[grads[q, k] for k in range(3)] for q in range(fields)]
        chi_grad, lapse_grad = grad[0], grad[7]
        shift_grad = [[grad[8 + i][k] for i in range(3)] for k in range(3)]
        trace_k = extrinsic + 2.0 * theta

        stress = symmetric([tensors[p - 1, s] for s in range(6)])
        held = [fluid_value(q) for q in range(5)]
        shrink = volume_over(conformal)
        energy = held[4] + held[0]
        third_k = trace_k * (1.0 / 3.0)
        curved = [
            [
                (traceless[i][j] + metric[i][j] * third_k) if i <= j else None for j in range(3)
            ]
            for i in range(3)
        ]
        work = (
            stress[0][0] * curved[0][0]
            + stress[1][1] * curved[1][1]
            + stress[2][2] * curved[2][2]
            + 2.0
            * (
                stress[0][1] * curved[0][1]
                + stress[0][2] * curved[0][2]
                + stress[1][2] * curved[1][2]
            )
        )
        rates = [tensors[p - 1, 6 + q] for q in range(5)]
        for i in range(3):
            rates[1 + i] = (
                rates[1 + i]
                - energy * lapse_grad[i]
                + total([held[1 + k] * grad[8 + k][i] for k in range(3)])
            )
        rates[4] = (
            rates[4] + lapse * work * over_chi / shrink - dot(held[1:4], lapse_grad)
        )
        for q in range(5):
            hydro_rate[q, pl.ds(base, half), :] = rates[q]
        density = energy * shrink
        momentum = [held[1 + i] * shrink for i in range(3)]

        lowered = [[[None] * 3 for _ in range(3)] for _ in range(3)]
        for i in range(3):
            for j in range(3):
                for k in range(j, 3):
                    got = 0.5 * (
                        grad[1 + slot_of(i, k)][j]
                        + grad[1 + slot_of(i, j)][k]
                        - grad[1 + slot_of(j, k)][i]
                    )
                    lowered[i][j][k] = lowered[i][k][j] = got
        raised = [[[None] * 3 for _ in range(3)] for _ in range(3)]
        for i in range(3):
            for j in range(3):
                for k in range(j, 3):
                    got = total([inverse[i][l] * lowered[l][j][k] for l in range(3)])
                    raised[i][j][k] = raised[i][k][j] = got
        contracted = [trace_with(inverse, raised[i]) for i in range(3)]

        def hessian_trace(q):
            return (
                inverse[0][0] * seconds[q, 0]
                + inverse[1][1] * seconds[q, 3]
                + inverse[2][2] * seconds[q, 5]
                + 2.0 * (inverse[0][2] * seconds[q, 2] + inverse[1][2] * seconds[q, 4])
            )

        def second_cov(q, slope):
            bent = [total([raised[k][i][j] * slope[k] for k in range(3)]) for i, j in INDEX_PAIRS]
            return symmetric(
                [-bent[s] if s == 1 else seconds[q, s] - bent[s] for s in range(len(bent))]
            )

        chi_cov = second_cov(0, chi_grad)
        chi_lap = trace_with(inverse, chi_cov)
        raised_chi = [dot(inverse[i], chi_grad) for i in range(3)]
        chi_square = dot(raised_chi, chi_grad)
        cross_term = dot(raised_chi, lapse_grad)
        half_chi = 0.5 * over_chi
        plain_cov = second_cov(7, lapse_grad)
        lapse_cov = symmetric(
            [
                plain_cov[i][j]
                + (
                    chi_grad[i] * lapse_grad[j]
                    + chi_grad[j] * lapse_grad[i]
                    - metric[i][j] * cross_term
                )
                * half_chi
                for i, j in INDEX_PAIRS
            ]
        )
        lapse_lap = conformal * trace_with(inverse, lapse_cov)

        mixed = [
            [[dot(inverse[l], lowered[k][j]) for j in range(3)] for k in range(3)]
            for l in range(3)
        ]
        quarter_sq = half_chi * half_chi
        metric_factor = chi_lap * half_chi - 3.0 * chi_square * quarter_sq
        ricci = []
        for i, j in INDEX_PAIRS:
            second_part = -0.5 * hessian_trace(1 + slot_of(i, j))
            connection_part = 0.5 * total(
                [metric[k][i] * grad[18 + k][j] + metric[k][j] * grad[18 + k][i] for k in range(3)]
            )
            contracted_part = 0.5 * total(
                [contracted[k] * (lowered[i][j][k] + lowered[j][i][k]) for k in range(3)]
            )
            if i == j:
                quadratic = total(
                    [
                        raised[k][l][i] * (2.0 * mixed[l][i][k] + mixed[l][k][i])
                        for k in range(3)
                        for l in range(3)
                    ]
                )
            else:
                quadratic = total(
                    [
                        raised[k][l][i] * (mixed[l][j][k] + mixed[l][k][j])
                        + raised[k][l][j] * mixed[l][i][k]
                        for k in range(3)
                        for l in range(3)
                    ]
                )
            conformal_part = (
                chi_cov[i][j] * half_chi
                + metric[i][j] * metric_factor
                - chi_grad[i] * chi_grad[j] * quarter_sq
            )
            ricci.append(
                second_part + connection_part + contracted_part + quadratic + conformal_part
            )
        ricci = symmetric(ricci)
        ricci_scalar = conformal * trace_with(inverse, ricci)
        stress_trace = conformal * trace_with(inverse, stress)

        up_a = [
            [total([inverse[i][k] * traceless[k][j] for k in range(3)]) for j in range(3)]
            for i in range(3)
        ]
        raised_a = symmetric(
            [total([up_a[i][l] * inverse[j][l] for l in range(3)]) for i, j in INDEX_PAIRS]
        )
        a_square = trace_with(traceless, raised_a)
        shift_div = shift_grad[0][0] + shift_grad[1][1] + shift_grad[2][2]
        two_thirds_div = (2.0 / 3.0) * shift_div

        def finish(q, rate):
            rate = rate + dot(shift, grad[q]) + damped[q]
            st_rate[q, pl.ds(base, half), :] = rate

        finish(0, (2.0 / 3.0) * conformal * (lapse * trace_k - shift_div))
        finish(7, -2.0 * lapse * extrinsic)
        for i in range(3):
            finish(8 + i, 0.75 * connection[i] - SHIFT_DAMPING * shift[i])
        finish(
            11,
            lapse
            * (
                a_square
                + trace_k * trace_k * (1.0 / 3.0)
                + FOUR_PI * (stress_trace + density)
                + KAPPA_ONE * theta
            )
            - lapse_lap,
        )
        source = symmetric(
            [
                lapse * (ricci[i][j] - 2.0 * FOUR_PI * stress[i][j]) - lapse_cov[i][j]
                for i, j in INDEX_PAIRS
            ]
        )
        third_trace = trace_with(inverse, source) * (1.0 / 3.0)
        for s, (i, j) in enumerate(INDEX_PAIRS):
            finish(
                1 + s,
                total(
                    [
                        metric[i][k] * shift_grad[j][k] + metric[j][k] * shift_grad[i][k]
                        for k in range(3)
                    ]
                )
                - metric[i][j] * two_thirds_div
                - 2.0 * lapse * traceless[i][j],
            )
            product = total([traceless[i][k] * up_a[k][j] for k in range(3)])
            finish(
                12 + s,
                total(
                    [
                        traceless[i][k] * shift_grad[j][k] + traceless[j][k] * shift_grad[i][k]
                        for k in range(3)
                    ]
                )
                - traceless[i][j] * two_thirds_div
                + conformal * (source[i][j] - metric[i][j] * third_trace)
                + lapse * (trace_k * traceless[i][j] - 2.0 * product),
            )
        for i in range(3):
            bracket = (
                trace_with(raised_a, raised[i])
                - 1.5 * dot(raised_a[i], chi_grad) * over_chi
                - dot(inverse[i], [2.0 * grad[11][j] + grad[21][j] for j in range(3)]) * (1.0 / 3.0)
                - 2.0 * FOUR_PI * dot(inverse[i], momentum)
            )
            spread = [
                seconds[8, 0] + seconds[10, 2],
                seconds[9, 3] + seconds[10, 4],
                seconds[8, 2] + seconds[9, 4] + seconds[10, 5],
            ]
            finish(
                18 + i,
                contracted[i] * two_thirds_div
                - total([contracted[j] * shift_grad[j][i] for j in range(3)])
                + hessian_trace(8 + i)
                + dot(inverse[i], spread) * (1.0 / 3.0)
                - 2.0 * dot(raised_a[i], lapse_grad)
                + 2.0
                * lapse
                * (bracket - KAPPA_ONE * (connection[i] - contracted[i])),
            )
        finish(
            21,
            0.5
            * lapse
            * (
                ricci_scalar
                - a_square
                + (2.0 / 3.0) * trace_k * trace_k
                - 4.0 * FOUR_PI * density
            )
            - 2.0 * KAPPA_ONE * lapse * theta,
        )

    for index in range(own):
        pair_step(index)


def late_kernel(
    cells, zst, zfl, x_below, y_below, x_above, y_above, c_below, c_above, tops,
    st_rate, hydro_rate, slopes, electric, st_out, fl_out,
):
    halo = Halo(cells, zst, zfl, x_below, y_below, x_above, y_above, c_below, c_above)
    t, fields, half, own = halo.t, halo.fields, halo.half, halo.own
    inner, span = halo.inner, halo.span

    dt = COURANT / jnp.max(tops[...], axis=0, keepdims=True)

    for p in inner:
        place = slice((p - 1) * half, p * half)
        mixed = []
        for q in range(CURVED):
            s_m, s_c, s_p = (
                halo.beside(q, n) if 1 <= n <= own else halo.corner(q, n) for n in (p - 1, p, p + 1)
            )
            slope = slopes[q, p - 1]
            slope_side = first_diff(s_m, t.odd_swapped(s_m, s_c), t.odd_swapped(s_c, s_p), s_p)
            mixed.append(
                first_diff(
                    t.y_down(slope, slope_side, 2),
                    t.y_down(slope, slope_side, 1),
                    t.y_up(slope, slope_side, 1),
                    t.y_up(slope, slope_side, 2),
                )
            )
        conformal, lapse = halo.main(0, p), halo.main(7, p)
        metric = [halo.main(1 + s, p) for s in range(6)]
        inverse = inverse_metric(symmetric(metric))
        half_chi = 0.5 / conformal
        cross = inverse[0][1]
        chi_trace = 2.0 * cross * mixed[0] * half_chi
        ricci = [metric[s] * chi_trace - cross * mixed[1 + s] for s in range(6)]
        ricci[1] = ricci[1] + mixed[0] * half_chi
        source = [lapse * r for r in ricci]
        source[1] = source[1] - mixed[7]
        third_trace = trace_with(inverse, symmetric(source)) * (1.0 / 3.0)
        extra = {
            11: -2.0 * conformal * cross * mixed[7],
            21: 0.5 * lapse * conformal * trace_with(inverse, symmetric(ricci)),
        }
        for s in range(6):
            extra[12 + s] = conformal * (source[s] - metric[s] * third_trace)
        for i in range(3):
            extra[18 + i] = 2.0 * cross * mixed[8 + i] + (1.0 / 3.0) * (
                inverse[i][0] * mixed[9] + inverse[i][1] * mixed[8]
            )
        for q in range(fields):
            rate = st_rate[q, place, :]
            if q in extra:
                rate = rate + extra[q]
            st_out[q, place, :] = halo.main(q, p) + dt * rate

    end = own + 1
    ends = (0, end)
    bx_face, by_face, bz_face = ({p: halo.corner(fields + 5 + i, p) for p in ends} for i in range(3))
    layers = {p: halo.corner_layers(p) for p in ends}
    bx_face[end] = layers[end]
    by_face[0] = jnp.where(t.slot < 2, layers[0], by_face[0])
    centred = [{}, {}, {}]
    for p in ends:
        following = halo.beside(fields + 5, 1) if p == 0 else bx_face[p]
        edge_cells = x_below if p == 0 else x_above
        dx = 0.5 * (t.odd_swapped(bx_face[p], following) - bx_face[p])
        dy = 0.5 * (t.y_up(by_face[p], edge_cells[fields + 6], 1) - by_face[p])
        centred[0][p] = bx_face[p] + dx
        centred[1][p] = by_face[p] + dy
        centred[2][p] = bz_face[p] - (dx + dy)
    corners = [{p: halo.corner(q, p) for p in ends} for q in [0, 7] + list(range(fields, fields + 5))]
    found = primitives(
        half, [(0, p) for p in ends], [[c] for c in corners[2:]], [[c] for c in centred],
        [corners[0]], [corners[1]], 2,
    )
    ez_h = [found[0, 0][10]] + [electric[own + p] for p in inner] + [found[0, end][10]]
    ez_x_h = [None] + [ez_h[p] + t.odd_swapped(ez_h[p - 1], ez_h[p]) for p in span[1:]]
    ez_x = [None] + [electric[p - 1] for p in span[1:]]
    edge_z = [None] + [ez_x[p] + t.y_down(ez_x[p], ez_x_h[p], 1) for p in span[1:]]
    quarter = 0.25 * dt
    for p in inner:
        place = slice((p - 1) * half, p * half)
        edge_z_h = ez_x_h[p] + t.y_down(ez_x_h[p], ez_x[p], 1)
        for q in range(5):
            fl_out[q, place, :] = halo.main(fields + q, p) + dt * hydro_rate[q, place, :]
        x_rate = hydro_rate[5, place, :] - (t.y_up(edge_z[p], edge_z_h, 1) - edge_z[p])
        y_rate = hydro_rate[6, place, :] + (t.odd(edge_z[p], edge_z[p + 1]) - edge_z[p])
        z_rate = hydro_rate[7, place, :]
        for i, rate in enumerate((x_rate, y_rate, z_rate)):
            fl_out[5 + i, place, :] = halo.main(fields + 5 + i, p) + quarter * rate


def per_device(spacetime, fluid):
    fields, cx, cy, cz = spacetime.shape
    rows = cx * cy
    st = spacetime.reshape(fields, rows, cz)
    fl = fluid.reshape(FLUID, rows, cz)
    sizes = [lax.axis_size(a) for a in ("gx", "gy", "gz")]
    tile = (2 * cy, cz)
    f32 = jnp.float32

    def shape(*dims):
        return jax.ShapeDtypeStruct(dims, f32)

    def beyond(cells):
        n = sizes[2]
        after = lax.ppermute(cells, "gz", [((i + 1) % n, i) for i in range(n)])
        if n == 2:
            return after
        before = lax.ppermute(cells, "gz", [(i, (i + 1) % n) for i in range(n)])
        lane = lax.broadcasted_iota(jnp.int32, cells.shape, 2)
        return jnp.where(lane < cz // 2, after, before)

    params = pltpu.CompilerParams(vmem_limit_bytes=48 * 1024 * 1024)
    zst, zfl = beyond(st), beyond(fl)
    cells = jnp.concatenate([st, fl], axis=0)
    face = shape(face_tiles(fields), *tile)
    corner = shape(CORNER_TILES, *tile)
    top = pl.pallas_call(
        speed_kernel, out_shape=shape(*tile), compiler_params=params, name="speed"
    )(cells)
    tops = lax.all_gather(top, ("gx", "gy", "gz"), axis=0, tiled=True)
    x_low, x_high, y_low, y_high = pl.pallas_call(
        pack_kernel, out_shape=[face] * 4, compiler_params=params, name="pack"
    )(cells, zst, zfl)

    def move(cells, dx, dy):
        nx, ny = sizes[0], sizes[1]
        hops = [
            (i * ny + j, ((i + dx) % nx) * ny + (j + dy) % ny) for i in range(nx) for j in range(ny)
        ]
        return lax.ppermute(cells, ("gx", "gy"), hops)

    x_below = move(x_high, 1, 0)
    y_below = move(y_high, 0, 1)
    x_above = move(x_low, -1, 0)
    y_above = move(y_low, 0, -1)
    c_low, c_high = pl.pallas_call(
        relay_kernel, out_shape=[corner] * 2, compiler_params=params, name="relay"
    )(x_below, x_above)
    c_above = move(c_low, 0, -1)
    c_below = move(c_high, 0, 1)
    own = cx // 2
    arrived = (cells, zst, zfl, x_below, y_below, x_above, y_above)
    early = pl.pallas_call(
        early_kernel,
        out_shape=[
            shape(*st.shape),
            shape(FLUID, rows, cz),
            shape(CURVED, own, *tile),
            shape(2 * own + 1, *tile),
        ],
        scratch_shapes=[
            pltpu.VMEM((fields, own + 4) + tile, f32),
            pltpu.VMEM((fields, own) + tile, f32),
            pltpu.VMEM((fields, own) + tile, f32),
            pltpu.VMEM((CURVED, own + 2) + tile, f32),
            pltpu.VMEM((CURVED, own) + tile, f32),
            pltpu.VMEM((fields, 3) + tile, f32),
            pltpu.VMEM((CURVED, 6) + tile, f32),
            pltpu.VMEM((fields,) + tile, f32),
            pltpu.VMEM((own, 11) + tile, f32),
        ],
        compiler_params=params,
        name="early",
    )(*arrived)
    st_next, fl_next = pl.pallas_call(
        late_kernel,
        out_shape=[shape(*st.shape), shape(*fl.shape)],
        compiler_params=params,
        name="late",
    )(*arrived, c_below, c_above, tops, *early)
    return st_next.reshape(spacetime.shape), fl_next.reshape(fluid.shape)


def solution(mesh):
    spec = P(None, "gx", "gy", "gz")
    return jax.shard_map(
        per_device, mesh=mesh, in_specs=(spec, spec), out_specs=(spec, spec), check_vma=False
    )
```

```python
import functools
import math

import jax
import jax.numpy as jnp
from jax import lax
from jax.experimental import pallas as pl
from jax.experimental.pallas import tpu as pltpu
from jax.sharding import PartitionSpec as P

RECOVERY_STEPS = 4
INDEX_PAIRS = ((0, 0), (0, 1), (0, 2), (1, 1), (1, 2), (2, 2))
COURANT = 0.25
DISSIPATION = 0.2
KAPPA_ONE = 0.02
SHIFT_DAMPING = 1.0
SPEED_CAP = 0.99
PRESSURE_FLOOR = 0.01
FOUR_PI = 4.0 * math.pi

BATCH = 6
CURVED = 11
FLUID = 8


def total(pieces):
    summed = pieces[0]
    for member in pieces[1:]:
        summed = summed + member
    return summed


def dot(first_vec, second_vec):
    return total([first_vec[i] * second_vec[i] for i in range(3)])


def slot_of(i, j):
    return INDEX_PAIRS.index((min(i, j), max(i, j)))


def symmetric(entries):
    return [[entries[slot_of(i, j)] for j in range(3)] for i in range(3)]


def trace_with(inverse, tensor):
    return (
        inverse[0][0] * tensor[0][0]
        + inverse[1][1] * tensor[1][1]
        + inverse[2][2] * tensor[2][2]
        + 2.0
        * (
            inverse[0][1] * tensor[0][1]
            + inverse[0][2] * tensor[0][2]
            + inverse[1][2] * tensor[1][2]
        )
    )


def inverse_metric(metric):
    cofactor = [
        metric[1][1] * metric[2][2] - metric[1][2] * metric[1][2],
        metric[0][2] * metric[1][2] - metric[0][1] * metric[2][2],
        metric[0][1] * metric[1][2] - metric[0][2] * metric[1][1],
        metric[0][0] * metric[2][2] - metric[0][2] * metric[0][2],
        metric[0][1] * metric[0][2] - metric[0][0] * metric[1][2],
        metric[0][0] * metric[1][1] - metric[0][1] * metric[0][1],
    ]
    determinant = (
        metric[0][0] * cofactor[0] + metric[0][1] * cofactor[1] + metric[0][2] * cofactor[2]
    )
    over = 1.0 / determinant
    return symmetric([c * over for c in cofactor])


class Tile:
    def __init__(self, cy, cz):
        self.cy, self.rows, self.lanes = cy, 2 * cy, cz
        shape = (self.rows, cz)
        self.row = lax.broadcasted_iota(jnp.int32, shape, 0)
        self.lane = lax.broadcasted_iota(jnp.int32, shape, 1)
        self.slot = lax.rem(self.row, cy)

    def turn(self, tile, amount):
        amount = amount % self.rows
        return tile if amount == 0 else pltpu.roll(tile, amount, 0)

    def spin(self, tile, amount):
        amount = amount % self.lanes
        return tile if amount == 0 else pltpu.roll(tile, amount, 1)

    def swap(self, tile):
        return self.turn(tile, self.cy)

    def odd(self, a, b):
        return self.turn(jnp.where(self.row < self.cy, b, a), self.cy)

    def odd_swapped(self, a, b):
        return self.turn(jnp.where(self.row < self.cy, a, b), self.cy)

    def y_up(self, main, beyond, k):
        return self.turn(jnp.where(self.slot < k, beyond, main), -k)

    def y_down(self, main, beyond, k):
        return self.turn(jnp.where(self.slot >= self.cy - k, beyond, main), k)

    def z_up(self, main, beyond, k):
        return self.spin(jnp.where(self.lane < k, beyond, main), -k)

    def z_down(self, main, beyond, k):
        return self.spin(jnp.where(self.lane >= self.lanes - k, beyond, main), k)

    def corner_rows(self, side, turn):
        places = ((0, 2), (self.cy - 1, self.cy + 1))[side]
        first, second = [(place + turn) % self.rows for place in places]
        return (self.row == first) | (self.row == second)

    def join_low(self, u, v):
        return jnp.where(self.slot < 2, self.swap(u), self.turn(v, 2))

    def join_high(self, u, v):
        return jnp.where(self.slot >= self.cy - 2, self.swap(u), self.turn(self.swap(v), -2))

    def part_first(self, from_above, from_below):
        return jnp.where(self.slot < 2, from_above, from_below)

    def part_second(self, from_above, from_below):
        return self.turn(jnp.where(self.slot < 2, from_below, from_above), 2)


def edge_list(tiles):
    fields = next(n for n in range(tiles) if face_tiles(n) == tiles)
    return list(range(CURVED)) + list(range(fields, fields + FLUID))


CORNER_TURNS = (0, 1, 4, 5)
CORNER_TILES = CURVED + FLUID // 4 + 1
TOP_ROW = 6


class SplitFace:
    def __init__(self, near, rest):
        count = near.shape[0] + rest.shape[0]
        self.shape = (count,) + tuple(near.shape[1:])
        first = edge_list(count) + [count - 1]
        second = [q for q in range(count) if q not in first]
        self.places = {q: (near, n) for n, q in enumerate(first)}
        self.places.update({q: (rest, n) for n, q in enumerate(second)})

    def __getitem__(self, key):
        q, rows = (key[0], key[1:]) if isinstance(key, tuple) else (key, ())
        ref, n = self.places[q]
        return ref[(n,) + rows]

    def __setitem__(self, q, tile):
        ref, n = self.places[q]
        ref[n] = tile


def face_tiles(fields):
    return fields + FLUID + len(pairs_of(third_list(fields))) + 1


def third_list(fields):
    return list(range(fields + 1))


def pairs_of(items):
    return [(items[i], items[min(i + 1, len(items) - 1)]) for i in range(0, len(items), 2)]


def top_speed(st):
    inverse = inverse_metric(symmetric([st[1 + s] for s in range(6)]))
    scale = 2.0 * st[7] * st[0]
    speeds = [jnp.abs(st[8 + d]) + jnp.sqrt(scale * inverse[d][d]) for d in range(3)]
    top = jnp.maximum(jnp.maximum(speeds[0], speeds[1]), speeds[2])
    return jnp.max(jnp.max(top, axis=1, keepdims=True), axis=0, keepdims=True)


def speed_kernel(cells, zst, out):
    top = jnp.maximum(top_speed(cells), top_speed(zst))
    out[...] = jnp.broadcast_to(top, out.shape)


def face_parts(cells, zst, zfl):
    fields, rows, lanes = zst.shape
    t = Tile(rows // 4, lanes)
    half = t.rows

    def own(ref, q):
        return [ref[q, 0:half, :], ref[q, half : 2 * half, :]]

    tiles = [own(cells, q) for q in range(fields + FLUID)]
    beyond = {q: own(zst, q) for q in range(CURVED)}
    beyond.update({fields + q: own(zfl, q) for q in range(FLUID)})
    third_x = pairs_of([tiles[q] for q in range(fields)] + [tiles[fields + 5]])
    third_y = pairs_of([tiles[q] for q in range(fields)] + [tiles[fields + 6]])
    return t, tiles, beyond, third_x, third_y


def z_lanes(t, pieces, top):
    packed = t.spin(pieces[0], 2)
    for place in range(1, len(pieces)):
        packed = jnp.where(t.lane < 4 * place, packed, t.spin(pieces[place], 4 * place + 2))
    return jnp.where(t.lane < 4 * len(pieces), packed, top)


def pack_up_kernel(cells, zst, zfl, top, x_high_near, y_high):
    t, tiles, beyond, _, third_y = face_parts(cells, zst, zfl)
    for n, q in enumerate(beyond):
        x_high_near[n] = tiles[q][1]
    for q, (first, second) in enumerate(tiles):
        y_high[q] = t.join_high(first, second)
    s = t.slot
    for n, (a, b) in enumerate(third_y):
        w = [t.swap(a[0]), t.swap(a[1]), t.swap(b[0]), t.swap(b[1])]
        y_high[len(tiles) + n] = jnp.where(
            s == 1,
            w[0],
            jnp.where(s == 0, t.turn(w[1], -1), jnp.where(s == 3, t.turn(w[2], 2), t.turn(w[3], 1))),
        )
    found = beyond.values()
    x_high_near[len(found)] = z_lanes(t, [second for _, second in found], top[...])
    y_high[y_high.shape[0] - 1] = z_lanes(t, [t.join_high(*pair) for pair in found], top[...])


def pack_down_kernel(cells, zst, zfl, top, top_two, x_low_near, y_low, x_low_rest, x_high_rest):
    t, tiles, beyond, third_x, third_y = face_parts(cells, zst, zfl)
    top = jnp.maximum(top[...], top_two[...])
    for n, q in enumerate(beyond):
        x_low_near[n] = tiles[q][0]
    rest = [q for q in range(len(tiles)) if q not in beyond]
    for n, q in enumerate(rest):
        x_low_rest[n] = tiles[q][0]
        x_high_rest[n] = tiles[q][1]
    for q, (first, second) in enumerate(tiles):
        y_low[q] = t.join_low(first, second)
    for n, (a, b) in enumerate(third_x):
        x_low_rest[len(rest) + n] = jnp.where(t.row < t.cy, a[1], t.swap(b[1]))
        x_high_rest[len(rest) + n] = jnp.where(t.row < t.cy, t.swap(b[0]), a[0])
    s = t.slot
    for n, (a, b) in enumerate(third_y):
        w = [t.swap(a[0]), t.swap(a[1]), t.swap(b[0]), t.swap(b[1])]
        y_low[len(tiles) + n] = jnp.where(
            s == 2,
            w[0],
            jnp.where(s == 3, t.turn(w[1], 1), jnp.where(s == 0, t.turn(w[2], -2), t.turn(w[3], -1))),
        )
    found = beyond.values()
    x_low_near[len(found)] = z_lanes(t, [first for first, _ in found], top)
    y_low[y_low.shape[0] - 1] = z_lanes(t, [t.join_low(*pair) for pair in found], top)


def relay_kernel(x_below, x_above, y_below, top, top_two, to_low, to_high, line_top):
    cy, lanes = x_below.shape[1] // 2, x_below.shape[2]
    t = Tile(cy, lanes)
    line = jnp.maximum(top[...], top_two[...])
    for beside in (x_below, x_above, y_below):
        end = beside.shape[0] - 1
        line = jnp.maximum(line, beside[end, 0:1, lanes - 1 : lanes])
    line_top[...] = line
    edge = list(range(x_below.shape[0] - 1))
    for q in range(CURVED):
        to_low[q] = t.join_low(x_below[q], x_above[q])
        to_high[q] = t.join_high(x_below[q], x_above[q])
    for n in range(0, FLUID, 4):
        low, high = None, None
        for turn, q in zip(CORNER_TURNS, edge[CURVED + n : CURVED + n + 4]):
            below = t.turn(t.join_low(x_below[q], x_above[q]), turn)
            above = t.turn(t.join_high(x_below[q], x_above[q]), turn)
            if low is None:
                low, high = below, above
            else:
                low = jnp.where(t.corner_rows(0, turn), below, low)
                high = jnp.where(t.corner_rows(1, turn), above, high)
        to_low[CURVED + n // 4] = low
        to_high[CURVED + n // 4] = high
    along_x, along_y = edge[CURVED + 5], edge[CURVED + 6]
    low = t.join_low(x_below[along_y], x_above[along_y])
    high = t.join_high(x_below[along_x], x_above[along_x])
    to_low[CORNER_TILES - 1] = jnp.where(t.row == TOP_ROW, line, low)
    to_high[CORNER_TILES - 1] = jnp.where(t.row == TOP_ROW, line, high)


def limited(a, b):
    return jnp.maximum(jnp.minimum(a, b), 0.0) + jnp.minimum(jnp.maximum(a, b), 0.0)


def recover(conserved, magnetic):
    density = conserved[0]
    momenta = conserved[1:4]
    energy = conserved[4] + density
    mom_sq = dot(momenta, momenta)
    mag_sq = dot(magnetic, magnetic)
    cross = dot(momenta, magnetic)
    cross_sq = cross * cross

    def state(z):
        grown = z + mag_sq
        over = 1.0 / (z * grown)
        speed_sq = (mom_sq * z * z + cross_sq * (2.0 * z + mag_sq)) * over * over
        kept = 1.0 - jnp.minimum(speed_sq, SPEED_CAP)
        rest = density * jnp.sqrt(kept)
        return kept, rest, 0.5 * (z * kept - rest), grown * over

    z = jnp.maximum(energy - 0.5 * mag_sq, density)
    for _ in range(RECOVERY_STEPS):
        kept, rest, pressure, over_z = state(z)
        residual = (
            z
            + mag_sq
            - pressure
            - 0.5 * mag_sq * kept
            - 0.5 * cross_sq * over_z * over_z
            - energy
        )
        z = jnp.maximum(z - residual / (1.0 - 0.5 * kept), density)
    kept, rest, pressure, over_z = state(z)
    pressure = jnp.maximum(pressure, PRESSURE_FLOOR * rest)
    scale = lax.rsqrt(kept) / (z + mag_sq)
    along = cross * over_z
    four_vel = [scale * (momenta[i] + along * magnetic[i]) for i in range(3)]
    return [rest, pressure] + four_vel


def stress_parts(rest, pressure, u, magnetic):
    lorentz_sq = 1.0 + dot(u, u)
    over = lax.rsqrt(lorentz_sq)
    over_sq = over * over
    time_b = dot(u, magnetic)
    grown_b = [magnetic[i] + time_b * u[i] for i in range(3)]
    b_square = (dot(magnetic, magnetic) + time_b * time_b) * over_sq
    enthalpy = rest + 2.0 * pressure
    inertia = enthalpy + b_square
    return lorentz_sq, over, over_sq, time_b, grown_b, b_square, enthalpy, inertia


def face_state(rest, pressure, u, magnetic, d):
    lorentz_sq, over, over_sq, time_b, grown_b, b_square, enthalpy, inertia = stress_parts(
        rest, pressure, u, magnetic
    )
    total_pressure = pressure + 0.5 * b_square
    lorentz = lorentz_sq * over
    density = rest * lorentz
    carried = inertia * lorentz
    time_over = time_b * over
    conserved = [density]
    conserved += [carried * u[j] - time_over * grown_b[j] for j in range(3)]
    conserved += [inertia * lorentz_sq - total_pressure - time_b * time_b - density]
    mass_flux = rest * u[d]
    flux = [mass_flux]
    pushed = inertia * u[d]
    b_over = grown_b[d] * over_sq
    for j in range(3):
        flux_j = pushed * u[j] - b_over * grown_b[j]
        flux.append(flux_j + total_pressure if j == d else flux_j)
    flux.append(carried * u[d] - time_over * grown_b[d] - mass_flux)
    ratio = 1.0 / (enthalpy * inertia)
    sound_sq = 2.0 * pressure * inertia * ratio
    alfven_sq = b_square * enthalpy * ratio
    fast_sq = sound_sq + alfven_sq - sound_sq * alfven_sq
    slow = 1.0 - fast_sq
    velocity = u[d] * over
    rest_part = 1.0 - dot(u, u) * over_sq * fast_sq
    spread = jnp.sqrt(fast_sq * over_sq * (rest_part - velocity * velocity * slow))
    fastest = (jnp.abs(velocity * slow) + spread) / rest_part
    return conserved, flux, fastest


def face_flux(left, right, normal, weight, d):
    sides = []
    for state in (left, right):
        magnetic = [normal if i == d else state[5 + i] for i in range(3)]
        sides.append(face_state(state[0], state[1], state[2:5], magnetic, d))
    (cons_l, flux_l, fast_l), (cons_r, flux_r, fast_r) = sides
    signal = jnp.maximum(fast_l, fast_r)
    scale = 0.5 * weight
    return [scale * (flux_l[q] + flux_r[q] - signal * (cons_r[q] - cons_l[q])) for q in range(5)]


def volume_over(conformal):
    return conformal * jnp.sqrt(conformal)


def first_diff(down_two, down, up, up_two):
    return (8.0 / 12.0) * (up - down) + (1.0 / 12.0) * (down_two - up_two)


class Halo:
    def __init__(
        self, cells, zst, zfl, x_below, y_below, x_above, y_above, x_below_rest, x_above_rest,
        c_below, c_above,
    ):
        x_below = SplitFace(x_below, x_below_rest)
        x_above = SplitFace(x_above, x_above_rest)
        self.fields, self.block, self.lanes = zst.shape
        self.st = cells.at[0 : self.fields]
        self.fl = cells.at[self.fields : self.fields + FLUID]
        self.zst, self.zfl = zst, zfl
        self.x_below, self.x_above = x_below, x_above
        self.y_below, self.y_above = y_below, y_above
        self.c_below, self.c_above = c_below, c_above
        self.cy = self.block // 4
        self.t = Tile(self.cy, self.lanes)
        self.half = self.t.rows
        self.own = self.block // self.half
        self.inner = range(1, self.own + 1)
        self.span = range(self.own + 2)
        self.edge = edge_list(x_below.shape[0])
        self.last = x_below.shape[0] - 1

    def rows_of(self, ref, q, p):
        return ref[q, (p - 1) * self.half : p * self.half, :]

    def main(self, q, p):
        if q < self.fields:
            return self.rows_of(self.st, q, p)
        return self.rows_of(self.fl, q - self.fields, p)

    def beyond(self, q, p):
        if q < self.fields:
            return self.rows_of(self.zst, q, p)
        return self.rows_of(self.zfl, q - self.fields, p)

    def part(self, second):
        return self.t.part_second if second else self.t.part_first

    def beside(self, q, p):
        return self.part(p == 2)(self.y_above[q], self.y_below[q])

    def third_place(self, q):
        return self.fields + FLUID + q // 2, q % 2

    def x_third(self, q, upper):
        tile, which = self.third_place(q)
        found = self.x_above[tile] if upper else self.x_below[tile]
        return self.t.swap(found) if which else found

    def y_third(self, q, p):
        t = self.t
        tile, which = self.third_place(q)
        turn_above, turn_below = ((0, 0), (-1, 1), (2, -2), (1, -1))[2 * which + p - 1]
        above, below = t.turn(self.y_above[tile], turn_above), t.turn(self.y_below[tile], turn_below)
        return jnp.where(t.slot == 2, above, below)

    def z_place(self, q):
        return 4 * self.edge.index(q) + 2

    def x_beyond(self, q, upper):
        tile = self.x_above[self.last] if upper else self.x_below[self.last]
        return self.t.spin(tile, -self.z_place(q))

    def y_beyond(self, q, p):
        return self.t.spin(self.beside(self.last, p), -self.z_place(q))

    def corner(self, q, p):
        place, turn = q, 0
        if q >= CURVED:
            n = q - self.fields
            place, turn = CURVED + n // 4, CORNER_TURNS[n % 4]
        above, below = self.t.turn(self.c_above[place], -turn), self.t.turn(self.c_below[place], -turn)
        return self.part(p > 0)(above, below)

    def corner_layers(self, p):
        place = CORNER_TILES - 1
        return self.part(p > 0)(self.c_above[place], self.c_below[place])

    def plane(self, q):
        inner = self.inner
        return (
            [self.x_below[q]] + [self.main(q, p) for p in inner] + [self.x_above[q]],
            [None] + [self.beside(q, p) for p in inner] + [None],
            [self.x_beyond(q, False)]
            + [self.beyond(q, p) for p in inner]
            + [self.x_beyond(q, True)],
            [None] + [self.y_beyond(q, p) for p in inner] + [None],
        )


def weigh(chi_face, alpha_face):
    shrink = volume_over(chi_face)
    return shrink, alpha_face / shrink


def primitives(half, spots, cons, centred, chi, alpha, batch):
    found = {}
    for start in range(0, len(spots), batch):
        group = spots[start : start + batch]

        def gather(planes):
            return jnp.concatenate([planes[k][p] for k, p in group], axis=0)

        shrink = volume_over(gather(chi))
        mag_raw = [gather(centred[i]) for i in range(3)]
        mag = [m * shrink for m in mag_raw]
        values = recover([gather(c) * shrink for c in cons], mag)
        u = values[2:5]
        factor = gather(alpha) * lax.rsqrt(1.0 + dot(u, u))
        field = [
            factor * (u[(i + 2) % 3] * mag_raw[(i + 1) % 3] - u[(i + 1) % 3] * mag_raw[(i + 2) % 3])
            for i in range(3)
        ]
        for n, spot in enumerate(group):
            found[spot] = [value[n * half : (n + 1) * half] for value in values + mag + field]
    return found


def ring_fluxes(prims, chi, alpha, normals, d, up, down):
    found = []
    for here, there in ((0, 1), (1, 0)):
        left, right = [], []
        for a, b in zip(prims[here], prims[there]):
            below = down(a, b, 1)
            middle = a - below
            left.append(below + 0.5 * limited(below - down(a, b, 2), middle))
            right.append(a - 0.5 * limited(middle, up(a, b, 1) - a))
        shrink, weight = weigh(
            0.5 * (chi[here] + down(chi[here], chi[there], 1)),
            0.5 * (alpha[here] + down(alpha[here], alpha[there], 1)),
        )
        found.append(face_flux(left, right, normals[here] * shrink, weight, d))
    return [a - up(a, b, 1) for a, b in zip(*found)]


def early_kernel(
    cells, zst, zfl, x_below, y_below, x_above, y_above, x_below_rest, x_above_rest,
    st_rate, hydro_rate, slopes, electric, pairs, sides, thirds, pairs_z, sides_z, grads, seconds, damped, tensors,
):
    halo = Halo(
        cells, zst, zfl, x_below, y_below, x_above, y_above, x_below_rest, x_above_rest, None, None
    )
    x_below, x_above = halo.x_below, halo.x_above
    t, fields, half, own, cy = halo.t, halo.fields, halo.half, halo.own, halo.cy
    st, fl, inner = halo.st, halo.fl, halo.inner

    for q in range(fields):
        pairs[q, 0] = halo.x_third(q, False)
        pairs[q, 1] = x_below[q]
        for p in inner:
            pairs[q, 1 + p] = halo.main(q, p)
            sides[q, p - 1] = halo.beside(q, p)
            thirds[q, p - 1] = halo.y_third(q, p)
        pairs[q, 2 + own] = x_above[q]
        pairs[q, 3 + own] = halo.x_third(q, True)
        if q < CURVED:
            pairs_z[q, 0] = halo.x_beyond(q, False)
            pairs_z[q, own + 1] = halo.x_beyond(q, True)
            for p in inner:
                pairs_z[q, p] = halo.beyond(q, p)
                sides_z[q, p - 1] = halo.y_beyond(q, p)

    span = halo.span
    face = [halo.plane(fields + 5 + i) for i in range(3)]

    def halves(kind, p):
        own_x, own_y, own_z = (f[kind][p] for f in face)
        pair = kind in (0, 2)
        known_x = pair or p < own
        last = kind == 0 and p == own + 1
        if pair:
            next_x = halo.x_third(fields, True) if last else face[0][kind][min(p + 1, own + 1)]
            next_x = t.odd(own_x, next_x)
        else:
            next_x = t.odd_swapped(own_x, face[0][kind][p + 1] if known_x else own_x)
        dx = 0.5 * (next_x - own_x)
        dz = 0.5 * (t.z_up(own_z, face[2][kind ^ 2][p], 1) - own_z)
        inside = 1 <= p <= own
        if not pair:
            here = jnp.where(t.slot == 2, halo.y_third(fields, p), own_y) if kind == 1 else own_y
            next_y = t.y_up(here, face[1][kind ^ 1][p], 1)
        else:
            next_y = t.y_up(own_y, face[1][kind ^ 1][p] if inside else own_y, 1)
        dy = 0.5 * (next_y - own_y)
        if pair and not inside:
            dy = jnp.where(t.slot == cy - 1, -(dx + dz), dy)
        if not pair and not known_x:
            dx = jnp.where(t.row < cy, -(dy + dz), dx)
        return own_x + dx, own_y + dy, own_z + dz

    spots = [(0, p) for p in span] + [(1, p) for p in inner]
    spots += [(2, p) for p in span] + [(3, p) for p in inner]
    centred = [[[None] * (own + 2) for _ in range(4)] for _ in range(3)]
    for k, p in spots:
        for i, value in enumerate(halves(k, p)):
            centred[i][k][p] = value
    chi, alpha = halo.plane(0), halo.plane(7)
    found = primitives(
        half, spots, [halo.plane(fields + q) for q in range(5)], centred, chi, alpha, BATCH
    )

    lines = [[found[0, p][i] for p in span] for i in range(8)] + [chi[0], alpha[0]]
    odd_lines = [[t.odd(f[p], f[min(p + 1, own + 1)]) for p in span] for f in lines]
    fluxes = [None]
    for p in range(1, own + 2):
        left, right = [], []
        for f, o in zip(lines[:8], odd_lines):
            here = f[p] - o[p - 1]
            left.append(o[p - 1] + 0.5 * limited(o[p - 1] - f[p - 1], here))
            right.append(f[p] - 0.5 * limited(here, o[p] - f[p]))
        shrink, weight = weigh(
            0.5 * (lines[8][p] + odd_lines[8][p - 1]), 0.5 * (lines[9][p] + odd_lines[9][p - 1])
        )
        fluxes.append(face_flux(left, right, face[0][0][p] * shrink, weight, 0))
    for p in inner:
        changes = [
            ring_fluxes(
                [found[k, p][:8] for k in (0, kind)],
                [chi[k][p] for k in (0, kind)],
                [alpha[k][p] for k in (0, kind)],
                [face[d][k][p] for k in (0, kind)],
                d,
                up,
                down,
            )
            for d, kind, up, down in ((1, 1, t.y_up, t.y_down), (2, 2, t.z_up, t.z_down))
        ]
        for q in range(5):
            change = fluxes[p][q] - t.odd(fluxes[p][q], fluxes[p + 1][q])
            tensors[p - 1, 6 + q] = change + changes[0][q] + changes[1][q]
        rest, pressure = found[0, p][:2]
        u = found[0, p][2:5]
        parts = stress_parts(rest, pressure, u, found[0, p][5:8])
        lorentz_sq, over, over_sq, time_b, grown_b, b_square, enthalpy, inertia = parts
        total_pressure = pressure + 0.5 * b_square
        for s, (i, j) in enumerate(INDEX_PAIRS):
            value = inertia * u[i] * u[j] - over_sq * (grown_b[i] * grown_b[j])
            tensors[p - 1, s] = value + total_pressure if i == j else value

    ex, ey, ez = (
        [[found[k, p][8 + i] if (k, p) in found else None for p in span] for k in range(4)]
        for i in range(3)
    )
    ey_x = [
        [ey[k][p] + t.odd(ey[k][p - 1], ey[k][p]) if p else None for p in span] for k in (0, 2)
    ]
    edge_y = [None] + [ey_x[0][p] + t.z_down(ey_x[0][p], ey_x[1][p], 1) for p in span[1:]]
    for p in span[1:]:
        electric[p - 1] = ez[0][p] + t.odd(ez[0][p - 1], ez[0][p])
    for p in inner:
        electric[own + p] = ez[1][p]
        edge_y_z = ey_x[1][p] + t.z_down(ey_x[1][p], ey_x[0][p], 1)
        ex_y = ex[0][p] + t.y_down(ex[0][p], ex[1][p], 1)
        ex_y_h = ex[1][p] + t.y_down(ex[1][p], ex[0][p], 1)
        ex_y_z = ex[2][p] + t.y_down(ex[2][p], ex[3][p], 1)
        ex_y_hz = ex[3][p] + t.y_down(ex[3][p], ex[2][p], 1)
        edge_x = ex_y + t.z_down(ex_y, ex_y_z, 1)
        edge_x_h = ex_y_h + t.z_down(ex_y_h, ex_y_hz, 1)
        edge_x_z = ex_y_z + t.z_down(ex_y_z, ex_y, 1)
        place = slice((p - 1) * half, p * half)
        hydro_rate[5, place, :] = t.z_up(edge_y[p], edge_y_z, 1) - edge_y[p]
        hydro_rate[6, place, :] = edge_x - t.z_up(edge_x, edge_x_z, 1)
        hydro_rate[7, place, :] = (t.y_up(edge_x, edge_x_h, 1) - edge_x) - (
            t.odd(edge_y[p], edge_y[p + 1]) - edge_y[p]
        )

    def pair_step(index):
        p = index + 1
        base = index * half

        for q in range(fields):
            centre = pairs[q, p + 1]
            x_m3 = t.odd(pairs[q, p - 1], pairs[q, p])
            x_m2 = pairs[q, p]
            x_m1 = t.odd(pairs[q, p], centre)
            x_p1 = t.odd(centre, pairs[q, p + 2])
            x_p2 = pairs[q, p + 2]
            x_p3 = t.odd(pairs[q, p + 2], pairs[q, p + 3])
            side, third = sides[q, index], thirds[q, index]
            y_m1, y_m2 = t.y_down(centre, side, 1), t.y_down(centre, side, 2)
            y_p1, y_p2 = t.y_up(centre, side, 1), t.y_up(centre, side, 2)
            y_m3 = t.turn(
                jnp.where(t.slot >= cy - 2, side, jnp.where(t.slot == cy - 3, third, centre)), 3
            )
            y_p3 = t.turn(jnp.where(t.slot < 2, side, jnp.where(t.slot == 2, third, centre)), -3)
            beyond = zst[q, pl.ds(base, half), :]
            z_m1, z_m2, z_m3 = (t.z_down(centre, beyond, k) for k in (1, 2, 3))
            z_p1, z_p2, z_p3 = (t.z_up(centre, beyond, k) for k in (1, 2, 3))
            dx = first_diff(x_m2, x_m1, x_p1, x_p2)
            dy = first_diff(y_m2, y_m1, y_p1, y_p2)
            grads[q, 0] = dx
            if q < CURVED:
                slopes[q, index] = dx
            grads[q, 1] = dy
            grads[q, 2] = first_diff(z_m2, z_m1, z_p1, z_p2)
            near = [x_m1 + x_p1, y_m1 + y_p1, z_m1 + z_p1]
            far = [x_m2 + x_p2, y_m2 + y_p2, z_m2 + z_p2]
            outer = (x_m3 + x_p3) + (y_m3 + y_p3) + (z_m3 + z_p3)
            damped[q] = (DISSIPATION / 64.0) * (
                outer - 6.0 * (far[0] + far[1] + far[2]) + 15.0 * (near[0] + near[1] + near[2])
                - 60.0 * centre
            )
            if q < CURVED:
                for s, d in ((0, 0), (3, 1), (5, 2)):
                    seconds[q, s] = (1.0 / 12.0) * (16.0 * near[d] - far[d] - 30.0 * centre)
                b_m, b_c, b_p = pairs_z[q, p - 1], pairs_z[q, p], pairs_z[q, p + 1]
                dx_z = first_diff(b_m, t.odd(b_m, b_c), t.odd(b_c, b_p), b_p)
                b_s = sides_z[q, p - 1]
                dy_z = first_diff(
                    t.y_down(b_c, b_s, 2),
                    t.y_down(b_c, b_s, 1),
                    t.y_up(b_c, b_s, 1),
                    t.y_up(b_c, b_s, 2),
                )
                for s, inside, outside in ((2, dx, dx_z), (4, dy, dy_z)):
                    seconds[q, s] = first_diff(
                        t.z_down(inside, outside, 2),
                        t.z_down(inside, outside, 1),
                        t.z_up(inside, outside, 1),
                        t.z_up(inside, outside, 2),
                    )

        def value(q):
            return pairs[q, p + 1]

        def fluid_value(q):
            return fl[q, pl.ds(base, half), :]

        conformal, lapse = value(0), value(7)
        over_chi = 1.0 / conformal
        metric = symmetric([value(1 + s) for s in range(6)])
        shift = [value(8 + i) for i in range(3)]
        extrinsic, theta = value(11), value(21)
        traceless = symmetric([value(12 + s) for s in range(6)])
        connection = [value(18 + i) for i in range(3)]
        inverse = inverse_metric(metric)
        grad = [[grads[q, k] for k in range(3)] for q in range(fields)]
        chi_grad, lapse_grad = grad[0], grad[7]
        shift_grad = [[grad[8 + i][k] for i in range(3)] for k in range(3)]
        trace_k = extrinsic + 2.0 * theta

        stress = symmetric([tensors[p - 1, s] for s in range(6)])
        held = [fluid_value(q) for q in range(5)]
        shrink = volume_over(conformal)
        energy = held[4] + held[0]
        third_k = trace_k * (1.0 / 3.0)
        curved = [
            [
                (traceless[i][j] + metric[i][j] * third_k) if i <= j else None for j in range(3)
            ]
            for i in range(3)
        ]
        work = (
            stress[0][0] * curved[0][0]
            + stress[1][1] * curved[1][1]
            + stress[2][2] * curved[2][2]
            + 2.0
            * (
                stress[0][1] * curved[0][1]
                + stress[0][2] * curved[0][2]
                + stress[1][2] * curved[1][2]
            )
        )
        rates = [tensors[p - 1, 6 + q] for q in range(5)]
        for i in range(3):
            rates[1 + i] = (
                rates[1 + i]
                - energy * lapse_grad[i]
                + total([held[1 + k] * grad[8 + k][i] for k in range(3)])
            )
        rates[4] = (
            rates[4] + lapse * work * over_chi / shrink - dot(held[1:4], lapse_grad)
        )
        for q in range(5):
            hydro_rate[q, pl.ds(base, half), :] = rates[q]
        density = energy * shrink
        momentum = [held[1 + i] * shrink for i in range(3)]

        lowered = [[[None] * 3 for _ in range(3)] for _ in range(3)]
        for i in range(3):
            for j in range(3):
                for k in range(j, 3):
                    got = 0.5 * (
                        grad[1 + slot_of(i, k)][j]
                        + grad[1 + slot_of(i, j)][k]
                        - grad[1 + slot_of(j, k)][i]
                    )
                    lowered[i][j][k] = lowered[i][k][j] = got
        raised = [[[None] * 3 for _ in range(3)] for _ in range(3)]
        for i in range(3):
            for j in range(3):
                for k in range(j, 3):
                    got = total([inverse[i][l] * lowered[l][j][k] for l in range(3)])
                    raised[i][j][k] = raised[i][k][j] = got
        contracted = [trace_with(inverse, raised[i]) for i in range(3)]

        def hessian_trace(q):
            return (
                inverse[0][0] * seconds[q, 0]
                + inverse[1][1] * seconds[q, 3]
                + inverse[2][2] * seconds[q, 5]
                + 2.0 * (inverse[0][2] * seconds[q, 2] + inverse[1][2] * seconds[q, 4])
            )

        def second_cov(q, slope):
            bent = [total([raised[k][i][j] * slope[k] for k in range(3)]) for i, j in INDEX_PAIRS]
            return symmetric(
                [-bent[s] if s == 1 else seconds[q, s] - bent[s] for s in range(len(bent))]
            )

        chi_cov = second_cov(0, chi_grad)
        chi_lap = trace_with(inverse, chi_cov)
        raised_chi = [dot(inverse[i], chi_grad) for i in range(3)]
        chi_square = dot(raised_chi, chi_grad)
        cross_term = dot(raised_chi, lapse_grad)
        half_chi = 0.5 * over_chi
        plain_cov = second_cov(7, lapse_grad)
        lapse_cov = symmetric(
            [
                plain_cov[i][j]
                + (
                    chi_grad[i] * lapse_grad[j]
                    + chi_grad[j] * lapse_grad[i]
                    - metric[i][j] * cross_term
                )
                * half_chi
                for i, j in INDEX_PAIRS
            ]
        )
        lapse_lap = conformal * trace_with(inverse, lapse_cov)

        mixed = [
            [[dot(inverse[l], lowered[k][j]) for j in range(3)] for k in range(3)]
            for l in range(3)
        ]
        quarter_sq = half_chi * half_chi
        metric_factor = chi_lap * half_chi - 3.0 * chi_square * quarter_sq
        ricci = []
        for i, j in INDEX_PAIRS:
            second_part = -0.5 * hessian_trace(1 + slot_of(i, j))
            connection_part = 0.5 * total(
                [metric[k][i] * grad[18 + k][j] + metric[k][j] * grad[18 + k][i] for k in range(3)]
            )
            contracted_part = 0.5 * total(
                [contracted[k] * (lowered[i][j][k] + lowered[j][i][k]) for k in range(3)]
            )
            if i == j:
                quadratic = total(
                    [
                        raised[k][l][i] * (2.0 * mixed[l][i][k] + mixed[l][k][i])
                        for k in range(3)
                        for l in range(3)
                    ]
                )
            else:
                quadratic = total(
                    [
                        raised[k][l][i] * (mixed[l][j][k] + mixed[l][k][j])
                        + raised[k][l][j] * mixed[l][i][k]
                        for k in range(3)
                        for l in range(3)
                    ]
                )
            conformal_part = (
                chi_cov[i][j] * half_chi
                + metric[i][j] * metric_factor
                - chi_grad[i] * chi_grad[j] * quarter_sq
            )
            ricci.append(
                second_part + connection_part + contracted_part + quadratic + conformal_part
            )
        ricci = symmetric(ricci)
        ricci_scalar = conformal * trace_with(inverse, ricci)
        stress_trace = conformal * trace_with(inverse, stress)

        up_a = [
            [total([inverse[i][k] * traceless[k][j] for k in range(3)]) for j in range(3)]
            for i in range(3)
        ]
        raised_a = symmetric(
            [total([up_a[i][l] * inverse[j][l] for l in range(3)]) for i, j in INDEX_PAIRS]
        )
        a_square = trace_with(traceless, raised_a)
        shift_div = shift_grad[0][0] + shift_grad[1][1] + shift_grad[2][2]
        two_thirds_div = (2.0 / 3.0) * shift_div

        def finish(q, rate):
            rate = rate + dot(shift, grad[q]) + damped[q]
            st_rate[q, pl.ds(base, half), :] = rate

        finish(0, (2.0 / 3.0) * conformal * (lapse * trace_k - shift_div))
        finish(7, -2.0 * lapse * extrinsic)
        for i in range(3):
            finish(8 + i, 0.75 * connection[i] - SHIFT_DAMPING * shift[i])
        finish(
            11,
            lapse
            * (
                a_square
                + trace_k * trace_k * (1.0 / 3.0)
                + FOUR_PI * (stress_trace + density)
                + KAPPA_ONE * theta
            )
            - lapse_lap,
        )
        source = symmetric(
            [
                lapse * (ricci[i][j] - 2.0 * FOUR_PI * stress[i][j]) - lapse_cov[i][j]
                for i, j in INDEX_PAIRS
            ]
        )
        third_trace = trace_with(inverse, source) * (1.0 / 3.0)
        for s, (i, j) in enumerate(INDEX_PAIRS):
            finish(
                1 + s,
                total(
                    [
                        metric[i][k] * shift_grad[j][k] + metric[j][k] * shift_grad[i][k]
                        for k in range(3)
                    ]
                )
                - metric[i][j] * two_thirds_div
                - 2.0 * lapse * traceless[i][j],
            )
            product = total([traceless[i][k] * up_a[k][j] for k in range(3)])
            finish(
                12 + s,
                total(
                    [
                        traceless[i][k] * shift_grad[j][k] + traceless[j][k] * shift_grad[i][k]
                        for k in range(3)
                    ]
                )
                - traceless[i][j] * two_thirds_div
                + conformal * (source[i][j] - metric[i][j] * third_trace)
                + lapse * (trace_k * traceless[i][j] - 2.0 * product),
            )
        for i in range(3):
            bracket = (
                trace_with(raised_a, raised[i])
                - 1.5 * dot(raised_a[i], chi_grad) * over_chi
                - dot(inverse[i], [2.0 * grad[11][j] + grad[21][j] for j in range(3)]) * (1.0 / 3.0)
                - 2.0 * FOUR_PI * dot(inverse[i], momentum)
            )
            spread = [
                seconds[8, 0] + seconds[10, 2],
                seconds[9, 3] + seconds[10, 4],
                seconds[8, 2] + seconds[9, 4] + seconds[10, 5],
            ]
            finish(
                18 + i,
                contracted[i] * two_thirds_div
                - total([contracted[j] * shift_grad[j][i] for j in range(3)])
                + hessian_trace(8 + i)
                + dot(inverse[i], spread) * (1.0 / 3.0)
                - 2.0 * dot(raised_a[i], lapse_grad)
                + 2.0
                * lapse
                * (bracket - KAPPA_ONE * (connection[i] - contracted[i])),
            )
        finish(
            21,
            0.5
            * lapse
            * (
                ricci_scalar
                - a_square
                + (2.0 / 3.0) * trace_k * trace_k
                - 4.0 * FOUR_PI * density
            )
            - 2.0 * KAPPA_ONE * lapse * theta,
        )

    for index in range(own):
        pair_step(index)


def late_kernel(
    cells, zst, zfl, x_below, y_below, x_above, y_above, x_below_rest, x_above_rest,
    c_below, c_above, line_two, line_top,
    st_rate, hydro_rate, slopes, electric, st_out, fl_out,
):
    halo = Halo(
        cells, zst, zfl, x_below, y_below, x_above, y_above, x_below_rest, x_above_rest,
        c_below, c_above,
    )
    x_below, x_above = halo.x_below, halo.x_above
    t, fields, half, own = halo.t, halo.fields, halo.half, halo.own
    inner, span = halo.inner, halo.span

    top = jnp.maximum(line_top[...], line_two[...])
    for lines in (c_below, c_above):
        top = jnp.maximum(top, lines[CORNER_TILES - 1, TOP_ROW : TOP_ROW + 1, :])
    dt = COURANT / top

    for p in inner:
        place = slice((p - 1) * half, p * half)
        mixed = []
        for q in range(CURVED):
            s_m, s_c, s_p = (
                halo.beside(q, n) if 1 <= n <= own else halo.corner(q, n) for n in (p - 1, p, p + 1)
            )
            slope = slopes[q, p - 1]
            slope_side = first_diff(s_m, t.odd_swapped(s_m, s_c), t.odd_swapped(s_c, s_p), s_p)
            mixed.append(
                first_diff(
                    t.y_down(slope, slope_side, 2),
                    t.y_down(slope, slope_side, 1),
                    t.y_up(slope, slope_side, 1),
                    t.y_up(slope, slope_side, 2),
                )
            )
        conformal, lapse = halo.main(0, p), halo.main(7, p)
        metric = [halo.main(1 + s, p) for s in range(6)]
        inverse = inverse_metric(symmetric(metric))
        half_chi = 0.5 / conformal
        cross = inverse[0][1]
        chi_trace = 2.0 * cross * mixed[0] * half_chi
        ricci = [metric[s] * chi_trace - cross * mixed[1 + s] for s in range(6)]
        ricci[1] = ricci[1] + mixed[0] * half_chi
        source = [lapse * r for r in ricci]
        source[1] = source[1] - mixed[7]
        third_trace = trace_with(inverse, symmetric(source)) * (1.0 / 3.0)
        extra = {
            11: -2.0 * conformal * cross * mixed[7],
            21: 0.5 * lapse * conformal * trace_with(inverse, symmetric(ricci)),
        }
        for s in range(6):
            extra[12 + s] = conformal * (source[s] - metric[s] * third_trace)
        for i in range(3):
            extra[18 + i] = 2.0 * cross * mixed[8 + i] + (1.0 / 3.0) * (
                inverse[i][0] * mixed[9] + inverse[i][1] * mixed[8]
            )
        for q in range(fields):
            rate = st_rate[q, place, :]
            if q in extra:
                rate = rate + extra[q]
            st_out[q, place, :] = halo.main(q, p) + dt * rate

    end = own + 1
    ends = (0, end)
    bx_face, by_face, bz_face = ({p: halo.corner(fields + 5 + i, p) for p in ends} for i in range(3))
    layers = {p: halo.corner_layers(p) for p in ends}
    bx_face[end] = layers[end]
    by_face[0] = jnp.where(t.slot < 2, layers[0], by_face[0])
    centred = [{}, {}, {}]
    for p in ends:
        following = halo.beside(fields + 5, 1) if p == 0 else bx_face[p]
        edge_cells = x_below if p == 0 else x_above
        dx = 0.5 * (t.odd_swapped(bx_face[p], following) - bx_face[p])
        dy = 0.5 * (t.y_up(by_face[p], edge_cells[fields + 6], 1) - by_face[p])
        centred[0][p] = bx_face[p] + dx
        centred[1][p] = by_face[p] + dy
        centred[2][p] = bz_face[p] - (dx + dy)
    corners = [{p: halo.corner(q, p) for p in ends} for q in [0, 7] + list(range(fields, fields + 5))]
    found = primitives(
        half, [(0, p) for p in ends], [[c] for c in corners[2:]], [[c] for c in centred],
        [corners[0]], [corners[1]], 2,
    )
    ez_h = [found[0, 0][10]] + [electric[own + p] for p in inner] + [found[0, end][10]]
    ez_x_h = [None] + [ez_h[p] + t.odd_swapped(ez_h[p - 1], ez_h[p]) for p in span[1:]]
    ez_x = [None] + [electric[p - 1] for p in span[1:]]
    edge_z = [None] + [ez_x[p] + t.y_down(ez_x[p], ez_x_h[p], 1) for p in span[1:]]
    quarter = 0.25 * dt
    for p in inner:
        place = slice((p - 1) * half, p * half)
        edge_z_h = ez_x_h[p] + t.y_down(ez_x_h[p], ez_x[p], 1)
        for q in range(5):
            fl_out[q, place, :] = halo.main(fields + q, p) + dt * hydro_rate[q, place, :]
        x_rate = hydro_rate[5, place, :] - (t.y_up(edge_z[p], edge_z_h, 1) - edge_z[p])
        y_rate = hydro_rate[6, place, :] + (t.odd(edge_z[p], edge_z[p + 1]) - edge_z[p])
        z_rate = hydro_rate[7, place, :]
        for i, rate in enumerate((x_rate, y_rate, z_rate)):
            fl_out[5 + i, place, :] = halo.main(fields + 5 + i, p) + quarter * rate


def per_device(spacetime, fluid):
    fields, cx, cy, cz = spacetime.shape
    rows = cx * cy
    st = spacetime.reshape(fields, rows, cz)
    fl = fluid.reshape(FLUID, rows, cz)
    sizes = [lax.axis_size(a) for a in ("gx", "gy", "gz")]
    tile = (2 * cy, cz)
    f32 = jnp.float32

    def shape(*dims):
        return jax.ShapeDtypeStruct(dims, f32)

    def beyond(cells):
        n = sizes[2]
        after = lax.ppermute(cells, "gz", [((i + 1) % n, i) for i in range(n)])
        if n == 2:
            return after
        before = lax.ppermute(cells, "gz", [(i, (i + 1) % n) for i in range(n)])
        lane = lax.broadcasted_iota(jnp.int32, cells.shape, 2)
        return jnp.where(lane < cz // 2, after, before)

    params = pltpu.CompilerParams(vmem_limit_bytes=48 * 1024 * 1024)
    zst, zfl = beyond(st), beyond(fl)
    cells = jnp.concatenate([st, fl], axis=0)
    face = shape(face_tiles(fields), *tile)
    corner = shape(CORNER_TILES, *tile)
    lane_row = shape(1, cz)
    near = shape(CURVED + FLUID + 1, *tile)
    rest = shape(face.shape[0] - near.shape[0], *tile)
    top = pl.pallas_call(
        speed_kernel, out_shape=lane_row, compiler_params=params, name="speed"
    )(cells, zst)

    def move(cells, dx, dy):
        nx, ny = sizes[0], sizes[1]
        hops = [
            (i * ny + j, ((i + dx) % nx) * ny + (j + dy) % ny) for i in range(nx) for j in range(ny)
        ]
        return lax.ppermute(cells, ("gx", "gy"), hops)

    short = sizes[0] <= 4 and sizes[1] <= 4 and sizes[2] <= 2
    top_two = move(top, 2, 0) if short and sizes[0] == 4 else top
    x_high, y_high = pl.pallas_call(
        pack_up_kernel, out_shape=[near, face], compiler_params=params, name="pack_up"
    )(cells, zst, zfl, top)
    x_below = move(x_high, 1, 0)
    y_below = move(y_high, 0, 1)
    x_low, y_low, x_low_rest, x_high_rest = pl.pallas_call(
        pack_down_kernel,
        out_shape=[near, face, rest, rest],
        compiler_params=params,
        name="pack_down",
    )(cells, zst, zfl, top, top_two)
    x_above = move(x_low, -1, 0)
    y_above = move(y_low, 0, -1)
    x_below_rest = move(x_high_rest, 1, 0)
    x_above_rest = move(x_low_rest, -1, 0)
    c_low, c_high, line_top = pl.pallas_call(
        relay_kernel,
        out_shape=[corner, corner, lane_row],
        compiler_params=params,
        name="relay",
    )(x_below, x_above, y_below, top, top_two)
    c_above = move(c_low, 0, -1)
    c_below = move(c_high, 0, 1)
    if not short:
        line_two = lax.pmax(line_top, ("gx", "gy", "gz"))
    else:
        line_two = move(line_top, 0, 2) if sizes[1] == 4 else line_top
    own = cx // 2
    arrived = (cells, zst, zfl, x_below, y_below, x_above, y_above, x_below_rest, x_above_rest)
    early = pl.pallas_call(
        early_kernel,
        out_shape=[
            shape(*st.shape),
            shape(FLUID, rows, cz),
            shape(CURVED, own, *tile),
            shape(2 * own + 1, *tile),
        ],
        scratch_shapes=[
            pltpu.VMEM((fields, own + 4) + tile, f32),
            pltpu.VMEM((fields, own) + tile, f32),
            pltpu.VMEM((fields, own) + tile, f32),
            pltpu.VMEM((CURVED, own + 2) + tile, f32),
            pltpu.VMEM((CURVED, own) + tile, f32),
            pltpu.VMEM((fields, 3) + tile, f32),
            pltpu.VMEM((CURVED, 6) + tile, f32),
            pltpu.VMEM((fields,) + tile, f32),
            pltpu.VMEM((own, 11) + tile, f32),
        ],
        compiler_params=params,
        name="early",
    )(*arrived)
    st_next, fl_next = pl.pallas_call(
        late_kernel,
        out_shape=[shape(*st.shape), shape(*fl.shape)],
        compiler_params=params,
        name="late",
    )(*arrived, c_below, c_above, line_two, line_top, *early)
    return st_next.reshape(spacetime.shape), fl_next.reshape(fluid.shape)


def solution(mesh):
    spec = P(None, "gx", "gy", "gz")
    return jax.shard_map(
        per_device, mesh=mesh, in_specs=(spec, spec), out_specs=(spec, spec), check_vma=False
    )
```

```python
import functools
import math

import jax
import jax.numpy as jnp
from jax import lax
from jax.experimental import pallas as pl
from jax.experimental.pallas import tpu as pltpu
from jax.sharding import PartitionSpec as P

RECOVERY_STEPS = 4
INDEX_PAIRS = ((0, 0), (0, 1), (0, 2), (1, 1), (1, 2), (2, 2))
COURANT = 0.25
DISSIPATION = 0.2
KAPPA_ONE = 0.02
SHIFT_DAMPING = 1.0
SPEED_CAP = 0.99
PRESSURE_FLOOR = 0.01
FOUR_PI = 4.0 * math.pi

BATCH = 6
CURVED = 11
FLUID = 8


def total(pieces):
    summed = pieces[0]
    for member in pieces[1:]:
        summed = summed + member
    return summed


def dot(first_vec, second_vec):
    return total([first_vec[i] * second_vec[i] for i in range(3)])


def slot_of(i, j):
    return INDEX_PAIRS.index((min(i, j), max(i, j)))


def symmetric(entries):
    return [[entries[slot_of(i, j)] for j in range(3)] for i in range(3)]


def trace_with(inverse, tensor):
    return (
        inverse[0][0] * tensor[0][0]
        + inverse[1][1] * tensor[1][1]
        + inverse[2][2] * tensor[2][2]
        + 2.0
        * (
            inverse[0][1] * tensor[0][1]
            + inverse[0][2] * tensor[0][2]
            + inverse[1][2] * tensor[1][2]
        )
    )


def inverse_metric(metric):
    cofactor = [
        metric[1][1] * metric[2][2] - metric[1][2] * metric[1][2],
        metric[0][2] * metric[1][2] - metric[0][1] * metric[2][2],
        metric[0][1] * metric[1][2] - metric[0][2] * metric[1][1],
        metric[0][0] * metric[2][2] - metric[0][2] * metric[0][2],
        metric[0][1] * metric[0][2] - metric[0][0] * metric[1][2],
        metric[0][0] * metric[1][1] - metric[0][1] * metric[0][1],
    ]
    determinant = (
        metric[0][0] * cofactor[0] + metric[0][1] * cofactor[1] + metric[0][2] * cofactor[2]
    )
    over = 1.0 / determinant
    return symmetric([c * over for c in cofactor])


class Tile:
    def __init__(self, cy, cz):
        self.cy, self.rows, self.lanes = cy, 2 * cy, cz
        shape = (self.rows, cz)
        self.row = lax.broadcasted_iota(jnp.int32, shape, 0)
        self.lane = lax.broadcasted_iota(jnp.int32, shape, 1)
        self.slot = lax.rem(self.row, cy)

    def turn(self, tile, amount):
        amount = amount % self.rows
        return tile if amount == 0 else pltpu.roll(tile, amount, 0)

    def spin(self, tile, amount):
        amount = amount % self.lanes
        return tile if amount == 0 else pltpu.roll(tile, amount, 1)

    def swap(self, tile):
        return self.turn(tile, self.cy)

    def odd(self, a, b):
        return self.turn(jnp.where(self.row < self.cy, b, a), self.cy)

    def odd_swapped(self, a, b):
        return self.turn(jnp.where(self.row < self.cy, a, b), self.cy)

    def y_up(self, main, beyond, k):
        return self.turn(jnp.where(self.slot < k, beyond, main), -k)

    def y_down(self, main, beyond, k):
        return self.turn(jnp.where(self.slot >= self.cy - k, beyond, main), k)

    def z_up(self, main, beyond, k):
        return self.spin(jnp.where(self.lane < k, beyond, main), -k)

    def z_down(self, main, beyond, k):
        return self.spin(jnp.where(self.lane >= self.lanes - k, beyond, main), k)

    def corner_rows(self, side, turn):
        places = ((0, 2), (self.cy - 1, self.cy + 1))[side]
        first, second = [(place + turn) % self.rows for place in places]
        return (self.row == first) | (self.row == second)

    def join_low(self, u, v):
        return jnp.where(self.slot < 2, self.swap(u), self.turn(v, 2))

    def join_high(self, u, v):
        return jnp.where(self.slot >= self.cy - 2, self.swap(u), self.turn(self.swap(v), -2))

    def part_first(self, from_above, from_below):
        return jnp.where(self.slot < 2, from_above, from_below)

    def part_second(self, from_above, from_below):
        return self.turn(jnp.where(self.slot < 2, from_below, from_above), 2)


def edge_list(tiles):
    fields = next(n for n in range(tiles) if face_tiles(n) == tiles)
    return list(range(CURVED)) + list(range(fields, fields + FLUID))


CORNER_TURNS = (0, 1, 4, 5)
CORNER_TILES = CURVED + FLUID // 4 + 1
TOP_ROW = 6


def face_tiles(fields):
    return fields + FLUID + len(pairs_of(third_list(fields))) + 1


def third_list(fields):
    return list(range(fields + 1))


def pairs_of(items):
    return [(items[i], items[min(i + 1, len(items) - 1)]) for i in range(0, len(items), 2)]


def top_speed(st):
    inverse = inverse_metric(symmetric([st[1 + s] for s in range(6)]))
    scale = 2.0 * st[7] * st[0]
    speeds = [jnp.abs(st[8 + d]) + jnp.sqrt(scale * inverse[d][d]) for d in range(3)]
    top = jnp.maximum(jnp.maximum(speeds[0], speeds[1]), speeds[2])
    return jnp.max(jnp.max(top, axis=1, keepdims=True), axis=0, keepdims=True)


class Chosen:
    def __init__(self, first, second, swapped):
        self.first, self.second, self.swapped, self.shape = first, second, swapped, first.shape

    def __getitem__(self, key):
        return jnp.where(self.swapped, self.second[key], self.first[key])


class Sent:
    def __init__(self, first, second, swapped):
        self.first, self.second, self.swapped, self.shape = first, second, swapped, first.shape

    def put(self, key, lower, upper):
        self.first[key] = jnp.where(self.swapped, upper, lower)
        self.second[key] = jnp.where(self.swapped, lower, upper)


def odd_places(place, tile):
    return [jnp.full(tile, place[n], jnp.int32) == 1 for n in range(2)]


def pack_kernel(place, cells, zst, zfl, *outs):
    fields, rows, lanes = zst.shape
    st, fl = cells.at[0:fields], cells.at[fields : fields + FLUID]
    cy = rows // 4
    t = Tile(cy, lanes)
    x_first, x_second, y_first, y_second, top_out = outs
    half = t.rows
    odd_x, odd_y = odd_places(place, (half, lanes))
    to_x, to_y = Sent(x_first, x_second, odd_x), Sent(y_first, y_second, odd_y)

    def own(ref, q):
        return [ref[q, 0:half, :], ref[q, half : 2 * half, :]]

    tiles, beyond = [], []
    for q in range(fields):
        tiles.append(own(st, q))
        beyond.append(own(zst, q) if q < CURVED else None)
    for q in range(FLUID):
        tiles.append(own(fl, q))
        beyond.append(own(zfl, q))

    packed = [None] * 4
    place_count = 0
    for q, (first, second) in enumerate(tiles):
        to_x.put(q, first, second)
        to_y.put(q, t.join_low(first, second), t.join_high(first, second))
        if beyond[q] is not None:
            zf, zs = beyond[q]
            for m, piece in enumerate((zf, zs, t.join_low(zf, zs), t.join_high(zf, zs))):
                piece = t.spin(piece, 4 * place_count + 2)
                packed[m] = (
                    piece if place_count == 0 else jnp.where(t.lane < 4 * place_count, packed[m], piece)
                )
            place_count += 1
    for n, (a, b) in enumerate(pairs_of(third_list(fields))):
        slot = fields + FLUID + n
        xa, xb = (tiles[q if q < fields else fields + 5] for q in (a, b))
        to_x.put(
            slot,
            jnp.where(t.row < cy, xa[1], t.swap(xb[1])),
            jnp.where(t.row < cy, t.swap(xb[0]), xa[0]),
        )
        ya, yb = (tiles[q if q < fields else fields + 6] for q in (a, b))
        w = [t.swap(ya[0]), t.swap(ya[1]), t.swap(yb[0]), t.swap(yb[1])]
        s = t.slot
        low = jnp.where(s == 0, t.turn(w[2], -2), t.turn(w[3], -1))
        low = jnp.where(s == 2, w[0], jnp.where(s == 3, t.turn(w[1], 1), low))
        high = jnp.where(s == 3, t.turn(w[2], 2), t.turn(w[3], 1))
        high = jnp.where(s == 1, w[0], jnp.where(s == 0, t.turn(w[1], -1), high))
        to_y.put(slot, low, high)
    top = jnp.maximum(top_speed(st), top_speed(zst))
    top_out[...] = jnp.broadcast_to(top, top_out.shape)
    last = x_first.shape[0] - 1
    x_lanes = [jnp.where(t.lane < 4 * place_count, piece, top) for piece in packed[:2]]
    y_lanes = [jnp.where(t.lane < 4 * place_count, piece, top) for piece in packed[2:]]
    to_x.put(last, *x_lanes)
    to_y.put(last, *y_lanes)


def relay_kernel(place, x_first, x_second, y_first, top, top_two, c_first, c_second, line_top):
    cy, lanes = x_first.shape[1] // 2, x_first.shape[2]
    t = Tile(cy, lanes)
    odd_x, odd_y = odd_places(place, (t.rows, lanes))
    x_below, x_above = Chosen(x_first, x_second, odd_x), Chosen(x_second, x_first, odd_x)
    to_y = Sent(c_first, c_second, odd_y)
    last = x_first.shape[0] - 1
    line = jnp.maximum(top[...], top_two[...])
    for beside in (x_first, x_second, y_first):
        line = jnp.maximum(line, beside[last, 0:1, lanes - 1 : lanes])
    line_top[...] = line
    edge = edge_list(x_below.shape[0])
    for q in range(CURVED):
        below, above = x_below[q], x_above[q]
        to_y.put(q, t.join_low(below, above), t.join_high(below, above))
    for n in range(0, FLUID, 4):
        low, high = None, None
        for turn, q in zip(CORNER_TURNS, edge[CURVED + n : CURVED + n + 4]):
            below, above = x_below[q], x_above[q]
            below, above = (t.turn(j(below, above), turn) for j in (t.join_low, t.join_high))
            if low is None:
                low, high = below, above
            else:
                low = jnp.where(t.corner_rows(0, turn), below, low)
                high = jnp.where(t.corner_rows(1, turn), above, high)
        to_y.put(CURVED + n // 4, low, high)
    along_x, along_y = edge[CURVED + 5], edge[CURVED + 6]
    low = t.join_low(x_below[along_y], x_above[along_y])
    high = t.join_high(x_below[along_x], x_above[along_x])
    low, high = (jnp.where(t.row == TOP_ROW, line, tile) for tile in (low, high))
    to_y.put(CORNER_TILES - 1, low, high)


def limited(a, b):
    return jnp.maximum(jnp.minimum(a, b), 0.0) + jnp.minimum(jnp.maximum(a, b), 0.0)


def recover(conserved, magnetic):
    density = conserved[0]
    momenta = conserved[1:4]
    energy = conserved[4] + density
    mom_sq = dot(momenta, momenta)
    mag_sq = dot(magnetic, magnetic)
    cross = dot(momenta, magnetic)
    cross_sq = cross * cross

    def state(z):
        grown = z + mag_sq
        over = 1.0 / (z * grown)
        speed_sq = (mom_sq * z * z + cross_sq * (2.0 * z + mag_sq)) * over * over
        kept = 1.0 - jnp.minimum(speed_sq, SPEED_CAP)
        rest = density * jnp.sqrt(kept)
        return kept, rest, 0.5 * (z * kept - rest), grown * over

    z = jnp.maximum(energy - 0.5 * mag_sq, density)
    for _ in range(RECOVERY_STEPS):
        kept, rest, pressure, over_z = state(z)
        residual = (
            z
            + mag_sq
            - pressure
            - 0.5 * mag_sq * kept
            - 0.5 * cross_sq * over_z * over_z
            - energy
        )
        z = jnp.maximum(z - residual / (1.0 - 0.5 * kept), density)
    kept, rest, pressure, over_z = state(z)
    pressure = jnp.maximum(pressure, PRESSURE_FLOOR * rest)
    scale = lax.rsqrt(kept) / (z + mag_sq)
    along = cross * over_z
    four_vel = [scale * (momenta[i] + along * magnetic[i]) for i in range(3)]
    return [rest, pressure] + four_vel


def stress_parts(rest, pressure, u, magnetic):
    lorentz_sq = 1.0 + dot(u, u)
    over = lax.rsqrt(lorentz_sq)
    over_sq = over * over
    time_b = dot(u, magnetic)
    grown_b = [magnetic[i] + time_b * u[i] for i in range(3)]
    b_square = (dot(magnetic, magnetic) + time_b * time_b) * over_sq
    enthalpy = rest + 2.0 * pressure
    inertia = enthalpy + b_square
    return lorentz_sq, over, over_sq, time_b, grown_b, b_square, enthalpy, inertia


def face_state(rest, pressure, u, magnetic, d):
    lorentz_sq, over, over_sq, time_b, grown_b, b_square, enthalpy, inertia = stress_parts(
        rest, pressure, u, magnetic
    )
    total_pressure = pressure + 0.5 * b_square
    lorentz = lorentz_sq * over
    density = rest * lorentz
    carried = inertia * lorentz
    time_over = time_b * over
    conserved = [density]
    conserved += [carried * u[j] - time_over * grown_b[j] for j in range(3)]
    conserved += [inertia * lorentz_sq - total_pressure - time_b * time_b - density]
    mass_flux = rest * u[d]
    flux = [mass_flux]
    pushed = inertia * u[d]
    b_over = grown_b[d] * over_sq
    for j in range(3):
        flux_j = pushed * u[j] - b_over * grown_b[j]
        flux.append(flux_j + total_pressure if j == d else flux_j)
    flux.append(carried * u[d] - time_over * grown_b[d] - mass_flux)
    ratio = 1.0 / (enthalpy * inertia)
    sound_sq = 2.0 * pressure * inertia * ratio
    alfven_sq = b_square * enthalpy * ratio
    fast_sq = sound_sq + alfven_sq - sound_sq * alfven_sq
    slow = 1.0 - fast_sq
    velocity = u[d] * over
    rest_part = 1.0 - dot(u, u) * over_sq * fast_sq
    spread = jnp.sqrt(fast_sq * over_sq * (rest_part - velocity * velocity * slow))
    fastest = (jnp.abs(velocity * slow) + spread) / rest_part
    return conserved, flux, fastest


def face_flux(left, right, normal, weight, d):
    sides = []
    for state in (left, right):
        magnetic = [normal if i == d else state[5 + i] for i in range(3)]
        sides.append(face_state(state[0], state[1], state[2:5], magnetic, d))
    (cons_l, flux_l, fast_l), (cons_r, flux_r, fast_r) = sides
    signal = jnp.maximum(fast_l, fast_r)
    scale = 0.5 * weight
    return [scale * (flux_l[q] + flux_r[q] - signal * (cons_r[q] - cons_l[q])) for q in range(5)]


def volume_over(conformal):
    return conformal * jnp.sqrt(conformal)


def first_diff(down_two, down, up, up_two):
    return (8.0 / 12.0) * (up - down) + (1.0 / 12.0) * (down_two - up_two)


class Halo:
    def __init__(self, place, cells, zst, zfl, x_first, y_first, x_second, y_second, *corners):
        self.fields, self.block, self.lanes = zst.shape
        odd_x, odd_y = odd_places(place, (self.block // 2, self.lanes))
        x_below, x_above = Chosen(x_first, x_second, odd_x), Chosen(x_second, x_first, odd_x)
        y_below, y_above = Chosen(y_first, y_second, odd_y), Chosen(y_second, y_first, odd_y)
        if corners:
            c_first, c_second = corners
            self.c_below = Chosen(c_first, c_second, odd_y)
            self.c_above = Chosen(c_second, c_first, odd_y)
        self.st = cells.at[0 : self.fields]
        self.fl = cells.at[self.fields : self.fields + FLUID]
        self.zst, self.zfl = zst, zfl
        self.x_below, self.x_above = x_below, x_above
        self.y_below, self.y_above = y_below, y_above
        self.cy = self.block // 4
        self.t = Tile(self.cy, self.lanes)
        self.half = self.t.rows
        self.own = self.block // self.half
        self.inner = range(1, self.own + 1)
        self.span = range(self.own + 2)
        self.edge = edge_list(x_below.shape[0])
        self.last = x_below.shape[0] - 1

    def rows_of(self, ref, q, p):
        return ref[q, (p - 1) * self.half : p * self.half, :]

    def main(self, q, p):
        if q < self.fields:
            return self.rows_of(self.st, q, p)
        return self.rows_of(self.fl, q - self.fields, p)

    def beyond(self, q, p):
        if q < self.fields:
            return self.rows_of(self.zst, q, p)
        return self.rows_of(self.zfl, q - self.fields, p)

    def part(self, second):
        return self.t.part_second if second else self.t.part_first

    def beside(self, q, p):
        return self.part(p == 2)(self.y_above[q], self.y_below[q])

    def third_place(self, q):
        return self.fields + FLUID + q // 2, q % 2

    def x_third(self, q, upper):
        tile, which = self.third_place(q)
        found = self.x_above[tile] if upper else self.x_below[tile]
        return self.t.swap(found) if which else found

    def y_third(self, q, p):
        t = self.t
        tile, which = self.third_place(q)
        turn_above, turn_below = ((0, 0), (-1, 1), (2, -2), (1, -1))[2 * which + p - 1]
        above, below = t.turn(self.y_above[tile], turn_above), t.turn(self.y_below[tile], turn_below)
        return jnp.where(t.slot == 2, above, below)

    def z_place(self, q):
        return 4 * self.edge.index(q) + 2

    def x_beyond(self, q, upper):
        tile = self.x_above[self.last] if upper else self.x_below[self.last]
        return self.t.spin(tile, -self.z_place(q))

    def y_beyond(self, q, p):
        return self.t.spin(self.beside(self.last, p), -self.z_place(q))

    def corner(self, q, p):
        place, turn = q, 0
        if q >= CURVED:
            n = q - self.fields
            place, turn = CURVED + n // 4, CORNER_TURNS[n % 4]
        above, below = self.t.turn(self.c_above[place], -turn), self.t.turn(self.c_below[place], -turn)
        return self.part(p > 0)(above, below)

    def corner_layers(self, p):
        place = CORNER_TILES - 1
        return self.part(p > 0)(self.c_above[place], self.c_below[place])

    def plane(self, q):
        inner = self.inner
        return (
            [self.x_below[q]] + [self.main(q, p) for p in inner] + [self.x_above[q]],
            [None] + [self.beside(q, p) for p in inner] + [None],
            [self.x_beyond(q, False)]
            + [self.beyond(q, p) for p in inner]
            + [self.x_beyond(q, True)],
            [None] + [self.y_beyond(q, p) for p in inner] + [None],
        )


def weigh(chi_face, alpha_face):
    shrink = volume_over(chi_face)
    return shrink, alpha_face / shrink


def primitives(half, spots, cons, centred, chi, alpha, batch):
    found = {}
    for start in range(0, len(spots), batch):
        group = spots[start : start + batch]

        def gather(planes):
            return jnp.concatenate([planes[k][p] for k, p in group], axis=0)

        shrink = volume_over(gather(chi))
        mag_raw = [gather(centred[i]) for i in range(3)]
        mag = [m * shrink for m in mag_raw]
        values = recover([gather(c) * shrink for c in cons], mag)
        u = values[2:5]
        factor = gather(alpha) * lax.rsqrt(1.0 + dot(u, u))
        field = [
            factor * (u[(i + 2) % 3] * mag_raw[(i + 1) % 3] - u[(i + 1) % 3] * mag_raw[(i + 2) % 3])
            for i in range(3)
        ]
        for n, spot in enumerate(group):
            found[spot] = [value[n * half : (n + 1) * half] for value in values + mag + field]
    return found


def ring_fluxes(prims, chi, alpha, normals, d, up, down):
    found = []
    for here, there in ((0, 1), (1, 0)):
        left, right = [], []
        for a, b in zip(prims[here], prims[there]):
            below = down(a, b, 1)
            middle = a - below
            left.append(below + 0.5 * limited(below - down(a, b, 2), middle))
            right.append(a - 0.5 * limited(middle, up(a, b, 1) - a))
        shrink, weight = weigh(
            0.5 * (chi[here] + down(chi[here], chi[there], 1)),
            0.5 * (alpha[here] + down(alpha[here], alpha[there], 1)),
        )
        found.append(face_flux(left, right, normals[here] * shrink, weight, d))
    return [a - up(a, b, 1) for a, b in zip(*found)]


def early_kernel(
    place, cells, zst, zfl, x_first, y_first, x_second, y_second,
    st_rate, hydro_rate, slopes, electric, pairs, sides, thirds, pairs_z, sides_z, grads, seconds, damped, tensors,
):
    halo = Halo(place, cells, zst, zfl, x_first, y_first, x_second, y_second)
    x_below, x_above = halo.x_below, halo.x_above
    t, fields, half, own, cy = halo.t, halo.fields, halo.half, halo.own, halo.cy
    st, fl, inner = halo.st, halo.fl, halo.inner

    for q in range(fields):
        pairs[q, 0] = halo.x_third(q, False)
        pairs[q, 1] = x_below[q]
        for p in inner:
            pairs[q, 1 + p] = halo.main(q, p)
            sides[q, p - 1] = halo.beside(q, p)
            thirds[q, p - 1] = halo.y_third(q, p)
        pairs[q, 2 + own] = x_above[q]
        pairs[q, 3 + own] = halo.x_third(q, True)
        if q < CURVED:
            pairs_z[q, 0] = halo.x_beyond(q, False)
            pairs_z[q, own + 1] = halo.x_beyond(q, True)
            for p in inner:
                pairs_z[q, p] = halo.beyond(q, p)
                sides_z[q, p - 1] = halo.y_beyond(q, p)

    span = halo.span
    face = [halo.plane(fields + 5 + i) for i in range(3)]

    def halves(kind, p):
        own_x, own_y, own_z = (f[kind][p] for f in face)
        pair = kind in (0, 2)
        known_x = pair or p < own
        last = kind == 0 and p == own + 1
        if pair:
            next_x = halo.x_third(fields, True) if last else face[0][kind][min(p + 1, own + 1)]
            next_x = t.odd(own_x, next_x)
        else:
            next_x = t.odd_swapped(own_x, face[0][kind][p + 1] if known_x else own_x)
        dx = 0.5 * (next_x - own_x)
        dz = 0.5 * (t.z_up(own_z, face[2][kind ^ 2][p], 1) - own_z)
        inside = 1 <= p <= own
        if not pair:
            here = jnp.where(t.slot == 2, halo.y_third(fields, p), own_y) if kind == 1 else own_y
            next_y = t.y_up(here, face[1][kind ^ 1][p], 1)
        else:
            next_y = t.y_up(own_y, face[1][kind ^ 1][p] if inside else own_y, 1)
        dy = 0.5 * (next_y - own_y)
        if pair and not inside:
            dy = jnp.where(t.slot == cy - 1, -(dx + dz), dy)
        if not pair and not known_x:
            dx = jnp.where(t.row < cy, -(dy + dz), dx)
        return own_x + dx, own_y + dy, own_z + dz

    spots = [(0, p) for p in span] + [(1, p) for p in inner]
    spots += [(2, p) for p in span] + [(3, p) for p in inner]
    centred = [[[None] * (own + 2) for _ in range(4)] for _ in range(3)]
    for k, p in spots:
        for i, value in enumerate(halves(k, p)):
            centred[i][k][p] = value
    chi, alpha = halo.plane(0), halo.plane(7)
    found = primitives(
        half, spots, [halo.plane(fields + q) for q in range(5)], centred, chi, alpha, BATCH
    )

    lines = [[found[0, p][i] for p in span] for i in range(8)] + [chi[0], alpha[0]]
    odd_lines = [[t.odd(f[p], f[min(p + 1, own + 1)]) for p in span] for f in lines]
    fluxes = [None]
    for p in range(1, own + 2):
        left, right = [], []
        for f, o in zip(lines[:8], odd_lines):
            here = f[p] - o[p - 1]
            left.append(o[p - 1] + 0.5 * limited(o[p - 1] - f[p - 1], here))
            right.append(f[p] - 0.5 * limited(here, o[p] - f[p]))
        shrink, weight = weigh(
            0.5 * (lines[8][p] + odd_lines[8][p - 1]), 0.5 * (lines[9][p] + odd_lines[9][p - 1])
        )
        fluxes.append(face_flux(left, right, face[0][0][p] * shrink, weight, 0))
    for p in inner:
        changes = [
            ring_fluxes(
                [found[k, p][:8] for k in (0, kind)],
                [chi[k][p] for k in (0, kind)],
                [alpha[k][p] for k in (0, kind)],
                [face[d][k][p] for k in (0, kind)],
                d,
                up,
                down,
            )
            for d, kind, up, down in ((1, 1, t.y_up, t.y_down), (2, 2, t.z_up, t.z_down))
        ]
        for q in range(5):
            change = fluxes[p][q] - t.odd(fluxes[p][q], fluxes[p + 1][q])
            tensors[p - 1, 6 + q] = change + changes[0][q] + changes[1][q]
        rest, pressure = found[0, p][:2]
        u = found[0, p][2:5]
        parts = stress_parts(rest, pressure, u, found[0, p][5:8])
        lorentz_sq, over, over_sq, time_b, grown_b, b_square, enthalpy, inertia = parts
        total_pressure = pressure + 0.5 * b_square
        for s, (i, j) in enumerate(INDEX_PAIRS):
            value = inertia * u[i] * u[j] - over_sq * (grown_b[i] * grown_b[j])
            tensors[p - 1, s] = value + total_pressure if i == j else value

    ex, ey, ez = (
        [[found[k, p][8 + i] if (k, p) in found else None for p in span] for k in range(4)]
        for i in range(3)
    )
    ey_x = [
        [ey[k][p] + t.odd(ey[k][p - 1], ey[k][p]) if p else None for p in span] for k in (0, 2)
    ]
    edge_y = [None] + [ey_x[0][p] + t.z_down(ey_x[0][p], ey_x[1][p], 1) for p in span[1:]]
    for p in span[1:]:
        electric[p - 1] = ez[0][p] + t.odd(ez[0][p - 1], ez[0][p])
    for p in inner:
        electric[own + p] = ez[1][p]
        edge_y_z = ey_x[1][p] + t.z_down(ey_x[1][p], ey_x[0][p], 1)
        ex_y = ex[0][p] + t.y_down(ex[0][p], ex[1][p], 1)
        ex_y_h = ex[1][p] + t.y_down(ex[1][p], ex[0][p], 1)
        ex_y_z = ex[2][p] + t.y_down(ex[2][p], ex[3][p], 1)
        ex_y_hz = ex[3][p] + t.y_down(ex[3][p], ex[2][p], 1)
        edge_x = ex_y + t.z_down(ex_y, ex_y_z, 1)
        edge_x_h = ex_y_h + t.z_down(ex_y_h, ex_y_hz, 1)
        edge_x_z = ex_y_z + t.z_down(ex_y_z, ex_y, 1)
        place = slice((p - 1) * half, p * half)
        hydro_rate[5, place, :] = t.z_up(edge_y[p], edge_y_z, 1) - edge_y[p]
        hydro_rate[6, place, :] = edge_x - t.z_up(edge_x, edge_x_z, 1)
        hydro_rate[7, place, :] = (t.y_up(edge_x, edge_x_h, 1) - edge_x) - (
            t.odd(edge_y[p], edge_y[p + 1]) - edge_y[p]
        )

    def pair_step(index):
        p = index + 1
        base = index * half

        for q in range(fields):
            centre = pairs[q, p + 1]
            x_m3 = t.odd(pairs[q, p - 1], pairs[q, p])
            x_m2 = pairs[q, p]
            x_m1 = t.odd(pairs[q, p], centre)
            x_p1 = t.odd(centre, pairs[q, p + 2])
            x_p2 = pairs[q, p + 2]
            x_p3 = t.odd(pairs[q, p + 2], pairs[q, p + 3])
            side, third = sides[q, index], thirds[q, index]
            y_m1, y_m2 = t.y_down(centre, side, 1), t.y_down(centre, side, 2)
            y_p1, y_p2 = t.y_up(centre, side, 1), t.y_up(centre, side, 2)
            y_m3 = t.turn(
                jnp.where(t.slot >= cy - 2, side, jnp.where(t.slot == cy - 3, third, centre)), 3
            )
            y_p3 = t.turn(jnp.where(t.slot < 2, side, jnp.where(t.slot == 2, third, centre)), -3)
            beyond = zst[q, pl.ds(base, half), :]
            z_m1, z_m2, z_m3 = (t.z_down(centre, beyond, k) for k in (1, 2, 3))
            z_p1, z_p2, z_p3 = (t.z_up(centre, beyond, k) for k in (1, 2, 3))
            dx = first_diff(x_m2, x_m1, x_p1, x_p2)
            dy = first_diff(y_m2, y_m1, y_p1, y_p2)
            grads[q, 0] = dx
            if q < CURVED:
                slopes[q, index] = dx
            grads[q, 1] = dy
            grads[q, 2] = first_diff(z_m2, z_m1, z_p1, z_p2)
            near = [x_m1 + x_p1, y_m1 + y_p1, z_m1 + z_p1]
            far = [x_m2 + x_p2, y_m2 + y_p2, z_m2 + z_p2]
            outer = (x_m3 + x_p3) + (y_m3 + y_p3) + (z_m3 + z_p3)
            damped[q] = (DISSIPATION / 64.0) * (
                outer - 6.0 * (far[0] + far[1] + far[2]) + 15.0 * (near[0] + near[1] + near[2])
                - 60.0 * centre
            )
            if q < CURVED:
                for s, d in ((0, 0), (3, 1), (5, 2)):
                    seconds[q, s] = (1.0 / 12.0) * (16.0 * near[d] - far[d] - 30.0 * centre)
                b_m, b_c, b_p = pairs_z[q, p - 1], pairs_z[q, p], pairs_z[q, p + 1]
                dx_z = first_diff(b_m, t.odd(b_m, b_c), t.odd(b_c, b_p), b_p)
                b_s = sides_z[q, p - 1]
                dy_z = first_diff(
                    t.y_down(b_c, b_s, 2),
                    t.y_down(b_c, b_s, 1),
                    t.y_up(b_c, b_s, 1),
                    t.y_up(b_c, b_s, 2),
                )
                for s, inside, outside in ((2, dx, dx_z), (4, dy, dy_z)):
                    seconds[q, s] = first_diff(
                        t.z_down(inside, outside, 2),
                        t.z_down(inside, outside, 1),
                        t.z_up(inside, outside, 1),
                        t.z_up(inside, outside, 2),
                    )

        def value(q):
            return pairs[q, p + 1]

        def fluid_value(q):
            return fl[q, pl.ds(base, half), :]

        conformal, lapse = value(0), value(7)
        over_chi = 1.0 / conformal
        metric = symmetric([value(1 + s) for s in range(6)])
        shift = [value(8 + i) for i in range(3)]
        extrinsic, theta = value(11), value(21)
        traceless = symmetric([value(12 + s) for s in range(6)])
        connection = [value(18 + i) for i in range(3)]
        inverse = inverse_metric(metric)
        grad = [[grads[q, k] for k in range(3)] for q in range(fields)]
        chi_grad, lapse_grad = grad[0], grad[7]
        shift_grad = [[grad[8 + i][k] for i in range(3)] for k in range(3)]
        trace_k = extrinsic + 2.0 * theta

        stress = symmetric([tensors[p - 1, s] for s in range(6)])
        held = [fluid_value(q) for q in range(5)]
        shrink = volume_over(conformal)
        energy = held[4] + held[0]
        third_k = trace_k * (1.0 / 3.0)
        curved = [
            [
                (traceless[i][j] + metric[i][j] * third_k) if i <= j else None for j in range(3)
            ]
            for i in range(3)
        ]
        work = (
            stress[0][0] * curved[0][0]
            + stress[1][1] * curved[1][1]
            + stress[2][2] * curved[2][2]
            + 2.0
            * (
                stress[0][1] * curved[0][1]
                + stress[0][2] * curved[0][2]
                + stress[1][2] * curved[1][2]
            )
        )
        rates = [tensors[p - 1, 6 + q] for q in range(5)]
        for i in range(3):
            rates[1 + i] = (
                rates[1 + i]
                - energy * lapse_grad[i]
                + total([held[1 + k] * grad[8 + k][i] for k in range(3)])
            )
        rates[4] = (
            rates[4] + lapse * work * over_chi / shrink - dot(held[1:4], lapse_grad)
        )
        for q in range(5):
            hydro_rate[q, pl.ds(base, half), :] = rates[q]
        density = energy * shrink
        momentum = [held[1 + i] * shrink for i in range(3)]

        lowered = [[[None] * 3 for _ in range(3)] for _ in range(3)]
        for i in range(3):
            for j in range(3):
                for k in range(j, 3):
                    got = 0.5 * (
                        grad[1 + slot_of(i, k)][j]
                        + grad[1 + slot_of(i, j)][k]
                        - grad[1 + slot_of(j, k)][i]
                    )
                    lowered[i][j][k] = lowered[i][k][j] = got
        raised = [[[None] * 3 for _ in range(3)] for _ in range(3)]
        for i in range(3):
            for j in range(3):
                for k in range(j, 3):
                    got = total([inverse[i][l] * lowered[l][j][k] for l in range(3)])
                    raised[i][j][k] = raised[i][k][j] = got
        contracted = [trace_with(inverse, raised[i]) for i in range(3)]

        def hessian_trace(q):
            return (
                inverse[0][0] * seconds[q, 0]
                + inverse[1][1] * seconds[q, 3]
                + inverse[2][2] * seconds[q, 5]
                + 2.0 * (inverse[0][2] * seconds[q, 2] + inverse[1][2] * seconds[q, 4])
            )

        def second_cov(q, slope):
            bent = [total([raised[k][i][j] * slope[k] for k in range(3)]) for i, j in INDEX_PAIRS]
            return symmetric(
                [-bent[s] if s == 1 else seconds[q, s] - bent[s] for s in range(len(bent))]
            )

        chi_cov = second_cov(0, chi_grad)
        chi_lap = trace_with(inverse, chi_cov)
        raised_chi = [dot(inverse[i], chi_grad) for i in range(3)]
        chi_square = dot(raised_chi, chi_grad)
        cross_term = dot(raised_chi, lapse_grad)
        half_chi = 0.5 * over_chi
        plain_cov = second_cov(7, lapse_grad)
        lapse_cov = symmetric(
            [
                plain_cov[i][j]
                + (
                    chi_grad[i] * lapse_grad[j]
                    + chi_grad[j] * lapse_grad[i]
                    - metric[i][j] * cross_term
                )
                * half_chi
                for i, j in INDEX_PAIRS
            ]
        )
        lapse_lap = conformal * trace_with(inverse, lapse_cov)

        mixed = [
            [[dot(inverse[l], lowered[k][j]) for j in range(3)] for k in range(3)]
            for l in range(3)
        ]
        quarter_sq = half_chi * half_chi
        metric_factor = chi_lap * half_chi - 3.0 * chi_square * quarter_sq
        ricci = []
        for i, j in INDEX_PAIRS:
            second_part = -0.5 * hessian_trace(1 + slot_of(i, j))
            connection_part = 0.5 * total(
                [metric[k][i] * grad[18 + k][j] + metric[k][j] * grad[18 + k][i] for k in range(3)]
            )
            contracted_part = 0.5 * total(
                [contracted[k] * (lowered[i][j][k] + lowered[j][i][k]) for k in range(3)]
            )
            if i == j:
                quadratic = total(
                    [
                        raised[k][l][i] * (2.0 * mixed[l][i][k] + mixed[l][k][i])
                        for k in range(3)
                        for l in range(3)
                    ]
                )
            else:
                quadratic = total(
                    [
                        raised[k][l][i] * (mixed[l][j][k] + mixed[l][k][j])
                        + raised[k][l][j] * mixed[l][i][k]
                        for k in range(3)
                        for l in range(3)
                    ]
                )
            conformal_part = (
                chi_cov[i][j] * half_chi
                + metric[i][j] * metric_factor
                - chi_grad[i] * chi_grad[j] * quarter_sq
            )
            ricci.append(
                second_part + connection_part + contracted_part + quadratic + conformal_part
            )
        ricci = symmetric(ricci)
        ricci_scalar = conformal * trace_with(inverse, ricci)
        stress_trace = conformal * trace_with(inverse, stress)

        up_a = [
            [total([inverse[i][k] * traceless[k][j] for k in range(3)]) for j in range(3)]
            for i in range(3)
        ]
        raised_a = symmetric(
            [total([up_a[i][l] * inverse[j][l] for l in range(3)]) for i, j in INDEX_PAIRS]
        )
        a_square = trace_with(traceless, raised_a)
        shift_div = shift_grad[0][0] + shift_grad[1][1] + shift_grad[2][2]
        two_thirds_div = (2.0 / 3.0) * shift_div

        def finish(q, rate):
            rate = rate + dot(shift, grad[q]) + damped[q]
            st_rate[q, pl.ds(base, half), :] = rate

        finish(0, (2.0 / 3.0) * conformal * (lapse * trace_k - shift_div))
        finish(7, -2.0 * lapse * extrinsic)
        for i in range(3):
            finish(8 + i, 0.75 * connection[i] - SHIFT_DAMPING * shift[i])
        finish(
            11,
            lapse
            * (
                a_square
                + trace_k * trace_k * (1.0 / 3.0)
                + FOUR_PI * (stress_trace + density)
                + KAPPA_ONE * theta
            )
            - lapse_lap,
        )
        source = symmetric(
            [
                lapse * (ricci[i][j] - 2.0 * FOUR_PI * stress[i][j]) - lapse_cov[i][j]
                for i, j in INDEX_PAIRS
            ]
        )
        third_trace = trace_with(inverse, source) * (1.0 / 3.0)
        for s, (i, j) in enumerate(INDEX_PAIRS):
            finish(
                1 + s,
                total(
                    [
                        metric[i][k] * shift_grad[j][k] + metric[j][k] * shift_grad[i][k]
                        for k in range(3)
                    ]
                )
                - metric[i][j] * two_thirds_div
                - 2.0 * lapse * traceless[i][j],
            )
            product = total([traceless[i][k] * up_a[k][j] for k in range(3)])
            finish(
                12 + s,
                total(
                    [
                        traceless[i][k] * shift_grad[j][k] + traceless[j][k] * shift_grad[i][k]
                        for k in range(3)
                    ]
                )
                - traceless[i][j] * two_thirds_div
                + conformal * (source[i][j] - metric[i][j] * third_trace)
                + lapse * (trace_k * traceless[i][j] - 2.0 * product),
            )
        for i in range(3):
            bracket = (
                trace_with(raised_a, raised[i])
                - 1.5 * dot(raised_a[i], chi_grad) * over_chi
                - dot(inverse[i], [2.0 * grad[11][j] + grad[21][j] for j in range(3)]) * (1.0 / 3.0)
                - 2.0 * FOUR_PI * dot(inverse[i], momentum)
            )
            spread = [
                seconds[8, 0] + seconds[10, 2],
                seconds[9, 3] + seconds[10, 4],
                seconds[8, 2] + seconds[9, 4] + seconds[10, 5],
            ]
            finish(
                18 + i,
                contracted[i] * two_thirds_div
                - total([contracted[j] * shift_grad[j][i] for j in range(3)])
                + hessian_trace(8 + i)
                + dot(inverse[i], spread) * (1.0 / 3.0)
                - 2.0 * dot(raised_a[i], lapse_grad)
                + 2.0
                * lapse
                * (bracket - KAPPA_ONE * (connection[i] - contracted[i])),
            )
        finish(
            21,
            0.5
            * lapse
            * (
                ricci_scalar
                - a_square
                + (2.0 / 3.0) * trace_k * trace_k
                - 4.0 * FOUR_PI * density
            )
            - 2.0 * KAPPA_ONE * lapse * theta,
        )

    for index in range(own):
        pair_step(index)


def late_kernel(
    place, cells, zst, zfl, x_first, y_first, x_second, y_second, c_first, c_second, line_two, line_top,
    st_rate, hydro_rate, slopes, electric, st_out, fl_out,
):
    halo = Halo(
        place, cells, zst, zfl, x_first, y_first, x_second, y_second, c_first, c_second
    )
    x_below, x_above = halo.x_below, halo.x_above
    t, fields, half, own = halo.t, halo.fields, halo.half, halo.own
    inner, span = halo.inner, halo.span

    top = jnp.maximum(line_top[...], line_two[...])
    for lines in (c_first, c_second):
        top = jnp.maximum(top, lines[CORNER_TILES - 1, TOP_ROW : TOP_ROW + 1, :])
    dt = COURANT / top

    for p in inner:
        place = slice((p - 1) * half, p * half)
        mixed = []
        for q in range(CURVED):
            s_m, s_c, s_p = (
                halo.beside(q, n) if 1 <= n <= own else halo.corner(q, n) for n in (p - 1, p, p + 1)
            )
            slope = slopes[q, p - 1]
            slope_side = first_diff(s_m, t.odd_swapped(s_m, s_c), t.odd_swapped(s_c, s_p), s_p)
            mixed.append(
                first_diff(
                    t.y_down(slope, slope_side, 2),
                    t.y_down(slope, slope_side, 1),
                    t.y_up(slope, slope_side, 1),
                    t.y_up(slope, slope_side, 2),
                )
            )
        conformal, lapse = halo.main(0, p), halo.main(7, p)
        metric = [halo.main(1 + s, p) for s in range(6)]
        inverse = inverse_metric(symmetric(metric))
        half_chi = 0.5 / conformal
        cross = inverse[0][1]
        chi_trace = 2.0 * cross * mixed[0] * half_chi
        ricci = [metric[s] * chi_trace - cross * mixed[1 + s] for s in range(6)]
        ricci[1] = ricci[1] + mixed[0] * half_chi
        source = [lapse * r for r in ricci]
        source[1] = source[1] - mixed[7]
        third_trace = trace_with(inverse, symmetric(source)) * (1.0 / 3.0)
        extra = {
            11: -2.0 * conformal * cross * mixed[7],
            21: 0.5 * lapse * conformal * trace_with(inverse, symmetric(ricci)),
        }
        for s in range(6):
            extra[12 + s] = conformal * (source[s] - metric[s] * third_trace)
        for i in range(3):
            extra[18 + i] = 2.0 * cross * mixed[8 + i] + (1.0 / 3.0) * (
                inverse[i][0] * mixed[9] + inverse[i][1] * mixed[8]
            )
        for q in range(fields):
            rate = st_rate[q, place, :]
            if q in extra:
                rate = rate + extra[q]
            st_out[q, place, :] = halo.main(q, p) + dt * rate

    end = own + 1
    ends = (0, end)
    bx_face, by_face, bz_face = ({p: halo.corner(fields + 5 + i, p) for p in ends} for i in range(3))
    layers = {p: halo.corner_layers(p) for p in ends}
    bx_face[end] = layers[end]
    by_face[0] = jnp.where(t.slot < 2, layers[0], by_face[0])
    centred = [{}, {}, {}]
    for p in ends:
        following = halo.beside(fields + 5, 1) if p == 0 else bx_face[p]
        edge_cells = x_below if p == 0 else x_above
        dx = 0.5 * (t.odd_swapped(bx_face[p], following) - bx_face[p])
        dy = 0.5 * (t.y_up(by_face[p], edge_cells[fields + 6], 1) - by_face[p])
        centred[0][p] = bx_face[p] + dx
        centred[1][p] = by_face[p] + dy
        centred[2][p] = bz_face[p] - (dx + dy)
    corners = [{p: halo.corner(q, p) for p in ends} for q in [0, 7] + list(range(fields, fields + 5))]
    found = primitives(
        half, [(0, p) for p in ends], [[c] for c in corners[2:]], [[c] for c in centred],
        [corners[0]], [corners[1]], 2,
    )
    ez_h = [found[0, 0][10]] + [electric[own + p] for p in inner] + [found[0, end][10]]
    ez_x_h = [None] + [ez_h[p] + t.odd_swapped(ez_h[p - 1], ez_h[p]) for p in span[1:]]
    ez_x = [None] + [electric[p - 1] for p in span[1:]]
    edge_z = [None] + [ez_x[p] + t.y_down(ez_x[p], ez_x_h[p], 1) for p in span[1:]]
    quarter = 0.25 * dt
    for p in inner:
        place = slice((p - 1) * half, p * half)
        edge_z_h = ez_x_h[p] + t.y_down(ez_x_h[p], ez_x[p], 1)
        for q in range(5):
            fl_out[q, place, :] = halo.main(fields + q, p) + dt * hydro_rate[q, place, :]
        x_rate = hydro_rate[5, place, :] - (t.y_up(edge_z[p], edge_z_h, 1) - edge_z[p])
        y_rate = hydro_rate[6, place, :] + (t.odd(edge_z[p], edge_z[p + 1]) - edge_z[p])
        z_rate = hydro_rate[7, place, :]
        for i, rate in enumerate((x_rate, y_rate, z_rate)):
            fl_out[5 + i, place, :] = halo.main(fields + 5 + i, p) + quarter * rate


def per_device(spacetime, fluid):
    fields, cx, cy, cz = spacetime.shape
    rows = cx * cy
    st = spacetime.reshape(fields, rows, cz)
    fl = fluid.reshape(FLUID, rows, cz)
    sizes = [lax.axis_size(a) for a in ("gx", "gy", "gz")]
    tile = (2 * cy, cz)
    f32 = jnp.float32

    def shape(*dims):
        return jax.ShapeDtypeStruct(dims, f32)

    def beyond(cells):
        n = sizes[2]
        after = lax.ppermute(cells, "gz", [((i + 1) % n, i) for i in range(n)])
        if n == 2:
            return after
        before = lax.ppermute(cells, "gz", [(i, (i + 1) % n) for i in range(n)])
        lane = lax.broadcasted_iota(jnp.int32, cells.shape, 2)
        return jnp.where(lane < cz // 2, after, before)

    params = pltpu.CompilerParams(vmem_limit_bytes=48 * 1024 * 1024)
    zst, zfl = beyond(st), beyond(fl)
    cells = jnp.concatenate([st, fl], axis=0)
    face = shape(face_tiles(fields), *tile)
    corner = shape(CORNER_TILES, *tile)
    lane_row = shape(1, cz)
    place = jnp.stack([lax.rem(lax.axis_index(axis), 2) for axis in ("gx", "gy")])
    place = place.astype(jnp.int32)
    scalars = pl.BlockSpec(memory_space=pltpu.SMEM)

    def call(kernel, outs, name, operands, scratch=()):
        return pl.pallas_call(
            kernel,
            out_shape=outs,
            in_specs=[scalars] + [pl.BlockSpec(memory_space=pltpu.VMEM)] * len(operands),
            scratch_shapes=scratch,
            compiler_params=params,
            name=name,
        )(place, *operands)

    def trade(cells, axis, first):
        n = lax.axis_size(axis)
        step = [-1, 1] if first else [1, -1]
        return lax.ppermute(cells, axis, [(i, (i + step[i % 2]) % n) for i in range(n)])

    def two_away(cells, axis):
        n = lax.axis_size(axis)
        return lax.ppermute(cells, axis, [(i, (i + 2) % n) for i in range(n)]) if n == 4 else cells

    short = sizes[0] <= 4 and sizes[1] <= 4 and sizes[2] <= 2
    x_first, x_second, y_first, y_second, top = call(
        pack_kernel, [face] * 4 + [lane_row], "pack", (cells, zst, zfl)
    )
    x_first = trade(x_first, "gx", True)
    y_first = trade(y_first, "gy", True)
    x_second = trade(x_second, "gx", False)
    y_second = trade(y_second, "gy", False)
    top_two = two_away(top, "gx")
    c_first, c_second, line_top = call(
        relay_kernel,
        [corner, corner, lane_row],
        "relay",
        (x_first, x_second, y_first, top, top_two),
    )
    c_first = trade(c_first, "gy", True)
    c_second = trade(c_second, "gy", False)
    if short:
        line_two = two_away(line_top, "gy")
    else:
        line_two = lax.pmax(line_top, ("gx", "gy", "gz"))
    own = cx // 2
    arrived = (cells, zst, zfl, x_first, y_first, x_second, y_second)
    early = call(
        early_kernel,
        [
            shape(*st.shape),
            shape(FLUID, rows, cz),
            shape(CURVED, own, *tile),
            shape(2 * own + 1, *tile),
        ],
        "early",
        arrived,
        [
            pltpu.VMEM((fields, own + 4) + tile, f32),
            pltpu.VMEM((fields, own) + tile, f32),
            pltpu.VMEM((fields, own) + tile, f32),
            pltpu.VMEM((CURVED, own + 2) + tile, f32),
            pltpu.VMEM((CURVED, own) + tile, f32),
            pltpu.VMEM((fields, 3) + tile, f32),
            pltpu.VMEM((CURVED, 6) + tile, f32),
            pltpu.VMEM((fields,) + tile, f32),
            pltpu.VMEM((own, 11) + tile, f32),
        ],
    )
    st_next, fl_next = call(
        late_kernel,
        [shape(*st.shape), shape(*fl.shape)],
        "late",
        (*arrived, c_first, c_second, line_two, line_top, *early),
    )
    return st_next.reshape(spacetime.shape), fl_next.reshape(fluid.shape)


def solution(mesh):
    spec = P(None, "gx", "gy", "gz")
    return jax.shard_map(
        per_device, mesh=mesh, in_specs=(spec, spec), out_specs=(spec, spec), check_vma=False
    )
```

```python
import functools
import math

import jax
import jax.numpy as jnp
from jax import lax
from jax.experimental import pallas as pl
from jax.experimental.pallas import tpu as pltpu
from jax.sharding import PartitionSpec as P

RECOVERY_STEPS = 4
INDEX_PAIRS = ((0, 0), (0, 1), (0, 2), (1, 1), (1, 2), (2, 2))
COURANT = 0.25
DISSIPATION = 0.2
KAPPA_ONE = 0.02
SHIFT_DAMPING = 1.0
SPEED_CAP = 0.99
PRESSURE_FLOOR = 0.01
FOUR_PI = 4.0 * math.pi

BATCH = 6
CURVED = 11
FLUID = 8


def total(pieces):
    summed = pieces[0]
    for member in pieces[1:]:
        summed = summed + member
    return summed


def dot(first_vec, second_vec):
    return total([first_vec[i] * second_vec[i] for i in range(3)])


def slot_of(i, j):
    return INDEX_PAIRS.index((min(i, j), max(i, j)))


def symmetric(entries):
    return [[entries[slot_of(i, j)] for j in range(3)] for i in range(3)]


def trace_with(inverse, tensor):
    return (
        inverse[0][0] * tensor[0][0]
        + inverse[1][1] * tensor[1][1]
        + inverse[2][2] * tensor[2][2]
        + 2.0
        * (
            inverse[0][1] * tensor[0][1]
            + inverse[0][2] * tensor[0][2]
            + inverse[1][2] * tensor[1][2]
        )
    )


def inverse_metric(metric):
    cofactor = [
        metric[1][1] * metric[2][2] - metric[1][2] * metric[1][2],
        metric[0][2] * metric[1][2] - metric[0][1] * metric[2][2],
        metric[0][1] * metric[1][2] - metric[0][2] * metric[1][1],
        metric[0][0] * metric[2][2] - metric[0][2] * metric[0][2],
        metric[0][1] * metric[0][2] - metric[0][0] * metric[1][2],
        metric[0][0] * metric[1][1] - metric[0][1] * metric[0][1],
    ]
    determinant = (
        metric[0][0] * cofactor[0] + metric[0][1] * cofactor[1] + metric[0][2] * cofactor[2]
    )
    over = 1.0 / determinant
    return symmetric([c * over for c in cofactor])


class Tile:
    def __init__(self, cy, cz):
        self.cy, self.rows, self.lanes = cy, 2 * cy, cz
        shape = (self.rows, cz)
        self.row = lax.broadcasted_iota(jnp.int32, shape, 0)
        self.lane = lax.broadcasted_iota(jnp.int32, shape, 1)
        self.slot = lax.rem(self.row, cy)

    def turn(self, tile, amount):
        amount = amount % self.rows
        return tile if amount == 0 else pltpu.roll(tile, amount, 0)

    def spin(self, tile, amount):
        amount = amount % self.lanes
        return tile if amount == 0 else pltpu.roll(tile, amount, 1)

    def swap(self, tile):
        return self.turn(tile, self.cy)

    def odd(self, a, b):
        return self.turn(jnp.where(self.row < self.cy, b, a), self.cy)

    def odd_swapped(self, a, b):
        return self.turn(jnp.where(self.row < self.cy, a, b), self.cy)

    def y_up(self, main, beyond, k):
        return self.turn(jnp.where(self.slot < k, beyond, main), -k)

    def y_down(self, main, beyond, k):
        return self.turn(jnp.where(self.slot >= self.cy - k, beyond, main), k)

    def z_up(self, main, beyond, k):
        return self.spin(jnp.where(self.lane < k, beyond, main), -k)

    def z_down(self, main, beyond, k):
        return self.spin(jnp.where(self.lane >= self.lanes - k, beyond, main), k)

    def corner_rows(self, side, turn):
        places = ((0, 2), (self.cy - 1, self.cy + 1))[side]
        first, second = [(place + turn) % self.rows for place in places]
        return (self.row == first) | (self.row == second)

    def join_low(self, u, v):
        return jnp.where(self.slot < 2, self.swap(u), self.turn(v, 2))

    def join_high(self, u, v):
        return jnp.where(self.slot >= self.cy - 2, self.swap(u), self.turn(self.swap(v), -2))

    def part_first(self, from_above, from_below):
        return jnp.where(self.slot < 2, from_above, from_below)

    def part_second(self, from_above, from_below):
        return self.turn(jnp.where(self.slot < 2, from_below, from_above), 2)


def edge_list(tiles):
    fields = next(n for n in range(tiles) if face_tiles(n) == tiles)
    return list(range(CURVED)) + list(range(fields, fields + FLUID))


CORNER_TURNS = (0, 1, 4, 5)
CORNER_TILES = CURVED + FLUID // 4 + 1
TOP_ROW = 6


def face_tiles(fields):
    return fields + FLUID + len(pairs_of(third_list(fields))) + 1


def third_list(fields):
    return list(range(fields + 1))


def pairs_of(items):
    return [(items[i], items[min(i + 1, len(items) - 1)]) for i in range(0, len(items), 2)]


def top_speed(st):
    inverse = inverse_metric(symmetric([st[1 + s] for s in range(6)]))
    scale = 2.0 * st[7] * st[0]
    speeds = [jnp.abs(st[8 + d]) + jnp.sqrt(scale * inverse[d][d]) for d in range(3)]
    top = jnp.maximum(jnp.maximum(speeds[0], speeds[1]), speeds[2])
    return jnp.max(jnp.max(top, axis=1, keepdims=True), axis=0, keepdims=True)


class Chosen:
    def __init__(self, first, second, swapped):
        self.first, self.second, self.swapped, self.shape = first, second, swapped, first.shape

    def __getitem__(self, key):
        return jnp.where(self.swapped, self.second[key], self.first[key])


class Sent:
    def __init__(self, first, second, swapped):
        self.first, self.second, self.swapped, self.shape = first, second, swapped, first.shape

    def put(self, key, lower, upper):
        self.first[key] = jnp.where(self.swapped, upper, lower)
        self.second[key] = jnp.where(self.swapped, lower, upper)


def even_places(place):
    return [place[n] > 0.5 for n in range(2)]


def pack_kernel(place, cells, zst, zfl, *outs):
    fields, rows, lanes = zst.shape
    st, fl = cells.at[0:fields], cells.at[fields : fields + FLUID]
    cy = rows // 4
    t = Tile(cy, lanes)
    x_first, x_second, y_first, y_second, top_out = outs
    half = t.rows
    even_x, even_y = even_places(place)
    to_x, to_y = Sent(x_first, x_second, even_x), Sent(y_first, y_second, even_y)

    def own(ref, q):
        return [ref[q, 0:half, :], ref[q, half : 2 * half, :]]

    tiles, beyond = [], []
    for q in range(fields):
        tiles.append(own(st, q))
        beyond.append(own(zst, q) if q < CURVED else None)
    for q in range(FLUID):
        tiles.append(own(fl, q))
        beyond.append(own(zfl, q))

    packed = [None] * 4
    place_count = 0
    for q, (first, second) in enumerate(tiles):
        to_x.put(q, first, second)
        to_y.put(q, t.join_low(first, second), t.join_high(first, second))
        if beyond[q] is not None:
            zf, zs = beyond[q]
            for m, piece in enumerate((zf, zs, t.join_low(zf, zs), t.join_high(zf, zs))):
                piece = t.spin(piece, 4 * place_count + 2)
                packed[m] = (
                    piece if place_count == 0 else jnp.where(t.lane < 4 * place_count, packed[m], piece)
                )
            place_count += 1
    for n, (a, b) in enumerate(pairs_of(third_list(fields))):
        slot = fields + FLUID + n
        xa, xb = (tiles[q if q < fields else fields + 5] for q in (a, b))
        to_x.put(
            slot,
            jnp.where(t.row < cy, xa[1], t.swap(xb[1])),
            jnp.where(t.row < cy, t.swap(xb[0]), xa[0]),
        )
        ya, yb = (tiles[q if q < fields else fields + 6] for q in (a, b))
        w = [t.swap(ya[0]), t.swap(ya[1]), t.swap(yb[0]), t.swap(yb[1])]
        s = t.slot
        low = jnp.where(s == 0, t.turn(w[2], -2), t.turn(w[3], -1))
        low = jnp.where(s == 2, w[0], jnp.where(s == 3, t.turn(w[1], 1), low))
        high = jnp.where(s == 3, t.turn(w[2], 2), t.turn(w[3], 1))
        high = jnp.where(s == 1, w[0], jnp.where(s == 0, t.turn(w[1], -1), high))
        to_y.put(slot, low, high)
    top = jnp.maximum(top_speed(st), top_speed(zst))
    top_out[...] = jnp.broadcast_to(top, top_out.shape)
    last = x_first.shape[0] - 1
    x_lanes = [jnp.where(t.lane < 4 * place_count, piece, top) for piece in packed[:2]]
    y_lanes = [jnp.where(t.lane < 4 * place_count, piece, top) for piece in packed[2:]]
    to_x.put(last, *x_lanes)
    to_y.put(last, *y_lanes)


def relay_kernel(place, x_first, x_second, y_first, top, top_two, c_first, c_second, line_top):
    cy, lanes = x_first.shape[1] // 2, x_first.shape[2]
    t = Tile(cy, lanes)
    even_x, even_y = even_places(place)
    x_below, x_above = Chosen(x_first, x_second, even_x), Chosen(x_second, x_first, even_x)
    to_y = Sent(c_first, c_second, even_y)
    last = x_first.shape[0] - 1
    line = jnp.maximum(top[...], top_two[...])
    for beside in (x_first, x_second, y_first):
        line = jnp.maximum(line, beside[last, 0:1, lanes - 1 : lanes])
    line_top[...] = line
    edge = edge_list(x_below.shape[0])
    for q in range(CURVED):
        below, above = x_below[q], x_above[q]
        to_y.put(q, t.join_low(below, above), t.join_high(below, above))
    for n in range(0, FLUID, 4):
        low, high = None, None
        for turn, q in zip(CORNER_TURNS, edge[CURVED + n : CURVED + n + 4]):
            below, above = x_below[q], x_above[q]
            below, above = (t.turn(j(below, above), turn) for j in (t.join_low, t.join_high))
            if low is None:
                low, high = below, above
            else:
                low = jnp.where(t.corner_rows(0, turn), below, low)
                high = jnp.where(t.corner_rows(1, turn), above, high)
        to_y.put(CURVED + n // 4, low, high)
    along_x, along_y = edge[CURVED + 5], edge[CURVED + 6]
    low = t.join_low(x_below[along_y], x_above[along_y])
    high = t.join_high(x_below[along_x], x_above[along_x])
    low, high = (jnp.where(t.row == TOP_ROW, line, tile) for tile in (low, high))
    to_y.put(CORNER_TILES - 1, low, high)


def limited(a, b):
    return jnp.maximum(jnp.minimum(a, b), 0.0) + jnp.minimum(jnp.maximum(a, b), 0.0)


def recover(conserved, magnetic):
    density = conserved[0]
    momenta = conserved[1:4]
    energy = conserved[4] + density
    mom_sq = dot(momenta, momenta)
    mag_sq = dot(magnetic, magnetic)
    cross = dot(momenta, magnetic)
    cross_sq = cross * cross

    def state(z):
        grown = z + mag_sq
        over = 1.0 / (z * grown)
        speed_sq = (mom_sq * z * z + cross_sq * (2.0 * z + mag_sq)) * over * over
        kept = 1.0 - jnp.minimum(speed_sq, SPEED_CAP)
        rest = density * jnp.sqrt(kept)
        return kept, rest, 0.5 * (z * kept - rest), grown * over

    z = jnp.maximum(energy - 0.5 * mag_sq, density)
    for _ in range(RECOVERY_STEPS):
        kept, rest, pressure, over_z = state(z)
        residual = (
            z
            + mag_sq
            - pressure
            - 0.5 * mag_sq * kept
            - 0.5 * cross_sq * over_z * over_z
            - energy
        )
        z = jnp.maximum(z - residual / (1.0 - 0.5 * kept), density)
    kept, rest, pressure, over_z = state(z)
    pressure = jnp.maximum(pressure, PRESSURE_FLOOR * rest)
    scale = lax.rsqrt(kept) / (z + mag_sq)
    along = cross * over_z
    four_vel = [scale * (momenta[i] + along * magnetic[i]) for i in range(3)]
    return [rest, pressure] + four_vel


def stress_parts(rest, pressure, u, magnetic):
    lorentz_sq = 1.0 + dot(u, u)
    over = lax.rsqrt(lorentz_sq)
    over_sq = over * over
    time_b = dot(u, magnetic)
    grown_b = [magnetic[i] + time_b * u[i] for i in range(3)]
    b_square = (dot(magnetic, magnetic) + time_b * time_b) * over_sq
    enthalpy = rest + 2.0 * pressure
    inertia = enthalpy + b_square
    return lorentz_sq, over, over_sq, time_b, grown_b, b_square, enthalpy, inertia


def face_state(rest, pressure, u, magnetic, d):
    lorentz_sq, over, over_sq, time_b, grown_b, b_square, enthalpy, inertia = stress_parts(
        rest, pressure, u, magnetic
    )
    total_pressure = pressure + 0.5 * b_square
    lorentz = lorentz_sq * over
    density = rest * lorentz
    carried = inertia * lorentz
    time_over = time_b * over
    conserved = [density]
    conserved += [carried * u[j] - time_over * grown_b[j] for j in range(3)]
    conserved += [inertia * lorentz_sq - total_pressure - time_b * time_b - density]
    mass_flux = rest * u[d]
    flux = [mass_flux]
    pushed = inertia * u[d]
    b_over = grown_b[d] * over_sq
    for j in range(3):
        flux_j = pushed * u[j] - b_over * grown_b[j]
        flux.append(flux_j + total_pressure if j == d else flux_j)
    flux.append(carried * u[d] - time_over * grown_b[d] - mass_flux)
    ratio = 1.0 / (enthalpy * inertia)
    sound_sq = 2.0 * pressure * inertia * ratio
    alfven_sq = b_square * enthalpy * ratio
    fast_sq = sound_sq + alfven_sq - sound_sq * alfven_sq
    slow = 1.0 - fast_sq
    velocity = u[d] * over
    rest_part = 1.0 - dot(u, u) * over_sq * fast_sq
    spread = jnp.sqrt(fast_sq * over_sq * (rest_part - velocity * velocity * slow))
    fastest = (jnp.abs(velocity * slow) + spread) / rest_part
    return conserved, flux, fastest


def face_flux(left, right, normal, weight, d):
    sides = []
    for state in (left, right):
        magnetic = [normal if i == d else state[5 + i] for i in range(3)]
        sides.append(face_state(state[0], state[1], state[2:5], magnetic, d))
    (cons_l, flux_l, fast_l), (cons_r, flux_r, fast_r) = sides
    signal = jnp.maximum(fast_l, fast_r)
    scale = 0.5 * weight
    return [scale * (flux_l[q] + flux_r[q] - signal * (cons_r[q] - cons_l[q])) for q in range(5)]


def volume_over(conformal):
    return conformal * jnp.sqrt(conformal)


def first_diff(down_two, down, up, up_two):
    return (8.0 / 12.0) * (up - down) + (1.0 / 12.0) * (down_two - up_two)


class Halo:
    def __init__(self, place, cells, zst, zfl, x_first, y_first, x_second, y_second, *corners):
        self.fields, self.block, self.lanes = zst.shape
        even_x, even_y = even_places(place)
        x_below, x_above = Chosen(x_first, x_second, even_x), Chosen(x_second, x_first, even_x)
        y_below, y_above = Chosen(y_first, y_second, even_y), Chosen(y_second, y_first, even_y)
        if corners:
            c_first, c_second = corners
            self.c_below = Chosen(c_first, c_second, even_y)
            self.c_above = Chosen(c_second, c_first, even_y)
        self.st = cells.at[0 : self.fields]
        self.fl = cells.at[self.fields : self.fields + FLUID]
        self.zst, self.zfl = zst, zfl
        self.x_below, self.x_above = x_below, x_above
        self.y_below, self.y_above = y_below, y_above
        self.cy = self.block // 4
        self.t = Tile(self.cy, self.lanes)
        self.half = self.t.rows
        self.own = self.block // self.half
        self.inner = range(1, self.own + 1)
        self.span = range(self.own + 2)
        self.edge = edge_list(x_below.shape[0])
        self.last = x_below.shape[0] - 1

    def rows_of(self, ref, q, p):
        return ref[q, (p - 1) * self.half : p * self.half, :]

    def main(self, q, p):
        if q < self.fields:
            return self.rows_of(self.st, q, p)
        return self.rows_of(self.fl, q - self.fields, p)

    def beyond(self, q, p):
        if q < self.fields:
            return self.rows_of(self.zst, q, p)
        return self.rows_of(self.zfl, q - self.fields, p)

    def part(self, second):
        return self.t.part_second if second else self.t.part_first

    def beside(self, q, p):
        return self.part(p == 2)(self.y_above[q], self.y_below[q])

    def third_place(self, q):
        return self.fields + FLUID + q // 2, q % 2

    def x_third(self, q, upper):
        tile, which = self.third_place(q)
        found = self.x_above[tile] if upper else self.x_below[tile]
        return self.t.swap(found) if which else found

    def y_third(self, q, p):
        t = self.t
        tile, which = self.third_place(q)
        turn_above, turn_below = ((0, 0), (-1, 1), (2, -2), (1, -1))[2 * which + p - 1]
        above, below = t.turn(self.y_above[tile], turn_above), t.turn(self.y_below[tile], turn_below)
        return jnp.where(t.slot == 2, above, below)

    def z_place(self, q):
        return 4 * self.edge.index(q) + 2

    def x_beyond(self, q, upper):
        tile = self.x_above[self.last] if upper else self.x_below[self.last]
        return self.t.spin(tile, -self.z_place(q))

    def y_beyond(self, q, p):
        return self.t.spin(self.beside(self.last, p), -self.z_place(q))

    def corner(self, q, p):
        place, turn = q, 0
        if q >= CURVED:
            n = q - self.fields
            place, turn = CURVED + n // 4, CORNER_TURNS[n % 4]
        above, below = self.t.turn(self.c_above[place], -turn), self.t.turn(self.c_below[place], -turn)
        return self.part(p > 0)(above, below)

    def corner_layers(self, p):
        place = CORNER_TILES - 1
        return self.part(p > 0)(self.c_above[place], self.c_below[place])

    def plane(self, q):
        inner = self.inner
        return (
            [self.x_below[q]] + [self.main(q, p) for p in inner] + [self.x_above[q]],
            [None] + [self.beside(q, p) for p in inner] + [None],
            [self.x_beyond(q, False)]
            + [self.beyond(q, p) for p in inner]
            + [self.x_beyond(q, True)],
            [None] + [self.y_beyond(q, p) for p in inner] + [None],
        )


def weigh(chi_face, alpha_face):
    shrink = volume_over(chi_face)
    return shrink, alpha_face / shrink


def primitives(half, spots, cons, centred, chi, alpha, batch):
    found = {}
    for start in range(0, len(spots), batch):
        group = spots[start : start + batch]

        def gather(planes):
            return jnp.concatenate([planes[k][p] for k, p in group], axis=0)

        shrink = volume_over(gather(chi))
        mag_raw = [gather(centred[i]) for i in range(3)]
        mag = [m * shrink for m in mag_raw]
        values = recover([gather(c) * shrink for c in cons], mag)
        u = values[2:5]
        factor = gather(alpha) * lax.rsqrt(1.0 + dot(u, u))
        field = [
            factor * (u[(i + 2) % 3] * mag_raw[(i + 1) % 3] - u[(i + 1) % 3] * mag_raw[(i + 2) % 3])
            for i in range(3)
        ]
        for n, spot in enumerate(group):
            found[spot] = [value[n * half : (n + 1) * half] for value in values + mag + field]
    return found


def ring_fluxes(prims, chi, alpha, normals, d, up, down):
    found = []
    for here, there in ((0, 1), (1, 0)):
        left, right = [], []
        for a, b in zip(prims[here], prims[there]):
            below = down(a, b, 1)
            middle = a - below
            left.append(below + 0.5 * limited(below - down(a, b, 2), middle))
            right.append(a - 0.5 * limited(middle, up(a, b, 1) - a))
        shrink, weight = weigh(
            0.5 * (chi[here] + down(chi[here], chi[there], 1)),
            0.5 * (alpha[here] + down(alpha[here], alpha[there], 1)),
        )
        found.append(face_flux(left, right, normals[here] * shrink, weight, d))
    return [a - up(a, b, 1) for a, b in zip(*found)]


def early_kernel(
    place, cells, zst, zfl, x_first, y_first, x_second, y_second,
    st_rate, hydro_rate, slopes, electric, pairs, sides, thirds, pairs_z, sides_z, grads, seconds, damped, tensors,
):
    halo = Halo(place, cells, zst, zfl, x_first, y_first, x_second, y_second)
    x_below, x_above = halo.x_below, halo.x_above
    t, fields, half, own, cy = halo.t, halo.fields, halo.half, halo.own, halo.cy
    st, fl, inner = halo.st, halo.fl, halo.inner

    for q in range(fields):
        pairs[q, 0] = halo.x_third(q, False)
        pairs[q, 1] = x_below[q]
        for p in inner:
            pairs[q, 1 + p] = halo.main(q, p)
            sides[q, p - 1] = halo.beside(q, p)
            thirds[q, p - 1] = halo.y_third(q, p)
        pairs[q, 2 + own] = x_above[q]
        pairs[q, 3 + own] = halo.x_third(q, True)
        if q < CURVED:
            pairs_z[q, 0] = halo.x_beyond(q, False)
            pairs_z[q, own + 1] = halo.x_beyond(q, True)
            for p in inner:
                pairs_z[q, p] = halo.beyond(q, p)
                sides_z[q, p - 1] = halo.y_beyond(q, p)

    span = halo.span
    face = [halo.plane(fields + 5 + i) for i in range(3)]

    def halves(kind, p):
        own_x, own_y, own_z = (f[kind][p] for f in face)
        pair = kind in (0, 2)
        known_x = pair or p < own
        last = kind == 0 and p == own + 1
        if pair:
            next_x = halo.x_third(fields, True) if last else face[0][kind][min(p + 1, own + 1)]
            next_x = t.odd(own_x, next_x)
        else:
            next_x = t.odd_swapped(own_x, face[0][kind][p + 1] if known_x else own_x)
        dx = 0.5 * (next_x - own_x)
        dz = 0.5 * (t.z_up(own_z, face[2][kind ^ 2][p], 1) - own_z)
        inside = 1 <= p <= own
        if not pair:
            here = jnp.where(t.slot == 2, halo.y_third(fields, p), own_y) if kind == 1 else own_y
            next_y = t.y_up(here, face[1][kind ^ 1][p], 1)
        else:
            next_y = t.y_up(own_y, face[1][kind ^ 1][p] if inside else own_y, 1)
        dy = 0.5 * (next_y - own_y)
        if pair and not inside:
            dy = jnp.where(t.slot == cy - 1, -(dx + dz), dy)
        if not pair and not known_x:
            dx = jnp.where(t.row < cy, -(dy + dz), dx)
        return own_x + dx, own_y + dy, own_z + dz

    spots = [(0, p) for p in span] + [(1, p) for p in inner]
    spots += [(2, p) for p in span] + [(3, p) for p in inner]
    centred = [[[None] * (own + 2) for _ in range(4)] for _ in range(3)]
    for k, p in spots:
        for i, value in enumerate(halves(k, p)):
            centred[i][k][p] = value
    chi, alpha = halo.plane(0), halo.plane(7)
    found = primitives(
        half, spots, [halo.plane(fields + q) for q in range(5)], centred, chi, alpha, BATCH
    )

    lines = [[found[0, p][i] for p in span] for i in range(8)] + [chi[0], alpha[0]]
    odd_lines = [[t.odd(f[p], f[min(p + 1, own + 1)]) for p in span] for f in lines]
    fluxes = [None]
    for p in range(1, own + 2):
        left, right = [], []
        for f, o in zip(lines[:8], odd_lines):
            here = f[p] - o[p - 1]
            left.append(o[p - 1] + 0.5 * limited(o[p - 1] - f[p - 1], here))
            right.append(f[p] - 0.5 * limited(here, o[p] - f[p]))
        shrink, weight = weigh(
            0.5 * (lines[8][p] + odd_lines[8][p - 1]), 0.5 * (lines[9][p] + odd_lines[9][p - 1])
        )
        fluxes.append(face_flux(left, right, face[0][0][p] * shrink, weight, 0))
    for p in inner:
        changes = [
            ring_fluxes(
                [found[k, p][:8] for k in (0, kind)],
                [chi[k][p] for k in (0, kind)],
                [alpha[k][p] for k in (0, kind)],
                [face[d][k][p] for k in (0, kind)],
                d,
                up,
                down,
            )
            for d, kind, up, down in ((1, 1, t.y_up, t.y_down), (2, 2, t.z_up, t.z_down))
        ]
        for q in range(5):
            change = fluxes[p][q] - t.odd(fluxes[p][q], fluxes[p + 1][q])
            tensors[p - 1, 6 + q] = change + changes[0][q] + changes[1][q]
        rest, pressure = found[0, p][:2]
        u = found[0, p][2:5]
        parts = stress_parts(rest, pressure, u, found[0, p][5:8])
        lorentz_sq, over, over_sq, time_b, grown_b, b_square, enthalpy, inertia = parts
        total_pressure = pressure + 0.5 * b_square
        for s, (i, j) in enumerate(INDEX_PAIRS):
            value = inertia * u[i] * u[j] - over_sq * (grown_b[i] * grown_b[j])
            tensors[p - 1, s] = value + total_pressure if i == j else value

    ex, ey, ez = (
        [[found[k, p][8 + i] if (k, p) in found else None for p in span] for k in range(4)]
        for i in range(3)
    )
    ey_x = [
        [ey[k][p] + t.odd(ey[k][p - 1], ey[k][p]) if p else None for p in span] for k in (0, 2)
    ]
    edge_y = [None] + [ey_x[0][p] + t.z_down(ey_x[0][p], ey_x[1][p], 1) for p in span[1:]]
    for p in span[1:]:
        electric[p - 1] = ez[0][p] + t.odd(ez[0][p - 1], ez[0][p])
    for p in inner:
        electric[own + p] = ez[1][p]
        edge_y_z = ey_x[1][p] + t.z_down(ey_x[1][p], ey_x[0][p], 1)
        ex_y = ex[0][p] + t.y_down(ex[0][p], ex[1][p], 1)
        ex_y_h = ex[1][p] + t.y_down(ex[1][p], ex[0][p], 1)
        ex_y_z = ex[2][p] + t.y_down(ex[2][p], ex[3][p], 1)
        ex_y_hz = ex[3][p] + t.y_down(ex[3][p], ex[2][p], 1)
        edge_x = ex_y + t.z_down(ex_y, ex_y_z, 1)
        edge_x_h = ex_y_h + t.z_down(ex_y_h, ex_y_hz, 1)
        edge_x_z = ex_y_z + t.z_down(ex_y_z, ex_y, 1)
        place = slice((p - 1) * half, p * half)
        hydro_rate[5, place, :] = t.z_up(edge_y[p], edge_y_z, 1) - edge_y[p]
        hydro_rate[6, place, :] = edge_x - t.z_up(edge_x, edge_x_z, 1)
        hydro_rate[7, place, :] = (t.y_up(edge_x, edge_x_h, 1) - edge_x) - (
            t.odd(edge_y[p], edge_y[p + 1]) - edge_y[p]
        )

    def pair_step(index):
        p = index + 1
        base = index * half

        for q in range(fields):
            centre = pairs[q, p + 1]
            x_m3 = t.odd(pairs[q, p - 1], pairs[q, p])
            x_m2 = pairs[q, p]
            x_m1 = t.odd(pairs[q, p], centre)
            x_p1 = t.odd(centre, pairs[q, p + 2])
            x_p2 = pairs[q, p + 2]
            x_p3 = t.odd(pairs[q, p + 2], pairs[q, p + 3])
            side, third = sides[q, index], thirds[q, index]
            y_m1, y_m2 = t.y_down(centre, side, 1), t.y_down(centre, side, 2)
            y_p1, y_p2 = t.y_up(centre, side, 1), t.y_up(centre, side, 2)
            y_m3 = t.turn(
                jnp.where(t.slot >= cy - 2, side, jnp.where(t.slot == cy - 3, third, centre)), 3
            )
            y_p3 = t.turn(jnp.where(t.slot < 2, side, jnp.where(t.slot == 2, third, centre)), -3)
            beyond = zst[q, pl.ds(base, half), :]
            z_m1, z_m2, z_m3 = (t.z_down(centre, beyond, k) for k in (1, 2, 3))
            z_p1, z_p2, z_p3 = (t.z_up(centre, beyond, k) for k in (1, 2, 3))
            dx = first_diff(x_m2, x_m1, x_p1, x_p2)
            dy = first_diff(y_m2, y_m1, y_p1, y_p2)
            grads[q, 0] = dx
            if q < CURVED:
                slopes[q, index] = dx
            grads[q, 1] = dy
            grads[q, 2] = first_diff(z_m2, z_m1, z_p1, z_p2)
            near = [x_m1 + x_p1, y_m1 + y_p1, z_m1 + z_p1]
            far = [x_m2 + x_p2, y_m2 + y_p2, z_m2 + z_p2]
            outer = (x_m3 + x_p3) + (y_m3 + y_p3) + (z_m3 + z_p3)
            damped[q] = (DISSIPATION / 64.0) * (
                outer - 6.0 * (far[0] + far[1] + far[2]) + 15.0 * (near[0] + near[1] + near[2])
                - 60.0 * centre
            )
            if q < CURVED:
                for s, d in ((0, 0), (3, 1), (5, 2)):
                    seconds[q, s] = (1.0 / 12.0) * (16.0 * near[d] - far[d] - 30.0 * centre)
                b_m, b_c, b_p = pairs_z[q, p - 1], pairs_z[q, p], pairs_z[q, p + 1]
                dx_z = first_diff(b_m, t.odd(b_m, b_c), t.odd(b_c, b_p), b_p)
                b_s = sides_z[q, p - 1]
                dy_z = first_diff(
                    t.y_down(b_c, b_s, 2),
                    t.y_down(b_c, b_s, 1),
                    t.y_up(b_c, b_s, 1),
                    t.y_up(b_c, b_s, 2),
                )
                for s, inside, outside in ((2, dx, dx_z), (4, dy, dy_z)):
                    seconds[q, s] = first_diff(
                        t.z_down(inside, outside, 2),
                        t.z_down(inside, outside, 1),
                        t.z_up(inside, outside, 1),
                        t.z_up(inside, outside, 2),
                    )

        def value(q):
            return pairs[q, p + 1]

        def fluid_value(q):
            return fl[q, pl.ds(base, half), :]

        conformal, lapse = value(0), value(7)
        over_chi = 1.0 / conformal
        metric = symmetric([value(1 + s) for s in range(6)])
        shift = [value(8 + i) for i in range(3)]
        extrinsic, theta = value(11), value(21)
        traceless = symmetric([value(12 + s) for s in range(6)])
        connection = [value(18 + i) for i in range(3)]
        inverse = inverse_metric(metric)
        grad = [[grads[q, k] for k in range(3)] for q in range(fields)]
        chi_grad, lapse_grad = grad[0], grad[7]
        shift_grad = [[grad[8 + i][k] for i in range(3)] for k in range(3)]
        trace_k = extrinsic + 2.0 * theta

        stress = symmetric([tensors[p - 1, s] for s in range(6)])
        held = [fluid_value(q) for q in range(5)]
        shrink = volume_over(conformal)
        energy = held[4] + held[0]
        third_k = trace_k * (1.0 / 3.0)
        curved = [
            [
                (traceless[i][j] + metric[i][j] * third_k) if i <= j else None for j in range(3)
            ]
            for i in range(3)
        ]
        work = (
            stress[0][0] * curved[0][0]
            + stress[1][1] * curved[1][1]
            + stress[2][2] * curved[2][2]
            + 2.0
            * (
                stress[0][1] * curved[0][1]
                + stress[0][2] * curved[0][2]
                + stress[1][2] * curved[1][2]
            )
        )
        rates = [tensors[p - 1, 6 + q] for q in range(5)]
        for i in range(3):
            rates[1 + i] = (
                rates[1 + i]
                - energy * lapse_grad[i]
                + total([held[1 + k] * grad[8 + k][i] for k in range(3)])
            )
        rates[4] = (
            rates[4] + lapse * work * over_chi / shrink - dot(held[1:4], lapse_grad)
        )
        for q in range(5):
            hydro_rate[q, pl.ds(base, half), :] = rates[q]
        density = energy * shrink
        momentum = [held[1 + i] * shrink for i in range(3)]

        lowered = [[[None] * 3 for _ in range(3)] for _ in range(3)]
        for i in range(3):
            for j in range(3):
                for k in range(j, 3):
                    got = 0.5 * (
                        grad[1 + slot_of(i, k)][j]
                        + grad[1 + slot_of(i, j)][k]
                        - grad[1 + slot_of(j, k)][i]
                    )
                    lowered[i][j][k] = lowered[i][k][j] = got
        raised = [[[None] * 3 for _ in range(3)] for _ in range(3)]
        for i in range(3):
            for j in range(3):
                for k in range(j, 3):
                    got = total([inverse[i][l] * lowered[l][j][k] for l in range(3)])
                    raised[i][j][k] = raised[i][k][j] = got
        contracted = [trace_with(inverse, raised[i]) for i in range(3)]

        def hessian_trace(q):
            return (
                inverse[0][0] * seconds[q, 0]
                + inverse[1][1] * seconds[q, 3]
                + inverse[2][2] * seconds[q, 5]
                + 2.0 * (inverse[0][2] * seconds[q, 2] + inverse[1][2] * seconds[q, 4])
            )

        def second_cov(q, slope):
            bent = [total([raised[k][i][j] * slope[k] for k in range(3)]) for i, j in INDEX_PAIRS]
            return symmetric(
                [-bent[s] if s == 1 else seconds[q, s] - bent[s] for s in range(len(bent))]
            )

        chi_cov = second_cov(0, chi_grad)
        chi_lap = trace_with(inverse, chi_cov)
        raised_chi = [dot(inverse[i], chi_grad) for i in range(3)]
        chi_square = dot(raised_chi, chi_grad)
        cross_term = dot(raised_chi, lapse_grad)
        half_chi = 0.5 * over_chi
        plain_cov = second_cov(7, lapse_grad)
        lapse_cov = symmetric(
            [
                plain_cov[i][j]
                + (
                    chi_grad[i] * lapse_grad[j]
                    + chi_grad[j] * lapse_grad[i]
                    - metric[i][j] * cross_term
                )
                * half_chi
                for i, j in INDEX_PAIRS
            ]
        )
        lapse_lap = conformal * trace_with(inverse, lapse_cov)

        mixed = [
            [[dot(inverse[l], lowered[k][j]) for j in range(3)] for k in range(3)]
            for l in range(3)
        ]
        quarter_sq = half_chi * half_chi
        metric_factor = chi_lap * half_chi - 3.0 * chi_square * quarter_sq
        ricci = []
        for i, j in INDEX_PAIRS:
            second_part = -0.5 * hessian_trace(1 + slot_of(i, j))
            connection_part = 0.5 * total(
                [metric[k][i] * grad[18 + k][j] + metric[k][j] * grad[18 + k][i] for k in range(3)]
            )
            contracted_part = 0.5 * total(
                [contracted[k] * (lowered[i][j][k] + lowered[j][i][k]) for k in range(3)]
            )
            if i == j:
                quadratic = total(
                    [
                        raised[k][l][i] * (2.0 * mixed[l][i][k] + mixed[l][k][i])
                        for k in range(3)
                        for l in range(3)
                    ]
                )
            else:
                quadratic = total(
                    [
                        raised[k][l][i] * (mixed[l][j][k] + mixed[l][k][j])
                        + raised[k][l][j] * mixed[l][i][k]
                        for k in range(3)
                        for l in range(3)
                    ]
                )
            conformal_part = (
                chi_cov[i][j] * half_chi
                + metric[i][j] * metric_factor
                - chi_grad[i] * chi_grad[j] * quarter_sq
            )
            ricci.append(
                second_part + connection_part + contracted_part + quadratic + conformal_part
            )
        ricci = symmetric(ricci)
        ricci_scalar = conformal * trace_with(inverse, ricci)
        stress_trace = conformal * trace_with(inverse, stress)

        up_a = [
            [total([inverse[i][k] * traceless[k][j] for k in range(3)]) for j in range(3)]
            for i in range(3)
        ]
        raised_a = symmetric(
            [total([up_a[i][l] * inverse[j][l] for l in range(3)]) for i, j in INDEX_PAIRS]
        )
        a_square = trace_with(traceless, raised_a)
        shift_div = shift_grad[0][0] + shift_grad[1][1] + shift_grad[2][2]
        two_thirds_div = (2.0 / 3.0) * shift_div

        def finish(q, rate):
            rate = rate + dot(shift, grad[q]) + damped[q]
            st_rate[q, pl.ds(base, half), :] = rate

        finish(0, (2.0 / 3.0) * conformal * (lapse * trace_k - shift_div))
        finish(7, -2.0 * lapse * extrinsic)
        for i in range(3):
            finish(8 + i, 0.75 * connection[i] - SHIFT_DAMPING * shift[i])
        finish(
            11,
            lapse
            * (
                a_square
                + trace_k * trace_k * (1.0 / 3.0)
                + FOUR_PI * (stress_trace + density)
                + KAPPA_ONE * theta
            )
            - lapse_lap,
        )
        source = symmetric(
            [
                lapse * (ricci[i][j] - 2.0 * FOUR_PI * stress[i][j]) - lapse_cov[i][j]
                for i, j in INDEX_PAIRS
            ]
        )
        third_trace = trace_with(inverse, source) * (1.0 / 3.0)
        for s, (i, j) in enumerate(INDEX_PAIRS):
            finish(
                1 + s,
                total(
                    [
                        metric[i][k] * shift_grad[j][k] + metric[j][k] * shift_grad[i][k]
                        for k in range(3)
                    ]
                )
                - metric[i][j] * two_thirds_div
                - 2.0 * lapse * traceless[i][j],
            )
            product = total([traceless[i][k] * up_a[k][j] for k in range(3)])
            finish(
                12 + s,
                total(
                    [
                        traceless[i][k] * shift_grad[j][k] + traceless[j][k] * shift_grad[i][k]
                        for k in range(3)
                    ]
                )
                - traceless[i][j] * two_thirds_div
                + conformal * (source[i][j] - metric[i][j] * third_trace)
                + lapse * (trace_k * traceless[i][j] - 2.0 * product),
            )
        for i in range(3):
            bracket = (
                trace_with(raised_a, raised[i])
                - 1.5 * dot(raised_a[i], chi_grad) * over_chi
                - dot(inverse[i], [2.0 * grad[11][j] + grad[21][j] for j in range(3)]) * (1.0 / 3.0)
                - 2.0 * FOUR_PI * dot(inverse[i], momentum)
            )
            spread = [
                seconds[8, 0] + seconds[10, 2],
                seconds[9, 3] + seconds[10, 4],
                seconds[8, 2] + seconds[9, 4] + seconds[10, 5],
            ]
            finish(
                18 + i,
                contracted[i] * two_thirds_div
                - total([contracted[j] * shift_grad[j][i] for j in range(3)])
                + hessian_trace(8 + i)
                + dot(inverse[i], spread) * (1.0 / 3.0)
                - 2.0 * dot(raised_a[i], lapse_grad)
                + 2.0
                * lapse
                * (bracket - KAPPA_ONE * (connection[i] - contracted[i])),
            )
        finish(
            21,
            0.5
            * lapse
            * (
                ricci_scalar
                - a_square
                + (2.0 / 3.0) * trace_k * trace_k
                - 4.0 * FOUR_PI * density
            )
            - 2.0 * KAPPA_ONE * lapse * theta,
        )

    for index in range(own):
        pair_step(index)


def late_kernel(
    place, cells, zst, zfl, x_first, y_first, x_second, y_second, c_first, c_second, line_two, line_top,
    st_rate, hydro_rate, slopes, electric, st_out, fl_out,
):
    halo = Halo(
        place, cells, zst, zfl, x_first, y_first, x_second, y_second, c_first, c_second
    )
    x_below, x_above = halo.x_below, halo.x_above
    t, fields, half, own = halo.t, halo.fields, halo.half, halo.own
    inner, span = halo.inner, halo.span

    top = jnp.maximum(line_top[...], line_two[...])
    for lines in (c_first, c_second):
        top = jnp.maximum(top, lines[CORNER_TILES - 1, TOP_ROW : TOP_ROW + 1, :])
    dt = COURANT / top

    for p in inner:
        place = slice((p - 1) * half, p * half)
        mixed = []
        for q in range(CURVED):
            s_m, s_c, s_p = (
                halo.beside(q, n) if 1 <= n <= own else halo.corner(q, n) for n in (p - 1, p, p + 1)
            )
            slope = slopes[q, p - 1]
            slope_side = first_diff(s_m, t.odd_swapped(s_m, s_c), t.odd_swapped(s_c, s_p), s_p)
            mixed.append(
                first_diff(
                    t.y_down(slope, slope_side, 2),
                    t.y_down(slope, slope_side, 1),
                    t.y_up(slope, slope_side, 1),
                    t.y_up(slope, slope_side, 2),
                )
            )
        conformal, lapse = halo.main(0, p), halo.main(7, p)
        metric = [halo.main(1 + s, p) for s in range(6)]
        inverse = inverse_metric(symmetric(metric))
        half_chi = 0.5 / conformal
        cross = inverse[0][1]
        chi_trace = 2.0 * cross * mixed[0] * half_chi
        ricci = [metric[s] * chi_trace - cross * mixed[1 + s] for s in range(6)]
        ricci[1] = ricci[1] + mixed[0] * half_chi
        source = [lapse * r for r in ricci]
        source[1] = source[1] - mixed[7]
        third_trace = trace_with(inverse, symmetric(source)) * (1.0 / 3.0)
        extra = {
            11: -2.0 * conformal * cross * mixed[7],
            21: 0.5 * lapse * conformal * trace_with(inverse, symmetric(ricci)),
        }
        for s in range(6):
            extra[12 + s] = conformal * (source[s] - metric[s] * third_trace)
        for i in range(3):
            extra[18 + i] = 2.0 * cross * mixed[8 + i] + (1.0 / 3.0) * (
                inverse[i][0] * mixed[9] + inverse[i][1] * mixed[8]
            )
        for q in range(fields):
            rate = st_rate[q, place, :]
            if q in extra:
                rate = rate + extra[q]
            st_out[q, place, :] = halo.main(q, p) + dt * rate

    end = own + 1
    ends = (0, end)
    bx_face, by_face, bz_face = ({p: halo.corner(fields + 5 + i, p) for p in ends} for i in range(3))
    layers = {p: halo.corner_layers(p) for p in ends}
    bx_face[end] = layers[end]
    by_face[0] = jnp.where(t.slot < 2, layers[0], by_face[0])
    centred = [{}, {}, {}]
    for p in ends:
        following = halo.beside(fields + 5, 1) if p == 0 else bx_face[p]
        edge_cells = x_below if p == 0 else x_above
        dx = 0.5 * (t.odd_swapped(bx_face[p], following) - bx_face[p])
        dy = 0.5 * (t.y_up(by_face[p], edge_cells[fields + 6], 1) - by_face[p])
        centred[0][p] = bx_face[p] + dx
        centred[1][p] = by_face[p] + dy
        centred[2][p] = bz_face[p] - (dx + dy)
    corners = [{p: halo.corner(q, p) for p in ends} for q in [0, 7] + list(range(fields, fields + 5))]
    found = primitives(
        half, [(0, p) for p in ends], [[c] for c in corners[2:]], [[c] for c in centred],
        [corners[0]], [corners[1]], 2,
    )
    ez_h = [found[0, 0][10]] + [electric[own + p] for p in inner] + [found[0, end][10]]
    ez_x_h = [None] + [ez_h[p] + t.odd_swapped(ez_h[p - 1], ez_h[p]) for p in span[1:]]
    ez_x = [None] + [electric[p - 1] for p in span[1:]]
    edge_z = [None] + [ez_x[p] + t.y_down(ez_x[p], ez_x_h[p], 1) for p in span[1:]]
    quarter = 0.25 * dt
    for p in inner:
        place = slice((p - 1) * half, p * half)
        edge_z_h = ez_x_h[p] + t.y_down(ez_x_h[p], ez_x[p], 1)
        for q in range(5):
            fl_out[q, place, :] = halo.main(fields + q, p) + dt * hydro_rate[q, place, :]
        x_rate = hydro_rate[5, place, :] - (t.y_up(edge_z[p], edge_z_h, 1) - edge_z[p])
        y_rate = hydro_rate[6, place, :] + (t.odd(edge_z[p], edge_z[p + 1]) - edge_z[p])
        z_rate = hydro_rate[7, place, :]
        for i, rate in enumerate((x_rate, y_rate, z_rate)):
            fl_out[5 + i, place, :] = halo.main(fields + 5 + i, p) + quarter * rate


def per_device(spacetime, fluid):
    fields, cx, cy, cz = spacetime.shape
    rows = cx * cy
    st = spacetime.reshape(fields, rows, cz)
    fl = fluid.reshape(FLUID, rows, cz)
    sizes = [lax.axis_size(a) for a in ("gx", "gy", "gz")]
    tile = (2 * cy, cz)
    f32 = jnp.float32

    def shape(*dims):
        return jax.ShapeDtypeStruct(dims, f32)

    def beyond(cells):
        n = sizes[2]
        after = lax.ppermute(cells, "gz", [((i + 1) % n, i) for i in range(n)])
        if n == 2:
            return after
        before = lax.ppermute(cells, "gz", [(i, (i + 1) % n) for i in range(n)])
        lane = lax.broadcasted_iota(jnp.int32, cells.shape, 2)
        return jnp.where(lane < cz // 2, after, before)

    params = pltpu.CompilerParams(vmem_limit_bytes=48 * 1024 * 1024)
    zst, zfl = beyond(st), beyond(fl)
    cells = jnp.concatenate([st, fl], axis=0)
    face = shape(face_tiles(fields), *tile)
    corner = shape(CORNER_TILES, *tile)
    lane_row = shape(1, cz)
    even = jnp.stack([1 - lax.rem(lax.axis_index(axis), 2) for axis in ("gx", "gy")])
    place = jnp.broadcast_to(even.astype(f32)[:, None, None], (2,) + tile)

    def call(kernel, outs, name, operands, scratch=()):
        return pl.pallas_call(
            kernel,
            out_shape=outs,
            scratch_shapes=scratch,
            compiler_params=params,
            name=name,
        )(place, *operands)

    def trade(cells, axis, first):
        n = lax.axis_size(axis)
        step = [1, -1] if first else [-1, 1]
        return lax.ppermute(cells, axis, [(i, (i + step[i % 2]) % n) for i in range(n)])

    def two_away(cells, axis):
        n = lax.axis_size(axis)
        return lax.ppermute(cells, axis, [(i, (i + 2) % n) for i in range(n)]) if n == 4 else cells

    short = sizes[0] <= 4 and sizes[1] <= 4 and sizes[2] <= 2
    x_first, x_second, y_first, y_second, top = call(
        pack_kernel, [face] * 4 + [lane_row], "pack", (cells, zst, zfl)
    )
    x_first = trade(x_first, "gx", True)
    y_first = trade(y_first, "gy", True)
    x_second = trade(x_second, "gx", False)
    y_second = trade(y_second, "gy", False)
    top_two = two_away(top, "gx")
    c_first, c_second, line_top = call(
        relay_kernel,
        [corner, corner, lane_row],
        "relay",
        (x_first, x_second, y_first, top, top_two),
    )
    c_first = trade(c_first, "gy", True)
    c_second = trade(c_second, "gy", False)
    if short:
        line_two = two_away(line_top, "gy")
    else:
        line_two = lax.pmax(line_top, ("gx", "gy", "gz"))
    own = cx // 2
    arrived = (cells, zst, zfl, x_first, y_first, x_second, y_second)
    early = call(
        early_kernel,
        [
            shape(*st.shape),
            shape(FLUID, rows, cz),
            shape(CURVED, own, *tile),
            shape(2 * own + 1, *tile),
        ],
        "early",
        arrived,
        [
            pltpu.VMEM((fields, own + 4) + tile, f32),
            pltpu.VMEM((fields, own) + tile, f32),
            pltpu.VMEM((fields, own) + tile, f32),
            pltpu.VMEM((CURVED, own + 2) + tile, f32),
            pltpu.VMEM((CURVED, own) + tile, f32),
            pltpu.VMEM((fields, 3) + tile, f32),
            pltpu.VMEM((CURVED, 6) + tile, f32),
            pltpu.VMEM((fields,) + tile, f32),
            pltpu.VMEM((own, 11) + tile, f32),
        ],
    )
    st_next, fl_next = call(
        late_kernel,
        [shape(*st.shape), shape(*fl.shape)],
        "late",
        (*arrived, c_first, c_second, line_two, line_top, *early),
    )
    return st_next.reshape(spacetime.shape), fl_next.reshape(fluid.shape)


def solution(mesh):
    spec = P(None, "gx", "gy", "gz")
    return jax.shard_map(
        per_device, mesh=mesh, in_specs=(spec, spec), out_specs=(spec, spec), check_vma=False
    )
```

```python
import functools
import math

import jax
import jax.numpy as jnp
from jax import lax
from jax.experimental import pallas as pl
from jax.experimental.pallas import tpu as pltpu
from jax.sharding import PartitionSpec as P

RECOVERY_STEPS = 4
INDEX_PAIRS = ((0, 0), (0, 1), (0, 2), (1, 1), (1, 2), (2, 2))
COURANT = 0.25
DISSIPATION = 0.2
KAPPA_ONE = 0.02
SHIFT_DAMPING = 1.0
SPEED_CAP = 0.99
PRESSURE_FLOOR = 0.01
FOUR_PI = 4.0 * math.pi

BATCH = 6
CURVED = 11
FLUID = 8


def total(pieces):
    summed = pieces[0]
    for member in pieces[1:]:
        summed = summed + member
    return summed


def dot(first_vec, second_vec):
    return total([first_vec[i] * second_vec[i] for i in range(3)])


def slot_of(i, j):
    return INDEX_PAIRS.index((min(i, j), max(i, j)))


def symmetric(entries):
    return [[entries[slot_of(i, j)] for j in range(3)] for i in range(3)]


def trace_with(inverse, tensor):
    return (
        inverse[0][0] * tensor[0][0]
        + inverse[1][1] * tensor[1][1]
        + inverse[2][2] * tensor[2][2]
        + 2.0
        * (
            inverse[0][1] * tensor[0][1]
            + inverse[0][2] * tensor[0][2]
            + inverse[1][2] * tensor[1][2]
        )
    )


def inverse_metric(metric):
    cofactor = [
        metric[1][1] * metric[2][2] - metric[1][2] * metric[1][2],
        metric[0][2] * metric[1][2] - metric[0][1] * metric[2][2],
        metric[0][1] * metric[1][2] - metric[0][2] * metric[1][1],
        metric[0][0] * metric[2][2] - metric[0][2] * metric[0][2],
        metric[0][1] * metric[0][2] - metric[0][0] * metric[1][2],
        metric[0][0] * metric[1][1] - metric[0][1] * metric[0][1],
    ]
    determinant = (
        metric[0][0] * cofactor[0] + metric[0][1] * cofactor[1] + metric[0][2] * cofactor[2]
    )
    over = 1.0 / determinant
    return symmetric([c * over for c in cofactor])


class Tile:
    def __init__(self, cy, cz):
        self.cy, self.rows, self.lanes = cy, 2 * cy, cz
        shape = (self.rows, cz)
        self.row = lax.broadcasted_iota(jnp.int32, shape, 0)
        self.lane = lax.broadcasted_iota(jnp.int32, shape, 1)
        self.slot = lax.rem(self.row, cy)

    def turn(self, tile, amount):
        amount = amount % self.rows
        return tile if amount == 0 else pltpu.roll(tile, amount, 0)

    def spin(self, tile, amount):
        amount = amount % self.lanes
        return tile if amount == 0 else pltpu.roll(tile, amount, 1)

    def swap(self, tile):
        return self.turn(tile, self.cy)

    def odd(self, a, b):
        return self.turn(jnp.where(self.row < self.cy, b, a), self.cy)

    def odd_swapped(self, a, b):
        return self.turn(jnp.where(self.row < self.cy, a, b), self.cy)

    def y_up(self, main, beyond, k):
        return self.turn(jnp.where(self.slot < k, beyond, main), -k)

    def y_down(self, main, beyond, k):
        return self.turn(jnp.where(self.slot >= self.cy - k, beyond, main), k)

    def z_up(self, main, beyond, k):
        return self.spin(jnp.where(self.lane < k, beyond, main), -k)

    def z_down(self, main, beyond, k):
        return self.spin(jnp.where(self.lane >= self.lanes - k, beyond, main), k)

    def corner_rows(self, side, turn):
        places = ((0, 2), (self.cy - 1, self.cy + 1))[side]
        first, second = [(place + turn) % self.rows for place in places]
        return (self.row == first) | (self.row == second)

    def join_low(self, u, v):
        return jnp.where(self.slot < 2, self.swap(u), self.turn(v, 2))

    def join_high(self, u, v):
        return jnp.where(self.slot >= self.cy - 2, self.swap(u), self.turn(self.swap(v), -2))

    def part_first(self, from_above, from_below):
        return jnp.where(self.slot < 2, from_above, from_below)

    def part_second(self, from_above, from_below):
        return self.turn(jnp.where(self.slot < 2, from_below, from_above), 2)


def edge_list(tiles):
    fields = next(n for n in range(tiles) if face_tiles(n) == tiles)
    return list(range(CURVED)) + list(range(fields, fields + FLUID))


CORNER_TURNS = (0, 1, 4, 5)
CORNER_TILES = CURVED + FLUID // 4 + 1
TOP_ROW = 6


def face_tiles(fields):
    return fields + FLUID + len(pairs_of(third_list(fields))) + 1


def third_list(fields):
    return list(range(fields + 1))


def pairs_of(items):
    return [(items[i], items[min(i + 1, len(items) - 1)]) for i in range(0, len(items), 2)]


def top_speed(st):
    inverse = inverse_metric(symmetric([st[1 + s] for s in range(6)]))
    scale = 2.0 * st[7] * st[0]
    speeds = [jnp.abs(st[8 + d]) + jnp.sqrt(scale * inverse[d][d]) for d in range(3)]
    top = jnp.maximum(jnp.maximum(speeds[0], speeds[1]), speeds[2])
    return jnp.max(jnp.max(top, axis=1, keepdims=True), axis=0, keepdims=True)


class Chosen:
    def __init__(self, first, second, swapped):
        self.first, self.second, self.swapped, self.shape = first, second, swapped, first.shape

    def __getitem__(self, key):
        return jnp.where(self.swapped, self.second[key], self.first[key])


class Sent:
    def __init__(self, first, second, swapped):
        self.first, self.second, self.swapped, self.shape = first, second, swapped, first.shape

    def put(self, key, lower, upper):
        self.first[key] = jnp.where(self.swapped, upper, lower)
        self.second[key] = jnp.where(self.swapped, lower, upper)


def even_along_y(tile):
    return jnp.full(tile, lax.rem(lax.axis_index("gy"), 2), jnp.int32) == 0


def pack_kernel(cells, zst, zfl, *outs):
    fields, rows, lanes = zst.shape
    st, fl = cells.at[0:fields], cells.at[fields : fields + FLUID]
    cy = rows // 4
    t = Tile(cy, lanes)
    x_low, x_high, y_first, y_second, top_out = outs
    half = t.rows
    to_y = Sent(y_first, y_second, even_along_y((half, lanes)))

    def own(ref, q):
        return [ref[q, 0:half, :], ref[q, half : 2 * half, :]]

    tiles, beyond = [], []
    for q in range(fields):
        tiles.append(own(st, q))
        beyond.append(own(zst, q) if q < CURVED else None)
    for q in range(FLUID):
        tiles.append(own(fl, q))
        beyond.append(own(zfl, q))

    packed = [None] * 4
    place_count = 0
    for q, (first, second) in enumerate(tiles):
        x_low[q] = first
        x_high[q] = second
        to_y.put(q, t.join_low(first, second), t.join_high(first, second))
        if beyond[q] is not None:
            zf, zs = beyond[q]
            for m, piece in enumerate((zf, zs, t.join_low(zf, zs), t.join_high(zf, zs))):
                piece = t.spin(piece, 4 * place_count + 2)
                packed[m] = (
                    piece if place_count == 0 else jnp.where(t.lane < 4 * place_count, packed[m], piece)
                )
            place_count += 1
    for n, (a, b) in enumerate(pairs_of(third_list(fields))):
        slot = fields + FLUID + n
        xa, xb = (tiles[q if q < fields else fields + 5] for q in (a, b))
        x_low[slot] = jnp.where(t.row < cy, xa[1], t.swap(xb[1]))
        x_high[slot] = jnp.where(t.row < cy, t.swap(xb[0]), xa[0])
        ya, yb = (tiles[q if q < fields else fields + 6] for q in (a, b))
        w = [t.swap(ya[0]), t.swap(ya[1]), t.swap(yb[0]), t.swap(yb[1])]
        s = t.slot
        low = jnp.where(s == 0, t.turn(w[2], -2), t.turn(w[3], -1))
        low = jnp.where(s == 2, w[0], jnp.where(s == 3, t.turn(w[1], 1), low))
        high = jnp.where(s == 3, t.turn(w[2], 2), t.turn(w[3], 1))
        high = jnp.where(s == 1, w[0], jnp.where(s == 0, t.turn(w[1], -1), high))
        to_y.put(slot, low, high)
    top = jnp.maximum(top_speed(st), top_speed(zst))
    top_out[...] = jnp.broadcast_to(top, top_out.shape)
    last = x_low.shape[0] - 1
    x_lanes = [jnp.where(t.lane < 4 * place_count, piece, top) for piece in packed[:2]]
    y_lanes = [jnp.where(t.lane < 4 * place_count, piece, top) for piece in packed[2:]]
    x_low[last], x_high[last] = x_lanes
    to_y.put(last, *y_lanes)


def relay_kernel(x_below, x_above, y_first, top, top_two, c_first, c_second, line_top):
    cy, lanes = x_below.shape[1] // 2, x_below.shape[2]
    t = Tile(cy, lanes)
    to_y = Sent(c_first, c_second, even_along_y((t.rows, lanes)))
    last = x_below.shape[0] - 1
    line = jnp.maximum(top[...], top_two[...])
    for beside in (x_below, x_above, y_first):
        line = jnp.maximum(line, beside[last, 0:1, lanes - 1 : lanes])
    line_top[...] = line
    edge = edge_list(x_below.shape[0])
    for q in range(CURVED):
        below, above = x_below[q], x_above[q]
        to_y.put(q, t.join_low(below, above), t.join_high(below, above))
    for n in range(0, FLUID, 4):
        low, high = None, None
        for turn, q in zip(CORNER_TURNS, edge[CURVED + n : CURVED + n + 4]):
            below, above = x_below[q], x_above[q]
            below, above = (t.turn(j(below, above), turn) for j in (t.join_low, t.join_high))
            if low is None:
                low, high = below, above
            else:
                low = jnp.where(t.corner_rows(0, turn), below, low)
                high = jnp.where(t.corner_rows(1, turn), above, high)
        to_y.put(CURVED + n // 4, low, high)
    along_x, along_y = edge[CURVED + 5], edge[CURVED + 6]
    low = t.join_low(x_below[along_y], x_above[along_y])
    high = t.join_high(x_below[along_x], x_above[along_x])
    low, high = (jnp.where(t.row == TOP_ROW, line, tile) for tile in (low, high))
    to_y.put(CORNER_TILES - 1, low, high)


def limited(a, b):
    return jnp.maximum(jnp.minimum(a, b), 0.0) + jnp.minimum(jnp.maximum(a, b), 0.0)


def recover(conserved, magnetic):
    density = conserved[0]
    momenta = conserved[1:4]
    energy = conserved[4] + density
    mom_sq = dot(momenta, momenta)
    mag_sq = dot(magnetic, magnetic)
    cross = dot(momenta, magnetic)
    cross_sq = cross * cross

    def state(z):
        grown = z + mag_sq
        over = 1.0 / (z * grown)
        speed_sq = (mom_sq * z * z + cross_sq * (2.0 * z + mag_sq)) * over * over
        kept = 1.0 - jnp.minimum(speed_sq, SPEED_CAP)
        rest = density * jnp.sqrt(kept)
        return kept, rest, 0.5 * (z * kept - rest), grown * over

    z = jnp.maximum(energy - 0.5 * mag_sq, density)
    for _ in range(RECOVERY_STEPS):
        kept, rest, pressure, over_z = state(z)
        residual = (
            z
            + mag_sq
            - pressure
            - 0.5 * mag_sq * kept
            - 0.5 * cross_sq * over_z * over_z
            - energy
        )
        z = jnp.maximum(z - residual / (1.0 - 0.5 * kept), density)
    kept, rest, pressure, over_z = state(z)
    pressure = jnp.maximum(pressure, PRESSURE_FLOOR * rest)
    scale = lax.rsqrt(kept) / (z + mag_sq)
    along = cross * over_z
    four_vel = [scale * (momenta[i] + along * magnetic[i]) for i in range(3)]
    return [rest, pressure] + four_vel


def stress_parts(rest, pressure, u, magnetic):
    lorentz_sq = 1.0 + dot(u, u)
    over = lax.rsqrt(lorentz_sq)
    over_sq = over * over
    time_b = dot(u, magnetic)
    grown_b = [magnetic[i] + time_b * u[i] for i in range(3)]
    b_square = (dot(magnetic, magnetic) + time_b * time_b) * over_sq
    enthalpy = rest + 2.0 * pressure
    inertia = enthalpy + b_square
    return lorentz_sq, over, over_sq, time_b, grown_b, b_square, enthalpy, inertia


def face_state(rest, pressure, u, magnetic, d):
    lorentz_sq, over, over_sq, time_b, grown_b, b_square, enthalpy, inertia = stress_parts(
        rest, pressure, u, magnetic
    )
    total_pressure = pressure + 0.5 * b_square
    lorentz = lorentz_sq * over
    density = rest * lorentz
    carried = inertia * lorentz
    time_over = time_b * over
    conserved = [density]
    conserved += [carried * u[j] - time_over * grown_b[j] for j in range(3)]
    conserved += [inertia * lorentz_sq - total_pressure - time_b * time_b - density]
    mass_flux = rest * u[d]
    flux = [mass_flux]
    pushed = inertia * u[d]
    b_over = grown_b[d] * over_sq
    for j in range(3):
        flux_j = pushed * u[j] - b_over * grown_b[j]
        flux.append(flux_j + total_pressure if j == d else flux_j)
    flux.append(carried * u[d] - time_over * grown_b[d] - mass_flux)
    ratio = 1.0 / (enthalpy * inertia)
    sound_sq = 2.0 * pressure * inertia * ratio
    alfven_sq = b_square * enthalpy * ratio
    fast_sq = sound_sq + alfven_sq - sound_sq * alfven_sq
    slow = 1.0 - fast_sq
    velocity = u[d] * over
    rest_part = 1.0 - dot(u, u) * over_sq * fast_sq
    spread = jnp.sqrt(fast_sq * over_sq * (rest_part - velocity * velocity * slow))
    fastest = (jnp.abs(velocity * slow) + spread) / rest_part
    return conserved, flux, fastest


def face_flux(left, right, normal, weight, d):
    sides = []
    for state in (left, right):
        magnetic = [normal if i == d else state[5 + i] for i in range(3)]
        sides.append(face_state(state[0], state[1], state[2:5], magnetic, d))
    (cons_l, flux_l, fast_l), (cons_r, flux_r, fast_r) = sides
    signal = jnp.maximum(fast_l, fast_r)
    scale = 0.5 * weight
    return [scale * (flux_l[q] + flux_r[q] - signal * (cons_r[q] - cons_l[q])) for q in range(5)]


def volume_over(conformal):
    return conformal * jnp.sqrt(conformal)


def first_diff(down_two, down, up, up_two):
    return (8.0 / 12.0) * (up - down) + (1.0 / 12.0) * (down_two - up_two)


class Halo:
    def __init__(self, cells, zst, zfl, x_below, y_first, x_above, y_second, *corners):
        self.fields, self.block, self.lanes = zst.shape
        even_y = even_along_y((self.block // 2, self.lanes))
        y_below, y_above = Chosen(y_first, y_second, even_y), Chosen(y_second, y_first, even_y)
        if corners:
            c_first, c_second = corners
            self.c_below = Chosen(c_first, c_second, even_y)
            self.c_above = Chosen(c_second, c_first, even_y)
        self.st = cells.at[0 : self.fields]
        self.fl = cells.at[self.fields : self.fields + FLUID]
        self.zst, self.zfl = zst, zfl
        self.x_below, self.x_above = x_below, x_above
        self.y_below, self.y_above = y_below, y_above
        self.cy = self.block // 4
        self.t = Tile(self.cy, self.lanes)
        self.half = self.t.rows
        self.own = self.block // self.half
        self.inner = range(1, self.own + 1)
        self.span = range(self.own + 2)
        self.edge = edge_list(x_below.shape[0])
        self.last = x_below.shape[0] - 1

    def rows_of(self, ref, q, p):
        return ref[q, (p - 1) * self.half : p * self.half, :]

    def main(self, q, p):
        if q < self.fields:
            return self.rows_of(self.st, q, p)
        return self.rows_of(self.fl, q - self.fields, p)

    def beyond(self, q, p):
        if q < self.fields:
            return self.rows_of(self.zst, q, p)
        return self.rows_of(self.zfl, q - self.fields, p)

    def part(self, second):
        return self.t.part_second if second else self.t.part_first

    def beside(self, q, p):
        return self.part(p == 2)(self.y_above[q], self.y_below[q])

    def third_place(self, q):
        return self.fields + FLUID + q // 2, q % 2

    def x_third(self, q, upper):
        tile, which = self.third_place(q)
        found = self.x_above[tile] if upper else self.x_below[tile]
        return self.t.swap(found) if which else found

    def y_third(self, q, p):
        t = self.t
        tile, which = self.third_place(q)
        turn_above, turn_below = ((0, 0), (-1, 1), (2, -2), (1, -1))[2 * which + p - 1]
        above, below = t.turn(self.y_above[tile], turn_above), t.turn(self.y_below[tile], turn_below)
        return jnp.where(t.slot == 2, above, below)

    def z_place(self, q):
        return 4 * self.edge.index(q) + 2

    def x_beyond(self, q, upper):
        tile = self.x_above[self.last] if upper else self.x_below[self.last]
        return self.t.spin(tile, -self.z_place(q))

    def y_beyond(self, q, p):
        return self.t.spin(self.beside(self.last, p), -self.z_place(q))

    def corner(self, q, p):
        place, turn = q, 0
        if q >= CURVED:
            n = q - self.fields
            place, turn = CURVED + n // 4, CORNER_TURNS[n % 4]
        above, below = self.t.turn(self.c_above[place], -turn), self.t.turn(self.c_below[place], -turn)
        return self.part(p > 0)(above, below)

    def corner_layers(self, p):
        place = CORNER_TILES - 1
        return self.part(p > 0)(self.c_above[place], self.c_below[place])

    def plane(self, q):
        inner = self.inner
        return (
            [self.x_below[q]] + [self.main(q, p) for p in inner] + [self.x_above[q]],
            [None] + [self.beside(q, p) for p in inner] + [None],
            [self.x_beyond(q, False)]
            + [self.beyond(q, p) for p in inner]
            + [self.x_beyond(q, True)],
            [None] + [self.y_beyond(q, p) for p in inner] + [None],
        )


def weigh(chi_face, alpha_face):
    shrink = volume_over(chi_face)
    return shrink, alpha_face / shrink


def primitives(half, spots, cons, centred, chi, alpha, batch):
    found = {}
    for start in range(0, len(spots), batch):
        group = spots[start : start + batch]

        def gather(planes):
            return jnp.concatenate([planes[k][p] for k, p in group], axis=0)

        shrink = volume_over(gather(chi))
        mag_raw = [gather(centred[i]) for i in range(3)]
        mag = [m * shrink for m in mag_raw]
        values = recover([gather(c) * shrink for c in cons], mag)
        u = values[2:5]
        factor = gather(alpha) * lax.rsqrt(1.0 + dot(u, u))
        field = [
            factor * (u[(i + 2) % 3] * mag_raw[(i + 1) % 3] - u[(i + 1) % 3] * mag_raw[(i + 2) % 3])
            for i in range(3)
        ]
        for n, spot in enumerate(group):
            found[spot] = [value[n * half : (n + 1) * half] for value in values + mag + field]
    return found


def ring_fluxes(prims, chi, alpha, normals, d, up, down):
    found = []
    for here, there in ((0, 1), (1, 0)):
        left, right = [], []
        for a, b in zip(prims[here], prims[there]):
            below = down(a, b, 1)
            middle = a - below
            left.append(below + 0.5 * limited(below - down(a, b, 2), middle))
            right.append(a - 0.5 * limited(middle, up(a, b, 1) - a))
        shrink, weight = weigh(
            0.5 * (chi[here] + down(chi[here], chi[there], 1)),
            0.5 * (alpha[here] + down(alpha[here], alpha[there], 1)),
        )
        found.append(face_flux(left, right, normals[here] * shrink, weight, d))
    return [a - up(a, b, 1) for a, b in zip(*found)]


def early_kernel(
    cells, zst, zfl, x_below, y_first, x_above, y_second,
    st_rate, hydro_rate, slopes, electric, pairs, sides, thirds, pairs_z, sides_z, grads, seconds, damped, tensors,
):
    halo = Halo(cells, zst, zfl, x_below, y_first, x_above, y_second)
    t, fields, half, own, cy = halo.t, halo.fields, halo.half, halo.own, halo.cy
    st, fl, inner = halo.st, halo.fl, halo.inner

    for q in range(fields):
        pairs[q, 0] = halo.x_third(q, False)
        pairs[q, 1] = x_below[q]
        for p in inner:
            pairs[q, 1 + p] = halo.main(q, p)
            sides[q, p - 1] = halo.beside(q, p)
            thirds[q, p - 1] = halo.y_third(q, p)
        pairs[q, 2 + own] = x_above[q]
        pairs[q, 3 + own] = halo.x_third(q, True)
        if q < CURVED:
            pairs_z[q, 0] = halo.x_beyond(q, False)
            pairs_z[q, own + 1] = halo.x_beyond(q, True)
            for p in inner:
                pairs_z[q, p] = halo.beyond(q, p)
                sides_z[q, p - 1] = halo.y_beyond(q, p)

    span = halo.span
    face = [halo.plane(fields + 5 + i) for i in range(3)]

    def halves(kind, p):
        own_x, own_y, own_z = (f[kind][p] for f in face)
        pair = kind in (0, 2)
        known_x = pair or p < own
        last = kind == 0 and p == own + 1
        if pair:
            next_x = halo.x_third(fields, True) if last else face[0][kind][min(p + 1, own + 1)]
            next_x = t.odd(own_x, next_x)
        else:
            next_x = t.odd_swapped(own_x, face[0][kind][p + 1] if known_x else own_x)
        dx = 0.5 * (next_x - own_x)
        dz = 0.5 * (t.z_up(own_z, face[2][kind ^ 2][p], 1) - own_z)
        inside = 1 <= p <= own
        if not pair:
            here = jnp.where(t.slot == 2, halo.y_third(fields, p), own_y) if kind == 1 else own_y
            next_y = t.y_up(here, face[1][kind ^ 1][p], 1)
        else:
            next_y = t.y_up(own_y, face[1][kind ^ 1][p] if inside else own_y, 1)
        dy = 0.5 * (next_y - own_y)
        if pair and not inside:
            dy = jnp.where(t.slot == cy - 1, -(dx + dz), dy)
        if not pair and not known_x:
            dx = jnp.where(t.row < cy, -(dy + dz), dx)
        return own_x + dx, own_y + dy, own_z + dz

    spots = [(0, p) for p in span] + [(1, p) for p in inner]
    spots += [(2, p) for p in span] + [(3, p) for p in inner]
    centred = [[[None] * (own + 2) for _ in range(4)] for _ in range(3)]
    for k, p in spots:
        for i, value in enumerate(halves(k, p)):
            centred[i][k][p] = value
    chi, alpha = halo.plane(0), halo.plane(7)
    found = primitives(
        half, spots, [halo.plane(fields + q) for q in range(5)], centred, chi, alpha, BATCH
    )

    lines = [[found[0, p][i] for p in span] for i in range(8)] + [chi[0], alpha[0]]
    odd_lines = [[t.odd(f[p], f[min(p + 1, own + 1)]) for p in span] for f in lines]
    fluxes = [None]
    for p in range(1, own + 2):
        left, right = [], []
        for f, o in zip(lines[:8], odd_lines):
            here = f[p] - o[p - 1]
            left.append(o[p - 1] + 0.5 * limited(o[p - 1] - f[p - 1], here))
            right.append(f[p] - 0.5 * limited(here, o[p] - f[p]))
        shrink, weight = weigh(
            0.5 * (lines[8][p] + odd_lines[8][p - 1]), 0.5 * (lines[9][p] + odd_lines[9][p - 1])
        )
        fluxes.append(face_flux(left, right, face[0][0][p] * shrink, weight, 0))
    for p in inner:
        changes = [
            ring_fluxes(
                [found[k, p][:8] for k in (0, kind)],
                [chi[k][p] for k in (0, kind)],
                [alpha[k][p] for k in (0, kind)],
                [face[d][k][p] for k in (0, kind)],
                d,
                up,
                down,
            )
            for d, kind, up, down in ((1, 1, t.y_up, t.y_down), (2, 2, t.z_up, t.z_down))
        ]
        for q in range(5):
            change = fluxes[p][q] - t.odd(fluxes[p][q], fluxes[p + 1][q])
            tensors[p - 1, 6 + q] = change + changes[0][q] + changes[1][q]
        rest, pressure = found[0, p][:2]
        u = found[0, p][2:5]
        parts = stress_parts(rest, pressure, u, found[0, p][5:8])
        lorentz_sq, over, over_sq, time_b, grown_b, b_square, enthalpy, inertia = parts
        total_pressure = pressure + 0.5 * b_square
        for s, (i, j) in enumerate(INDEX_PAIRS):
            value = inertia * u[i] * u[j] - over_sq * (grown_b[i] * grown_b[j])
            tensors[p - 1, s] = value + total_pressure if i == j else value

    ex, ey, ez = (
        [[found[k, p][8 + i] if (k, p) in found else None for p in span] for k in range(4)]
        for i in range(3)
    )
    ey_x = [
        [ey[k][p] + t.odd(ey[k][p - 1], ey[k][p]) if p else None for p in span] for k in (0, 2)
    ]
    edge_y = [None] + [ey_x[0][p] + t.z_down(ey_x[0][p], ey_x[1][p], 1) for p in span[1:]]
    for p in span[1:]:
        electric[p - 1] = ez[0][p] + t.odd(ez[0][p - 1], ez[0][p])
    for p in inner:
        electric[own + p] = ez[1][p]
        edge_y_z = ey_x[1][p] + t.z_down(ey_x[1][p], ey_x[0][p], 1)
        ex_y = ex[0][p] + t.y_down(ex[0][p], ex[1][p], 1)
        ex_y_h = ex[1][p] + t.y_down(ex[1][p], ex[0][p], 1)
        ex_y_z = ex[2][p] + t.y_down(ex[2][p], ex[3][p], 1)
        ex_y_hz = ex[3][p] + t.y_down(ex[3][p], ex[2][p], 1)
        edge_x = ex_y + t.z_down(ex_y, ex_y_z, 1)
        edge_x_h = ex_y_h + t.z_down(ex_y_h, ex_y_hz, 1)
        edge_x_z = ex_y_z + t.z_down(ex_y_z, ex_y, 1)
        place = slice((p - 1) * half, p * half)
        hydro_rate[5, place, :] = t.z_up(edge_y[p], edge_y_z, 1) - edge_y[p]
        hydro_rate[6, place, :] = edge_x - t.z_up(edge_x, edge_x_z, 1)
        hydro_rate[7, place, :] = (t.y_up(edge_x, edge_x_h, 1) - edge_x) - (
            t.odd(edge_y[p], edge_y[p + 1]) - edge_y[p]
        )

    def pair_step(index):
        p = index + 1
        base = index * half

        for q in range(fields):
            centre = pairs[q, p + 1]
            x_m3 = t.odd(pairs[q, p - 1], pairs[q, p])
            x_m2 = pairs[q, p]
            x_m1 = t.odd(pairs[q, p], centre)
            x_p1 = t.odd(centre, pairs[q, p + 2])
            x_p2 = pairs[q, p + 2]
            x_p3 = t.odd(pairs[q, p + 2], pairs[q, p + 3])
            side, third = sides[q, index], thirds[q, index]
            y_m1, y_m2 = t.y_down(centre, side, 1), t.y_down(centre, side, 2)
            y_p1, y_p2 = t.y_up(centre, side, 1), t.y_up(centre, side, 2)
            y_m3 = t.turn(
                jnp.where(t.slot >= cy - 2, side, jnp.where(t.slot == cy - 3, third, centre)), 3
            )
            y_p3 = t.turn(jnp.where(t.slot < 2, side, jnp.where(t.slot == 2, third, centre)), -3)
            beyond = zst[q, pl.ds(base, half), :]
            z_m1, z_m2, z_m3 = (t.z_down(centre, beyond, k) for k in (1, 2, 3))
            z_p1, z_p2, z_p3 = (t.z_up(centre, beyond, k) for k in (1, 2, 3))
            dx = first_diff(x_m2, x_m1, x_p1, x_p2)
            dy = first_diff(y_m2, y_m1, y_p1, y_p2)
            grads[q, 0] = dx
            if q < CURVED:
                slopes[q, index] = dx
            grads[q, 1] = dy
            grads[q, 2] = first_diff(z_m2, z_m1, z_p1, z_p2)
            near = [x_m1 + x_p1, y_m1 + y_p1, z_m1 + z_p1]
            far = [x_m2 + x_p2, y_m2 + y_p2, z_m2 + z_p2]
            outer = (x_m3 + x_p3) + (y_m3 + y_p3) + (z_m3 + z_p3)
            damped[q] = (DISSIPATION / 64.0) * (
                outer - 6.0 * (far[0] + far[1] + far[2]) + 15.0 * (near[0] + near[1] + near[2])
                - 60.0 * centre
            )
            if q < CURVED:
                for s, d in ((0, 0), (3, 1), (5, 2)):
                    seconds[q, s] = (1.0 / 12.0) * (16.0 * near[d] - far[d] - 30.0 * centre)
                b_m, b_c, b_p = pairs_z[q, p - 1], pairs_z[q, p], pairs_z[q, p + 1]
                dx_z = first_diff(b_m, t.odd(b_m, b_c), t.odd(b_c, b_p), b_p)
                b_s = sides_z[q, p - 1]
                dy_z = first_diff(
                    t.y_down(b_c, b_s, 2),
                    t.y_down(b_c, b_s, 1),
                    t.y_up(b_c, b_s, 1),
                    t.y_up(b_c, b_s, 2),
                )
                for s, inside, outside in ((2, dx, dx_z), (4, dy, dy_z)):
                    seconds[q, s] = first_diff(
                        t.z_down(inside, outside, 2),
                        t.z_down(inside, outside, 1),
                        t.z_up(inside, outside, 1),
                        t.z_up(inside, outside, 2),
                    )

        def value(q):
            return pairs[q, p + 1]

        def fluid_value(q):
            return fl[q, pl.ds(base, half), :]

        conformal, lapse = value(0), value(7)
        over_chi = 1.0 / conformal
        metric = symmetric([value(1 + s) for s in range(6)])
        shift = [value(8 + i) for i in range(3)]
        extrinsic, theta = value(11), value(21)
        traceless = symmetric([value(12 + s) for s in range(6)])
        connection = [value(18 + i) for i in range(3)]
        inverse = inverse_metric(metric)
        grad = [[grads[q, k] for k in range(3)] for q in range(fields)]
        chi_grad, lapse_grad = grad[0], grad[7]
        shift_grad = [[grad[8 + i][k] for i in range(3)] for k in range(3)]
        trace_k = extrinsic + 2.0 * theta

        stress = symmetric([tensors[p - 1, s] for s in range(6)])
        held = [fluid_value(q) for q in range(5)]
        shrink = volume_over(conformal)
        energy = held[4] + held[0]
        third_k = trace_k * (1.0 / 3.0)
        curved = [
            [
                (traceless[i][j] + metric[i][j] * third_k) if i <= j else None for j in range(3)
            ]
            for i in range(3)
        ]
        work = (
            stress[0][0] * curved[0][0]
            + stress[1][1] * curved[1][1]
            + stress[2][2] * curved[2][2]
            + 2.0
            * (
                stress[0][1] * curved[0][1]
                + stress[0][2] * curved[0][2]
                + stress[1][2] * curved[1][2]
            )
        )
        rates = [tensors[p - 1, 6 + q] for q in range(5)]
        for i in range(3):
            rates[1 + i] = (
                rates[1 + i]
                - energy * lapse_grad[i]
                + total([held[1 + k] * grad[8 + k][i] for k in range(3)])
            )
        rates[4] = (
            rates[4] + lapse * work * over_chi / shrink - dot(held[1:4], lapse_grad)
        )
        for q in range(5):
            hydro_rate[q, pl.ds(base, half), :] = rates[q]
        density = energy * shrink
        momentum = [held[1 + i] * shrink for i in range(3)]

        lowered = [[[None] * 3 for _ in range(3)] for _ in range(3)]
        for i in range(3):
            for j in range(3):
                for k in range(j, 3):
                    got = 0.5 * (
                        grad[1 + slot_of(i, k)][j]
                        + grad[1 + slot_of(i, j)][k]
                        - grad[1 + slot_of(j, k)][i]
                    )
                    lowered[i][j][k] = lowered[i][k][j] = got
        raised = [[[None] * 3 for _ in range(3)] for _ in range(3)]
        for i in range(3):
            for j in range(3):
                for k in range(j, 3):
                    got = total([inverse[i][l] * lowered[l][j][k] for l in range(3)])
                    raised[i][j][k] = raised[i][k][j] = got
        contracted = [trace_with(inverse, raised[i]) for i in range(3)]

        def hessian_trace(q):
            return (
                inverse[0][0] * seconds[q, 0]
                + inverse[1][1] * seconds[q, 3]
                + inverse[2][2] * seconds[q, 5]
                + 2.0 * (inverse[0][2] * seconds[q, 2] + inverse[1][2] * seconds[q, 4])
            )

        def second_cov(q, slope):
            bent = [total([raised[k][i][j] * slope[k] for k in range(3)]) for i, j in INDEX_PAIRS]
            return symmetric(
                [-bent[s] if s == 1 else seconds[q, s] - bent[s] for s in range(len(bent))]
            )

        chi_cov = second_cov(0, chi_grad)
        chi_lap = trace_with(inverse, chi_cov)
        raised_chi = [dot(inverse[i], chi_grad) for i in range(3)]
        chi_square = dot(raised_chi, chi_grad)
        cross_term = dot(raised_chi, lapse_grad)
        half_chi = 0.5 * over_chi
        plain_cov = second_cov(7, lapse_grad)
        lapse_cov = symmetric(
            [
                plain_cov[i][j]
                + (
                    chi_grad[i] * lapse_grad[j]
                    + chi_grad[j] * lapse_grad[i]
                    - metric[i][j] * cross_term
                )
                * half_chi
                for i, j in INDEX_PAIRS
            ]
        )
        lapse_lap = conformal * trace_with(inverse, lapse_cov)

        mixed = [
            [[dot(inverse[l], lowered[k][j]) for j in range(3)] for k in range(3)]
            for l in range(3)
        ]
        quarter_sq = half_chi * half_chi
        metric_factor = chi_lap * half_chi - 3.0 * chi_square * quarter_sq
        ricci = []
        for i, j in INDEX_PAIRS:
            second_part = -0.5 * hessian_trace(1 + slot_of(i, j))
            connection_part = 0.5 * total(
                [metric[k][i] * grad[18 + k][j] + metric[k][j] * grad[18 + k][i] for k in range(3)]
            )
            contracted_part = 0.5 * total(
                [contracted[k] * (lowered[i][j][k] + lowered[j][i][k]) for k in range(3)]
            )
            if i == j:
                quadratic = total(
                    [
                        raised[k][l][i] * (2.0 * mixed[l][i][k] + mixed[l][k][i])
                        for k in range(3)
                        for l in range(3)
                    ]
                )
            else:
                quadratic = total(
                    [
                        raised[k][l][i] * (mixed[l][j][k] + mixed[l][k][j])
                        + raised[k][l][j] * mixed[l][i][k]
                        for k in range(3)
                        for l in range(3)
                    ]
                )
            conformal_part = (
                chi_cov[i][j] * half_chi
                + metric[i][j] * metric_factor
                - chi_grad[i] * chi_grad[j] * quarter_sq
            )
            ricci.append(
                second_part + connection_part + contracted_part + quadratic + conformal_part
            )
        ricci = symmetric(ricci)
        ricci_scalar = conformal * trace_with(inverse, ricci)
        stress_trace = conformal * trace_with(inverse, stress)

        up_a = [
            [total([inverse[i][k] * traceless[k][j] for k in range(3)]) for j in range(3)]
            for i in range(3)
        ]
        raised_a = symmetric(
            [total([up_a[i][l] * inverse[j][l] for l in range(3)]) for i, j in INDEX_PAIRS]
        )
        a_square = trace_with(traceless, raised_a)
        shift_div = shift_grad[0][0] + shift_grad[1][1] + shift_grad[2][2]
        two_thirds_div = (2.0 / 3.0) * shift_div

        def finish(q, rate):
            rate = rate + dot(shift, grad[q]) + damped[q]
            st_rate[q, pl.ds(base, half), :] = rate

        finish(0, (2.0 / 3.0) * conformal * (lapse * trace_k - shift_div))
        finish(7, -2.0 * lapse * extrinsic)
        for i in range(3):
            finish(8 + i, 0.75 * connection[i] - SHIFT_DAMPING * shift[i])
        finish(
            11,
            lapse
            * (
                a_square
                + trace_k * trace_k * (1.0 / 3.0)
                + FOUR_PI * (stress_trace + density)
                + KAPPA_ONE * theta
            )
            - lapse_lap,
        )
        source = symmetric(
            [
                lapse * (ricci[i][j] - 2.0 * FOUR_PI * stress[i][j]) - lapse_cov[i][j]
                for i, j in INDEX_PAIRS
            ]
        )
        third_trace = trace_with(inverse, source) * (1.0 / 3.0)
        for s, (i, j) in enumerate(INDEX_PAIRS):
            finish(
                1 + s,
                total(
                    [
                        metric[i][k] * shift_grad[j][k] + metric[j][k] * shift_grad[i][k]
                        for k in range(3)
                    ]
                )
                - metric[i][j] * two_thirds_div
                - 2.0 * lapse * traceless[i][j],
            )
            product = total([traceless[i][k] * up_a[k][j] for k in range(3)])
            finish(
                12 + s,
                total(
                    [
                        traceless[i][k] * shift_grad[j][k] + traceless[j][k] * shift_grad[i][k]
                        for k in range(3)
                    ]
                )
                - traceless[i][j] * two_thirds_div
                + conformal * (source[i][j] - metric[i][j] * third_trace)
                + lapse * (trace_k * traceless[i][j] - 2.0 * product),
            )
        for i in range(3):
            bracket = (
                trace_with(raised_a, raised[i])
                - 1.5 * dot(raised_a[i], chi_grad) * over_chi
                - dot(inverse[i], [2.0 * grad[11][j] + grad[21][j] for j in range(3)]) * (1.0 / 3.0)
                - 2.0 * FOUR_PI * dot(inverse[i], momentum)
            )
            spread = [
                seconds[8, 0] + seconds[10, 2],
                seconds[9, 3] + seconds[10, 4],
                seconds[8, 2] + seconds[9, 4] + seconds[10, 5],
            ]
            finish(
                18 + i,
                contracted[i] * two_thirds_div
                - total([contracted[j] * shift_grad[j][i] for j in range(3)])
                + hessian_trace(8 + i)
                + dot(inverse[i], spread) * (1.0 / 3.0)
                - 2.0 * dot(raised_a[i], lapse_grad)
                + 2.0
                * lapse
                * (bracket - KAPPA_ONE * (connection[i] - contracted[i])),
            )
        finish(
            21,
            0.5
            * lapse
            * (
                ricci_scalar
                - a_square
                + (2.0 / 3.0) * trace_k * trace_k
                - 4.0 * FOUR_PI * density
            )
            - 2.0 * KAPPA_ONE * lapse * theta,
        )

    for index in range(own):
        pair_step(index)


def late_kernel(
    cells, zst, zfl, x_below, y_first, x_above, y_second, c_first, c_second, line_two, line_top,
    st_rate, hydro_rate, slopes, electric, st_out, fl_out,
):
    halo = Halo(
        cells, zst, zfl, x_below, y_first, x_above, y_second, c_first, c_second
    )
    x_below, x_above = halo.x_below, halo.x_above
    t, fields, half, own = halo.t, halo.fields, halo.half, halo.own
    inner, span = halo.inner, halo.span

    top = jnp.maximum(line_top[...], line_two[...])
    for lines in (c_first, c_second):
        top = jnp.maximum(top, lines[CORNER_TILES - 1, TOP_ROW : TOP_ROW + 1, :])
    dt = COURANT / top

    for p in inner:
        place = slice((p - 1) * half, p * half)
        mixed = []
        for q in range(CURVED):
            s_m, s_c, s_p = (
                halo.beside(q, n) if 1 <= n <= own else halo.corner(q, n) for n in (p - 1, p, p + 1)
            )
            slope = slopes[q, p - 1]
            slope_side = first_diff(s_m, t.odd_swapped(s_m, s_c), t.odd_swapped(s_c, s_p), s_p)
            mixed.append(
                first_diff(
                    t.y_down(slope, slope_side, 2),
                    t.y_down(slope, slope_side, 1),
                    t.y_up(slope, slope_side, 1),
                    t.y_up(slope, slope_side, 2),
                )
            )
        conformal, lapse = halo.main(0, p), halo.main(7, p)
        metric = [halo.main(1 + s, p) for s in range(6)]
        inverse = inverse_metric(symmetric(metric))
        half_chi = 0.5 / conformal
        cross = inverse[0][1]
        chi_trace = 2.0 * cross * mixed[0] * half_chi
        ricci = [metric[s] * chi_trace - cross * mixed[1 + s] for s in range(6)]
        ricci[1] = ricci[1] + mixed[0] * half_chi
        source = [lapse * r for r in ricci]
        source[1] = source[1] - mixed[7]
        third_trace = trace_with(inverse, symmetric(source)) * (1.0 / 3.0)
        extra = {
            11: -2.0 * conformal * cross * mixed[7],
            21: 0.5 * lapse * conformal * trace_with(inverse, symmetric(ricci)),
        }
        for s in range(6):
            extra[12 + s] = conformal * (source[s] - metric[s] * third_trace)
        for i in range(3):
            extra[18 + i] = 2.0 * cross * mixed[8 + i] + (1.0 / 3.0) * (
                inverse[i][0] * mixed[9] + inverse[i][1] * mixed[8]
            )
        for q in range(fields):
            rate = st_rate[q, place, :]
            if q in extra:
                rate = rate + extra[q]
            st_out[q, place, :] = halo.main(q, p) + dt * rate

    end = own + 1
    ends = (0, end)
    bx_face, by_face, bz_face = ({p: halo.corner(fields + 5 + i, p) for p in ends} for i in range(3))
    layers = {p: halo.corner_layers(p) for p in ends}
    bx_face[end] = layers[end]
    by_face[0] = jnp.where(t.slot < 2, layers[0], by_face[0])
    centred = [{}, {}, {}]
    for p in ends:
        following = halo.beside(fields + 5, 1) if p == 0 else bx_face[p]
        edge_cells = x_below if p == 0 else x_above
        dx = 0.5 * (t.odd_swapped(bx_face[p], following) - bx_face[p])
        dy = 0.5 * (t.y_up(by_face[p], edge_cells[fields + 6], 1) - by_face[p])
        centred[0][p] = bx_face[p] + dx
        centred[1][p] = by_face[p] + dy
        centred[2][p] = bz_face[p] - (dx + dy)
    corners = [{p: halo.corner(q, p) for p in ends} for q in [0, 7] + list(range(fields, fields + 5))]
    found = primitives(
        half, [(0, p) for p in ends], [[c] for c in corners[2:]], [[c] for c in centred],
        [corners[0]], [corners[1]], 2,
    )
    ez_h = [found[0, 0][10]] + [electric[own + p] for p in inner] + [found[0, end][10]]
    ez_x_h = [None] + [ez_h[p] + t.odd_swapped(ez_h[p - 1], ez_h[p]) for p in span[1:]]
    ez_x = [None] + [electric[p - 1] for p in span[1:]]
    edge_z = [None] + [ez_x[p] + t.y_down(ez_x[p], ez_x_h[p], 1) for p in span[1:]]
    quarter = 0.25 * dt
    for p in inner:
        place = slice((p - 1) * half, p * half)
        edge_z_h = ez_x_h[p] + t.y_down(ez_x_h[p], ez_x[p], 1)
        for q in range(5):
            fl_out[q, place, :] = halo.main(fields + q, p) + dt * hydro_rate[q, place, :]
        x_rate = hydro_rate[5, place, :] - (t.y_up(edge_z[p], edge_z_h, 1) - edge_z[p])
        y_rate = hydro_rate[6, place, :] + (t.odd(edge_z[p], edge_z[p + 1]) - edge_z[p])
        z_rate = hydro_rate[7, place, :]
        for i, rate in enumerate((x_rate, y_rate, z_rate)):
            fl_out[5 + i, place, :] = halo.main(fields + 5 + i, p) + quarter * rate


def per_device(spacetime, fluid):
    fields, cx, cy, cz = spacetime.shape
    rows = cx * cy
    st = spacetime.reshape(fields, rows, cz)
    fl = fluid.reshape(FLUID, rows, cz)
    sizes = [lax.axis_size(a) for a in ("gx", "gy", "gz")]
    tile = (2 * cy, cz)
    f32 = jnp.float32

    def shape(*dims):
        return jax.ShapeDtypeStruct(dims, f32)

    def beyond(cells):
        n = sizes[2]
        after = lax.ppermute(cells, "gz", [((i + 1) % n, i) for i in range(n)])
        if n == 2:
            return after
        before = lax.ppermute(cells, "gz", [(i, (i + 1) % n) for i in range(n)])
        lane = lax.broadcasted_iota(jnp.int32, cells.shape, 2)
        return jnp.where(lane < cz // 2, after, before)

    params = pltpu.CompilerParams(vmem_limit_bytes=48 * 1024 * 1024)
    zst, zfl = beyond(st), beyond(fl)
    cells = jnp.concatenate([st, fl], axis=0)
    face = shape(face_tiles(fields), *tile)
    corner = shape(CORNER_TILES, *tile)
    lane_row = shape(1, cz)
    def call(kernel, outs, name, operands, scratch=()):
        return pl.pallas_call(
            kernel,
            out_shape=outs,
            scratch_shapes=scratch,
            compiler_params=params,
            name=name,
        )(*operands)

    def shift(cells, step):
        n = lax.axis_size("gx")
        return lax.ppermute(cells, "gx", [(i, (i + step) % n) for i in range(n)])

    def trade(cells, first):
        axis = "gy"
        n = lax.axis_size(axis)
        step = [1, -1] if first else [-1, 1]
        return lax.ppermute(cells, axis, [(i, (i + step[i % 2]) % n) for i in range(n)])

    def two_away(cells, axis):
        n = lax.axis_size(axis)
        return lax.ppermute(cells, axis, [(i, (i + 2) % n) for i in range(n)]) if n == 4 else cells

    short = sizes[0] <= 4 and sizes[1] <= 4 and sizes[2] <= 2
    x_low, x_high, y_first, y_second, top = call(
        pack_kernel, [face] * 4 + [lane_row], "pack", (cells, zst, zfl)
    )
    x_below = shift(x_high, 1)
    y_first = trade(y_first, True)
    x_above = shift(x_low, -1)
    y_second = trade(y_second, False)
    top_two = two_away(top, "gx")
    c_first, c_second, line_top = call(
        relay_kernel,
        [corner, corner, lane_row],
        "relay",
        (x_below, x_above, y_first, top, top_two),
    )
    c_first = trade(c_first, True)
    c_second = trade(c_second, False)
    if short:
        line_two = two_away(line_top, "gy")
    else:
        line_two = lax.pmax(line_top, ("gx", "gy", "gz"))
    own = cx // 2
    arrived = (cells, zst, zfl, x_below, y_first, x_above, y_second)
    early = call(
        early_kernel,
        [
            shape(*st.shape),
            shape(FLUID, rows, cz),
            shape(CURVED, own, *tile),
            shape(2 * own + 1, *tile),
        ],
        "early",
        arrived,
        [
            pltpu.VMEM((fields, own + 4) + tile, f32),
            pltpu.VMEM((fields, own) + tile, f32),
            pltpu.VMEM((fields, own) + tile, f32),
            pltpu.VMEM((CURVED, own + 2) + tile, f32),
            pltpu.VMEM((CURVED, own) + tile, f32),
            pltpu.VMEM((fields, 3) + tile, f32),
            pltpu.VMEM((CURVED, 6) + tile, f32),
            pltpu.VMEM((fields,) + tile, f32),
            pltpu.VMEM((own, 11) + tile, f32),
        ],
    )
    st_next, fl_next = call(
        late_kernel,
        [shape(*st.shape), shape(*fl.shape)],
        "late",
        (*arrived, c_first, c_second, line_two, line_top, *early),
    )
    return st_next.reshape(spacetime.shape), fl_next.reshape(fluid.shape)


def solution(mesh):
    spec = P(None, "gx", "gy", "gz")
    return jax.shard_map(
        per_device, mesh=mesh, in_specs=(spec, spec), out_specs=(spec, spec), check_vma=False
    )
```

```python
import functools
import math

import jax
import jax.numpy as jnp
from jax import lax
from jax.experimental import pallas as pl
from jax.experimental.pallas import tpu as pltpu
from jax.sharding import PartitionSpec as P

RECOVERY_STEPS = 4
INDEX_PAIRS = ((0, 0), (0, 1), (0, 2), (1, 1), (1, 2), (2, 2))
COURANT = 0.25
DISSIPATION = 0.2
KAPPA_ONE = 0.02
SHIFT_DAMPING = 1.0
SPEED_CAP = 0.99
PRESSURE_FLOOR = 0.01
FOUR_PI = 4.0 * math.pi

BATCH = 6
CURVED = 11
FLUID = 8


def total(pieces):
    summed = pieces[0]
    for member in pieces[1:]:
        summed = summed + member
    return summed


def dot(first_vec, second_vec):
    return total([first_vec[i] * second_vec[i] for i in range(3)])


def slot_of(i, j):
    return INDEX_PAIRS.index((min(i, j), max(i, j)))


def symmetric(entries):
    return [[entries[slot_of(i, j)] for j in range(3)] for i in range(3)]


def trace_with(inverse, tensor):
    return (
        inverse[0][0] * tensor[0][0]
        + inverse[1][1] * tensor[1][1]
        + inverse[2][2] * tensor[2][2]
        + 2.0
        * (
            inverse[0][1] * tensor[0][1]
            + inverse[0][2] * tensor[0][2]
            + inverse[1][2] * tensor[1][2]
        )
    )


def inverse_metric(metric):
    cofactor = [
        metric[1][1] * metric[2][2] - metric[1][2] * metric[1][2],
        metric[0][2] * metric[1][2] - metric[0][1] * metric[2][2],
        metric[0][1] * metric[1][2] - metric[0][2] * metric[1][1],
        metric[0][0] * metric[2][2] - metric[0][2] * metric[0][2],
        metric[0][1] * metric[0][2] - metric[0][0] * metric[1][2],
        metric[0][0] * metric[1][1] - metric[0][1] * metric[0][1],
    ]
    determinant = (
        metric[0][0] * cofactor[0] + metric[0][1] * cofactor[1] + metric[0][2] * cofactor[2]
    )
    over = 1.0 / determinant
    return symmetric([c * over for c in cofactor])


class Tile:
    def __init__(self, cy, cz):
        self.cy, self.rows, self.lanes = cy, 2 * cy, cz
        shape = (self.rows, cz)
        self.row = lax.broadcasted_iota(jnp.int32, shape, 0)
        self.lane = lax.broadcasted_iota(jnp.int32, shape, 1)
        self.slot = lax.rem(self.row, cy)

    def turn(self, tile, amount):
        amount = amount % self.rows
        return tile if amount == 0 else pltpu.roll(tile, amount, 0)

    def spin(self, tile, amount):
        amount = amount % self.lanes
        return tile if amount == 0 else pltpu.roll(tile, amount, 1)

    def swap(self, tile):
        return self.turn(tile, self.cy)

    def odd(self, a, b):
        return self.turn(jnp.where(self.row < self.cy, b, a), self.cy)

    def odd_swapped(self, a, b):
        return self.turn(jnp.where(self.row < self.cy, a, b), self.cy)

    def y_up(self, main, beyond, k):
        return self.turn(jnp.where(self.slot < k, beyond, main), -k)

    def y_down(self, main, beyond, k):
        return self.turn(jnp.where(self.slot >= self.cy - k, beyond, main), k)

    def z_up(self, main, beyond, k):
        return self.spin(jnp.where(self.lane < k, beyond, main), -k)

    def z_down(self, main, beyond, k):
        return self.spin(jnp.where(self.lane >= self.lanes - k, beyond, main), k)

    def corner_rows(self, side, turn):
        places = ((0, 2), (self.cy - 1, self.cy + 1))[side]
        first, second = [(place + turn) % self.rows for place in places]
        return (self.row == first) | (self.row == second)

    def join_low(self, u, v):
        return jnp.where(self.slot < 2, self.swap(u), self.turn(v, 2))

    def join_high(self, u, v):
        return jnp.where(self.slot >= self.cy - 2, self.swap(u), self.turn(self.swap(v), -2))

    def part_first(self, from_above, from_below):
        return jnp.where(self.slot < 2, from_above, from_below)

    def part_second(self, from_above, from_below):
        return self.turn(jnp.where(self.slot < 2, from_below, from_above), 2)


def edge_list(tiles):
    fields = next(n for n in range(tiles) if face_tiles(n) == tiles)
    return list(range(CURVED)) + list(range(fields, fields + FLUID))


CORNER_TURNS = (0, 1, 4, 5)
CORNER_TILES = CURVED + FLUID // 4 + 1
TOP_ROW = 6


def face_tiles(fields):
    return fields + FLUID + len(pairs_of(third_list(fields))) + 1


def third_list(fields):
    return list(range(fields + 1))


def pairs_of(items):
    return [(items[i], items[min(i + 1, len(items) - 1)]) for i in range(0, len(items), 2)]


def top_speed(st):
    inverse = inverse_metric(symmetric([st[1 + s] for s in range(6)]))
    scale = 2.0 * st[7] * st[0]
    speeds = [jnp.abs(st[8 + d]) + jnp.sqrt(scale * inverse[d][d]) for d in range(3)]
    top = jnp.maximum(jnp.maximum(speeds[0], speeds[1]), speeds[2])
    return jnp.max(jnp.max(top, axis=1, keepdims=True), axis=0, keepdims=True)


class Chosen:
    def __init__(self, first, second, swapped):
        self.first, self.second, self.swapped, self.shape = first, second, swapped, first.shape

    def __getitem__(self, key):
        return jnp.where(self.swapped, self.second[key], self.first[key])


class Sent:
    def __init__(self, first, second, swapped):
        self.first, self.second, self.swapped, self.shape = first, second, swapped, first.shape

    def put(self, key, lower, upper):
        self.first[key] = jnp.where(self.swapped, upper, lower)
        self.second[key] = jnp.where(self.swapped, lower, upper)


class Joined:
    def __init__(self, tiles, tail):
        self.tiles, self.tail = tiles, tail
        self.shape = tuple(tiles.shape)

    def __getitem__(self, key):
        q, rows = (key[0], key[1:]) if isinstance(key, tuple) else (key, ())
        if q == self.tiles.shape[0] - 1:
            return self.tail[(0,) + rows]
        return self.tiles[(q,) + rows]


def even_along_y(tile):
    return jnp.full(tile, lax.rem(lax.axis_index("gy"), 2), jnp.int32) == 0


def pack_up_kernel(cells, x_high):
    count, rows, lanes = cells.shape
    fields, half = count - FLUID, rows // 2
    t = Tile(rows // 4, lanes)
    for q in range(count):
        x_high[q] = cells[q, half:rows, :]
    for n, (a, b) in enumerate(pairs_of(list(range(fields)) + [fields + 5])):
        x_high[count + n] = jnp.where(
            t.row < t.cy, t.swap(cells[b, 0:half, :]), cells[a, 0:half, :]
        )
    x_high[x_high.shape[0] - 1] = jnp.zeros_like(x_high[0])


def pack_kernel(cells, zst, zfl, *outs):
    fields, rows, lanes = zst.shape
    st, fl = cells.at[0:fields], cells.at[fields : fields + FLUID]
    cy = rows // 4
    t = Tile(cy, lanes)
    x_low, x_high_lanes, y_first, y_second, top_out = outs
    half = t.rows
    to_y = Sent(y_first, y_second, even_along_y((half, lanes)))

    def own(ref, q):
        return [ref[q, 0:half, :], ref[q, half : 2 * half, :]]

    tiles, beyond = [], []
    for q in range(fields):
        tiles.append(own(st, q))
        beyond.append(own(zst, q) if q < CURVED else None)
    for q in range(FLUID):
        tiles.append(own(fl, q))
        beyond.append(own(zfl, q))

    packed = [None] * 4
    place_count = 0
    for q, (first, second) in enumerate(tiles):
        x_low[q] = first
        to_y.put(q, t.join_low(first, second), t.join_high(first, second))
        if beyond[q] is not None:
            zf, zs = beyond[q]
            for m, piece in enumerate((zf, zs, t.join_low(zf, zs), t.join_high(zf, zs))):
                piece = t.spin(piece, 4 * place_count + 2)
                packed[m] = (
                    piece if place_count == 0 else jnp.where(t.lane < 4 * place_count, packed[m], piece)
                )
            place_count += 1
    for n, (a, b) in enumerate(pairs_of(third_list(fields))):
        slot = fields + FLUID + n
        xa, xb = (tiles[q if q < fields else fields + 5] for q in (a, b))
        x_low[slot] = jnp.where(t.row < cy, xa[1], t.swap(xb[1]))
        ya, yb = (tiles[q if q < fields else fields + 6] for q in (a, b))
        w = [t.swap(ya[0]), t.swap(ya[1]), t.swap(yb[0]), t.swap(yb[1])]
        s = t.slot
        low = jnp.where(s == 0, t.turn(w[2], -2), t.turn(w[3], -1))
        low = jnp.where(s == 2, w[0], jnp.where(s == 3, t.turn(w[1], 1), low))
        high = jnp.where(s == 3, t.turn(w[2], 2), t.turn(w[3], 1))
        high = jnp.where(s == 1, w[0], jnp.where(s == 0, t.turn(w[1], -1), high))
        to_y.put(slot, low, high)
    top = jnp.maximum(top_speed(st), top_speed(zst))
    top_out[...] = jnp.broadcast_to(top, top_out.shape)
    last = x_low.shape[0] - 1
    x_lanes = [jnp.where(t.lane < 4 * place_count, piece, top) for piece in packed[:2]]
    y_lanes = [jnp.where(t.lane < 4 * place_count, piece, top) for piece in packed[2:]]
    x_low[last], x_high_lanes[0] = x_lanes
    to_y.put(last, *y_lanes)


def relay_kernel(x_below, below_lanes, x_above, y_first, top, top_two, c_first, c_second, line_top):
    cy, lanes = x_below.shape[1] // 2, x_below.shape[2]
    t = Tile(cy, lanes)
    to_y = Sent(c_first, c_second, even_along_y((t.rows, lanes)))
    x_below = Joined(x_below, below_lanes)
    last = x_below.shape[0] - 1
    line = jnp.maximum(top[...], top_two[...])
    for beside in (x_below, x_above, y_first):
        line = jnp.maximum(line, beside[last, 0:1, lanes - 1 : lanes])
    line_top[...] = line
    edge = edge_list(x_below.shape[0])
    for q in range(CURVED):
        below, above = x_below[q], x_above[q]
        to_y.put(q, t.join_low(below, above), t.join_high(below, above))
    for n in range(0, FLUID, 4):
        low, high = None, None
        for turn, q in zip(CORNER_TURNS, edge[CURVED + n : CURVED + n + 4]):
            below, above = x_below[q], x_above[q]
            below, above = (t.turn(j(below, above), turn) for j in (t.join_low, t.join_high))
            if low is None:
                low, high = below, above
            else:
                low = jnp.where(t.corner_rows(0, turn), below, low)
                high = jnp.where(t.corner_rows(1, turn), above, high)
        to_y.put(CURVED + n // 4, low, high)
    along_x, along_y = edge[CURVED + 5], edge[CURVED + 6]
    low = t.join_low(x_below[along_y], x_above[along_y])
    high = t.join_high(x_below[along_x], x_above[along_x])
    low, high = (jnp.where(t.row == TOP_ROW, line, tile) for tile in (low, high))
    to_y.put(CORNER_TILES - 1, low, high)


def limited(a, b):
    return jnp.maximum(jnp.minimum(a, b), 0.0) + jnp.minimum(jnp.maximum(a, b), 0.0)


def recover(conserved, magnetic):
    density = conserved[0]
    momenta = conserved[1:4]
    energy = conserved[4] + density
    mom_sq = dot(momenta, momenta)
    mag_sq = dot(magnetic, magnetic)
    cross = dot(momenta, magnetic)
    cross_sq = cross * cross

    def state(z):
        grown = z + mag_sq
        over = 1.0 / (z * grown)
        speed_sq = (mom_sq * z * z + cross_sq * (2.0 * z + mag_sq)) * over * over
        kept = 1.0 - jnp.minimum(speed_sq, SPEED_CAP)
        rest = density * jnp.sqrt(kept)
        return kept, rest, 0.5 * (z * kept - rest), grown * over

    z = jnp.maximum(energy - 0.5 * mag_sq, density)
    for _ in range(RECOVERY_STEPS):
        kept, rest, pressure, over_z = state(z)
        residual = (
            z
            + mag_sq
            - pressure
            - 0.5 * mag_sq * kept
            - 0.5 * cross_sq * over_z * over_z
            - energy
        )
        z = jnp.maximum(z - residual / (1.0 - 0.5 * kept), density)
    kept, rest, pressure, over_z = state(z)
    pressure = jnp.maximum(pressure, PRESSURE_FLOOR * rest)
    scale = lax.rsqrt(kept) / (z + mag_sq)
    along = cross * over_z
    four_vel = [scale * (momenta[i] + along * magnetic[i]) for i in range(3)]
    return [rest, pressure] + four_vel


def stress_parts(rest, pressure, u, magnetic):
    lorentz_sq = 1.0 + dot(u, u)
    over = lax.rsqrt(lorentz_sq)
    over_sq = over * over
    time_b = dot(u, magnetic)
    grown_b = [magnetic[i] + time_b * u[i] for i in range(3)]
    b_square = (dot(magnetic, magnetic) + time_b * time_b) * over_sq
    enthalpy = rest + 2.0 * pressure
    inertia = enthalpy + b_square
    return lorentz_sq, over, over_sq, time_b, grown_b, b_square, enthalpy, inertia


def face_state(rest, pressure, u, magnetic, d):
    lorentz_sq, over, over_sq, time_b, grown_b, b_square, enthalpy, inertia = stress_parts(
        rest, pressure, u, magnetic
    )
    total_pressure = pressure + 0.5 * b_square
    lorentz = lorentz_sq * over
    density = rest * lorentz
    carried = inertia * lorentz
    time_over = time_b * over
    conserved = [density]
    conserved += [carried * u[j] - time_over * grown_b[j] for j in range(3)]
    conserved += [inertia * lorentz_sq - total_pressure - time_b * time_b - density]
    mass_flux = rest * u[d]
    flux = [mass_flux]
    pushed = inertia * u[d]
    b_over = grown_b[d] * over_sq
    for j in range(3):
        flux_j = pushed * u[j] - b_over * grown_b[j]
        flux.append(flux_j + total_pressure if j == d else flux_j)
    flux.append(carried * u[d] - time_over * grown_b[d] - mass_flux)
    ratio = 1.0 / (enthalpy * inertia)
    sound_sq = 2.0 * pressure * inertia * ratio
    alfven_sq = b_square * enthalpy * ratio
    fast_sq = sound_sq + alfven_sq - sound_sq * alfven_sq
    slow = 1.0 - fast_sq
    velocity = u[d] * over
    rest_part = 1.0 - dot(u, u) * over_sq * fast_sq
    spread = jnp.sqrt(fast_sq * over_sq * (rest_part - velocity * velocity * slow))
    fastest = (jnp.abs(velocity * slow) + spread) / rest_part
    return conserved, flux, fastest


def face_flux(left, right, normal, weight, d):
    sides = []
    for state in (left, right):
        magnetic = [normal if i == d else state[5 + i] for i in range(3)]
        sides.append(face_state(state[0], state[1], state[2:5], magnetic, d))
    (cons_l, flux_l, fast_l), (cons_r, flux_r, fast_r) = sides
    signal = jnp.maximum(fast_l, fast_r)
    scale = 0.5 * weight
    return [scale * (flux_l[q] + flux_r[q] - signal * (cons_r[q] - cons_l[q])) for q in range(5)]


def volume_over(conformal):
    return conformal * jnp.sqrt(conformal)


def first_diff(down_two, down, up, up_two):
    return (8.0 / 12.0) * (up - down) + (1.0 / 12.0) * (down_two - up_two)


class Halo:
    def __init__(self, cells, zst, zfl, x_below, y_first, x_above, y_second, below_lanes, *corners):
        x_below = Joined(x_below, below_lanes)
        self.fields, self.block, self.lanes = zst.shape
        even_y = even_along_y((self.block // 2, self.lanes))
        y_below, y_above = Chosen(y_first, y_second, even_y), Chosen(y_second, y_first, even_y)
        if corners:
            c_first, c_second = corners
            self.c_below = Chosen(c_first, c_second, even_y)
            self.c_above = Chosen(c_second, c_first, even_y)
        self.st = cells.at[0 : self.fields]
        self.fl = cells.at[self.fields : self.fields + FLUID]
        self.zst, self.zfl = zst, zfl
        self.x_below, self.x_above = x_below, x_above
        self.y_below, self.y_above = y_below, y_above
        self.cy = self.block // 4
        self.t = Tile(self.cy, self.lanes)
        self.half = self.t.rows
        self.own = self.block // self.half
        self.inner = range(1, self.own + 1)
        self.span = range(self.own + 2)
        self.edge = edge_list(x_below.shape[0])
        self.last = x_below.shape[0] - 1

    def rows_of(self, ref, q, p):
        return ref[q, (p - 1) * self.half : p * self.half, :]

    def main(self, q, p):
        if q < self.fields:
            return self.rows_of(self.st, q, p)
        return self.rows_of(self.fl, q - self.fields, p)

    def beyond(self, q, p):
        if q < self.fields:
            return self.rows_of(self.zst, q, p)
        return self.rows_of(self.zfl, q - self.fields, p)

    def part(self, second):
        return self.t.part_second if second else self.t.part_first

    def beside(self, q, p):
        return self.part(p == 2)(self.y_above[q], self.y_below[q])

    def third_place(self, q):
        return self.fields + FLUID + q // 2, q % 2

    def x_third(self, q, upper):
        tile, which = self.third_place(q)
        found = self.x_above[tile] if upper else self.x_below[tile]
        return self.t.swap(found) if which else found

    def y_third(self, q, p):
        t = self.t
        tile, which = self.third_place(q)
        turn_above, turn_below = ((0, 0), (-1, 1), (2, -2), (1, -1))[2 * which + p - 1]
        above, below = t.turn(self.y_above[tile], turn_above), t.turn(self.y_below[tile], turn_below)
        return jnp.where(t.slot == 2, above, below)

    def z_place(self, q):
        return 4 * self.edge.index(q) + 2

    def x_beyond(self, q, upper):
        tile = self.x_above[self.last] if upper else self.x_below[self.last]
        return self.t.spin(tile, -self.z_place(q))

    def y_beyond(self, q, p):
        return self.t.spin(self.beside(self.last, p), -self.z_place(q))

    def corner(self, q, p):
        place, turn = q, 0
        if q >= CURVED:
            n = q - self.fields
            place, turn = CURVED + n // 4, CORNER_TURNS[n % 4]
        above, below = self.t.turn(self.c_above[place], -turn), self.t.turn(self.c_below[place], -turn)
        return self.part(p > 0)(above, below)

    def corner_layers(self, p):
        place = CORNER_TILES - 1
        return self.part(p > 0)(self.c_above[place], self.c_below[place])

    def plane(self, q):
        inner = self.inner
        return (
            [self.x_below[q]] + [self.main(q, p) for p in inner] + [self.x_above[q]],
            [None] + [self.beside(q, p) for p in inner] + [None],
            [self.x_beyond(q, False)]
            + [self.beyond(q, p) for p in inner]
            + [self.x_beyond(q, True)],
            [None] + [self.y_beyond(q, p) for p in inner] + [None],
        )


def weigh(chi_face, alpha_face):
    shrink = volume_over(chi_face)
    return shrink, alpha_face / shrink


def primitives(half, spots, cons, centred, chi, alpha, batch):
    found = {}
    for start in range(0, len(spots), batch):
        group = spots[start : start + batch]

        def gather(planes):
            return jnp.concatenate([planes[k][p] for k, p in group], axis=0)

        shrink = volume_over(gather(chi))
        mag_raw = [gather(centred[i]) for i in range(3)]
        mag = [m * shrink for m in mag_raw]
        values = recover([gather(c) * shrink for c in cons], mag)
        u = values[2:5]
        factor = gather(alpha) * lax.rsqrt(1.0 + dot(u, u))
        field = [
            factor * (u[(i + 2) % 3] * mag_raw[(i + 1) % 3] - u[(i + 1) % 3] * mag_raw[(i + 2) % 3])
            for i in range(3)
        ]
        for n, spot in enumerate(group):
            found[spot] = [value[n * half : (n + 1) * half] for value in values + mag + field]
    return found


def ring_fluxes(prims, chi, alpha, normals, d, up, down):
    found = []
    for here, there in ((0, 1), (1, 0)):
        left, right = [], []
        for a, b in zip(prims[here], prims[there]):
            below = down(a, b, 1)
            middle = a - below
            left.append(below + 0.5 * limited(below - down(a, b, 2), middle))
            right.append(a - 0.5 * limited(middle, up(a, b, 1) - a))
        shrink, weight = weigh(
            0.5 * (chi[here] + down(chi[here], chi[there], 1)),
            0.5 * (alpha[here] + down(alpha[here], alpha[there], 1)),
        )
        found.append(face_flux(left, right, normals[here] * shrink, weight, d))
    return [a - up(a, b, 1) for a, b in zip(*found)]


def early_kernel(
    cells, zst, zfl, x_below, y_first, x_above, y_second, below_lanes,
    st_rate, hydro_rate, slopes, electric, pairs, sides, thirds, pairs_z, sides_z, grads, seconds, damped, tensors,
):
    halo = Halo(cells, zst, zfl, x_below, y_first, x_above, y_second, below_lanes)
    t, fields, half, own, cy = halo.t, halo.fields, halo.half, halo.own, halo.cy
    st, fl, inner = halo.st, halo.fl, halo.inner

    for q in range(fields):
        pairs[q, 0] = halo.x_third(q, False)
        pairs[q, 1] = x_below[q]
        for p in inner:
            pairs[q, 1 + p] = halo.main(q, p)
            sides[q, p - 1] = halo.beside(q, p)
            thirds[q, p - 1] = halo.y_third(q, p)
        pairs[q, 2 + own] = x_above[q]
        pairs[q, 3 + own] = halo.x_third(q, True)
        if q < CURVED:
            pairs_z[q, 0] = halo.x_beyond(q, False)
            pairs_z[q, own + 1] = halo.x_beyond(q, True)
            for p in inner:
                pairs_z[q, p] = halo.beyond(q, p)
                sides_z[q, p - 1] = halo.y_beyond(q, p)

    span = halo.span
    face = [halo.plane(fields + 5 + i) for i in range(3)]

    def halves(kind, p):
        own_x, own_y, own_z = (f[kind][p] for f in face)
        pair = kind in (0, 2)
        known_x = pair or p < own
        last = kind == 0 and p == own + 1
        if pair:
            next_x = halo.x_third(fields, True) if last else face[0][kind][min(p + 1, own + 1)]
            next_x = t.odd(own_x, next_x)
        else:
            next_x = t.odd_swapped(own_x, face[0][kind][p + 1] if known_x else own_x)
        dx = 0.5 * (next_x - own_x)
        dz = 0.5 * (t.z_up(own_z, face[2][kind ^ 2][p], 1) - own_z)
        inside = 1 <= p <= own
        if not pair:
            here = jnp.where(t.slot == 2, halo.y_third(fields, p), own_y) if kind == 1 else own_y
            next_y = t.y_up(here, face[1][kind ^ 1][p], 1)
        else:
            next_y = t.y_up(own_y, face[1][kind ^ 1][p] if inside else own_y, 1)
        dy = 0.5 * (next_y - own_y)
        if pair and not inside:
            dy = jnp.where(t.slot == cy - 1, -(dx + dz), dy)
        if not pair and not known_x:
            dx = jnp.where(t.row < cy, -(dy + dz), dx)
        return own_x + dx, own_y + dy, own_z + dz

    spots = [(0, p) for p in span] + [(1, p) for p in inner]
    spots += [(2, p) for p in span] + [(3, p) for p in inner]
    centred = [[[None] * (own + 2) for _ in range(4)] for _ in range(3)]
    for k, p in spots:
        for i, value in enumerate(halves(k, p)):
            centred[i][k][p] = value
    chi, alpha = halo.plane(0), halo.plane(7)
    found = primitives(
        half, spots, [halo.plane(fields + q) for q in range(5)], centred, chi, alpha, BATCH
    )

    lines = [[found[0, p][i] for p in span] for i in range(8)] + [chi[0], alpha[0]]
    odd_lines = [[t.odd(f[p], f[min(p + 1, own + 1)]) for p in span] for f in lines]
    fluxes = [None]
    for p in range(1, own + 2):
        left, right = [], []
        for f, o in zip(lines[:8], odd_lines):
            here = f[p] - o[p - 1]
            left.append(o[p - 1] + 0.5 * limited(o[p - 1] - f[p - 1], here))
            right.append(f[p] - 0.5 * limited(here, o[p] - f[p]))
        shrink, weight = weigh(
            0.5 * (lines[8][p] + odd_lines[8][p - 1]), 0.5 * (lines[9][p] + odd_lines[9][p - 1])
        )
        fluxes.append(face_flux(left, right, face[0][0][p] * shrink, weight, 0))
    for p in inner:
        changes = [
            ring_fluxes(
                [found[k, p][:8] for k in (0, kind)],
                [chi[k][p] for k in (0, kind)],
                [alpha[k][p] for k in (0, kind)],
                [face[d][k][p] for k in (0, kind)],
                d,
                up,
                down,
            )
            for d, kind, up, down in ((1, 1, t.y_up, t.y_down), (2, 2, t.z_up, t.z_down))
        ]
        for q in range(5):
            change = fluxes[p][q] - t.odd(fluxes[p][q], fluxes[p + 1][q])
            tensors[p - 1, 6 + q] = change + changes[0][q] + changes[1][q]
        rest, pressure = found[0, p][:2]
        u = found[0, p][2:5]
        parts = stress_parts(rest, pressure, u, found[0, p][5:8])
        lorentz_sq, over, over_sq, time_b, grown_b, b_square, enthalpy, inertia = parts
        total_pressure = pressure + 0.5 * b_square
        for s, (i, j) in enumerate(INDEX_PAIRS):
            value = inertia * u[i] * u[j] - over_sq * (grown_b[i] * grown_b[j])
            tensors[p - 1, s] = value + total_pressure if i == j else value

    ex, ey, ez = (
        [[found[k, p][8 + i] if (k, p) in found else None for p in span] for k in range(4)]
        for i in range(3)
    )
    ey_x = [
        [ey[k][p] + t.odd(ey[k][p - 1], ey[k][p]) if p else None for p in span] for k in (0, 2)
    ]
    edge_y = [None] + [ey_x[0][p] + t.z_down(ey_x[0][p], ey_x[1][p], 1) for p in span[1:]]
    for p in span[1:]:
        electric[p - 1] = ez[0][p] + t.odd(ez[0][p - 1], ez[0][p])
    for p in inner:
        electric[own + p] = ez[1][p]
        edge_y_z = ey_x[1][p] + t.z_down(ey_x[1][p], ey_x[0][p], 1)
        ex_y = ex[0][p] + t.y_down(ex[0][p], ex[1][p], 1)
        ex_y_h = ex[1][p] + t.y_down(ex[1][p], ex[0][p], 1)
        ex_y_z = ex[2][p] + t.y_down(ex[2][p], ex[3][p], 1)
        ex_y_hz = ex[3][p] + t.y_down(ex[3][p], ex[2][p], 1)
        edge_x = ex_y + t.z_down(ex_y, ex_y_z, 1)
        edge_x_h = ex_y_h + t.z_down(ex_y_h, ex_y_hz, 1)
        edge_x_z = ex_y_z + t.z_down(ex_y_z, ex_y, 1)
        place = slice((p - 1) * half, p * half)
        hydro_rate[5, place, :] = t.z_up(edge_y[p], edge_y_z, 1) - edge_y[p]
        hydro_rate[6, place, :] = edge_x - t.z_up(edge_x, edge_x_z, 1)
        hydro_rate[7, place, :] = (t.y_up(edge_x, edge_x_h, 1) - edge_x) - (
            t.odd(edge_y[p], edge_y[p + 1]) - edge_y[p]
        )

    def pair_step(index):
        p = index + 1
        base = index * half

        for q in range(fields):
            centre = pairs[q, p + 1]
            x_m3 = t.odd(pairs[q, p - 1], pairs[q, p])
            x_m2 = pairs[q, p]
            x_m1 = t.odd(pairs[q, p], centre)
            x_p1 = t.odd(centre, pairs[q, p + 2])
            x_p2 = pairs[q, p + 2]
            x_p3 = t.odd(pairs[q, p + 2], pairs[q, p + 3])
            side, third = sides[q, index], thirds[q, index]
            y_m1, y_m2 = t.y_down(centre, side, 1), t.y_down(centre, side, 2)
            y_p1, y_p2 = t.y_up(centre, side, 1), t.y_up(centre, side, 2)
            y_m3 = t.turn(
                jnp.where(t.slot >= cy - 2, side, jnp.where(t.slot == cy - 3, third, centre)), 3
            )
            y_p3 = t.turn(jnp.where(t.slot < 2, side, jnp.where(t.slot == 2, third, centre)), -3)
            beyond = zst[q, pl.ds(base, half), :]
            z_m1, z_m2, z_m3 = (t.z_down(centre, beyond, k) for k in (1, 2, 3))
            z_p1, z_p2, z_p3 = (t.z_up(centre, beyond, k) for k in (1, 2, 3))
            dx = first_diff(x_m2, x_m1, x_p1, x_p2)
            dy = first_diff(y_m2, y_m1, y_p1, y_p2)
            grads[q, 0] = dx
            if q < CURVED:
                slopes[q, index] = dx
            grads[q, 1] = dy
            grads[q, 2] = first_diff(z_m2, z_m1, z_p1, z_p2)
            near = [x_m1 + x_p1, y_m1 + y_p1, z_m1 + z_p1]
            far = [x_m2 + x_p2, y_m2 + y_p2, z_m2 + z_p2]
            outer = (x_m3 + x_p3) + (y_m3 + y_p3) + (z_m3 + z_p3)
            damped[q] = (DISSIPATION / 64.0) * (
                outer - 6.0 * (far[0] + far[1] + far[2]) + 15.0 * (near[0] + near[1] + near[2])
                - 60.0 * centre
            )
            if q < CURVED:
                for s, d in ((0, 0), (3, 1), (5, 2)):
                    seconds[q, s] = (1.0 / 12.0) * (16.0 * near[d] - far[d] - 30.0 * centre)
                b_m, b_c, b_p = pairs_z[q, p - 1], pairs_z[q, p], pairs_z[q, p + 1]
                dx_z = first_diff(b_m, t.odd(b_m, b_c), t.odd(b_c, b_p), b_p)
                b_s = sides_z[q, p - 1]
                dy_z = first_diff(
                    t.y_down(b_c, b_s, 2),
                    t.y_down(b_c, b_s, 1),
                    t.y_up(b_c, b_s, 1),
                    t.y_up(b_c, b_s, 2),
                )
                for s, inside, outside in ((2, dx, dx_z), (4, dy, dy_z)):
                    seconds[q, s] = first_diff(
                        t.z_down(inside, outside, 2),
                        t.z_down(inside, outside, 1),
                        t.z_up(inside, outside, 1),
                        t.z_up(inside, outside, 2),
                    )

        def value(q):
            return pairs[q, p + 1]

        def fluid_value(q):
            return fl[q, pl.ds(base, half), :]

        conformal, lapse = value(0), value(7)
        over_chi = 1.0 / conformal
        metric = symmetric([value(1 + s) for s in range(6)])
        shift = [value(8 + i) for i in range(3)]
        extrinsic, theta = value(11), value(21)
        traceless = symmetric([value(12 + s) for s in range(6)])
        connection = [value(18 + i) for i in range(3)]
        inverse = inverse_metric(metric)
        grad = [[grads[q, k] for k in range(3)] for q in range(fields)]
        chi_grad, lapse_grad = grad[0], grad[7]
        shift_grad = [[grad[8 + i][k] for i in range(3)] for k in range(3)]
        trace_k = extrinsic + 2.0 * theta

        stress = symmetric([tensors[p - 1, s] for s in range(6)])
        held = [fluid_value(q) for q in range(5)]
        shrink = volume_over(conformal)
        energy = held[4] + held[0]
        third_k = trace_k * (1.0 / 3.0)
        curved = [
            [
                (traceless[i][j] + metric[i][j] * third_k) if i <= j else None for j in range(3)
            ]
            for i in range(3)
        ]
        work = (
            stress[0][0] * curved[0][0]
            + stress[1][1] * curved[1][1]
            + stress[2][2] * curved[2][2]
            + 2.0
            * (
                stress[0][1] * curved[0][1]
                + stress[0][2] * curved[0][2]
                + stress[1][2] * curved[1][2]
            )
        )
        rates = [tensors[p - 1, 6 + q] for q in range(5)]
        for i in range(3):
            rates[1 + i] = (
                rates[1 + i]
                - energy * lapse_grad[i]
                + total([held[1 + k] * grad[8 + k][i] for k in range(3)])
            )
        rates[4] = (
            rates[4] + lapse * work * over_chi / shrink - dot(held[1:4], lapse_grad)
        )
        for q in range(5):
            hydro_rate[q, pl.ds(base, half), :] = rates[q]
        density = energy * shrink
        momentum = [held[1 + i] * shrink for i in range(3)]

        lowered = [[[None] * 3 for _ in range(3)] for _ in range(3)]
        for i in range(3):
            for j in range(3):
                for k in range(j, 3):
                    got = 0.5 * (
                        grad[1 + slot_of(i, k)][j]
                        + grad[1 + slot_of(i, j)][k]
                        - grad[1 + slot_of(j, k)][i]
                    )
                    lowered[i][j][k] = lowered[i][k][j] = got
        raised = [[[None] * 3 for _ in range(3)] for _ in range(3)]
        for i in range(3):
            for j in range(3):
                for k in range(j, 3):
                    got = total([inverse[i][l] * lowered[l][j][k] for l in range(3)])
                    raised[i][j][k] = raised[i][k][j] = got
        contracted = [trace_with(inverse, raised[i]) for i in range(3)]

        def hessian_trace(q):
            return (
                inverse[0][0] * seconds[q, 0]
                + inverse[1][1] * seconds[q, 3]
                + inverse[2][2] * seconds[q, 5]
                + 2.0 * (inverse[0][2] * seconds[q, 2] + inverse[1][2] * seconds[q, 4])
            )

        def second_cov(q, slope):
            bent = [total([raised[k][i][j] * slope[k] for k in range(3)]) for i, j in INDEX_PAIRS]
            return symmetric(
                [-bent[s] if s == 1 else seconds[q, s] - bent[s] for s in range(len(bent))]
            )

        chi_cov = second_cov(0, chi_grad)
        chi_lap = trace_with(inverse, chi_cov)
        raised_chi = [dot(inverse[i], chi_grad) for i in range(3)]
        chi_square = dot(raised_chi, chi_grad)
        cross_term = dot(raised_chi, lapse_grad)
        half_chi = 0.5 * over_chi
        plain_cov = second_cov(7, lapse_grad)
        lapse_cov = symmetric(
            [
                plain_cov[i][j]
                + (
                    chi_grad[i] * lapse_grad[j]
                    + chi_grad[j] * lapse_grad[i]
                    - metric[i][j] * cross_term
                )
                * half_chi
                for i, j in INDEX_PAIRS
            ]
        )
        lapse_lap = conformal * trace_with(inverse, lapse_cov)

        mixed = [
            [[dot(inverse[l], lowered[k][j]) for j in range(3)] for k in range(3)]
            for l in range(3)
        ]
        quarter_sq = half_chi * half_chi
        metric_factor = chi_lap * half_chi - 3.0 * chi_square * quarter_sq
        ricci = []
        for i, j in INDEX_PAIRS:
            second_part = -0.5 * hessian_trace(1 + slot_of(i, j))
            connection_part = 0.5 * total(
                [metric[k][i] * grad[18 + k][j] + metric[k][j] * grad[18 + k][i] for k in range(3)]
            )
            contracted_part = 0.5 * total(
                [contracted[k] * (lowered[i][j][k] + lowered[j][i][k]) for k in range(3)]
            )
            if i == j:
                quadratic = total(
                    [
                        raised[k][l][i] * (2.0 * mixed[l][i][k] + mixed[l][k][i])
                        for k in range(3)
                        for l in range(3)
                    ]
                )
            else:
                quadratic = total(
                    [
                        raised[k][l][i] * (mixed[l][j][k] + mixed[l][k][j])
                        + raised[k][l][j] * mixed[l][i][k]
                        for k in range(3)
                        for l in range(3)
                    ]
                )
            conformal_part = (
                chi_cov[i][j] * half_chi
                + metric[i][j] * metric_factor
                - chi_grad[i] * chi_grad[j] * quarter_sq
            )
            ricci.append(
                second_part + connection_part + contracted_part + quadratic + conformal_part
            )
        ricci = symmetric(ricci)
        ricci_scalar = conformal * trace_with(inverse, ricci)
        stress_trace = conformal * trace_with(inverse, stress)

        up_a = [
            [total([inverse[i][k] * traceless[k][j] for k in range(3)]) for j in range(3)]
            for i in range(3)
        ]
        raised_a = symmetric(
            [total([up_a[i][l] * inverse[j][l] for l in range(3)]) for i, j in INDEX_PAIRS]
        )
        a_square = trace_with(traceless, raised_a)
        shift_div = shift_grad[0][0] + shift_grad[1][1] + shift_grad[2][2]
        two_thirds_div = (2.0 / 3.0) * shift_div

        def finish(q, rate):
            rate = rate + dot(shift, grad[q]) + damped[q]
            st_rate[q, pl.ds(base, half), :] = rate

        finish(0, (2.0 / 3.0) * conformal * (lapse * trace_k - shift_div))
        finish(7, -2.0 * lapse * extrinsic)
        for i in range(3):
            finish(8 + i, 0.75 * connection[i] - SHIFT_DAMPING * shift[i])
        finish(
            11,
            lapse
            * (
                a_square
                + trace_k * trace_k * (1.0 / 3.0)
                + FOUR_PI * (stress_trace + density)
                + KAPPA_ONE * theta
            )
            - lapse_lap,
        )
        source = symmetric(
            [
                lapse * (ricci[i][j] - 2.0 * FOUR_PI * stress[i][j]) - lapse_cov[i][j]
                for i, j in INDEX_PAIRS
            ]
        )
        third_trace = trace_with(inverse, source) * (1.0 / 3.0)
        for s, (i, j) in enumerate(INDEX_PAIRS):
            finish(
                1 + s,
                total(
                    [
                        metric[i][k] * shift_grad[j][k] + metric[j][k] * shift_grad[i][k]
                        for k in range(3)
                    ]
                )
                - metric[i][j] * two_thirds_div
                - 2.0 * lapse * traceless[i][j],
            )
            product = total([traceless[i][k] * up_a[k][j] for k in range(3)])
            finish(
                12 + s,
                total(
                    [
                        traceless[i][k] * shift_grad[j][k] + traceless[j][k] * shift_grad[i][k]
                        for k in range(3)
                    ]
                )
                - traceless[i][j] * two_thirds_div
                + conformal * (source[i][j] - metric[i][j] * third_trace)
                + lapse * (trace_k * traceless[i][j] - 2.0 * product),
            )
        for i in range(3):
            bracket = (
                trace_with(raised_a, raised[i])
                - 1.5 * dot(raised_a[i], chi_grad) * over_chi
                - dot(inverse[i], [2.0 * grad[11][j] + grad[21][j] for j in range(3)]) * (1.0 / 3.0)
                - 2.0 * FOUR_PI * dot(inverse[i], momentum)
            )
            spread = [
                seconds[8, 0] + seconds[10, 2],
                seconds[9, 3] + seconds[10, 4],
                seconds[8, 2] + seconds[9, 4] + seconds[10, 5],
            ]
            finish(
                18 + i,
                contracted[i] * two_thirds_div
                - total([contracted[j] * shift_grad[j][i] for j in range(3)])
                + hessian_trace(8 + i)
                + dot(inverse[i], spread) * (1.0 / 3.0)
                - 2.0 * dot(raised_a[i], lapse_grad)
                + 2.0
                * lapse
                * (bracket - KAPPA_ONE * (connection[i] - contracted[i])),
            )
        finish(
            21,
            0.5
            * lapse
            * (
                ricci_scalar
                - a_square
                + (2.0 / 3.0) * trace_k * trace_k
                - 4.0 * FOUR_PI * density
            )
            - 2.0 * KAPPA_ONE * lapse * theta,
        )

    for index in range(own):
        pair_step(index)


def late_kernel(
    cells, zst, zfl, x_below, y_first, x_above, y_second, below_lanes, c_first, c_second, line_two, line_top,
    st_rate, hydro_rate, slopes, electric, st_out, fl_out,
):
    halo = Halo(
        cells, zst, zfl, x_below, y_first, x_above, y_second, below_lanes, c_first, c_second
    )
    x_below, x_above = halo.x_below, halo.x_above
    t, fields, half, own = halo.t, halo.fields, halo.half, halo.own
    inner, span = halo.inner, halo.span

    top = jnp.maximum(line_top[...], line_two[...])
    for lines in (c_first, c_second):
        top = jnp.maximum(top, lines[CORNER_TILES - 1, TOP_ROW : TOP_ROW + 1, :])
    dt = COURANT / top

    for p in inner:
        place = slice((p - 1) * half, p * half)
        mixed = []
        for q in range(CURVED):
            s_m, s_c, s_p = (
                halo.beside(q, n) if 1 <= n <= own else halo.corner(q, n) for n in (p - 1, p, p + 1)
            )
            slope = slopes[q, p - 1]
            slope_side = first_diff(s_m, t.odd_swapped(s_m, s_c), t.odd_swapped(s_c, s_p), s_p)
            mixed.append(
                first_diff(
                    t.y_down(slope, slope_side, 2),
                    t.y_down(slope, slope_side, 1),
                    t.y_up(slope, slope_side, 1),
                    t.y_up(slope, slope_side, 2),
                )
            )
        conformal, lapse = halo.main(0, p), halo.main(7, p)
        metric = [halo.main(1 + s, p) for s in range(6)]
        inverse = inverse_metric(symmetric(metric))
        half_chi = 0.5 / conformal
        cross = inverse[0][1]
        chi_trace = 2.0 * cross * mixed[0] * half_chi
        ricci = [metric[s] * chi_trace - cross * mixed[1 + s] for s in range(6)]
        ricci[1] = ricci[1] + mixed[0] * half_chi
        source = [lapse * r for r in ricci]
        source[1] = source[1] - mixed[7]
        third_trace = trace_with(inverse, symmetric(source)) * (1.0 / 3.0)
        extra = {
            11: -2.0 * conformal * cross * mixed[7],
            21: 0.5 * lapse * conformal * trace_with(inverse, symmetric(ricci)),
        }
        for s in range(6):
            extra[12 + s] = conformal * (source[s] - metric[s] * third_trace)
        for i in range(3):
            extra[18 + i] = 2.0 * cross * mixed[8 + i] + (1.0 / 3.0) * (
                inverse[i][0] * mixed[9] + inverse[i][1] * mixed[8]
            )
        for q in range(fields):
            rate = st_rate[q, place, :]
            if q in extra:
                rate = rate + extra[q]
            st_out[q, place, :] = halo.main(q, p) + dt * rate

    end = own + 1
    ends = (0, end)
    bx_face, by_face, bz_face = ({p: halo.corner(fields + 5 + i, p) for p in ends} for i in range(3))
    layers = {p: halo.corner_layers(p) for p in ends}
    bx_face[end] = layers[end]
    by_face[0] = jnp.where(t.slot < 2, layers[0], by_face[0])
    centred = [{}, {}, {}]
    for p in ends:
        following = halo.beside(fields + 5, 1) if p == 0 else bx_face[p]
        edge_cells = x_below if p == 0 else x_above
        dx = 0.5 * (t.odd_swapped(bx_face[p], following) - bx_face[p])
        dy = 0.5 * (t.y_up(by_face[p], edge_cells[fields + 6], 1) - by_face[p])
        centred[0][p] = bx_face[p] + dx
        centred[1][p] = by_face[p] + dy
        centred[2][p] = bz_face[p] - (dx + dy)
    corners = [{p: halo.corner(q, p) for p in ends} for q in [0, 7] + list(range(fields, fields + 5))]
    found = primitives(
        half, [(0, p) for p in ends], [[c] for c in corners[2:]], [[c] for c in centred],
        [corners[0]], [corners[1]], 2,
    )
    ez_h = [found[0, 0][10]] + [electric[own + p] for p in inner] + [found[0, end][10]]
    ez_x_h = [None] + [ez_h[p] + t.odd_swapped(ez_h[p - 1], ez_h[p]) for p in span[1:]]
    ez_x = [None] + [electric[p - 1] for p in span[1:]]
    edge_z = [None] + [ez_x[p] + t.y_down(ez_x[p], ez_x_h[p], 1) for p in span[1:]]
    quarter = 0.25 * dt
    for p in inner:
        place = slice((p - 1) * half, p * half)
        edge_z_h = ez_x_h[p] + t.y_down(ez_x_h[p], ez_x[p], 1)
        for q in range(5):
            fl_out[q, place, :] = halo.main(fields + q, p) + dt * hydro_rate[q, place, :]
        x_rate = hydro_rate[5, place, :] - (t.y_up(edge_z[p], edge_z_h, 1) - edge_z[p])
        y_rate = hydro_rate[6, place, :] + (t.odd(edge_z[p], edge_z[p + 1]) - edge_z[p])
        z_rate = hydro_rate[7, place, :]
        for i, rate in enumerate((x_rate, y_rate, z_rate)):
            fl_out[5 + i, place, :] = halo.main(fields + 5 + i, p) + quarter * rate


def per_device(spacetime, fluid):
    fields, cx, cy, cz = spacetime.shape
    rows = cx * cy
    st = spacetime.reshape(fields, rows, cz)
    fl = fluid.reshape(FLUID, rows, cz)
    sizes = [lax.axis_size(a) for a in ("gx", "gy", "gz")]
    tile = (2 * cy, cz)
    f32 = jnp.float32

    def shape(*dims):
        return jax.ShapeDtypeStruct(dims, f32)

    def beyond(cells):
        n = sizes[2]
        after = lax.ppermute(cells, "gz", [((i + 1) % n, i) for i in range(n)])
        if n == 2:
            return after
        before = lax.ppermute(cells, "gz", [(i, (i + 1) % n) for i in range(n)])
        lane = lax.broadcasted_iota(jnp.int32, cells.shape, 2)
        return jnp.where(lane < cz // 2, after, before)

    params = pltpu.CompilerParams(vmem_limit_bytes=48 * 1024 * 1024)
    zst, zfl = beyond(st), beyond(fl)
    cells = jnp.concatenate([st, fl], axis=0)
    face = shape(face_tiles(fields), *tile)
    corner = shape(CORNER_TILES, *tile)
    lane_row = shape(1, cz)
    def call(kernel, outs, name, operands, scratch=()):
        return pl.pallas_call(
            kernel,
            out_shape=outs,
            scratch_shapes=scratch,
            compiler_params=params,
            name=name,
        )(*operands)

    def shift(cells, step):
        n = lax.axis_size("gx")
        return lax.ppermute(cells, "gx", [(i, (i + step) % n) for i in range(n)])

    def trade(cells, first):
        axis = "gy"
        n = lax.axis_size(axis)
        step = [1, -1] if first else [-1, 1]
        return lax.ppermute(cells, axis, [(i, (i + step[i % 2]) % n) for i in range(n)])

    def two_away(cells, axis):
        n = lax.axis_size(axis)
        return lax.ppermute(cells, axis, [(i, (i + 2) % n) for i in range(n)]) if n == 4 else cells

    short = sizes[0] <= 4 and sizes[1] <= 4 and sizes[2] <= 2
    x_high = call(pack_up_kernel, face, "pack_up", (cells,))
    x_below = shift(x_high, 1)
    x_low, high_lanes, y_first, y_second, top = call(
        pack_kernel, [face, shape(1, *tile), face, face, lane_row], "pack", (cells, zst, zfl)
    )
    below_lanes = shift(high_lanes, 1)
    y_first = trade(y_first, True)
    x_above = shift(x_low, -1)
    y_second = trade(y_second, False)
    top_two = two_away(top, "gx")
    c_first, c_second, line_top = call(
        relay_kernel,
        [corner, corner, lane_row],
        "relay",
        (x_below, below_lanes, x_above, y_first, top, top_two),
    )
    c_first = trade(c_first, True)
    c_second = trade(c_second, False)
    if short:
        line_two = two_away(line_top, "gy")
    else:
        line_two = lax.pmax(line_top, ("gx", "gy", "gz"))
    own = cx // 2
    arrived = (cells, zst, zfl, x_below, y_first, x_above, y_second, below_lanes)
    early = call(
        early_kernel,
        [
            shape(*st.shape),
            shape(FLUID, rows, cz),
            shape(CURVED, own, *tile),
            shape(2 * own + 1, *tile),
        ],
        "early",
        arrived,
        [
            pltpu.VMEM((fields, own + 4) + tile, f32),
            pltpu.VMEM((fields, own) + tile, f32),
            pltpu.VMEM((fields, own) + tile, f32),
            pltpu.VMEM((CURVED, own + 2) + tile, f32),
            pltpu.VMEM((CURVED, own) + tile, f32),
            pltpu.VMEM((fields, 3) + tile, f32),
            pltpu.VMEM((CURVED, 6) + tile, f32),
            pltpu.VMEM((fields,) + tile, f32),
            pltpu.VMEM((own, 11) + tile, f32),
        ],
    )
    st_next, fl_next = call(
        late_kernel,
        [shape(*st.shape), shape(*fl.shape)],
        "late",
        (*arrived, c_first, c_second, line_two, line_top, *early),
    )
    return st_next.reshape(spacetime.shape), fl_next.reshape(fluid.shape)


def solution(mesh):
    spec = P(None, "gx", "gy", "gz")
    return jax.shard_map(
        per_device, mesh=mesh, in_specs=(spec, spec), out_specs=(spec, spec), check_vma=False
    )
```

```python
import functools
import math

import jax
import jax.numpy as jnp
from jax import lax
from jax.experimental import pallas as pl
from jax.experimental.pallas import tpu as pltpu
from jax.sharding import PartitionSpec as P

RECOVERY_STEPS = 4
INDEX_PAIRS = ((0, 0), (0, 1), (0, 2), (1, 1), (1, 2), (2, 2))
COURANT = 0.25
DISSIPATION = 0.2
KAPPA_ONE = 0.02
SHIFT_DAMPING = 1.0
SPEED_CAP = 0.99
PRESSURE_FLOOR = 0.01
FOUR_PI = 4.0 * math.pi

BATCH = 6
CURVED = 11
FLUID = 8


def total(pieces):
    summed = pieces[0]
    for member in pieces[1:]:
        summed = summed + member
    return summed


def dot(first_vec, second_vec):
    return total([first_vec[i] * second_vec[i] for i in range(3)])


def slot_of(i, j):
    return INDEX_PAIRS.index((min(i, j), max(i, j)))


def symmetric(entries):
    return [[entries[slot_of(i, j)] for j in range(3)] for i in range(3)]


def trace_with(inverse, tensor):
    return (
        inverse[0][0] * tensor[0][0]
        + inverse[1][1] * tensor[1][1]
        + inverse[2][2] * tensor[2][2]
        + 2.0
        * (
            inverse[0][1] * tensor[0][1]
            + inverse[0][2] * tensor[0][2]
            + inverse[1][2] * tensor[1][2]
        )
    )


def inverse_metric(metric):
    cofactor = [
        metric[1][1] * metric[2][2] - metric[1][2] * metric[1][2],
        metric[0][2] * metric[1][2] - metric[0][1] * metric[2][2],
        metric[0][1] * metric[1][2] - metric[0][2] * metric[1][1],
        metric[0][0] * metric[2][2] - metric[0][2] * metric[0][2],
        metric[0][1] * metric[0][2] - metric[0][0] * metric[1][2],
        metric[0][0] * metric[1][1] - metric[0][1] * metric[0][1],
    ]
    determinant = (
        metric[0][0] * cofactor[0] + metric[0][1] * cofactor[1] + metric[0][2] * cofactor[2]
    )
    over = 1.0 / determinant
    return symmetric([c * over for c in cofactor])


class Tile:
    def __init__(self, cy, cz):
        self.cy, self.rows, self.lanes = cy, 2 * cy, cz
        shape = (self.rows, cz)
        self.row = lax.broadcasted_iota(jnp.int32, shape, 0)
        self.lane = lax.broadcasted_iota(jnp.int32, shape, 1)
        self.slot = lax.rem(self.row, cy)

    def turn(self, tile, amount):
        amount = amount % self.rows
        return tile if amount == 0 else pltpu.roll(tile, amount, 0)

    def spin(self, tile, amount):
        amount = amount % self.lanes
        return tile if amount == 0 else pltpu.roll(tile, amount, 1)

    def swap(self, tile):
        return self.turn(tile, self.cy)

    def odd(self, a, b):
        return self.turn(jnp.where(self.row < self.cy, b, a), self.cy)

    def odd_swapped(self, a, b):
        return self.turn(jnp.where(self.row < self.cy, a, b), self.cy)

    def y_up(self, main, beyond, k):
        return self.turn(jnp.where(self.slot < k, beyond, main), -k)

    def y_down(self, main, beyond, k):
        return self.turn(jnp.where(self.slot >= self.cy - k, beyond, main), k)

    def z_up(self, main, beyond, k):
        return self.spin(jnp.where(self.lane < k, beyond, main), -k)

    def z_down(self, main, beyond, k):
        return self.spin(jnp.where(self.lane >= self.lanes - k, beyond, main), k)

    def corner_rows(self, side, turn):
        places = ((0, 2), (self.cy - 1, self.cy + 1))[side]
        first, second = [(place + turn) % self.rows for place in places]
        return (self.row == first) | (self.row == second)

    def join_low(self, u, v):
        return jnp.where(self.slot < 2, self.swap(u), self.turn(v, 2))

    def join_high(self, u, v):
        return jnp.where(self.slot >= self.cy - 2, self.swap(u), self.turn(self.swap(v), -2))

    def part_first(self, from_above, from_below):
        return jnp.where(self.slot < 2, from_above, from_below)

    def part_second(self, from_above, from_below):
        return self.turn(jnp.where(self.slot < 2, from_below, from_above), 2)


def edge_list(tiles):
    fields = next(n for n in range(tiles) if face_tiles(n) == tiles)
    return list(range(CURVED)) + list(range(fields, fields + FLUID))


CORNER_TURNS = (0, 1, 4, 5)
TOP_TILES = 2
CORNER_TILES = CURVED + FLUID // 4 + 1
TOP_ROW = 6


def face_tiles(fields):
    return fields + FLUID + len(pairs_of(third_list(fields))) + 1


def third_list(fields):
    return list(range(fields + 1))


def pairs_of(items):
    return [(items[i], items[min(i + 1, len(items) - 1)]) for i in range(0, len(items), 2)]


def top_speed(st):
    inverse = inverse_metric(symmetric([st[1 + s] for s in range(6)]))
    scale = 2.0 * st[7] * st[0]
    speeds = [jnp.abs(st[8 + d]) + jnp.sqrt(scale * inverse[d][d]) for d in range(3)]
    top = jnp.maximum(jnp.maximum(speeds[0], speeds[1]), speeds[2])
    return jnp.max(jnp.max(top, axis=1, keepdims=True), axis=0, keepdims=True)


class Chosen:
    def __init__(self, first, second, swapped):
        self.first, self.second, self.swapped, self.shape = first, second, swapped, first.shape

    def __getitem__(self, key):
        return jnp.where(self.swapped, self.second[key], self.first[key])


class Sent:
    def __init__(self, first, second, swapped):
        self.first, self.second, self.swapped, self.shape = first, second, swapped, first.shape

    def put(self, key, lower, upper):
        self.first[key] = jnp.where(self.swapped, upper, lower)
        self.second[key] = jnp.where(self.swapped, lower, upper)


class Joined:
    def __init__(self, tiles, tail):
        self.tiles, self.tail = tiles, tail
        self.shape = tuple(tiles.shape)

    def __getitem__(self, key):
        q, rows = (key[0], key[1:]) if isinstance(key, tuple) else (key, ())
        if q == self.tiles.shape[0] - 1:
            return self.tail[(0,) + rows]
        return self.tiles[(q,) + rows]


def even_along_y(tile):
    return jnp.full(tile, lax.rem(lax.axis_index("gy"), 2), jnp.int32) == 0


def pack_up_kernel(cells, x_high):
    count, rows, lanes = cells.shape
    fields, half = count - FLUID, rows // 2
    t = Tile(rows // 4, lanes)
    for q in range(count):
        x_high[q] = cells[q, half:rows, :]
    for n, (a, b) in enumerate(pairs_of(list(range(fields)) + [fields + 5])):
        x_high[count + n] = jnp.where(
            t.row < t.cy, t.swap(cells[b, 0:half, :]), cells[a, 0:half, :]
        )
    x_high[x_high.shape[0] - 1] = jnp.broadcast_to(top_speed(cells), t.row.shape)


def lanes_kernel(x_below, out):
    t = Tile(x_below.shape[1] // 2, x_below.shape[2])
    last = x_below.shape[0] - 1
    packed = x_below[last]
    for place, q in enumerate(edge_list(x_below.shape[0])):
        piece = t.spin(x_below[q], 4 * place + 2)
        here = (t.lane >= 4 * place) & (t.lane < 4 * place + 4)
        packed = jnp.where(here, piece, packed)
    out[0] = packed


def pack_kernel(cells, zst, zfl, *outs):
    fields, rows, lanes = zst.shape
    st, fl = cells.at[0:fields], cells.at[fields : fields + FLUID]
    cy = rows // 4
    t = Tile(cy, lanes)
    x_low, y_first, y_second, top_out = outs
    half = t.rows
    to_y = Sent(y_first, y_second, even_along_y((half, lanes)))

    def own(ref, q):
        return [ref[q, 0:half, :], ref[q, half : 2 * half, :]]

    tiles, beyond = [], []
    for q in range(fields):
        tiles.append(own(st, q))
        beyond.append(own(zst, q) if q < CURVED else None)
    for q in range(FLUID):
        tiles.append(own(fl, q))
        beyond.append(own(zfl, q))

    packed = [None] * 4
    place_count = 0
    for q, (first, second) in enumerate(tiles):
        x_low[q] = first
        to_y.put(q, t.join_low(first, second), t.join_high(first, second))
        if beyond[q] is not None:
            zf, zs = beyond[q]
            for m, piece in enumerate((zf, zs, t.join_low(zf, zs), t.join_high(zf, zs))):
                piece = t.spin(piece, 4 * place_count + 2)
                packed[m] = (
                    piece if place_count == 0 else jnp.where(t.lane < 4 * place_count, packed[m], piece)
                )
            place_count += 1
    for n, (a, b) in enumerate(pairs_of(third_list(fields))):
        slot = fields + FLUID + n
        xa, xb = (tiles[q if q < fields else fields + 5] for q in (a, b))
        x_low[slot] = jnp.where(t.row < cy, xa[1], t.swap(xb[1]))
        ya, yb = (tiles[q if q < fields else fields + 6] for q in (a, b))
        w = [t.swap(ya[0]), t.swap(ya[1]), t.swap(yb[0]), t.swap(yb[1])]
        s = t.slot
        low = jnp.where(s == 0, t.turn(w[2], -2), t.turn(w[3], -1))
        low = jnp.where(s == 2, w[0], jnp.where(s == 3, t.turn(w[1], 1), low))
        high = jnp.where(s == 3, t.turn(w[2], 2), t.turn(w[3], 1))
        high = jnp.where(s == 1, w[0], jnp.where(s == 0, t.turn(w[1], -1), high))
        to_y.put(slot, low, high)
    top = jnp.maximum(top_speed(st), top_speed(zst))
    top_out[...] = jnp.broadcast_to(top, top_out.shape)
    last = x_low.shape[0] - 1
    x_lanes = [jnp.where(t.lane < 4 * place_count, piece, top) for piece in packed[:2]]
    y_lanes = [jnp.where(t.lane < 4 * place_count, piece, top) for piece in packed[2:]]
    x_low[last] = x_lanes[0]
    to_y.put(last, *y_lanes)


def relay_kernel(x_below, below_lanes, x_above, y_first, top, top_two, c_first, c_second, line_top):
    cy, lanes = x_below.shape[1] // 2, x_below.shape[2]
    t = Tile(cy, lanes)
    to_y = Sent(c_first, c_second, even_along_y((t.rows, lanes)))
    last = x_below.shape[0] - 1
    line = jnp.maximum(top[0, 0:1, :], top_two[0, 0:1, :])
    line = jnp.maximum(line, x_below[last, 0:1, lanes - 1 : lanes])
    x_below = Joined(x_below, below_lanes)
    for beside in (x_below, x_above, y_first):
        line = jnp.maximum(line, beside[last, 0:1, lanes - 1 : lanes])
    line_top[...] = line
    edge = edge_list(x_below.shape[0])
    for q in range(CURVED):
        below, above = x_below[q], x_above[q]
        to_y.put(q, t.join_low(below, above), t.join_high(below, above))
    for n in range(0, FLUID, 4):
        low, high = None, None
        for turn, q in zip(CORNER_TURNS, edge[CURVED + n : CURVED + n + 4]):
            below, above = x_below[q], x_above[q]
            below, above = (t.turn(j(below, above), turn) for j in (t.join_low, t.join_high))
            if low is None:
                low, high = below, above
            else:
                low = jnp.where(t.corner_rows(0, turn), below, low)
                high = jnp.where(t.corner_rows(1, turn), above, high)
        to_y.put(CURVED + n // 4, low, high)
    along_x, along_y = edge[CURVED + 5], edge[CURVED + 6]
    low = t.join_low(x_below[along_y], x_above[along_y])
    high = t.join_high(x_below[along_x], x_above[along_x])
    low, high = (jnp.where(t.row == TOP_ROW, line, tile) for tile in (low, high))
    to_y.put(CORNER_TILES - 1, low, high)


def limited(a, b):
    return jnp.maximum(jnp.minimum(a, b), 0.0) + jnp.minimum(jnp.maximum(a, b), 0.0)


def recover(conserved, magnetic):
    density = conserved[0]
    momenta = conserved[1:4]
    energy = conserved[4] + density
    mom_sq = dot(momenta, momenta)
    mag_sq = dot(magnetic, magnetic)
    cross = dot(momenta, magnetic)
    cross_sq = cross * cross

    def state(z):
        grown = z + mag_sq
        over = 1.0 / (z * grown)
        speed_sq = (mom_sq * z * z + cross_sq * (2.0 * z + mag_sq)) * over * over
        kept = 1.0 - jnp.minimum(speed_sq, SPEED_CAP)
        rest = density * jnp.sqrt(kept)
        return kept, rest, 0.5 * (z * kept - rest), grown * over

    z = jnp.maximum(energy - 0.5 * mag_sq, density)
    for _ in range(RECOVERY_STEPS):
        kept, rest, pressure, over_z = state(z)
        residual = (
            z
            + mag_sq
            - pressure
            - 0.5 * mag_sq * kept
            - 0.5 * cross_sq * over_z * over_z
            - energy
        )
        z = jnp.maximum(z - residual / (1.0 - 0.5 * kept), density)
    kept, rest, pressure, over_z = state(z)
    pressure = jnp.maximum(pressure, PRESSURE_FLOOR * rest)
    scale = lax.rsqrt(kept) / (z + mag_sq)
    along = cross * over_z
    four_vel = [scale * (momenta[i] + along * magnetic[i]) for i in range(3)]
    return [rest, pressure] + four_vel


def stress_parts(rest, pressure, u, magnetic):
    lorentz_sq = 1.0 + dot(u, u)
    over = lax.rsqrt(lorentz_sq)
    over_sq = over * over
    time_b = dot(u, magnetic)
    grown_b = [magnetic[i] + time_b * u[i] for i in range(3)]
    b_square = (dot(magnetic, magnetic) + time_b * time_b) * over_sq
    enthalpy = rest + 2.0 * pressure
    inertia = enthalpy + b_square
    return lorentz_sq, over, over_sq, time_b, grown_b, b_square, enthalpy, inertia


def face_state(rest, pressure, u, magnetic, d):
    lorentz_sq, over, over_sq, time_b, grown_b, b_square, enthalpy, inertia = stress_parts(
        rest, pressure, u, magnetic
    )
    total_pressure = pressure + 0.5 * b_square
    lorentz = lorentz_sq * over
    density = rest * lorentz
    carried = inertia * lorentz
    time_over = time_b * over
    conserved = [density]
    conserved += [carried * u[j] - time_over * grown_b[j] for j in range(3)]
    conserved += [inertia * lorentz_sq - total_pressure - time_b * time_b - density]
    mass_flux = rest * u[d]
    flux = [mass_flux]
    pushed = inertia * u[d]
    b_over = grown_b[d] * over_sq
    for j in range(3):
        flux_j = pushed * u[j] - b_over * grown_b[j]
        flux.append(flux_j + total_pressure if j == d else flux_j)
    flux.append(carried * u[d] - time_over * grown_b[d] - mass_flux)
    ratio = 1.0 / (enthalpy * inertia)
    sound_sq = 2.0 * pressure * inertia * ratio
    alfven_sq = b_square * enthalpy * ratio
    fast_sq = sound_sq + alfven_sq - sound_sq * alfven_sq
    slow = 1.0 - fast_sq
    velocity = u[d] * over
    rest_part = 1.0 - dot(u, u) * over_sq * fast_sq
    spread = jnp.sqrt(fast_sq * over_sq * (rest_part - velocity * velocity * slow))
    fastest = (jnp.abs(velocity * slow) + spread) / rest_part
    return conserved, flux, fastest


def face_flux(left, right, normal, weight, d):
    sides = []
    for state in (left, right):
        magnetic = [normal if i == d else state[5 + i] for i in range(3)]
        sides.append(face_state(state[0], state[1], state[2:5], magnetic, d))
    (cons_l, flux_l, fast_l), (cons_r, flux_r, fast_r) = sides
    signal = jnp.maximum(fast_l, fast_r)
    scale = 0.5 * weight
    return [scale * (flux_l[q] + flux_r[q] - signal * (cons_r[q] - cons_l[q])) for q in range(5)]


def volume_over(conformal):
    return conformal * jnp.sqrt(conformal)


def first_diff(down_two, down, up, up_two):
    return (8.0 / 12.0) * (up - down) + (1.0 / 12.0) * (down_two - up_two)


class Halo:
    def __init__(self, cells, zst, zfl, x_below, y_first, x_above, y_second, below_lanes, *corners):
        x_below = Joined(x_below, below_lanes)
        self.fields, self.block, self.lanes = zst.shape
        even_y = even_along_y((self.block // 2, self.lanes))
        y_below, y_above = Chosen(y_first, y_second, even_y), Chosen(y_second, y_first, even_y)
        if corners:
            c_first, c_second = corners
            self.c_below = Chosen(c_first, c_second, even_y)
            self.c_above = Chosen(c_second, c_first, even_y)
        self.st = cells.at[0 : self.fields]
        self.fl = cells.at[self.fields : self.fields + FLUID]
        self.zst, self.zfl = zst, zfl
        self.x_below, self.x_above = x_below, x_above
        self.y_below, self.y_above = y_below, y_above
        self.cy = self.block // 4
        self.t = Tile(self.cy, self.lanes)
        self.half = self.t.rows
        self.own = self.block // self.half
        self.inner = range(1, self.own + 1)
        self.span = range(self.own + 2)
        self.edge = edge_list(x_below.shape[0])
        self.last = x_below.shape[0] - 1

    def rows_of(self, ref, q, p):
        return ref[q, (p - 1) * self.half : p * self.half, :]

    def main(self, q, p):
        if q < self.fields:
            return self.rows_of(self.st, q, p)
        return self.rows_of(self.fl, q - self.fields, p)

    def beyond(self, q, p):
        if q < self.fields:
            return self.rows_of(self.zst, q, p)
        return self.rows_of(self.zfl, q - self.fields, p)

    def part(self, second):
        return self.t.part_second if second else self.t.part_first

    def beside(self, q, p):
        return self.part(p == 2)(self.y_above[q], self.y_below[q])

    def third_place(self, q):
        return self.fields + FLUID + q // 2, q % 2

    def x_third(self, q, upper):
        tile, which = self.third_place(q)
        found = self.x_above[tile] if upper else self.x_below[tile]
        return self.t.swap(found) if which else found

    def y_third(self, q, p):
        t = self.t
        tile, which = self.third_place(q)
        turn_above, turn_below = ((0, 0), (-1, 1), (2, -2), (1, -1))[2 * which + p - 1]
        above, below = t.turn(self.y_above[tile], turn_above), t.turn(self.y_below[tile], turn_below)
        return jnp.where(t.slot == 2, above, below)

    def z_place(self, q):
        return 4 * self.edge.index(q) + 2

    def x_beyond(self, q, upper):
        tile = self.x_above[self.last] if upper else self.x_below[self.last]
        return self.t.spin(tile, -self.z_place(q))

    def y_beyond(self, q, p):
        return self.t.spin(self.beside(self.last, p), -self.z_place(q))

    def corner(self, q, p):
        place, turn = q, 0
        if q >= CURVED:
            n = q - self.fields
            place, turn = CURVED + n // 4, CORNER_TURNS[n % 4]
        above, below = self.t.turn(self.c_above[place], -turn), self.t.turn(self.c_below[place], -turn)
        return self.part(p > 0)(above, below)

    def corner_layers(self, p):
        place = CORNER_TILES - 1
        return self.part(p > 0)(self.c_above[place], self.c_below[place])

    def plane(self, q):
        inner = self.inner
        return (
            [self.x_below[q]] + [self.main(q, p) for p in inner] + [self.x_above[q]],
            [None] + [self.beside(q, p) for p in inner] + [None],
            [self.x_beyond(q, False)]
            + [self.beyond(q, p) for p in inner]
            + [self.x_beyond(q, True)],
            [None] + [self.y_beyond(q, p) for p in inner] + [None],
        )


def weigh(chi_face, alpha_face):
    shrink = volume_over(chi_face)
    return shrink, alpha_face / shrink


def primitives(half, spots, cons, centred, chi, alpha, batch):
    found = {}
    for start in range(0, len(spots), batch):
        group = spots[start : start + batch]

        def gather(planes):
            return jnp.concatenate([planes[k][p] for k, p in group], axis=0)

        shrink = volume_over(gather(chi))
        mag_raw = [gather(centred[i]) for i in range(3)]
        mag = [m * shrink for m in mag_raw]
        values = recover([gather(c) * shrink for c in cons], mag)
        u = values[2:5]
        factor = gather(alpha) * lax.rsqrt(1.0 + dot(u, u))
        field = [
            factor * (u[(i + 2) % 3] * mag_raw[(i + 1) % 3] - u[(i + 1) % 3] * mag_raw[(i + 2) % 3])
            for i in range(3)
        ]
        for n, spot in enumerate(group):
            found[spot] = [value[n * half : (n + 1) * half] for value in values + mag + field]
    return found


def ring_fluxes(prims, chi, alpha, normals, d, up, down):
    found = []
    for here, there in ((0, 1), (1, 0)):
        left, right = [], []
        for a, b in zip(prims[here], prims[there]):
            below = down(a, b, 1)
            middle = a - below
            left.append(below + 0.5 * limited(below - down(a, b, 2), middle))
            right.append(a - 0.5 * limited(middle, up(a, b, 1) - a))
        shrink, weight = weigh(
            0.5 * (chi[here] + down(chi[here], chi[there], 1)),
            0.5 * (alpha[here] + down(alpha[here], alpha[there], 1)),
        )
        found.append(face_flux(left, right, normals[here] * shrink, weight, d))
    return [a - up(a, b, 1) for a, b in zip(*found)]


def early_kernel(
    cells, zst, zfl, x_below, y_first, x_above, y_second, below_lanes,
    st_rate, hydro_rate, slopes, electric, pairs, sides, thirds, pairs_z, sides_z, grads, seconds, damped, tensors,
):
    halo = Halo(cells, zst, zfl, x_below, y_first, x_above, y_second, below_lanes)
    t, fields, half, own, cy = halo.t, halo.fields, halo.half, halo.own, halo.cy
    st, fl, inner = halo.st, halo.fl, halo.inner

    for q in range(fields):
        pairs[q, 0] = halo.x_third(q, False)
        pairs[q, 1] = x_below[q]
        for p in inner:
            pairs[q, 1 + p] = halo.main(q, p)
            sides[q, p - 1] = halo.beside(q, p)
            thirds[q, p - 1] = halo.y_third(q, p)
        pairs[q, 2 + own] = x_above[q]
        pairs[q, 3 + own] = halo.x_third(q, True)
        if q < CURVED:
            pairs_z[q, 0] = halo.x_beyond(q, False)
            pairs_z[q, own + 1] = halo.x_beyond(q, True)
            for p in inner:
                pairs_z[q, p] = halo.beyond(q, p)
                sides_z[q, p - 1] = halo.y_beyond(q, p)

    span = halo.span
    face = [halo.plane(fields + 5 + i) for i in range(3)]

    def halves(kind, p):
        own_x, own_y, own_z = (f[kind][p] for f in face)
        pair = kind in (0, 2)
        known_x = pair or p < own
        last = kind == 0 and p == own + 1
        if pair:
            next_x = halo.x_third(fields, True) if last else face[0][kind][min(p + 1, own + 1)]
            next_x = t.odd(own_x, next_x)
        else:
            next_x = t.odd_swapped(own_x, face[0][kind][p + 1] if known_x else own_x)
        dx = 0.5 * (next_x - own_x)
        dz = 0.5 * (t.z_up(own_z, face[2][kind ^ 2][p], 1) - own_z)
        inside = 1 <= p <= own
        if not pair:
            here = jnp.where(t.slot == 2, halo.y_third(fields, p), own_y) if kind == 1 else own_y
            next_y = t.y_up(here, face[1][kind ^ 1][p], 1)
        else:
            next_y = t.y_up(own_y, face[1][kind ^ 1][p] if inside else own_y, 1)
        dy = 0.5 * (next_y - own_y)
        if pair and not inside:
            dy = jnp.where(t.slot == cy - 1, -(dx + dz), dy)
        if not pair and not known_x:
            dx = jnp.where(t.row < cy, -(dy + dz), dx)
        return own_x + dx, own_y + dy, own_z + dz

    spots = [(0, p) for p in span] + [(1, p) for p in inner]
    spots += [(2, p) for p in span] + [(3, p) for p in inner]
    centred = [[[None] * (own + 2) for _ in range(4)] for _ in range(3)]
    for k, p in spots:
        for i, value in enumerate(halves(k, p)):
            centred[i][k][p] = value
    chi, alpha = halo.plane(0), halo.plane(7)
    found = primitives(
        half, spots, [halo.plane(fields + q) for q in range(5)], centred, chi, alpha, BATCH
    )

    lines = [[found[0, p][i] for p in span] for i in range(8)] + [chi[0], alpha[0]]
    odd_lines = [[t.odd(f[p], f[min(p + 1, own + 1)]) for p in span] for f in lines]
    fluxes = [None]
    for p in range(1, own + 2):
        left, right = [], []
        for f, o in zip(lines[:8], odd_lines):
            here = f[p] - o[p - 1]
            left.append(o[p - 1] + 0.5 * limited(o[p - 1] - f[p - 1], here))
            right.append(f[p] - 0.5 * limited(here, o[p] - f[p]))
        shrink, weight = weigh(
            0.5 * (lines[8][p] + odd_lines[8][p - 1]), 0.5 * (lines[9][p] + odd_lines[9][p - 1])
        )
        fluxes.append(face_flux(left, right, face[0][0][p] * shrink, weight, 0))
    for p in inner:
        changes = [
            ring_fluxes(
                [found[k, p][:8] for k in (0, kind)],
                [chi[k][p] for k in (0, kind)],
                [alpha[k][p] for k in (0, kind)],
                [face[d][k][p] for k in (0, kind)],
                d,
                up,
                down,
            )
            for d, kind, up, down in ((1, 1, t.y_up, t.y_down), (2, 2, t.z_up, t.z_down))
        ]
        for q in range(5):
            change = fluxes[p][q] - t.odd(fluxes[p][q], fluxes[p + 1][q])
            tensors[p - 1, 6 + q] = change + changes[0][q] + changes[1][q]
        rest, pressure = found[0, p][:2]
        u = found[0, p][2:5]
        parts = stress_parts(rest, pressure, u, found[0, p][5:8])
        lorentz_sq, over, over_sq, time_b, grown_b, b_square, enthalpy, inertia = parts
        total_pressure = pressure + 0.5 * b_square
        for s, (i, j) in enumerate(INDEX_PAIRS):
            value = inertia * u[i] * u[j] - over_sq * (grown_b[i] * grown_b[j])
            tensors[p - 1, s] = value + total_pressure if i == j else value

    ex, ey, ez = (
        [[found[k, p][8 + i] if (k, p) in found else None for p in span] for k in range(4)]
        for i in range(3)
    )
    ey_x = [
        [ey[k][p] + t.odd(ey[k][p - 1], ey[k][p]) if p else None for p in span] for k in (0, 2)
    ]
    edge_y = [None] + [ey_x[0][p] + t.z_down(ey_x[0][p], ey_x[1][p], 1) for p in span[1:]]
    for p in span[1:]:
        electric[p - 1] = ez[0][p] + t.odd(ez[0][p - 1], ez[0][p])
    for p in inner:
        electric[own + p] = ez[1][p]
        edge_y_z = ey_x[1][p] + t.z_down(ey_x[1][p], ey_x[0][p], 1)
        ex_y = ex[0][p] + t.y_down(ex[0][p], ex[1][p], 1)
        ex_y_h = ex[1][p] + t.y_down(ex[1][p], ex[0][p], 1)
        ex_y_z = ex[2][p] + t.y_down(ex[2][p], ex[3][p], 1)
        ex_y_hz = ex[3][p] + t.y_down(ex[3][p], ex[2][p], 1)
        edge_x = ex_y + t.z_down(ex_y, ex_y_z, 1)
        edge_x_h = ex_y_h + t.z_down(ex_y_h, ex_y_hz, 1)
        edge_x_z = ex_y_z + t.z_down(ex_y_z, ex_y, 1)
        place = slice((p - 1) * half, p * half)
        hydro_rate[5, place, :] = t.z_up(edge_y[p], edge_y_z, 1) - edge_y[p]
        hydro_rate[6, place, :] = edge_x - t.z_up(edge_x, edge_x_z, 1)
        hydro_rate[7, place, :] = (t.y_up(edge_x, edge_x_h, 1) - edge_x) - (
            t.odd(edge_y[p], edge_y[p + 1]) - edge_y[p]
        )

    def pair_step(index):
        p = index + 1
        base = index * half

        for q in range(fields):
            centre = pairs[q, p + 1]
            x_m3 = t.odd(pairs[q, p - 1], pairs[q, p])
            x_m2 = pairs[q, p]
            x_m1 = t.odd(pairs[q, p], centre)
            x_p1 = t.odd(centre, pairs[q, p + 2])
            x_p2 = pairs[q, p + 2]
            x_p3 = t.odd(pairs[q, p + 2], pairs[q, p + 3])
            side, third = sides[q, index], thirds[q, index]
            y_m1, y_m2 = t.y_down(centre, side, 1), t.y_down(centre, side, 2)
            y_p1, y_p2 = t.y_up(centre, side, 1), t.y_up(centre, side, 2)
            y_m3 = t.turn(
                jnp.where(t.slot >= cy - 2, side, jnp.where(t.slot == cy - 3, third, centre)), 3
            )
            y_p3 = t.turn(jnp.where(t.slot < 2, side, jnp.where(t.slot == 2, third, centre)), -3)
            beyond = zst[q, pl.ds(base, half), :]
            z_m1, z_m2, z_m3 = (t.z_down(centre, beyond, k) for k in (1, 2, 3))
            z_p1, z_p2, z_p3 = (t.z_up(centre, beyond, k) for k in (1, 2, 3))
            dx = first_diff(x_m2, x_m1, x_p1, x_p2)
            dy = first_diff(y_m2, y_m1, y_p1, y_p2)
            grads[q, 0] = dx
            if q < CURVED:
                slopes[q, index] = dx
            grads[q, 1] = dy
            grads[q, 2] = first_diff(z_m2, z_m1, z_p1, z_p2)
            near = [x_m1 + x_p1, y_m1 + y_p1, z_m1 + z_p1]
            far = [x_m2 + x_p2, y_m2 + y_p2, z_m2 + z_p2]
            outer = (x_m3 + x_p3) + (y_m3 + y_p3) + (z_m3 + z_p3)
            damped[q] = (DISSIPATION / 64.0) * (
                outer - 6.0 * (far[0] + far[1] + far[2]) + 15.0 * (near[0] + near[1] + near[2])
                - 60.0 * centre
            )
            if q < CURVED:
                for s, d in ((0, 0), (3, 1), (5, 2)):
                    seconds[q, s] = (1.0 / 12.0) * (16.0 * near[d] - far[d] - 30.0 * centre)
                b_m, b_c, b_p = pairs_z[q, p - 1], pairs_z[q, p], pairs_z[q, p + 1]
                dx_z = first_diff(b_m, t.odd(b_m, b_c), t.odd(b_c, b_p), b_p)
                b_s = sides_z[q, p - 1]
                dy_z = first_diff(
                    t.y_down(b_c, b_s, 2),
                    t.y_down(b_c, b_s, 1),
                    t.y_up(b_c, b_s, 1),
                    t.y_up(b_c, b_s, 2),
                )
                for s, inside, outside in ((2, dx, dx_z), (4, dy, dy_z)):
                    seconds[q, s] = first_diff(
                        t.z_down(inside, outside, 2),
                        t.z_down(inside, outside, 1),
                        t.z_up(inside, outside, 1),
                        t.z_up(inside, outside, 2),
                    )

        def value(q):
            return pairs[q, p + 1]

        def fluid_value(q):
            return fl[q, pl.ds(base, half), :]

        conformal, lapse = value(0), value(7)
        over_chi = 1.0 / conformal
        metric = symmetric([value(1 + s) for s in range(6)])
        shift = [value(8 + i) for i in range(3)]
        extrinsic, theta = value(11), value(21)
        traceless = symmetric([value(12 + s) for s in range(6)])
        connection = [value(18 + i) for i in range(3)]
        inverse = inverse_metric(metric)
        grad = [[grads[q, k] for k in range(3)] for q in range(fields)]
        chi_grad, lapse_grad = grad[0], grad[7]
        shift_grad = [[grad[8 + i][k] for i in range(3)] for k in range(3)]
        trace_k = extrinsic + 2.0 * theta

        stress = symmetric([tensors[p - 1, s] for s in range(6)])
        held = [fluid_value(q) for q in range(5)]
        shrink = volume_over(conformal)
        energy = held[4] + held[0]
        third_k = trace_k * (1.0 / 3.0)
        curved = [
            [
                (traceless[i][j] + metric[i][j] * third_k) if i <= j else None for j in range(3)
            ]
            for i in range(3)
        ]
        work = (
            stress[0][0] * curved[0][0]
            + stress[1][1] * curved[1][1]
            + stress[2][2] * curved[2][2]
            + 2.0
            * (
                stress[0][1] * curved[0][1]
                + stress[0][2] * curved[0][2]
                + stress[1][2] * curved[1][2]
            )
        )
        rates = [tensors[p - 1, 6 + q] for q in range(5)]
        for i in range(3):
            rates[1 + i] = (
                rates[1 + i]
                - energy * lapse_grad[i]
                + total([held[1 + k] * grad[8 + k][i] for k in range(3)])
            )
        rates[4] = (
            rates[4] + lapse * work * over_chi / shrink - dot(held[1:4], lapse_grad)
        )
        for q in range(5):
            hydro_rate[q, pl.ds(base, half), :] = rates[q]
        density = energy * shrink
        momentum = [held[1 + i] * shrink for i in range(3)]

        lowered = [[[None] * 3 for _ in range(3)] for _ in range(3)]
        for i in range(3):
            for j in range(3):
                for k in range(j, 3):
                    got = 0.5 * (
                        grad[1 + slot_of(i, k)][j]
                        + grad[1 + slot_of(i, j)][k]
                        - grad[1 + slot_of(j, k)][i]
                    )
                    lowered[i][j][k] = lowered[i][k][j] = got
        raised = [[[None] * 3 for _ in range(3)] for _ in range(3)]
        for i in range(3):
            for j in range(3):
                for k in range(j, 3):
                    got = total([inverse[i][l] * lowered[l][j][k] for l in range(3)])
                    raised[i][j][k] = raised[i][k][j] = got
        contracted = [trace_with(inverse, raised[i]) for i in range(3)]

        def hessian_trace(q):
            return (
                inverse[0][0] * seconds[q, 0]
                + inverse[1][1] * seconds[q, 3]
                + inverse[2][2] * seconds[q, 5]
                + 2.0 * (inverse[0][2] * seconds[q, 2] + inverse[1][2] * seconds[q, 4])
            )

        def second_cov(q, slope):
            bent = [total([raised[k][i][j] * slope[k] for k in range(3)]) for i, j in INDEX_PAIRS]
            return symmetric(
                [-bent[s] if s == 1 else seconds[q, s] - bent[s] for s in range(len(bent))]
            )

        chi_cov = second_cov(0, chi_grad)
        chi_lap = trace_with(inverse, chi_cov)
        raised_chi = [dot(inverse[i], chi_grad) for i in range(3)]
        chi_square = dot(raised_chi, chi_grad)
        cross_term = dot(raised_chi, lapse_grad)
        half_chi = 0.5 * over_chi
        plain_cov = second_cov(7, lapse_grad)
        lapse_cov = symmetric(
            [
                plain_cov[i][j]
                + (
                    chi_grad[i] * lapse_grad[j]
                    + chi_grad[j] * lapse_grad[i]
                    - metric[i][j] * cross_term
                )
                * half_chi
                for i, j in INDEX_PAIRS
            ]
        )
        lapse_lap = conformal * trace_with(inverse, lapse_cov)

        mixed = [
            [[dot(inverse[l], lowered[k][j]) for j in range(3)] for k in range(3)]
            for l in range(3)
        ]
        quarter_sq = half_chi * half_chi
        metric_factor = chi_lap * half_chi - 3.0 * chi_square * quarter_sq
        ricci = []
        for i, j in INDEX_PAIRS:
            second_part = -0.5 * hessian_trace(1 + slot_of(i, j))
            connection_part = 0.5 * total(
                [metric[k][i] * grad[18 + k][j] + metric[k][j] * grad[18 + k][i] for k in range(3)]
            )
            contracted_part = 0.5 * total(
                [contracted[k] * (lowered[i][j][k] + lowered[j][i][k]) for k in range(3)]
            )
            if i == j:
                quadratic = total(
                    [
                        raised[k][l][i] * (2.0 * mixed[l][i][k] + mixed[l][k][i])
                        for k in range(3)
                        for l in range(3)
                    ]
                )
            else:
                quadratic = total(
                    [
                        raised[k][l][i] * (mixed[l][j][k] + mixed[l][k][j])
                        + raised[k][l][j] * mixed[l][i][k]
                        for k in range(3)
                        for l in range(3)
                    ]
                )
            conformal_part = (
                chi_cov[i][j] * half_chi
                + metric[i][j] * metric_factor
                - chi_grad[i] * chi_grad[j] * quarter_sq
            )
            ricci.append(
                second_part + connection_part + contracted_part + quadratic + conformal_part
            )
        ricci = symmetric(ricci)
        ricci_scalar = conformal * trace_with(inverse, ricci)
        stress_trace = conformal * trace_with(inverse, stress)

        up_a = [
            [total([inverse[i][k] * traceless[k][j] for k in range(3)]) for j in range(3)]
            for i in range(3)
        ]
        raised_a = symmetric(
            [total([up_a[i][l] * inverse[j][l] for l in range(3)]) for i, j in INDEX_PAIRS]
        )
        a_square = trace_with(traceless, raised_a)
        shift_div = shift_grad[0][0] + shift_grad[1][1] + shift_grad[2][2]
        two_thirds_div = (2.0 / 3.0) * shift_div

        def finish(q, rate):
            rate = rate + dot(shift, grad[q]) + damped[q]
            st_rate[q, pl.ds(base, half), :] = rate

        finish(0, (2.0 / 3.0) * conformal * (lapse * trace_k - shift_div))
        finish(7, -2.0 * lapse * extrinsic)
        for i in range(3):
            finish(8 + i, 0.75 * connection[i] - SHIFT_DAMPING * shift[i])
        finish(
            11,
            lapse
            * (
                a_square
                + trace_k * trace_k * (1.0 / 3.0)
                + FOUR_PI * (stress_trace + density)
                + KAPPA_ONE * theta
            )
            - lapse_lap,
        )
        source = symmetric(
            [
                lapse * (ricci[i][j] - 2.0 * FOUR_PI * stress[i][j]) - lapse_cov[i][j]
                for i, j in INDEX_PAIRS
            ]
        )
        third_trace = trace_with(inverse, source) * (1.0 / 3.0)
        for s, (i, j) in enumerate(INDEX_PAIRS):
            finish(
                1 + s,
                total(
                    [
                        metric[i][k] * shift_grad[j][k] + metric[j][k] * shift_grad[i][k]
                        for k in range(3)
                    ]
                )
                - metric[i][j] * two_thirds_div
                - 2.0 * lapse * traceless[i][j],
            )
            product = total([traceless[i][k] * up_a[k][j] for k in range(3)])
            finish(
                12 + s,
                total(
                    [
                        traceless[i][k] * shift_grad[j][k] + traceless[j][k] * shift_grad[i][k]
                        for k in range(3)
                    ]
                )
                - traceless[i][j] * two_thirds_div
                + conformal * (source[i][j] - metric[i][j] * third_trace)
                + lapse * (trace_k * traceless[i][j] - 2.0 * product),
            )
        for i in range(3):
            bracket = (
                trace_with(raised_a, raised[i])
                - 1.5 * dot(raised_a[i], chi_grad) * over_chi
                - dot(inverse[i], [2.0 * grad[11][j] + grad[21][j] for j in range(3)]) * (1.0 / 3.0)
                - 2.0 * FOUR_PI * dot(inverse[i], momentum)
            )
            spread = [
                seconds[8, 0] + seconds[10, 2],
                seconds[9, 3] + seconds[10, 4],
                seconds[8, 2] + seconds[9, 4] + seconds[10, 5],
            ]
            finish(
                18 + i,
                contracted[i] * two_thirds_div
                - total([contracted[j] * shift_grad[j][i] for j in range(3)])
                + hessian_trace(8 + i)
                + dot(inverse[i], spread) * (1.0 / 3.0)
                - 2.0 * dot(raised_a[i], lapse_grad)
                + 2.0
                * lapse
                * (bracket - KAPPA_ONE * (connection[i] - contracted[i])),
            )
        finish(
            21,
            0.5
            * lapse
            * (
                ricci_scalar
                - a_square
                + (2.0 / 3.0) * trace_k * trace_k
                - 4.0 * FOUR_PI * density
            )
            - 2.0 * KAPPA_ONE * lapse * theta,
        )

    for index in range(own):
        pair_step(index)


def late_kernel(
    cells, zst, zfl, x_below, y_first, x_above, y_second, below_lanes, c_first, c_second, line_two, line_top,
    st_rate, hydro_rate, slopes, electric, st_out, fl_out,
):
    halo = Halo(
        cells, zst, zfl, x_below, y_first, x_above, y_second, below_lanes, c_first, c_second
    )
    x_below, x_above = halo.x_below, halo.x_above
    t, fields, half, own = halo.t, halo.fields, halo.half, halo.own
    inner, span = halo.inner, halo.span

    top = jnp.maximum(line_top[...], line_two[...])
    for lines in (c_first, c_second):
        top = jnp.maximum(top, lines[CORNER_TILES - 1, TOP_ROW : TOP_ROW + 1, :])
    dt = COURANT / top

    for p in inner:
        place = slice((p - 1) * half, p * half)
        mixed = []
        for q in range(CURVED):
            s_m, s_c, s_p = (
                halo.beside(q, n) if 1 <= n <= own else halo.corner(q, n) for n in (p - 1, p, p + 1)
            )
            slope = slopes[q, p - 1]
            slope_side = first_diff(s_m, t.odd_swapped(s_m, s_c), t.odd_swapped(s_c, s_p), s_p)
            mixed.append(
                first_diff(
                    t.y_down(slope, slope_side, 2),
                    t.y_down(slope, slope_side, 1),
                    t.y_up(slope, slope_side, 1),
                    t.y_up(slope, slope_side, 2),
                )
            )
        conformal, lapse = halo.main(0, p), halo.main(7, p)
        metric = [halo.main(1 + s, p) for s in range(6)]
        inverse = inverse_metric(symmetric(metric))
        half_chi = 0.5 / conformal
        cross = inverse[0][1]
        chi_trace = 2.0 * cross * mixed[0] * half_chi
        ricci = [metric[s] * chi_trace - cross * mixed[1 + s] for s in range(6)]
        ricci[1] = ricci[1] + mixed[0] * half_chi
        source = [lapse * r for r in ricci]
        source[1] = source[1] - mixed[7]
        third_trace = trace_with(inverse, symmetric(source)) * (1.0 / 3.0)
        extra = {
            11: -2.0 * conformal * cross * mixed[7],
            21: 0.5 * lapse * conformal * trace_with(inverse, symmetric(ricci)),
        }
        for s in range(6):
            extra[12 + s] = conformal * (source[s] - metric[s] * third_trace)
        for i in range(3):
            extra[18 + i] = 2.0 * cross * mixed[8 + i] + (1.0 / 3.0) * (
                inverse[i][0] * mixed[9] + inverse[i][1] * mixed[8]
            )
        for q in range(fields):
            rate = st_rate[q, place, :]
            if q in extra:
                rate = rate + extra[q]
            st_out[q, place, :] = halo.main(q, p) + dt * rate

    end = own + 1
    ends = (0, end)
    bx_face, by_face, bz_face = ({p: halo.corner(fields + 5 + i, p) for p in ends} for i in range(3))
    layers = {p: halo.corner_layers(p) for p in ends}
    bx_face[end] = layers[end]
    by_face[0] = jnp.where(t.slot < 2, layers[0], by_face[0])
    centred = [{}, {}, {}]
    for p in ends:
        following = halo.beside(fields + 5, 1) if p == 0 else bx_face[p]
        edge_cells = x_below if p == 0 else x_above
        dx = 0.5 * (t.odd_swapped(bx_face[p], following) - bx_face[p])
        dy = 0.5 * (t.y_up(by_face[p], edge_cells[fields + 6], 1) - by_face[p])
        centred[0][p] = bx_face[p] + dx
        centred[1][p] = by_face[p] + dy
        centred[2][p] = bz_face[p] - (dx + dy)
    corners = [{p: halo.corner(q, p) for p in ends} for q in [0, 7] + list(range(fields, fields + 5))]
    found = primitives(
        half, [(0, p) for p in ends], [[c] for c in corners[2:]], [[c] for c in centred],
        [corners[0]], [corners[1]], 2,
    )
    ez_h = [found[0, 0][10]] + [electric[own + p] for p in inner] + [found[0, end][10]]
    ez_x_h = [None] + [ez_h[p] + t.odd_swapped(ez_h[p - 1], ez_h[p]) for p in span[1:]]
    ez_x = [None] + [electric[p - 1] for p in span[1:]]
    edge_z = [None] + [ez_x[p] + t.y_down(ez_x[p], ez_x_h[p], 1) for p in span[1:]]
    quarter = 0.25 * dt
    for p in inner:
        place = slice((p - 1) * half, p * half)
        edge_z_h = ez_x_h[p] + t.y_down(ez_x_h[p], ez_x[p], 1)
        for q in range(5):
            fl_out[q, place, :] = halo.main(fields + q, p) + dt * hydro_rate[q, place, :]
        x_rate = hydro_rate[5, place, :] - (t.y_up(edge_z[p], edge_z_h, 1) - edge_z[p])
        y_rate = hydro_rate[6, place, :] + (t.odd(edge_z[p], edge_z[p + 1]) - edge_z[p])
        z_rate = hydro_rate[7, place, :]
        for i, rate in enumerate((x_rate, y_rate, z_rate)):
            fl_out[5 + i, place, :] = halo.main(fields + 5 + i, p) + quarter * rate


def per_device(spacetime, fluid):
    fields, cx, cy, cz = spacetime.shape
    rows = cx * cy
    st = spacetime.reshape(fields, rows, cz)
    fl = fluid.reshape(FLUID, rows, cz)
    sizes = [lax.axis_size(a) for a in ("gx", "gy", "gz")]
    tile = (2 * cy, cz)
    f32 = jnp.float32

    def shape(*dims):
        return jax.ShapeDtypeStruct(dims, f32)

    def beyond(cells):
        n = sizes[2]
        after = lax.ppermute(cells, "gz", [((i + 1) % n, i) for i in range(n)])
        if n == 2:
            return after
        before = lax.ppermute(cells, "gz", [(i, (i + 1) % n) for i in range(n)])
        lane = lax.broadcasted_iota(jnp.int32, cells.shape, 2)
        return jnp.where(lane < cz // 2, after, before)

    def beyond_lanes(packed):
        n = sizes[2]
        after = lax.ppermute(packed, "gz", [((i + 1) % n, i) for i in range(n)])
        if n == 2:
            return after
        before = lax.ppermute(packed, "gz", [(i, (i + 1) % n) for i in range(n)])
        lane = lax.broadcasted_iota(jnp.int32, packed.shape, 2)
        return jnp.where(lane % 4 < 2, before, after)

    params = pltpu.CompilerParams(vmem_limit_bytes=48 * 1024 * 1024)
    zst, zfl = beyond(st), beyond(fl)
    cells = jnp.concatenate([st, fl], axis=0)
    face = shape(face_tiles(fields), *tile)
    corner = shape(CORNER_TILES, *tile)
    lane_row = shape(1, cz)
    def call(kernel, outs, name, operands, scratch=()):
        return pl.pallas_call(
            kernel,
            out_shape=outs,
            scratch_shapes=scratch,
            compiler_params=params,
            name=name,
        )(*operands)

    def shift(cells, step):
        n = lax.axis_size("gx")
        return lax.ppermute(cells, "gx", [(i, (i + step) % n) for i in range(n)])

    def trade(cells, first):
        axis = "gy"
        n = lax.axis_size(axis)
        step = [1, -1] if first else [-1, 1]
        return lax.ppermute(cells, axis, [(i, (i + step[i % 2]) % n) for i in range(n)])

    def two_away(cells, axis):
        n = lax.axis_size(axis)
        return lax.ppermute(cells, axis, [(i, (i + 2) % n) for i in range(n)]) if n == 4 else cells

    short = sizes[0] <= 4 and sizes[1] <= 4 and sizes[2] <= 2
    x_high = call(pack_up_kernel, face, "pack_up", (cells,))
    x_below = shift(x_high, 1)
    x_low, y_first, y_second, top = call(
        pack_kernel, [face, face, face, shape(TOP_TILES, *tile)], "pack", (cells, zst, zfl)
    )
    below_lanes = beyond_lanes(call(lanes_kernel, shape(1, *tile), "lanes", (x_below,)))
    y_first = trade(y_first, True)
    x_above = shift(x_low, -1)
    y_second = trade(y_second, False)
    top_two = two_away(top, "gx")
    c_first, c_second, line_top = call(
        relay_kernel,
        [corner, corner, lane_row],
        "relay",
        (x_below, below_lanes, x_above, y_first, top, top_two),
    )
    c_first = trade(c_first, True)
    c_second = trade(c_second, False)
    if short:
        line_two = two_away(line_top, "gy")
    else:
        line_two = lax.pmax(line_top, ("gx", "gy", "gz"))
    own = cx // 2
    arrived = (cells, zst, zfl, x_below, y_first, x_above, y_second, below_lanes)
    early = call(
        early_kernel,
        [
            shape(*st.shape),
            shape(FLUID, rows, cz),
            shape(CURVED, own, *tile),
            shape(2 * own + 1, *tile),
        ],
        "early",
        arrived,
        [
            pltpu.VMEM((fields, own + 4) + tile, f32),
            pltpu.VMEM((fields, own) + tile, f32),
            pltpu.VMEM((fields, own) + tile, f32),
            pltpu.VMEM((CURVED, own + 2) + tile, f32),
            pltpu.VMEM((CURVED, own) + tile, f32),
            pltpu.VMEM((fields, 3) + tile, f32),
            pltpu.VMEM((CURVED, 6) + tile, f32),
            pltpu.VMEM((fields,) + tile, f32),
            pltpu.VMEM((own, 11) + tile, f32),
        ],
    )
    st_next, fl_next = call(
        late_kernel,
        [shape(*st.shape), shape(*fl.shape)],
        "late",
        (*arrived, c_first, c_second, line_two, line_top, *early),
    )
    return st_next.reshape(spacetime.shape), fl_next.reshape(fluid.shape)


def solution(mesh):
    spec = P(None, "gx", "gy", "gz")
    return jax.shard_map(
        per_device, mesh=mesh, in_specs=(spec, spec), out_specs=(spec, spec), check_vma=False
    )
```

```python
import functools
import math

import jax
import jax.numpy as jnp
from jax import lax
from jax.experimental import pallas as pl
from jax.experimental.pallas import tpu as pltpu
from jax.sharding import PartitionSpec as P

RECOVERY_STEPS = 4
INDEX_PAIRS = ((0, 0), (0, 1), (0, 2), (1, 1), (1, 2), (2, 2))
COURANT = 0.25
DISSIPATION = 0.2
KAPPA_ONE = 0.02
SHIFT_DAMPING = 1.0
SPEED_CAP = 0.99
PRESSURE_FLOOR = 0.01
FOUR_PI = 4.0 * math.pi

BATCH = 6
CURVED = 11
FLUID = 8


def total(pieces):
    summed = pieces[0]
    for member in pieces[1:]:
        summed = summed + member
    return summed


def dot(first_vec, second_vec):
    return total([first_vec[i] * second_vec[i] for i in range(3)])


def slot_of(i, j):
    return INDEX_PAIRS.index((min(i, j), max(i, j)))


def symmetric(entries):
    return [[entries[slot_of(i, j)] for j in range(3)] for i in range(3)]


def trace_with(inverse, tensor):
    return (
        inverse[0][0] * tensor[0][0]
        + inverse[1][1] * tensor[1][1]
        + inverse[2][2] * tensor[2][2]
        + 2.0
        * (
            inverse[0][1] * tensor[0][1]
            + inverse[0][2] * tensor[0][2]
            + inverse[1][2] * tensor[1][2]
        )
    )


def inverse_metric(metric):
    cofactor = [
        metric[1][1] * metric[2][2] - metric[1][2] * metric[1][2],
        metric[0][2] * metric[1][2] - metric[0][1] * metric[2][2],
        metric[0][1] * metric[1][2] - metric[0][2] * metric[1][1],
        metric[0][0] * metric[2][2] - metric[0][2] * metric[0][2],
        metric[0][1] * metric[0][2] - metric[0][0] * metric[1][2],
        metric[0][0] * metric[1][1] - metric[0][1] * metric[0][1],
    ]
    determinant = (
        metric[0][0] * cofactor[0] + metric[0][1] * cofactor[1] + metric[0][2] * cofactor[2]
    )
    over = 1.0 / determinant
    return symmetric([c * over for c in cofactor])


class Tile:
    def __init__(self, cy, cz):
        self.cy, self.rows, self.lanes = cy, 2 * cy, cz
        shape = (self.rows, cz)
        self.row = lax.broadcasted_iota(jnp.int32, shape, 0)
        self.lane = lax.broadcasted_iota(jnp.int32, shape, 1)
        self.slot = lax.rem(self.row, cy)

    def turn(self, tile, amount):
        amount = amount % self.rows
        return tile if amount == 0 else pltpu.roll(tile, amount, 0)

    def spin(self, tile, amount):
        amount = amount % self.lanes
        return tile if amount == 0 else pltpu.roll(tile, amount, 1)

    def swap(self, tile):
        return self.turn(tile, self.cy)

    def odd(self, a, b):
        return self.turn(jnp.where(self.row < self.cy, b, a), self.cy)

    def odd_swapped(self, a, b):
        return self.turn(jnp.where(self.row < self.cy, a, b), self.cy)

    def y_up(self, main, beyond, k):
        return self.turn(jnp.where(self.slot < k, beyond, main), -k)

    def y_down(self, main, beyond, k):
        return self.turn(jnp.where(self.slot >= self.cy - k, beyond, main), k)

    def z_up(self, main, beyond, k):
        return self.spin(jnp.where(self.lane < k, beyond, main), -k)

    def z_down(self, main, beyond, k):
        return self.spin(jnp.where(self.lane >= self.lanes - k, beyond, main), k)

    def corner_rows(self, side, turn):
        places = ((0, 2), (self.cy - 1, self.cy + 1))[side]
        first, second = [(place + turn) % self.rows for place in places]
        return (self.row == first) | (self.row == second)

    def join_low(self, u, v):
        return jnp.where(self.slot < 2, self.swap(u), self.turn(v, 2))

    def join_high(self, u, v):
        return jnp.where(self.slot >= self.cy - 2, self.swap(u), self.turn(self.swap(v), -2))

    def part_first(self, from_above, from_below):
        return jnp.where(self.slot < 2, from_above, from_below)

    def part_second(self, from_above, from_below):
        return self.turn(jnp.where(self.slot < 2, from_below, from_above), 2)


def edge_list(tiles):
    fields = next(n for n in range(tiles) if face_tiles(n) == tiles)
    return list(range(CURVED)) + list(range(fields, fields + FLUID))


CORNER_TURNS = (0, 1, 4, 5)
TOP_TILES = 2
CORNER_TILES = CURVED + FLUID // 4 + 1
TOP_ROW = 6


def face_tiles(fields):
    return fields + FLUID + len(pairs_of(third_list(fields))) + 1


def third_list(fields):
    return list(range(fields + 1))


def pairs_of(items):
    return [(items[i], items[min(i + 1, len(items) - 1)]) for i in range(0, len(items), 2)]


def top_speed(st):
    inverse = inverse_metric(symmetric([st[1 + s] for s in range(6)]))
    scale = 2.0 * st[7] * st[0]
    speeds = [jnp.abs(st[8 + d]) + jnp.sqrt(scale * inverse[d][d]) for d in range(3)]
    top = jnp.maximum(jnp.maximum(speeds[0], speeds[1]), speeds[2])
    return jnp.max(jnp.max(top, axis=1, keepdims=True), axis=0, keepdims=True)


class Chosen:
    def __init__(self, first, second, swapped):
        self.first, self.second, self.swapped, self.shape = first, second, swapped, first.shape

    def __getitem__(self, key):
        return jnp.where(self.swapped, self.second[key], self.first[key])


class Sent:
    def __init__(self, first, second, swapped):
        self.first, self.second, self.swapped, self.shape = first, second, swapped, first.shape

    def put(self, key, lower, upper):
        self.first[key] = jnp.where(self.swapped, upper, lower)
        self.second[key] = jnp.where(self.swapped, lower, upper)


class Joined:
    def __init__(self, tiles, tail):
        self.tiles, self.tail = tiles, tail
        self.shape = tuple(tiles.shape)

    def __getitem__(self, key):
        q, rows = (key[0], key[1:]) if isinstance(key, tuple) else (key, ())
        if q == self.tiles.shape[0] - 1:
            return self.tail[(0,) + rows]
        return self.tiles[(q,) + rows]


def even_along_y(tile):
    return jnp.full(tile, lax.rem(lax.axis_index("gy"), 2), jnp.int32) == 0


def pack_up_kernel(cells, x_high):
    count, rows, lanes = cells.shape
    fields, half = count - FLUID, rows // 2
    t = Tile(rows // 4, lanes)
    for q in range(count):
        x_high[q] = cells[q, half:rows, :]
    for n, (a, b) in enumerate(pairs_of(list(range(fields)) + [fields + 5])):
        x_high[count + n] = jnp.where(
            t.row < t.cy, t.swap(cells[b, 0:half, :]), cells[a, 0:half, :]
        )
    x_high[x_high.shape[0] - 1] = jnp.broadcast_to(top_speed(cells), t.row.shape)


def lanes_kernel(x_below, out):
    t = Tile(x_below.shape[1] // 2, x_below.shape[2])
    last = x_below.shape[0] - 1
    packed = x_below[last]
    for place, q in enumerate(edge_list(x_below.shape[0])):
        piece = t.spin(x_below[q], 4 * place + 2)
        here = (t.lane >= 4 * place) & (t.lane < 4 * place + 4)
        packed = jnp.where(here, piece, packed)
    out[0] = packed


def pack_kernel(cells, zst, zfl, *outs):
    fields, rows, lanes = zst.shape
    st, fl = cells.at[0:fields], cells.at[fields : fields + FLUID]
    cy = rows // 4
    t = Tile(cy, lanes)
    x_low, y_first, y_second, top_out = outs
    half = t.rows
    to_y = Sent(y_first, y_second, even_along_y((half, lanes)))

    def own(ref, q):
        return [ref[q, 0:half, :], ref[q, half : 2 * half, :]]

    tiles, beyond = [], []
    for q in range(fields):
        tiles.append(own(st, q))
        beyond.append(own(zst, q) if q < CURVED else None)
    for q in range(FLUID):
        tiles.append(own(fl, q))
        beyond.append(own(zfl, q))

    packed = [None] * 4
    place_count = 0
    for q, (first, second) in enumerate(tiles):
        x_low[q] = first
        to_y.put(q, t.join_low(first, second), t.join_high(first, second))
        if beyond[q] is not None:
            zf, zs = beyond[q]
            for m, piece in enumerate((zf, zs, t.join_low(zf, zs), t.join_high(zf, zs))):
                piece = t.spin(piece, 4 * place_count + 2)
                packed[m] = (
                    piece if place_count == 0 else jnp.where(t.lane < 4 * place_count, packed[m], piece)
                )
            place_count += 1
    for n, (a, b) in enumerate(pairs_of(third_list(fields))):
        slot = fields + FLUID + n
        xa, xb = (tiles[q if q < fields else fields + 5] for q in (a, b))
        x_low[slot] = jnp.where(t.row < cy, xa[1], t.swap(xb[1]))
        ya, yb = (tiles[q if q < fields else fields + 6] for q in (a, b))
        w = [t.swap(ya[0]), t.swap(ya[1]), t.swap(yb[0]), t.swap(yb[1])]
        s = t.slot
        low = jnp.where(s == 0, t.turn(w[2], -2), t.turn(w[3], -1))
        low = jnp.where(s == 2, w[0], jnp.where(s == 3, t.turn(w[1], 1), low))
        high = jnp.where(s == 3, t.turn(w[2], 2), t.turn(w[3], 1))
        high = jnp.where(s == 1, w[0], jnp.where(s == 0, t.turn(w[1], -1), high))
        to_y.put(slot, low, high)
    top = jnp.maximum(top_speed(st), top_speed(zst))
    top_out[...] = jnp.broadcast_to(top, top_out.shape)
    last = x_low.shape[0] - 1
    x_lanes = [jnp.where(t.lane < 4 * place_count, piece, top) for piece in packed[:2]]
    y_lanes = [jnp.where(t.lane < 4 * place_count, piece, top) for piece in packed[2:]]
    x_low[last] = x_lanes[0]
    to_y.put(last, *y_lanes)


def relay_kernel(x_below, below_lanes, x_above, top, top_two, c_first, c_second, line_top):
    cy, lanes = x_below.shape[1] // 2, x_below.shape[2]
    t = Tile(cy, lanes)
    to_y = Sent(c_first, c_second, even_along_y((t.rows, lanes)))
    last = x_below.shape[0] - 1
    line = jnp.maximum(top[0, 0:1, :], top_two[0, 0:1, :])
    line = jnp.maximum(line, x_below[last, 0:1, lanes - 1 : lanes])
    x_below = Joined(x_below, below_lanes)
    for beside in (x_below, x_above):
        line = jnp.maximum(line, beside[last, 0:1, lanes - 1 : lanes])
    line_top[...] = line
    edge = edge_list(x_below.shape[0])
    for q in range(CURVED):
        below, above = x_below[q], x_above[q]
        to_y.put(q, t.join_low(below, above), t.join_high(below, above))
    for n in range(0, FLUID, 4):
        low, high = None, None
        for turn, q in zip(CORNER_TURNS, edge[CURVED + n : CURVED + n + 4]):
            below, above = x_below[q], x_above[q]
            below, above = (t.turn(j(below, above), turn) for j in (t.join_low, t.join_high))
            if low is None:
                low, high = below, above
            else:
                low = jnp.where(t.corner_rows(0, turn), below, low)
                high = jnp.where(t.corner_rows(1, turn), above, high)
        to_y.put(CURVED + n // 4, low, high)
    along_x, along_y = edge[CURVED + 5], edge[CURVED + 6]
    low = t.join_low(x_below[along_y], x_above[along_y])
    high = t.join_high(x_below[along_x], x_above[along_x])
    low, high = (jnp.where(t.row == TOP_ROW, line, tile) for tile in (low, high))
    to_y.put(CORNER_TILES - 1, low, high)


def limited(a, b):
    return jnp.maximum(jnp.minimum(a, b), 0.0) + jnp.minimum(jnp.maximum(a, b), 0.0)


def recover(conserved, magnetic):
    density = conserved[0]
    momenta = conserved[1:4]
    energy = conserved[4] + density
    mom_sq = dot(momenta, momenta)
    mag_sq = dot(magnetic, magnetic)
    cross = dot(momenta, magnetic)
    cross_sq = cross * cross

    def state(z):
        grown = z + mag_sq
        over = 1.0 / (z * grown)
        speed_sq = (mom_sq * z * z + cross_sq * (2.0 * z + mag_sq)) * over * over
        kept = 1.0 - jnp.minimum(speed_sq, SPEED_CAP)
        rest = density * jnp.sqrt(kept)
        return kept, rest, 0.5 * (z * kept - rest), grown * over

    z = jnp.maximum(energy - 0.5 * mag_sq, density)
    for _ in range(RECOVERY_STEPS):
        kept, rest, pressure, over_z = state(z)
        residual = (
            z
            + mag_sq
            - pressure
            - 0.5 * mag_sq * kept
            - 0.5 * cross_sq * over_z * over_z
            - energy
        )
        z = jnp.maximum(z - residual / (1.0 - 0.5 * kept), density)
    kept, rest, pressure, over_z = state(z)
    pressure = jnp.maximum(pressure, PRESSURE_FLOOR * rest)
    scale = lax.rsqrt(kept) / (z + mag_sq)
    along = cross * over_z
    four_vel = [scale * (momenta[i] + along * magnetic[i]) for i in range(3)]
    return [rest, pressure] + four_vel


def stress_parts(rest, pressure, u, magnetic):
    lorentz_sq = 1.0 + dot(u, u)
    over = lax.rsqrt(lorentz_sq)
    over_sq = over * over
    time_b = dot(u, magnetic)
    grown_b = [magnetic[i] + time_b * u[i] for i in range(3)]
    b_square = (dot(magnetic, magnetic) + time_b * time_b) * over_sq
    enthalpy = rest + 2.0 * pressure
    inertia = enthalpy + b_square
    return lorentz_sq, over, over_sq, time_b, grown_b, b_square, enthalpy, inertia


def face_state(rest, pressure, u, magnetic, d):
    lorentz_sq, over, over_sq, time_b, grown_b, b_square, enthalpy, inertia = stress_parts(
        rest, pressure, u, magnetic
    )
    total_pressure = pressure + 0.5 * b_square
    lorentz = lorentz_sq * over
    density = rest * lorentz
    carried = inertia * lorentz
    time_over = time_b * over
    conserved = [density]
    conserved += [carried * u[j] - time_over * grown_b[j] for j in range(3)]
    conserved += [inertia * lorentz_sq - total_pressure - time_b * time_b - density]
    mass_flux = rest * u[d]
    flux = [mass_flux]
    pushed = inertia * u[d]
    b_over = grown_b[d] * over_sq
    for j in range(3):
        flux_j = pushed * u[j] - b_over * grown_b[j]
        flux.append(flux_j + total_pressure if j == d else flux_j)
    flux.append(carried * u[d] - time_over * grown_b[d] - mass_flux)
    ratio = 1.0 / (enthalpy * inertia)
    sound_sq = 2.0 * pressure * inertia * ratio
    alfven_sq = b_square * enthalpy * ratio
    fast_sq = sound_sq + alfven_sq - sound_sq * alfven_sq
    slow = 1.0 - fast_sq
    velocity = u[d] * over
    rest_part = 1.0 - dot(u, u) * over_sq * fast_sq
    spread = jnp.sqrt(fast_sq * over_sq * (rest_part - velocity * velocity * slow))
    fastest = (jnp.abs(velocity * slow) + spread) / rest_part
    return conserved, flux, fastest


def face_flux(left, right, normal, weight, d):
    sides = []
    for state in (left, right):
        magnetic = [normal if i == d else state[5 + i] for i in range(3)]
        sides.append(face_state(state[0], state[1], state[2:5], magnetic, d))
    (cons_l, flux_l, fast_l), (cons_r, flux_r, fast_r) = sides
    signal = jnp.maximum(fast_l, fast_r)
    scale = 0.5 * weight
    return [scale * (flux_l[q] + flux_r[q] - signal * (cons_r[q] - cons_l[q])) for q in range(5)]


def volume_over(conformal):
    return conformal * jnp.sqrt(conformal)


def first_diff(down_two, down, up, up_two):
    return (8.0 / 12.0) * (up - down) + (1.0 / 12.0) * (down_two - up_two)


class Halo:
    def __init__(self, cells, zst, zfl, x_below, y_first, x_above, y_second, below_lanes, *corners):
        x_below = Joined(x_below, below_lanes)
        self.fields, self.block, self.lanes = zst.shape
        even_y = even_along_y((self.block // 2, self.lanes))
        y_below, y_above = Chosen(y_first, y_second, even_y), Chosen(y_second, y_first, even_y)
        if corners:
            c_first, c_second = corners
            self.c_below = Chosen(c_first, c_second, even_y)
            self.c_above = Chosen(c_second, c_first, even_y)
        self.st = cells.at[0 : self.fields]
        self.fl = cells.at[self.fields : self.fields + FLUID]
        self.zst, self.zfl = zst, zfl
        self.x_below, self.x_above = x_below, x_above
        self.y_below, self.y_above = y_below, y_above
        self.cy = self.block // 4
        self.t = Tile(self.cy, self.lanes)
        self.half = self.t.rows
        self.own = self.block // self.half
        self.inner = range(1, self.own + 1)
        self.span = range(self.own + 2)
        self.edge = edge_list(x_below.shape[0])
        self.last = x_below.shape[0] - 1

    def rows_of(self, ref, q, p):
        return ref[q, (p - 1) * self.half : p * self.half, :]

    def main(self, q, p):
        if q < self.fields:
            return self.rows_of(self.st, q, p)
        return self.rows_of(self.fl, q - self.fields, p)

    def beyond(self, q, p):
        if q < self.fields:
            return self.rows_of(self.zst, q, p)
        return self.rows_of(self.zfl, q - self.fields, p)

    def part(self, second):
        return self.t.part_second if second else self.t.part_first

    def beside(self, q, p):
        return self.part(p == 2)(self.y_above[q], self.y_below[q])

    def third_place(self, q):
        return self.fields + FLUID + q // 2, q % 2

    def x_third(self, q, upper):
        tile, which = self.third_place(q)
        found = self.x_above[tile] if upper else self.x_below[tile]
        return self.t.swap(found) if which else found

    def y_third(self, q, p):
        t = self.t
        tile, which = self.third_place(q)
        turn_above, turn_below = ((0, 0), (-1, 1), (2, -2), (1, -1))[2 * which + p - 1]
        above, below = t.turn(self.y_above[tile], turn_above), t.turn(self.y_below[tile], turn_below)
        return jnp.where(t.slot == 2, above, below)

    def z_place(self, q):
        return 4 * self.edge.index(q) + 2

    def x_beyond(self, q, upper):
        tile = self.x_above[self.last] if upper else self.x_below[self.last]
        return self.t.spin(tile, -self.z_place(q))

    def y_beyond(self, q, p):
        return self.t.spin(self.beside(self.last, p), -self.z_place(q))

    def corner(self, q, p):
        place, turn = q, 0
        if q >= CURVED:
            n = q - self.fields
            place, turn = CURVED + n // 4, CORNER_TURNS[n % 4]
        above, below = self.t.turn(self.c_above[place], -turn), self.t.turn(self.c_below[place], -turn)
        return self.part(p > 0)(above, below)

    def corner_layers(self, p):
        place = CORNER_TILES - 1
        return self.part(p > 0)(self.c_above[place], self.c_below[place])

    def plane(self, q):
        inner = self.inner
        return (
            [self.x_below[q]] + [self.main(q, p) for p in inner] + [self.x_above[q]],
            [None] + [self.beside(q, p) for p in inner] + [None],
            [self.x_beyond(q, False)]
            + [self.beyond(q, p) for p in inner]
            + [self.x_beyond(q, True)],
            [None] + [self.y_beyond(q, p) for p in inner] + [None],
        )


def weigh(chi_face, alpha_face):
    shrink = volume_over(chi_face)
    return shrink, alpha_face / shrink


def primitives(half, spots, cons, centred, chi, alpha, batch):
    found = {}
    for start in range(0, len(spots), batch):
        group = spots[start : start + batch]

        def gather(planes):
            return jnp.concatenate([planes[k][p] for k, p in group], axis=0)

        shrink = volume_over(gather(chi))
        mag_raw = [gather(centred[i]) for i in range(3)]
        mag = [m * shrink for m in mag_raw]
        values = recover([gather(c) * shrink for c in cons], mag)
        u = values[2:5]
        factor = gather(alpha) * lax.rsqrt(1.0 + dot(u, u))
        field = [
            factor * (u[(i + 2) % 3] * mag_raw[(i + 1) % 3] - u[(i + 1) % 3] * mag_raw[(i + 2) % 3])
            for i in range(3)
        ]
        for n, spot in enumerate(group):
            found[spot] = [value[n * half : (n + 1) * half] for value in values + mag + field]
    return found


def ring_fluxes(prims, chi, alpha, normals, d, up, down):
    found = []
    for here, there in ((0, 1), (1, 0)):
        left, right = [], []
        for a, b in zip(prims[here], prims[there]):
            below = down(a, b, 1)
            middle = a - below
            left.append(below + 0.5 * limited(below - down(a, b, 2), middle))
            right.append(a - 0.5 * limited(middle, up(a, b, 1) - a))
        shrink, weight = weigh(
            0.5 * (chi[here] + down(chi[here], chi[there], 1)),
            0.5 * (alpha[here] + down(alpha[here], alpha[there], 1)),
        )
        found.append(face_flux(left, right, normals[here] * shrink, weight, d))
    return [a - up(a, b, 1) for a, b in zip(*found)]


def early_kernel(
    cells, zst, zfl, x_below, y_first, x_above, y_second, below_lanes,
    st_rate, hydro_rate, slopes, electric, pairs, sides, thirds, pairs_z, sides_z, grads, seconds, damped, tensors,
):
    halo = Halo(cells, zst, zfl, x_below, y_first, x_above, y_second, below_lanes)
    t, fields, half, own, cy = halo.t, halo.fields, halo.half, halo.own, halo.cy
    st, fl, inner = halo.st, halo.fl, halo.inner

    for q in range(fields):
        pairs[q, 0] = halo.x_third(q, False)
        pairs[q, 1] = x_below[q]
        for p in inner:
            pairs[q, 1 + p] = halo.main(q, p)
            sides[q, p - 1] = halo.beside(q, p)
            thirds[q, p - 1] = halo.y_third(q, p)
        pairs[q, 2 + own] = x_above[q]
        pairs[q, 3 + own] = halo.x_third(q, True)
        if q < CURVED:
            pairs_z[q, 0] = halo.x_beyond(q, False)
            pairs_z[q, own + 1] = halo.x_beyond(q, True)
            for p in inner:
                pairs_z[q, p] = halo.beyond(q, p)
                sides_z[q, p - 1] = halo.y_beyond(q, p)

    span = halo.span
    face = [halo.plane(fields + 5 + i) for i in range(3)]

    def halves(kind, p):
        own_x, own_y, own_z = (f[kind][p] for f in face)
        pair = kind in (0, 2)
        known_x = pair or p < own
        last = kind == 0 and p == own + 1
        if pair:
            next_x = halo.x_third(fields, True) if last else face[0][kind][min(p + 1, own + 1)]
            next_x = t.odd(own_x, next_x)
        else:
            next_x = t.odd_swapped(own_x, face[0][kind][p + 1] if known_x else own_x)
        dx = 0.5 * (next_x - own_x)
        dz = 0.5 * (t.z_up(own_z, face[2][kind ^ 2][p], 1) - own_z)
        inside = 1 <= p <= own
        if not pair:
            here = jnp.where(t.slot == 2, halo.y_third(fields, p), own_y) if kind == 1 else own_y
            next_y = t.y_up(here, face[1][kind ^ 1][p], 1)
        else:
            next_y = t.y_up(own_y, face[1][kind ^ 1][p] if inside else own_y, 1)
        dy = 0.5 * (next_y - own_y)
        if pair and not inside:
            dy = jnp.where(t.slot == cy - 1, -(dx + dz), dy)
        if not pair and not known_x:
            dx = jnp.where(t.row < cy, -(dy + dz), dx)
        return own_x + dx, own_y + dy, own_z + dz

    spots = [(0, p) for p in span] + [(1, p) for p in inner]
    spots += [(2, p) for p in span] + [(3, p) for p in inner]
    centred = [[[None] * (own + 2) for _ in range(4)] for _ in range(3)]
    for k, p in spots:
        for i, value in enumerate(halves(k, p)):
            centred[i][k][p] = value
    chi, alpha = halo.plane(0), halo.plane(7)
    found = primitives(
        half, spots, [halo.plane(fields + q) for q in range(5)], centred, chi, alpha, BATCH
    )

    lines = [[found[0, p][i] for p in span] for i in range(8)] + [chi[0], alpha[0]]
    odd_lines = [[t.odd(f[p], f[min(p + 1, own + 1)]) for p in span] for f in lines]
    fluxes = [None]
    for p in range(1, own + 2):
        left, right = [], []
        for f, o in zip(lines[:8], odd_lines):
            here = f[p] - o[p - 1]
            left.append(o[p - 1] + 0.5 * limited(o[p - 1] - f[p - 1], here))
            right.append(f[p] - 0.5 * limited(here, o[p] - f[p]))
        shrink, weight = weigh(
            0.5 * (lines[8][p] + odd_lines[8][p - 1]), 0.5 * (lines[9][p] + odd_lines[9][p - 1])
        )
        fluxes.append(face_flux(left, right, face[0][0][p] * shrink, weight, 0))
    for p in inner:
        changes = [
            ring_fluxes(
                [found[k, p][:8] for k in (0, kind)],
                [chi[k][p] for k in (0, kind)],
                [alpha[k][p] for k in (0, kind)],
                [face[d][k][p] for k in (0, kind)],
                d,
                up,
                down,
            )
            for d, kind, up, down in ((1, 1, t.y_up, t.y_down), (2, 2, t.z_up, t.z_down))
        ]
        for q in range(5):
            change = fluxes[p][q] - t.odd(fluxes[p][q], fluxes[p + 1][q])
            tensors[p - 1, 6 + q] = change + changes[0][q] + changes[1][q]
        rest, pressure = found[0, p][:2]
        u = found[0, p][2:5]
        parts = stress_parts(rest, pressure, u, found[0, p][5:8])
        lorentz_sq, over, over_sq, time_b, grown_b, b_square, enthalpy, inertia = parts
        total_pressure = pressure + 0.5 * b_square
        for s, (i, j) in enumerate(INDEX_PAIRS):
            value = inertia * u[i] * u[j] - over_sq * (grown_b[i] * grown_b[j])
            tensors[p - 1, s] = value + total_pressure if i == j else value

    ex, ey, ez = (
        [[found[k, p][8 + i] if (k, p) in found else None for p in span] for k in range(4)]
        for i in range(3)
    )
    ey_x = [
        [ey[k][p] + t.odd(ey[k][p - 1], ey[k][p]) if p else None for p in span] for k in (0, 2)
    ]
    edge_y = [None] + [ey_x[0][p] + t.z_down(ey_x[0][p], ey_x[1][p], 1) for p in span[1:]]
    for p in span[1:]:
        electric[p - 1] = ez[0][p] + t.odd(ez[0][p - 1], ez[0][p])
    for p in inner:
        electric[own + p] = ez[1][p]
        edge_y_z = ey_x[1][p] + t.z_down(ey_x[1][p], ey_x[0][p], 1)
        ex_y = ex[0][p] + t.y_down(ex[0][p], ex[1][p], 1)
        ex_y_h = ex[1][p] + t.y_down(ex[1][p], ex[0][p], 1)
        ex_y_z = ex[2][p] + t.y_down(ex[2][p], ex[3][p], 1)
        ex_y_hz = ex[3][p] + t.y_down(ex[3][p], ex[2][p], 1)
        edge_x = ex_y + t.z_down(ex_y, ex_y_z, 1)
        edge_x_h = ex_y_h + t.z_down(ex_y_h, ex_y_hz, 1)
        edge_x_z = ex_y_z + t.z_down(ex_y_z, ex_y, 1)
        place = slice((p - 1) * half, p * half)
        hydro_rate[5, place, :] = t.z_up(edge_y[p], edge_y_z, 1) - edge_y[p]
        hydro_rate[6, place, :] = edge_x - t.z_up(edge_x, edge_x_z, 1)
        hydro_rate[7, place, :] = (t.y_up(edge_x, edge_x_h, 1) - edge_x) - (
            t.odd(edge_y[p], edge_y[p + 1]) - edge_y[p]
        )

    def pair_step(index):
        p = index + 1
        base = index * half

        for q in range(fields):
            centre = pairs[q, p + 1]
            x_m3 = t.odd(pairs[q, p - 1], pairs[q, p])
            x_m2 = pairs[q, p]
            x_m1 = t.odd(pairs[q, p], centre)
            x_p1 = t.odd(centre, pairs[q, p + 2])
            x_p2 = pairs[q, p + 2]
            x_p3 = t.odd(pairs[q, p + 2], pairs[q, p + 3])
            side, third = sides[q, index], thirds[q, index]
            y_m1, y_m2 = t.y_down(centre, side, 1), t.y_down(centre, side, 2)
            y_p1, y_p2 = t.y_up(centre, side, 1), t.y_up(centre, side, 2)
            y_m3 = t.turn(
                jnp.where(t.slot >= cy - 2, side, jnp.where(t.slot == cy - 3, third, centre)), 3
            )
            y_p3 = t.turn(jnp.where(t.slot < 2, side, jnp.where(t.slot == 2, third, centre)), -3)
            beyond = zst[q, pl.ds(base, half), :]
            z_m1, z_m2, z_m3 = (t.z_down(centre, beyond, k) for k in (1, 2, 3))
            z_p1, z_p2, z_p3 = (t.z_up(centre, beyond, k) for k in (1, 2, 3))
            dx = first_diff(x_m2, x_m1, x_p1, x_p2)
            dy = first_diff(y_m2, y_m1, y_p1, y_p2)
            grads[q, 0] = dx
            if q < CURVED:
                slopes[q, index] = dx
            grads[q, 1] = dy
            grads[q, 2] = first_diff(z_m2, z_m1, z_p1, z_p2)
            near = [x_m1 + x_p1, y_m1 + y_p1, z_m1 + z_p1]
            far = [x_m2 + x_p2, y_m2 + y_p2, z_m2 + z_p2]
            outer = (x_m3 + x_p3) + (y_m3 + y_p3) + (z_m3 + z_p3)
            damped[q] = (DISSIPATION / 64.0) * (
                outer - 6.0 * (far[0] + far[1] + far[2]) + 15.0 * (near[0] + near[1] + near[2])
                - 60.0 * centre
            )
            if q < CURVED:
                for s, d in ((0, 0), (3, 1), (5, 2)):
                    seconds[q, s] = (1.0 / 12.0) * (16.0 * near[d] - far[d] - 30.0 * centre)
                b_m, b_c, b_p = pairs_z[q, p - 1], pairs_z[q, p], pairs_z[q, p + 1]
                dx_z = first_diff(b_m, t.odd(b_m, b_c), t.odd(b_c, b_p), b_p)
                b_s = sides_z[q, p - 1]
                dy_z = first_diff(
                    t.y_down(b_c, b_s, 2),
                    t.y_down(b_c, b_s, 1),
                    t.y_up(b_c, b_s, 1),
                    t.y_up(b_c, b_s, 2),
                )
                for s, inside, outside in ((2, dx, dx_z), (4, dy, dy_z)):
                    seconds[q, s] = first_diff(
                        t.z_down(inside, outside, 2),
                        t.z_down(inside, outside, 1),
                        t.z_up(inside, outside, 1),
                        t.z_up(inside, outside, 2),
                    )

        def value(q):
            return pairs[q, p + 1]

        def fluid_value(q):
            return fl[q, pl.ds(base, half), :]

        conformal, lapse = value(0), value(7)
        over_chi = 1.0 / conformal
        metric = symmetric([value(1 + s) for s in range(6)])
        shift = [value(8 + i) for i in range(3)]
        extrinsic, theta = value(11), value(21)
        traceless = symmetric([value(12 + s) for s in range(6)])
        connection = [value(18 + i) for i in range(3)]
        inverse = inverse_metric(metric)
        grad = [[grads[q, k] for k in range(3)] for q in range(fields)]
        chi_grad, lapse_grad = grad[0], grad[7]
        shift_grad = [[grad[8 + i][k] for i in range(3)] for k in range(3)]
        trace_k = extrinsic + 2.0 * theta

        stress = symmetric([tensors[p - 1, s] for s in range(6)])
        held = [fluid_value(q) for q in range(5)]
        shrink = volume_over(conformal)
        energy = held[4] + held[0]
        third_k = trace_k * (1.0 / 3.0)
        curved = [
            [
                (traceless[i][j] + metric[i][j] * third_k) if i <= j else None for j in range(3)
            ]
            for i in range(3)
        ]
        work = (
            stress[0][0] * curved[0][0]
            + stress[1][1] * curved[1][1]
            + stress[2][2] * curved[2][2]
            + 2.0
            * (
                stress[0][1] * curved[0][1]
                + stress[0][2] * curved[0][2]
                + stress[1][2] * curved[1][2]
            )
        )
        rates = [tensors[p - 1, 6 + q] for q in range(5)]
        for i in range(3):
            rates[1 + i] = (
                rates[1 + i]
                - energy * lapse_grad[i]
                + total([held[1 + k] * grad[8 + k][i] for k in range(3)])
            )
        rates[4] = (
            rates[4] + lapse * work * over_chi / shrink - dot(held[1:4], lapse_grad)
        )
        for q in range(5):
            hydro_rate[q, pl.ds(base, half), :] = rates[q]
        density = energy * shrink
        momentum = [held[1 + i] * shrink for i in range(3)]

        lowered = [[[None] * 3 for _ in range(3)] for _ in range(3)]
        for i in range(3):
            for j in range(3):
                for k in range(j, 3):
                    got = 0.5 * (
                        grad[1 + slot_of(i, k)][j]
                        + grad[1 + slot_of(i, j)][k]
                        - grad[1 + slot_of(j, k)][i]
                    )
                    lowered[i][j][k] = lowered[i][k][j] = got
        raised = [[[None] * 3 for _ in range(3)] for _ in range(3)]
        for i in range(3):
            for j in range(3):
                for k in range(j, 3):
                    got = total([inverse[i][l] * lowered[l][j][k] for l in range(3)])
                    raised[i][j][k] = raised[i][k][j] = got
        contracted = [trace_with(inverse, raised[i]) for i in range(3)]

        def hessian_trace(q):
            return (
                inverse[0][0] * seconds[q, 0]
                + inverse[1][1] * seconds[q, 3]
                + inverse[2][2] * seconds[q, 5]
                + 2.0 * (inverse[0][2] * seconds[q, 2] + inverse[1][2] * seconds[q, 4])
            )

        def second_cov(q, slope):
            bent = [total([raised[k][i][j] * slope[k] for k in range(3)]) for i, j in INDEX_PAIRS]
            return symmetric(
                [-bent[s] if s == 1 else seconds[q, s] - bent[s] for s in range(len(bent))]
            )

        chi_cov = second_cov(0, chi_grad)
        chi_lap = trace_with(inverse, chi_cov)
        raised_chi = [dot(inverse[i], chi_grad) for i in range(3)]
        chi_square = dot(raised_chi, chi_grad)
        cross_term = dot(raised_chi, lapse_grad)
        half_chi = 0.5 * over_chi
        plain_cov = second_cov(7, lapse_grad)
        lapse_cov = symmetric(
            [
                plain_cov[i][j]
                + (
                    chi_grad[i] * lapse_grad[j]
                    + chi_grad[j] * lapse_grad[i]
                    - metric[i][j] * cross_term
                )
                * half_chi
                for i, j in INDEX_PAIRS
            ]
        )
        lapse_lap = conformal * trace_with(inverse, lapse_cov)

        mixed = [
            [[dot(inverse[l], lowered[k][j]) for j in range(3)] for k in range(3)]
            for l in range(3)
        ]
        quarter_sq = half_chi * half_chi
        metric_factor = chi_lap * half_chi - 3.0 * chi_square * quarter_sq
        ricci = []
        for i, j in INDEX_PAIRS:
            second_part = -0.5 * hessian_trace(1 + slot_of(i, j))
            connection_part = 0.5 * total(
                [metric[k][i] * grad[18 + k][j] + metric[k][j] * grad[18 + k][i] for k in range(3)]
            )
            contracted_part = 0.5 * total(
                [contracted[k] * (lowered[i][j][k] + lowered[j][i][k]) for k in range(3)]
            )
            if i == j:
                quadratic = total(
                    [
                        raised[k][l][i] * (2.0 * mixed[l][i][k] + mixed[l][k][i])
                        for k in range(3)
                        for l in range(3)
                    ]
                )
            else:
                quadratic = total(
                    [
                        raised[k][l][i] * (mixed[l][j][k] + mixed[l][k][j])
                        + raised[k][l][j] * mixed[l][i][k]
                        for k in range(3)
                        for l in range(3)
                    ]
                )
            conformal_part = (
                chi_cov[i][j] * half_chi
                + metric[i][j] * metric_factor
                - chi_grad[i] * chi_grad[j] * quarter_sq
            )
            ricci.append(
                second_part + connection_part + contracted_part + quadratic + conformal_part
            )
        ricci = symmetric(ricci)
        ricci_scalar = conformal * trace_with(inverse, ricci)
        stress_trace = conformal * trace_with(inverse, stress)

        up_a = [
            [total([inverse[i][k] * traceless[k][j] for k in range(3)]) for j in range(3)]
            for i in range(3)
        ]
        raised_a = symmetric(
            [total([up_a[i][l] * inverse[j][l] for l in range(3)]) for i, j in INDEX_PAIRS]
        )
        a_square = trace_with(traceless, raised_a)
        shift_div = shift_grad[0][0] + shift_grad[1][1] + shift_grad[2][2]
        two_thirds_div = (2.0 / 3.0) * shift_div

        def finish(q, rate):
            rate = rate + dot(shift, grad[q]) + damped[q]
            st_rate[q, pl.ds(base, half), :] = rate

        finish(0, (2.0 / 3.0) * conformal * (lapse * trace_k - shift_div))
        finish(7, -2.0 * lapse * extrinsic)
        for i in range(3):
            finish(8 + i, 0.75 * connection[i] - SHIFT_DAMPING * shift[i])
        finish(
            11,
            lapse
            * (
                a_square
                + trace_k * trace_k * (1.0 / 3.0)
                + FOUR_PI * (stress_trace + density)
                + KAPPA_ONE * theta
            )
            - lapse_lap,
        )
        source = symmetric(
            [
                lapse * (ricci[i][j] - 2.0 * FOUR_PI * stress[i][j]) - lapse_cov[i][j]
                for i, j in INDEX_PAIRS
            ]
        )
        third_trace = trace_with(inverse, source) * (1.0 / 3.0)
        for s, (i, j) in enumerate(INDEX_PAIRS):
            finish(
                1 + s,
                total(
                    [
                        metric[i][k] * shift_grad[j][k] + metric[j][k] * shift_grad[i][k]
                        for k in range(3)
                    ]
                )
                - metric[i][j] * two_thirds_div
                - 2.0 * lapse * traceless[i][j],
            )
            product = total([traceless[i][k] * up_a[k][j] for k in range(3)])
            finish(
                12 + s,
                total(
                    [
                        traceless[i][k] * shift_grad[j][k] + traceless[j][k] * shift_grad[i][k]
                        for k in range(3)
                    ]
                )
                - traceless[i][j] * two_thirds_div
                + conformal * (source[i][j] - metric[i][j] * third_trace)
                + lapse * (trace_k * traceless[i][j] - 2.0 * product),
            )
        for i in range(3):
            bracket = (
                trace_with(raised_a, raised[i])
                - 1.5 * dot(raised_a[i], chi_grad) * over_chi
                - dot(inverse[i], [2.0 * grad[11][j] + grad[21][j] for j in range(3)]) * (1.0 / 3.0)
                - 2.0 * FOUR_PI * dot(inverse[i], momentum)
            )
            spread = [
                seconds[8, 0] + seconds[10, 2],
                seconds[9, 3] + seconds[10, 4],
                seconds[8, 2] + seconds[9, 4] + seconds[10, 5],
            ]
            finish(
                18 + i,
                contracted[i] * two_thirds_div
                - total([contracted[j] * shift_grad[j][i] for j in range(3)])
                + hessian_trace(8 + i)
                + dot(inverse[i], spread) * (1.0 / 3.0)
                - 2.0 * dot(raised_a[i], lapse_grad)
                + 2.0
                * lapse
                * (bracket - KAPPA_ONE * (connection[i] - contracted[i])),
            )
        finish(
            21,
            0.5
            * lapse
            * (
                ricci_scalar
                - a_square
                + (2.0 / 3.0) * trace_k * trace_k
                - 4.0 * FOUR_PI * density
            )
            - 2.0 * KAPPA_ONE * lapse * theta,
        )

    for index in range(own):
        pair_step(index)


def late_kernel(
    cells, zst, zfl, x_below, y_first, x_above, y_second, below_lanes, c_first, c_second, line_two, line_top,
    st_rate, hydro_rate, slopes, electric, st_out, fl_out,
):
    halo = Halo(
        cells, zst, zfl, x_below, y_first, x_above, y_second, below_lanes, c_first, c_second
    )
    x_below, x_above = halo.x_below, halo.x_above
    t, fields, half, own = halo.t, halo.fields, halo.half, halo.own
    inner, span = halo.inner, halo.span

    top = jnp.maximum(line_top[...], line_two[...])
    for lines in (c_first, c_second):
        top = jnp.maximum(top, lines[CORNER_TILES - 1, TOP_ROW : TOP_ROW + 1, :])
    dt = COURANT / top

    for p in inner:
        place = slice((p - 1) * half, p * half)
        mixed = []
        for q in range(CURVED):
            s_m, s_c, s_p = (
                halo.beside(q, n) if 1 <= n <= own else halo.corner(q, n) for n in (p - 1, p, p + 1)
            )
            slope = slopes[q, p - 1]
            slope_side = first_diff(s_m, t.odd_swapped(s_m, s_c), t.odd_swapped(s_c, s_p), s_p)
            mixed.append(
                first_diff(
                    t.y_down(slope, slope_side, 2),
                    t.y_down(slope, slope_side, 1),
                    t.y_up(slope, slope_side, 1),
                    t.y_up(slope, slope_side, 2),
                )
            )
        conformal, lapse = halo.main(0, p), halo.main(7, p)
        metric = [halo.main(1 + s, p) for s in range(6)]
        inverse = inverse_metric(symmetric(metric))
        half_chi = 0.5 / conformal
        cross = inverse[0][1]
        chi_trace = 2.0 * cross * mixed[0] * half_chi
        ricci = [metric[s] * chi_trace - cross * mixed[1 + s] for s in range(6)]
        ricci[1] = ricci[1] + mixed[0] * half_chi
        source = [lapse * r for r in ricci]
        source[1] = source[1] - mixed[7]
        third_trace = trace_with(inverse, symmetric(source)) * (1.0 / 3.0)
        extra = {
            11: -2.0 * conformal * cross * mixed[7],
            21: 0.5 * lapse * conformal * trace_with(inverse, symmetric(ricci)),
        }
        for s in range(6):
            extra[12 + s] = conformal * (source[s] - metric[s] * third_trace)
        for i in range(3):
            extra[18 + i] = 2.0 * cross * mixed[8 + i] + (1.0 / 3.0) * (
                inverse[i][0] * mixed[9] + inverse[i][1] * mixed[8]
            )
        for q in range(fields):
            rate = st_rate[q, place, :]
            if q in extra:
                rate = rate + extra[q]
            st_out[q, place, :] = halo.main(q, p) + dt * rate

    end = own + 1
    ends = (0, end)
    bx_face, by_face, bz_face = ({p: halo.corner(fields + 5 + i, p) for p in ends} for i in range(3))
    layers = {p: halo.corner_layers(p) for p in ends}
    bx_face[end] = layers[end]
    by_face[0] = jnp.where(t.slot < 2, layers[0], by_face[0])
    centred = [{}, {}, {}]
    for p in ends:
        following = halo.beside(fields + 5, 1) if p == 0 else bx_face[p]
        edge_cells = x_below if p == 0 else x_above
        dx = 0.5 * (t.odd_swapped(bx_face[p], following) - bx_face[p])
        dy = 0.5 * (t.y_up(by_face[p], edge_cells[fields + 6], 1) - by_face[p])
        centred[0][p] = bx_face[p] + dx
        centred[1][p] = by_face[p] + dy
        centred[2][p] = bz_face[p] - (dx + dy)
    corners = [{p: halo.corner(q, p) for p in ends} for q in [0, 7] + list(range(fields, fields + 5))]
    found = primitives(
        half, [(0, p) for p in ends], [[c] for c in corners[2:]], [[c] for c in centred],
        [corners[0]], [corners[1]], 2,
    )
    ez_h = [found[0, 0][10]] + [electric[own + p] for p in inner] + [found[0, end][10]]
    ez_x_h = [None] + [ez_h[p] + t.odd_swapped(ez_h[p - 1], ez_h[p]) for p in span[1:]]
    ez_x = [None] + [electric[p - 1] for p in span[1:]]
    edge_z = [None] + [ez_x[p] + t.y_down(ez_x[p], ez_x_h[p], 1) for p in span[1:]]
    quarter = 0.25 * dt
    for p in inner:
        place = slice((p - 1) * half, p * half)
        edge_z_h = ez_x_h[p] + t.y_down(ez_x_h[p], ez_x[p], 1)
        for q in range(5):
            fl_out[q, place, :] = halo.main(fields + q, p) + dt * hydro_rate[q, place, :]
        x_rate = hydro_rate[5, place, :] - (t.y_up(edge_z[p], edge_z_h, 1) - edge_z[p])
        y_rate = hydro_rate[6, place, :] + (t.odd(edge_z[p], edge_z[p + 1]) - edge_z[p])
        z_rate = hydro_rate[7, place, :]
        for i, rate in enumerate((x_rate, y_rate, z_rate)):
            fl_out[5 + i, place, :] = halo.main(fields + 5 + i, p) + quarter * rate


def per_device(spacetime, fluid):
    fields, cx, cy, cz = spacetime.shape
    rows = cx * cy
    st = spacetime.reshape(fields, rows, cz)
    fl = fluid.reshape(FLUID, rows, cz)
    sizes = [lax.axis_size(a) for a in ("gx", "gy", "gz")]
    tile = (2 * cy, cz)
    f32 = jnp.float32

    def shape(*dims):
        return jax.ShapeDtypeStruct(dims, f32)

    def beyond(cells):
        n = sizes[2]
        after = lax.ppermute(cells, "gz", [((i + 1) % n, i) for i in range(n)])
        if n == 2:
            return after
        before = lax.ppermute(cells, "gz", [(i, (i + 1) % n) for i in range(n)])
        lane = lax.broadcasted_iota(jnp.int32, cells.shape, 2)
        return jnp.where(lane < cz // 2, after, before)

    def beyond_lanes(packed):
        n = sizes[2]
        after = lax.ppermute(packed, "gz", [((i + 1) % n, i) for i in range(n)])
        if n == 2:
            return after
        before = lax.ppermute(packed, "gz", [(i, (i + 1) % n) for i in range(n)])
        lane = lax.broadcasted_iota(jnp.int32, packed.shape, 2)
        return jnp.where(lane % 4 < 2, before, after)

    params = pltpu.CompilerParams(vmem_limit_bytes=48 * 1024 * 1024)
    zst, zfl = beyond(st), beyond(fl)
    cells = jnp.concatenate([st, fl], axis=0)
    face = shape(face_tiles(fields), *tile)
    corner = shape(CORNER_TILES, *tile)
    lane_row = shape(1, cz)
    def call(kernel, outs, name, operands, scratch=()):
        return pl.pallas_call(
            kernel,
            out_shape=outs,
            scratch_shapes=scratch,
            compiler_params=params,
            name=name,
        )(*operands)

    def shift(cells, step):
        n = lax.axis_size("gx")
        return lax.ppermute(cells, "gx", [(i, (i + step) % n) for i in range(n)])

    def trade(cells, first):
        axis = "gy"
        n = lax.axis_size(axis)
        step = [1, -1] if first else [-1, 1]
        return lax.ppermute(cells, axis, [(i, (i + step[i % 2]) % n) for i in range(n)])

    def two_away(cells, axis):
        n = lax.axis_size(axis)
        return lax.ppermute(cells, axis, [(i, (i + 2) % n) for i in range(n)]) if n == 4 else cells

    short = sizes[0] <= 4 and sizes[1] <= 4 and sizes[2] <= 2
    x_high = call(pack_up_kernel, face, "pack_up", (cells,))
    x_below = shift(x_high, 1)
    x_low, y_first, y_second, top = call(
        pack_kernel, [face, face, face, shape(TOP_TILES, *tile)], "pack", (cells, zst, zfl)
    )
    below_lanes = beyond_lanes(call(lanes_kernel, shape(1, *tile), "lanes", (x_below,)))
    y_first = trade(y_first, True)
    x_above = shift(x_low, -1)
    y_second = trade(y_second, False)
    top_two = two_away(top, "gx")
    c_first, c_second, line_top = call(
        relay_kernel,
        [corner, corner, lane_row],
        "relay",
        (x_below, below_lanes, x_above, top, top_two),
    )
    c_first = trade(c_first, True)
    c_second = trade(c_second, False)
    if short:
        line_two = two_away(line_top, "gy")
    else:
        line_two = lax.pmax(line_top, ("gx", "gy", "gz"))
    own = cx // 2
    arrived = (cells, zst, zfl, x_below, y_first, x_above, y_second, below_lanes)
    early = call(
        early_kernel,
        [
            shape(*st.shape),
            shape(FLUID, rows, cz),
            shape(CURVED, own, *tile),
            shape(2 * own + 1, *tile),
        ],
        "early",
        arrived,
        [
            pltpu.VMEM((fields, own + 4) + tile, f32),
            pltpu.VMEM((fields, own) + tile, f32),
            pltpu.VMEM((fields, own) + tile, f32),
            pltpu.VMEM((CURVED, own + 2) + tile, f32),
            pltpu.VMEM((CURVED, own) + tile, f32),
            pltpu.VMEM((fields, 3) + tile, f32),
            pltpu.VMEM((CURVED, 6) + tile, f32),
            pltpu.VMEM((fields,) + tile, f32),
            pltpu.VMEM((own, 11) + tile, f32),
        ],
    )
    st_next, fl_next = call(
        late_kernel,
        [shape(*st.shape), shape(*fl.shape)],
        "late",
        (*arrived, c_first, c_second, line_two, line_top, *early),
    )
    return st_next.reshape(spacetime.shape), fl_next.reshape(fluid.shape)


def solution(mesh):
    spec = P(None, "gx", "gy", "gz")
    return jax.shard_map(
        per_device, mesh=mesh, in_specs=(spec, spec), out_specs=(spec, spec), check_vma=False
    )
```

```python
import functools
import math

import jax
import jax.numpy as jnp
from jax import lax
from jax.experimental import pallas as pl
from jax.experimental.pallas import tpu as pltpu
from jax.sharding import PartitionSpec as P

RECOVERY_STEPS = 4
INDEX_PAIRS = ((0, 0), (0, 1), (0, 2), (1, 1), (1, 2), (2, 2))
COURANT = 0.25
DISSIPATION = 0.2
KAPPA_ONE = 0.02
SHIFT_DAMPING = 1.0
SPEED_CAP = 0.99
PRESSURE_FLOOR = 0.01
FOUR_PI = 4.0 * math.pi

BATCH = 6
CURVED = 11
FLUID = 8


def total(pieces):
    summed = pieces[0]
    for member in pieces[1:]:
        summed = summed + member
    return summed


def dot(first_vec, second_vec):
    return total([first_vec[i] * second_vec[i] for i in range(3)])


def slot_of(i, j):
    return INDEX_PAIRS.index((min(i, j), max(i, j)))


def symmetric(entries):
    return [[entries[slot_of(i, j)] for j in range(3)] for i in range(3)]


def trace_with(inverse, tensor):
    return (
        inverse[0][0] * tensor[0][0]
        + inverse[1][1] * tensor[1][1]
        + inverse[2][2] * tensor[2][2]
        + 2.0
        * (
            inverse[0][1] * tensor[0][1]
            + inverse[0][2] * tensor[0][2]
            + inverse[1][2] * tensor[1][2]
        )
    )


def inverse_metric(metric):
    cofactor = [
        metric[1][1] * metric[2][2] - metric[1][2] * metric[1][2],
        metric[0][2] * metric[1][2] - metric[0][1] * metric[2][2],
        metric[0][1] * metric[1][2] - metric[0][2] * metric[1][1],
        metric[0][0] * metric[2][2] - metric[0][2] * metric[0][2],
        metric[0][1] * metric[0][2] - metric[0][0] * metric[1][2],
        metric[0][0] * metric[1][1] - metric[0][1] * metric[0][1],
    ]
    determinant = (
        metric[0][0] * cofactor[0] + metric[0][1] * cofactor[1] + metric[0][2] * cofactor[2]
    )
    over = 1.0 / determinant
    return symmetric([c * over for c in cofactor])


class Tile:
    def __init__(self, cy, cz):
        self.cy, self.rows, self.lanes = cy, 2 * cy, cz
        shape = (self.rows, cz)
        self.row = lax.broadcasted_iota(jnp.int32, shape, 0)
        self.lane = lax.broadcasted_iota(jnp.int32, shape, 1)
        self.slot = lax.rem(self.row, cy)

    def turn(self, tile, amount):
        amount = amount % self.rows
        return tile if amount == 0 else pltpu.roll(tile, amount, 0)

    def spin(self, tile, amount):
        amount = amount % self.lanes
        return tile if amount == 0 else pltpu.roll(tile, amount, 1)

    def swap(self, tile):
        return self.turn(tile, self.cy)

    def odd(self, a, b):
        return self.turn(jnp.where(self.row < self.cy, b, a), self.cy)

    def odd_swapped(self, a, b):
        return self.turn(jnp.where(self.row < self.cy, a, b), self.cy)

    def y_up(self, main, beyond, k):
        return self.turn(jnp.where(self.slot < k, beyond, main), -k)

    def y_down(self, main, beyond, k):
        return self.turn(jnp.where(self.slot >= self.cy - k, beyond, main), k)

    def z_up(self, main, beyond, k):
        return self.spin(jnp.where(self.lane < k, beyond, main), -k)

    def z_down(self, main, beyond, k):
        return self.spin(jnp.where(self.lane >= self.lanes - k, beyond, main), k)

    def corner_rows(self, side, turn):
        places = ((0, 2), (self.cy - 1, self.cy + 1))[side]
        first, second = [(place + turn) % self.rows for place in places]
        return (self.row == first) | (self.row == second)

    def join_low(self, u, v):
        return jnp.where(self.slot < 2, self.swap(u), self.turn(v, 2))

    def join_high(self, u, v):
        return jnp.where(self.slot >= self.cy - 2, self.swap(u), self.turn(self.swap(v), -2))

    def part_first(self, from_above, from_below):
        return jnp.where(self.slot < 2, from_above, from_below)

    def part_second(self, from_above, from_below):
        return self.turn(jnp.where(self.slot < 2, from_below, from_above), 2)


def edge_list(tiles):
    fields = next(n for n in range(tiles) if face_tiles(n) == tiles)
    return list(range(CURVED)) + list(range(fields, fields + FLUID))


CORNER_TURNS = (0, 1, 4, 5)
TOP_TILES = 2
CORNER_TILES = CURVED + FLUID // 4 + 1
TOP_ROW = 6


def face_tiles(fields):
    return fields + FLUID + len(pairs_of(third_list(fields))) + 1


def third_list(fields):
    return list(range(fields + 1))


def pairs_of(items):
    return [(items[i], items[min(i + 1, len(items) - 1)]) for i in range(0, len(items), 2)]


def top_speed(st):
    inverse = inverse_metric(symmetric([st[1 + s] for s in range(6)]))
    scale = 2.0 * st[7] * st[0]
    speeds = [jnp.abs(st[8 + d]) + jnp.sqrt(scale * inverse[d][d]) for d in range(3)]
    top = jnp.maximum(jnp.maximum(speeds[0], speeds[1]), speeds[2])
    return jnp.max(jnp.max(top, axis=1, keepdims=True), axis=0, keepdims=True)


class Chosen:
    def __init__(self, first, second, swapped):
        self.first, self.second, self.swapped, self.shape = first, second, swapped, first.shape

    def __getitem__(self, key):
        return jnp.where(self.swapped, self.second[key], self.first[key])


class Sent:
    def __init__(self, first, second, swapped):
        self.first, self.second, self.swapped = first, second, swapped

    def put(self, key, lower, upper):
        if self.first is not None:
            self.first[key] = jnp.where(self.swapped, upper, lower)
        if self.second is not None:
            self.second[key] = jnp.where(self.swapped, lower, upper)


class Joined:
    def __init__(self, tiles, tail):
        self.tiles, self.tail = tiles, tail
        self.shape = tuple(tiles.shape)

    def __getitem__(self, key):
        q, rows = (key[0], key[1:]) if isinstance(key, tuple) else (key, ())
        if q == self.tiles.shape[0] - 1:
            return self.tail[(0,) + rows]
        return self.tiles[(q,) + rows]


def even_along_y(tile):
    return jnp.full(tile, lax.rem(lax.axis_index("gy"), 2), jnp.int32) == 0


def pack_up_kernel(cells, x_high):
    count, rows, lanes = cells.shape
    fields, half = count - FLUID, rows // 2
    t = Tile(rows // 4, lanes)
    for q in range(count):
        x_high[q] = cells[q, half:rows, :]
    for n, (a, b) in enumerate(pairs_of(list(range(fields)) + [fields + 5])):
        x_high[count + n] = jnp.where(
            t.row < t.cy, t.swap(cells[b, 0:half, :]), cells[a, 0:half, :]
        )
    x_high[x_high.shape[0] - 1] = jnp.broadcast_to(top_speed(cells), t.row.shape)


def lanes_kernel(x_below, out):
    t = Tile(x_below.shape[1] // 2, x_below.shape[2])
    last = x_below.shape[0] - 1
    packed = x_below[last]
    for place, q in enumerate(edge_list(x_below.shape[0])):
        piece = t.spin(x_below[q], 4 * place + 2)
        here = (t.lane >= 4 * place) & (t.lane < 4 * place + 4)
        packed = jnp.where(here, piece, packed)
    out[0] = packed


def pack_kernel(cells, zst, zfl, x_low, y_first, top_out):
    top = jnp.maximum(top_speed(cells), top_speed(zst))
    top_out[...] = jnp.broadcast_to(top, top_out.shape)
    pack(cells, zst, zfl, top, x_low, y_first, None)


def pack_second_kernel(cells, zst, zfl, top, top_two, y_second):
    top = jnp.maximum(top[0, 0:1, :], top_two[0, 0:1, :])
    pack(cells, zst, zfl, top, None, None, y_second)


def pack(cells, zst, zfl, top, x_low, y_first, y_second):
    fields, rows, lanes = zst.shape
    st, fl = cells.at[0:fields], cells.at[fields : fields + FLUID]
    cy = rows // 4
    t = Tile(cy, lanes)
    half = t.rows
    to_y = Sent(y_first, y_second, even_along_y((half, lanes)))

    def own(ref, q):
        return [ref[q, 0:half, :], ref[q, half : 2 * half, :]]

    tiles, beyond = [], []
    for q in range(fields):
        tiles.append(own(st, q))
        beyond.append(own(zst, q) if q < CURVED else None)
    for q in range(FLUID):
        tiles.append(own(fl, q))
        beyond.append(own(zfl, q))

    packed = [None] * 4
    place_count = 0
    for q, (first, second) in enumerate(tiles):
        if x_low is not None:
            x_low[q] = first
        to_y.put(q, t.join_low(first, second), t.join_high(first, second))
        if beyond[q] is not None:
            zf, zs = beyond[q]
            for m, piece in enumerate((zf, zs, t.join_low(zf, zs), t.join_high(zf, zs))):
                piece = t.spin(piece, 4 * place_count + 2)
                packed[m] = (
                    piece if place_count == 0 else jnp.where(t.lane < 4 * place_count, packed[m], piece)
                )
            place_count += 1
    for n, (a, b) in enumerate(pairs_of(third_list(fields))):
        slot = fields + FLUID + n
        xa, xb = (tiles[q if q < fields else fields + 5] for q in (a, b))
        if x_low is not None:
            x_low[slot] = jnp.where(t.row < cy, xa[1], t.swap(xb[1]))
        ya, yb = (tiles[q if q < fields else fields + 6] for q in (a, b))
        w = [t.swap(ya[0]), t.swap(ya[1]), t.swap(yb[0]), t.swap(yb[1])]
        s = t.slot
        low = jnp.where(s == 0, t.turn(w[2], -2), t.turn(w[3], -1))
        low = jnp.where(s == 2, w[0], jnp.where(s == 3, t.turn(w[1], 1), low))
        high = jnp.where(s == 3, t.turn(w[2], 2), t.turn(w[3], 1))
        high = jnp.where(s == 1, w[0], jnp.where(s == 0, t.turn(w[1], -1), high))
        to_y.put(slot, low, high)
    last = (y_second if x_low is None else x_low).shape[0] - 1
    x_lanes = [jnp.where(t.lane < 4 * place_count, piece, top) for piece in packed[:2]]
    y_lanes = [jnp.where(t.lane < 4 * place_count, piece, top) for piece in packed[2:]]
    if x_low is not None:
        x_low[last] = x_lanes[0]
    to_y.put(last, *y_lanes)


def relay_kernel(x_below, below_lanes, x_above, top, top_two, c_first, c_second, line_top):
    cy, lanes = x_below.shape[1] // 2, x_below.shape[2]
    t = Tile(cy, lanes)
    to_y = Sent(c_first, c_second, even_along_y((t.rows, lanes)))
    last = x_below.shape[0] - 1
    line = jnp.maximum(top[0, 0:1, :], top_two[0, 0:1, :])
    line = jnp.maximum(line, x_below[last, 0:1, lanes - 1 : lanes])
    x_below = Joined(x_below, below_lanes)
    for beside in (x_below, x_above):
        line = jnp.maximum(line, beside[last, 0:1, lanes - 1 : lanes])
    line_top[...] = line
    edge = edge_list(x_below.shape[0])
    for q in range(CURVED):
        below, above = x_below[q], x_above[q]
        to_y.put(q, t.join_low(below, above), t.join_high(below, above))
    for n in range(0, FLUID, 4):
        low, high = None, None
        for turn, q in zip(CORNER_TURNS, edge[CURVED + n : CURVED + n + 4]):
            below, above = x_below[q], x_above[q]
            below, above = (t.turn(j(below, above), turn) for j in (t.join_low, t.join_high))
            if low is None:
                low, high = below, above
            else:
                low = jnp.where(t.corner_rows(0, turn), below, low)
                high = jnp.where(t.corner_rows(1, turn), above, high)
        to_y.put(CURVED + n // 4, low, high)
    along_x, along_y = edge[CURVED + 5], edge[CURVED + 6]
    low = t.join_low(x_below[along_y], x_above[along_y])
    high = t.join_high(x_below[along_x], x_above[along_x])
    low, high = (jnp.where(t.row == TOP_ROW, line, tile) for tile in (low, high))
    to_y.put(CORNER_TILES - 1, low, high)


def limited(a, b):
    return jnp.maximum(jnp.minimum(a, b), 0.0) + jnp.minimum(jnp.maximum(a, b), 0.0)


def recover(conserved, magnetic):
    density = conserved[0]
    momenta = conserved[1:4]
    energy = conserved[4] + density
    mom_sq = dot(momenta, momenta)
    mag_sq = dot(magnetic, magnetic)
    cross = dot(momenta, magnetic)
    cross_sq = cross * cross

    def state(z):
        grown = z + mag_sq
        over = 1.0 / (z * grown)
        speed_sq = (mom_sq * z * z + cross_sq * (2.0 * z + mag_sq)) * over * over
        kept = 1.0 - jnp.minimum(speed_sq, SPEED_CAP)
        rest = density * jnp.sqrt(kept)
        return kept, rest, 0.5 * (z * kept - rest), grown * over

    z = jnp.maximum(energy - 0.5 * mag_sq, density)
    for _ in range(RECOVERY_STEPS):
        kept, rest, pressure, over_z = state(z)
        residual = (
            z
            + mag_sq
            - pressure
            - 0.5 * mag_sq * kept
            - 0.5 * cross_sq * over_z * over_z
            - energy
        )
        z = jnp.maximum(z - residual / (1.0 - 0.5 * kept), density)
    kept, rest, pressure, over_z = state(z)
    pressure = jnp.maximum(pressure, PRESSURE_FLOOR * rest)
    scale = lax.rsqrt(kept) / (z + mag_sq)
    along = cross * over_z
    four_vel = [scale * (momenta[i] + along * magnetic[i]) for i in range(3)]
    return [rest, pressure] + four_vel


def stress_parts(rest, pressure, u, magnetic):
    lorentz_sq = 1.0 + dot(u, u)
    over = lax.rsqrt(lorentz_sq)
    over_sq = over * over
    time_b = dot(u, magnetic)
    grown_b = [magnetic[i] + time_b * u[i] for i in range(3)]
    b_square = (dot(magnetic, magnetic) + time_b * time_b) * over_sq
    enthalpy = rest + 2.0 * pressure
    inertia = enthalpy + b_square
    return lorentz_sq, over, over_sq, time_b, grown_b, b_square, enthalpy, inertia


def face_state(rest, pressure, u, magnetic, d):
    lorentz_sq, over, over_sq, time_b, grown_b, b_square, enthalpy, inertia = stress_parts(
        rest, pressure, u, magnetic
    )
    total_pressure = pressure + 0.5 * b_square
    lorentz = lorentz_sq * over
    density = rest * lorentz
    carried = inertia * lorentz
    time_over = time_b * over
    conserved = [density]
    conserved += [carried * u[j] - time_over * grown_b[j] for j in range(3)]
    conserved += [inertia * lorentz_sq - total_pressure - time_b * time_b - density]
    mass_flux = rest * u[d]
    flux = [mass_flux]
    pushed = inertia * u[d]
    b_over = grown_b[d] * over_sq
    for j in range(3):
        flux_j = pushed * u[j] - b_over * grown_b[j]
        flux.append(flux_j + total_pressure if j == d else flux_j)
    flux.append(carried * u[d] - time_over * grown_b[d] - mass_flux)
    ratio = 1.0 / (enthalpy * inertia)
    sound_sq = 2.0 * pressure * inertia * ratio
    alfven_sq = b_square * enthalpy * ratio
    fast_sq = sound_sq + alfven_sq - sound_sq * alfven_sq
    slow = 1.0 - fast_sq
    velocity = u[d] * over
    rest_part = 1.0 - dot(u, u) * over_sq * fast_sq
    spread = jnp.sqrt(fast_sq * over_sq * (rest_part - velocity * velocity * slow))
    fastest = (jnp.abs(velocity * slow) + spread) / rest_part
    return conserved, flux, fastest


def face_flux(left, right, normal, weight, d):
    sides = []
    for state in (left, right):
        magnetic = [normal if i == d else state[5 + i] for i in range(3)]
        sides.append(face_state(state[0], state[1], state[2:5], magnetic, d))
    (cons_l, flux_l, fast_l), (cons_r, flux_r, fast_r) = sides
    signal = jnp.maximum(fast_l, fast_r)
    scale = 0.5 * weight
    return [scale * (flux_l[q] + flux_r[q] - signal * (cons_r[q] - cons_l[q])) for q in range(5)]


def volume_over(conformal):
    return conformal * jnp.sqrt(conformal)


def first_diff(down_two, down, up, up_two):
    return (8.0 / 12.0) * (up - down) + (1.0 / 12.0) * (down_two - up_two)


class Halo:
    def __init__(self, cells, zst, zfl, x_below, y_first, x_above, y_second, below_lanes, *corners):
        x_below = Joined(x_below, below_lanes)
        self.fields, self.block, self.lanes = zst.shape
        even_y = even_along_y((self.block // 2, self.lanes))
        y_below, y_above = Chosen(y_first, y_second, even_y), Chosen(y_second, y_first, even_y)
        if corners:
            c_first, c_second = corners
            self.c_below = Chosen(c_first, c_second, even_y)
            self.c_above = Chosen(c_second, c_first, even_y)
        self.st = cells.at[0 : self.fields]
        self.fl = cells.at[self.fields : self.fields + FLUID]
        self.zst, self.zfl = zst, zfl
        self.x_below, self.x_above = x_below, x_above
        self.y_below, self.y_above = y_below, y_above
        self.cy = self.block // 4
        self.t = Tile(self.cy, self.lanes)
        self.half = self.t.rows
        self.own = self.block // self.half
        self.inner = range(1, self.own + 1)
        self.span = range(self.own + 2)
        self.edge = edge_list(x_below.shape[0])
        self.last = x_below.shape[0] - 1

    def rows_of(self, ref, q, p):
        return ref[q, (p - 1) * self.half : p * self.half, :]

    def main(self, q, p):
        if q < self.fields:
            return self.rows_of(self.st, q, p)
        return self.rows_of(self.fl, q - self.fields, p)

    def beyond(self, q, p):
        if q < self.fields:
            return self.rows_of(self.zst, q, p)
        return self.rows_of(self.zfl, q - self.fields, p)

    def part(self, second):
        return self.t.part_second if second else self.t.part_first

    def beside(self, q, p):
        return self.part(p == 2)(self.y_above[q], self.y_below[q])

    def third_place(self, q):
        return self.fields + FLUID + q // 2, q % 2

    def x_third(self, q, upper):
        tile, which = self.third_place(q)
        found = self.x_above[tile] if upper else self.x_below[tile]
        return self.t.swap(found) if which else found

    def y_third(self, q, p):
        t = self.t
        tile, which = self.third_place(q)
        turn_above, turn_below = ((0, 0), (-1, 1), (2, -2), (1, -1))[2 * which + p - 1]
        above, below = t.turn(self.y_above[tile], turn_above), t.turn(self.y_below[tile], turn_below)
        return jnp.where(t.slot == 2, above, below)

    def z_place(self, q):
        return 4 * self.edge.index(q) + 2

    def x_beyond(self, q, upper):
        tile = self.x_above[self.last] if upper else self.x_below[self.last]
        return self.t.spin(tile, -self.z_place(q))

    def y_beyond(self, q, p):
        return self.t.spin(self.beside(self.last, p), -self.z_place(q))

    def corner(self, q, p):
        place, turn = q, 0
        if q >= CURVED:
            n = q - self.fields
            place, turn = CURVED + n // 4, CORNER_TURNS[n % 4]
        above, below = self.t.turn(self.c_above[place], -turn), self.t.turn(self.c_below[place], -turn)
        return self.part(p > 0)(above, below)

    def corner_layers(self, p):
        place = CORNER_TILES - 1
        return self.part(p > 0)(self.c_above[place], self.c_below[place])

    def plane(self, q):
        inner = self.inner
        return (
            [self.x_below[q]] + [self.main(q, p) for p in inner] + [self.x_above[q]],
            [None] + [self.beside(q, p) for p in inner] + [None],
            [self.x_beyond(q, False)]
            + [self.beyond(q, p) for p in inner]
            + [self.x_beyond(q, True)],
            [None] + [self.y_beyond(q, p) for p in inner] + [None],
        )


def weigh(chi_face, alpha_face):
    shrink = volume_over(chi_face)
    return shrink, alpha_face / shrink


def primitives(half, spots, cons, centred, chi, alpha, batch):
    found = {}
    for start in range(0, len(spots), batch):
        group = spots[start : start + batch]

        def gather(planes):
            return jnp.concatenate([planes[k][p] for k, p in group], axis=0)

        shrink = volume_over(gather(chi))
        mag_raw = [gather(centred[i]) for i in range(3)]
        mag = [m * shrink for m in mag_raw]
        values = recover([gather(c) * shrink for c in cons], mag)
        u = values[2:5]
        factor = gather(alpha) * lax.rsqrt(1.0 + dot(u, u))
        field = [
            factor * (u[(i + 2) % 3] * mag_raw[(i + 1) % 3] - u[(i + 1) % 3] * mag_raw[(i + 2) % 3])
            for i in range(3)
        ]
        for n, spot in enumerate(group):
            found[spot] = [value[n * half : (n + 1) * half] for value in values + mag + field]
    return found


def ring_fluxes(prims, chi, alpha, normals, d, up, down):
    found = []
    for here, there in ((0, 1), (1, 0)):
        left, right = [], []
        for a, b in zip(prims[here], prims[there]):
            below = down(a, b, 1)
            middle = a - below
            left.append(below + 0.5 * limited(below - down(a, b, 2), middle))
            right.append(a - 0.5 * limited(middle, up(a, b, 1) - a))
        shrink, weight = weigh(
            0.5 * (chi[here] + down(chi[here], chi[there], 1)),
            0.5 * (alpha[here] + down(alpha[here], alpha[there], 1)),
        )
        found.append(face_flux(left, right, normals[here] * shrink, weight, d))
    return [a - up(a, b, 1) for a, b in zip(*found)]


def early_kernel(
    cells, zst, zfl, x_below, y_first, x_above, y_second, below_lanes,
    st_rate, hydro_rate, slopes, electric, pairs, sides, thirds, pairs_z, sides_z, grads, seconds, damped, tensors,
):
    halo = Halo(cells, zst, zfl, x_below, y_first, x_above, y_second, below_lanes)
    t, fields, half, own, cy = halo.t, halo.fields, halo.half, halo.own, halo.cy
    st, fl, inner = halo.st, halo.fl, halo.inner

    for q in range(fields):
        pairs[q, 0] = halo.x_third(q, False)
        pairs[q, 1] = x_below[q]
        for p in inner:
            pairs[q, 1 + p] = halo.main(q, p)
            sides[q, p - 1] = halo.beside(q, p)
            thirds[q, p - 1] = halo.y_third(q, p)
        pairs[q, 2 + own] = x_above[q]
        pairs[q, 3 + own] = halo.x_third(q, True)
        if q < CURVED:
            pairs_z[q, 0] = halo.x_beyond(q, False)
            pairs_z[q, own + 1] = halo.x_beyond(q, True)
            for p in inner:
                pairs_z[q, p] = halo.beyond(q, p)
                sides_z[q, p - 1] = halo.y_beyond(q, p)

    span = halo.span
    face = [halo.plane(fields + 5 + i) for i in range(3)]

    def halves(kind, p):
        own_x, own_y, own_z = (f[kind][p] for f in face)
        pair = kind in (0, 2)
        known_x = pair or p < own
        last = kind == 0 and p == own + 1
        if pair:
            next_x = halo.x_third(fields, True) if last else face[0][kind][min(p + 1, own + 1)]
            next_x = t.odd(own_x, next_x)
        else:
            next_x = t.odd_swapped(own_x, face[0][kind][p + 1] if known_x else own_x)
        dx = 0.5 * (next_x - own_x)
        dz = 0.5 * (t.z_up(own_z, face[2][kind ^ 2][p], 1) - own_z)
        inside = 1 <= p <= own
        if not pair:
            here = jnp.where(t.slot == 2, halo.y_third(fields, p), own_y) if kind == 1 else own_y
            next_y = t.y_up(here, face[1][kind ^ 1][p], 1)
        else:
            next_y = t.y_up(own_y, face[1][kind ^ 1][p] if inside else own_y, 1)
        dy = 0.5 * (next_y - own_y)
        if pair and not inside:
            dy = jnp.where(t.slot == cy - 1, -(dx + dz), dy)
        if not pair and not known_x:
            dx = jnp.where(t.row < cy, -(dy + dz), dx)
        return own_x + dx, own_y + dy, own_z + dz

    spots = [(0, p) for p in span] + [(1, p) for p in inner]
    spots += [(2, p) for p in span] + [(3, p) for p in inner]
    centred = [[[None] * (own + 2) for _ in range(4)] for _ in range(3)]
    for k, p in spots:
        for i, value in enumerate(halves(k, p)):
            centred[i][k][p] = value
    chi, alpha = halo.plane(0), halo.plane(7)
    found = primitives(
        half, spots, [halo.plane(fields + q) for q in range(5)], centred, chi, alpha, BATCH
    )

    lines = [[found[0, p][i] for p in span] for i in range(8)] + [chi[0], alpha[0]]
    odd_lines = [[t.odd(f[p], f[min(p + 1, own + 1)]) for p in span] for f in lines]
    fluxes = [None]
    for p in range(1, own + 2):
        left, right = [], []
        for f, o in zip(lines[:8], odd_lines):
            here = f[p] - o[p - 1]
            left.append(o[p - 1] + 0.5 * limited(o[p - 1] - f[p - 1], here))
            right.append(f[p] - 0.5 * limited(here, o[p] - f[p]))
        shrink, weight = weigh(
            0.5 * (lines[8][p] + odd_lines[8][p - 1]), 0.5 * (lines[9][p] + odd_lines[9][p - 1])
        )
        fluxes.append(face_flux(left, right, face[0][0][p] * shrink, weight, 0))
    for p in inner:
        changes = [
            ring_fluxes(
                [found[k, p][:8] for k in (0, kind)],
                [chi[k][p] for k in (0, kind)],
                [alpha[k][p] for k in (0, kind)],
                [face[d][k][p] for k in (0, kind)],
                d,
                up,
                down,
            )
            for d, kind, up, down in ((1, 1, t.y_up, t.y_down), (2, 2, t.z_up, t.z_down))
        ]
        for q in range(5):
            change = fluxes[p][q] - t.odd(fluxes[p][q], fluxes[p + 1][q])
            tensors[p - 1, 6 + q] = change + changes[0][q] + changes[1][q]
        rest, pressure = found[0, p][:2]
        u = found[0, p][2:5]
        parts = stress_parts(rest, pressure, u, found[0, p][5:8])
        lorentz_sq, over, over_sq, time_b, grown_b, b_square, enthalpy, inertia = parts
        total_pressure = pressure + 0.5 * b_square
        for s, (i, j) in enumerate(INDEX_PAIRS):
            value = inertia * u[i] * u[j] - over_sq * (grown_b[i] * grown_b[j])
            tensors[p - 1, s] = value + total_pressure if i == j else value

    ex, ey, ez = (
        [[found[k, p][8 + i] if (k, p) in found else None for p in span] for k in range(4)]
        for i in range(3)
    )
    ey_x = [
        [ey[k][p] + t.odd(ey[k][p - 1], ey[k][p]) if p else None for p in span] for k in (0, 2)
    ]
    edge_y = [None] + [ey_x[0][p] + t.z_down(ey_x[0][p], ey_x[1][p], 1) for p in span[1:]]
    for p in span[1:]:
        electric[p - 1] = ez[0][p] + t.odd(ez[0][p - 1], ez[0][p])
    for p in inner:
        electric[own + p] = ez[1][p]
        edge_y_z = ey_x[1][p] + t.z_down(ey_x[1][p], ey_x[0][p], 1)
        ex_y = ex[0][p] + t.y_down(ex[0][p], ex[1][p], 1)
        ex_y_h = ex[1][p] + t.y_down(ex[1][p], ex[0][p], 1)
        ex_y_z = ex[2][p] + t.y_down(ex[2][p], ex[3][p], 1)
        ex_y_hz = ex[3][p] + t.y_down(ex[3][p], ex[2][p], 1)
        edge_x = ex_y + t.z_down(ex_y, ex_y_z, 1)
        edge_x_h = ex_y_h + t.z_down(ex_y_h, ex_y_hz, 1)
        edge_x_z = ex_y_z + t.z_down(ex_y_z, ex_y, 1)
        place = slice((p - 1) * half, p * half)
        hydro_rate[5, place, :] = t.z_up(edge_y[p], edge_y_z, 1) - edge_y[p]
        hydro_rate[6, place, :] = edge_x - t.z_up(edge_x, edge_x_z, 1)
        hydro_rate[7, place, :] = (t.y_up(edge_x, edge_x_h, 1) - edge_x) - (
            t.odd(edge_y[p], edge_y[p + 1]) - edge_y[p]
        )

    def pair_step(index):
        p = index + 1
        base = index * half

        for q in range(fields):
            centre = pairs[q, p + 1]
            x_m3 = t.odd(pairs[q, p - 1], pairs[q, p])
            x_m2 = pairs[q, p]
            x_m1 = t.odd(pairs[q, p], centre)
            x_p1 = t.odd(centre, pairs[q, p + 2])
            x_p2 = pairs[q, p + 2]
            x_p3 = t.odd(pairs[q, p + 2], pairs[q, p + 3])
            side, third = sides[q, index], thirds[q, index]
            y_m1, y_m2 = t.y_down(centre, side, 1), t.y_down(centre, side, 2)
            y_p1, y_p2 = t.y_up(centre, side, 1), t.y_up(centre, side, 2)
            y_m3 = t.turn(
                jnp.where(t.slot >= cy - 2, side, jnp.where(t.slot == cy - 3, third, centre)), 3
            )
            y_p3 = t.turn(jnp.where(t.slot < 2, side, jnp.where(t.slot == 2, third, centre)), -3)
            beyond = zst[q, pl.ds(base, half), :]
            z_m1, z_m2, z_m3 = (t.z_down(centre, beyond, k) for k in (1, 2, 3))
            z_p1, z_p2, z_p3 = (t.z_up(centre, beyond, k) for k in (1, 2, 3))
            dx = first_diff(x_m2, x_m1, x_p1, x_p2)
            dy = first_diff(y_m2, y_m1, y_p1, y_p2)
            grads[q, 0] = dx
            if q < CURVED:
                slopes[q, index] = dx
            grads[q, 1] = dy
            grads[q, 2] = first_diff(z_m2, z_m1, z_p1, z_p2)
            near = [x_m1 + x_p1, y_m1 + y_p1, z_m1 + z_p1]
            far = [x_m2 + x_p2, y_m2 + y_p2, z_m2 + z_p2]
            outer = (x_m3 + x_p3) + (y_m3 + y_p3) + (z_m3 + z_p3)
            damped[q] = (DISSIPATION / 64.0) * (
                outer - 6.0 * (far[0] + far[1] + far[2]) + 15.0 * (near[0] + near[1] + near[2])
                - 60.0 * centre
            )
            if q < CURVED:
                for s, d in ((0, 0), (3, 1), (5, 2)):
                    seconds[q, s] = (1.0 / 12.0) * (16.0 * near[d] - far[d] - 30.0 * centre)
                b_m, b_c, b_p = pairs_z[q, p - 1], pairs_z[q, p], pairs_z[q, p + 1]
                dx_z = first_diff(b_m, t.odd(b_m, b_c), t.odd(b_c, b_p), b_p)
                b_s = sides_z[q, p - 1]
                dy_z = first_diff(
                    t.y_down(b_c, b_s, 2),
                    t.y_down(b_c, b_s, 1),
                    t.y_up(b_c, b_s, 1),
                    t.y_up(b_c, b_s, 2),
                )
                for s, inside, outside in ((2, dx, dx_z), (4, dy, dy_z)):
                    seconds[q, s] = first_diff(
                        t.z_down(inside, outside, 2),
                        t.z_down(inside, outside, 1),
                        t.z_up(inside, outside, 1),
                        t.z_up(inside, outside, 2),
                    )

        def value(q):
            return pairs[q, p + 1]

        def fluid_value(q):
            return fl[q, pl.ds(base, half), :]

        conformal, lapse = value(0), value(7)
        over_chi = 1.0 / conformal
        metric = symmetric([value(1 + s) for s in range(6)])
        shift = [value(8 + i) for i in range(3)]
        extrinsic, theta = value(11), value(21)
        traceless = symmetric([value(12 + s) for s in range(6)])
        connection = [value(18 + i) for i in range(3)]
        inverse = inverse_metric(metric)
        grad = [[grads[q, k] for k in range(3)] for q in range(fields)]
        chi_grad, lapse_grad = grad[0], grad[7]
        shift_grad = [[grad[8 + i][k] for i in range(3)] for k in range(3)]
        trace_k = extrinsic + 2.0 * theta

        stress = symmetric([tensors[p - 1, s] for s in range(6)])
        held = [fluid_value(q) for q in range(5)]
        shrink = volume_over(conformal)
        energy = held[4] + held[0]
        third_k = trace_k * (1.0 / 3.0)
        curved = [
            [
                (traceless[i][j] + metric[i][j] * third_k) if i <= j else None for j in range(3)
            ]
            for i in range(3)
        ]
        work = (
            stress[0][0] * curved[0][0]
            + stress[1][1] * curved[1][1]
            + stress[2][2] * curved[2][2]
            + 2.0
            * (
                stress[0][1] * curved[0][1]
                + stress[0][2] * curved[0][2]
                + stress[1][2] * curved[1][2]
            )
        )
        rates = [tensors[p - 1, 6 + q] for q in range(5)]
        for i in range(3):
            rates[1 + i] = (
                rates[1 + i]
                - energy * lapse_grad[i]
                + total([held[1 + k] * grad[8 + k][i] for k in range(3)])
            )
        rates[4] = (
            rates[4] + lapse * work * over_chi / shrink - dot(held[1:4], lapse_grad)
        )
        for q in range(5):
            hydro_rate[q, pl.ds(base, half), :] = rates[q]
        density = energy * shrink
        momentum = [held[1 + i] * shrink for i in range(3)]

        lowered = [[[None] * 3 for _ in range(3)] for _ in range(3)]
        for i in range(3):
            for j in range(3):
                for k in range(j, 3):
                    got = 0.5 * (
                        grad[1 + slot_of(i, k)][j]
                        + grad[1 + slot_of(i, j)][k]
                        - grad[1 + slot_of(j, k)][i]
                    )
                    lowered[i][j][k] = lowered[i][k][j] = got
        raised = [[[None] * 3 for _ in range(3)] for _ in range(3)]
        for i in range(3):
            for j in range(3):
                for k in range(j, 3):
                    got = total([inverse[i][l] * lowered[l][j][k] for l in range(3)])
                    raised[i][j][k] = raised[i][k][j] = got
        contracted = [trace_with(inverse, raised[i]) for i in range(3)]

        def hessian_trace(q):
            return (
                inverse[0][0] * seconds[q, 0]
                + inverse[1][1] * seconds[q, 3]
                + inverse[2][2] * seconds[q, 5]
                + 2.0 * (inverse[0][2] * seconds[q, 2] + inverse[1][2] * seconds[q, 4])
            )

        def second_cov(q, slope):
            bent = [total([raised[k][i][j] * slope[k] for k in range(3)]) for i, j in INDEX_PAIRS]
            return symmetric(
                [-bent[s] if s == 1 else seconds[q, s] - bent[s] for s in range(len(bent))]
            )

        chi_cov = second_cov(0, chi_grad)
        chi_lap = trace_with(inverse, chi_cov)
        raised_chi = [dot(inverse[i], chi_grad) for i in range(3)]
        chi_square = dot(raised_chi, chi_grad)
        cross_term = dot(raised_chi, lapse_grad)
        half_chi = 0.5 * over_chi
        plain_cov = second_cov(7, lapse_grad)
        lapse_cov = symmetric(
            [
                plain_cov[i][j]
                + (
                    chi_grad[i] * lapse_grad[j]
                    + chi_grad[j] * lapse_grad[i]
                    - metric[i][j] * cross_term
                )
                * half_chi
                for i, j in INDEX_PAIRS
            ]
        )
        lapse_lap = conformal * trace_with(inverse, lapse_cov)

        mixed = [
            [[dot(inverse[l], lowered[k][j]) for j in range(3)] for k in range(3)]
            for l in range(3)
        ]
        quarter_sq = half_chi * half_chi
        metric_factor = chi_lap * half_chi - 3.0 * chi_square * quarter_sq
        ricci = []
        for i, j in INDEX_PAIRS:
            second_part = -0.5 * hessian_trace(1 + slot_of(i, j))
            connection_part = 0.5 * total(
                [metric[k][i] * grad[18 + k][j] + metric[k][j] * grad[18 + k][i] for k in range(3)]
            )
            contracted_part = 0.5 * total(
                [contracted[k] * (lowered[i][j][k] + lowered[j][i][k]) for k in range(3)]
            )
            if i == j:
                quadratic = total(
                    [
                        raised[k][l][i] * (2.0 * mixed[l][i][k] + mixed[l][k][i])
                        for k in range(3)
                        for l in range(3)
                    ]
                )
            else:
                quadratic = total(
                    [
                        raised[k][l][i] * (mixed[l][j][k] + mixed[l][k][j])
                        + raised[k][l][j] * mixed[l][i][k]
                        for k in range(3)
                        for l in range(3)
                    ]
                )
            conformal_part = (
                chi_cov[i][j] * half_chi
                + metric[i][j] * metric_factor
                - chi_grad[i] * chi_grad[j] * quarter_sq
            )
            ricci.append(
                second_part + connection_part + contracted_part + quadratic + conformal_part
            )
        ricci = symmetric(ricci)
        ricci_scalar = conformal * trace_with(inverse, ricci)
        stress_trace = conformal * trace_with(inverse, stress)

        up_a = [
            [total([inverse[i][k] * traceless[k][j] for k in range(3)]) for j in range(3)]
            for i in range(3)
        ]
        raised_a = symmetric(
            [total([up_a[i][l] * inverse[j][l] for l in range(3)]) for i, j in INDEX_PAIRS]
        )
        a_square = trace_with(traceless, raised_a)
        shift_div = shift_grad[0][0] + shift_grad[1][1] + shift_grad[2][2]
        two_thirds_div = (2.0 / 3.0) * shift_div

        def finish(q, rate):
            rate = rate + dot(shift, grad[q]) + damped[q]
            st_rate[q, pl.ds(base, half), :] = rate

        finish(0, (2.0 / 3.0) * conformal * (lapse * trace_k - shift_div))
        finish(7, -2.0 * lapse * extrinsic)
        for i in range(3):
            finish(8 + i, 0.75 * connection[i] - SHIFT_DAMPING * shift[i])
        finish(
            11,
            lapse
            * (
                a_square
                + trace_k * trace_k * (1.0 / 3.0)
                + FOUR_PI * (stress_trace + density)
                + KAPPA_ONE * theta
            )
            - lapse_lap,
        )
        source = symmetric(
            [
                lapse * (ricci[i][j] - 2.0 * FOUR_PI * stress[i][j]) - lapse_cov[i][j]
                for i, j in INDEX_PAIRS
            ]
        )
        third_trace = trace_with(inverse, source) * (1.0 / 3.0)
        for s, (i, j) in enumerate(INDEX_PAIRS):
            finish(
                1 + s,
                total(
                    [
                        metric[i][k] * shift_grad[j][k] + metric[j][k] * shift_grad[i][k]
                        for k in range(3)
                    ]
                )
                - metric[i][j] * two_thirds_div
                - 2.0 * lapse * traceless[i][j],
            )
            product = total([traceless[i][k] * up_a[k][j] for k in range(3)])
            finish(
                12 + s,
                total(
                    [
                        traceless[i][k] * shift_grad[j][k] + traceless[j][k] * shift_grad[i][k]
                        for k in range(3)
                    ]
                )
                - traceless[i][j] * two_thirds_div
                + conformal * (source[i][j] - metric[i][j] * third_trace)
                + lapse * (trace_k * traceless[i][j] - 2.0 * product),
            )
        for i in range(3):
            bracket = (
                trace_with(raised_a, raised[i])
                - 1.5 * dot(raised_a[i], chi_grad) * over_chi
                - dot(inverse[i], [2.0 * grad[11][j] + grad[21][j] for j in range(3)]) * (1.0 / 3.0)
                - 2.0 * FOUR_PI * dot(inverse[i], momentum)
            )
            spread = [
                seconds[8, 0] + seconds[10, 2],
                seconds[9, 3] + seconds[10, 4],
                seconds[8, 2] + seconds[9, 4] + seconds[10, 5],
            ]
            finish(
                18 + i,
                contracted[i] * two_thirds_div
                - total([contracted[j] * shift_grad[j][i] for j in range(3)])
                + hessian_trace(8 + i)
                + dot(inverse[i], spread) * (1.0 / 3.0)
                - 2.0 * dot(raised_a[i], lapse_grad)
                + 2.0
                * lapse
                * (bracket - KAPPA_ONE * (connection[i] - contracted[i])),
            )
        finish(
            21,
            0.5
            * lapse
            * (
                ricci_scalar
                - a_square
                + (2.0 / 3.0) * trace_k * trace_k
                - 4.0 * FOUR_PI * density
            )
            - 2.0 * KAPPA_ONE * lapse * theta,
        )

    for index in range(own):
        pair_step(index)


def late_kernel(
    cells, zst, zfl, x_below, y_first, x_above, y_second, below_lanes, c_first, c_second, line_two, line_top,
    st_rate, hydro_rate, slopes, electric, st_out, fl_out,
):
    halo = Halo(
        cells, zst, zfl, x_below, y_first, x_above, y_second, below_lanes, c_first, c_second
    )
    x_below, x_above = halo.x_below, halo.x_above
    t, fields, half, own = halo.t, halo.fields, halo.half, halo.own
    inner, span = halo.inner, halo.span

    top = jnp.maximum(line_top[...], line_two[...])
    for lines in (c_first, c_second):
        top = jnp.maximum(top, lines[CORNER_TILES - 1, TOP_ROW : TOP_ROW + 1, :])
    dt = COURANT / top

    for p in inner:
        place = slice((p - 1) * half, p * half)
        mixed = []
        for q in range(CURVED):
            s_m, s_c, s_p = (
                halo.beside(q, n) if 1 <= n <= own else halo.corner(q, n) for n in (p - 1, p, p + 1)
            )
            slope = slopes[q, p - 1]
            slope_side = first_diff(s_m, t.odd_swapped(s_m, s_c), t.odd_swapped(s_c, s_p), s_p)
            mixed.append(
                first_diff(
                    t.y_down(slope, slope_side, 2),
                    t.y_down(slope, slope_side, 1),
                    t.y_up(slope, slope_side, 1),
                    t.y_up(slope, slope_side, 2),
                )
            )
        conformal, lapse = halo.main(0, p), halo.main(7, p)
        metric = [halo.main(1 + s, p) for s in range(6)]
        inverse = inverse_metric(symmetric(metric))
        half_chi = 0.5 / conformal
        cross = inverse[0][1]
        chi_trace = 2.0 * cross * mixed[0] * half_chi
        ricci = [metric[s] * chi_trace - cross * mixed[1 + s] for s in range(6)]
        ricci[1] = ricci[1] + mixed[0] * half_chi
        source = [lapse * r for r in ricci]
        source[1] = source[1] - mixed[7]
        third_trace = trace_with(inverse, symmetric(source)) * (1.0 / 3.0)
        extra = {
            11: -2.0 * conformal * cross * mixed[7],
            21: 0.5 * lapse * conformal * trace_with(inverse, symmetric(ricci)),
        }
        for s in range(6):
            extra[12 + s] = conformal * (source[s] - metric[s] * third_trace)
        for i in range(3):
            extra[18 + i] = 2.0 * cross * mixed[8 + i] + (1.0 / 3.0) * (
                inverse[i][0] * mixed[9] + inverse[i][1] * mixed[8]
            )
        for q in range(fields):
            rate = st_rate[q, place, :]
            if q in extra:
                rate = rate + extra[q]
            st_out[q, place, :] = halo.main(q, p) + dt * rate

    end = own + 1
    ends = (0, end)
    bx_face, by_face, bz_face = ({p: halo.corner(fields + 5 + i, p) for p in ends} for i in range(3))
    layers = {p: halo.corner_layers(p) for p in ends}
    bx_face[end] = layers[end]
    by_face[0] = jnp.where(t.slot < 2, layers[0], by_face[0])
    centred = [{}, {}, {}]
    for p in ends:
        following = halo.beside(fields + 5, 1) if p == 0 else bx_face[p]
        edge_cells = x_below if p == 0 else x_above
        dx = 0.5 * (t.odd_swapped(bx_face[p], following) - bx_face[p])
        dy = 0.5 * (t.y_up(by_face[p], edge_cells[fields + 6], 1) - by_face[p])
        centred[0][p] = bx_face[p] + dx
        centred[1][p] = by_face[p] + dy
        centred[2][p] = bz_face[p] - (dx + dy)
    corners = [{p: halo.corner(q, p) for p in ends} for q in [0, 7] + list(range(fields, fields + 5))]
    found = primitives(
        half, [(0, p) for p in ends], [[c] for c in corners[2:]], [[c] for c in centred],
        [corners[0]], [corners[1]], 2,
    )
    ez_h = [found[0, 0][10]] + [electric[own + p] for p in inner] + [found[0, end][10]]
    ez_x_h = [None] + [ez_h[p] + t.odd_swapped(ez_h[p - 1], ez_h[p]) for p in span[1:]]
    ez_x = [None] + [electric[p - 1] for p in span[1:]]
    edge_z = [None] + [ez_x[p] + t.y_down(ez_x[p], ez_x_h[p], 1) for p in span[1:]]
    quarter = 0.25 * dt
    for p in inner:
        place = slice((p - 1) * half, p * half)
        edge_z_h = ez_x_h[p] + t.y_down(ez_x_h[p], ez_x[p], 1)
        for q in range(5):
            fl_out[q, place, :] = halo.main(fields + q, p) + dt * hydro_rate[q, place, :]
        x_rate = hydro_rate[5, place, :] - (t.y_up(edge_z[p], edge_z_h, 1) - edge_z[p])
        y_rate = hydro_rate[6, place, :] + (t.odd(edge_z[p], edge_z[p + 1]) - edge_z[p])
        z_rate = hydro_rate[7, place, :]
        for i, rate in enumerate((x_rate, y_rate, z_rate)):
            fl_out[5 + i, place, :] = halo.main(fields + 5 + i, p) + quarter * rate


def per_device(spacetime, fluid):
    fields, cx, cy, cz = spacetime.shape
    rows = cx * cy
    st = spacetime.reshape(fields, rows, cz)
    fl = fluid.reshape(FLUID, rows, cz)
    sizes = [lax.axis_size(a) for a in ("gx", "gy", "gz")]
    tile = (2 * cy, cz)
    f32 = jnp.float32

    def shape(*dims):
        return jax.ShapeDtypeStruct(dims, f32)

    def beyond(cells):
        n = sizes[2]
        after = lax.ppermute(cells, "gz", [((i + 1) % n, i) for i in range(n)])
        if n == 2:
            return after
        before = lax.ppermute(cells, "gz", [(i, (i + 1) % n) for i in range(n)])
        lane = lax.broadcasted_iota(jnp.int32, cells.shape, 2)
        return jnp.where(lane < cz // 2, after, before)

    def beyond_lanes(packed):
        n = sizes[2]
        after = lax.ppermute(packed, "gz", [((i + 1) % n, i) for i in range(n)])
        if n == 2:
            return after
        before = lax.ppermute(packed, "gz", [(i, (i + 1) % n) for i in range(n)])
        lane = lax.broadcasted_iota(jnp.int32, packed.shape, 2)
        return jnp.where(lane % 4 < 2, before, after)

    params = pltpu.CompilerParams(vmem_limit_bytes=48 * 1024 * 1024)
    zst, zfl = beyond(st), beyond(fl)
    cells = jnp.concatenate([st, fl], axis=0)
    face = shape(face_tiles(fields), *tile)
    corner = shape(CORNER_TILES, *tile)
    lane_row = shape(1, cz)
    def call(kernel, outs, name, operands, scratch=()):
        return pl.pallas_call(
            kernel,
            out_shape=outs,
            scratch_shapes=scratch,
            compiler_params=params,
            name=name,
        )(*operands)

    def shift(cells, step):
        n = lax.axis_size("gx")
        return lax.ppermute(cells, "gx", [(i, (i + step) % n) for i in range(n)])

    def trade(cells, first):
        axis = "gy"
        n = lax.axis_size(axis)
        step = [1, -1] if first else [-1, 1]
        return lax.ppermute(cells, axis, [(i, (i + step[i % 2]) % n) for i in range(n)])

    def two_away(cells, axis):
        n = lax.axis_size(axis)
        return lax.ppermute(cells, axis, [(i, (i + 2) % n) for i in range(n)]) if n == 4 else cells

    short = sizes[0] <= 4 and sizes[1] <= 4 and sizes[2] <= 2
    x_high = call(pack_up_kernel, face, "pack_up", (cells,))
    x_below = shift(x_high, 1)
    x_low, y_first, top = call(
        pack_kernel, [face, face, shape(TOP_TILES, *tile)], "pack", (cells, zst, zfl)
    )
    top_two = two_away(top, "gx")
    y_second = call(pack_second_kernel, face, "pack_second", (cells, zst, zfl, top, top_two))
    below_lanes = beyond_lanes(call(lanes_kernel, shape(1, *tile), "lanes", (x_below,)))
    y_first = trade(y_first, True)
    x_above = shift(x_low, -1)
    y_second = trade(y_second, False)
    c_first, c_second, line_top = call(
        relay_kernel,
        [corner, corner, lane_row],
        "relay",
        (x_below, below_lanes, x_above, top, top_two),
    )
    c_first = trade(c_first, True)
    c_second = trade(c_second, False)
    if short:
        line_two = two_away(line_top, "gy")
    else:
        line_two = lax.pmax(line_top, ("gx", "gy", "gz"))
    own = cx // 2
    arrived = (cells, zst, zfl, x_below, y_first, x_above, y_second, below_lanes)
    early = call(
        early_kernel,
        [
            shape(*st.shape),
            shape(FLUID, rows, cz),
            shape(CURVED, own, *tile),
            shape(2 * own + 1, *tile),
        ],
        "early",
        arrived,
        [
            pltpu.VMEM((fields, own + 4) + tile, f32),
            pltpu.VMEM((fields, own) + tile, f32),
            pltpu.VMEM((fields, own) + tile, f32),
            pltpu.VMEM((CURVED, own + 2) + tile, f32),
            pltpu.VMEM((CURVED, own) + tile, f32),
            pltpu.VMEM((fields, 3) + tile, f32),
            pltpu.VMEM((CURVED, 6) + tile, f32),
            pltpu.VMEM((fields,) + tile, f32),
            pltpu.VMEM((own, 11) + tile, f32),
        ],
    )
    st_next, fl_next = call(
        late_kernel,
        [shape(*st.shape), shape(*fl.shape)],
        "late",
        (*arrived, c_first, c_second, line_two, line_top, *early),
    )
    return st_next.reshape(spacetime.shape), fl_next.reshape(fluid.shape)


def solution(mesh):
    spec = P(None, "gx", "gy", "gz")
    return jax.shard_map(
        per_device, mesh=mesh, in_specs=(spec, spec), out_specs=(spec, spec), check_vma=False
    )
```

```python
import functools
import math

import jax
import jax.numpy as jnp
from jax import lax
from jax.experimental import pallas as pl
from jax.experimental.pallas import tpu as pltpu
from jax.sharding import PartitionSpec as P

RECOVERY_STEPS = 4
INDEX_PAIRS = ((0, 0), (0, 1), (0, 2), (1, 1), (1, 2), (2, 2))
COURANT = 0.25
DISSIPATION = 0.2
KAPPA_ONE = 0.02
SHIFT_DAMPING = 1.0
SPEED_CAP = 0.99
PRESSURE_FLOOR = 0.01
FOUR_PI = 4.0 * math.pi

BATCH = 6
CURVED = 11
FLUID = 8


def total(pieces):
    summed = pieces[0]
    for member in pieces[1:]:
        summed = summed + member
    return summed


def dot(first_vec, second_vec):
    return total([first_vec[i] * second_vec[i] for i in range(3)])


def slot_of(i, j):
    return INDEX_PAIRS.index((min(i, j), max(i, j)))


def symmetric(entries):
    return [[entries[slot_of(i, j)] for j in range(3)] for i in range(3)]


def trace_with(inverse, tensor):
    return (
        inverse[0][0] * tensor[0][0]
        + inverse[1][1] * tensor[1][1]
        + inverse[2][2] * tensor[2][2]
        + 2.0
        * (
            inverse[0][1] * tensor[0][1]
            + inverse[0][2] * tensor[0][2]
            + inverse[1][2] * tensor[1][2]
        )
    )


def inverse_metric(metric):
    cofactor = [
        metric[1][1] * metric[2][2] - metric[1][2] * metric[1][2],
        metric[0][2] * metric[1][2] - metric[0][1] * metric[2][2],
        metric[0][1] * metric[1][2] - metric[0][2] * metric[1][1],
        metric[0][0] * metric[2][2] - metric[0][2] * metric[0][2],
        metric[0][1] * metric[0][2] - metric[0][0] * metric[1][2],
        metric[0][0] * metric[1][1] - metric[0][1] * metric[0][1],
    ]
    determinant = (
        metric[0][0] * cofactor[0] + metric[0][1] * cofactor[1] + metric[0][2] * cofactor[2]
    )
    over = 1.0 / determinant
    return symmetric([c * over for c in cofactor])


class Tile:
    def __init__(self, cy, cz):
        self.cy, self.rows, self.lanes = cy, 2 * cy, cz
        shape = (self.rows, cz)
        self.row = lax.broadcasted_iota(jnp.int32, shape, 0)
        self.lane = lax.broadcasted_iota(jnp.int32, shape, 1)
        self.slot = lax.rem(self.row, cy)

    def turn(self, tile, amount):
        amount = amount % self.rows
        return tile if amount == 0 else pltpu.roll(tile, amount, 0)

    def spin(self, tile, amount):
        amount = amount % self.lanes
        return tile if amount == 0 else pltpu.roll(tile, amount, 1)

    def swap(self, tile):
        return self.turn(tile, self.cy)

    def odd(self, a, b):
        return self.turn(jnp.where(self.row < self.cy, b, a), self.cy)

    def odd_swapped(self, a, b):
        return self.turn(jnp.where(self.row < self.cy, a, b), self.cy)

    def y_up(self, main, beyond, k):
        return self.turn(jnp.where(self.slot < k, beyond, main), -k)

    def y_down(self, main, beyond, k):
        return self.turn(jnp.where(self.slot >= self.cy - k, beyond, main), k)

    def z_up(self, main, beyond, k):
        return self.spin(jnp.where(self.lane < k, beyond, main), -k)

    def z_down(self, main, beyond, k):
        return self.spin(jnp.where(self.lane >= self.lanes - k, beyond, main), k)

    def corner_rows(self, side, turn):
        places = ((0, 2), (self.cy - 1, self.cy + 1))[side]
        first, second = [(place + turn) % self.rows for place in places]
        return (self.row == first) | (self.row == second)

    def join_low(self, u, v):
        return jnp.where(self.slot < 2, self.swap(u), self.turn(v, 2))

    def join_high(self, u, v):
        return jnp.where(self.slot >= self.cy - 2, self.swap(u), self.turn(self.swap(v), -2))

    def part_first(self, from_above, from_below):
        return jnp.where(self.slot < 2, from_above, from_below)

    def part_second(self, from_above, from_below):
        return self.turn(jnp.where(self.slot < 2, from_below, from_above), 2)


def edge_list(tiles):
    fields = next(n for n in range(tiles) if face_tiles(n) == tiles)
    return list(range(CURVED)) + list(range(fields, fields + FLUID))


CORNER_TURNS = (0, 1, 4, 5)
TOP_TILES = 2
CORNER_TILES = CURVED + FLUID // 4 + 1
TOP_ROW = 6


def face_tiles(fields):
    return fields + FLUID + len(pairs_of(third_list(fields))) + 1


def third_list(fields):
    return list(range(fields + 1))


def pairs_of(items):
    return [(items[i], items[min(i + 1, len(items) - 1)]) for i in range(0, len(items), 2)]


def top_speed(st):
    inverse = inverse_metric(symmetric([st[1 + s] for s in range(6)]))
    scale = 2.0 * st[7] * st[0]
    speeds = [jnp.abs(st[8 + d]) + jnp.sqrt(scale * inverse[d][d]) for d in range(3)]
    top = jnp.maximum(jnp.maximum(speeds[0], speeds[1]), speeds[2])
    return jnp.max(jnp.max(top, axis=1, keepdims=True), axis=0, keepdims=True)


class Chosen:
    def __init__(self, first, second, swapped):
        self.first, self.second, self.swapped, self.shape = first, second, swapped, first.shape

    def __getitem__(self, key):
        return jnp.where(self.swapped, self.second[key], self.first[key])


class Sent:
    def __init__(self, first, second, swapped):
        self.first, self.second, self.swapped, self.shape = first, second, swapped, first.shape

    def put(self, key, lower, upper):
        self.first[key] = jnp.where(self.swapped, upper, lower)
        self.second[key] = jnp.where(self.swapped, lower, upper)


class Joined:
    def __init__(self, tiles, tail):
        self.tiles, self.tail = tiles, tail
        self.shape = tuple(tiles.shape)

    def __getitem__(self, key):
        q, rows = (key[0], key[1:]) if isinstance(key, tuple) else (key, ())
        if q == self.tiles.shape[0] - 1:
            return self.tail[(0,) + rows]
        return self.tiles[(q,) + rows]


def even_along_y(tile):
    return jnp.full(tile, lax.rem(lax.axis_index("gy"), 2), jnp.int32) == 0


def pack_up_kernel(cells, x_high):
    count, rows, lanes = cells.shape
    fields, half = count - FLUID, rows // 2
    t = Tile(rows // 4, lanes)
    for q in range(count):
        x_high[q] = cells[q, half:rows, :]
    for n, (a, b) in enumerate(pairs_of(list(range(fields)) + [fields + 5])):
        x_high[count + n] = jnp.where(
            t.row < t.cy, t.swap(cells[b, 0:half, :]), cells[a, 0:half, :]
        )
    x_high[x_high.shape[0] - 1] = jnp.broadcast_to(top_speed(cells), t.row.shape)


def lanes_kernel(x_below, out):
    t = Tile(x_below.shape[1] // 2, x_below.shape[2])
    last = x_below.shape[0] - 1
    packed = x_below[last]
    for place, q in enumerate(edge_list(x_below.shape[0])):
        piece = t.spin(x_below[q], 4 * place + 2)
        here = (t.lane >= 4 * place) & (t.lane < 4 * place + 4)
        packed = jnp.where(here, piece, packed)
    out[0] = packed


def pack_kernel(cells, zst, zfl, *outs):
    fields, rows, lanes = zst.shape
    st, fl = cells.at[0:fields], cells.at[fields : fields + FLUID]
    cy = rows // 4
    t = Tile(cy, lanes)
    x_low, y_first, y_second, top_out = outs
    half = t.rows
    to_y = Sent(y_first, y_second, even_along_y((half, lanes)))

    def own(ref, q):
        return [ref[q, 0:half, :], ref[q, half : 2 * half, :]]

    tiles, beyond = [], []
    for q in range(fields):
        tiles.append(own(st, q))
        beyond.append(own(zst, q) if q < CURVED else None)
    for q in range(FLUID):
        tiles.append(own(fl, q))
        beyond.append(own(zfl, q))

    packed = [None] * 4
    place_count = 0
    for q, (first, second) in enumerate(tiles):
        x_low[q] = first
        to_y.put(q, t.join_low(first, second), t.join_high(first, second))
        if beyond[q] is not None:
            zf, zs = beyond[q]
            for m, piece in enumerate((zf, zs, t.join_low(zf, zs), t.join_high(zf, zs))):
                piece = t.spin(piece, 4 * place_count + 2)
                packed[m] = (
                    piece if place_count == 0 else jnp.where(t.lane < 4 * place_count, packed[m], piece)
                )
            place_count += 1
    for n, (a, b) in enumerate(pairs_of(third_list(fields))):
        slot = fields + FLUID + n
        xa, xb = (tiles[q if q < fields else fields + 5] for q in (a, b))
        x_low[slot] = jnp.where(t.row < cy, xa[1], t.swap(xb[1]))
        ya, yb = (tiles[q if q < fields else fields + 6] for q in (a, b))
        w = [t.swap(ya[0]), t.swap(ya[1]), t.swap(yb[0]), t.swap(yb[1])]
        s = t.slot
        low = jnp.where(s == 0, t.turn(w[2], -2), t.turn(w[3], -1))
        low = jnp.where(s == 2, w[0], jnp.where(s == 3, t.turn(w[1], 1), low))
        high = jnp.where(s == 3, t.turn(w[2], 2), t.turn(w[3], 1))
        high = jnp.where(s == 1, w[0], jnp.where(s == 0, t.turn(w[1], -1), high))
        to_y.put(slot, low, high)
    top = jnp.maximum(top_speed(st), top_speed(zst))
    top_out[...] = jnp.broadcast_to(top, top_out.shape)
    last = x_low.shape[0] - 1
    x_lanes = [jnp.where(t.lane < 4 * place_count, piece, top) for piece in packed[:2]]
    y_lanes = [jnp.where(t.lane < 4 * place_count, piece, top) for piece in packed[2:]]
    x_low[last] = x_lanes[0]
    to_y.put(last, *y_lanes)


def relay_kernel(
    x_below, below_lanes, x_above, y_first, y_second, top, top_two, chunks, line_top
):
    cy, lanes = x_below.shape[1] // 2, x_below.shape[2]
    t = Tile(cy, lanes)
    count, place = chunks.shape[0], lax.axis_index("gy")
    to_low = chunks.at[lax.rem(place + count - 1, count)]
    to_high = chunks.at[lax.rem(place + 1, count)]
    last = x_below.shape[0] - 1
    line = jnp.maximum(top[0, 0:1, :], top_two[0, 0:1, :])
    line = jnp.maximum(line, x_below[last, 0:1, lanes - 1 : lanes])
    x_below = Joined(x_below, below_lanes)
    for beside in (x_below, x_above, y_first, y_second):
        line = jnp.maximum(line, beside[last, 0:1, lanes - 1 : lanes])
    line_top[...] = line
    edge = edge_list(x_below.shape[0])
    for q in range(CURVED):
        below, above = x_below[q], x_above[q]
        to_low[q] = t.join_low(below, above)
        to_high[q] = t.join_high(below, above)
    for n in range(0, FLUID, 4):
        low, high = None, None
        for turn, q in zip(CORNER_TURNS, edge[CURVED + n : CURVED + n + 4]):
            below, above = x_below[q], x_above[q]
            below, above = (t.turn(j(below, above), turn) for j in (t.join_low, t.join_high))
            if low is None:
                low, high = below, above
            else:
                low = jnp.where(t.corner_rows(0, turn), below, low)
                high = jnp.where(t.corner_rows(1, turn), above, high)
        to_low[CURVED + n // 4] = low
        to_high[CURVED + n // 4] = high
    along_x, along_y = edge[CURVED + 5], edge[CURVED + 6]
    low = t.join_low(x_below[along_y], x_above[along_y])
    high = t.join_high(x_below[along_x], x_above[along_x])
    for other in range(count):
        chunks[other, CORNER_TILES - 1] = jnp.broadcast_to(line, (t.rows, lanes))
    to_low[CORNER_TILES - 1] = jnp.where(t.row == TOP_ROW, line, low)
    to_high[CORNER_TILES - 1] = jnp.where(t.row == TOP_ROW, line, high)


def limited(a, b):
    return jnp.maximum(jnp.minimum(a, b), 0.0) + jnp.minimum(jnp.maximum(a, b), 0.0)


def recover(conserved, magnetic):
    density = conserved[0]
    momenta = conserved[1:4]
    energy = conserved[4] + density
    mom_sq = dot(momenta, momenta)
    mag_sq = dot(magnetic, magnetic)
    cross = dot(momenta, magnetic)
    cross_sq = cross * cross

    def state(z):
        grown = z + mag_sq
        over = 1.0 / (z * grown)
        speed_sq = (mom_sq * z * z + cross_sq * (2.0 * z + mag_sq)) * over * over
        kept = 1.0 - jnp.minimum(speed_sq, SPEED_CAP)
        rest = density * jnp.sqrt(kept)
        return kept, rest, 0.5 * (z * kept - rest), grown * over

    z = jnp.maximum(energy - 0.5 * mag_sq, density)
    for _ in range(RECOVERY_STEPS):
        kept, rest, pressure, over_z = state(z)
        residual = (
            z
            + mag_sq
            - pressure
            - 0.5 * mag_sq * kept
            - 0.5 * cross_sq * over_z * over_z
            - energy
        )
        z = jnp.maximum(z - residual / (1.0 - 0.5 * kept), density)
    kept, rest, pressure, over_z = state(z)
    pressure = jnp.maximum(pressure, PRESSURE_FLOOR * rest)
    scale = lax.rsqrt(kept) / (z + mag_sq)
    along = cross * over_z
    four_vel = [scale * (momenta[i] + along * magnetic[i]) for i in range(3)]
    return [rest, pressure] + four_vel


def stress_parts(rest, pressure, u, magnetic):
    lorentz_sq = 1.0 + dot(u, u)
    over = lax.rsqrt(lorentz_sq)
    over_sq = over * over
    time_b = dot(u, magnetic)
    grown_b = [magnetic[i] + time_b * u[i] for i in range(3)]
    b_square = (dot(magnetic, magnetic) + time_b * time_b) * over_sq
    enthalpy = rest + 2.0 * pressure
    inertia = enthalpy + b_square
    return lorentz_sq, over, over_sq, time_b, grown_b, b_square, enthalpy, inertia


def face_state(rest, pressure, u, magnetic, d):
    lorentz_sq, over, over_sq, time_b, grown_b, b_square, enthalpy, inertia = stress_parts(
        rest, pressure, u, magnetic
    )
    total_pressure = pressure + 0.5 * b_square
    lorentz = lorentz_sq * over
    density = rest * lorentz
    carried = inertia * lorentz
    time_over = time_b * over
    conserved = [density]
    conserved += [carried * u[j] - time_over * grown_b[j] for j in range(3)]
    conserved += [inertia * lorentz_sq - total_pressure - time_b * time_b - density]
    mass_flux = rest * u[d]
    flux = [mass_flux]
    pushed = inertia * u[d]
    b_over = grown_b[d] * over_sq
    for j in range(3):
        flux_j = pushed * u[j] - b_over * grown_b[j]
        flux.append(flux_j + total_pressure if j == d else flux_j)
    flux.append(carried * u[d] - time_over * grown_b[d] - mass_flux)
    ratio = 1.0 / (enthalpy * inertia)
    sound_sq = 2.0 * pressure * inertia * ratio
    alfven_sq = b_square * enthalpy * ratio
    fast_sq = sound_sq + alfven_sq - sound_sq * alfven_sq
    slow = 1.0 - fast_sq
    velocity = u[d] * over
    rest_part = 1.0 - dot(u, u) * over_sq * fast_sq
    spread = jnp.sqrt(fast_sq * over_sq * (rest_part - velocity * velocity * slow))
    fastest = (jnp.abs(velocity * slow) + spread) / rest_part
    return conserved, flux, fastest


def face_flux(left, right, normal, weight, d):
    sides = []
    for state in (left, right):
        magnetic = [normal if i == d else state[5 + i] for i in range(3)]
        sides.append(face_state(state[0], state[1], state[2:5], magnetic, d))
    (cons_l, flux_l, fast_l), (cons_r, flux_r, fast_r) = sides
    signal = jnp.maximum(fast_l, fast_r)
    scale = 0.5 * weight
    return [scale * (flux_l[q] + flux_r[q] - signal * (cons_r[q] - cons_l[q])) for q in range(5)]


def volume_over(conformal):
    return conformal * jnp.sqrt(conformal)


def first_diff(down_two, down, up, up_two):
    return (8.0 / 12.0) * (up - down) + (1.0 / 12.0) * (down_two - up_two)


class Halo:
    def __init__(self, cells, zst, zfl, x_below, y_first, x_above, y_second, below_lanes, chunks=None):
        x_below = Joined(x_below, below_lanes)
        self.fields, self.block, self.lanes = zst.shape
        even_y = even_along_y((self.block // 2, self.lanes))
        y_below, y_above = Chosen(y_first, y_second, even_y), Chosen(y_second, y_first, even_y)
        if chunks is not None:
            count, place = chunks.shape[0], lax.axis_index("gy")
            self.c_below = chunks.at[lax.rem(place + count - 1, count)]
            self.c_above = chunks.at[lax.rem(place + 1, count)]
        self.st = cells.at[0 : self.fields]
        self.fl = cells.at[self.fields : self.fields + FLUID]
        self.zst, self.zfl = zst, zfl
        self.x_below, self.x_above = x_below, x_above
        self.y_below, self.y_above = y_below, y_above
        self.cy = self.block // 4
        self.t = Tile(self.cy, self.lanes)
        self.half = self.t.rows
        self.own = self.block // self.half
        self.inner = range(1, self.own + 1)
        self.span = range(self.own + 2)
        self.edge = edge_list(x_below.shape[0])
        self.last = x_below.shape[0] - 1

    def rows_of(self, ref, q, p):
        return ref[q, (p - 1) * self.half : p * self.half, :]

    def main(self, q, p):
        if q < self.fields:
            return self.rows_of(self.st, q, p)
        return self.rows_of(self.fl, q - self.fields, p)

    def beyond(self, q, p):
        if q < self.fields:
            return self.rows_of(self.zst, q, p)
        return self.rows_of(self.zfl, q - self.fields, p)

    def part(self, second):
        return self.t.part_second if second else self.t.part_first

    def beside(self, q, p):
        return self.part(p == 2)(self.y_above[q], self.y_below[q])

    def third_place(self, q):
        return self.fields + FLUID + q // 2, q % 2

    def x_third(self, q, upper):
        tile, which = self.third_place(q)
        found = self.x_above[tile] if upper else self.x_below[tile]
        return self.t.swap(found) if which else found

    def y_third(self, q, p):
        t = self.t
        tile, which = self.third_place(q)
        turn_above, turn_below = ((0, 0), (-1, 1), (2, -2), (1, -1))[2 * which + p - 1]
        above, below = t.turn(self.y_above[tile], turn_above), t.turn(self.y_below[tile], turn_below)
        return jnp.where(t.slot == 2, above, below)

    def z_place(self, q):
        return 4 * self.edge.index(q) + 2

    def x_beyond(self, q, upper):
        tile = self.x_above[self.last] if upper else self.x_below[self.last]
        return self.t.spin(tile, -self.z_place(q))

    def y_beyond(self, q, p):
        return self.t.spin(self.beside(self.last, p), -self.z_place(q))

    def corner(self, q, p):
        place, turn = q, 0
        if q >= CURVED:
            n = q - self.fields
            place, turn = CURVED + n // 4, CORNER_TURNS[n % 4]
        above, below = self.t.turn(self.c_above[place], -turn), self.t.turn(self.c_below[place], -turn)
        return self.part(p > 0)(above, below)

    def corner_layers(self, p):
        place = CORNER_TILES - 1
        return self.part(p > 0)(self.c_above[place], self.c_below[place])

    def plane(self, q):
        inner = self.inner
        return (
            [self.x_below[q]] + [self.main(q, p) for p in inner] + [self.x_above[q]],
            [None] + [self.beside(q, p) for p in inner] + [None],
            [self.x_beyond(q, False)]
            + [self.beyond(q, p) for p in inner]
            + [self.x_beyond(q, True)],
            [None] + [self.y_beyond(q, p) for p in inner] + [None],
        )


def weigh(chi_face, alpha_face):
    shrink = volume_over(chi_face)
    return shrink, alpha_face / shrink


def primitives(half, spots, cons, centred, chi, alpha, batch):
    found = {}
    for start in range(0, len(spots), batch):
        group = spots[start : start + batch]

        def gather(planes):
            return jnp.concatenate([planes[k][p] for k, p in group], axis=0)

        shrink = volume_over(gather(chi))
        mag_raw = [gather(centred[i]) for i in range(3)]
        mag = [m * shrink for m in mag_raw]
        values = recover([gather(c) * shrink for c in cons], mag)
        u = values[2:5]
        factor = gather(alpha) * lax.rsqrt(1.0 + dot(u, u))
        field = [
            factor * (u[(i + 2) % 3] * mag_raw[(i + 1) % 3] - u[(i + 1) % 3] * mag_raw[(i + 2) % 3])
            for i in range(3)
        ]
        for n, spot in enumerate(group):
            found[spot] = [value[n * half : (n + 1) * half] for value in values + mag + field]
    return found


def ring_fluxes(prims, chi, alpha, normals, d, up, down):
    found = []
    for here, there in ((0, 1), (1, 0)):
        left, right = [], []
        for a, b in zip(prims[here], prims[there]):
            below = down(a, b, 1)
            middle = a - below
            left.append(below + 0.5 * limited(below - down(a, b, 2), middle))
            right.append(a - 0.5 * limited(middle, up(a, b, 1) - a))
        shrink, weight = weigh(
            0.5 * (chi[here] + down(chi[here], chi[there], 1)),
            0.5 * (alpha[here] + down(alpha[here], alpha[there], 1)),
        )
        found.append(face_flux(left, right, normals[here] * shrink, weight, d))
    return [a - up(a, b, 1) for a, b in zip(*found)]


def early_kernel(
    cells, zst, zfl, x_below, y_first, x_above, y_second, below_lanes,
    st_rate, hydro_rate, slopes, electric, pairs, sides, thirds, pairs_z, sides_z, grads, seconds, damped, tensors,
):
    halo = Halo(cells, zst, zfl, x_below, y_first, x_above, y_second, below_lanes)
    t, fields, half, own, cy = halo.t, halo.fields, halo.half, halo.own, halo.cy
    st, fl, inner = halo.st, halo.fl, halo.inner

    for q in range(fields):
        pairs[q, 0] = halo.x_third(q, False)
        pairs[q, 1] = x_below[q]
        for p in inner:
            pairs[q, 1 + p] = halo.main(q, p)
            sides[q, p - 1] = halo.beside(q, p)
            thirds[q, p - 1] = halo.y_third(q, p)
        pairs[q, 2 + own] = x_above[q]
        pairs[q, 3 + own] = halo.x_third(q, True)
        if q < CURVED:
            pairs_z[q, 0] = halo.x_beyond(q, False)
            pairs_z[q, own + 1] = halo.x_beyond(q, True)
            for p in inner:
                pairs_z[q, p] = halo.beyond(q, p)
                sides_z[q, p - 1] = halo.y_beyond(q, p)

    span = halo.span
    face = [halo.plane(fields + 5 + i) for i in range(3)]

    def halves(kind, p):
        own_x, own_y, own_z = (f[kind][p] for f in face)
        pair = kind in (0, 2)
        known_x = pair or p < own
        last = kind == 0 and p == own + 1
        if pair:
            next_x = halo.x_third(fields, True) if last else face[0][kind][min(p + 1, own + 1)]
            next_x = t.odd(own_x, next_x)
        else:
            next_x = t.odd_swapped(own_x, face[0][kind][p + 1] if known_x else own_x)
        dx = 0.5 * (next_x - own_x)
        dz = 0.5 * (t.z_up(own_z, face[2][kind ^ 2][p], 1) - own_z)
        inside = 1 <= p <= own
        if not pair:
            here = jnp.where(t.slot == 2, halo.y_third(fields, p), own_y) if kind == 1 else own_y
            next_y = t.y_up(here, face[1][kind ^ 1][p], 1)
        else:
            next_y = t.y_up(own_y, face[1][kind ^ 1][p] if inside else own_y, 1)
        dy = 0.5 * (next_y - own_y)
        if pair and not inside:
            dy = jnp.where(t.slot == cy - 1, -(dx + dz), dy)
        if not pair and not known_x:
            dx = jnp.where(t.row < cy, -(dy + dz), dx)
        return own_x + dx, own_y + dy, own_z + dz

    spots = [(0, p) for p in span] + [(1, p) for p in inner]
    spots += [(2, p) for p in span] + [(3, p) for p in inner]
    centred = [[[None] * (own + 2) for _ in range(4)] for _ in range(3)]
    for k, p in spots:
        for i, value in enumerate(halves(k, p)):
            centred[i][k][p] = value
    chi, alpha = halo.plane(0), halo.plane(7)
    found = primitives(
        half, spots, [halo.plane(fields + q) for q in range(5)], centred, chi, alpha, BATCH
    )

    lines = [[found[0, p][i] for p in span] for i in range(8)] + [chi[0], alpha[0]]
    odd_lines = [[t.odd(f[p], f[min(p + 1, own + 1)]) for p in span] for f in lines]
    fluxes = [None]
    for p in range(1, own + 2):
        left, right = [], []
        for f, o in zip(lines[:8], odd_lines):
            here = f[p] - o[p - 1]
            left.append(o[p - 1] + 0.5 * limited(o[p - 1] - f[p - 1], here))
            right.append(f[p] - 0.5 * limited(here, o[p] - f[p]))
        shrink, weight = weigh(
            0.5 * (lines[8][p] + odd_lines[8][p - 1]), 0.5 * (lines[9][p] + odd_lines[9][p - 1])
        )
        fluxes.append(face_flux(left, right, face[0][0][p] * shrink, weight, 0))
    for p in inner:
        changes = [
            ring_fluxes(
                [found[k, p][:8] for k in (0, kind)],
                [chi[k][p] for k in (0, kind)],
                [alpha[k][p] for k in (0, kind)],
                [face[d][k][p] for k in (0, kind)],
                d,
                up,
                down,
            )
            for d, kind, up, down in ((1, 1, t.y_up, t.y_down), (2, 2, t.z_up, t.z_down))
        ]
        for q in range(5):
            change = fluxes[p][q] - t.odd(fluxes[p][q], fluxes[p + 1][q])
            tensors[p - 1, 6 + q] = change + changes[0][q] + changes[1][q]
        rest, pressure = found[0, p][:2]
        u = found[0, p][2:5]
        parts = stress_parts(rest, pressure, u, found[0, p][5:8])
        lorentz_sq, over, over_sq, time_b, grown_b, b_square, enthalpy, inertia = parts
        total_pressure = pressure + 0.5 * b_square
        for s, (i, j) in enumerate(INDEX_PAIRS):
            value = inertia * u[i] * u[j] - over_sq * (grown_b[i] * grown_b[j])
            tensors[p - 1, s] = value + total_pressure if i == j else value

    ex, ey, ez = (
        [[found[k, p][8 + i] if (k, p) in found else None for p in span] for k in range(4)]
        for i in range(3)
    )
    ey_x = [
        [ey[k][p] + t.odd(ey[k][p - 1], ey[k][p]) if p else None for p in span] for k in (0, 2)
    ]
    edge_y = [None] + [ey_x[0][p] + t.z_down(ey_x[0][p], ey_x[1][p], 1) for p in span[1:]]
    for p in span[1:]:
        electric[p - 1] = ez[0][p] + t.odd(ez[0][p - 1], ez[0][p])
    for p in inner:
        electric[own + p] = ez[1][p]
        edge_y_z = ey_x[1][p] + t.z_down(ey_x[1][p], ey_x[0][p], 1)
        ex_y = ex[0][p] + t.y_down(ex[0][p], ex[1][p], 1)
        ex_y_h = ex[1][p] + t.y_down(ex[1][p], ex[0][p], 1)
        ex_y_z = ex[2][p] + t.y_down(ex[2][p], ex[3][p], 1)
        ex_y_hz = ex[3][p] + t.y_down(ex[3][p], ex[2][p], 1)
        edge_x = ex_y + t.z_down(ex_y, ex_y_z, 1)
        edge_x_h = ex_y_h + t.z_down(ex_y_h, ex_y_hz, 1)
        edge_x_z = ex_y_z + t.z_down(ex_y_z, ex_y, 1)
        place = slice((p - 1) * half, p * half)
        hydro_rate[5, place, :] = t.z_up(edge_y[p], edge_y_z, 1) - edge_y[p]
        hydro_rate[6, place, :] = edge_x - t.z_up(edge_x, edge_x_z, 1)
        hydro_rate[7, place, :] = (t.y_up(edge_x, edge_x_h, 1) - edge_x) - (
            t.odd(edge_y[p], edge_y[p + 1]) - edge_y[p]
        )

    def pair_step(index):
        p = index + 1
        base = index * half

        for q in range(fields):
            centre = pairs[q, p + 1]
            x_m3 = t.odd(pairs[q, p - 1], pairs[q, p])
            x_m2 = pairs[q, p]
            x_m1 = t.odd(pairs[q, p], centre)
            x_p1 = t.odd(centre, pairs[q, p + 2])
            x_p2 = pairs[q, p + 2]
            x_p3 = t.odd(pairs[q, p + 2], pairs[q, p + 3])
            side, third = sides[q, index], thirds[q, index]
            y_m1, y_m2 = t.y_down(centre, side, 1), t.y_down(centre, side, 2)
            y_p1, y_p2 = t.y_up(centre, side, 1), t.y_up(centre, side, 2)
            y_m3 = t.turn(
                jnp.where(t.slot >= cy - 2, side, jnp.where(t.slot == cy - 3, third, centre)), 3
            )
            y_p3 = t.turn(jnp.where(t.slot < 2, side, jnp.where(t.slot == 2, third, centre)), -3)
            beyond = zst[q, pl.ds(base, half), :]
            z_m1, z_m2, z_m3 = (t.z_down(centre, beyond, k) for k in (1, 2, 3))
            z_p1, z_p2, z_p3 = (t.z_up(centre, beyond, k) for k in (1, 2, 3))
            dx = first_diff(x_m2, x_m1, x_p1, x_p2)
            dy = first_diff(y_m2, y_m1, y_p1, y_p2)
            grads[q, 0] = dx
            if q < CURVED:
                slopes[q, index] = dx
            grads[q, 1] = dy
            grads[q, 2] = first_diff(z_m2, z_m1, z_p1, z_p2)
            near = [x_m1 + x_p1, y_m1 + y_p1, z_m1 + z_p1]
            far = [x_m2 + x_p2, y_m2 + y_p2, z_m2 + z_p2]
            outer = (x_m3 + x_p3) + (y_m3 + y_p3) + (z_m3 + z_p3)
            damped[q] = (DISSIPATION / 64.0) * (
                outer - 6.0 * (far[0] + far[1] + far[2]) + 15.0 * (near[0] + near[1] + near[2])
                - 60.0 * centre
            )
            if q < CURVED:
                for s, d in ((0, 0), (3, 1), (5, 2)):
                    seconds[q, s] = (1.0 / 12.0) * (16.0 * near[d] - far[d] - 30.0 * centre)
                b_m, b_c, b_p = pairs_z[q, p - 1], pairs_z[q, p], pairs_z[q, p + 1]
                dx_z = first_diff(b_m, t.odd(b_m, b_c), t.odd(b_c, b_p), b_p)
                b_s = sides_z[q, p - 1]
                dy_z = first_diff(
                    t.y_down(b_c, b_s, 2),
                    t.y_down(b_c, b_s, 1),
                    t.y_up(b_c, b_s, 1),
                    t.y_up(b_c, b_s, 2),
                )
                for s, inside, outside in ((2, dx, dx_z), (4, dy, dy_z)):
                    seconds[q, s] = first_diff(
                        t.z_down(inside, outside, 2),
                        t.z_down(inside, outside, 1),
                        t.z_up(inside, outside, 1),
                        t.z_up(inside, outside, 2),
                    )

        def value(q):
            return pairs[q, p + 1]

        def fluid_value(q):
            return fl[q, pl.ds(base, half), :]

        conformal, lapse = value(0), value(7)
        over_chi = 1.0 / conformal
        metric = symmetric([value(1 + s) for s in range(6)])
        shift = [value(8 + i) for i in range(3)]
        extrinsic, theta = value(11), value(21)
        traceless = symmetric([value(12 + s) for s in range(6)])
        connection = [value(18 + i) for i in range(3)]
        inverse = inverse_metric(metric)
        grad = [[grads[q, k] for k in range(3)] for q in range(fields)]
        chi_grad, lapse_grad = grad[0], grad[7]
        shift_grad = [[grad[8 + i][k] for i in range(3)] for k in range(3)]
        trace_k = extrinsic + 2.0 * theta

        stress = symmetric([tensors[p - 1, s] for s in range(6)])
        held = [fluid_value(q) for q in range(5)]
        shrink = volume_over(conformal)
        energy = held[4] + held[0]
        third_k = trace_k * (1.0 / 3.0)
        curved = [
            [
                (traceless[i][j] + metric[i][j] * third_k) if i <= j else None for j in range(3)
            ]
            for i in range(3)
        ]
        work = (
            stress[0][0] * curved[0][0]
            + stress[1][1] * curved[1][1]
            + stress[2][2] * curved[2][2]
            + 2.0
            * (
                stress[0][1] * curved[0][1]
                + stress[0][2] * curved[0][2]
                + stress[1][2] * curved[1][2]
            )
        )
        rates = [tensors[p - 1, 6 + q] for q in range(5)]
        for i in range(3):
            rates[1 + i] = (
                rates[1 + i]
                - energy * lapse_grad[i]
                + total([held[1 + k] * grad[8 + k][i] for k in range(3)])
            )
        rates[4] = (
            rates[4] + lapse * work * over_chi / shrink - dot(held[1:4], lapse_grad)
        )
        for q in range(5):
            hydro_rate[q, pl.ds(base, half), :] = rates[q]
        density = energy * shrink
        momentum = [held[1 + i] * shrink for i in range(3)]

        lowered = [[[None] * 3 for _ in range(3)] for _ in range(3)]
        for i in range(3):
            for j in range(3):
                for k in range(j, 3):
                    got = 0.5 * (
                        grad[1 + slot_of(i, k)][j]
                        + grad[1 + slot_of(i, j)][k]
                        - grad[1 + slot_of(j, k)][i]
                    )
                    lowered[i][j][k] = lowered[i][k][j] = got
        raised = [[[None] * 3 for _ in range(3)] for _ in range(3)]
        for i in range(3):
            for j in range(3):
                for k in range(j, 3):
                    got = total([inverse[i][l] * lowered[l][j][k] for l in range(3)])
                    raised[i][j][k] = raised[i][k][j] = got
        contracted = [trace_with(inverse, raised[i]) for i in range(3)]

        def hessian_trace(q):
            return (
                inverse[0][0] * seconds[q, 0]
                + inverse[1][1] * seconds[q, 3]
                + inverse[2][2] * seconds[q, 5]
                + 2.0 * (inverse[0][2] * seconds[q, 2] + inverse[1][2] * seconds[q, 4])
            )

        def second_cov(q, slope):
            bent = [total([raised[k][i][j] * slope[k] for k in range(3)]) for i, j in INDEX_PAIRS]
            return symmetric(
                [-bent[s] if s == 1 else seconds[q, s] - bent[s] for s in range(len(bent))]
            )

        chi_cov = second_cov(0, chi_grad)
        chi_lap = trace_with(inverse, chi_cov)
        raised_chi = [dot(inverse[i], chi_grad) for i in range(3)]
        chi_square = dot(raised_chi, chi_grad)
        cross_term = dot(raised_chi, lapse_grad)
        half_chi = 0.5 * over_chi
        plain_cov = second_cov(7, lapse_grad)
        lapse_cov = symmetric(
            [
                plain_cov[i][j]
                + (
                    chi_grad[i] * lapse_grad[j]
                    + chi_grad[j] * lapse_grad[i]
                    - metric[i][j] * cross_term
                )
                * half_chi
                for i, j in INDEX_PAIRS
            ]
        )
        lapse_lap = conformal * trace_with(inverse, lapse_cov)

        mixed = [
            [[dot(inverse[l], lowered[k][j]) for j in range(3)] for k in range(3)]
            for l in range(3)
        ]
        quarter_sq = half_chi * half_chi
        metric_factor = chi_lap * half_chi - 3.0 * chi_square * quarter_sq
        ricci = []
        for i, j in INDEX_PAIRS:
            second_part = -0.5 * hessian_trace(1 + slot_of(i, j))
            connection_part = 0.5 * total(
                [metric[k][i] * grad[18 + k][j] + metric[k][j] * grad[18 + k][i] for k in range(3)]
            )
            contracted_part = 0.5 * total(
                [contracted[k] * (lowered[i][j][k] + lowered[j][i][k]) for k in range(3)]
            )
            if i == j:
                quadratic = total(
                    [
                        raised[k][l][i] * (2.0 * mixed[l][i][k] + mixed[l][k][i])
                        for k in range(3)
                        for l in range(3)
                    ]
                )
            else:
                quadratic = total(
                    [
                        raised[k][l][i] * (mixed[l][j][k] + mixed[l][k][j])
                        + raised[k][l][j] * mixed[l][i][k]
                        for k in range(3)
                        for l in range(3)
                    ]
                )
            conformal_part = (
                chi_cov[i][j] * half_chi
                + metric[i][j] * metric_factor
                - chi_grad[i] * chi_grad[j] * quarter_sq
            )
            ricci.append(
                second_part + connection_part + contracted_part + quadratic + conformal_part
            )
        ricci = symmetric(ricci)
        ricci_scalar = conformal * trace_with(inverse, ricci)
        stress_trace = conformal * trace_with(inverse, stress)

        up_a = [
            [total([inverse[i][k] * traceless[k][j] for k in range(3)]) for j in range(3)]
            for i in range(3)
        ]
        raised_a = symmetric(
            [total([up_a[i][l] * inverse[j][l] for l in range(3)]) for i, j in INDEX_PAIRS]
        )
        a_square = trace_with(traceless, raised_a)
        shift_div = shift_grad[0][0] + shift_grad[1][1] + shift_grad[2][2]
        two_thirds_div = (2.0 / 3.0) * shift_div

        def finish(q, rate):
            rate = rate + dot(shift, grad[q]) + damped[q]
            st_rate[q, pl.ds(base, half), :] = rate

        finish(0, (2.0 / 3.0) * conformal * (lapse * trace_k - shift_div))
        finish(7, -2.0 * lapse * extrinsic)
        for i in range(3):
            finish(8 + i, 0.75 * connection[i] - SHIFT_DAMPING * shift[i])
        finish(
            11,
            lapse
            * (
                a_square
                + trace_k * trace_k * (1.0 / 3.0)
                + FOUR_PI * (stress_trace + density)
                + KAPPA_ONE * theta
            )
            - lapse_lap,
        )
        source = symmetric(
            [
                lapse * (ricci[i][j] - 2.0 * FOUR_PI * stress[i][j]) - lapse_cov[i][j]
                for i, j in INDEX_PAIRS
            ]
        )
        third_trace = trace_with(inverse, source) * (1.0 / 3.0)
        for s, (i, j) in enumerate(INDEX_PAIRS):
            finish(
                1 + s,
                total(
                    [
                        metric[i][k] * shift_grad[j][k] + metric[j][k] * shift_grad[i][k]
                        for k in range(3)
                    ]
                )
                - metric[i][j] * two_thirds_div
                - 2.0 * lapse * traceless[i][j],
            )
            product = total([traceless[i][k] * up_a[k][j] for k in range(3)])
            finish(
                12 + s,
                total(
                    [
                        traceless[i][k] * shift_grad[j][k] + traceless[j][k] * shift_grad[i][k]
                        for k in range(3)
                    ]
                )
                - traceless[i][j] * two_thirds_div
                + conformal * (source[i][j] - metric[i][j] * third_trace)
                + lapse * (trace_k * traceless[i][j] - 2.0 * product),
            )
        for i in range(3):
            bracket = (
                trace_with(raised_a, raised[i])
                - 1.5 * dot(raised_a[i], chi_grad) * over_chi
                - dot(inverse[i], [2.0 * grad[11][j] + grad[21][j] for j in range(3)]) * (1.0 / 3.0)
                - 2.0 * FOUR_PI * dot(inverse[i], momentum)
            )
            spread = [
                seconds[8, 0] + seconds[10, 2],
                seconds[9, 3] + seconds[10, 4],
                seconds[8, 2] + seconds[9, 4] + seconds[10, 5],
            ]
            finish(
                18 + i,
                contracted[i] * two_thirds_div
                - total([contracted[j] * shift_grad[j][i] for j in range(3)])
                + hessian_trace(8 + i)
                + dot(inverse[i], spread) * (1.0 / 3.0)
                - 2.0 * dot(raised_a[i], lapse_grad)
                + 2.0
                * lapse
                * (bracket - KAPPA_ONE * (connection[i] - contracted[i])),
            )
        finish(
            21,
            0.5
            * lapse
            * (
                ricci_scalar
                - a_square
                + (2.0 / 3.0) * trace_k * trace_k
                - 4.0 * FOUR_PI * density
            )
            - 2.0 * KAPPA_ONE * lapse * theta,
        )

    for index in range(own):
        pair_step(index)


def late_kernel(
    cells, zst, zfl, x_below, y_first, x_above, y_second, below_lanes, chunks, line_top,
    st_rate, hydro_rate, slopes, electric, st_out, fl_out,
):
    halo = Halo(
        cells, zst, zfl, x_below, y_first, x_above, y_second, below_lanes, chunks
    )
    x_below, x_above = halo.x_below, halo.x_above
    t, fields, half, own = halo.t, halo.fields, halo.half, halo.own
    inner, span = halo.inner, halo.span

    top = line_top[...]
    for other in range(chunks.shape[0]):
        top = jnp.maximum(top, chunks[other, CORNER_TILES - 1, TOP_ROW : TOP_ROW + 1, :])
    dt = COURANT / top

    for p in inner:
        place = slice((p - 1) * half, p * half)
        mixed = []
        for q in range(CURVED):
            s_m, s_c, s_p = (
                halo.beside(q, n) if 1 <= n <= own else halo.corner(q, n) for n in (p - 1, p, p + 1)
            )
            slope = slopes[q, p - 1]
            slope_side = first_diff(s_m, t.odd_swapped(s_m, s_c), t.odd_swapped(s_c, s_p), s_p)
            mixed.append(
                first_diff(
                    t.y_down(slope, slope_side, 2),
                    t.y_down(slope, slope_side, 1),
                    t.y_up(slope, slope_side, 1),
                    t.y_up(slope, slope_side, 2),
                )
            )
        conformal, lapse = halo.main(0, p), halo.main(7, p)
        metric = [halo.main(1 + s, p) for s in range(6)]
        inverse = inverse_metric(symmetric(metric))
        half_chi = 0.5 / conformal
        cross = inverse[0][1]
        chi_trace = 2.0 * cross * mixed[0] * half_chi
        ricci = [metric[s] * chi_trace - cross * mixed[1 + s] for s in range(6)]
        ricci[1] = ricci[1] + mixed[0] * half_chi
        source = [lapse * r for r in ricci]
        source[1] = source[1] - mixed[7]
        third_trace = trace_with(inverse, symmetric(source)) * (1.0 / 3.0)
        extra = {
            11: -2.0 * conformal * cross * mixed[7],
            21: 0.5 * lapse * conformal * trace_with(inverse, symmetric(ricci)),
        }
        for s in range(6):
            extra[12 + s] = conformal * (source[s] - metric[s] * third_trace)
        for i in range(3):
            extra[18 + i] = 2.0 * cross * mixed[8 + i] + (1.0 / 3.0) * (
                inverse[i][0] * mixed[9] + inverse[i][1] * mixed[8]
            )
        for q in range(fields):
            rate = st_rate[q, place, :]
            if q in extra:
                rate = rate + extra[q]
            st_out[q, place, :] = halo.main(q, p) + dt * rate

    end = own + 1
    ends = (0, end)
    bx_face, by_face, bz_face = ({p: halo.corner(fields + 5 + i, p) for p in ends} for i in range(3))
    layers = {p: halo.corner_layers(p) for p in ends}
    bx_face[end] = layers[end]
    by_face[0] = jnp.where(t.slot < 2, layers[0], by_face[0])
    centred = [{}, {}, {}]
    for p in ends:
        following = halo.beside(fields + 5, 1) if p == 0 else bx_face[p]
        edge_cells = x_below if p == 0 else x_above
        dx = 0.5 * (t.odd_swapped(bx_face[p], following) - bx_face[p])
        dy = 0.5 * (t.y_up(by_face[p], edge_cells[fields + 6], 1) - by_face[p])
        centred[0][p] = bx_face[p] + dx
        centred[1][p] = by_face[p] + dy
        centred[2][p] = bz_face[p] - (dx + dy)
    corners = [{p: halo.corner(q, p) for p in ends} for q in [0, 7] + list(range(fields, fields + 5))]
    found = primitives(
        half, [(0, p) for p in ends], [[c] for c in corners[2:]], [[c] for c in centred],
        [corners[0]], [corners[1]], 2,
    )
    ez_h = [found[0, 0][10]] + [electric[own + p] for p in inner] + [found[0, end][10]]
    ez_x_h = [None] + [ez_h[p] + t.odd_swapped(ez_h[p - 1], ez_h[p]) for p in span[1:]]
    ez_x = [None] + [electric[p - 1] for p in span[1:]]
    edge_z = [None] + [ez_x[p] + t.y_down(ez_x[p], ez_x_h[p], 1) for p in span[1:]]
    quarter = 0.25 * dt
    for p in inner:
        place = slice((p - 1) * half, p * half)
        edge_z_h = ez_x_h[p] + t.y_down(ez_x_h[p], ez_x[p], 1)
        for q in range(5):
            fl_out[q, place, :] = halo.main(fields + q, p) + dt * hydro_rate[q, place, :]
        x_rate = hydro_rate[5, place, :] - (t.y_up(edge_z[p], edge_z_h, 1) - edge_z[p])
        y_rate = hydro_rate[6, place, :] + (t.odd(edge_z[p], edge_z[p + 1]) - edge_z[p])
        z_rate = hydro_rate[7, place, :]
        for i, rate in enumerate((x_rate, y_rate, z_rate)):
            fl_out[5 + i, place, :] = halo.main(fields + 5 + i, p) + quarter * rate


def per_device(spacetime, fluid):
    fields, cx, cy, cz = spacetime.shape
    rows = cx * cy
    st = spacetime.reshape(fields, rows, cz)
    fl = fluid.reshape(FLUID, rows, cz)
    sizes = [lax.axis_size(a) for a in ("gx", "gy", "gz")]
    tile = (2 * cy, cz)
    f32 = jnp.float32

    def shape(*dims):
        return jax.ShapeDtypeStruct(dims, f32)

    def beyond(cells):
        n = sizes[2]
        after = lax.ppermute(cells, "gz", [((i + 1) % n, i) for i in range(n)])
        if n == 2:
            return after
        before = lax.ppermute(cells, "gz", [(i, (i + 1) % n) for i in range(n)])
        lane = lax.broadcasted_iota(jnp.int32, cells.shape, 2)
        return jnp.where(lane < cz // 2, after, before)

    def beyond_lanes(packed):
        n = sizes[2]
        after = lax.ppermute(packed, "gz", [((i + 1) % n, i) for i in range(n)])
        if n == 2:
            return after
        before = lax.ppermute(packed, "gz", [(i, (i + 1) % n) for i in range(n)])
        lane = lax.broadcasted_iota(jnp.int32, packed.shape, 2)
        return jnp.where(lane % 4 < 2, before, after)

    params = pltpu.CompilerParams(vmem_limit_bytes=48 * 1024 * 1024)
    zst, zfl = beyond(st), beyond(fl)
    cells = jnp.concatenate([st, fl], axis=0)
    face = shape(face_tiles(fields), *tile)
    corner = shape(CORNER_TILES, *tile)
    lane_row = shape(1, cz)
    def call(kernel, outs, name, operands, scratch=()):
        return pl.pallas_call(
            kernel,
            out_shape=outs,
            scratch_shapes=scratch,
            compiler_params=params,
            name=name,
        )(*operands)

    def shift(cells, step):
        n = lax.axis_size("gx")
        return lax.ppermute(cells, "gx", [(i, (i + step) % n) for i in range(n)])

    def trade(cells, first):
        axis = "gy"
        n = lax.axis_size(axis)
        step = [1, -1] if first else [-1, 1]
        return lax.ppermute(cells, axis, [(i, (i + step[i % 2]) % n) for i in range(n)])

    def two_away(cells, axis):
        n = lax.axis_size(axis)
        return lax.ppermute(cells, axis, [(i, (i + 2) % n) for i in range(n)]) if n == 4 else cells

    short = sizes[0] <= 4 and sizes[2] <= 2
    x_high = call(pack_up_kernel, face, "pack_up", (cells,))
    x_below = shift(x_high, 1)
    x_low, y_first, y_second, top = call(
        pack_kernel, [face, face, face, shape(TOP_TILES, *tile)], "pack", (cells, zst, zfl)
    )
    below_lanes = beyond_lanes(call(lanes_kernel, shape(1, *tile), "lanes", (x_below,)))
    y_first = trade(y_first, True)
    x_above = shift(x_low, -1)
    y_second = trade(y_second, False)
    top_two = two_away(top, "gx")
    chunks, line_top = call(
        relay_kernel,
        [shape(sizes[1], *corner.shape), lane_row],
        "relay",
        (x_below, below_lanes, x_above, y_first, y_second, top, top_two),
    )
    chunks = lax.all_to_all(chunks, "gy", 0, 0)
    if not short:
        line_top = lax.pmax(line_top, ("gx", "gy", "gz"))
    own = cx // 2
    arrived = (cells, zst, zfl, x_below, y_first, x_above, y_second, below_lanes)
    early = call(
        early_kernel,
        [
            shape(*st.shape),
            shape(FLUID, rows, cz),
            shape(CURVED, own, *tile),
            shape(2 * own + 1, *tile),
        ],
        "early",
        arrived,
        [
            pltpu.VMEM((fields, own + 4) + tile, f32),
            pltpu.VMEM((fields, own) + tile, f32),
            pltpu.VMEM((fields, own) + tile, f32),
            pltpu.VMEM((CURVED, own + 2) + tile, f32),
            pltpu.VMEM((CURVED, own) + tile, f32),
            pltpu.VMEM((fields, 3) + tile, f32),
            pltpu.VMEM((CURVED, 6) + tile, f32),
            pltpu.VMEM((fields,) + tile, f32),
            pltpu.VMEM((own, 11) + tile, f32),
        ],
    )
    st_next, fl_next = call(
        late_kernel,
        [shape(*st.shape), shape(*fl.shape)],
        "late",
        (*arrived, chunks, line_top, *early),
    )
    return st_next.reshape(spacetime.shape), fl_next.reshape(fluid.shape)


def solution(mesh):
    spec = P(None, "gx", "gy", "gz")
    return jax.shard_map(
        per_device, mesh=mesh, in_specs=(spec, spec), out_specs=(spec, spec), check_vma=False
    )
```

```python
import functools
import math

import jax
import jax.numpy as jnp
from jax import lax
from jax.experimental import pallas as pl
from jax.experimental.pallas import tpu as pltpu
from jax.sharding import PartitionSpec as P

RECOVERY_STEPS = 4
INDEX_PAIRS = ((0, 0), (0, 1), (0, 2), (1, 1), (1, 2), (2, 2))
COURANT = 0.25
DISSIPATION = 0.2
KAPPA_ONE = 0.02
SHIFT_DAMPING = 1.0
SPEED_CAP = 0.99
PRESSURE_FLOOR = 0.01
FOUR_PI = 4.0 * math.pi

BATCH = 6
CURVED = 11
FLUID = 8


def total(pieces):
    summed = pieces[0]
    for member in pieces[1:]:
        summed = summed + member
    return summed


def dot(first_vec, second_vec):
    return total([first_vec[i] * second_vec[i] for i in range(3)])


def slot_of(i, j):
    return INDEX_PAIRS.index((min(i, j), max(i, j)))


def symmetric(entries):
    return [[entries[slot_of(i, j)] for j in range(3)] for i in range(3)]


def trace_with(inverse, tensor):
    return (
        inverse[0][0] * tensor[0][0]
        + inverse[1][1] * tensor[1][1]
        + inverse[2][2] * tensor[2][2]
        + 2.0
        * (
            inverse[0][1] * tensor[0][1]
            + inverse[0][2] * tensor[0][2]
            + inverse[1][2] * tensor[1][2]
        )
    )


def inverse_metric(metric):
    cofactor = [
        metric[1][1] * metric[2][2] - metric[1][2] * metric[1][2],
        metric[0][2] * metric[1][2] - metric[0][1] * metric[2][2],
        metric[0][1] * metric[1][2] - metric[0][2] * metric[1][1],
        metric[0][0] * metric[2][2] - metric[0][2] * metric[0][2],
        metric[0][1] * metric[0][2] - metric[0][0] * metric[1][2],
        metric[0][0] * metric[1][1] - metric[0][1] * metric[0][1],
    ]
    determinant = (
        metric[0][0] * cofactor[0] + metric[0][1] * cofactor[1] + metric[0][2] * cofactor[2]
    )
    over = 1.0 / determinant
    return symmetric([c * over for c in cofactor])


class Tile:
    def __init__(self, cy, cz):
        self.cy, self.rows, self.lanes = cy, 2 * cy, cz
        shape = (self.rows, cz)
        self.row = lax.broadcasted_iota(jnp.int32, shape, 0)
        self.lane = lax.broadcasted_iota(jnp.int32, shape, 1)
        self.slot = lax.rem(self.row, cy)

    def turn(self, tile, amount):
        amount = amount % self.rows
        return tile if amount == 0 else pltpu.roll(tile, amount, 0)

    def spin(self, tile, amount):
        amount = amount % self.lanes
        return tile if amount == 0 else pltpu.roll(tile, amount, 1)

    def swap(self, tile):
        return self.turn(tile, self.cy)

    def odd(self, a, b):
        return self.turn(jnp.where(self.row < self.cy, b, a), self.cy)

    def odd_swapped(self, a, b):
        return self.turn(jnp.where(self.row < self.cy, a, b), self.cy)

    def y_up(self, main, beyond, k):
        return self.turn(jnp.where(self.slot < k, beyond, main), -k)

    def y_down(self, main, beyond, k):
        return self.turn(jnp.where(self.slot >= self.cy - k, beyond, main), k)

    def z_up(self, main, beyond, k):
        return self.spin(jnp.where(self.lane < k, beyond, main), -k)

    def z_down(self, main, beyond, k):
        return self.spin(jnp.where(self.lane >= self.lanes - k, beyond, main), k)

    def corner_rows(self, side, turn):
        places = ((0, 2), (self.cy - 1, self.cy + 1))[side]
        first, second = [(place + turn) % self.rows for place in places]
        return (self.row == first) | (self.row == second)

    def join_low(self, u, v):
        return jnp.where(self.slot < 2, self.swap(u), self.turn(v, 2))

    def join_high(self, u, v):
        return jnp.where(self.slot >= self.cy - 2, self.swap(u), self.turn(self.swap(v), -2))

    def part_first(self, from_above, from_below):
        return jnp.where(self.slot < 2, from_above, from_below)

    def part_second(self, from_above, from_below):
        return self.turn(jnp.where(self.slot < 2, from_below, from_above), 2)


def edge_list(tiles):
    fields = next(n for n in range(tiles) if face_tiles(n) == tiles)
    return list(range(CURVED)) + list(range(fields, fields + FLUID))


CORNER_TURNS = (0, 1, 4, 5)
TOP_TILES = 2
LINE_TILES = 16
CORNER_TILES = CURVED + FLUID // 4 + 1
TOP_ROW = 6


def face_tiles(fields):
    return fields + FLUID + len(pairs_of(third_list(fields))) + 1


def third_list(fields):
    return list(range(fields + 1))


def pairs_of(items):
    return [(items[i], items[min(i + 1, len(items) - 1)]) for i in range(0, len(items), 2)]


def top_speed(st):
    inverse = inverse_metric(symmetric([st[1 + s] for s in range(6)]))
    scale = 2.0 * st[7] * st[0]
    speeds = [jnp.abs(st[8 + d]) + jnp.sqrt(scale * inverse[d][d]) for d in range(3)]
    top = jnp.maximum(jnp.maximum(speeds[0], speeds[1]), speeds[2])
    return jnp.max(jnp.max(top, axis=1, keepdims=True), axis=0, keepdims=True)


class Chosen:
    def __init__(self, first, second, swapped):
        self.first, self.second, self.swapped, self.shape = first, second, swapped, first.shape

    def __getitem__(self, key):
        return jnp.where(self.swapped, self.second[key], self.first[key])


class Sent:
    def __init__(self, first, second, swapped):
        self.first, self.second, self.swapped, self.shape = first, second, swapped, first.shape

    def put(self, key, lower, upper):
        self.first[key] = jnp.where(self.swapped, upper, lower)
        self.second[key] = jnp.where(self.swapped, lower, upper)


class Joined:
    def __init__(self, tiles, tail):
        self.tiles, self.tail = tiles, tail
        self.shape = tuple(tiles.shape)

    def __getitem__(self, key):
        q, rows = (key[0], key[1:]) if isinstance(key, tuple) else (key, ())
        if q == self.tiles.shape[0] - 1:
            return self.tail[(0,) + rows]
        return self.tiles[(q,) + rows]


def even_along_y(tile):
    return jnp.full(tile, lax.rem(lax.axis_index("gy"), 2), jnp.int32) == 0


def pack_up_kernel(cells, x_high):
    count, rows, lanes = cells.shape
    fields, half = count - FLUID, rows // 2
    t = Tile(rows // 4, lanes)
    for q in range(count):
        x_high[q] = cells[q, half:rows, :]
    for n, (a, b) in enumerate(pairs_of(list(range(fields)) + [fields + 5])):
        x_high[count + n] = jnp.where(
            t.row < t.cy, t.swap(cells[b, 0:half, :]), cells[a, 0:half, :]
        )
    x_high[x_high.shape[0] - 1] = jnp.broadcast_to(top_speed(cells), t.row.shape)


def lanes_kernel(x_below, out):
    t = Tile(x_below.shape[1] // 2, x_below.shape[2])
    last = x_below.shape[0] - 1
    packed = x_below[last]
    for place, q in enumerate(edge_list(x_below.shape[0])):
        piece = t.spin(x_below[q], 4 * place + 2)
        here = (t.lane >= 4 * place) & (t.lane < 4 * place + 4)
        packed = jnp.where(here, piece, packed)
    out[0] = packed


def pack_kernel(cells, zst, zfl, *outs):
    fields, rows, lanes = zst.shape
    st, fl = cells.at[0:fields], cells.at[fields : fields + FLUID]
    cy = rows // 4
    t = Tile(cy, lanes)
    x_low, y_first, y_second, top_out = outs
    half = t.rows
    to_y = Sent(y_first, y_second, even_along_y((half, lanes)))

    def own(ref, q):
        return [ref[q, 0:half, :], ref[q, half : 2 * half, :]]

    tiles, beyond = [], []
    for q in range(fields):
        tiles.append(own(st, q))
        beyond.append(own(zst, q) if q < CURVED else None)
    for q in range(FLUID):
        tiles.append(own(fl, q))
        beyond.append(own(zfl, q))

    packed = [None] * 4
    place_count = 0
    for q, (first, second) in enumerate(tiles):
        x_low[q] = first
        to_y.put(q, t.join_low(first, second), t.join_high(first, second))
        if beyond[q] is not None:
            zf, zs = beyond[q]
            for m, piece in enumerate((zf, zs, t.join_low(zf, zs), t.join_high(zf, zs))):
                piece = t.spin(piece, 4 * place_count + 2)
                packed[m] = (
                    piece if place_count == 0 else jnp.where(t.lane < 4 * place_count, packed[m], piece)
                )
            place_count += 1
    for n, (a, b) in enumerate(pairs_of(third_list(fields))):
        slot = fields + FLUID + n
        xa, xb = (tiles[q if q < fields else fields + 5] for q in (a, b))
        x_low[slot] = jnp.where(t.row < cy, xa[1], t.swap(xb[1]))
        ya, yb = (tiles[q if q < fields else fields + 6] for q in (a, b))
        w = [t.swap(ya[0]), t.swap(ya[1]), t.swap(yb[0]), t.swap(yb[1])]
        s = t.slot
        low = jnp.where(s == 0, t.turn(w[2], -2), t.turn(w[3], -1))
        low = jnp.where(s == 2, w[0], jnp.where(s == 3, t.turn(w[1], 1), low))
        high = jnp.where(s == 3, t.turn(w[2], 2), t.turn(w[3], 1))
        high = jnp.where(s == 1, w[0], jnp.where(s == 0, t.turn(w[1], -1), high))
        to_y.put(slot, low, high)
    top = jnp.maximum(top_speed(st), top_speed(zst))
    top_out[...] = jnp.broadcast_to(top, top_out.shape)
    last = x_low.shape[0] - 1
    x_lanes = [jnp.where(t.lane < 4 * place_count, piece, top) for piece in packed[:2]]
    y_lanes = [jnp.where(t.lane < 4 * place_count, piece, top) for piece in packed[2:]]
    x_low[last] = x_lanes[0]
    to_y.put(last, *y_lanes)


def relay_kernel(x_below, below_lanes, x_above, top, top_two, c_first, c_second, line_top):
    cy, lanes = x_below.shape[1] // 2, x_below.shape[2]
    t = Tile(cy, lanes)
    to_y = Sent(c_first, c_second, even_along_y((t.rows, lanes)))
    last = x_below.shape[0] - 1
    line = jnp.maximum(top[0, 0:1, :], top_two[0, 0:1, :])
    line = jnp.maximum(line, x_below[last, 0:1, lanes - 1 : lanes])
    x_below = Joined(x_below, below_lanes)
    for beside in (x_below, x_above):
        line = jnp.maximum(line, beside[last, 0:1, lanes - 1 : lanes])
    line_top[...] = jnp.broadcast_to(line, line_top.shape)
    edge = edge_list(x_below.shape[0])
    for q in range(CURVED):
        below, above = x_below[q], x_above[q]
        to_y.put(q, t.join_low(below, above), t.join_high(below, above))
    for n in range(0, FLUID, 4):
        low, high = None, None
        for turn, q in zip(CORNER_TURNS, edge[CURVED + n : CURVED + n + 4]):
            below, above = x_below[q], x_above[q]
            below, above = (t.turn(j(below, above), turn) for j in (t.join_low, t.join_high))
            if low is None:
                low, high = below, above
            else:
                low = jnp.where(t.corner_rows(0, turn), below, low)
                high = jnp.where(t.corner_rows(1, turn), above, high)
        to_y.put(CURVED + n // 4, low, high)
    along_x, along_y = edge[CURVED + 5], edge[CURVED + 6]
    low = t.join_low(x_below[along_y], x_above[along_y])
    high = t.join_high(x_below[along_x], x_above[along_x])
    low, high = (jnp.where(t.row == TOP_ROW, line, tile) for tile in (low, high))
    to_y.put(CORNER_TILES - 1, low, high)


def limited(a, b):
    return jnp.maximum(jnp.minimum(a, b), 0.0) + jnp.minimum(jnp.maximum(a, b), 0.0)


def recover(conserved, magnetic):
    density = conserved[0]
    momenta = conserved[1:4]
    energy = conserved[4] + density
    mom_sq = dot(momenta, momenta)
    mag_sq = dot(magnetic, magnetic)
    cross = dot(momenta, magnetic)
    cross_sq = cross * cross

    def state(z):
        grown = z + mag_sq
        over = 1.0 / (z * grown)
        speed_sq = (mom_sq * z * z + cross_sq * (2.0 * z + mag_sq)) * over * over
        kept = 1.0 - jnp.minimum(speed_sq, SPEED_CAP)
        rest = density * jnp.sqrt(kept)
        return kept, rest, 0.5 * (z * kept - rest), grown * over

    z = jnp.maximum(energy - 0.5 * mag_sq, density)
    for _ in range(RECOVERY_STEPS):
        kept, rest, pressure, over_z = state(z)
        residual = (
            z
            + mag_sq
            - pressure
            - 0.5 * mag_sq * kept
            - 0.5 * cross_sq * over_z * over_z
            - energy
        )
        z = jnp.maximum(z - residual / (1.0 - 0.5 * kept), density)
    kept, rest, pressure, over_z = state(z)
    pressure = jnp.maximum(pressure, PRESSURE_FLOOR * rest)
    scale = lax.rsqrt(kept) / (z + mag_sq)
    along = cross * over_z
    four_vel = [scale * (momenta[i] + along * magnetic[i]) for i in range(3)]
    return [rest, pressure] + four_vel


def stress_parts(rest, pressure, u, magnetic):
    lorentz_sq = 1.0 + dot(u, u)
    over = lax.rsqrt(lorentz_sq)
    over_sq = over * over
    time_b = dot(u, magnetic)
    grown_b = [magnetic[i] + time_b * u[i] for i in range(3)]
    b_square = (dot(magnetic, magnetic) + time_b * time_b) * over_sq
    enthalpy = rest + 2.0 * pressure
    inertia = enthalpy + b_square
    return lorentz_sq, over, over_sq, time_b, grown_b, b_square, enthalpy, inertia


def face_state(rest, pressure, u, magnetic, d):
    lorentz_sq, over, over_sq, time_b, grown_b, b_square, enthalpy, inertia = stress_parts(
        rest, pressure, u, magnetic
    )
    total_pressure = pressure + 0.5 * b_square
    lorentz = lorentz_sq * over
    density = rest * lorentz
    carried = inertia * lorentz
    time_over = time_b * over
    conserved = [density]
    conserved += [carried * u[j] - time_over * grown_b[j] for j in range(3)]
    conserved += [inertia * lorentz_sq - total_pressure - time_b * time_b - density]
    mass_flux = rest * u[d]
    flux = [mass_flux]
    pushed = inertia * u[d]
    b_over = grown_b[d] * over_sq
    for j in range(3):
        flux_j = pushed * u[j] - b_over * grown_b[j]
        flux.append(flux_j + total_pressure if j == d else flux_j)
    flux.append(carried * u[d] - time_over * grown_b[d] - mass_flux)
    ratio = 1.0 / (enthalpy * inertia)
    sound_sq = 2.0 * pressure * inertia * ratio
    alfven_sq = b_square * enthalpy * ratio
    fast_sq = sound_sq + alfven_sq - sound_sq * alfven_sq
    slow = 1.0 - fast_sq
    velocity = u[d] * over
    rest_part = 1.0 - dot(u, u) * over_sq * fast_sq
    spread = jnp.sqrt(fast_sq * over_sq * (rest_part - velocity * velocity * slow))
    fastest = (jnp.abs(velocity * slow) + spread) / rest_part
    return conserved, flux, fastest


def face_flux(left, right, normal, weight, d):
    sides = []
    for state in (left, right):
        magnetic = [normal if i == d else state[5 + i] for i in range(3)]
        sides.append(face_state(state[0], state[1], state[2:5], magnetic, d))
    (cons_l, flux_l, fast_l), (cons_r, flux_r, fast_r) = sides
    signal = jnp.maximum(fast_l, fast_r)
    scale = 0.5 * weight
    return [scale * (flux_l[q] + flux_r[q] - signal * (cons_r[q] - cons_l[q])) for q in range(5)]


def volume_over(conformal):
    return conformal * jnp.sqrt(conformal)


def first_diff(down_two, down, up, up_two):
    return (8.0 / 12.0) * (up - down) + (1.0 / 12.0) * (down_two - up_two)


class Halo:
    def __init__(self, cells, zst, zfl, x_below, y_first, x_above, y_second, below_lanes, *corners):
        x_below = Joined(x_below, below_lanes)
        self.fields, self.block, self.lanes = zst.shape
        even_y = even_along_y((self.block // 2, self.lanes))
        y_below, y_above = Chosen(y_first, y_second, even_y), Chosen(y_second, y_first, even_y)
        if corners:
            c_first, c_second = corners
            self.c_below = Chosen(c_first, c_second, even_y)
            self.c_above = Chosen(c_second, c_first, even_y)
        self.st = cells.at[0 : self.fields]
        self.fl = cells.at[self.fields : self.fields + FLUID]
        self.zst, self.zfl = zst, zfl
        self.x_below, self.x_above = x_below, x_above
        self.y_below, self.y_above = y_below, y_above
        self.cy = self.block // 4
        self.t = Tile(self.cy, self.lanes)
        self.half = self.t.rows
        self.own = self.block // self.half
        self.inner = range(1, self.own + 1)
        self.span = range(self.own + 2)
        self.edge = edge_list(x_below.shape[0])
        self.last = x_below.shape[0] - 1

    def rows_of(self, ref, q, p):
        return ref[q, (p - 1) * self.half : p * self.half, :]

    def main(self, q, p):
        if q < self.fields:
            return self.rows_of(self.st, q, p)
        return self.rows_of(self.fl, q - self.fields, p)

    def beyond(self, q, p):
        if q < self.fields:
            return self.rows_of(self.zst, q, p)
        return self.rows_of(self.zfl, q - self.fields, p)

    def part(self, second):
        return self.t.part_second if second else self.t.part_first

    def beside(self, q, p):
        return self.part(p == 2)(self.y_above[q], self.y_below[q])

    def third_place(self, q):
        return self.fields + FLUID + q // 2, q % 2

    def x_third(self, q, upper):
        tile, which = self.third_place(q)
        found = self.x_above[tile] if upper else self.x_below[tile]
        return self.t.swap(found) if which else found

    def y_third(self, q, p):
        t = self.t
        tile, which = self.third_place(q)
        turn_above, turn_below = ((0, 0), (-1, 1), (2, -2), (1, -1))[2 * which + p - 1]
        above, below = t.turn(self.y_above[tile], turn_above), t.turn(self.y_below[tile], turn_below)
        return jnp.where(t.slot == 2, above, below)

    def z_place(self, q):
        return 4 * self.edge.index(q) + 2

    def x_beyond(self, q, upper):
        tile = self.x_above[self.last] if upper else self.x_below[self.last]
        return self.t.spin(tile, -self.z_place(q))

    def y_beyond(self, q, p):
        return self.t.spin(self.beside(self.last, p), -self.z_place(q))

    def corner(self, q, p):
        place, turn = q, 0
        if q >= CURVED:
            n = q - self.fields
            place, turn = CURVED + n // 4, CORNER_TURNS[n % 4]
        above, below = self.t.turn(self.c_above[place], -turn), self.t.turn(self.c_below[place], -turn)
        return self.part(p > 0)(above, below)

    def corner_layers(self, p):
        place = CORNER_TILES - 1
        return self.part(p > 0)(self.c_above[place], self.c_below[place])

    def plane(self, q):
        inner = self.inner
        return (
            [self.x_below[q]] + [self.main(q, p) for p in inner] + [self.x_above[q]],
            [None] + [self.beside(q, p) for p in inner] + [None],
            [self.x_beyond(q, False)]
            + [self.beyond(q, p) for p in inner]
            + [self.x_beyond(q, True)],
            [None] + [self.y_beyond(q, p) for p in inner] + [None],
        )


def weigh(chi_face, alpha_face):
    shrink = volume_over(chi_face)
    return shrink, alpha_face / shrink


def primitives(half, spots, cons, centred, chi, alpha, batch):
    found = {}
    for start in range(0, len(spots), batch):
        group = spots[start : start + batch]

        def gather(planes):
            return jnp.concatenate([planes[k][p] for k, p in group], axis=0)

        shrink = volume_over(gather(chi))
        mag_raw = [gather(centred[i]) for i in range(3)]
        mag = [m * shrink for m in mag_raw]
        values = recover([gather(c) * shrink for c in cons], mag)
        u = values[2:5]
        factor = gather(alpha) * lax.rsqrt(1.0 + dot(u, u))
        field = [
            factor * (u[(i + 2) % 3] * mag_raw[(i + 1) % 3] - u[(i + 1) % 3] * mag_raw[(i + 2) % 3])
            for i in range(3)
        ]
        for n, spot in enumerate(group):
            found[spot] = [value[n * half : (n + 1) * half] for value in values + mag + field]
    return found


def ring_fluxes(prims, chi, alpha, normals, d, up, down):
    found = []
    for here, there in ((0, 1), (1, 0)):
        left, right = [], []
        for a, b in zip(prims[here], prims[there]):
            below = down(a, b, 1)
            middle = a - below
            left.append(below + 0.5 * limited(below - down(a, b, 2), middle))
            right.append(a - 0.5 * limited(middle, up(a, b, 1) - a))
        shrink, weight = weigh(
            0.5 * (chi[here] + down(chi[here], chi[there], 1)),
            0.5 * (alpha[here] + down(alpha[here], alpha[there], 1)),
        )
        found.append(face_flux(left, right, normals[here] * shrink, weight, d))
    return [a - up(a, b, 1) for a, b in zip(*found)]


def early_kernel(
    cells, zst, zfl, x_below, y_first, x_above, y_second, below_lanes,
    st_rate, hydro_rate, slopes, electric, pairs, sides, thirds, pairs_z, sides_z, grads, seconds, damped, tensors,
):
    halo = Halo(cells, zst, zfl, x_below, y_first, x_above, y_second, below_lanes)
    t, fields, half, own, cy = halo.t, halo.fields, halo.half, halo.own, halo.cy
    st, fl, inner = halo.st, halo.fl, halo.inner

    for q in range(fields):
        pairs[q, 0] = halo.x_third(q, False)
        pairs[q, 1] = x_below[q]
        for p in inner:
            pairs[q, 1 + p] = halo.main(q, p)
            sides[q, p - 1] = halo.beside(q, p)
            thirds[q, p - 1] = halo.y_third(q, p)
        pairs[q, 2 + own] = x_above[q]
        pairs[q, 3 + own] = halo.x_third(q, True)
        if q < CURVED:
            pairs_z[q, 0] = halo.x_beyond(q, False)
            pairs_z[q, own + 1] = halo.x_beyond(q, True)
            for p in inner:
                pairs_z[q, p] = halo.beyond(q, p)
                sides_z[q, p - 1] = halo.y_beyond(q, p)

    span = halo.span
    face = [halo.plane(fields + 5 + i) for i in range(3)]

    def halves(kind, p):
        own_x, own_y, own_z = (f[kind][p] for f in face)
        pair = kind in (0, 2)
        known_x = pair or p < own
        last = kind == 0 and p == own + 1
        if pair:
            next_x = halo.x_third(fields, True) if last else face[0][kind][min(p + 1, own + 1)]
            next_x = t.odd(own_x, next_x)
        else:
            next_x = t.odd_swapped(own_x, face[0][kind][p + 1] if known_x else own_x)
        dx = 0.5 * (next_x - own_x)
        dz = 0.5 * (t.z_up(own_z, face[2][kind ^ 2][p], 1) - own_z)
        inside = 1 <= p <= own
        if not pair:
            here = jnp.where(t.slot == 2, halo.y_third(fields, p), own_y) if kind == 1 else own_y
            next_y = t.y_up(here, face[1][kind ^ 1][p], 1)
        else:
            next_y = t.y_up(own_y, face[1][kind ^ 1][p] if inside else own_y, 1)
        dy = 0.5 * (next_y - own_y)
        if pair and not inside:
            dy = jnp.where(t.slot == cy - 1, -(dx + dz), dy)
        if not pair and not known_x:
            dx = jnp.where(t.row < cy, -(dy + dz), dx)
        return own_x + dx, own_y + dy, own_z + dz

    spots = [(0, p) for p in span] + [(1, p) for p in inner]
    spots += [(2, p) for p in span] + [(3, p) for p in inner]
    centred = [[[None] * (own + 2) for _ in range(4)] for _ in range(3)]
    for k, p in spots:
        for i, value in enumerate(halves(k, p)):
            centred[i][k][p] = value
    chi, alpha = halo.plane(0), halo.plane(7)
    found = primitives(
        half, spots, [halo.plane(fields + q) for q in range(5)], centred, chi, alpha, BATCH
    )

    lines = [[found[0, p][i] for p in span] for i in range(8)] + [chi[0], alpha[0]]
    odd_lines = [[t.odd(f[p], f[min(p + 1, own + 1)]) for p in span] for f in lines]
    fluxes = [None]
    for p in range(1, own + 2):
        left, right = [], []
        for f, o in zip(lines[:8], odd_lines):
            here = f[p] - o[p - 1]
            left.append(o[p - 1] + 0.5 * limited(o[p - 1] - f[p - 1], here))
            right.append(f[p] - 0.5 * limited(here, o[p] - f[p]))
        shrink, weight = weigh(
            0.5 * (lines[8][p] + odd_lines[8][p - 1]), 0.5 * (lines[9][p] + odd_lines[9][p - 1])
        )
        fluxes.append(face_flux(left, right, face[0][0][p] * shrink, weight, 0))
    for p in inner:
        changes = [
            ring_fluxes(
                [found[k, p][:8] for k in (0, kind)],
                [chi[k][p] for k in (0, kind)],
                [alpha[k][p] for k in (0, kind)],
                [face[d][k][p] for k in (0, kind)],
                d,
                up,
                down,
            )
            for d, kind, up, down in ((1, 1, t.y_up, t.y_down), (2, 2, t.z_up, t.z_down))
        ]
        for q in range(5):
            change = fluxes[p][q] - t.odd(fluxes[p][q], fluxes[p + 1][q])
            tensors[p - 1, 6 + q] = change + changes[0][q] + changes[1][q]
        rest, pressure = found[0, p][:2]
        u = found[0, p][2:5]
        parts = stress_parts(rest, pressure, u, found[0, p][5:8])
        lorentz_sq, over, over_sq, time_b, grown_b, b_square, enthalpy, inertia = parts
        total_pressure = pressure + 0.5 * b_square
        for s, (i, j) in enumerate(INDEX_PAIRS):
            value = inertia * u[i] * u[j] - over_sq * (grown_b[i] * grown_b[j])
            tensors[p - 1, s] = value + total_pressure if i == j else value

    ex, ey, ez = (
        [[found[k, p][8 + i] if (k, p) in found else None for p in span] for k in range(4)]
        for i in range(3)
    )
    ey_x = [
        [ey[k][p] + t.odd(ey[k][p - 1], ey[k][p]) if p else None for p in span] for k in (0, 2)
    ]
    edge_y = [None] + [ey_x[0][p] + t.z_down(ey_x[0][p], ey_x[1][p], 1) for p in span[1:]]
    for p in span[1:]:
        electric[p - 1] = ez[0][p] + t.odd(ez[0][p - 1], ez[0][p])
    for p in inner:
        electric[own + p] = ez[1][p]
        edge_y_z = ey_x[1][p] + t.z_down(ey_x[1][p], ey_x[0][p], 1)
        ex_y = ex[0][p] + t.y_down(ex[0][p], ex[1][p], 1)
        ex_y_h = ex[1][p] + t.y_down(ex[1][p], ex[0][p], 1)
        ex_y_z = ex[2][p] + t.y_down(ex[2][p], ex[3][p], 1)
        ex_y_hz = ex[3][p] + t.y_down(ex[3][p], ex[2][p], 1)
        edge_x = ex_y + t.z_down(ex_y, ex_y_z, 1)
        edge_x_h = ex_y_h + t.z_down(ex_y_h, ex_y_hz, 1)
        edge_x_z = ex_y_z + t.z_down(ex_y_z, ex_y, 1)
        place = slice((p - 1) * half, p * half)
        hydro_rate[5, place, :] = t.z_up(edge_y[p], edge_y_z, 1) - edge_y[p]
        hydro_rate[6, place, :] = edge_x - t.z_up(edge_x, edge_x_z, 1)
        hydro_rate[7, place, :] = (t.y_up(edge_x, edge_x_h, 1) - edge_x) - (
            t.odd(edge_y[p], edge_y[p + 1]) - edge_y[p]
        )

    def pair_step(index):
        p = index + 1
        base = index * half

        for q in range(fields):
            centre = pairs[q, p + 1]
            x_m3 = t.odd(pairs[q, p - 1], pairs[q, p])
            x_m2 = pairs[q, p]
            x_m1 = t.odd(pairs[q, p], centre)
            x_p1 = t.odd(centre, pairs[q, p + 2])
            x_p2 = pairs[q, p + 2]
            x_p3 = t.odd(pairs[q, p + 2], pairs[q, p + 3])
            side, third = sides[q, index], thirds[q, index]
            y_m1, y_m2 = t.y_down(centre, side, 1), t.y_down(centre, side, 2)
            y_p1, y_p2 = t.y_up(centre, side, 1), t.y_up(centre, side, 2)
            y_m3 = t.turn(
                jnp.where(t.slot >= cy - 2, side, jnp.where(t.slot == cy - 3, third, centre)), 3
            )
            y_p3 = t.turn(jnp.where(t.slot < 2, side, jnp.where(t.slot == 2, third, centre)), -3)
            beyond = zst[q, pl.ds(base, half), :]
            z_m1, z_m2, z_m3 = (t.z_down(centre, beyond, k) for k in (1, 2, 3))
            z_p1, z_p2, z_p3 = (t.z_up(centre, beyond, k) for k in (1, 2, 3))
            dx = first_diff(x_m2, x_m1, x_p1, x_p2)
            dy = first_diff(y_m2, y_m1, y_p1, y_p2)
            grads[q, 0] = dx
            if q < CURVED:
                slopes[q, index] = dx
            grads[q, 1] = dy
            grads[q, 2] = first_diff(z_m2, z_m1, z_p1, z_p2)
            near = [x_m1 + x_p1, y_m1 + y_p1, z_m1 + z_p1]
            far = [x_m2 + x_p2, y_m2 + y_p2, z_m2 + z_p2]
            outer = (x_m3 + x_p3) + (y_m3 + y_p3) + (z_m3 + z_p3)
            damped[q] = (DISSIPATION / 64.0) * (
                outer - 6.0 * (far[0] + far[1] + far[2]) + 15.0 * (near[0] + near[1] + near[2])
                - 60.0 * centre
            )
            if q < CURVED:
                for s, d in ((0, 0), (3, 1), (5, 2)):
                    seconds[q, s] = (1.0 / 12.0) * (16.0 * near[d] - far[d] - 30.0 * centre)
                b_m, b_c, b_p = pairs_z[q, p - 1], pairs_z[q, p], pairs_z[q, p + 1]
                dx_z = first_diff(b_m, t.odd(b_m, b_c), t.odd(b_c, b_p), b_p)
                b_s = sides_z[q, p - 1]
                dy_z = first_diff(
                    t.y_down(b_c, b_s, 2),
                    t.y_down(b_c, b_s, 1),
                    t.y_up(b_c, b_s, 1),
                    t.y_up(b_c, b_s, 2),
                )
                for s, inside, outside in ((2, dx, dx_z), (4, dy, dy_z)):
                    seconds[q, s] = first_diff(
                        t.z_down(inside, outside, 2),
                        t.z_down(inside, outside, 1),
                        t.z_up(inside, outside, 1),
                        t.z_up(inside, outside, 2),
                    )

        def value(q):
            return pairs[q, p + 1]

        def fluid_value(q):
            return fl[q, pl.ds(base, half), :]

        conformal, lapse = value(0), value(7)
        over_chi = 1.0 / conformal
        metric = symmetric([value(1 + s) for s in range(6)])
        shift = [value(8 + i) for i in range(3)]
        extrinsic, theta = value(11), value(21)
        traceless = symmetric([value(12 + s) for s in range(6)])
        connection = [value(18 + i) for i in range(3)]
        inverse = inverse_metric(metric)
        grad = [[grads[q, k] for k in range(3)] for q in range(fields)]
        chi_grad, lapse_grad = grad[0], grad[7]
        shift_grad = [[grad[8 + i][k] for i in range(3)] for k in range(3)]
        trace_k = extrinsic + 2.0 * theta

        stress = symmetric([tensors[p - 1, s] for s in range(6)])
        held = [fluid_value(q) for q in range(5)]
        shrink = volume_over(conformal)
        energy = held[4] + held[0]
        third_k = trace_k * (1.0 / 3.0)
        curved = [
            [
                (traceless[i][j] + metric[i][j] * third_k) if i <= j else None for j in range(3)
            ]
            for i in range(3)
        ]
        work = (
            stress[0][0] * curved[0][0]
            + stress[1][1] * curved[1][1]
            + stress[2][2] * curved[2][2]
            + 2.0
            * (
                stress[0][1] * curved[0][1]
                + stress[0][2] * curved[0][2]
                + stress[1][2] * curved[1][2]
            )
        )
        rates = [tensors[p - 1, 6 + q] for q in range(5)]
        for i in range(3):
            rates[1 + i] = (
                rates[1 + i]
                - energy * lapse_grad[i]
                + total([held[1 + k] * grad[8 + k][i] for k in range(3)])
            )
        rates[4] = (
            rates[4] + lapse * work * over_chi / shrink - dot(held[1:4], lapse_grad)
        )
        for q in range(5):
            hydro_rate[q, pl.ds(base, half), :] = rates[q]
        density = energy * shrink
        momentum = [held[1 + i] * shrink for i in range(3)]

        lowered = [[[None] * 3 for _ in range(3)] for _ in range(3)]
        for i in range(3):
            for j in range(3):
                for k in range(j, 3):
                    got = 0.5 * (
                        grad[1 + slot_of(i, k)][j]
                        + grad[1 + slot_of(i, j)][k]
                        - grad[1 + slot_of(j, k)][i]
                    )
                    lowered[i][j][k] = lowered[i][k][j] = got
        raised = [[[None] * 3 for _ in range(3)] for _ in range(3)]
        for i in range(3):
            for j in range(3):
                for k in range(j, 3):
                    got = total([inverse[i][l] * lowered[l][j][k] for l in range(3)])
                    raised[i][j][k] = raised[i][k][j] = got
        contracted = [trace_with(inverse, raised[i]) for i in range(3)]

        def hessian_trace(q):
            return (
                inverse[0][0] * seconds[q, 0]
                + inverse[1][1] * seconds[q, 3]
                + inverse[2][2] * seconds[q, 5]
                + 2.0 * (inverse[0][2] * seconds[q, 2] + inverse[1][2] * seconds[q, 4])
            )

        def second_cov(q, slope):
            bent = [total([raised[k][i][j] * slope[k] for k in range(3)]) for i, j in INDEX_PAIRS]
            return symmetric(
                [-bent[s] if s == 1 else seconds[q, s] - bent[s] for s in range(len(bent))]
            )

        chi_cov = second_cov(0, chi_grad)
        chi_lap = trace_with(inverse, chi_cov)
        raised_chi = [dot(inverse[i], chi_grad) for i in range(3)]
        chi_square = dot(raised_chi, chi_grad)
        cross_term = dot(raised_chi, lapse_grad)
        half_chi = 0.5 * over_chi
        plain_cov = second_cov(7, lapse_grad)
        lapse_cov = symmetric(
            [
                plain_cov[i][j]
                + (
                    chi_grad[i] * lapse_grad[j]
                    + chi_grad[j] * lapse_grad[i]
                    - metric[i][j] * cross_term
                )
                * half_chi
                for i, j in INDEX_PAIRS
            ]
        )
        lapse_lap = conformal * trace_with(inverse, lapse_cov)

        mixed = [
            [[dot(inverse[l], lowered[k][j]) for j in range(3)] for k in range(3)]
            for l in range(3)
        ]
        quarter_sq = half_chi * half_chi
        metric_factor = chi_lap * half_chi - 3.0 * chi_square * quarter_sq
        ricci = []
        for i, j in INDEX_PAIRS:
            second_part = -0.5 * hessian_trace(1 + slot_of(i, j))
            connection_part = 0.5 * total(
                [metric[k][i] * grad[18 + k][j] + metric[k][j] * grad[18 + k][i] for k in range(3)]
            )
            contracted_part = 0.5 * total(
                [contracted[k] * (lowered[i][j][k] + lowered[j][i][k]) for k in range(3)]
            )
            if i == j:
                quadratic = total(
                    [
                        raised[k][l][i] * (2.0 * mixed[l][i][k] + mixed[l][k][i])
                        for k in range(3)
                        for l in range(3)
                    ]
                )
            else:
                quadratic = total(
                    [
                        raised[k][l][i] * (mixed[l][j][k] + mixed[l][k][j])
                        + raised[k][l][j] * mixed[l][i][k]
                        for k in range(3)
                        for l in range(3)
                    ]
                )
            conformal_part = (
                chi_cov[i][j] * half_chi
                + metric[i][j] * metric_factor
                - chi_grad[i] * chi_grad[j] * quarter_sq
            )
            ricci.append(
                second_part + connection_part + contracted_part + quadratic + conformal_part
            )
        ricci = symmetric(ricci)
        ricci_scalar = conformal * trace_with(inverse, ricci)
        stress_trace = conformal * trace_with(inverse, stress)

        up_a = [
            [total([inverse[i][k] * traceless[k][j] for k in range(3)]) for j in range(3)]
            for i in range(3)
        ]
        raised_a = symmetric(
            [total([up_a[i][l] * inverse[j][l] for l in range(3)]) for i, j in INDEX_PAIRS]
        )
        a_square = trace_with(traceless, raised_a)
        shift_div = shift_grad[0][0] + shift_grad[1][1] + shift_grad[2][2]
        two_thirds_div = (2.0 / 3.0) * shift_div

        def finish(q, rate):
            rate = rate + dot(shift, grad[q]) + damped[q]
            st_rate[q, pl.ds(base, half), :] = rate

        finish(0, (2.0 / 3.0) * conformal * (lapse * trace_k - shift_div))
        finish(7, -2.0 * lapse * extrinsic)
        for i in range(3):
            finish(8 + i, 0.75 * connection[i] - SHIFT_DAMPING * shift[i])
        finish(
            11,
            lapse
            * (
                a_square
                + trace_k * trace_k * (1.0 / 3.0)
                + FOUR_PI * (stress_trace + density)
                + KAPPA_ONE * theta
            )
            - lapse_lap,
        )
        source = symmetric(
            [
                lapse * (ricci[i][j] - 2.0 * FOUR_PI * stress[i][j]) - lapse_cov[i][j]
                for i, j in INDEX_PAIRS
            ]
        )
        third_trace = trace_with(inverse, source) * (1.0 / 3.0)
        for s, (i, j) in enumerate(INDEX_PAIRS):
            finish(
                1 + s,
                total(
                    [
                        metric[i][k] * shift_grad[j][k] + metric[j][k] * shift_grad[i][k]
                        for k in range(3)
                    ]
                )
                - metric[i][j] * two_thirds_div
                - 2.0 * lapse * traceless[i][j],
            )
            product = total([traceless[i][k] * up_a[k][j] for k in range(3)])
            finish(
                12 + s,
                total(
                    [
                        traceless[i][k] * shift_grad[j][k] + traceless[j][k] * shift_grad[i][k]
                        for k in range(3)
                    ]
                )
                - traceless[i][j] * two_thirds_div
                + conformal * (source[i][j] - metric[i][j] * third_trace)
                + lapse * (trace_k * traceless[i][j] - 2.0 * product),
            )
        for i in range(3):
            bracket = (
                trace_with(raised_a, raised[i])
                - 1.5 * dot(raised_a[i], chi_grad) * over_chi
                - dot(inverse[i], [2.0 * grad[11][j] + grad[21][j] for j in range(3)]) * (1.0 / 3.0)
                - 2.0 * FOUR_PI * dot(inverse[i], momentum)
            )
            spread = [
                seconds[8, 0] + seconds[10, 2],
                seconds[9, 3] + seconds[10, 4],
                seconds[8, 2] + seconds[9, 4] + seconds[10, 5],
            ]
            finish(
                18 + i,
                contracted[i] * two_thirds_div
                - total([contracted[j] * shift_grad[j][i] for j in range(3)])
                + hessian_trace(8 + i)
                + dot(inverse[i], spread) * (1.0 / 3.0)
                - 2.0 * dot(raised_a[i], lapse_grad)
                + 2.0
                * lapse
                * (bracket - KAPPA_ONE * (connection[i] - contracted[i])),
            )
        finish(
            21,
            0.5
            * lapse
            * (
                ricci_scalar
                - a_square
                + (2.0 / 3.0) * trace_k * trace_k
                - 4.0 * FOUR_PI * density
            )
            - 2.0 * KAPPA_ONE * lapse * theta,
        )

    for index in range(own):
        pair_step(index)


def late_kernel(
    cells, zst, zfl, x_below, y_first, x_above, y_second, below_lanes, c_first, c_second, line_two, line_top,
    st_rate, hydro_rate, slopes, electric, st_out, fl_out,
):
    halo = Halo(
        cells, zst, zfl, x_below, y_first, x_above, y_second, below_lanes, c_first, c_second
    )
    x_below, x_above = halo.x_below, halo.x_above
    t, fields, half, own = halo.t, halo.fields, halo.half, halo.own
    inner, span = halo.inner, halo.span

    top = jnp.maximum(line_top[0, 0:1, :], line_two[0, 0:1, :])
    for lines in (c_first, c_second):
        top = jnp.maximum(top, lines[CORNER_TILES - 1, TOP_ROW : TOP_ROW + 1, :])
    dt = COURANT / top

    for p in inner:
        place = slice((p - 1) * half, p * half)
        mixed = []
        for q in range(CURVED):
            s_m, s_c, s_p = (
                halo.beside(q, n) if 1 <= n <= own else halo.corner(q, n) for n in (p - 1, p, p + 1)
            )
            slope = slopes[q, p - 1]
            slope_side = first_diff(s_m, t.odd_swapped(s_m, s_c), t.odd_swapped(s_c, s_p), s_p)
            mixed.append(
                first_diff(
                    t.y_down(slope, slope_side, 2),
                    t.y_down(slope, slope_side, 1),
                    t.y_up(slope, slope_side, 1),
                    t.y_up(slope, slope_side, 2),
                )
            )
        conformal, lapse = halo.main(0, p), halo.main(7, p)
        metric = [halo.main(1 + s, p) for s in range(6)]
        inverse = inverse_metric(symmetric(metric))
        half_chi = 0.5 / conformal
        cross = inverse[0][1]
        chi_trace = 2.0 * cross * mixed[0] * half_chi
        ricci = [metric[s] * chi_trace - cross * mixed[1 + s] for s in range(6)]
        ricci[1] = ricci[1] + mixed[0] * half_chi
        source = [lapse * r for r in ricci]
        source[1] = source[1] - mixed[7]
        third_trace = trace_with(inverse, symmetric(source)) * (1.0 / 3.0)
        extra = {
            11: -2.0 * conformal * cross * mixed[7],
            21: 0.5 * lapse * conformal * trace_with(inverse, symmetric(ricci)),
        }
        for s in range(6):
            extra[12 + s] = conformal * (source[s] - metric[s] * third_trace)
        for i in range(3):
            extra[18 + i] = 2.0 * cross * mixed[8 + i] + (1.0 / 3.0) * (
                inverse[i][0] * mixed[9] + inverse[i][1] * mixed[8]
            )
        for q in range(fields):
            rate = st_rate[q, place, :]
            if q in extra:
                rate = rate + extra[q]
            st_out[q, place, :] = halo.main(q, p) + dt * rate

    end = own + 1
    ends = (0, end)
    bx_face, by_face, bz_face = ({p: halo.corner(fields + 5 + i, p) for p in ends} for i in range(3))
    layers = {p: halo.corner_layers(p) for p in ends}
    bx_face[end] = layers[end]
    by_face[0] = jnp.where(t.slot < 2, layers[0], by_face[0])
    centred = [{}, {}, {}]
    for p in ends:
        following = halo.beside(fields + 5, 1) if p == 0 else bx_face[p]
        edge_cells = x_below if p == 0 else x_above
        dx = 0.5 * (t.odd_swapped(bx_face[p], following) - bx_face[p])
        dy = 0.5 * (t.y_up(by_face[p], edge_cells[fields + 6], 1) - by_face[p])
        centred[0][p] = bx_face[p] + dx
        centred[1][p] = by_face[p] + dy
        centred[2][p] = bz_face[p] - (dx + dy)
    corners = [{p: halo.corner(q, p) for p in ends} for q in [0, 7] + list(range(fields, fields + 5))]
    found = primitives(
        half, [(0, p) for p in ends], [[c] for c in corners[2:]], [[c] for c in centred],
        [corners[0]], [corners[1]], 2,
    )
    ez_h = [found[0, 0][10]] + [electric[own + p] for p in inner] + [found[0, end][10]]
    ez_x_h = [None] + [ez_h[p] + t.odd_swapped(ez_h[p - 1], ez_h[p]) for p in span[1:]]
    ez_x = [None] + [electric[p - 1] for p in span[1:]]
    edge_z = [None] + [ez_x[p] + t.y_down(ez_x[p], ez_x_h[p], 1) for p in span[1:]]
    quarter = 0.25 * dt
    for p in inner:
        place = slice((p - 1) * half, p * half)
        edge_z_h = ez_x_h[p] + t.y_down(ez_x_h[p], ez_x[p], 1)
        for q in range(5):
            fl_out[q, place, :] = halo.main(fields + q, p) + dt * hydro_rate[q, place, :]
        x_rate = hydro_rate[5, place, :] - (t.y_up(edge_z[p], edge_z_h, 1) - edge_z[p])
        y_rate = hydro_rate[6, place, :] + (t.odd(edge_z[p], edge_z[p + 1]) - edge_z[p])
        z_rate = hydro_rate[7, place, :]
        for i, rate in enumerate((x_rate, y_rate, z_rate)):
            fl_out[5 + i, place, :] = halo.main(fields + 5 + i, p) + quarter * rate


def per_device(spacetime, fluid):
    fields, cx, cy, cz = spacetime.shape
    rows = cx * cy
    st = spacetime.reshape(fields, rows, cz)
    fl = fluid.reshape(FLUID, rows, cz)
    sizes = [lax.axis_size(a) for a in ("gx", "gy", "gz")]
    tile = (2 * cy, cz)
    f32 = jnp.float32

    def shape(*dims):
        return jax.ShapeDtypeStruct(dims, f32)

    def beyond(cells):
        n = sizes[2]
        after = lax.ppermute(cells, "gz", [((i + 1) % n, i) for i in range(n)])
        if n == 2:
            return after
        before = lax.ppermute(cells, "gz", [(i, (i + 1) % n) for i in range(n)])
        lane = lax.broadcasted_iota(jnp.int32, cells.shape, 2)
        return jnp.where(lane < cz // 2, after, before)

    def beyond_lanes(packed):
        n = sizes[2]
        after = lax.ppermute(packed, "gz", [((i + 1) % n, i) for i in range(n)])
        if n == 2:
            return after
        before = lax.ppermute(packed, "gz", [(i, (i + 1) % n) for i in range(n)])
        lane = lax.broadcasted_iota(jnp.int32, packed.shape, 2)
        return jnp.where(lane % 4 < 2, before, after)

    params = pltpu.CompilerParams(vmem_limit_bytes=48 * 1024 * 1024)
    zst, zfl = beyond(st), beyond(fl)
    cells = jnp.concatenate([st, fl], axis=0)
    face = shape(face_tiles(fields), *tile)
    corner = shape(CORNER_TILES, *tile)
    lane_row = shape(1, cz)
    def call(kernel, outs, name, operands, scratch=()):
        return pl.pallas_call(
            kernel,
            out_shape=outs,
            scratch_shapes=scratch,
            compiler_params=params,
            name=name,
        )(*operands)

    def shift(cells, step):
        n = lax.axis_size("gx")
        return lax.ppermute(cells, "gx", [(i, (i + step) % n) for i in range(n)])

    def trade(cells, first):
        axis = "gy"
        n = lax.axis_size(axis)
        step = [1, -1] if first else [-1, 1]
        return lax.ppermute(cells, axis, [(i, (i + step[i % 2]) % n) for i in range(n)])

    def two_away(cells, axis):
        n = lax.axis_size(axis)
        return lax.ppermute(cells, axis, [(i, (i + 2) % n) for i in range(n)]) if n == 4 else cells

    short = sizes[0] <= 4 and sizes[1] <= 4 and sizes[2] <= 2
    x_high = call(pack_up_kernel, face, "pack_up", (cells,))
    x_below = shift(x_high, 1)
    x_low, y_first, y_second, top = call(
        pack_kernel, [face, face, face, shape(TOP_TILES, *tile)], "pack", (cells, zst, zfl)
    )
    below_lanes = beyond_lanes(call(lanes_kernel, shape(1, *tile), "lanes", (x_below,)))
    y_first = trade(y_first, True)
    x_above = shift(x_low, -1)
    y_second = trade(y_second, False)
    top_two = two_away(top, "gx")
    c_first, c_second, line_top = call(
        relay_kernel,
        [corner, corner, shape(LINE_TILES, *tile)],
        "relay",
        (x_below, below_lanes, x_above, top, top_two),
    )
    c_first = trade(c_first, True)
    c_second = trade(c_second, False)
    if short:
        line_two = two_away(line_top, "gy")
    else:
        line_two = lax.pmax(line_top, ("gx", "gy", "gz"))
    own = cx // 2
    arrived = (cells, zst, zfl, x_below, y_first, x_above, y_second, below_lanes)
    early = call(
        early_kernel,
        [
            shape(*st.shape),
            shape(FLUID, rows, cz),
            shape(CURVED, own, *tile),
            shape(2 * own + 1, *tile),
        ],
        "early",
        arrived,
        [
            pltpu.VMEM((fields, own + 4) + tile, f32),
            pltpu.VMEM((fields, own) + tile, f32),
            pltpu.VMEM((fields, own) + tile, f32),
            pltpu.VMEM((CURVED, own + 2) + tile, f32),
            pltpu.VMEM((CURVED, own) + tile, f32),
            pltpu.VMEM((fields, 3) + tile, f32),
            pltpu.VMEM((CURVED, 6) + tile, f32),
            pltpu.VMEM((fields,) + tile, f32),
            pltpu.VMEM((own, 11) + tile, f32),
        ],
    )
    st_next, fl_next = call(
        late_kernel,
        [shape(*st.shape), shape(*fl.shape)],
        "late",
        (*arrived, c_first, c_second, line_two, line_top, *early),
    )
    return st_next.reshape(spacetime.shape), fl_next.reshape(fluid.shape)


def solution(mesh):
    spec = P(None, "gx", "gy", "gz")
    return jax.shard_map(
        per_device, mesh=mesh, in_specs=(spec, spec), out_specs=(spec, spec), check_vma=False
    )
```

```python
import functools
import math

import jax
import jax.numpy as jnp
from jax import lax
from jax.experimental import pallas as pl
from jax.experimental.pallas import tpu as pltpu
from jax.sharding import PartitionSpec as P

RECOVERY_STEPS = 4
INDEX_PAIRS = ((0, 0), (0, 1), (0, 2), (1, 1), (1, 2), (2, 2))
COURANT = 0.25
DISSIPATION = 0.2
KAPPA_ONE = 0.02
SHIFT_DAMPING = 1.0
SPEED_CAP = 0.99
PRESSURE_FLOOR = 0.01
FOUR_PI = 4.0 * math.pi

BATCH = 6
CURVED = 11
FLUID = 8


def total(pieces):
    summed = pieces[0]
    for member in pieces[1:]:
        summed = summed + member
    return summed


def dot(first_vec, second_vec):
    return total([first_vec[i] * second_vec[i] for i in range(3)])


def slot_of(i, j):
    return INDEX_PAIRS.index((min(i, j), max(i, j)))


def symmetric(entries):
    return [[entries[slot_of(i, j)] for j in range(3)] for i in range(3)]


def trace_with(inverse, tensor):
    return (
        inverse[0][0] * tensor[0][0]
        + inverse[1][1] * tensor[1][1]
        + inverse[2][2] * tensor[2][2]
        + 2.0
        * (
            inverse[0][1] * tensor[0][1]
            + inverse[0][2] * tensor[0][2]
            + inverse[1][2] * tensor[1][2]
        )
    )


def inverse_metric(metric):
    cofactor = [
        metric[1][1] * metric[2][2] - metric[1][2] * metric[1][2],
        metric[0][2] * metric[1][2] - metric[0][1] * metric[2][2],
        metric[0][1] * metric[1][2] - metric[0][2] * metric[1][1],
        metric[0][0] * metric[2][2] - metric[0][2] * metric[0][2],
        metric[0][1] * metric[0][2] - metric[0][0] * metric[1][2],
        metric[0][0] * metric[1][1] - metric[0][1] * metric[0][1],
    ]
    determinant = (
        metric[0][0] * cofactor[0] + metric[0][1] * cofactor[1] + metric[0][2] * cofactor[2]
    )
    over = 1.0 / determinant
    return symmetric([c * over for c in cofactor])


class Tile:
    def __init__(self, cy, cz):
        self.cy, self.rows, self.lanes = cy, 2 * cy, cz
        shape = (self.rows, cz)
        self.row = lax.broadcasted_iota(jnp.int32, shape, 0)
        self.lane = lax.broadcasted_iota(jnp.int32, shape, 1)
        self.slot = lax.rem(self.row, cy)

    def turn(self, tile, amount):
        amount = amount % self.rows
        return tile if amount == 0 else pltpu.roll(tile, amount, 0)

    def spin(self, tile, amount):
        amount = amount % self.lanes
        return tile if amount == 0 else pltpu.roll(tile, amount, 1)

    def swap(self, tile):
        return self.turn(tile, self.cy)

    def odd(self, a, b):
        return self.turn(jnp.where(self.row < self.cy, b, a), self.cy)

    def odd_swapped(self, a, b):
        return self.turn(jnp.where(self.row < self.cy, a, b), self.cy)

    def y_up(self, main, beyond, k):
        return self.turn(jnp.where(self.slot < k, beyond, main), -k)

    def y_down(self, main, beyond, k):
        return self.turn(jnp.where(self.slot >= self.cy - k, beyond, main), k)

    def z_up(self, main, beyond, k):
        return self.spin(jnp.where(self.lane < k, beyond, main), -k)

    def z_down(self, main, beyond, k):
        return self.spin(jnp.where(self.lane >= self.lanes - k, beyond, main), k)

    def corner_rows(self, side, turn):
        places = ((0, 2), (self.cy - 1, self.cy + 1))[side]
        first, second = [(place + turn) % self.rows for place in places]
        return (self.row == first) | (self.row == second)

    def join_low(self, u, v):
        return jnp.where(self.slot < 2, self.swap(u), self.turn(v, 2))

    def join_high(self, u, v):
        return jnp.where(self.slot >= self.cy - 2, self.swap(u), self.turn(self.swap(v), -2))

    def part_first(self, from_above, from_below):
        return jnp.where(self.slot < 2, from_above, from_below)

    def part_second(self, from_above, from_below):
        return self.turn(jnp.where(self.slot < 2, from_below, from_above), 2)


def edge_list(tiles):
    fields = next(n for n in range(tiles) if face_tiles(n) == tiles)
    return list(range(CURVED)) + list(range(fields, fields + FLUID))


CORNER_TURNS = (0, 1, 4, 5)
TOP_TILES = 2
CORNER_TILES = CURVED + FLUID // 4 + 1
TOP_ROW = 6


def face_tiles(fields):
    return fields + FLUID + len(pairs_of(third_list(fields))) + 1


def third_list(fields):
    return list(range(fields + 1))


def pairs_of(items):
    return [(items[i], items[min(i + 1, len(items) - 1)]) for i in range(0, len(items), 2)]


def top_speed(st):
    inverse = inverse_metric(symmetric([st[1 + s] for s in range(6)]))
    scale = 2.0 * st[7] * st[0]
    speeds = [jnp.abs(st[8 + d]) + jnp.sqrt(scale * inverse[d][d]) for d in range(3)]
    top = jnp.maximum(jnp.maximum(speeds[0], speeds[1]), speeds[2])
    return jnp.max(jnp.max(top, axis=1, keepdims=True), axis=0, keepdims=True)


class Chosen:
    def __init__(self, first, second, swapped):
        self.first, self.second, self.swapped, self.shape = first, second, swapped, first.shape

    def __getitem__(self, key):
        return jnp.where(self.swapped, self.second[key], self.first[key])


class Sent:
    def __init__(self, first, second, swapped):
        self.first, self.second, self.swapped, self.shape = first, second, swapped, first.shape

    def put(self, key, lower, upper):
        self.first[key] = jnp.where(self.swapped, upper, lower)
        self.second[key] = jnp.where(self.swapped, lower, upper)


class Joined:
    def __init__(self, tiles, tail):
        self.tiles, self.tail = tiles, tail
        self.shape = tuple(tiles.shape)

    def __getitem__(self, key):
        q, rows = (key[0], key[1:]) if isinstance(key, tuple) else (key, ())
        if q == self.tiles.shape[0] - 1:
            return self.tail[(0,) + rows]
        return self.tiles[(q,) + rows]


def even_along_y(tile):
    return jnp.full(tile, lax.rem(lax.axis_index("gy"), 2), jnp.int32) == 0


def odd_along_y(tile):
    return jnp.full(tile, lax.rem(lax.axis_index("gy"), 2), jnp.int32) == 1


def pack_up_kernel(cells, x_high):
    count, rows, lanes = cells.shape
    fields, half = count - FLUID, rows // 2
    t = Tile(rows // 4, lanes)
    for q in range(count):
        x_high[q] = cells[q, half:rows, :]
    for n, (a, b) in enumerate(pairs_of(list(range(fields)) + [fields + 5])):
        x_high[count + n] = jnp.where(
            t.row < t.cy, t.swap(cells[b, 0:half, :]), cells[a, 0:half, :]
        )
    x_high[x_high.shape[0] - 1] = jnp.broadcast_to(top_speed(cells), t.row.shape)


def lanes_kernel(x_below, out):
    t = Tile(x_below.shape[1] // 2, x_below.shape[2])
    last = x_below.shape[0] - 1
    packed = x_below[last]
    for place, q in enumerate(edge_list(x_below.shape[0])):
        piece = t.spin(x_below[q], 4 * place + 2)
        here = (t.lane >= 4 * place) & (t.lane < 4 * place + 4)
        packed = jnp.where(here, piece, packed)
    out[0] = packed


def pack_kernel(cells, zst, zfl, *outs):
    fields, rows, lanes = zst.shape
    st, fl = cells.at[0:fields], cells.at[fields : fields + FLUID]
    cy = rows // 4
    t = Tile(cy, lanes)
    x_low, y_first, y_second, top_out = outs
    half = t.rows
    to_y = Sent(y_first, y_second, even_along_y((half, lanes)))

    def own(ref, q):
        return [ref[q, 0:half, :], ref[q, half : 2 * half, :]]

    tiles, beyond = [], []
    for q in range(fields):
        tiles.append(own(st, q))
        beyond.append(own(zst, q) if q < CURVED else None)
    for q in range(FLUID):
        tiles.append(own(fl, q))
        beyond.append(own(zfl, q))

    packed = [None] * 4
    place_count = 0
    for q, (first, second) in enumerate(tiles):
        x_low[q] = first
        to_y.put(q, t.join_low(first, second), t.join_high(first, second))
        if beyond[q] is not None:
            zf, zs = beyond[q]
            for m, piece in enumerate((zf, zs, t.join_low(zf, zs), t.join_high(zf, zs))):
                piece = t.spin(piece, 4 * place_count + 2)
                packed[m] = (
                    piece if place_count == 0 else jnp.where(t.lane < 4 * place_count, packed[m], piece)
                )
            place_count += 1
    for n, (a, b) in enumerate(pairs_of(third_list(fields))):
        slot = fields + FLUID + n
        xa, xb = (tiles[q if q < fields else fields + 5] for q in (a, b))
        x_low[slot] = jnp.where(t.row < cy, xa[1], t.swap(xb[1]))
        ya, yb = (tiles[q if q < fields else fields + 6] for q in (a, b))
        w = [t.swap(ya[0]), t.swap(ya[1]), t.swap(yb[0]), t.swap(yb[1])]
        s = t.slot
        low = jnp.where(s == 0, t.turn(w[2], -2), t.turn(w[3], -1))
        low = jnp.where(s == 2, w[0], jnp.where(s == 3, t.turn(w[1], 1), low))
        high = jnp.where(s == 3, t.turn(w[2], 2), t.turn(w[3], 1))
        high = jnp.where(s == 1, w[0], jnp.where(s == 0, t.turn(w[1], -1), high))
        to_y.put(slot, low, high)
    top = jnp.maximum(top_speed(st), top_speed(zst))
    top_out[...] = jnp.broadcast_to(top, top_out.shape)
    last = x_low.shape[0] - 1
    x_lanes = [jnp.where(t.lane < 4 * place_count, piece, top) for piece in packed[:2]]
    y_lanes = [jnp.where(t.lane < 4 * place_count, piece, top) for piece in packed[2:]]
    x_low[last] = x_lanes[0]
    to_y.put(last, *y_lanes)


def relay_kernel(x_below, below_lanes, x_above, top, top_two, c_first, c_second, line_top):
    cy, lanes = x_below.shape[1] // 2, x_below.shape[2]
    t = Tile(cy, lanes)
    to_y = Sent(c_first, c_second, odd_along_y((t.rows, lanes)))
    last = x_below.shape[0] - 1
    line = jnp.maximum(top[0, 0:1, :], top_two[0, 0:1, :])
    line = jnp.maximum(line, x_below[last, 0:1, lanes - 1 : lanes])
    x_below = Joined(x_below, below_lanes)
    for beside in (x_below, x_above):
        line = jnp.maximum(line, beside[last, 0:1, lanes - 1 : lanes])
    line_top[...] = line
    edge = edge_list(x_below.shape[0])
    for q in range(CURVED):
        below, above = x_below[q], x_above[q]
        to_y.put(q, t.join_low(below, above), t.join_high(below, above))
    for n in range(0, FLUID, 4):
        low, high = None, None
        for turn, q in zip(CORNER_TURNS, edge[CURVED + n : CURVED + n + 4]):
            below, above = x_below[q], x_above[q]
            below, above = (t.turn(j(below, above), turn) for j in (t.join_low, t.join_high))
            if low is None:
                low, high = below, above
            else:
                low = jnp.where(t.corner_rows(0, turn), below, low)
                high = jnp.where(t.corner_rows(1, turn), above, high)
        to_y.put(CURVED + n // 4, low, high)
    along_x, along_y = edge[CURVED + 5], edge[CURVED + 6]
    low = t.join_low(x_below[along_y], x_above[along_y])
    high = t.join_high(x_below[along_x], x_above[along_x])
    low, high = (jnp.where(t.row == TOP_ROW, line, tile) for tile in (low, high))
    to_y.put(CORNER_TILES - 1, low, high)


def limited(a, b):
    return jnp.maximum(jnp.minimum(a, b), 0.0) + jnp.minimum(jnp.maximum(a, b), 0.0)


def recover(conserved, magnetic):
    density = conserved[0]
    momenta = conserved[1:4]
    energy = conserved[4] + density
    mom_sq = dot(momenta, momenta)
    mag_sq = dot(magnetic, magnetic)
    cross = dot(momenta, magnetic)
    cross_sq = cross * cross

    def state(z):
        grown = z + mag_sq
        over = 1.0 / (z * grown)
        speed_sq = (mom_sq * z * z + cross_sq * (2.0 * z + mag_sq)) * over * over
        kept = 1.0 - jnp.minimum(speed_sq, SPEED_CAP)
        rest = density * jnp.sqrt(kept)
        return kept, rest, 0.5 * (z * kept - rest), grown * over

    z = jnp.maximum(energy - 0.5 * mag_sq, density)
    for _ in range(RECOVERY_STEPS):
        kept, rest, pressure, over_z = state(z)
        residual = (
            z
            + mag_sq
            - pressure
            - 0.5 * mag_sq * kept
            - 0.5 * cross_sq * over_z * over_z
            - energy
        )
        z = jnp.maximum(z - residual / (1.0 - 0.5 * kept), density)
    kept, rest, pressure, over_z = state(z)
    pressure = jnp.maximum(pressure, PRESSURE_FLOOR * rest)
    scale = lax.rsqrt(kept) / (z + mag_sq)
    along = cross * over_z
    four_vel = [scale * (momenta[i] + along * magnetic[i]) for i in range(3)]
    return [rest, pressure] + four_vel


def stress_parts(rest, pressure, u, magnetic):
    lorentz_sq = 1.0 + dot(u, u)
    over = lax.rsqrt(lorentz_sq)
    over_sq = over * over
    time_b = dot(u, magnetic)
    grown_b = [magnetic[i] + time_b * u[i] for i in range(3)]
    b_square = (dot(magnetic, magnetic) + time_b * time_b) * over_sq
    enthalpy = rest + 2.0 * pressure
    inertia = enthalpy + b_square
    return lorentz_sq, over, over_sq, time_b, grown_b, b_square, enthalpy, inertia


def face_state(rest, pressure, u, magnetic, d):
    lorentz_sq, over, over_sq, time_b, grown_b, b_square, enthalpy, inertia = stress_parts(
        rest, pressure, u, magnetic
    )
    total_pressure = pressure + 0.5 * b_square
    lorentz = lorentz_sq * over
    density = rest * lorentz
    carried = inertia * lorentz
    time_over = time_b * over
    conserved = [density]
    conserved += [carried * u[j] - time_over * grown_b[j] for j in range(3)]
    conserved += [inertia * lorentz_sq - total_pressure - time_b * time_b - density]
    mass_flux = rest * u[d]
    flux = [mass_flux]
    pushed = inertia * u[d]
    b_over = grown_b[d] * over_sq
    for j in range(3):
        flux_j = pushed * u[j] - b_over * grown_b[j]
        flux.append(flux_j + total_pressure if j == d else flux_j)
    flux.append(carried * u[d] - time_over * grown_b[d] - mass_flux)
    ratio = 1.0 / (enthalpy * inertia)
    sound_sq = 2.0 * pressure * inertia * ratio
    alfven_sq = b_square * enthalpy * ratio
    fast_sq = sound_sq + alfven_sq - sound_sq * alfven_sq
    slow = 1.0 - fast_sq
    velocity = u[d] * over
    rest_part = 1.0 - dot(u, u) * over_sq * fast_sq
    spread = jnp.sqrt(fast_sq * over_sq * (rest_part - velocity * velocity * slow))
    fastest = (jnp.abs(velocity * slow) + spread) / rest_part
    return conserved, flux, fastest


def face_flux(left, right, normal, weight, d):
    sides = []
    for state in (left, right):
        magnetic = [normal if i == d else state[5 + i] for i in range(3)]
        sides.append(face_state(state[0], state[1], state[2:5], magnetic, d))
    (cons_l, flux_l, fast_l), (cons_r, flux_r, fast_r) = sides
    signal = jnp.maximum(fast_l, fast_r)
    scale = 0.5 * weight
    return [scale * (flux_l[q] + flux_r[q] - signal * (cons_r[q] - cons_l[q])) for q in range(5)]


def volume_over(conformal):
    return conformal * jnp.sqrt(conformal)


def first_diff(down_two, down, up, up_two):
    return (8.0 / 12.0) * (up - down) + (1.0 / 12.0) * (down_two - up_two)


class Halo:
    def __init__(self, cells, zst, zfl, x_below, y_first, x_above, y_second, below_lanes, *corners):
        x_below = Joined(x_below, below_lanes)
        self.fields, self.block, self.lanes = zst.shape
        even_y = even_along_y((self.block // 2, self.lanes))
        y_below, y_above = Chosen(y_first, y_second, even_y), Chosen(y_second, y_first, even_y)
        if corners:
            c_first, c_second = corners
            odd_y = odd_along_y((self.block // 2, self.lanes))
            self.c_below = Chosen(c_first, c_second, odd_y)
            self.c_above = Chosen(c_second, c_first, odd_y)
        self.st = cells.at[0 : self.fields]
        self.fl = cells.at[self.fields : self.fields + FLUID]
        self.zst, self.zfl = zst, zfl
        self.x_below, self.x_above = x_below, x_above
        self.y_below, self.y_above = y_below, y_above
        self.cy = self.block // 4
        self.t = Tile(self.cy, self.lanes)
        self.half = self.t.rows
        self.own = self.block // self.half
        self.inner = range(1, self.own + 1)
        self.span = range(self.own + 2)
        self.edge = edge_list(x_below.shape[0])
        self.last = x_below.shape[0] - 1

    def rows_of(self, ref, q, p):
        return ref[q, (p - 1) * self.half : p * self.half, :]

    def main(self, q, p):
        if q < self.fields:
            return self.rows_of(self.st, q, p)
        return self.rows_of(self.fl, q - self.fields, p)

    def beyond(self, q, p):
        if q < self.fields:
            return self.rows_of(self.zst, q, p)
        return self.rows_of(self.zfl, q - self.fields, p)

    def part(self, second):
        return self.t.part_second if second else self.t.part_first

    def beside(self, q, p):
        return self.part(p == 2)(self.y_above[q], self.y_below[q])

    def third_place(self, q):
        return self.fields + FLUID + q // 2, q % 2

    def x_third(self, q, upper):
        tile, which = self.third_place(q)
        found = self.x_above[tile] if upper else self.x_below[tile]
        return self.t.swap(found) if which else found

    def y_third(self, q, p):
        t = self.t
        tile, which = self.third_place(q)
        turn_above, turn_below = ((0, 0), (-1, 1), (2, -2), (1, -1))[2 * which + p - 1]
        above, below = t.turn(self.y_above[tile], turn_above), t.turn(self.y_below[tile], turn_below)
        return jnp.where(t.slot == 2, above, below)

    def z_place(self, q):
        return 4 * self.edge.index(q) + 2

    def x_beyond(self, q, upper):
        tile = self.x_above[self.last] if upper else self.x_below[self.last]
        return self.t.spin(tile, -self.z_place(q))

    def y_beyond(self, q, p):
        return self.t.spin(self.beside(self.last, p), -self.z_place(q))

    def corner(self, q, p):
        place, turn = q, 0
        if q >= CURVED:
            n = q - self.fields
            place, turn = CURVED + n // 4, CORNER_TURNS[n % 4]
        above, below = self.t.turn(self.c_above[place], -turn), self.t.turn(self.c_below[place], -turn)
        return self.part(p > 0)(above, below)

    def corner_layers(self, p):
        place = CORNER_TILES - 1
        return self.part(p > 0)(self.c_above[place], self.c_below[place])

    def plane(self, q):
        inner = self.inner
        return (
            [self.x_below[q]] + [self.main(q, p) for p in inner] + [self.x_above[q]],
            [None] + [self.beside(q, p) for p in inner] + [None],
            [self.x_beyond(q, False)]
            + [self.beyond(q, p) for p in inner]
            + [self.x_beyond(q, True)],
            [None] + [self.y_beyond(q, p) for p in inner] + [None],
        )


def weigh(chi_face, alpha_face):
    shrink = volume_over(chi_face)
    return shrink, alpha_face / shrink


def primitives(half, spots, cons, centred, chi, alpha, batch):
    found = {}
    for start in range(0, len(spots), batch):
        group = spots[start : start + batch]

        def gather(planes):
            return jnp.concatenate([planes[k][p] for k, p in group], axis=0)

        shrink = volume_over(gather(chi))
        mag_raw = [gather(centred[i]) for i in range(3)]
        mag = [m * shrink for m in mag_raw]
        values = recover([gather(c) * shrink for c in cons], mag)
        u = values[2:5]
        factor = gather(alpha) * lax.rsqrt(1.0 + dot(u, u))
        field = [
            factor * (u[(i + 2) % 3] * mag_raw[(i + 1) % 3] - u[(i + 1) % 3] * mag_raw[(i + 2) % 3])
            for i in range(3)
        ]
        for n, spot in enumerate(group):
            found[spot] = [value[n * half : (n + 1) * half] for value in values + mag + field]
    return found


def ring_fluxes(prims, chi, alpha, normals, d, up, down):
    found = []
    for here, there in ((0, 1), (1, 0)):
        left, right = [], []
        for a, b in zip(prims[here], prims[there]):
            below = down(a, b, 1)
            middle = a - below
            left.append(below + 0.5 * limited(below - down(a, b, 2), middle))
            right.append(a - 0.5 * limited(middle, up(a, b, 1) - a))
        shrink, weight = weigh(
            0.5 * (chi[here] + down(chi[here], chi[there], 1)),
            0.5 * (alpha[here] + down(alpha[here], alpha[there], 1)),
        )
        found.append(face_flux(left, right, normals[here] * shrink, weight, d))
    return [a - up(a, b, 1) for a, b in zip(*found)]


def early_kernel(
    cells, zst, zfl, x_below, y_first, x_above, y_second, below_lanes,
    st_rate, hydro_rate, slopes, electric, pairs, sides, thirds, pairs_z, sides_z, grads, seconds, damped, tensors,
):
    halo = Halo(cells, zst, zfl, x_below, y_first, x_above, y_second, below_lanes)
    t, fields, half, own, cy = halo.t, halo.fields, halo.half, halo.own, halo.cy
    st, fl, inner = halo.st, halo.fl, halo.inner

    for q in range(fields):
        pairs[q, 0] = halo.x_third(q, False)
        pairs[q, 1] = x_below[q]
        for p in inner:
            pairs[q, 1 + p] = halo.main(q, p)
            sides[q, p - 1] = halo.beside(q, p)
            thirds[q, p - 1] = halo.y_third(q, p)
        pairs[q, 2 + own] = x_above[q]
        pairs[q, 3 + own] = halo.x_third(q, True)
        if q < CURVED:
            pairs_z[q, 0] = halo.x_beyond(q, False)
            pairs_z[q, own + 1] = halo.x_beyond(q, True)
            for p in inner:
                pairs_z[q, p] = halo.beyond(q, p)
                sides_z[q, p - 1] = halo.y_beyond(q, p)

    span = halo.span
    face = [halo.plane(fields + 5 + i) for i in range(3)]

    def halves(kind, p):
        own_x, own_y, own_z = (f[kind][p] for f in face)
        pair = kind in (0, 2)
        known_x = pair or p < own
        last = kind == 0 and p == own + 1
        if pair:
            next_x = halo.x_third(fields, True) if last else face[0][kind][min(p + 1, own + 1)]
            next_x = t.odd(own_x, next_x)
        else:
            next_x = t.odd_swapped(own_x, face[0][kind][p + 1] if known_x else own_x)
        dx = 0.5 * (next_x - own_x)
        dz = 0.5 * (t.z_up(own_z, face[2][kind ^ 2][p], 1) - own_z)
        inside = 1 <= p <= own
        if not pair:
            here = jnp.where(t.slot == 2, halo.y_third(fields, p), own_y) if kind == 1 else own_y
            next_y = t.y_up(here, face[1][kind ^ 1][p], 1)
        else:
            next_y = t.y_up(own_y, face[1][kind ^ 1][p] if inside else own_y, 1)
        dy = 0.5 * (next_y - own_y)
        if pair and not inside:
            dy = jnp.where(t.slot == cy - 1, -(dx + dz), dy)
        if not pair and not known_x:
            dx = jnp.where(t.row < cy, -(dy + dz), dx)
        return own_x + dx, own_y + dy, own_z + dz

    spots = [(0, p) for p in span] + [(1, p) for p in inner]
    spots += [(2, p) for p in span] + [(3, p) for p in inner]
    centred = [[[None] * (own + 2) for _ in range(4)] for _ in range(3)]
    for k, p in spots:
        for i, value in enumerate(halves(k, p)):
            centred[i][k][p] = value
    chi, alpha = halo.plane(0), halo.plane(7)
    found = primitives(
        half, spots, [halo.plane(fields + q) for q in range(5)], centred, chi, alpha, BATCH
    )

    lines = [[found[0, p][i] for p in span] for i in range(8)] + [chi[0], alpha[0]]
    odd_lines = [[t.odd(f[p], f[min(p + 1, own + 1)]) for p in span] for f in lines]
    fluxes = [None]
    for p in range(1, own + 2):
        left, right = [], []
        for f, o in zip(lines[:8], odd_lines):
            here = f[p] - o[p - 1]
            left.append(o[p - 1] + 0.5 * limited(o[p - 1] - f[p - 1], here))
            right.append(f[p] - 0.5 * limited(here, o[p] - f[p]))
        shrink, weight = weigh(
            0.5 * (lines[8][p] + odd_lines[8][p - 1]), 0.5 * (lines[9][p] + odd_lines[9][p - 1])
        )
        fluxes.append(face_flux(left, right, face[0][0][p] * shrink, weight, 0))
    for p in inner:
        changes = [
            ring_fluxes(
                [found[k, p][:8] for k in (0, kind)],
                [chi[k][p] for k in (0, kind)],
                [alpha[k][p] for k in (0, kind)],
                [face[d][k][p] for k in (0, kind)],
                d,
                up,
                down,
            )
            for d, kind, up, down in ((1, 1, t.y_up, t.y_down), (2, 2, t.z_up, t.z_down))
        ]
        for q in range(5):
            change = fluxes[p][q] - t.odd(fluxes[p][q], fluxes[p + 1][q])
            tensors[p - 1, 6 + q] = change + changes[0][q] + changes[1][q]
        rest, pressure = found[0, p][:2]
        u = found[0, p][2:5]
        parts = stress_parts(rest, pressure, u, found[0, p][5:8])
        lorentz_sq, over, over_sq, time_b, grown_b, b_square, enthalpy, inertia = parts
        total_pressure = pressure + 0.5 * b_square
        for s, (i, j) in enumerate(INDEX_PAIRS):
            value = inertia * u[i] * u[j] - over_sq * (grown_b[i] * grown_b[j])
            tensors[p - 1, s] = value + total_pressure if i == j else value

    ex, ey, ez = (
        [[found[k, p][8 + i] if (k, p) in found else None for p in span] for k in range(4)]
        for i in range(3)
    )
    ey_x = [
        [ey[k][p] + t.odd(ey[k][p - 1], ey[k][p]) if p else None for p in span] for k in (0, 2)
    ]
    edge_y = [None] + [ey_x[0][p] + t.z_down(ey_x[0][p], ey_x[1][p], 1) for p in span[1:]]
    for p in span[1:]:
        electric[p - 1] = ez[0][p] + t.odd(ez[0][p - 1], ez[0][p])
    for p in inner:
        electric[own + p] = ez[1][p]
        edge_y_z = ey_x[1][p] + t.z_down(ey_x[1][p], ey_x[0][p], 1)
        ex_y = ex[0][p] + t.y_down(ex[0][p], ex[1][p], 1)
        ex_y_h = ex[1][p] + t.y_down(ex[1][p], ex[0][p], 1)
        ex_y_z = ex[2][p] + t.y_down(ex[2][p], ex[3][p], 1)
        ex_y_hz = ex[3][p] + t.y_down(ex[3][p], ex[2][p], 1)
        edge_x = ex_y + t.z_down(ex_y, ex_y_z, 1)
        edge_x_h = ex_y_h + t.z_down(ex_y_h, ex_y_hz, 1)
        edge_x_z = ex_y_z + t.z_down(ex_y_z, ex_y, 1)
        place = slice((p - 1) * half, p * half)
        hydro_rate[5, place, :] = t.z_up(edge_y[p], edge_y_z, 1) - edge_y[p]
        hydro_rate[6, place, :] = edge_x - t.z_up(edge_x, edge_x_z, 1)
        hydro_rate[7, place, :] = (t.y_up(edge_x, edge_x_h, 1) - edge_x) - (
            t.odd(edge_y[p], edge_y[p + 1]) - edge_y[p]
        )

    def pair_step(index):
        p = index + 1
        base = index * half

        for q in range(fields):
            centre = pairs[q, p + 1]
            x_m3 = t.odd(pairs[q, p - 1], pairs[q, p])
            x_m2 = pairs[q, p]
            x_m1 = t.odd(pairs[q, p], centre)
            x_p1 = t.odd(centre, pairs[q, p + 2])
            x_p2 = pairs[q, p + 2]
            x_p3 = t.odd(pairs[q, p + 2], pairs[q, p + 3])
            side, third = sides[q, index], thirds[q, index]
            y_m1, y_m2 = t.y_down(centre, side, 1), t.y_down(centre, side, 2)
            y_p1, y_p2 = t.y_up(centre, side, 1), t.y_up(centre, side, 2)
            y_m3 = t.turn(
                jnp.where(t.slot >= cy - 2, side, jnp.where(t.slot == cy - 3, third, centre)), 3
            )
            y_p3 = t.turn(jnp.where(t.slot < 2, side, jnp.where(t.slot == 2, third, centre)), -3)
            beyond = zst[q, pl.ds(base, half), :]
            z_m1, z_m2, z_m3 = (t.z_down(centre, beyond, k) for k in (1, 2, 3))
            z_p1, z_p2, z_p3 = (t.z_up(centre, beyond, k) for k in (1, 2, 3))
            dx = first_diff(x_m2, x_m1, x_p1, x_p2)
            dy = first_diff(y_m2, y_m1, y_p1, y_p2)
            grads[q, 0] = dx
            if q < CURVED:
                slopes[q, index] = dx
            grads[q, 1] = dy
            grads[q, 2] = first_diff(z_m2, z_m1, z_p1, z_p2)
            near = [x_m1 + x_p1, y_m1 + y_p1, z_m1 + z_p1]
            far = [x_m2 + x_p2, y_m2 + y_p2, z_m2 + z_p2]
            outer = (x_m3 + x_p3) + (y_m3 + y_p3) + (z_m3 + z_p3)
            damped[q] = (DISSIPATION / 64.0) * (
                outer - 6.0 * (far[0] + far[1] + far[2]) + 15.0 * (near[0] + near[1] + near[2])
                - 60.0 * centre
            )
            if q < CURVED:
                for s, d in ((0, 0), (3, 1), (5, 2)):
                    seconds[q, s] = (1.0 / 12.0) * (16.0 * near[d] - far[d] - 30.0 * centre)
                b_m, b_c, b_p = pairs_z[q, p - 1], pairs_z[q, p], pairs_z[q, p + 1]
                dx_z = first_diff(b_m, t.odd(b_m, b_c), t.odd(b_c, b_p), b_p)
                b_s = sides_z[q, p - 1]
                dy_z = first_diff(
                    t.y_down(b_c, b_s, 2),
                    t.y_down(b_c, b_s, 1),
                    t.y_up(b_c, b_s, 1),
                    t.y_up(b_c, b_s, 2),
                )
                for s, inside, outside in ((2, dx, dx_z), (4, dy, dy_z)):
                    seconds[q, s] = first_diff(
                        t.z_down(inside, outside, 2),
                        t.z_down(inside, outside, 1),
                        t.z_up(inside, outside, 1),
                        t.z_up(inside, outside, 2),
                    )

        def value(q):
            return pairs[q, p + 1]

        def fluid_value(q):
            return fl[q, pl.ds(base, half), :]

        conformal, lapse = value(0), value(7)
        over_chi = 1.0 / conformal
        metric = symmetric([value(1 + s) for s in range(6)])
        shift = [value(8 + i) for i in range(3)]
        extrinsic, theta = value(11), value(21)
        traceless = symmetric([value(12 + s) for s in range(6)])
        connection = [value(18 + i) for i in range(3)]
        inverse = inverse_metric(metric)
        grad = [[grads[q, k] for k in range(3)] for q in range(fields)]
        chi_grad, lapse_grad = grad[0], grad[7]
        shift_grad = [[grad[8 + i][k] for i in range(3)] for k in range(3)]
        trace_k = extrinsic + 2.0 * theta

        stress = symmetric([tensors[p - 1, s] for s in range(6)])
        held = [fluid_value(q) for q in range(5)]
        shrink = volume_over(conformal)
        energy = held[4] + held[0]
        third_k = trace_k * (1.0 / 3.0)
        curved = [
            [
                (traceless[i][j] + metric[i][j] * third_k) if i <= j else None for j in range(3)
            ]
            for i in range(3)
        ]
        work = (
            stress[0][0] * curved[0][0]
            + stress[1][1] * curved[1][1]
            + stress[2][2] * curved[2][2]
            + 2.0
            * (
                stress[0][1] * curved[0][1]
                + stress[0][2] * curved[0][2]
                + stress[1][2] * curved[1][2]
            )
        )
        rates = [tensors[p - 1, 6 + q] for q in range(5)]
        for i in range(3):
            rates[1 + i] = (
                rates[1 + i]
                - energy * lapse_grad[i]
                + total([held[1 + k] * grad[8 + k][i] for k in range(3)])
            )
        rates[4] = (
            rates[4] + lapse * work * over_chi / shrink - dot(held[1:4], lapse_grad)
        )
        for q in range(5):
            hydro_rate[q, pl.ds(base, half), :] = rates[q]
        density = energy * shrink
        momentum = [held[1 + i] * shrink for i in range(3)]

        lowered = [[[None] * 3 for _ in range(3)] for _ in range(3)]
        for i in range(3):
            for j in range(3):
                for k in range(j, 3):
                    got = 0.5 * (
                        grad[1 + slot_of(i, k)][j]
                        + grad[1 + slot_of(i, j)][k]
                        - grad[1 + slot_of(j, k)][i]
                    )
                    lowered[i][j][k] = lowered[i][k][j] = got
        raised = [[[None] * 3 for _ in range(3)] for _ in range(3)]
        for i in range(3):
            for j in range(3):
                for k in range(j, 3):
                    got = total([inverse[i][l] * lowered[l][j][k] for l in range(3)])
                    raised[i][j][k] = raised[i][k][j] = got
        contracted = [trace_with(inverse, raised[i]) for i in range(3)]

        def hessian_trace(q):
            return (
                inverse[0][0] * seconds[q, 0]
                + inverse[1][1] * seconds[q, 3]
                + inverse[2][2] * seconds[q, 5]
                + 2.0 * (inverse[0][2] * seconds[q, 2] + inverse[1][2] * seconds[q, 4])
            )

        def second_cov(q, slope):
            bent = [total([raised[k][i][j] * slope[k] for k in range(3)]) for i, j in INDEX_PAIRS]
            return symmetric(
                [-bent[s] if s == 1 else seconds[q, s] - bent[s] for s in range(len(bent))]
            )

        chi_cov = second_cov(0, chi_grad)
        chi_lap = trace_with(inverse, chi_cov)
        raised_chi = [dot(inverse[i], chi_grad) for i in range(3)]
        chi_square = dot(raised_chi, chi_grad)
        cross_term = dot(raised_chi, lapse_grad)
        half_chi = 0.5 * over_chi
        plain_cov = second_cov(7, lapse_grad)
        lapse_cov = symmetric(
            [
                plain_cov[i][j]
                + (
                    chi_grad[i] * lapse_grad[j]
                    + chi_grad[j] * lapse_grad[i]
                    - metric[i][j] * cross_term
                )
                * half_chi
                for i, j in INDEX_PAIRS
            ]
        )
        lapse_lap = conformal * trace_with(inverse, lapse_cov)

        mixed = [
            [[dot(inverse[l], lowered[k][j]) for j in range(3)] for k in range(3)]
            for l in range(3)
        ]
        quarter_sq = half_chi * half_chi
        metric_factor = chi_lap * half_chi - 3.0 * chi_square * quarter_sq
        ricci = []
        for i, j in INDEX_PAIRS:
            second_part = -0.5 * hessian_trace(1 + slot_of(i, j))
            connection_part = 0.5 * total(
                [metric[k][i] * grad[18 + k][j] + metric[k][j] * grad[18 + k][i] for k in range(3)]
            )
            contracted_part = 0.5 * total(
                [contracted[k] * (lowered[i][j][k] + lowered[j][i][k]) for k in range(3)]
            )
            if i == j:
                quadratic = total(
                    [
                        raised[k][l][i] * (2.0 * mixed[l][i][k] + mixed[l][k][i])
                        for k in range(3)
                        for l in range(3)
                    ]
                )
            else:
                quadratic = total(
                    [
                        raised[k][l][i] * (mixed[l][j][k] + mixed[l][k][j])
                        + raised[k][l][j] * mixed[l][i][k]
                        for k in range(3)
                        for l in range(3)
                    ]
                )
            conformal_part = (
                chi_cov[i][j] * half_chi
                + metric[i][j] * metric_factor
                - chi_grad[i] * chi_grad[j] * quarter_sq
            )
            ricci.append(
                second_part + connection_part + contracted_part + quadratic + conformal_part
            )
        ricci = symmetric(ricci)
        ricci_scalar = conformal * trace_with(inverse, ricci)
        stress_trace = conformal * trace_with(inverse, stress)

        up_a = [
            [total([inverse[i][k] * traceless[k][j] for k in range(3)]) for j in range(3)]
            for i in range(3)
        ]
        raised_a = symmetric(
            [total([up_a[i][l] * inverse[j][l] for l in range(3)]) for i, j in INDEX_PAIRS]
        )
        a_square = trace_with(traceless, raised_a)
        shift_div = shift_grad[0][0] + shift_grad[1][1] + shift_grad[2][2]
        two_thirds_div = (2.0 / 3.0) * shift_div

        def finish(q, rate):
            rate = rate + dot(shift, grad[q]) + damped[q]
            st_rate[q, pl.ds(base, half), :] = rate

        finish(0, (2.0 / 3.0) * conformal * (lapse * trace_k - shift_div))
        finish(7, -2.0 * lapse * extrinsic)
        for i in range(3):
            finish(8 + i, 0.75 * connection[i] - SHIFT_DAMPING * shift[i])
        finish(
            11,
            lapse
            * (
                a_square
                + trace_k * trace_k * (1.0 / 3.0)
                + FOUR_PI * (stress_trace + density)
                + KAPPA_ONE * theta
            )
            - lapse_lap,
        )
        source = symmetric(
            [
                lapse * (ricci[i][j] - 2.0 * FOUR_PI * stress[i][j]) - lapse_cov[i][j]
                for i, j in INDEX_PAIRS
            ]
        )
        third_trace = trace_with(inverse, source) * (1.0 / 3.0)
        for s, (i, j) in enumerate(INDEX_PAIRS):
            finish(
                1 + s,
                total(
                    [
                        metric[i][k] * shift_grad[j][k] + metric[j][k] * shift_grad[i][k]
                        for k in range(3)
                    ]
                )
                - metric[i][j] * two_thirds_div
                - 2.0 * lapse * traceless[i][j],
            )
            product = total([traceless[i][k] * up_a[k][j] for k in range(3)])
            finish(
                12 + s,
                total(
                    [
                        traceless[i][k] * shift_grad[j][k] + traceless[j][k] * shift_grad[i][k]
                        for k in range(3)
                    ]
                )
                - traceless[i][j] * two_thirds_div
                + conformal * (source[i][j] - metric[i][j] * third_trace)
                + lapse * (trace_k * traceless[i][j] - 2.0 * product),
            )
        for i in range(3):
            bracket = (
                trace_with(raised_a, raised[i])
                - 1.5 * dot(raised_a[i], chi_grad) * over_chi
                - dot(inverse[i], [2.0 * grad[11][j] + grad[21][j] for j in range(3)]) * (1.0 / 3.0)
                - 2.0 * FOUR_PI * dot(inverse[i], momentum)
            )
            spread = [
                seconds[8, 0] + seconds[10, 2],
                seconds[9, 3] + seconds[10, 4],
                seconds[8, 2] + seconds[9, 4] + seconds[10, 5],
            ]
            finish(
                18 + i,
                contracted[i] * two_thirds_div
                - total([contracted[j] * shift_grad[j][i] for j in range(3)])
                + hessian_trace(8 + i)
                + dot(inverse[i], spread) * (1.0 / 3.0)
                - 2.0 * dot(raised_a[i], lapse_grad)
                + 2.0
                * lapse
                * (bracket - KAPPA_ONE * (connection[i] - contracted[i])),
            )
        finish(
            21,
            0.5
            * lapse
            * (
                ricci_scalar
                - a_square
                + (2.0 / 3.0) * trace_k * trace_k
                - 4.0 * FOUR_PI * density
            )
            - 2.0 * KAPPA_ONE * lapse * theta,
        )

    for index in range(own):
        pair_step(index)


def late_kernel(
    cells, zst, zfl, x_below, y_first, x_above, y_second, below_lanes, c_first, c_second, line_two, line_top,
    st_rate, hydro_rate, slopes, electric, st_out, fl_out,
):
    halo = Halo(
        cells, zst, zfl, x_below, y_first, x_above, y_second, below_lanes, c_first, c_second
    )
    x_below, x_above = halo.x_below, halo.x_above
    t, fields, half, own = halo.t, halo.fields, halo.half, halo.own
    inner, span = halo.inner, halo.span

    top = jnp.maximum(line_top[...], line_two[...])
    for lines in (c_first, c_second):
        top = jnp.maximum(top, lines[CORNER_TILES - 1, TOP_ROW : TOP_ROW + 1, :])
    dt = COURANT / top

    for p in inner:
        place = slice((p - 1) * half, p * half)
        mixed = []
        for q in range(CURVED):
            s_m, s_c, s_p = (
                halo.beside(q, n) if 1 <= n <= own else halo.corner(q, n) for n in (p - 1, p, p + 1)
            )
            slope = slopes[q, p - 1]
            slope_side = first_diff(s_m, t.odd_swapped(s_m, s_c), t.odd_swapped(s_c, s_p), s_p)
            mixed.append(
                first_diff(
                    t.y_down(slope, slope_side, 2),
                    t.y_down(slope, slope_side, 1),
                    t.y_up(slope, slope_side, 1),
                    t.y_up(slope, slope_side, 2),
                )
            )
        conformal, lapse = halo.main(0, p), halo.main(7, p)
        metric = [halo.main(1 + s, p) for s in range(6)]
        inverse = inverse_metric(symmetric(metric))
        half_chi = 0.5 / conformal
        cross = inverse[0][1]
        chi_trace = 2.0 * cross * mixed[0] * half_chi
        ricci = [metric[s] * chi_trace - cross * mixed[1 + s] for s in range(6)]
        ricci[1] = ricci[1] + mixed[0] * half_chi
        source = [lapse * r for r in ricci]
        source[1] = source[1] - mixed[7]
        third_trace = trace_with(inverse, symmetric(source)) * (1.0 / 3.0)
        extra = {
            11: -2.0 * conformal * cross * mixed[7],
            21: 0.5 * lapse * conformal * trace_with(inverse, symmetric(ricci)),
        }
        for s in range(6):
            extra[12 + s] = conformal * (source[s] - metric[s] * third_trace)
        for i in range(3):
            extra[18 + i] = 2.0 * cross * mixed[8 + i] + (1.0 / 3.0) * (
                inverse[i][0] * mixed[9] + inverse[i][1] * mixed[8]
            )
        for q in range(fields):
            rate = st_rate[q, place, :]
            if q in extra:
                rate = rate + extra[q]
            st_out[q, place, :] = halo.main(q, p) + dt * rate

    end = own + 1
    ends = (0, end)
    bx_face, by_face, bz_face = ({p: halo.corner(fields + 5 + i, p) for p in ends} for i in range(3))
    layers = {p: halo.corner_layers(p) for p in ends}
    bx_face[end] = layers[end]
    by_face[0] = jnp.where(t.slot < 2, layers[0], by_face[0])
    centred = [{}, {}, {}]
    for p in ends:
        following = halo.beside(fields + 5, 1) if p == 0 else bx_face[p]
        edge_cells = x_below if p == 0 else x_above
        dx = 0.5 * (t.odd_swapped(bx_face[p], following) - bx_face[p])
        dy = 0.5 * (t.y_up(by_face[p], edge_cells[fields + 6], 1) - by_face[p])
        centred[0][p] = bx_face[p] + dx
        centred[1][p] = by_face[p] + dy
        centred[2][p] = bz_face[p] - (dx + dy)
    corners = [{p: halo.corner(q, p) for p in ends} for q in [0, 7] + list(range(fields, fields + 5))]
    found = primitives(
        half, [(0, p) for p in ends], [[c] for c in corners[2:]], [[c] for c in centred],
        [corners[0]], [corners[1]], 2,
    )
    ez_h = [found[0, 0][10]] + [electric[own + p] for p in inner] + [found[0, end][10]]
    ez_x_h = [None] + [ez_h[p] + t.odd_swapped(ez_h[p - 1], ez_h[p]) for p in span[1:]]
    ez_x = [None] + [electric[p - 1] for p in span[1:]]
    edge_z = [None] + [ez_x[p] + t.y_down(ez_x[p], ez_x_h[p], 1) for p in span[1:]]
    quarter = 0.25 * dt
    for p in inner:
        place = slice((p - 1) * half, p * half)
        edge_z_h = ez_x_h[p] + t.y_down(ez_x_h[p], ez_x[p], 1)
        for q in range(5):
            fl_out[q, place, :] = halo.main(fields + q, p) + dt * hydro_rate[q, place, :]
        x_rate = hydro_rate[5, place, :] - (t.y_up(edge_z[p], edge_z_h, 1) - edge_z[p])
        y_rate = hydro_rate[6, place, :] + (t.odd(edge_z[p], edge_z[p + 1]) - edge_z[p])
        z_rate = hydro_rate[7, place, :]
        for i, rate in enumerate((x_rate, y_rate, z_rate)):
            fl_out[5 + i, place, :] = halo.main(fields + 5 + i, p) + quarter * rate


def per_device(spacetime, fluid):
    fields, cx, cy, cz = spacetime.shape
    rows = cx * cy
    st = spacetime.reshape(fields, rows, cz)
    fl = fluid.reshape(FLUID, rows, cz)
    sizes = [lax.axis_size(a) for a in ("gx", "gy", "gz")]
    tile = (2 * cy, cz)
    f32 = jnp.float32

    def shape(*dims):
        return jax.ShapeDtypeStruct(dims, f32)

    def beyond(cells):
        n = sizes[2]
        after = lax.ppermute(cells, "gz", [((i + 1) % n, i) for i in range(n)])
        if n == 2:
            return after
        before = lax.ppermute(cells, "gz", [(i, (i + 1) % n) for i in range(n)])
        lane = lax.broadcasted_iota(jnp.int32, cells.shape, 2)
        return jnp.where(lane < cz // 2, after, before)

    def beyond_lanes(packed):
        n = sizes[2]
        after = lax.ppermute(packed, "gz", [((i + 1) % n, i) for i in range(n)])
        if n == 2:
            return after
        before = lax.ppermute(packed, "gz", [(i, (i + 1) % n) for i in range(n)])
        lane = lax.broadcasted_iota(jnp.int32, packed.shape, 2)
        return jnp.where(lane % 4 < 2, before, after)

    params = pltpu.CompilerParams(vmem_limit_bytes=48 * 1024 * 1024)
    zst, zfl = beyond(st), beyond(fl)
    cells = jnp.concatenate([st, fl], axis=0)
    face = shape(face_tiles(fields), *tile)
    corner = shape(CORNER_TILES, *tile)
    lane_row = shape(1, cz)
    def call(kernel, outs, name, operands, scratch=()):
        return pl.pallas_call(
            kernel,
            out_shape=outs,
            scratch_shapes=scratch,
            compiler_params=params,
            name=name,
        )(*operands)

    def shift(cells, step):
        n = lax.axis_size("gx")
        return lax.ppermute(cells, "gx", [(i, (i + step) % n) for i in range(n)])

    def trade(cells, first):
        axis = "gy"
        n = lax.axis_size(axis)
        step = [1, -1] if first else [-1, 1]
        return lax.ppermute(cells, axis, [(i, (i + step[i % 2]) % n) for i in range(n)])

    def two_away(cells, axis):
        n = lax.axis_size(axis)
        return lax.ppermute(cells, axis, [(i, (i + 2) % n) for i in range(n)]) if n == 4 else cells

    short = sizes[0] <= 4 and sizes[1] <= 4 and sizes[2] <= 2
    x_high = call(pack_up_kernel, face, "pack_up", (cells,))
    x_below = shift(x_high, 1)
    x_low, y_first, y_second, top = call(
        pack_kernel, [face, face, face, shape(TOP_TILES, *tile)], "pack", (cells, zst, zfl)
    )
    below_lanes = beyond_lanes(call(lanes_kernel, shape(1, *tile), "lanes", (x_below,)))
    y_first = trade(y_first, True)
    x_above = shift(x_low, -1)
    y_second = trade(y_second, False)
    top_two = two_away(top, "gx")
    c_first, c_second, line_top = call(
        relay_kernel,
        [corner, corner, lane_row],
        "relay",
        (x_below, below_lanes, x_above, top, top_two),
    )
    c_first = trade(c_first, False)
    c_second = trade(c_second, True)
    if short:
        line_two = two_away(line_top, "gy")
    else:
        line_two = lax.pmax(line_top, ("gx", "gy", "gz"))
    own = cx // 2
    arrived = (cells, zst, zfl, x_below, y_first, x_above, y_second, below_lanes)
    early = call(
        early_kernel,
        [
            shape(*st.shape),
            shape(FLUID, rows, cz),
            shape(CURVED, own, *tile),
            shape(2 * own + 1, *tile),
        ],
        "early",
        arrived,
        [
            pltpu.VMEM((fields, own + 4) + tile, f32),
            pltpu.VMEM((fields, own) + tile, f32),
            pltpu.VMEM((fields, own) + tile, f32),
            pltpu.VMEM((CURVED, own + 2) + tile, f32),
            pltpu.VMEM((CURVED, own) + tile, f32),
            pltpu.VMEM((fields, 3) + tile, f32),
            pltpu.VMEM((CURVED, 6) + tile, f32),
            pltpu.VMEM((fields,) + tile, f32),
            pltpu.VMEM((own, 11) + tile, f32),
        ],
    )
    st_next, fl_next = call(
        late_kernel,
        [shape(*st.shape), shape(*fl.shape)],
        "late",
        (*arrived, c_first, c_second, line_two, line_top, *early),
    )
    return st_next.reshape(spacetime.shape), fl_next.reshape(fluid.shape)


def solution(mesh):
    spec = P(None, "gx", "gy", "gz")
    return jax.shard_map(
        per_device, mesh=mesh, in_specs=(spec, spec), out_specs=(spec, spec), check_vma=False
    )
```

```python
import functools
import math

import jax
import jax.numpy as jnp
from jax import lax
from jax.experimental import pallas as pl
from jax.experimental.pallas import tpu as pltpu
from jax.sharding import PartitionSpec as P

RECOVERY_STEPS = 4
INDEX_PAIRS = ((0, 0), (0, 1), (0, 2), (1, 1), (1, 2), (2, 2))
COURANT = 0.25
DISSIPATION = 0.2
KAPPA_ONE = 0.02
SHIFT_DAMPING = 1.0
SPEED_CAP = 0.99
PRESSURE_FLOOR = 0.01
FOUR_PI = 4.0 * math.pi

BATCH = 6
CURVED = 11
FLUID = 8


def total(pieces):
    summed = pieces[0]
    for member in pieces[1:]:
        summed = summed + member
    return summed


def dot(first_vec, second_vec):
    return total([first_vec[i] * second_vec[i] for i in range(3)])


def slot_of(i, j):
    return INDEX_PAIRS.index((min(i, j), max(i, j)))


def symmetric(entries):
    return [[entries[slot_of(i, j)] for j in range(3)] for i in range(3)]


def trace_with(inverse, tensor):
    return (
        inverse[0][0] * tensor[0][0]
        + inverse[1][1] * tensor[1][1]
        + inverse[2][2] * tensor[2][2]
        + 2.0
        * (
            inverse[0][1] * tensor[0][1]
            + inverse[0][2] * tensor[0][2]
            + inverse[1][2] * tensor[1][2]
        )
    )


def inverse_metric(metric):
    cofactor = [
        metric[1][1] * metric[2][2] - metric[1][2] * metric[1][2],
        metric[0][2] * metric[1][2] - metric[0][1] * metric[2][2],
        metric[0][1] * metric[1][2] - metric[0][2] * metric[1][1],
        metric[0][0] * metric[2][2] - metric[0][2] * metric[0][2],
        metric[0][1] * metric[0][2] - metric[0][0] * metric[1][2],
        metric[0][0] * metric[1][1] - metric[0][1] * metric[0][1],
    ]
    determinant = (
        metric[0][0] * cofactor[0] + metric[0][1] * cofactor[1] + metric[0][2] * cofactor[2]
    )
    over = 1.0 / determinant
    return symmetric([c * over for c in cofactor])


class Tile:
    def __init__(self, cy, cz):
        self.cy, self.rows, self.lanes = cy, 2 * cy, cz
        shape = (self.rows, cz)
        self.row = lax.broadcasted_iota(jnp.int32, shape, 0)
        self.lane = lax.broadcasted_iota(jnp.int32, shape, 1)
        self.slot = lax.rem(self.row, cy)

    def turn(self, tile, amount):
        amount = amount % self.rows
        return tile if amount == 0 else pltpu.roll(tile, amount, 0)

    def spin(self, tile, amount):
        amount = amount % self.lanes
        return tile if amount == 0 else pltpu.roll(tile, amount, 1)

    def swap(self, tile):
        return self.turn(tile, self.cy)

    def odd(self, a, b):
        return self.turn(jnp.where(self.row < self.cy, b, a), self.cy)

    def odd_swapped(self, a, b):
        return self.turn(jnp.where(self.row < self.cy, a, b), self.cy)

    def y_up(self, main, beyond, k):
        return self.turn(jnp.where(self.slot < k, beyond, main), -k)

    def y_down(self, main, beyond, k):
        return self.turn(jnp.where(self.slot >= self.cy - k, beyond, main), k)

    def z_up(self, main, beyond, k):
        return self.spin(jnp.where(self.lane < k, beyond, main), -k)

    def z_down(self, main, beyond, k):
        return self.spin(jnp.where(self.lane >= self.lanes - k, beyond, main), k)

    def corner_rows(self, side, turn):
        places = ((0, 2), (self.cy - 1, self.cy + 1))[side]
        first, second = [(place + turn) % self.rows for place in places]
        return (self.row == first) | (self.row == second)

    def join_low(self, u, v):
        return jnp.where(self.slot < 2, self.swap(u), self.turn(v, 2))

    def join_high(self, u, v):
        return jnp.where(self.slot >= self.cy - 2, self.swap(u), self.turn(self.swap(v), -2))

    def part_first(self, from_above, from_below):
        return jnp.where(self.slot < 2, from_above, from_below)

    def part_second(self, from_above, from_below):
        return self.turn(jnp.where(self.slot < 2, from_below, from_above), 2)


def edge_list(tiles):
    fields = next(n for n in range(tiles) if face_tiles(n) == tiles)
    return list(range(CURVED)) + list(range(fields, fields + FLUID))


CORNER_TURNS = (0, 1, 4, 5)
TOP_TILES = 2
CORNER_TILES = CURVED + FLUID // 4 + 1
TOP_ROW = 6


def face_tiles(fields):
    return fields + FLUID + len(pairs_of(third_list(fields))) + 1


def third_list(fields):
    return list(range(fields + 1))


def pairs_of(items):
    return [(items[i], items[min(i + 1, len(items) - 1)]) for i in range(0, len(items), 2)]


def top_speed(st):
    inverse = inverse_metric(symmetric([st[1 + s] for s in range(6)]))
    scale = 2.0 * st[7] * st[0]
    speeds = [jnp.abs(st[8 + d]) + jnp.sqrt(scale * inverse[d][d]) for d in range(3)]
    top = jnp.maximum(jnp.maximum(speeds[0], speeds[1]), speeds[2])
    return jnp.max(jnp.max(top, axis=1, keepdims=True), axis=0, keepdims=True)


class Chosen:
    def __init__(self, first, second, swapped):
        self.first, self.second, self.swapped, self.shape = first, second, swapped, first.shape

    def __getitem__(self, key):
        return jnp.where(self.swapped, self.second[key], self.first[key])


class Sent:
    def __init__(self, first, second, swapped):
        self.first, self.second, self.swapped, self.shape = first, second, swapped, first.shape

    def put(self, key, lower, upper):
        self.first[key] = jnp.where(self.swapped, upper, lower)
        self.second[key] = jnp.where(self.swapped, lower, upper)


class Joined:
    def __init__(self, tiles, tail):
        self.tiles, self.tail = tiles, tail
        self.shape = tuple(tiles.shape)

    def __getitem__(self, key):
        q, rows = (key[0], key[1:]) if isinstance(key, tuple) else (key, ())
        if q == self.tiles.shape[0] - 1:
            return self.tail[(0,) + rows]
        return self.tiles[(q,) + rows]


def even_along_y(tile):
    return jnp.full(tile, lax.rem(lax.axis_index("gy"), 2), jnp.int32) == 0


def pack_up_kernel(cells, x_high):
    count, rows, lanes = cells.shape
    fields, half = count - FLUID, rows // 2
    t = Tile(rows // 4, lanes)
    for q in range(count):
        x_high[q] = cells[q, half:rows, :]
    for n, (a, b) in enumerate(pairs_of(list(range(fields)) + [fields + 5])):
        x_high[count + n] = jnp.where(
            t.row < t.cy, t.swap(cells[b, 0:half, :]), cells[a, 0:half, :]
        )
    x_high[x_high.shape[0] - 1] = jnp.broadcast_to(top_speed(cells), t.row.shape)


def lanes_kernel(x_below, out):
    t = Tile(x_below.shape[1] // 2, x_below.shape[2])
    last = x_below.shape[0] - 1
    packed = x_below[last]
    for place, q in enumerate(edge_list(x_below.shape[0])):
        piece = t.spin(x_below[q], 4 * place + 2)
        here = (t.lane >= 4 * place) & (t.lane < 4 * place + 4)
        packed = jnp.where(here, piece, packed)
    out[0] = packed


def pack_kernel(cells, zst, zfl, *outs):
    fields, rows, lanes = zst.shape
    st, fl = cells.at[0:fields], cells.at[fields : fields + FLUID]
    cy = rows // 4
    t = Tile(cy, lanes)
    x_low, y_first, y_second, top_out = outs
    half = t.rows
    to_y = Sent(y_first, y_second, even_along_y((half, lanes)))

    def own(ref, q):
        return [ref[q, 0:half, :], ref[q, half : 2 * half, :]]

    tiles, beyond = [], []
    for q in range(fields):
        tiles.append(own(st, q))
        beyond.append(own(zst, q) if q < CURVED else None)
    for q in range(FLUID):
        tiles.append(own(fl, q))
        beyond.append(own(zfl, q))

    packed = [None] * 4
    place_count = 0
    for q, (first, second) in enumerate(tiles):
        x_low[q] = first
        to_y.put(q, t.join_low(first, second), t.join_high(first, second))
        if beyond[q] is not None:
            zf, zs = beyond[q]
            for m, piece in enumerate((zf, zs, t.join_low(zf, zs), t.join_high(zf, zs))):
                piece = t.spin(piece, 4 * place_count + 2)
                packed[m] = (
                    piece if place_count == 0 else jnp.where(t.lane < 4 * place_count, packed[m], piece)
                )
            place_count += 1
    for n, (a, b) in enumerate(pairs_of(third_list(fields))):
        slot = fields + FLUID + n
        xa, xb = (tiles[q if q < fields else fields + 5] for q in (a, b))
        x_low[slot] = jnp.where(t.row < cy, xa[1], t.swap(xb[1]))
        ya, yb = (tiles[q if q < fields else fields + 6] for q in (a, b))
        w = [t.swap(ya[0]), t.swap(ya[1]), t.swap(yb[0]), t.swap(yb[1])]
        s = t.slot
        low = jnp.where(s == 0, t.turn(w[2], -2), t.turn(w[3], -1))
        low = jnp.where(s == 2, w[0], jnp.where(s == 3, t.turn(w[1], 1), low))
        high = jnp.where(s == 3, t.turn(w[2], 2), t.turn(w[3], 1))
        high = jnp.where(s == 1, w[0], jnp.where(s == 0, t.turn(w[1], -1), high))
        to_y.put(slot, low, high)
    top = jnp.maximum(top_speed(st), top_speed(zst))
    top_out[...] = jnp.broadcast_to(top, top_out.shape)
    last = x_low.shape[0] - 1
    x_lanes = [jnp.where(t.lane < 4 * place_count, piece, top) for piece in packed[:2]]
    y_lanes = [jnp.where(t.lane < 4 * place_count, piece, top) for piece in packed[2:]]
    x_low[last] = x_lanes[0]
    to_y.put(last, *y_lanes)


def relay_kernel(x_below, below_lanes, y_first, y_second, x_above, top, top_two, c_first, c_second, line_top):
    cy, lanes = x_below.shape[1] // 2, x_below.shape[2]
    t = Tile(cy, lanes)
    to_y = Sent(c_first, c_second, even_along_y((t.rows, lanes)))
    last = x_below.shape[0] - 1
    line = jnp.maximum(top[0, 0:1, :], top_two[0, 0:1, :])
    line = jnp.maximum(line, x_below[last, 0:1, lanes - 1 : lanes])
    x_below = Joined(x_below, below_lanes)
    for beside in (x_below, x_above, y_first, y_second):
        line = jnp.maximum(line, beside[last, 0:1, lanes - 1 : lanes])
    line_top[...] = line
    edge = edge_list(x_below.shape[0])
    for q in range(CURVED):
        below, above = x_below[q], x_above[q]
        to_y.put(q, t.join_low(below, above), t.join_high(below, above))
    for n in range(0, FLUID, 4):
        low, high = None, None
        for turn, q in zip(CORNER_TURNS, edge[CURVED + n : CURVED + n + 4]):
            below, above = x_below[q], x_above[q]
            below, above = (t.turn(j(below, above), turn) for j in (t.join_low, t.join_high))
            if low is None:
                low, high = below, above
            else:
                low = jnp.where(t.corner_rows(0, turn), below, low)
                high = jnp.where(t.corner_rows(1, turn), above, high)
        to_y.put(CURVED + n // 4, low, high)
    along_x, along_y = edge[CURVED + 5], edge[CURVED + 6]
    low = t.join_low(x_below[along_y], x_above[along_y])
    high = t.join_high(x_below[along_x], x_above[along_x])
    low, high = (jnp.where(t.row == TOP_ROW, line, tile) for tile in (low, high))
    to_y.put(CORNER_TILES - 1, low, high)


def limited(a, b):
    return jnp.maximum(jnp.minimum(a, b), 0.0) + jnp.minimum(jnp.maximum(a, b), 0.0)


def recover(conserved, magnetic):
    density = conserved[0]
    momenta = conserved[1:4]
    energy = conserved[4] + density
    mom_sq = dot(momenta, momenta)
    mag_sq = dot(magnetic, magnetic)
    cross = dot(momenta, magnetic)
    cross_sq = cross * cross

    def state(z):
        grown = z + mag_sq
        over = 1.0 / (z * grown)
        speed_sq = (mom_sq * z * z + cross_sq * (2.0 * z + mag_sq)) * over * over
        kept = 1.0 - jnp.minimum(speed_sq, SPEED_CAP)
        rest = density * jnp.sqrt(kept)
        return kept, rest, 0.5 * (z * kept - rest), grown * over

    z = jnp.maximum(energy - 0.5 * mag_sq, density)
    for _ in range(RECOVERY_STEPS):
        kept, rest, pressure, over_z = state(z)
        residual = (
            z
            + mag_sq
            - pressure
            - 0.5 * mag_sq * kept
            - 0.5 * cross_sq * over_z * over_z
            - energy
        )
        z = jnp.maximum(z - residual / (1.0 - 0.5 * kept), density)
    kept, rest, pressure, over_z = state(z)
    pressure = jnp.maximum(pressure, PRESSURE_FLOOR * rest)
    scale = lax.rsqrt(kept) / (z + mag_sq)
    along = cross * over_z
    four_vel = [scale * (momenta[i] + along * magnetic[i]) for i in range(3)]
    return [rest, pressure] + four_vel


def stress_parts(rest, pressure, u, magnetic):
    lorentz_sq = 1.0 + dot(u, u)
    over = lax.rsqrt(lorentz_sq)
    over_sq = over * over
    time_b = dot(u, magnetic)
    grown_b = [magnetic[i] + time_b * u[i] for i in range(3)]
    b_square = (dot(magnetic, magnetic) + time_b * time_b) * over_sq
    enthalpy = rest + 2.0 * pressure
    inertia = enthalpy + b_square
    return lorentz_sq, over, over_sq, time_b, grown_b, b_square, enthalpy, inertia


def face_state(rest, pressure, u, magnetic, d):
    lorentz_sq, over, over_sq, time_b, grown_b, b_square, enthalpy, inertia = stress_parts(
        rest, pressure, u, magnetic
    )
    total_pressure = pressure + 0.5 * b_square
    lorentz = lorentz_sq * over
    density = rest * lorentz
    carried = inertia * lorentz
    time_over = time_b * over
    conserved = [density]
    conserved += [carried * u[j] - time_over * grown_b[j] for j in range(3)]
    conserved += [inertia * lorentz_sq - total_pressure - time_b * time_b - density]
    mass_flux = rest * u[d]
    flux = [mass_flux]
    pushed = inertia * u[d]
    b_over = grown_b[d] * over_sq
    for j in range(3):
        flux_j = pushed * u[j] - b_over * grown_b[j]
        flux.append(flux_j + total_pressure if j == d else flux_j)
    flux.append(carried * u[d] - time_over * grown_b[d] - mass_flux)
    ratio = 1.0 / (enthalpy * inertia)
    sound_sq = 2.0 * pressure * inertia * ratio
    alfven_sq = b_square * enthalpy * ratio
    fast_sq = sound_sq + alfven_sq - sound_sq * alfven_sq
    slow = 1.0 - fast_sq
    velocity = u[d] * over
    rest_part = 1.0 - dot(u, u) * over_sq * fast_sq
    spread = jnp.sqrt(fast_sq * over_sq * (rest_part - velocity * velocity * slow))
    fastest = (jnp.abs(velocity * slow) + spread) / rest_part
    return conserved, flux, fastest


def face_flux(left, right, normal, weight, d):
    sides = []
    for state in (left, right):
        magnetic = [normal if i == d else state[5 + i] for i in range(3)]
        sides.append(face_state(state[0], state[1], state[2:5], magnetic, d))
    (cons_l, flux_l, fast_l), (cons_r, flux_r, fast_r) = sides
    signal = jnp.maximum(fast_l, fast_r)
    scale = 0.5 * weight
    return [scale * (flux_l[q] + flux_r[q] - signal * (cons_r[q] - cons_l[q])) for q in range(5)]


def volume_over(conformal):
    return conformal * jnp.sqrt(conformal)


def first_diff(down_two, down, up, up_two):
    return (8.0 / 12.0) * (up - down) + (1.0 / 12.0) * (down_two - up_two)


class Halo:
    def __init__(self, cells, zst, zfl, x_below, y_first, y_second, x_above, below_lanes, *corners):
        x_below = Joined(x_below, below_lanes)
        self.fields, self.block, self.lanes = zst.shape
        even_y = even_along_y((self.block // 2, self.lanes))
        y_below, y_above = Chosen(y_first, y_second, even_y), Chosen(y_second, y_first, even_y)
        if corners:
            c_first, c_second = corners
            self.c_below = Chosen(c_first, c_second, even_y)
            self.c_above = Chosen(c_second, c_first, even_y)
        self.st = cells.at[0 : self.fields]
        self.fl = cells.at[self.fields : self.fields + FLUID]
        self.zst, self.zfl = zst, zfl
        self.x_below, self.x_above = x_below, x_above
        self.y_below, self.y_above = y_below, y_above
        self.cy = self.block // 4
        self.t = Tile(self.cy, self.lanes)
        self.half = self.t.rows
        self.own = self.block // self.half
        self.inner = range(1, self.own + 1)
        self.span = range(self.own + 2)
        self.edge = edge_list(x_below.shape[0])
        self.last = x_below.shape[0] - 1

    def rows_of(self, ref, q, p):
        return ref[q, (p - 1) * self.half : p * self.half, :]

    def main(self, q, p):
        if q < self.fields:
            return self.rows_of(self.st, q, p)
        return self.rows_of(self.fl, q - self.fields, p)

    def beyond(self, q, p):
        if q < self.fields:
            return self.rows_of(self.zst, q, p)
        return self.rows_of(self.zfl, q - self.fields, p)

    def part(self, second):
        return self.t.part_second if second else self.t.part_first

    def beside(self, q, p):
        return self.part(p == 2)(self.y_above[q], self.y_below[q])

    def third_place(self, q):
        return self.fields + FLUID + q // 2, q % 2

    def x_third(self, q, upper):
        tile, which = self.third_place(q)
        found = self.x_above[tile] if upper else self.x_below[tile]
        return self.t.swap(found) if which else found

    def y_third(self, q, p):
        t = self.t
        tile, which = self.third_place(q)
        turn_above, turn_below = ((0, 0), (-1, 1), (2, -2), (1, -1))[2 * which + p - 1]
        above, below = t.turn(self.y_above[tile], turn_above), t.turn(self.y_below[tile], turn_below)
        return jnp.where(t.slot == 2, above, below)

    def z_place(self, q):
        return 4 * self.edge.index(q) + 2

    def x_beyond(self, q, upper):
        tile = self.x_above[self.last] if upper else self.x_below[self.last]
        return self.t.spin(tile, -self.z_place(q))

    def y_beyond(self, q, p):
        return self.t.spin(self.beside(self.last, p), -self.z_place(q))

    def corner(self, q, p):
        place, turn = q, 0
        if q >= CURVED:
            n = q - self.fields
            place, turn = CURVED + n // 4, CORNER_TURNS[n % 4]
        above, below = self.t.turn(self.c_above[place], -turn), self.t.turn(self.c_below[place], -turn)
        return self.part(p > 0)(above, below)

    def corner_layers(self, p):
        place = CORNER_TILES - 1
        return self.part(p > 0)(self.c_above[place], self.c_below[place])

    def plane(self, q):
        inner = self.inner
        return (
            [self.x_below[q]] + [self.main(q, p) for p in inner] + [self.x_above[q]],
            [None] + [self.beside(q, p) for p in inner] + [None],
            [self.x_beyond(q, False)]
            + [self.beyond(q, p) for p in inner]
            + [self.x_beyond(q, True)],
            [None] + [self.y_beyond(q, p) for p in inner] + [None],
        )


def weigh(chi_face, alpha_face):
    shrink = volume_over(chi_face)
    return shrink, alpha_face / shrink


def primitives(half, spots, cons, centred, chi, alpha, batch):
    found = {}
    for start in range(0, len(spots), batch):
        group = spots[start : start + batch]

        def gather(planes):
            return jnp.concatenate([planes[k][p] for k, p in group], axis=0)

        shrink = volume_over(gather(chi))
        mag_raw = [gather(centred[i]) for i in range(3)]
        mag = [m * shrink for m in mag_raw]
        values = recover([gather(c) * shrink for c in cons], mag)
        u = values[2:5]
        factor = gather(alpha) * lax.rsqrt(1.0 + dot(u, u))
        field = [
            factor * (u[(i + 2) % 3] * mag_raw[(i + 1) % 3] - u[(i + 1) % 3] * mag_raw[(i + 2) % 3])
            for i in range(3)
        ]
        for n, spot in enumerate(group):
            found[spot] = [value[n * half : (n + 1) * half] for value in values + mag + field]
    return found


def ring_fluxes(prims, chi, alpha, normals, d, up, down):
    found = []
    for here, there in ((0, 1), (1, 0)):
        left, right = [], []
        for a, b in zip(prims[here], prims[there]):
            below = down(a, b, 1)
            middle = a - below
            left.append(below + 0.5 * limited(below - down(a, b, 2), middle))
            right.append(a - 0.5 * limited(middle, up(a, b, 1) - a))
        shrink, weight = weigh(
            0.5 * (chi[here] + down(chi[here], chi[there], 1)),
            0.5 * (alpha[here] + down(alpha[here], alpha[there], 1)),
        )
        found.append(face_flux(left, right, normals[here] * shrink, weight, d))
    return [a - up(a, b, 1) for a, b in zip(*found)]


def early_kernel(
    cells, zst, zfl, x_below, y_first, y_second, x_above, below_lanes,
    st_rate, hydro_rate, slopes, electric, pairs, sides, thirds, pairs_z, sides_z, grads, seconds, damped, tensors,
):
    halo = Halo(cells, zst, zfl, x_below, y_first, y_second, x_above, below_lanes)
    t, fields, half, own, cy = halo.t, halo.fields, halo.half, halo.own, halo.cy
    st, fl, inner = halo.st, halo.fl, halo.inner

    for q in range(fields):
        pairs[q, 0] = halo.x_third(q, False)
        pairs[q, 1] = x_below[q]
        for p in inner:
            pairs[q, 1 + p] = halo.main(q, p)
            sides[q, p - 1] = halo.beside(q, p)
            thirds[q, p - 1] = halo.y_third(q, p)
        pairs[q, 2 + own] = x_above[q]
        pairs[q, 3 + own] = halo.x_third(q, True)
        if q < CURVED:
            pairs_z[q, 0] = halo.x_beyond(q, False)
            pairs_z[q, own + 1] = halo.x_beyond(q, True)
            for p in inner:
                pairs_z[q, p] = halo.beyond(q, p)
                sides_z[q, p - 1] = halo.y_beyond(q, p)

    span = halo.span
    face = [halo.plane(fields + 5 + i) for i in range(3)]

    def halves(kind, p):
        own_x, own_y, own_z = (f[kind][p] for f in face)
        pair = kind in (0, 2)
        known_x = pair or p < own
        last = kind == 0 and p == own + 1
        if pair:
            next_x = halo.x_third(fields, True) if last else face[0][kind][min(p + 1, own + 1)]
            next_x = t.odd(own_x, next_x)
        else:
            next_x = t.odd_swapped(own_x, face[0][kind][p + 1] if known_x else own_x)
        dx = 0.5 * (next_x - own_x)
        dz = 0.5 * (t.z_up(own_z, face[2][kind ^ 2][p], 1) - own_z)
        inside = 1 <= p <= own
        if not pair:
            here = jnp.where(t.slot == 2, halo.y_third(fields, p), own_y) if kind == 1 else own_y
            next_y = t.y_up(here, face[1][kind ^ 1][p], 1)
        else:
            next_y = t.y_up(own_y, face[1][kind ^ 1][p] if inside else own_y, 1)
        dy = 0.5 * (next_y - own_y)
        if pair and not inside:
            dy = jnp.where(t.slot == cy - 1, -(dx + dz), dy)
        if not pair and not known_x:
            dx = jnp.where(t.row < cy, -(dy + dz), dx)
        return own_x + dx, own_y + dy, own_z + dz

    spots = [(0, p) for p in span] + [(1, p) for p in inner]
    spots += [(2, p) for p in span] + [(3, p) for p in inner]
    centred = [[[None] * (own + 2) for _ in range(4)] for _ in range(3)]
    for k, p in spots:
        for i, value in enumerate(halves(k, p)):
            centred[i][k][p] = value
    chi, alpha = halo.plane(0), halo.plane(7)
    found = primitives(
        half, spots, [halo.plane(fields + q) for q in range(5)], centred, chi, alpha, BATCH
    )

    lines = [[found[0, p][i] for p in span] for i in range(8)] + [chi[0], alpha[0]]
    odd_lines = [[t.odd(f[p], f[min(p + 1, own + 1)]) for p in span] for f in lines]
    fluxes = [None]
    for p in range(1, own + 2):
        left, right = [], []
        for f, o in zip(lines[:8], odd_lines):
            here = f[p] - o[p - 1]
            left.append(o[p - 1] + 0.5 * limited(o[p - 1] - f[p - 1], here))
            right.append(f[p] - 0.5 * limited(here, o[p] - f[p]))
        shrink, weight = weigh(
            0.5 * (lines[8][p] + odd_lines[8][p - 1]), 0.5 * (lines[9][p] + odd_lines[9][p - 1])
        )
        fluxes.append(face_flux(left, right, face[0][0][p] * shrink, weight, 0))
    for p in inner:
        changes = [
            ring_fluxes(
                [found[k, p][:8] for k in (0, kind)],
                [chi[k][p] for k in (0, kind)],
                [alpha[k][p] for k in (0, kind)],
                [face[d][k][p] for k in (0, kind)],
                d,
                up,
                down,
            )
            for d, kind, up, down in ((1, 1, t.y_up, t.y_down), (2, 2, t.z_up, t.z_down))
        ]
        for q in range(5):
            change = fluxes[p][q] - t.odd(fluxes[p][q], fluxes[p + 1][q])
            tensors[p - 1, 6 + q] = change + changes[0][q] + changes[1][q]
        rest, pressure = found[0, p][:2]
        u = found[0, p][2:5]
        parts = stress_parts(rest, pressure, u, found[0, p][5:8])
        lorentz_sq, over, over_sq, time_b, grown_b, b_square, enthalpy, inertia = parts
        total_pressure = pressure + 0.5 * b_square
        for s, (i, j) in enumerate(INDEX_PAIRS):
            value = inertia * u[i] * u[j] - over_sq * (grown_b[i] * grown_b[j])
            tensors[p - 1, s] = value + total_pressure if i == j else value

    ex, ey, ez = (
        [[found[k, p][8 + i] if (k, p) in found else None for p in span] for k in range(4)]
        for i in range(3)
    )
    ey_x = [
        [ey[k][p] + t.odd(ey[k][p - 1], ey[k][p]) if p else None for p in span] for k in (0, 2)
    ]
    edge_y = [None] + [ey_x[0][p] + t.z_down(ey_x[0][p], ey_x[1][p], 1) for p in span[1:]]
    for p in span[1:]:
        electric[p - 1] = ez[0][p] + t.odd(ez[0][p - 1], ez[0][p])
    for p in inner:
        electric[own + p] = ez[1][p]
        edge_y_z = ey_x[1][p] + t.z_down(ey_x[1][p], ey_x[0][p], 1)
        ex_y = ex[0][p] + t.y_down(ex[0][p], ex[1][p], 1)
        ex_y_h = ex[1][p] + t.y_down(ex[1][p], ex[0][p], 1)
        ex_y_z = ex[2][p] + t.y_down(ex[2][p], ex[3][p], 1)
        ex_y_hz = ex[3][p] + t.y_down(ex[3][p], ex[2][p], 1)
        edge_x = ex_y + t.z_down(ex_y, ex_y_z, 1)
        edge_x_h = ex_y_h + t.z_down(ex_y_h, ex_y_hz, 1)
        edge_x_z = ex_y_z + t.z_down(ex_y_z, ex_y, 1)
        place = slice((p - 1) * half, p * half)
        hydro_rate[5, place, :] = t.z_up(edge_y[p], edge_y_z, 1) - edge_y[p]
        hydro_rate[6, place, :] = edge_x - t.z_up(edge_x, edge_x_z, 1)
        hydro_rate[7, place, :] = (t.y_up(edge_x, edge_x_h, 1) - edge_x) - (
            t.odd(edge_y[p], edge_y[p + 1]) - edge_y[p]
        )

    def pair_step(index):
        p = index + 1
        base = index * half

        for q in range(fields):
            centre = pairs[q, p + 1]
            x_m3 = t.odd(pairs[q, p - 1], pairs[q, p])
            x_m2 = pairs[q, p]
            x_m1 = t.odd(pairs[q, p], centre)
            x_p1 = t.odd(centre, pairs[q, p + 2])
            x_p2 = pairs[q, p + 2]
            x_p3 = t.odd(pairs[q, p + 2], pairs[q, p + 3])
            side, third = sides[q, index], thirds[q, index]
            y_m1, y_m2 = t.y_down(centre, side, 1), t.y_down(centre, side, 2)
            y_p1, y_p2 = t.y_up(centre, side, 1), t.y_up(centre, side, 2)
            y_m3 = t.turn(
                jnp.where(t.slot >= cy - 2, side, jnp.where(t.slot == cy - 3, third, centre)), 3
            )
            y_p3 = t.turn(jnp.where(t.slot < 2, side, jnp.where(t.slot == 2, third, centre)), -3)
            beyond = zst[q, pl.ds(base, half), :]
            z_m1, z_m2, z_m3 = (t.z_down(centre, beyond, k) for k in (1, 2, 3))
            z_p1, z_p2, z_p3 = (t.z_up(centre, beyond, k) for k in (1, 2, 3))
            dx = first_diff(x_m2, x_m1, x_p1, x_p2)
            dy = first_diff(y_m2, y_m1, y_p1, y_p2)
            grads[q, 0] = dx
            if q < CURVED:
                slopes[q, index] = dx
            grads[q, 1] = dy
            grads[q, 2] = first_diff(z_m2, z_m1, z_p1, z_p2)
            near = [x_m1 + x_p1, y_m1 + y_p1, z_m1 + z_p1]
            far = [x_m2 + x_p2, y_m2 + y_p2, z_m2 + z_p2]
            outer = (x_m3 + x_p3) + (y_m3 + y_p3) + (z_m3 + z_p3)
            damped[q] = (DISSIPATION / 64.0) * (
                outer - 6.0 * (far[0] + far[1] + far[2]) + 15.0 * (near[0] + near[1] + near[2])
                - 60.0 * centre
            )
            if q < CURVED:
                for s, d in ((0, 0), (3, 1), (5, 2)):
                    seconds[q, s] = (1.0 / 12.0) * (16.0 * near[d] - far[d] - 30.0 * centre)
                b_m, b_c, b_p = pairs_z[q, p - 1], pairs_z[q, p], pairs_z[q, p + 1]
                dx_z = first_diff(b_m, t.odd(b_m, b_c), t.odd(b_c, b_p), b_p)
                b_s = sides_z[q, p - 1]
                dy_z = first_diff(
                    t.y_down(b_c, b_s, 2),
                    t.y_down(b_c, b_s, 1),
                    t.y_up(b_c, b_s, 1),
                    t.y_up(b_c, b_s, 2),
                )
                for s, inside, outside in ((2, dx, dx_z), (4, dy, dy_z)):
                    seconds[q, s] = first_diff(
                        t.z_down(inside, outside, 2),
                        t.z_down(inside, outside, 1),
                        t.z_up(inside, outside, 1),
                        t.z_up(inside, outside, 2),
                    )

        def value(q):
            return pairs[q, p + 1]

        def fluid_value(q):
            return fl[q, pl.ds(base, half), :]

        conformal, lapse = value(0), value(7)
        over_chi = 1.0 / conformal
        metric = symmetric([value(1 + s) for s in range(6)])
        shift = [value(8 + i) for i in range(3)]
        extrinsic, theta = value(11), value(21)
        traceless = symmetric([value(12 + s) for s in range(6)])
        connection = [value(18 + i) for i in range(3)]
        inverse = inverse_metric(metric)
        grad = [[grads[q, k] for k in range(3)] for q in range(fields)]
        chi_grad, lapse_grad = grad[0], grad[7]
        shift_grad = [[grad[8 + i][k] for i in range(3)] for k in range(3)]
        trace_k = extrinsic + 2.0 * theta

        stress = symmetric([tensors[p - 1, s] for s in range(6)])
        held = [fluid_value(q) for q in range(5)]
        shrink = volume_over(conformal)
        energy = held[4] + held[0]
        third_k = trace_k * (1.0 / 3.0)
        curved = [
            [
                (traceless[i][j] + metric[i][j] * third_k) if i <= j else None for j in range(3)
            ]
            for i in range(3)
        ]
        work = (
            stress[0][0] * curved[0][0]
            + stress[1][1] * curved[1][1]
            + stress[2][2] * curved[2][2]
            + 2.0
            * (
                stress[0][1] * curved[0][1]
                + stress[0][2] * curved[0][2]
                + stress[1][2] * curved[1][2]
            )
        )
        rates = [tensors[p - 1, 6 + q] for q in range(5)]
        for i in range(3):
            rates[1 + i] = (
                rates[1 + i]
                - energy * lapse_grad[i]
                + total([held[1 + k] * grad[8 + k][i] for k in range(3)])
            )
        rates[4] = (
            rates[4] + lapse * work * over_chi / shrink - dot(held[1:4], lapse_grad)
        )
        for q in range(5):
            hydro_rate[q, pl.ds(base, half), :] = rates[q]
        density = energy * shrink
        momentum = [held[1 + i] * shrink for i in range(3)]

        lowered = [[[None] * 3 for _ in range(3)] for _ in range(3)]
        for i in range(3):
            for j in range(3):
                for k in range(j, 3):
                    got = 0.5 * (
                        grad[1 + slot_of(i, k)][j]
                        + grad[1 + slot_of(i, j)][k]
                        - grad[1 + slot_of(j, k)][i]
                    )
                    lowered[i][j][k] = lowered[i][k][j] = got
        raised = [[[None] * 3 for _ in range(3)] for _ in range(3)]
        for i in range(3):
            for j in range(3):
                for k in range(j, 3):
                    got = total([inverse[i][l] * lowered[l][j][k] for l in range(3)])
                    raised[i][j][k] = raised[i][k][j] = got
        contracted = [trace_with(inverse, raised[i]) for i in range(3)]

        def hessian_trace(q):
            return (
                inverse[0][0] * seconds[q, 0]
                + inverse[1][1] * seconds[q, 3]
                + inverse[2][2] * seconds[q, 5]
                + 2.0 * (inverse[0][2] * seconds[q, 2] + inverse[1][2] * seconds[q, 4])
            )

        def second_cov(q, slope):
            bent = [total([raised[k][i][j] * slope[k] for k in range(3)]) for i, j in INDEX_PAIRS]
            return symmetric(
                [-bent[s] if s == 1 else seconds[q, s] - bent[s] for s in range(len(bent))]
            )

        chi_cov = second_cov(0, chi_grad)
        chi_lap = trace_with(inverse, chi_cov)
        raised_chi = [dot(inverse[i], chi_grad) for i in range(3)]
        chi_square = dot(raised_chi, chi_grad)
        cross_term = dot(raised_chi, lapse_grad)
        half_chi = 0.5 * over_chi
        plain_cov = second_cov(7, lapse_grad)
        lapse_cov = symmetric(
            [
                plain_cov[i][j]
                + (
                    chi_grad[i] * lapse_grad[j]
                    + chi_grad[j] * lapse_grad[i]
                    - metric[i][j] * cross_term
                )
                * half_chi
                for i, j in INDEX_PAIRS
            ]
        )
        lapse_lap = conformal * trace_with(inverse, lapse_cov)

        mixed = [
            [[dot(inverse[l], lowered[k][j]) for j in range(3)] for k in range(3)]
            for l in range(3)
        ]
        quarter_sq = half_chi * half_chi
        metric_factor = chi_lap * half_chi - 3.0 * chi_square * quarter_sq
        ricci = []
        for i, j in INDEX_PAIRS:
            second_part = -0.5 * hessian_trace(1 + slot_of(i, j))
            connection_part = 0.5 * total(
                [metric[k][i] * grad[18 + k][j] + metric[k][j] * grad[18 + k][i] for k in range(3)]
            )
            contracted_part = 0.5 * total(
                [contracted[k] * (lowered[i][j][k] + lowered[j][i][k]) for k in range(3)]
            )
            if i == j:
                quadratic = total(
                    [
                        raised[k][l][i] * (2.0 * mixed[l][i][k] + mixed[l][k][i])
                        for k in range(3)
                        for l in range(3)
                    ]
                )
            else:
                quadratic = total(
                    [
                        raised[k][l][i] * (mixed[l][j][k] + mixed[l][k][j])
                        + raised[k][l][j] * mixed[l][i][k]
                        for k in range(3)
                        for l in range(3)
                    ]
                )
            conformal_part = (
                chi_cov[i][j] * half_chi
                + metric[i][j] * metric_factor
                - chi_grad[i] * chi_grad[j] * quarter_sq
            )
            ricci.append(
                second_part + connection_part + contracted_part + quadratic + conformal_part
            )
        ricci = symmetric(ricci)
        ricci_scalar = conformal * trace_with(inverse, ricci)
        stress_trace = conformal * trace_with(inverse, stress)

        up_a = [
            [total([inverse[i][k] * traceless[k][j] for k in range(3)]) for j in range(3)]
            for i in range(3)
        ]
        raised_a = symmetric(
            [total([up_a[i][l] * inverse[j][l] for l in range(3)]) for i, j in INDEX_PAIRS]
        )
        a_square = trace_with(traceless, raised_a)
        shift_div = shift_grad[0][0] + shift_grad[1][1] + shift_grad[2][2]
        two_thirds_div = (2.0 / 3.0) * shift_div

        def finish(q, rate):
            rate = rate + dot(shift, grad[q]) + damped[q]
            st_rate[q, pl.ds(base, half), :] = rate

        finish(0, (2.0 / 3.0) * conformal * (lapse * trace_k - shift_div))
        finish(7, -2.0 * lapse * extrinsic)
        for i in range(3):
            finish(8 + i, 0.75 * connection[i] - SHIFT_DAMPING * shift[i])
        finish(
            11,
            lapse
            * (
                a_square
                + trace_k * trace_k * (1.0 / 3.0)
                + FOUR_PI * (stress_trace + density)
                + KAPPA_ONE * theta
            )
            - lapse_lap,
        )
        source = symmetric(
            [
                lapse * (ricci[i][j] - 2.0 * FOUR_PI * stress[i][j]) - lapse_cov[i][j]
                for i, j in INDEX_PAIRS
            ]
        )
        third_trace = trace_with(inverse, source) * (1.0 / 3.0)
        for s, (i, j) in enumerate(INDEX_PAIRS):
            finish(
                1 + s,
                total(
                    [
                        metric[i][k] * shift_grad[j][k] + metric[j][k] * shift_grad[i][k]
                        for k in range(3)
                    ]
                )
                - metric[i][j] * two_thirds_div
                - 2.0 * lapse * traceless[i][j],
            )
            product = total([traceless[i][k] * up_a[k][j] for k in range(3)])
            finish(
                12 + s,
                total(
                    [
                        traceless[i][k] * shift_grad[j][k] + traceless[j][k] * shift_grad[i][k]
                        for k in range(3)
                    ]
                )
                - traceless[i][j] * two_thirds_div
                + conformal * (source[i][j] - metric[i][j] * third_trace)
                + lapse * (trace_k * traceless[i][j] - 2.0 * product),
            )
        for i in range(3):
            bracket = (
                trace_with(raised_a, raised[i])
                - 1.5 * dot(raised_a[i], chi_grad) * over_chi
                - dot(inverse[i], [2.0 * grad[11][j] + grad[21][j] for j in range(3)]) * (1.0 / 3.0)
                - 2.0 * FOUR_PI * dot(inverse[i], momentum)
            )
            spread = [
                seconds[8, 0] + seconds[10, 2],
                seconds[9, 3] + seconds[10, 4],
                seconds[8, 2] + seconds[9, 4] + seconds[10, 5],
            ]
            finish(
                18 + i,
                contracted[i] * two_thirds_div
                - total([contracted[j] * shift_grad[j][i] for j in range(3)])
                + hessian_trace(8 + i)
                + dot(inverse[i], spread) * (1.0 / 3.0)
                - 2.0 * dot(raised_a[i], lapse_grad)
                + 2.0
                * lapse
                * (bracket - KAPPA_ONE * (connection[i] - contracted[i])),
            )
        finish(
            21,
            0.5
            * lapse
            * (
                ricci_scalar
                - a_square
                + (2.0 / 3.0) * trace_k * trace_k
                - 4.0 * FOUR_PI * density
            )
            - 2.0 * KAPPA_ONE * lapse * theta,
        )

    for index in range(own):
        pair_step(index)


def late_kernel(
    cells, zst, zfl, x_below, y_first, y_second, x_above, below_lanes, c_first, c_second, line_two, line_top,
    st_rate, hydro_rate, slopes, electric, st_out, fl_out,
):
    halo = Halo(
        cells, zst, zfl, x_below, y_first, y_second, x_above, below_lanes, c_first, c_second
    )
    x_below, x_above = halo.x_below, halo.x_above
    t, fields, half, own = halo.t, halo.fields, halo.half, halo.own
    inner, span = halo.inner, halo.span

    top = jnp.maximum(line_top[...], line_two[...])
    for lines in (c_first, c_second):
        top = jnp.maximum(top, lines[CORNER_TILES - 1, TOP_ROW : TOP_ROW + 1, :])
    dt = COURANT / top

    for p in inner:
        place = slice((p - 1) * half, p * half)
        mixed = []
        for q in range(CURVED):
            s_m, s_c, s_p = (
                halo.beside(q, n) if 1 <= n <= own else halo.corner(q, n) for n in (p - 1, p, p + 1)
            )
            slope = slopes[q, p - 1]
            slope_side = first_diff(s_m, t.odd_swapped(s_m, s_c), t.odd_swapped(s_c, s_p), s_p)
            mixed.append(
                first_diff(
                    t.y_down(slope, slope_side, 2),
                    t.y_down(slope, slope_side, 1),
                    t.y_up(slope, slope_side, 1),
                    t.y_up(slope, slope_side, 2),
                )
            )
        conformal, lapse = halo.main(0, p), halo.main(7, p)
        metric = [halo.main(1 + s, p) for s in range(6)]
        inverse = inverse_metric(symmetric(metric))
        half_chi = 0.5 / conformal
        cross = inverse[0][1]
        chi_trace = 2.0 * cross * mixed[0] * half_chi
        ricci = [metric[s] * chi_trace - cross * mixed[1 + s] for s in range(6)]
        ricci[1] = ricci[1] + mixed[0] * half_chi
        source = [lapse * r for r in ricci]
        source[1] = source[1] - mixed[7]
        third_trace = trace_with(inverse, symmetric(source)) * (1.0 / 3.0)
        extra = {
            11: -2.0 * conformal * cross * mixed[7],
            21: 0.5 * lapse * conformal * trace_with(inverse, symmetric(ricci)),
        }
        for s in range(6):
            extra[12 + s] = conformal * (source[s] - metric[s] * third_trace)
        for i in range(3):
            extra[18 + i] = 2.0 * cross * mixed[8 + i] + (1.0 / 3.0) * (
                inverse[i][0] * mixed[9] + inverse[i][1] * mixed[8]
            )
        for q in range(fields):
            rate = st_rate[q, place, :]
            if q in extra:
                rate = rate + extra[q]
            st_out[q, place, :] = halo.main(q, p) + dt * rate

    end = own + 1
    ends = (0, end)
    bx_face, by_face, bz_face = ({p: halo.corner(fields + 5 + i, p) for p in ends} for i in range(3))
    layers = {p: halo.corner_layers(p) for p in ends}
    bx_face[end] = layers[end]
    by_face[0] = jnp.where(t.slot < 2, layers[0], by_face[0])
    centred = [{}, {}, {}]
    for p in ends:
        following = halo.beside(fields + 5, 1) if p == 0 else bx_face[p]
        edge_cells = x_below if p == 0 else x_above
        dx = 0.5 * (t.odd_swapped(bx_face[p], following) - bx_face[p])
        dy = 0.5 * (t.y_up(by_face[p], edge_cells[fields + 6], 1) - by_face[p])
        centred[0][p] = bx_face[p] + dx
        centred[1][p] = by_face[p] + dy
        centred[2][p] = bz_face[p] - (dx + dy)
    corners = [{p: halo.corner(q, p) for p in ends} for q in [0, 7] + list(range(fields, fields + 5))]
    found = primitives(
        half, [(0, p) for p in ends], [[c] for c in corners[2:]], [[c] for c in centred],
        [corners[0]], [corners[1]], 2,
    )
    ez_h = [found[0, 0][10]] + [electric[own + p] for p in inner] + [found[0, end][10]]
    ez_x_h = [None] + [ez_h[p] + t.odd_swapped(ez_h[p - 1], ez_h[p]) for p in span[1:]]
    ez_x = [None] + [electric[p - 1] for p in span[1:]]
    edge_z = [None] + [ez_x[p] + t.y_down(ez_x[p], ez_x_h[p], 1) for p in span[1:]]
    quarter = 0.25 * dt
    for p in inner:
        place = slice((p - 1) * half, p * half)
        edge_z_h = ez_x_h[p] + t.y_down(ez_x_h[p], ez_x[p], 1)
        for q in range(5):
            fl_out[q, place, :] = halo.main(fields + q, p) + dt * hydro_rate[q, place, :]
        x_rate = hydro_rate[5, place, :] - (t.y_up(edge_z[p], edge_z_h, 1) - edge_z[p])
        y_rate = hydro_rate[6, place, :] + (t.odd(edge_z[p], edge_z[p + 1]) - edge_z[p])
        z_rate = hydro_rate[7, place, :]
        for i, rate in enumerate((x_rate, y_rate, z_rate)):
            fl_out[5 + i, place, :] = halo.main(fields + 5 + i, p) + quarter * rate


def per_device(spacetime, fluid):
    fields, cx, cy, cz = spacetime.shape
    rows = cx * cy
    st = spacetime.reshape(fields, rows, cz)
    fl = fluid.reshape(FLUID, rows, cz)
    sizes = [lax.axis_size(a) for a in ("gx", "gy", "gz")]
    tile = (2 * cy, cz)
    f32 = jnp.float32

    def shape(*dims):
        return jax.ShapeDtypeStruct(dims, f32)

    def beyond(cells):
        n = sizes[2]
        after = lax.ppermute(cells, "gz", [((i + 1) % n, i) for i in range(n)])
        if n == 2:
            return after
        before = lax.ppermute(cells, "gz", [(i, (i + 1) % n) for i in range(n)])
        lane = lax.broadcasted_iota(jnp.int32, cells.shape, 2)
        return jnp.where(lane < cz // 2, after, before)

    def beyond_lanes(packed):
        n = sizes[2]
        after = lax.ppermute(packed, "gz", [((i + 1) % n, i) for i in range(n)])
        if n == 2:
            return after
        before = lax.ppermute(packed, "gz", [(i, (i + 1) % n) for i in range(n)])
        lane = lax.broadcasted_iota(jnp.int32, packed.shape, 2)
        return jnp.where(lane % 4 < 2, before, after)

    params = pltpu.CompilerParams(vmem_limit_bytes=48 * 1024 * 1024)
    zst, zfl = beyond(st), beyond(fl)
    cells = jnp.concatenate([st, fl], axis=0)
    face = shape(face_tiles(fields), *tile)
    corner = shape(CORNER_TILES, *tile)
    lane_row = shape(1, cz)
    def call(kernel, outs, name, operands, scratch=()):
        return pl.pallas_call(
            kernel,
            out_shape=outs,
            scratch_shapes=scratch,
            compiler_params=params,
            name=name,
        )(*operands)

    def shift(cells, step):
        n = lax.axis_size("gx")
        return lax.ppermute(cells, "gx", [(i, (i + step) % n) for i in range(n)])

    def trade(cells, first):
        axis = "gy"
        n = lax.axis_size(axis)
        step = [1, -1] if first else [-1, 1]
        return lax.ppermute(cells, axis, [(i, (i + step[i % 2]) % n) for i in range(n)])

    def two_away(cells, axis):
        n = lax.axis_size(axis)
        return lax.ppermute(cells, axis, [(i, (i + 2) % n) for i in range(n)]) if n == 4 else cells

    short = sizes[0] <= 4 and sizes[1] <= 4 and sizes[2] <= 2
    x_high = call(pack_up_kernel, face, "pack_up", (cells,))
    x_below = shift(x_high, 1)
    x_low, y_first, y_second, top = call(
        pack_kernel, [face, face, face, shape(TOP_TILES, *tile)], "pack", (cells, zst, zfl)
    )
    below_lanes = beyond_lanes(call(lanes_kernel, shape(1, *tile), "lanes", (x_below,)))
    y_first = trade(y_first, True)
    x_above = shift(x_low, -1)
    y_second = trade(y_second, False)
    top_two = two_away(top, "gx")
    c_first, c_second, line_top = call(
        relay_kernel,
        [corner, corner, lane_row],
        "relay",
        (x_below, below_lanes, y_first, y_second, x_above, top, top_two),
    )
    c_first = trade(c_first, True)
    c_second = trade(c_second, False)
    if short:
        line_two = two_away(line_top, "gy")
    else:
        line_two = lax.pmax(line_top, ("gx", "gy", "gz"))
    own = cx // 2
    arrived = (cells, zst, zfl, x_below, y_first, y_second, x_above, below_lanes)
    early = call(
        early_kernel,
        [
            shape(*st.shape),
            shape(FLUID, rows, cz),
            shape(CURVED, own, *tile),
            shape(2 * own + 1, *tile),
        ],
        "early",
        arrived,
        [
            pltpu.VMEM((fields, own + 4) + tile, f32),
            pltpu.VMEM((fields, own) + tile, f32),
            pltpu.VMEM((fields, own) + tile, f32),
            pltpu.VMEM((CURVED, own + 2) + tile, f32),
            pltpu.VMEM((CURVED, own) + tile, f32),
            pltpu.VMEM((fields, 3) + tile, f32),
            pltpu.VMEM((CURVED, 6) + tile, f32),
            pltpu.VMEM((fields,) + tile, f32),
            pltpu.VMEM((own, 11) + tile, f32),
        ],
    )
    st_next, fl_next = call(
        late_kernel,
        [shape(*st.shape), shape(*fl.shape)],
        "late",
        (*arrived, c_first, c_second, line_two, line_top, *early),
    )
    return st_next.reshape(spacetime.shape), fl_next.reshape(fluid.shape)


def solution(mesh):
    spec = P(None, "gx", "gy", "gz")
    return jax.shard_map(
        per_device, mesh=mesh, in_specs=(spec, spec), out_specs=(spec, spec), check_vma=False
    )
```

```python
import functools
import math

import jax
import jax.numpy as jnp
from jax import lax
from jax.experimental import pallas as pl
from jax.experimental.pallas import tpu as pltpu
from jax.sharding import PartitionSpec as P

RECOVERY_STEPS = 4
INDEX_PAIRS = ((0, 0), (0, 1), (0, 2), (1, 1), (1, 2), (2, 2))
COURANT = 0.25
DISSIPATION = 0.2
KAPPA_ONE = 0.02
SHIFT_DAMPING = 1.0
SPEED_CAP = 0.99
PRESSURE_FLOOR = 0.01
FOUR_PI = 4.0 * math.pi

BATCH = 6
CURVED = 11
FLUID = 8


def total(pieces):
    summed = pieces[0]
    for member in pieces[1:]:
        summed = summed + member
    return summed


def dot(first_vec, second_vec):
    return total([first_vec[i] * second_vec[i] for i in range(3)])


def slot_of(i, j):
    return INDEX_PAIRS.index((min(i, j), max(i, j)))


def symmetric(entries):
    return [[entries[slot_of(i, j)] for j in range(3)] for i in range(3)]


def trace_with(inverse, tensor):
    return (
        inverse[0][0] * tensor[0][0]
        + inverse[1][1] * tensor[1][1]
        + inverse[2][2] * tensor[2][2]
        + 2.0
        * (
            inverse[0][1] * tensor[0][1]
            + inverse[0][2] * tensor[0][2]
            + inverse[1][2] * tensor[1][2]
        )
    )


def inverse_metric(metric):
    cofactor = [
        metric[1][1] * metric[2][2] - metric[1][2] * metric[1][2],
        metric[0][2] * metric[1][2] - metric[0][1] * metric[2][2],
        metric[0][1] * metric[1][2] - metric[0][2] * metric[1][1],
        metric[0][0] * metric[2][2] - metric[0][2] * metric[0][2],
        metric[0][1] * metric[0][2] - metric[0][0] * metric[1][2],
        metric[0][0] * metric[1][1] - metric[0][1] * metric[0][1],
    ]
    determinant = (
        metric[0][0] * cofactor[0] + metric[0][1] * cofactor[1] + metric[0][2] * cofactor[2]
    )
    over = 1.0 / determinant
    return symmetric([c * over for c in cofactor])


class Tile:
    def __init__(self, cy, cz):
        self.cy, self.rows, self.lanes = cy, 2 * cy, cz
        shape = (self.rows, cz)
        self.row = lax.broadcasted_iota(jnp.int32, shape, 0)
        self.lane = lax.broadcasted_iota(jnp.int32, shape, 1)
        self.slot = lax.rem(self.row, cy)

    def turn(self, tile, amount):
        amount = amount % self.rows
        return tile if amount == 0 else pltpu.roll(tile, amount, 0)

    def spin(self, tile, amount):
        amount = amount % self.lanes
        return tile if amount == 0 else pltpu.roll(tile, amount, 1)

    def swap(self, tile):
        return self.turn(tile, self.cy)

    def odd(self, a, b):
        return self.turn(jnp.where(self.row < self.cy, b, a), self.cy)

    def odd_swapped(self, a, b):
        return self.turn(jnp.where(self.row < self.cy, a, b), self.cy)

    def y_up(self, main, beyond, k):
        return self.turn(jnp.where(self.slot < k, beyond, main), -k)

    def y_down(self, main, beyond, k):
        return self.turn(jnp.where(self.slot >= self.cy - k, beyond, main), k)

    def z_up(self, main, beyond, k):
        return self.spin(jnp.where(self.lane < k, beyond, main), -k)

    def z_down(self, main, beyond, k):
        return self.spin(jnp.where(self.lane >= self.lanes - k, beyond, main), k)

    def corner_rows(self, side, turn):
        places = ((0, 2), (self.cy - 1, self.cy + 1))[side]
        first, second = [(place + turn) % self.rows for place in places]
        return (self.row == first) | (self.row == second)

    def join_low(self, u, v):
        return jnp.where(self.slot < 2, self.swap(u), self.turn(v, 2))

    def join_high(self, u, v):
        return jnp.where(self.slot >= self.cy - 2, self.swap(u), self.turn(self.swap(v), -2))

    def part_first(self, from_above, from_below):
        return jnp.where(self.slot < 2, from_above, from_below)

    def part_second(self, from_above, from_below):
        return self.turn(jnp.where(self.slot < 2, from_below, from_above), 2)


def edge_list(tiles):
    fields = next(n for n in range(tiles) if face_tiles(n) == tiles)
    return list(range(CURVED)) + list(range(fields, fields + FLUID))


CORNER_TURNS = (0, 1, 4, 5)
TOP_TILES = 2
CORNER_TILES = CURVED + FLUID // 4 + 1
TOP_ROW = 6


def face_tiles(fields):
    return fields + FLUID + len(pairs_of(third_list(fields))) + 1


def third_list(fields):
    return list(range(fields + 1))


def pairs_of(items):
    return [(items[i], items[min(i + 1, len(items) - 1)]) for i in range(0, len(items), 2)]


def top_speed(st):
    inverse = inverse_metric(symmetric([st[1 + s] for s in range(6)]))
    scale = 2.0 * st[7] * st[0]
    speeds = [jnp.abs(st[8 + d]) + jnp.sqrt(scale * inverse[d][d]) for d in range(3)]
    top = jnp.maximum(jnp.maximum(speeds[0], speeds[1]), speeds[2])
    return jnp.max(jnp.max(top, axis=1, keepdims=True), axis=0, keepdims=True)


class Chosen:
    def __init__(self, first, second, swapped):
        self.first, self.second, self.swapped, self.shape = first, second, swapped, first.shape

    def __getitem__(self, key):
        return jnp.where(self.swapped, self.second[key], self.first[key])


class Sent:
    def __init__(self, first, second, swapped):
        self.first, self.second, self.swapped, self.shape = first, second, swapped, first.shape

    def put(self, key, lower, upper):
        self.first[key] = jnp.where(self.swapped, upper, lower)
        self.second[key] = jnp.where(self.swapped, lower, upper)


class Joined:
    def __init__(self, tiles, tail):
        self.tiles, self.tail = tiles, tail
        self.shape = tuple(tiles.shape)

    def __getitem__(self, key):
        q, rows = (key[0], key[1:]) if isinstance(key, tuple) else (key, ())
        if q == self.tiles.shape[0] - 1:
            return self.tail[(0,) + rows]
        return self.tiles[(q,) + rows]


def even_along_y(tile):
    return jnp.full(tile, lax.rem(lax.axis_index("gy"), 2), jnp.int32) == 0


def pack_up_kernel(cells, x_high):
    count, rows, lanes = cells.shape
    fields, half = count - FLUID, rows // 2
    t = Tile(rows // 4, lanes)
    for q in range(count):
        x_high[q] = cells[q, half:rows, :]
    for n, (a, b) in enumerate(pairs_of(list(range(fields)) + [fields + 5])):
        x_high[count + n] = jnp.where(
            t.row < t.cy, t.swap(cells[b, 0:half, :]), cells[a, 0:half, :]
        )
    x_high[x_high.shape[0] - 1] = jnp.broadcast_to(top_speed(cells), t.row.shape)


def lanes_kernel(x_below, out):
    t = Tile(x_below.shape[1] // 2, x_below.shape[2])
    last = x_below.shape[0] - 1
    packed = x_below[last]
    for place, q in enumerate(edge_list(x_below.shape[0])):
        piece = t.spin(x_below[q], 4 * place + 2)
        here = (t.lane >= 4 * place) & (t.lane < 4 * place + 4)
        packed = jnp.where(here, piece, packed)
    out[0] = packed


def pack_kernel(cells, zst, zfl, *outs):
    fields, rows, lanes = zst.shape
    st, fl = cells.at[0:fields], cells.at[fields : fields + FLUID]
    cy = rows // 4
    t = Tile(cy, lanes)
    x_low, y_first, y_second, top_out = outs
    half = t.rows
    to_y = Sent(y_first, y_second, even_along_y((half, lanes)))

    def own(ref, q):
        return [ref[q, 0:half, :], ref[q, half : 2 * half, :]]

    tiles, beyond = [], []
    for q in range(fields):
        tiles.append(own(st, q))
        beyond.append(own(zst, q) if q < CURVED else None)
    for q in range(FLUID):
        tiles.append(own(fl, q))
        beyond.append(own(zfl, q))

    packed = [None] * 4
    place_count = 0
    for q, (first, second) in enumerate(tiles):
        x_low[q] = first
        to_y.put(q, t.join_low(first, second), t.join_high(first, second))
        if beyond[q] is not None:
            zf, zs = beyond[q]
            for m, piece in enumerate((zf, zs, t.join_low(zf, zs), t.join_high(zf, zs))):
                piece = t.spin(piece, 4 * place_count + 2)
                packed[m] = (
                    piece if place_count == 0 else jnp.where(t.lane < 4 * place_count, packed[m], piece)
                )
            place_count += 1
    for n, (a, b) in enumerate(pairs_of(third_list(fields))):
        slot = fields + FLUID + n
        xa, xb = (tiles[q if q < fields else fields + 5] for q in (a, b))
        x_low[slot] = jnp.where(t.row < cy, xa[1], t.swap(xb[1]))
        ya, yb = (tiles[q if q < fields else fields + 6] for q in (a, b))
        w = [t.swap(ya[0]), t.swap(ya[1]), t.swap(yb[0]), t.swap(yb[1])]
        s = t.slot
        low = jnp.where(s == 0, t.turn(w[2], -2), t.turn(w[3], -1))
        low = jnp.where(s == 2, w[0], jnp.where(s == 3, t.turn(w[1], 1), low))
        high = jnp.where(s == 3, t.turn(w[2], 2), t.turn(w[3], 1))
        high = jnp.where(s == 1, w[0], jnp.where(s == 0, t.turn(w[1], -1), high))
        to_y.put(slot, low, high)
    top = jnp.maximum(top_speed(st), top_speed(zst))
    top_out[...] = jnp.broadcast_to(top, top_out.shape)
    last = x_low.shape[0] - 1
    x_lanes = [jnp.where(t.lane < 4 * place_count, piece, top) for piece in packed[:2]]
    y_lanes = [jnp.where(t.lane < 4 * place_count, piece, top) for piece in packed[2:]]
    x_low[last] = x_lanes[0]
    to_y.put(last, *y_lanes)


def relay_kernel(x_below, below_lanes, x_above, y_first, top, top_two, c_first, c_second, line_top):
    cy, lanes = x_below.shape[1] // 2, x_below.shape[2]
    t = Tile(cy, lanes)
    to_y = Sent(c_first, c_second, even_along_y((t.rows, lanes)))
    last = x_below.shape[0] - 1
    line = jnp.maximum(top[0, 0:1, :], top_two[0, 0:1, :])
    line = jnp.maximum(line, x_below[last, 0:1, lanes - 1 : lanes])
    x_below = Joined(x_below, below_lanes)
    for beside in (x_below, x_above, y_first):
        line = jnp.maximum(line, beside[last, 0:1, lanes - 1 : lanes])
    line_top[...] = line
    edge = edge_list(x_below.shape[0])
    for q in range(CURVED):
        below, above = x_below[q], x_above[q]
        to_y.put(q, t.join_low(below, above), t.join_high(below, above))
    for n in range(0, FLUID, 4):
        low, high = None, None
        for turn, q in zip(CORNER_TURNS, edge[CURVED + n : CURVED + n + 4]):
            below, above = x_below[q], x_above[q]
            below, above = (t.turn(j(below, above), turn) for j in (t.join_low, t.join_high))
            if low is None:
                low, high = below, above
            else:
                low = jnp.where(t.corner_rows(0, turn), below, low)
                high = jnp.where(t.corner_rows(1, turn), above, high)
        to_y.put(CURVED + n // 4, low, high)
    along_x, along_y = edge[CURVED + 5], edge[CURVED + 6]
    low = t.join_low(x_below[along_y], x_above[along_y])
    high = t.join_high(x_below[along_x], x_above[along_x])
    low, high = (jnp.where(t.row == TOP_ROW, line, tile) for tile in (low, high))
    to_y.put(CORNER_TILES - 1, low, high)


def limited(a, b):
    return jnp.maximum(jnp.minimum(a, b), 0.0) + jnp.minimum(jnp.maximum(a, b), 0.0)


def recover(conserved, magnetic):
    density = conserved[0]
    momenta = conserved[1:4]
    energy = conserved[4] + density
    mom_sq = dot(momenta, momenta)
    mag_sq = dot(magnetic, magnetic)
    cross = dot(momenta, magnetic)
    cross_sq = cross * cross

    def state(z):
        grown = z + mag_sq
        over = 1.0 / (z * grown)
        speed_sq = (mom_sq * z * z + cross_sq * (2.0 * z + mag_sq)) * over * over
        kept = 1.0 - jnp.minimum(speed_sq, SPEED_CAP)
        rest = density * jnp.sqrt(kept)
        return kept, rest, 0.5 * (z * kept - rest), grown * over

    z = jnp.maximum(energy - 0.5 * mag_sq, density)
    for _ in range(RECOVERY_STEPS):
        kept, rest, pressure, over_z = state(z)
        residual = (
            z
            + mag_sq
            - pressure
            - 0.5 * mag_sq * kept
            - 0.5 * cross_sq * over_z * over_z
            - energy
        )
        z = jnp.maximum(z - residual / (1.0 - 0.5 * kept), density)
    kept, rest, pressure, over_z = state(z)
    pressure = jnp.maximum(pressure, PRESSURE_FLOOR * rest)
    scale = lax.rsqrt(kept) / (z + mag_sq)
    along = cross * over_z
    four_vel = [scale * (momenta[i] + along * magnetic[i]) for i in range(3)]
    return [rest, pressure] + four_vel


def stress_parts(rest, pressure, u, magnetic):
    lorentz_sq = 1.0 + dot(u, u)
    over = lax.rsqrt(lorentz_sq)
    over_sq = over * over
    time_b = dot(u, magnetic)
    grown_b = [magnetic[i] + time_b * u[i] for i in range(3)]
    b_square = (dot(magnetic, magnetic) + time_b * time_b) * over_sq
    enthalpy = rest + 2.0 * pressure
    inertia = enthalpy + b_square
    return lorentz_sq, over, over_sq, time_b, grown_b, b_square, enthalpy, inertia


def face_state(rest, pressure, u, magnetic, d):
    lorentz_sq, over, over_sq, time_b, grown_b, b_square, enthalpy, inertia = stress_parts(
        rest, pressure, u, magnetic
    )
    total_pressure = pressure + 0.5 * b_square
    lorentz = lorentz_sq * over
    density = rest * lorentz
    carried = inertia * lorentz
    time_over = time_b * over
    conserved = [density]
    conserved += [carried * u[j] - time_over * grown_b[j] for j in range(3)]
    conserved += [inertia * lorentz_sq - total_pressure - time_b * time_b - density]
    mass_flux = rest * u[d]
    flux = [mass_flux]
    pushed = inertia * u[d]
    b_over = grown_b[d] * over_sq
    for j in range(3):
        flux_j = pushed * u[j] - b_over * grown_b[j]
        flux.append(flux_j + total_pressure if j == d else flux_j)
    flux.append(carried * u[d] - time_over * grown_b[d] - mass_flux)
    ratio = 1.0 / (enthalpy * inertia)
    sound_sq = 2.0 * pressure * inertia * ratio
    alfven_sq = b_square * enthalpy * ratio
    fast_sq = sound_sq + alfven_sq - sound_sq * alfven_sq
    slow = 1.0 - fast_sq
    velocity = u[d] * over
    rest_part = 1.0 - dot(u, u) * over_sq * fast_sq
    spread = jnp.sqrt(fast_sq * over_sq * (rest_part - velocity * velocity * slow))
    fastest = (jnp.abs(velocity * slow) + spread) / rest_part
    return conserved, flux, fastest


def face_flux(left, right, normal, weight, d):
    sides = []
    for state in (left, right):
        magnetic = [normal if i == d else state[5 + i] for i in range(3)]
        sides.append(face_state(state[0], state[1], state[2:5], magnetic, d))
    (cons_l, flux_l, fast_l), (cons_r, flux_r, fast_r) = sides
    signal = jnp.maximum(fast_l, fast_r)
    scale = 0.5 * weight
    return [scale * (flux_l[q] + flux_r[q] - signal * (cons_r[q] - cons_l[q])) for q in range(5)]


def volume_over(conformal):
    return conformal * jnp.sqrt(conformal)


def first_diff(down_two, down, up, up_two):
    return (8.0 / 12.0) * (up - down) + (1.0 / 12.0) * (down_two - up_two)


class Halo:
    def __init__(self, cells, zst, zfl, x_below, y_first, x_above, y_second, below_lanes, *corners):
        x_below = Joined(x_below, below_lanes)
        self.fields, self.block, self.lanes = zst.shape
        even_y = even_along_y((self.block // 2, self.lanes))
        y_below, y_above = Chosen(y_first, y_second, even_y), Chosen(y_second, y_first, even_y)
        if corners:
            c_first, c_second = corners
            self.c_below = Chosen(c_first, c_second, even_y)
            self.c_above = Chosen(c_second, c_first, even_y)
        self.st = cells.at[0 : self.fields]
        self.fl = cells.at[self.fields : self.fields + FLUID]
        self.zst, self.zfl = zst, zfl
        self.x_below, self.x_above = x_below, x_above
        self.y_below, self.y_above = y_below, y_above
        self.cy = self.block // 4
        self.t = Tile(self.cy, self.lanes)
        self.half = self.t.rows
        self.own = self.block // self.half
        self.inner = range(1, self.own + 1)
        self.span = range(self.own + 2)
        self.edge = edge_list(x_below.shape[0])
        self.last = x_below.shape[0] - 1

    def rows_of(self, ref, q, p):
        return ref[q, (p - 1) * self.half : p * self.half, :]

    def main(self, q, p):
        if q < self.fields:
            return self.rows_of(self.st, q, p)
        return self.rows_of(self.fl, q - self.fields, p)

    def beyond(self, q, p):
        if q < self.fields:
            return self.rows_of(self.zst, q, p)
        return self.rows_of(self.zfl, q - self.fields, p)

    def part(self, second):
        return self.t.part_second if second else self.t.part_first

    def beside(self, q, p):
        return self.part(p == 2)(self.y_above[q], self.y_below[q])

    def third_place(self, q):
        return self.fields + FLUID + q // 2, q % 2

    def x_third(self, q, upper):
        tile, which = self.third_place(q)
        found = self.x_above[tile] if upper else self.x_below[tile]
        return self.t.swap(found) if which else found

    def y_third(self, q, p):
        t = self.t
        tile, which = self.third_place(q)
        turn_above, turn_below = ((0, 0), (-1, 1), (2, -2), (1, -1))[2 * which + p - 1]
        above, below = t.turn(self.y_above[tile], turn_above), t.turn(self.y_below[tile], turn_below)
        return jnp.where(t.slot == 2, above, below)

    def z_place(self, q):
        return 4 * self.edge.index(q) + 2

    def x_beyond(self, q, upper):
        tile = self.x_above[self.last] if upper else self.x_below[self.last]
        return self.t.spin(tile, -self.z_place(q))

    def y_beyond(self, q, p):
        return self.t.spin(self.beside(self.last, p), -self.z_place(q))

    def corner(self, q, p):
        place, turn = q, 0
        if q >= CURVED:
            n = q - self.fields
            place, turn = CURVED + n // 4, CORNER_TURNS[n % 4]
        above, below = self.t.turn(self.c_above[place], -turn), self.t.turn(self.c_below[place], -turn)
        return self.part(p > 0)(above, below)

    def corner_layers(self, p):
        place = CORNER_TILES - 1
        return self.part(p > 0)(self.c_above[place], self.c_below[place])

    def plane(self, q):
        inner = self.inner
        return (
            [self.x_below[q]] + [self.main(q, p) for p in inner] + [self.x_above[q]],
            [None] + [self.beside(q, p) for p in inner] + [None],
            [self.x_beyond(q, False)]
            + [self.beyond(q, p) for p in inner]
            + [self.x_beyond(q, True)],
            [None] + [self.y_beyond(q, p) for p in inner] + [None],
        )


def weigh(chi_face, alpha_face):
    shrink = volume_over(chi_face)
    return shrink, alpha_face / shrink


def primitives(half, spots, cons, centred, chi, alpha, batch):
    found = {}
    for start in range(0, len(spots), batch):
        group = spots[start : start + batch]

        def gather(planes):
            return jnp.concatenate([planes[k][p] for k, p in group], axis=0)

        shrink = volume_over(gather(chi))
        mag_raw = [gather(centred[i]) for i in range(3)]
        mag = [m * shrink for m in mag_raw]
        values = recover([gather(c) * shrink for c in cons], mag)
        u = values[2:5]
        factor = gather(alpha) * lax.rsqrt(1.0 + dot(u, u))
        field = [
            factor * (u[(i + 2) % 3] * mag_raw[(i + 1) % 3] - u[(i + 1) % 3] * mag_raw[(i + 2) % 3])
            for i in range(3)
        ]
        for n, spot in enumerate(group):
            found[spot] = [value[n * half : (n + 1) * half] for value in values + mag + field]
    return found


def ring_fluxes(prims, chi, alpha, normals, d, up, down):
    found = []
    for here, there in ((0, 1), (1, 0)):
        left, right = [], []
        for a, b in zip(prims[here], prims[there]):
            below = down(a, b, 1)
            middle = a - below
            left.append(below + 0.5 * limited(below - down(a, b, 2), middle))
            right.append(a - 0.5 * limited(middle, up(a, b, 1) - a))
        shrink, weight = weigh(
            0.5 * (chi[here] + down(chi[here], chi[there], 1)),
            0.5 * (alpha[here] + down(alpha[here], alpha[there], 1)),
        )
        found.append(face_flux(left, right, normals[here] * shrink, weight, d))
    return [a - up(a, b, 1) for a, b in zip(*found)]


def early_kernel(
    cells, zst, zfl, x_below, y_first, x_above, y_second, below_lanes,
    st_rate, hydro_rate, slopes, electric, pairs, sides, thirds, pairs_z, sides_z, grads, seconds, damped, tensors,
):
    halo = Halo(cells, zst, zfl, x_below, y_first, x_above, y_second, below_lanes)
    t, fields, half, own, cy = halo.t, halo.fields, halo.half, halo.own, halo.cy
    st, fl, inner = halo.st, halo.fl, halo.inner

    for q in range(fields):
        pairs[q, 0] = halo.x_third(q, False)
        pairs[q, 1] = x_below[q]
        for p in inner:
            pairs[q, 1 + p] = halo.main(q, p)
            sides[q, p - 1] = halo.beside(q, p)
            thirds[q, p - 1] = halo.y_third(q, p)
        pairs[q, 2 + own] = x_above[q]
        pairs[q, 3 + own] = halo.x_third(q, True)
        if q < CURVED:
            pairs_z[q, 0] = halo.x_beyond(q, False)
            pairs_z[q, own + 1] = halo.x_beyond(q, True)
            for p in inner:
                pairs_z[q, p] = halo.beyond(q, p)
                sides_z[q, p - 1] = halo.y_beyond(q, p)

    span = halo.span
    face = [halo.plane(fields + 5 + i) for i in range(3)]

    def halves(kind, p):
        own_x, own_y, own_z = (f[kind][p] for f in face)
        pair = kind in (0, 2)
        known_x = pair or p < own
        last = kind == 0 and p == own + 1
        if pair:
            next_x = halo.x_third(fields, True) if last else face[0][kind][min(p + 1, own + 1)]
            next_x = t.odd(own_x, next_x)
        else:
            next_x = t.odd_swapped(own_x, face[0][kind][p + 1] if known_x else own_x)
        dx = 0.5 * (next_x - own_x)
        dz = 0.5 * (t.z_up(own_z, face[2][kind ^ 2][p], 1) - own_z)
        inside = 1 <= p <= own
        if not pair:
            here = jnp.where(t.slot == 2, halo.y_third(fields, p), own_y) if kind == 1 else own_y
            next_y = t.y_up(here, face[1][kind ^ 1][p], 1)
        else:
            next_y = t.y_up(own_y, face[1][kind ^ 1][p] if inside else own_y, 1)
        dy = 0.5 * (next_y - own_y)
        if pair and not inside:
            dy = jnp.where(t.slot == cy - 1, -(dx + dz), dy)
        if not pair and not known_x:
            dx = jnp.where(t.row < cy, -(dy + dz), dx)
        return own_x + dx, own_y + dy, own_z + dz

    spots = [(0, p) for p in span] + [(1, p) for p in inner]
    spots += [(2, p) for p in span] + [(3, p) for p in inner]
    centred = [[[None] * (own + 2) for _ in range(4)] for _ in range(3)]
    for k, p in spots:
        for i, value in enumerate(halves(k, p)):
            centred[i][k][p] = value
    chi, alpha = halo.plane(0), halo.plane(7)
    found = primitives(
        half, spots, [halo.plane(fields + q) for q in range(5)], centred, chi, alpha, BATCH
    )

    lines = [[found[0, p][i] for p in span] for i in range(8)] + [chi[0], alpha[0]]
    odd_lines = [[t.odd(f[p], f[min(p + 1, own + 1)]) for p in span] for f in lines]
    fluxes = [None]
    for p in range(1, own + 2):
        left, right = [], []
        for f, o in zip(lines[:8], odd_lines):
            here = f[p] - o[p - 1]
            left.append(o[p - 1] + 0.5 * limited(o[p - 1] - f[p - 1], here))
            right.append(f[p] - 0.5 * limited(here, o[p] - f[p]))
        shrink, weight = weigh(
            0.5 * (lines[8][p] + odd_lines[8][p - 1]), 0.5 * (lines[9][p] + odd_lines[9][p - 1])
        )
        fluxes.append(face_flux(left, right, face[0][0][p] * shrink, weight, 0))
    for p in inner:
        changes = [
            ring_fluxes(
                [found[k, p][:8] for k in (0, kind)],
                [chi[k][p] for k in (0, kind)],
                [alpha[k][p] for k in (0, kind)],
                [face[d][k][p] for k in (0, kind)],
                d,
                up,
                down,
            )
            for d, kind, up, down in ((1, 1, t.y_up, t.y_down), (2, 2, t.z_up, t.z_down))
        ]
        for q in range(5):
            change = fluxes[p][q] - t.odd(fluxes[p][q], fluxes[p + 1][q])
            tensors[p - 1, 6 + q] = change + changes[0][q] + changes[1][q]
        rest, pressure = found[0, p][:2]
        u = found[0, p][2:5]
        parts = stress_parts(rest, pressure, u, found[0, p][5:8])
        lorentz_sq, over, over_sq, time_b, grown_b, b_square, enthalpy, inertia = parts
        total_pressure = pressure + 0.5 * b_square
        for s, (i, j) in enumerate(INDEX_PAIRS):
            value = inertia * u[i] * u[j] - over_sq * (grown_b[i] * grown_b[j])
            tensors[p - 1, s] = value + total_pressure if i == j else value

    ex, ey, ez = (
        [[found[k, p][8 + i] if (k, p) in found else None for p in span] for k in range(4)]
        for i in range(3)
    )
    ey_x = [
        [ey[k][p] + t.odd(ey[k][p - 1], ey[k][p]) if p else None for p in span] for k in (0, 2)
    ]
    edge_y = [None] + [ey_x[0][p] + t.z_down(ey_x[0][p], ey_x[1][p], 1) for p in span[1:]]
    for p in span[1:]:
        electric[p - 1] = ez[0][p] + t.odd(ez[0][p - 1], ez[0][p])
    for p in inner:
        electric[own + p] = ez[1][p]
        edge_y_z = ey_x[1][p] + t.z_down(ey_x[1][p], ey_x[0][p], 1)
        ex_y = ex[0][p] + t.y_down(ex[0][p], ex[1][p], 1)
        ex_y_h = ex[1][p] + t.y_down(ex[1][p], ex[0][p], 1)
        ex_y_z = ex[2][p] + t.y_down(ex[2][p], ex[3][p], 1)
        ex_y_hz = ex[3][p] + t.y_down(ex[3][p], ex[2][p], 1)
        edge_x = ex_y + t.z_down(ex_y, ex_y_z, 1)
        edge_x_h = ex_y_h + t.z_down(ex_y_h, ex_y_hz, 1)
        edge_x_z = ex_y_z + t.z_down(ex_y_z, ex_y, 1)
        place = slice((p - 1) * half, p * half)
        hydro_rate[5, place, :] = t.z_up(edge_y[p], edge_y_z, 1) - edge_y[p]
        hydro_rate[6, place, :] = edge_x - t.z_up(edge_x, edge_x_z, 1)
        hydro_rate[7, place, :] = (t.y_up(edge_x, edge_x_h, 1) - edge_x) - (
            t.odd(edge_y[p], edge_y[p + 1]) - edge_y[p]
        )

    def pair_step(index):
        p = index + 1
        base = index * half

        for q in range(fields):
            centre = pairs[q, p + 1]
            x_m3 = t.odd(pairs[q, p - 1], pairs[q, p])
            x_m2 = pairs[q, p]
            x_m1 = t.odd(pairs[q, p], centre)
            x_p1 = t.odd(centre, pairs[q, p + 2])
            x_p2 = pairs[q, p + 2]
            x_p3 = t.odd(pairs[q, p + 2], pairs[q, p + 3])
            side, third = sides[q, index], thirds[q, index]
            y_m1, y_m2 = t.y_down(centre, side, 1), t.y_down(centre, side, 2)
            y_p1, y_p2 = t.y_up(centre, side, 1), t.y_up(centre, side, 2)
            y_m3 = t.turn(
                jnp.where(t.slot >= cy - 2, side, jnp.where(t.slot == cy - 3, third, centre)), 3
            )
            y_p3 = t.turn(jnp.where(t.slot < 2, side, jnp.where(t.slot == 2, third, centre)), -3)
            beyond = zst[q, pl.ds(base, half), :]
            z_m1, z_m2, z_m3 = (t.z_down(centre, beyond, k) for k in (1, 2, 3))
            z_p1, z_p2, z_p3 = (t.z_up(centre, beyond, k) for k in (1, 2, 3))
            dx = first_diff(x_m2, x_m1, x_p1, x_p2)
            dy = first_diff(y_m2, y_m1, y_p1, y_p2)
            grads[q, 0] = dx
            if q < CURVED:
                slopes[q, index] = dx
            grads[q, 1] = dy
            grads[q, 2] = first_diff(z_m2, z_m1, z_p1, z_p2)
            near = [x_m1 + x_p1, y_m1 + y_p1, z_m1 + z_p1]
            far = [x_m2 + x_p2, y_m2 + y_p2, z_m2 + z_p2]
            outer = (x_m3 + x_p3) + (y_m3 + y_p3) + (z_m3 + z_p3)
            damped[q] = (DISSIPATION / 64.0) * (
                outer - 6.0 * (far[0] + far[1] + far[2]) + 15.0 * (near[0] + near[1] + near[2])
                - 60.0 * centre
            )
            if q < CURVED:
                for s, d in ((0, 0), (3, 1), (5, 2)):
                    seconds[q, s] = (1.0 / 12.0) * (16.0 * near[d] - far[d] - 30.0 * centre)
                b_m, b_c, b_p = pairs_z[q, p - 1], pairs_z[q, p], pairs_z[q, p + 1]
                dx_z = first_diff(b_m, t.odd(b_m, b_c), t.odd(b_c, b_p), b_p)
                b_s = sides_z[q, p - 1]
                dy_z = first_diff(
                    t.y_down(b_c, b_s, 2),
                    t.y_down(b_c, b_s, 1),
                    t.y_up(b_c, b_s, 1),
                    t.y_up(b_c, b_s, 2),
                )
                for s, inside, outside in ((2, dx, dx_z), (4, dy, dy_z)):
                    seconds[q, s] = first_diff(
                        t.z_down(inside, outside, 2),
                        t.z_down(inside, outside, 1),
                        t.z_up(inside, outside, 1),
                        t.z_up(inside, outside, 2),
                    )

        def value(q):
            return pairs[q, p + 1]

        def fluid_value(q):
            return fl[q, pl.ds(base, half), :]

        conformal, lapse = value(0), value(7)
        over_chi = 1.0 / conformal
        metric = symmetric([value(1 + s) for s in range(6)])
        shift = [value(8 + i) for i in range(3)]
        extrinsic, theta = value(11), value(21)
        traceless = symmetric([value(12 + s) for s in range(6)])
        connection = [value(18 + i) for i in range(3)]
        inverse = inverse_metric(metric)
        grad = [[grads[q, k] for k in range(3)] for q in range(fields)]
        chi_grad, lapse_grad = grad[0], grad[7]
        shift_grad = [[grad[8 + i][k] for i in range(3)] for k in range(3)]
        trace_k = extrinsic + 2.0 * theta

        stress = symmetric([tensors[p - 1, s] for s in range(6)])
        held = [fluid_value(q) for q in range(5)]
        shrink = volume_over(conformal)
        energy = held[4] + held[0]
        third_k = trace_k * (1.0 / 3.0)
        curved = [
            [
                (traceless[i][j] + metric[i][j] * third_k) if i <= j else None for j in range(3)
            ]
            for i in range(3)
        ]
        work = (
            stress[0][0] * curved[0][0]
            + stress[1][1] * curved[1][1]
            + stress[2][2] * curved[2][2]
            + 2.0
            * (
                stress[0][1] * curved[0][1]
                + stress[0][2] * curved[0][2]
                + stress[1][2] * curved[1][2]
            )
        )
        rates = [tensors[p - 1, 6 + q] for q in range(5)]
        for i in range(3):
            rates[1 + i] = (
                rates[1 + i]
                - energy * lapse_grad[i]
                + total([held[1 + k] * grad[8 + k][i] for k in range(3)])
            )
        rates[4] = (
            rates[4] + lapse * work * over_chi / shrink - dot(held[1:4], lapse_grad)
        )
        for q in range(5):
            hydro_rate[q, pl.ds(base, half), :] = rates[q]
        density = energy * shrink
        momentum = [held[1 + i] * shrink for i in range(3)]

        lowered = [[[None] * 3 for _ in range(3)] for _ in range(3)]
        for i in range(3):
            for j in range(3):
                for k in range(j, 3):
                    got = 0.5 * (
                        grad[1 + slot_of(i, k)][j]
                        + grad[1 + slot_of(i, j)][k]
                        - grad[1 + slot_of(j, k)][i]
                    )
                    lowered[i][j][k] = lowered[i][k][j] = got
        raised = [[[None] * 3 for _ in range(3)] for _ in range(3)]
        for i in range(3):
            for j in range(3):
                for k in range(j, 3):
                    got = total([inverse[i][l] * lowered[l][j][k] for l in range(3)])
                    raised[i][j][k] = raised[i][k][j] = got
        contracted = [trace_with(inverse, raised[i]) for i in range(3)]

        def hessian_trace(q):
            return (
                inverse[0][0] * seconds[q, 0]
                + inverse[1][1] * seconds[q, 3]
                + inverse[2][2] * seconds[q, 5]
                + 2.0 * (inverse[0][2] * seconds[q, 2] + inverse[1][2] * seconds[q, 4])
            )

        def second_cov(q, slope):
            bent = [total([raised[k][i][j] * slope[k] for k in range(3)]) for i, j in INDEX_PAIRS]
            return symmetric(
                [-bent[s] if s == 1 else seconds[q, s] - bent[s] for s in range(len(bent))]
            )

        chi_cov = second_cov(0, chi_grad)
        chi_lap = trace_with(inverse, chi_cov)
        raised_chi = [dot(inverse[i], chi_grad) for i in range(3)]
        chi_square = dot(raised_chi, chi_grad)
        cross_term = dot(raised_chi, lapse_grad)
        half_chi = 0.5 * over_chi
        plain_cov = second_cov(7, lapse_grad)
        lapse_cov = symmetric(
            [
                plain_cov[i][j]
                + (
                    chi_grad[i] * lapse_grad[j]
                    + chi_grad[j] * lapse_grad[i]
                    - metric[i][j] * cross_term
                )
                * half_chi
                for i, j in INDEX_PAIRS
            ]
        )
        lapse_lap = conformal * trace_with(inverse, lapse_cov)

        mixed = [
            [[dot(inverse[l], lowered[k][j]) for j in range(3)] for k in range(3)]
            for l in range(3)
        ]
        quarter_sq = half_chi * half_chi
        metric_factor = chi_lap * half_chi - 3.0 * chi_square * quarter_sq
        ricci = []
        for i, j in INDEX_PAIRS:
            second_part = -0.5 * hessian_trace(1 + slot_of(i, j))
            connection_part = 0.5 * total(
                [metric[k][i] * grad[18 + k][j] + metric[k][j] * grad[18 + k][i] for k in range(3)]
            )
            contracted_part = 0.5 * total(
                [contracted[k] * (lowered[i][j][k] + lowered[j][i][k]) for k in range(3)]
            )
            if i == j:
                quadratic = total(
                    [
                        raised[k][l][i] * (2.0 * mixed[l][i][k] + mixed[l][k][i])
                        for k in range(3)
                        for l in range(3)
                    ]
                )
            else:
                quadratic = total(
                    [
                        raised[k][l][i] * (mixed[l][j][k] + mixed[l][k][j])
                        + raised[k][l][j] * mixed[l][i][k]
                        for k in range(3)
                        for l in range(3)
                    ]
                )
            conformal_part = (
                chi_cov[i][j] * half_chi
                + metric[i][j] * metric_factor
                - chi_grad[i] * chi_grad[j] * quarter_sq
            )
            ricci.append(
                second_part + connection_part + contracted_part + quadratic + conformal_part
            )
        ricci = symmetric(ricci)
        ricci_scalar = conformal * trace_with(inverse, ricci)
        stress_trace = conformal * trace_with(inverse, stress)

        up_a = [
            [total([inverse[i][k] * traceless[k][j] for k in range(3)]) for j in range(3)]
            for i in range(3)
        ]
        raised_a = symmetric(
            [total([up_a[i][l] * inverse[j][l] for l in range(3)]) for i, j in INDEX_PAIRS]
        )
        a_square = trace_with(traceless, raised_a)
        shift_div = shift_grad[0][0] + shift_grad[1][1] + shift_grad[2][2]
        two_thirds_div = (2.0 / 3.0) * shift_div

        def finish(q, rate):
            rate = rate + dot(shift, grad[q]) + damped[q]
            st_rate[q, pl.ds(base, half), :] = rate

        finish(0, (2.0 / 3.0) * conformal * (lapse * trace_k - shift_div))
        finish(7, -2.0 * lapse * extrinsic)
        for i in range(3):
            finish(8 + i, 0.75 * connection[i] - SHIFT_DAMPING * shift[i])
        finish(
            11,
            lapse
            * (
                a_square
                + trace_k * trace_k * (1.0 / 3.0)
                + FOUR_PI * (stress_trace + density)
                + KAPPA_ONE * theta
            )
            - lapse_lap,
        )
        source = symmetric(
            [
                lapse * (ricci[i][j] - 2.0 * FOUR_PI * stress[i][j]) - lapse_cov[i][j]
                for i, j in INDEX_PAIRS
            ]
        )
        third_trace = trace_with(inverse, source) * (1.0 / 3.0)
        for s, (i, j) in enumerate(INDEX_PAIRS):
            finish(
                1 + s,
                total(
                    [
                        metric[i][k] * shift_grad[j][k] + metric[j][k] * shift_grad[i][k]
                        for k in range(3)
                    ]
                )
                - metric[i][j] * two_thirds_div
                - 2.0 * lapse * traceless[i][j],
            )
            product = total([traceless[i][k] * up_a[k][j] for k in range(3)])
            finish(
                12 + s,
                total(
                    [
                        traceless[i][k] * shift_grad[j][k] + traceless[j][k] * shift_grad[i][k]
                        for k in range(3)
                    ]
                )
                - traceless[i][j] * two_thirds_div
                + conformal * (source[i][j] - metric[i][j] * third_trace)
                + lapse * (trace_k * traceless[i][j] - 2.0 * product),
            )
        for i in range(3):
            bracket = (
                trace_with(raised_a, raised[i])
                - 1.5 * dot(raised_a[i], chi_grad) * over_chi
                - dot(inverse[i], [2.0 * grad[11][j] + grad[21][j] for j in range(3)]) * (1.0 / 3.0)
                - 2.0 * FOUR_PI * dot(inverse[i], momentum)
            )
            spread = [
                seconds[8, 0] + seconds[10, 2],
                seconds[9, 3] + seconds[10, 4],
                seconds[8, 2] + seconds[9, 4] + seconds[10, 5],
            ]
            finish(
                18 + i,
                contracted[i] * two_thirds_div
                - total([contracted[j] * shift_grad[j][i] for j in range(3)])
                + hessian_trace(8 + i)
                + dot(inverse[i], spread) * (1.0 / 3.0)
                - 2.0 * dot(raised_a[i], lapse_grad)
                + 2.0
                * lapse
                * (bracket - KAPPA_ONE * (connection[i] - contracted[i])),
            )
        finish(
            21,
            0.5
            * lapse
            * (
                ricci_scalar
                - a_square
                + (2.0 / 3.0) * trace_k * trace_k
                - 4.0 * FOUR_PI * density
            )
            - 2.0 * KAPPA_ONE * lapse * theta,
        )

    for index in range(own):
        pair_step(index)


def late_kernel(
    cells, zst, zfl, x_below, y_first, x_above, y_second, below_lanes, c_first, c_second, line_top,
    st_rate, hydro_rate, slopes, electric, st_out, fl_out, top_out,
):
    halo = Halo(
        cells, zst, zfl, x_below, y_first, x_above, y_second, below_lanes, c_first, c_second
    )
    x_below, x_above = halo.x_below, halo.x_above
    t, fields, half, own = halo.t, halo.fields, halo.half, halo.own
    inner, span = halo.inner, halo.span

    top = line_top[...]
    for lines in (c_first, c_second):
        top = jnp.maximum(top, lines[CORNER_TILES - 1, TOP_ROW : TOP_ROW + 1, :])
    top_out[...] = top

    for p in inner:
        place = slice((p - 1) * half, p * half)
        mixed = []
        for q in range(CURVED):
            s_m, s_c, s_p = (
                halo.beside(q, n) if 1 <= n <= own else halo.corner(q, n) for n in (p - 1, p, p + 1)
            )
            slope = slopes[q, p - 1]
            slope_side = first_diff(s_m, t.odd_swapped(s_m, s_c), t.odd_swapped(s_c, s_p), s_p)
            mixed.append(
                first_diff(
                    t.y_down(slope, slope_side, 2),
                    t.y_down(slope, slope_side, 1),
                    t.y_up(slope, slope_side, 1),
                    t.y_up(slope, slope_side, 2),
                )
            )
        conformal, lapse = halo.main(0, p), halo.main(7, p)
        metric = [halo.main(1 + s, p) for s in range(6)]
        inverse = inverse_metric(symmetric(metric))
        half_chi = 0.5 / conformal
        cross = inverse[0][1]
        chi_trace = 2.0 * cross * mixed[0] * half_chi
        ricci = [metric[s] * chi_trace - cross * mixed[1 + s] for s in range(6)]
        ricci[1] = ricci[1] + mixed[0] * half_chi
        source = [lapse * r for r in ricci]
        source[1] = source[1] - mixed[7]
        third_trace = trace_with(inverse, symmetric(source)) * (1.0 / 3.0)
        extra = {
            11: -2.0 * conformal * cross * mixed[7],
            21: 0.5 * lapse * conformal * trace_with(inverse, symmetric(ricci)),
        }
        for s in range(6):
            extra[12 + s] = conformal * (source[s] - metric[s] * third_trace)
        for i in range(3):
            extra[18 + i] = 2.0 * cross * mixed[8 + i] + (1.0 / 3.0) * (
                inverse[i][0] * mixed[9] + inverse[i][1] * mixed[8]
            )
        for q in range(fields):
            rate = st_rate[q, place, :]
            if q in extra:
                rate = rate + extra[q]
            st_out[q, place, :] = rate

    end = own + 1
    ends = (0, end)
    bx_face, by_face, bz_face = ({p: halo.corner(fields + 5 + i, p) for p in ends} for i in range(3))
    layers = {p: halo.corner_layers(p) for p in ends}
    bx_face[end] = layers[end]
    by_face[0] = jnp.where(t.slot < 2, layers[0], by_face[0])
    centred = [{}, {}, {}]
    for p in ends:
        following = halo.beside(fields + 5, 1) if p == 0 else bx_face[p]
        edge_cells = x_below if p == 0 else x_above
        dx = 0.5 * (t.odd_swapped(bx_face[p], following) - bx_face[p])
        dy = 0.5 * (t.y_up(by_face[p], edge_cells[fields + 6], 1) - by_face[p])
        centred[0][p] = bx_face[p] + dx
        centred[1][p] = by_face[p] + dy
        centred[2][p] = bz_face[p] - (dx + dy)
    corners = [{p: halo.corner(q, p) for p in ends} for q in [0, 7] + list(range(fields, fields + 5))]
    found = primitives(
        half, [(0, p) for p in ends], [[c] for c in corners[2:]], [[c] for c in centred],
        [corners[0]], [corners[1]], 2,
    )
    ez_h = [found[0, 0][10]] + [electric[own + p] for p in inner] + [found[0, end][10]]
    ez_x_h = [None] + [ez_h[p] + t.odd_swapped(ez_h[p - 1], ez_h[p]) for p in span[1:]]
    ez_x = [None] + [electric[p - 1] for p in span[1:]]
    edge_z = [None] + [ez_x[p] + t.y_down(ez_x[p], ez_x_h[p], 1) for p in span[1:]]
    for p in inner:
        place = slice((p - 1) * half, p * half)
        edge_z_h = ez_x_h[p] + t.y_down(ez_x_h[p], ez_x[p], 1)
        for q in range(5):
            fl_out[q, place, :] = hydro_rate[q, place, :]
        x_rate = hydro_rate[5, place, :] - (t.y_up(edge_z[p], edge_z_h, 1) - edge_z[p])
        y_rate = hydro_rate[6, place, :] + (t.odd(edge_z[p], edge_z[p + 1]) - edge_z[p])
        z_rate = hydro_rate[7, place, :]
        for i, rate in enumerate((x_rate, y_rate, z_rate)):
            fl_out[5 + i, place, :] = 0.25 * rate


def step_kernel(cells, top, line_two, st_rate, fl_rate, st_out, fl_out):
    fields = st_out.shape[0]
    dt = COURANT / jnp.maximum(top[...], line_two[...])
    for q in range(fields):
        st_out[q] = cells[q] + dt * st_rate[q]
    for q in range(FLUID):
        fl_out[q] = cells[fields + q] + dt * fl_rate[q]


def per_device(spacetime, fluid):
    fields, cx, cy, cz = spacetime.shape
    rows = cx * cy
    st = spacetime.reshape(fields, rows, cz)
    fl = fluid.reshape(FLUID, rows, cz)
    sizes = [lax.axis_size(a) for a in ("gx", "gy", "gz")]
    tile = (2 * cy, cz)
    f32 = jnp.float32

    def shape(*dims):
        return jax.ShapeDtypeStruct(dims, f32)

    def beyond(cells):
        n = sizes[2]
        after = lax.ppermute(cells, "gz", [((i + 1) % n, i) for i in range(n)])
        if n == 2:
            return after
        before = lax.ppermute(cells, "gz", [(i, (i + 1) % n) for i in range(n)])
        lane = lax.broadcasted_iota(jnp.int32, cells.shape, 2)
        return jnp.where(lane < cz // 2, after, before)

    def beyond_lanes(packed):
        n = sizes[2]
        after = lax.ppermute(packed, "gz", [((i + 1) % n, i) for i in range(n)])
        if n == 2:
            return after
        before = lax.ppermute(packed, "gz", [(i, (i + 1) % n) for i in range(n)])
        lane = lax.broadcasted_iota(jnp.int32, packed.shape, 2)
        return jnp.where(lane % 4 < 2, before, after)

    params = pltpu.CompilerParams(vmem_limit_bytes=48 * 1024 * 1024)
    zst, zfl = beyond(st), beyond(fl)
    cells = jnp.concatenate([st, fl], axis=0)
    face = shape(face_tiles(fields), *tile)
    corner = shape(CORNER_TILES, *tile)
    lane_row = shape(1, cz)
    def call(kernel, outs, name, operands, scratch=()):
        return pl.pallas_call(
            kernel,
            out_shape=outs,
            scratch_shapes=scratch,
            compiler_params=params,
            name=name,
        )(*operands)

    def shift(cells, step):
        n = lax.axis_size("gx")
        return lax.ppermute(cells, "gx", [(i, (i + step) % n) for i in range(n)])

    def trade(cells, first):
        axis = "gy"
        n = lax.axis_size(axis)
        step = [1, -1] if first else [-1, 1]
        return lax.ppermute(cells, axis, [(i, (i + step[i % 2]) % n) for i in range(n)])

    def two_away(cells, axis):
        n = lax.axis_size(axis)
        return lax.ppermute(cells, axis, [(i, (i + 2) % n) for i in range(n)]) if n == 4 else cells

    short = sizes[0] <= 4 and sizes[1] <= 4 and sizes[2] <= 2
    x_high = call(pack_up_kernel, face, "pack_up", (cells,))
    x_below = shift(x_high, 1)
    x_low, y_first, y_second, top = call(
        pack_kernel, [face, face, face, shape(TOP_TILES, *tile)], "pack", (cells, zst, zfl)
    )
    below_lanes = beyond_lanes(call(lanes_kernel, shape(1, *tile), "lanes", (x_below,)))
    y_first = trade(y_first, True)
    x_above = shift(x_low, -1)
    y_second = trade(y_second, False)
    top_two = two_away(top, "gx")
    c_first, c_second, line_top = call(
        relay_kernel,
        [corner, corner, lane_row],
        "relay",
        (x_below, below_lanes, x_above, y_first, top, top_two),
    )
    c_first = trade(c_first, True)
    c_second = trade(c_second, False)
    if short:
        line_two = two_away(line_top, "gy")
    else:
        line_two = lax.pmax(line_top, ("gx", "gy", "gz"))
    own = cx // 2
    arrived = (cells, zst, zfl, x_below, y_first, x_above, y_second, below_lanes)
    early = call(
        early_kernel,
        [
            shape(*st.shape),
            shape(FLUID, rows, cz),
            shape(CURVED, own, *tile),
            shape(2 * own + 1, *tile),
        ],
        "early",
        arrived,
        [
            pltpu.VMEM((fields, own + 4) + tile, f32),
            pltpu.VMEM((fields, own) + tile, f32),
            pltpu.VMEM((fields, own) + tile, f32),
            pltpu.VMEM((CURVED, own + 2) + tile, f32),
            pltpu.VMEM((CURVED, own) + tile, f32),
            pltpu.VMEM((fields, 3) + tile, f32),
            pltpu.VMEM((CURVED, 6) + tile, f32),
            pltpu.VMEM((fields,) + tile, f32),
            pltpu.VMEM((own, 11) + tile, f32),
        ],
    )
    st_rate, fl_rate, top = call(
        late_kernel,
        [shape(*st.shape), shape(*fl.shape), lane_row],
        "late",
        (*arrived, c_first, c_second, line_top, *early),
    )
    st_next, fl_next = call(
        step_kernel,
        [shape(*st.shape), shape(*fl.shape)],
        "step",
        (cells, top, line_two, st_rate, fl_rate),
    )
    return st_next.reshape(spacetime.shape), fl_next.reshape(fluid.shape)


def solution(mesh):
    spec = P(None, "gx", "gy", "gz")
    return jax.shard_map(
        per_device, mesh=mesh, in_specs=(spec, spec), out_specs=(spec, spec), check_vma=False
    )
```
